32 devices in a mesh: client: 16 (over z, y, x), chan: 2 (over core).
Axes of the slice: x: 2, y: 2, z: 4, core: 2. Of those that a mesh axis runs over, the one named last changes fastest.
Arguments:
- features: bfloat16 [16, 3136, 2048], P('client', None, 'chan'), may hold values from -6 to 6
- labels: int32 [16, 64], P('client'), may hold values from 0 to 99
- mask: int32 [16], P('client'), may hold values 0 or 1
- base_master: float32 [32, 272, 512], P(('client', 'chan')), may hold values from -0.176776695 to 0.176776695, as said below
- base_momentum: float32 [32, 272, 512], P(('client', 'chan')), may hold values from -0.0234375 to 0.0234375
- global_base: float32 [32, 272, 512], P(('client', 'chan')), may hold values from -0.176776695 to 0.176776695, as said below
- norm_params: float32 [16, 2, 2, 1536], P('client', None, 'chan'), may hold values from -0.9 to 1.3, as said below
- norm_first: float32 [16, 2, 2, 1536], P('client', None, 'chan'), may hold values from -0.00061035156 to 0.00061035156
- norm_second: float32 [16, 2, 2, 1536], P('client', None, 'chan'), may hold values from 5.340576e-09 to 3.2043456e-08
- head: float32 [16, 2048, 100], P('client', 'chan'), may hold values from -0.25 to 0.25
- head_first: float32 [16, 2048, 100], P('client', 'chan'), may hold values from -0.015625 to 0.015625
- head_second: float32 [16, 2048, 100], P('client', 'chan'), may hold values from 4.6875e-06 to 1.5625e-05
Outputs:
- loss: float32 [2], replicated
- base_new: float32 [32, 272, 512], P(('client', 'chan'))
- base_momentum_new: float32 [32, 272, 512], P(('client', 'chan'))
- base_low: bfloat16 [32, 272, 512], P(('client', 'chan'))
- norm_new: float32 [16, 2, 2, 1536], P('client', None, 'chan')
- norm_first_new: float32 [16, 2, 2, 1536], P('client', None, 'chan')
- norm_second_new: float32 [16, 2, 2, 1536], P('client', None, 'chan')
- head_new: float32 [16, 2048, 100], P('client', 'chan')
- head_first_new: float32 [16, 2048, 100], P('client', 'chan')
- head_second_new: float32 [16, 2048, 100], P('client', 'chan')
The draws below stay inside these ranges and needn't reach their ends.
Inputs may be any that keep to these rules, and one draw needn't show every extreme that they name: `base_master`: base weights with entries of about one over the root of each matrix's fan-in. `global_base`: drawn like base_master, independently. `norm_params`: gains near one, biases of both signs.
All inputs are finite; a program needn't handle non-finite values. No bound on the sum of `mask` on one device may be relied on, other than what follows from the above.
Results may differ from the reference program's by a relative error of at most 0.012.
Values may be sent and summed in bfloat16 or wider, within the bound.
A program may use at most 512 MiB of HBM per device.

```python
import math
import jax
import jax.numpy as jnp
from jax import lax

C = 2048
M = 512
CLASSES = 100
IMG = 64
NS_STEPS = 5
STEP = 10
CLIENTS = 16
PIX = 3136
BLOCKS = 32
ROW_R = 64
ROW_M = 144
ROWS = 272
HALF = 1536


def layered_scale():
    position = jnp.arange(ROWS)
    inner = jnp.where(position < ROW_R + ROW_M, (9.0 * M) ** (-0.5), M ** (-0.5))
    return jnp.where(position < ROW_R, C ** (-0.5), inner).astype(jnp.float32)


def draw_base_master(key, part):
    key = jax.random.fold_in(key, 11)
    shape = (BLOCKS, ROWS, M)
    noise = jnp.clip(jax.random.normal(key, shape, jnp.float32), -4.0, 4.0)
    return noise * layered_scale()[None, :, None]


def draw_global_base(key, part):
    key = jax.random.fold_in(key, 12)
    shape = (BLOCKS, ROWS, M)
    noise = jnp.clip(jax.random.normal(key, shape, jnp.float32), -4.0, 4.0)
    return noise * layered_scale()[None, :, None]


def draw_norm_params(key, part):
    key = jax.random.fold_in(key, 13)
    gain_key, bias_key = jax.random.split(key)
    shape = (CLIENTS, 1, 2, HALF)
    gains = 1.0 + 0.3 * jax.random.uniform(gain_key, shape, jnp.float32, -1.0, 1.0)
    biases = jnp.clip(0.3 * jax.random.normal(bias_key, shape, jnp.float32), -0.9, 0.9)
    return jnp.concatenate([gains, biases], axis=1)


def with_ends(result, stream_key, low, top_value):
    longest = result.shape.index(max(result.shape))
    spots = []
    for shift in (0, 1):
        where = [jax.random.randint(jax.random.fold_in(stream_key, axis), (), 0, length) for axis, length in enumerate(result.shape)]
        where[longest] = (where[longest] + shift) % result.shape[longest]
        spots.append(tuple(where))
    return result.at[spots[0]].set(low).at[spots[1]].set(top_value)


def block_scale(stream_key, shape, cuts, least, top_value):
    level, own = 1.0, jax.random.fold_in(stream_key, 6)
    for axis_at, blocks in cuts:
        draws = jnp.exp(jax.random.uniform(jax.random.fold_in(own, axis_at), (blocks,), jnp.float32, least / len(cuts), top_value / len(cuts)))
        level = level * jnp.repeat(draws, shape[axis_at] // blocks).reshape([-1 if axis == axis_at else 1 for axis in range(len(shape))])
    return level


def scatter_about(stream_key, shape, scale, reach, pieces=(), kind=jnp.bfloat16):
    array = jax.random.normal(stream_key, shape, jnp.float32) * scale
    if len(pieces) > 0:
        array = block_scale(stream_key, shape, pieces, -0.22, 0.18) * array
    return jnp.clip(array, min=-reach, max=reach).astype(kind)


def setup_inputs(seed: int = 0) -> dict:
    arg_keys = jax.random.split(jax.random.key(seed), 13)
    features = scatter_about(arg_keys[0], (CLIENTS, PIX, C), 1.0, 6.0, ((0, 16), (2, 2)))
    labels = with_ends(jax.random.randint(arg_keys[1], (CLIENTS, IMG), 0, CLASSES), jax.random.fold_in(arg_keys[1], 1), 0, CLASSES - 1).astype(jnp.int32)
    mask = with_ends((jax.random.randint(arg_keys[2], (CLIENTS,), 0, 4) < 3).astype(jnp.int32), jax.random.fold_in(arg_keys[2], 1), 0, 1)
    base_master = draw_base_master(jax.random.fold_in(arg_keys[12], 71), 0)
    base_momentum = scatter_about(arg_keys[4], (BLOCKS, ROWS, M), (CLIENTS ** 0.5 / (7 * (IMG * C) ** 0.5)), 0.0234375, ((0, 32),), jnp.float32)
    global_base = draw_global_base(jax.random.fold_in(arg_keys[12], 71), 0)
    norm_params = draw_norm_params(jax.random.fold_in(arg_keys[12], 71), 0)
    norm_first = scatter_about(arg_keys[7], (CLIENTS, 2, 2, HALF), (0.016 / (IMG * C) ** 0.5), 0.00061035156, ((0, 16), (2, 2)), jnp.float32)
    norm_second = jnp.clip(jnp.exp(math.log(3.204345588869728e-08) - 1.7917595 * jax.random.uniform(arg_keys[8], (CLIENTS, 2, 2, HALF), jnp.float32) ** block_scale(arg_keys[8], (CLIENTS, 2, 2, HALF), ((0, 16), (2, 2)), -0.2, 0.2)), 5.340575981449547e-09, 3.204345588869728e-08)
    head = scatter_about(arg_keys[9], (CLIENTS, C, CLASSES), (C / 4) ** -0.5, 0.25, ((0, 16), (1, 2)), jnp.float32)
    head_first = scatter_about(arg_keys[10], (CLIENTS, C, CLASSES), (0.008 / IMG ** 0.5), 0.015625, ((0, 16), (1, 2)), jnp.float32)
    head_second = jnp.clip(jnp.exp(math.log(1.5625000742147677e-05) - 1.2039728 * jax.random.uniform(arg_keys[11], (CLIENTS, C, CLASSES), jnp.float32) ** block_scale(arg_keys[11], (CLIENTS, C, CLASSES), ((0, 16), (1, 2)), -0.2, 0.2)), 4.687500222644303e-06, 1.5625000742147677e-05)
    return {"features": features, "labels": labels, "mask": mask, "base_master": base_master, "base_momentum": base_momentum, "global_base": global_base, "norm_params": norm_params, "norm_first": norm_first, "norm_second": norm_second, "head": head, "head_first": head_first, "head_second": head_second}


@jax.custom_vjp
def low(v):
    return lax.optimization_barrier(v.astype(jnp.bfloat16)).astype(jnp.float32)

@jax.custom_vjp
def low_back(v):
    return v

def low_keep(v):
    return (low(v), None)

def low_pass(kept, grad):
    return (grad,)

def back_keep(v):
    return (v, None)

def back_low(kept, grad):
    return (low(grad),)
low.defvjp(low_keep, low_pass)
low_back.defvjp(back_keep, back_low)
precise = lax.Precision.HIGHEST
norm_epsilon = 1e-05
prox_weight = 0.05
momentum_decay = 0.95
muon_rate = 0.3
muon_decay = 0.1
schulz_first = 3.4445
schulz_second = -4.775
schulz_third = 2.0315
adam_first = 0.9
adam_second = 0.95
adam_epsilon = 1e-08
head_rate = 0.01
head_decay = 0.05
norm_rate = 0.5

def split_base(flat):
    reduce_weight = flat[:, :ROW_R, :].reshape(C, M)
    middle_weight = flat[:, ROW_R:ROW_R + ROW_M, :].reshape(9 * M, M)
    expand_weight = flat[:, ROW_R + ROW_M:, :].reshape(C, M)
    return (reduce_weight, middle_weight, expand_weight)

def join_base(first_part, middle_part, last_part):
    return jnp.concatenate([first_part.reshape(BLOCKS, ROW_R, M), middle_part.reshape(BLOCKS, ROW_M, M), last_part.reshape(BLOCKS, ROW_R, M)], axis=1)

def norm_layers(params):
    middle_half = M // 2
    bounds = ((0, middle_half), (middle_half, M), (M, HALF))
    layers = []
    for lower, upper in bounds:
        gain = jnp.concatenate([params[0, 0, lower:upper], params[0, 1, lower:upper]])
        bias = jnp.concatenate([params[1, 0, lower:upper], params[1, 1, lower:upper]])
        layers.append((gain, bias))
    return layers

def batch_norm(act, gain, bias):
    centred = act - lax.optimization_barrier(jnp.mean(act, axis=0))
    return centred * lax.rsqrt(lax.optimization_barrier(jnp.mean(centred * centred, axis=0)) + norm_epsilon) * gain + bias

def patches_of(hidden, images):
    width = hidden.shape[1]
    grid = jnp.pad(hidden.reshape(images, 7, 7, width), ((0, 0), (1, 1), (1, 1), (0, 0)))
    taps = [grid[:, shift_y:shift_y + 7, shift_x:shift_x + 7, :] for shift_y in range(3) for shift_x in range(3)]
    return jnp.concatenate(taps, axis=-1).reshape(images * 49, 9 * width)

def client_sum(reduce_weight, middle_weight, expand_weight, params, head_low, features, labels):
    (gain_one, bias_one), (gain_two, bias_two), (gain_three, bias_three) = norm_layers(params)
    inputs = features.astype(jnp.float32)
    act_one = low_back(jnp.dot(inputs, reduce_weight, precision=precise))
    hidden_one = low(jax.nn.silu(batch_norm(act_one, gain_one, bias_one)))
    act_two = low_back(jnp.dot(patches_of(hidden_one, IMG), middle_weight, precision=precise))
    hidden_two = low(jax.nn.silu(batch_norm(act_two, gain_two, bias_two)))
    act_three = low_back(jnp.dot(hidden_two, expand_weight.T, precision=precise))
    output = jax.nn.silu(batch_norm(act_three, gain_three, bias_three) + inputs)
    pooled = low(lax.optimization_barrier(jnp.mean(output.reshape(IMG, 49, C), axis=1)))
    logits = low_back(jnp.dot(pooled, head_low, precision=precise))
    picked = lax.optimization_barrier(jnp.sum(logits * jax.nn.one_hot(labels, CLASSES, dtype=logits.dtype), axis=1))
    return jnp.sum(jax.nn.logsumexp(logits, axis=1) - picked)

def orthogonal(matrix):
    current = matrix / (jnp.sqrt(jnp.sum(matrix * matrix)) + 1e-07)
    for turn in range(NS_STEPS):
        gram = jnp.dot(current.T, current, precision=precise)
        product = jnp.dot(current, gram, precision=precise)
        current = schulz_first * current + schulz_second * product + schulz_third * jnp.dot(product, gram, precision=precise)
    return current

def adam_update(param, grad, first, second, rate, decay):
    first = adam_first * first + (1.0 - adam_first) * grad
    second = adam_second * second + (1.0 - adam_second) * grad * grad
    first_hat = first / (1.0 - adam_first ** STEP)
    second_hat = second / (1.0 - adam_second ** STEP)
    return (param - rate * (first_hat / (jnp.sqrt(second_hat) + adam_epsilon) + decay * param), first, second)

def reference(features, labels, mask, base_master, base_momentum, global_base, norm_params, norm_first, norm_second, head, head_first, head_second):
    client_fn = jax.checkpoint(client_sum)

    def objective(flat, norms, heads):
        reduce_weight, middle_weight, expand_weight = split_base(flat)
        reduce_weight, middle_weight, expand_weight = (low(reduce_weight), low(middle_weight), low(expand_weight))

        def visit(carry, items):
            feats, labs, flag, params, head_one = items
            value = client_fn(reduce_weight, middle_weight, expand_weight, params, low(head_one), feats, labs)
            weight = flag.astype(value.dtype)
            return ((carry[0] + weight * value / IMG, carry[1] + weight * value), None)
        zero = jnp.zeros((), flat.dtype)
        (scaled, raw), unused = lax.scan(visit, (zero, zero), (features, labels, mask, norms, heads))
        diff = flat - global_base
        return (scaled + 0.5 * prox_weight * jnp.sum(diff * diff), raw)
    total, pullback, raw = jax.vjp(objective, base_master, norm_params, head, has_aux=True)
    grad_base, grad_norm, grad_head = pullback(jnp.ones_like(total))
    count = jnp.sum(mask).astype(raw.dtype) * IMG
    loss = jnp.stack([raw, count])
    momentum_new = momentum_decay * base_momentum + grad_base
    parts = split_base(momentum_new)
    ratio = (C / M) ** 0.5
    ortho = join_base(orthogonal(parts[0]) * ratio, orthogonal(parts[1]) * 3.0, orthogonal(parts[2]) * ratio)
    base_new = base_master - muon_rate * (ortho + muon_decay * base_master)
    norm_new, norm_first_new, norm_second_new = adam_update(norm_params, grad_norm, norm_first, norm_second, norm_rate, 0.0)
    head_new, head_first_new, head_second_new = adam_update(head, grad_head, head_first, head_second, head_rate, head_decay)
    return (loss, base_new, momentum_new, base_new.astype(jnp.bfloat16), norm_new, norm_first_new, norm_second_new, head_new, head_first_new, head_second_new)
```

```python
import jax
import jax.numpy as jnp
from jax import lax
from jax.sharding import PartitionSpec as P

NS_STEPS = 5
STEP = 10


precise = lax.Precision.HIGHEST
norm_epsilon = 1e-05
prox_weight = 0.05
momentum_decay = 0.95
muon_rate = 0.3
muon_decay = 0.1
schulz_first = 3.4445
schulz_second = -4.775
schulz_third = 2.0315
adam_first = 0.9
adam_second = 0.95
adam_epsilon = 1e-08
head_rate = 0.01
head_decay = 0.05
norm_rate = 0.5


def patches_of(hidden, images):
    width = hidden.shape[1]
    grid = jnp.pad(hidden.reshape(images, 7, 7, width), ((0, 0), (1, 1), (1, 1), (0, 0)))
    taps = [
        grid[:, shift_y : shift_y + 7, shift_x : shift_x + 7, :]
        for shift_y in range(3)
        for shift_x in range(3)
    ]
    return jnp.concatenate(taps, axis=-1).reshape(images * 49, 9 * width)


def fold_patches(grads, images, width):
    columns = grads.reshape(images, 7, 7, 9, width)
    total = jnp.zeros((images, 9, 9, width), jnp.float32)
    for shift_y in range(3):
        for shift_x in range(3):
            total = total + jnp.pad(
                columns[:, :, :, 3 * shift_y + shift_x, :],
                ((0, 0), (shift_y, 2 - shift_y), (shift_x, 2 - shift_x), (0, 0)),
            )
    return total[:, 1:8, 1:8, :].reshape(images * 49, width)


def norm_forward(act, gain, bias):
    centred = act - jnp.mean(act, axis=0)
    scale = lax.rsqrt(jnp.mean(centred * centred, axis=0) + norm_epsilon)
    normed = centred * scale
    return (normed * gain + bias, normed, scale)


def norm_backward(grad_out, normed, scale, gain):
    scaled = grad_out * gain
    grad_in = scale * (
        scaled - jnp.mean(scaled, axis=0) - normed * jnp.mean(scaled * normed, axis=0)
    )
    return (grad_in, jnp.sum(grad_out * normed, axis=0), jnp.sum(grad_out, axis=0))


def silu_slope(value):
    sigma = jax.nn.sigmoid(value)
    return sigma * (1.0 + value * (1.0 - sigma))


def contract_rows(left, right):
    return lax.dot_general(
        left, right, (((0,), (0,)), ((), ())), preferred_element_type=jnp.float32
    )


def contract_cols(left, right):
    return lax.dot_general(
        left, right, (((1,), (1,)), ((), ())), preferred_element_type=jnp.float32
    )


def gram_of(section):
    return lax.dot_general(section, section, (((0,), (0,)), ((), ())), precision=precise)


def gram_sum(first_part, middle_part, last_part):
    return lax.psum(
        (gram_of(first_part), gram_of(middle_part), gram_of(last_part)), ("client", "chan")
    )


def square(gram):
    return jnp.dot(gram, gram, precision=precise)


def times_poly(left, mixed):
    return schulz_first * left + jnp.dot(left, mixed, precision=precise)


def adam_update(param, grad, first, second, rate, decay):
    first = adam_first * first + (1.0 - adam_first) * grad
    second = adam_second * second + (1.0 - adam_second) * grad * grad
    first_hat = first / (1.0 - adam_first**STEP)
    second_hat = second / (1.0 - adam_second**STEP)
    return (
        param - rate * (first_hat / (jnp.sqrt(second_hat) + adam_epsilon) + decay * param),
        first,
        second,
    )


def on_device(
    features,
    labels,
    mask,
    base_master,
    base_momentum,
    global_base,
    norm_params,
    norm_first,
    norm_second,
    head,
    head_first,
    head_second,
):
    halves = lax.axis_size("chan")
    blocks = lax.axis_size("client") * halves
    local_x = features[0]
    pixels, feat_half = local_x.shape
    width = base_master.shape[2]
    channels = feat_half * halves
    images = labels.shape[1]
    rows_first = channels // blocks
    rows_mid = 9 * width // blocks
    middle_half = width // halves
    master = base_master[0]
    low_master = master.astype(jnp.bfloat16)
    first_piece, middle_piece, last_piece = (
        lax.all_to_all(low_master[:rows_first], "chan", split_axis=1, concat_axis=0, tiled=True),
        lax.all_to_all(
            low_master[rows_first : rows_first + rows_mid],
            "chan",
            split_axis=1,
            concat_axis=0,
            tiled=True,
        ),
        lax.all_to_all(
            low_master[rows_first + rows_mid :], "chan", split_axis=1, concat_axis=0, tiled=True
        ),
    )
    reduce_weight, middle_weight, expand_weight = (
        lax.all_gather(first_piece, "client", axis=0, tiled=True),
        lax.all_gather(middle_piece, "client", axis=0, tiled=True),
        lax.all_gather(last_piece, "client", axis=0, tiled=True),
    )
    params = norm_params[0, :, 0, :]
    gain_one, bias_one = (params[0, :middle_half], params[1, :middle_half])
    gain_two, bias_two = (params[0, middle_half:width], params[1, middle_half:width])
    gain_three, bias_three = (params[0, width:], params[1, width:])
    inputs_all = lax.all_gather(local_x, "chan", axis=1, tiled=True)
    act_one = jnp.dot(inputs_all, reduce_weight, preferred_element_type=jnp.float32)
    norm_one, normed_one, scale_one = norm_forward(act_one, gain_one, bias_one)
    hidden_one = jax.nn.silu(norm_one).astype(jnp.bfloat16)
    full_one = lax.all_gather(hidden_one, "chan", axis=1, tiled=True)
    patches = patches_of(full_one, images)
    act_two = jnp.dot(patches, middle_weight, preferred_element_type=jnp.float32)
    norm_two, normed_two, scale_two = norm_forward(act_two, gain_two, bias_two)
    hidden_two = jax.nn.silu(norm_two).astype(jnp.bfloat16)
    act_three = lax.psum_scatter(
        contract_cols(hidden_two, expand_weight).astype(jnp.bfloat16),
        "chan",
        scatter_dimension=1,
        tiled=True,
    ).astype(jnp.float32)
    norm_three, normed_three, scale_three = norm_forward(act_three, gain_three, bias_three)
    total = norm_three + local_x.astype(jnp.float32)
    output = jax.nn.silu(total)
    pooled = jnp.mean(output.reshape(images, 49, feat_half), axis=1).astype(jnp.bfloat16)
    head_low = head[0].astype(jnp.bfloat16)
    logits = lax.psum(jnp.dot(pooled, head_low, preferred_element_type=jnp.float32), "chan")
    onehot = (labels[0][:, None] == jnp.arange(logits.shape[1])[None, :]).astype(jnp.float32)
    each_loss = jax.nn.logsumexp(logits, axis=1) - jnp.sum(logits * onehot, axis=1)
    flag = mask[0].astype(jnp.float32)
    loss_sum, count = lax.psum((flag * jnp.sum(each_loss), flag * images), "client")
    loss = jnp.stack([loss_sum, count])
    grad_logits = (flag / images * (jax.nn.softmax(logits, axis=1) - onehot)).astype(jnp.bfloat16)
    grad_head = contract_rows(pooled, grad_logits)
    grad_pooled = contract_cols(grad_logits, head_low)
    grad_output = jnp.broadcast_to(grad_pooled[:, None, :] / 49.0, (images, 49, feat_half)).reshape(
        pixels, feat_half
    )
    grad_in_three, grad_gain_three, grad_bias_three = norm_backward(
        grad_output * silu_slope(total), normed_three, scale_three, gain_three
    )
    grad_act_three = grad_in_three.astype(jnp.bfloat16)
    grad_three_all = lax.all_gather(grad_act_three, "chan", axis=1, tiled=True)
    grad_hidden_two = jnp.dot(grad_three_all, expand_weight, preferred_element_type=jnp.float32)
    grad_expand = contract_rows(grad_three_all, hidden_two)
    grad_in_two, grad_gain_two, grad_bias_two = norm_backward(
        grad_hidden_two * silu_slope(norm_two), normed_two, scale_two, gain_two
    )
    grad_act_two = grad_in_two.astype(jnp.bfloat16)
    grad_middle = contract_rows(patches, grad_act_two)
    grad_full_one = fold_patches(contract_cols(grad_act_two, middle_weight), images, width)
    grad_hidden_one = lax.psum_scatter(
        grad_full_one.astype(jnp.bfloat16), "chan", scatter_dimension=1, tiled=True
    ).astype(jnp.float32)
    grad_in_one, grad_gain_one, grad_bias_one = norm_backward(
        grad_hidden_one * silu_slope(norm_one), normed_one, scale_one, gain_one
    )
    grad_reduce = contract_rows(inputs_all, grad_in_one.astype(jnp.bfloat16))
    sum_reduce, sum_middle, sum_expand = (
        lax.psum_scatter(grad_reduce, "client", scatter_dimension=0, tiled=True),
        lax.psum_scatter(grad_middle, "client", scatter_dimension=0, tiled=True),
        lax.psum_scatter(grad_expand, "client", scatter_dimension=0, tiled=True),
    )
    block_reduce, block_middle, block_expand = (
        lax.all_to_all(
            sum_reduce.astype(jnp.bfloat16), "chan", split_axis=0, concat_axis=1, tiled=True
        ).astype(sum_reduce.dtype),
        lax.all_to_all(
            sum_middle.astype(jnp.bfloat16), "chan", split_axis=0, concat_axis=1, tiled=True
        ).astype(sum_middle.dtype),
        lax.all_to_all(
            sum_expand.astype(jnp.bfloat16), "chan", split_axis=0, concat_axis=1, tiled=True
        ).astype(sum_expand.dtype),
    )
    grad_base = jnp.concatenate(
        [block_reduce, block_middle, block_expand], axis=0
    ) + prox_weight * (master - global_base[0])
    momentum_new = momentum_decay * base_momentum[0] + grad_base
    sections = [
        momentum_new[:rows_first],
        momentum_new[rows_first : rows_first + rows_mid],
        momentum_new[rows_first + rows_mid :],
    ]
    raw_grams = gram_sum(sections[0], sections[1], sections[2])
    factors = [1.0 / (jnp.sqrt(jnp.trace(raw_grams[slot])) + 1e-07) for slot in range(3)]
    current = [sections[slot] * factors[slot] for slot in range(3)]
    grams = [raw_grams[slot] * (factors[slot] * factors[slot]) for slot in range(3)]
    for turn in range(NS_STEPS):
        mixed = [schulz_second * gram + schulz_third * square(gram) for gram in grams]
        current = [times_poly(current[slot], mixed[slot]) for slot in range(3)]
        if turn + 1 < NS_STEPS:
            grams = [
                times_poly(times_poly(grams[slot], mixed[slot]), mixed[slot]) for slot in range(3)
            ]
    ratio = (channels / width) ** 0.5
    ortho = jnp.concatenate([current[0] * ratio, current[1] * 3.0, current[2] * ratio], axis=0)
    base_new = master - muon_rate * (ortho + muon_decay * master)
    grad_norm = jnp.stack(
        [
            jnp.concatenate([grad_gain_one, grad_gain_two, grad_gain_three]),
            jnp.concatenate([grad_bias_one, grad_bias_two, grad_bias_three]),
        ]
    )[None, :, None, :]
    norm_new, norm_first_new, norm_second_new = adam_update(
        norm_params, grad_norm, norm_first, norm_second, norm_rate, 0.0
    )
    head_new, head_first_new, head_second_new = adam_update(
        head, grad_head[None], head_first, head_second, head_rate, head_decay
    )
    return (
        loss,
        base_new[None],
        momentum_new[None],
        base_new.astype(jnp.bfloat16)[None],
        norm_new,
        norm_first_new,
        norm_second_new,
        head_new,
        head_first_new,
        head_second_new,
    )


def solution(mesh):
    return jax.shard_map(
        on_device,
        mesh=mesh,
        in_specs=(
            P("client", None, "chan"),
            P("client", None),
            P("client"),
            P(("client", "chan"), None, None),
            P(("client", "chan"), None, None),
            P(("client", "chan"), None, None),
            P("client", None, "chan", None),
            P("client", None, "chan", None),
            P("client", None, "chan", None),
            P("client", "chan", None),
            P("client", "chan", None),
            P("client", "chan", None),
        ),
        out_specs=(
            P(),
            P(("client", "chan"), None, None),
            P(("client", "chan"), None, None),
            P(("client", "chan"), None, None),
            P("client", None, "chan", None),
            P("client", None, "chan", None),
            P("client", None, "chan", None),
            P("client", "chan", None),
            P("client", "chan", None),
            P("client", "chan", None),
        ),
        check_vma=False,
    )
```

```python
import functools

import jax
import jax.numpy as jnp
from jax import lax
from jax.experimental import pallas as pl
from jax.experimental.pallas import tpu as pltpu
from jax.sharding import PartitionSpec as P

NS_STEPS = 5
STEP = 10

low_type = jnp.bfloat16
wide = jnp.float32
MESH = pl.DeviceIdType.MESH
precise = lax.Precision.HIGHEST
norm_epsilon = 1e-05
prox_weight = 0.05
momentum_decay = 0.95
muon_rate = 0.3
muon_decay = 0.1
schulz_first = 3.4445
schulz_second = -4.775
schulz_third = 2.0315
adam_first = 0.9
adam_second = 0.95
adam_epsilon = 1e-08
head_rate = 0.01
head_decay = 0.05
norm_rate = 0.5

SIDE = 7
PIXELS = SIDE * SIDE
LANES = 128
SPOTS = (4, 2, 2)
VMEM_BYTES = 62 * 2**20


def dot_nn(left, right):
    return jnp.dot(left, right, preferred_element_type=wide)


def dot_nt(left, right):
    return lax.dot_general(left, right, (((1,), (1,)), ((), ())), preferred_element_type=wide)


def dot_tn(left, right):
    return lax.dot_general(left, right, (((0,), (0,)), ((), ())), preferred_element_type=wide)


def flat_rows(block):
    return block.reshape(-1, block.shape[-1])


def sigmoid(value):
    return 0.5 * jnp.tanh(0.5 * value) + 0.5


def fold_rows(value):
    return jnp.sum(value.reshape(value.shape[0] // 8, 8, value.shape[1]), axis=0)


def column_sum(value):
    return jnp.sum(value, axis=0, keepdims=True)


def remote(src, dst, send_sem, recv_sem, client, core):
    return pltpu.make_async_remote_copy(
        src_ref=src,
        dst_ref=dst,
        send_sem=send_sem,
        recv_sem=recv_sem,
        device_id=(client, core),
        device_id_type=MESH,
    )


class Place:
    def __init__(self):
        self.client = lax.axis_index("client")
        self.core = lax.axis_index("chan")
        self.z = self.client // 4
        self.y = (self.client // 2) % 2
        self.x = self.client % 2
        self.others = [
            self.z + 1 - 2 * (self.z % 2),
            (self.z + 2) % 4,
            3 - self.z,
        ]

    def at(self, z, y, x):
        return z * 4 + y * 2 + x

    def along_x(self):
        return self.at(self.z, self.y, 1 - self.x)

    def along_y(self):
        return self.at(self.z, 1 - self.y, self.x)

    def along_z(self, step):
        return self.at(self.others[step], self.y, self.x)

    def greet(self, whole):
        barrier = pltpu.get_barrier_semaphore()
        pairs = [(self.client, 1 - self.core)]
        if whole:
            pairs += [(self.along_x(), self.core), (self.along_y(), self.core)]
            pairs += [(self.along_z(step), self.core) for step in range(3)]
        for pair in pairs:
            pl.semaphore_signal(barrier, inc=1, device_id=pair, device_id_type=MESH)
        pl.semaphore_wait(barrier, len(pairs))


class Spread:
    def __init__(self, place, weights, sems):
        self.place = place
        self.weights = weights
        self.z_sems, self.near_sems, self.far_sems, self.core_sems = sems
        self.order = [place.z] + place.others
        self.copies = []

    def z_copy(self, step, slot):
        p = self.place
        ref = self.weights[slot].at[p.z, p.y, p.x, p.core]
        sems = self.z_sems
        return remote(ref, ref, sems.at[0, step, slot], sems.at[1, step, slot], p.along_z(step), p.core)

    def near_copy(self, turn, slot):
        p = self.place
        ref = self.weights[slot].at[self.order[turn], p.y, p.x, p.core]
        to = p.along_y() if slot == 1 else p.along_x()
        sems = self.near_sems
        return remote(ref, ref, sems.at[0, turn, slot], sems.at[1, turn, slot], to, p.core)

    def far_copy(self, turn, slot):
        p = self.place
        if slot == 1:
            ref, to = self.weights[slot].at[self.order[turn], :, p.x, p.core], p.along_x()
        else:
            ref, to = self.weights[slot].at[self.order[turn], p.y, :, p.core], p.along_y()
        sems = self.far_sems
        return remote(ref, ref, sems.at[0, turn, slot], sems.at[1, turn, slot], to, p.core)

    def core_copy(self, turn, slot):
        p = self.place
        ref = self.weights[slot].at[self.order[turn], :, :, p.core]
        sems = self.core_sems
        return remote(ref, ref, sems.at[0, turn, slot], sems.at[1, turn, slot], p.client, 1 - p.core)

    def launch(self, copy):
        copy.start()
        self.copies.append(copy)

    def begin(self, master):
        p = self.place
        start = 0
        for slot in range(3):
            rows = self.weights[slot].shape[-2]
            self.weights[slot][p.z, p.y, p.x, p.core] = master[start : start + rows, :].astype(low_type)
            start += rows
        for slot in range(3):
            self.launch(self.near_copy(0, slot))
            for step in range(3):
                self.launch(self.z_copy(step, slot))

    def steps(self):
        listed = []
        for turn in range(6):
            for slot in range(3):
                if 1 <= turn < 4:
                    listed.append(functools.partial(self.near_step, turn, slot))
                if 1 <= turn < 5:
                    listed.append(functools.partial(self.far_step, turn - 1, slot))
                if 2 <= turn:
                    listed.append(functools.partial(self.core_step, turn - 2, slot))
        return listed

    def near_step(self, turn, slot):
        self.z_copy(turn - 1, slot).wait_recv()
        self.launch(self.near_copy(turn, slot))

    def far_step(self, turn, slot):
        self.near_copy(turn, slot).wait_recv()
        self.launch(self.far_copy(turn, slot))

    def core_step(self, turn, slot):
        self.far_copy(turn, slot).wait_recv()
        self.launch(self.core_copy(turn, slot))

    def arrive(self, slot):
        for turn in range(4):
            self.core_copy(turn, slot).wait_recv()

    def drain(self):
        for copy in self.copies:
            copy.wait_send()


def norm_stats(mine, theirs, count):
    gap = mine[0:1] - theirs[0:1]
    mean = 0.5 * (mine[0:1] + theirs[0:1])
    spread = mine[1:2] + theirs[1:2] + gap * gap * (0.5 * count)
    return mean, lax.rsqrt(spread / (2.0 * count) + norm_epsilon)


def client_kernel(
    gather,
    images,
    classes,
    features,
    labels,
    flag,
    params,
    head,
    *rest,
):
    if gather:
        master, *rest = rest
    else:
        first_in, middle_in, last_in, *rest = rest
    (
        grad_first_out,
        grad_middle_out,
        grad_last_out,
        grad_norm_out,
        grad_head_out,
        loss_out,
        x_all,
        mid_wide,
        w_first,
        w_middle,
        w_last,
        act_one,
        act_two,
        act_three,
        taps_one,
        taps_two,
        hidden_two,
        stage,
        outgoing,
        params_all,
        head_all,
        pool_acc,
        slope_acc,
        slope_normed_acc,
        grad_pool,
        pool_send,
        pool_all,
        logit_grads,
        sums_mine,
        sums_theirs,
        shift,
        fwd_stats,
        sem_local,
        sem_swap,
        sem_misc,
        *gather_sems,
    ) = rest
    place = Place()
    core = place.core
    mate = (place.client, 1 - core)
    count_rows, channels = x_all.shape
    half = channels // 2
    width = act_one.shape[1]
    part = width // 2
    mine_images = images // 2
    line = SIDE * mine_images
    total_rows = 2.0 * count_rows

    def tile(index):
        return pl.ds(pl.multiple_of(index * line, line), line)

    def lanes(index, size):
        return pl.ds(pl.multiple_of(index * size, size), size)

    place.greet(gather)

    own_rows = pl.ds(pl.multiple_of(core * count_rows, count_rows), count_rows)
    mate_rows = pl.ds(pl.multiple_of((1 - core) * count_rows, count_rows), count_rows)
    copy_own = pltpu.make_async_copy(features.at[own_rows, :], mid_wide.at[core], sem_local.at[0])
    copy_own.start()
    to_mate = [
        remote(params, params_all.at[core], sem_misc.at[0, 0], sem_misc.at[1, 0], *mate),
        remote(head, head_all.at[core], sem_misc.at[0, 1], sem_misc.at[1, 1], *mate),
        remote(features.at[mate_rows, :], mid_wide.at[core], sem_misc.at[0, 2], sem_misc.at[1, 2], *mate),
    ]
    for copy in to_mate:
        copy.start()
    params_all[core] = params[...]
    head_all[core] = head[...]

    weights = (w_first, w_middle, w_last)
    if gather:
        spread = Spread(place, weights, gather_sems)
        spread.begin(master)
    else:
        loads = [
            pltpu.make_async_copy(src, dst, sem_local.at[1 + slot])
            for slot, (src, dst) in enumerate(zip((first_in, middle_in, last_in), weights))
        ]
        for load in loads:
            load.start()

    taps_one[...] = jnp.zeros_like(taps_one)
    taps_two[...] = jnp.zeros_like(taps_two)

    copy_own.wait()
    for copy in to_mate:
        copy.wait_recv()

    def turn(index, carry):
        per_half = half // LANES
        stage[...] = mid_wide[index // per_half, :, lanes(index % per_half, LANES)].astype(wide)

        def pixel(spot, inner):
            x_all[
                pl.ds(pl.multiple_of(spot * mine_images, mine_images), mine_images),
                lanes(index, LANES),
            ] = stage[pl.ds(spot, mine_images, stride=PIXELS), :].astype(low_type)
            return inner

        return lax.fori_loop(0, PIXELS, pixel, carry, unroll=7)

    chunks = channels // LANES
    if gather:
        steps = spread.steps()
        for spot, step in enumerate(steps):
            step()
            lower, upper = spot * chunks // len(steps), (spot + 1) * chunks // len(steps)
            if upper > lower:
                lax.fori_loop(lower, upper, turn, 0)
        for slot in range(3):
            spread.arrive(slot)
    else:
        lax.fori_loop(0, chunks, turn, 0)
        for load in loads:
            load.wait()

    def swap(slot, size):
        return remote(
            sums_mine.at[slot, :, pl.ds(0, size)],
            sums_theirs.at[slot, :, pl.ds(0, size)],
            sem_swap.at[0, slot],
            sem_swap.at[1, slot],
            *mate,
        )

    def gain_bias(lower, upper):
        rows = []
        for kind in range(2):
            pieces = [params_all[side, kind : kind + 1, lower:upper] for side in range(2)]
            rows.append(jnp.concatenate(pieces, axis=1))
        return rows

    def collect(index, value, columns, size):
        @pl.when(index == 0)
        def _():
            shift[0:1, pl.ds(0, size)] = column_sum(fold_rows(value)) / value.shape[0]
            shift[8:24, pl.ds(0, size)] = jnp.zeros((16, size), wide)

        gap = value - shift[0:1, pl.ds(0, size)]
        shift[8:16, pl.ds(0, size)] += fold_rows(gap)
        shift[16:24, pl.ds(0, size)] += fold_rows(gap * gap)

    def close_stats(slot, columns, size):
        sum_gap = column_sum(shift[8:16, pl.ds(0, size)])
        sum_square = column_sum(shift[16:24, pl.ds(0, size)])
        sums_mine[slot, 0:1, columns] = shift[0:1, pl.ds(0, size)] + sum_gap / count_rows
        sums_mine[slot, 1:2, columns] = sum_square - sum_gap * sum_gap / count_rows

    def settle(slot, size):
        mean, scale = norm_stats(
            sums_mine[slot, 0:2, pl.ds(0, size)], sums_theirs[slot, 0:2, pl.ds(0, size)], float(count_rows)
        )
        fwd_stats[slot, 0:1, pl.ds(0, size)] = mean
        fwd_stats[slot, 1:2, pl.ds(0, size)] = scale

    whole_width = pl.ds(0, width)

    def first_tile(index, carry):
        value = dot_nn(x_all[tile(index), :], flat_rows(w_first[...]))
        act_one[tile(index), :] = value
        collect(index, value, whole_width, width)
        return carry

    lax.fori_loop(0, SIDE, first_tile, 0)
    close_stats(0, whole_width, width)
    move = swap(0, width)
    move.start()
    move.wait()
    settle(0, width)

    gain_one, bias_one = gain_bias(0, part)
    gain_two, bias_two = gain_bias(part, width)
    gain_three, bias_three = gain_bias(width, width + half)

    def spread_taps(buffer, index, value):
        base = pl.multiple_of((index + 1) * line, line)
        step = mine_images
        buffer[pl.ds(base, line), width : 2 * width] = value
        buffer[pl.ds(pl.multiple_of(base + step, step), line - step), 0:width] = value[: line - step]
        buffer[pl.ds(base, line - step), 2 * width : 3 * width] = value[step:]

    def normal(act, slot, index):
        mean = fwd_stats[slot, 0:1, pl.ds(0, width)]
        return (act[tile(index), :] - mean) * fwd_stats[slot, 1:2, pl.ds(0, width)]

    def hide_one(index, carry):
        value = normal(act_one, 0, index) * gain_one + bias_one
        spread_taps(taps_one, index, (value * sigmoid(value)).astype(low_type))
        return carry

    lax.fori_loop(0, SIDE, hide_one, 0)

    def shifted(buffer, index, down):
        return buffer[pl.ds(pl.multiple_of((index + down) * line, line), line), :]

    def second_tile(index, carry):
        kernel = flat_rows(w_middle[...])
        value = dot_nn(shifted(taps_one, index, 0), kernel[0 : 3 * width])
        value += dot_nn(shifted(taps_one, index, 1), kernel[3 * width : 6 * width])
        value += dot_nn(shifted(taps_one, index, 2), kernel[6 * width :])
        act_two[tile(index), :] = value
        collect(index, value, whole_width, width)
        return carry

    lax.fori_loop(0, SIDE, second_tile, 0)
    close_stats(1, whole_width, width)
    move_two = swap(1, width)
    move_two.start()
    move_two.wait()
    settle(1, width)

    def hide_two(index, carry):
        value = normal(act_two, 1, index) * gain_two + bias_two
        hidden_two[tile(index), :] = (value * sigmoid(value)).astype(low_type)
        return carry

    lax.fori_loop(0, SIDE, hide_two, 0)

    groups = w_last.shape[0]
    group = channels // groups

    def third_group(which, carry):
        columns = lanes(which, group)

        def third_tile(index, inner):
            value = dot_nt(hidden_two[tile(index), :], flat_rows(w_last[which]))
            act_three[tile(index), columns] = value
            collect(index, value, columns, group)
            return inner

        lax.fori_loop(0, SIDE, third_tile, 0)
        close_stats(2, columns, group)
        return carry

    lax.fori_loop(0, groups, third_group, 0)
    move_three = swap(2, channels)
    move_three.start()
    move_three.wait()
    settle(2, channels)
    fwd_stats[2, 2:3, :] = gain_three
    fwd_stats[2, 3:4, :] = bias_three

    per_half = half // LANES

    def block_of(spot):
        return pl.ds(pl.multiple_of(spot * mine_images, mine_images), mine_images)

    def emit(index, carry):
        columns = lanes(index, LANES)
        mean, scale = fwd_stats[2, 0:1, columns], fwd_stats[2, 1:2, columns]
        gain, bias = fwd_stats[2, 2:3, columns], fwd_stats[2, 3:4, columns]

        def pixel(spot, sums):
            pooled, slopes, slopes_normed = sums
            normed = (act_three[block_of(spot), columns] - mean) * scale
            total = normed * gain + bias + x_all[block_of(spot), columns].astype(wide)
            sig = sigmoid(total)
            out = total * sig
            slope = sig + out * (1.0 - sig)
            mid_wide[index // per_half, block_of(spot), lanes(index % per_half, LANES)] = slope.astype(low_type)
            return pooled + out, slopes + slope, slopes_normed + slope * normed

        zero = jnp.zeros((mine_images, LANES), wide)
        pooled, slopes, slopes_normed = lax.fori_loop(0, PIXELS, pixel, (zero, zero, zero), unroll=7)
        pool_acc[:, columns] = pooled
        slope_acc[:, columns] = slopes
        slope_normed_acc[:, columns] = slopes_normed
        return carry

    lax.fori_loop(0, channels // LANES, emit, 0)

    pooled = (pool_acc[...] / PIXELS).astype(low_type)
    head_full = flat_rows(head_all[...])
    logits = dot_nn(pooled, head_full)
    spots = lax.broadcasted_iota(jnp.int32, logits.shape, 1)
    inside = spots < classes
    onehot = (spots == labels[pl.ds(pl.multiple_of(core * mine_images, mine_images), mine_images), :]).astype(wide)
    top = jnp.max(jnp.where(inside, logits, -jnp.inf), axis=1, keepdims=True)
    powers = jnp.where(inside, jnp.exp(logits - top), 0.0)
    power_sum = jnp.sum(powers, axis=1, keepdims=True)
    picked = jnp.sum(logits * onehot, axis=1, keepdims=True)
    each_loss = top + jnp.log(power_sum) - picked
    taking = flag[0].astype(wide)
    loss_out[...] = jnp.full(loss_out.shape, taking * jnp.sum(each_loss), wide)
    grads = (taking / images * (powers / power_sum - onehot)).astype(low_type)
    grad_pool[...] = dot_nt(grads, head_full) / PIXELS
    logit_grads[core] = grads
    pool_all[core] = pooled[:, 0:half]
    pool_send[...] = pooled[:, half:]

    @pl.when(core == 1)
    def _():
        pool_all[core] = pooled[:, half:]
        pool_send[...] = pooled[:, 0:half]

    head_moves = [
        remote(pool_send, pool_all.at[core], sem_misc.at[0, 3], sem_misc.at[1, 3], *mate),
        remote(logit_grads.at[core], logit_grads.at[core], sem_misc.at[0, 4], sem_misc.at[1, 4], *mate),
    ]

    sums_mine[3, 0:1, :] = column_sum(grad_pool[...] * slope_acc[...])
    sums_mine[3, 1:2, :] = column_sum(grad_pool[...] * slope_normed_acc[...])
    move_back = swap(3, channels)
    move_back.start()
    for copy in head_moves:
        copy.start()
    move_back.wait()

    def back_terms(slot, layer, size, gain):
        columns = pl.ds(0, size)
        sums = sums_mine[slot, 0:2, columns] + sums_theirs[slot, 0:2, columns]
        sums_mine[slot, 2:4, columns] = sums
        scale = fwd_stats[layer, 1:2, columns]
        return (
            scale * gain,
            scale * gain * sums[0:1] / total_rows,
            scale * scale * gain * sums[1:2] / total_rows,
        )

    first, second, third = back_terms(3, 2, channels, gain_three)
    fwd_stats[2, 4:5, :] = first
    fwd_stats[2, 5:6, :] = second
    fwd_stats[2, 6:7, :] = third

    def pull(index, carry):
        columns = lanes(index, LANES)
        mean = fwd_stats[2, 0:1, columns]
        first, second = fwd_stats[2, 4:5, columns], fwd_stats[2, 5:6, columns]
        third = fwd_stats[2, 6:7, columns]
        reach = grad_pool[:, columns] * first

        def pixel(spot, inner):
            where = (index // per_half, block_of(spot), lanes(index % per_half, LANES))
            slope = mid_wide[where].astype(wide)
            gap = act_three[block_of(spot), columns] - mean
            mid_wide[where] = (reach * slope - second - third * gap).astype(low_type)
            return inner

        return lax.fori_loop(0, PIXELS, pixel, carry, unroll=7)

    lax.fori_loop(0, channels // LANES, pull, 0)
    for copy in head_moves:
        copy.wait_recv()
    grad_head_out[...] = dot_tn(flat_rows(pool_all[...]), flat_rows(logit_grads[...]))

    def drop_into(index, value, act, slot, gain, bias, columns):
        normed = normal(act, slot, index)
        norm = normed * gain + bias
        sig = sigmoid(norm)
        grad = value * (sig + norm * sig * (1.0 - sig))
        act_three[tile(index), columns] = grad
        size = pl.ds(0, width)

        @pl.when(index == 0)
        def _():
            shift[8:24, size] = jnp.zeros((16, width), wide)

        shift[8:16, size] += fold_rows(grad)
        shift[16:24, size] += fold_rows(grad * normed)

    def close_back(slot):
        size = pl.ds(0, width)
        sums_mine[slot, 0:1, size] = column_sum(shift[8:16, size])
        sums_mine[slot, 1:2, size] = column_sum(shift[16:24, size])

    space_two, space_one = pl.ds(0, width), pl.ds(width, width)

    def back_two(index, carry):
        kernel = flat_rows(w_last[...])
        value = dot_nn(mid_wide[0, tile(index), :], kernel[:half])
        value += dot_nn(mid_wide[1, tile(index), :], kernel[half:])
        drop_into(index, value, act_two, 1, gain_two, bias_two, space_two)
        return carry

    lax.fori_loop(0, SIDE, back_two, 0)
    close_back(4)
    move_back_two = swap(4, width)
    move_back_two.start()

    def put(out, block, value):
        slot = block % 2
        rows = lanes(block, group)

        @pl.when(block >= 2)
        def _():
            pltpu.make_async_copy(outgoing.at[slot], out.at[rows, :], sem_local.at[4 + slot]).wait()

        outgoing[slot] = value.astype(low_type)
        pltpu.make_async_copy(outgoing.at[slot], out.at[rows, :], sem_local.at[4 + slot]).start()

    def drain(out, blocks):
        for block in (blocks - 2, blocks - 1):
            slot = block % 2
            pltpu.make_async_copy(
                outgoing.at[slot], out.at[pl.ds(block * group, group), :], sem_local.at[4 + slot]
            ).wait()

    per_side = half // group

    def expand_block(block, carry):
        left = mid_wide[block // per_side, :, lanes(block % per_side, group)]
        put(grad_last_out, block, dot_tn(left, hidden_two[...]))
        return carry

    lax.fori_loop(0, channels // group, expand_block, 0)
    drain(grad_last_out, channels // group)
    move_back_two.wait()
    terms_two = back_terms(4, 1, width, gain_two)

    def back_act(terms, act, layer, index, columns):
        first, second, third = terms
        gap = act[tile(index), :] - fwd_stats[layer, 0:1, pl.ds(0, width)]
        return (first * act_three[tile(index), columns] - second - third * gap).astype(low_type)

    def grad_two(index, carry):
        spread_taps(taps_two, index, back_act(terms_two, act_two, 1, index, space_two))
        return carry

    lax.fori_loop(0, SIDE, grad_two, 0)

    def back_one(index, carry):
        kernel = flat_rows(w_middle[...])
        value = jnp.zeros((line, width), wide)
        for down in range(3):
            rows = shifted(taps_two, index, 2 - down)
            for over in range(3):
                tap = 3 * down + over
                value += dot_nt(
                    rows[:, (2 - over) * width : (3 - over) * width],
                    kernel[tap * width : (tap + 1) * width],
                )
        drop_into(index, value, act_one, 0, gain_one, bias_one, space_one)
        return carry

    lax.fori_loop(0, SIDE, back_one, 0)
    close_back(5)
    move_back_one = swap(5, width)
    move_back_one.start()

    def middle_block(block, carry):
        rows = pl.ds(pl.multiple_of((block // 3) * line, line), count_rows)
        left = taps_one[rows, lanes(block % 3, width)]
        put(grad_middle_out, block, dot_tn(left, taps_two[line : line + count_rows, width : 2 * width]))
        return carry

    lax.fori_loop(0, 9, middle_block, 0)
    drain(grad_middle_out, 9)
    move_back_one.wait()
    terms_one = back_terms(5, 0, width, gain_one)

    def grad_one(index, carry):
        hidden_two[tile(index), :] = back_act(terms_one, act_one, 0, index, space_one)
        return carry

    lax.fori_loop(0, SIDE, grad_one, 0)

    def reduce_block(block, carry):
        put(grad_first_out, block, dot_tn(x_all[:, lanes(block, group)], hidden_two[...]))
        return carry

    lax.fori_loop(0, channels // group, reduce_block, 0)

    for kind in range(2):
        row = 3 - kind
        grad_norm_out[kind : kind + 1, 0:part] = sums_mine[5, row : row + 1, lanes(core, part)]
        grad_norm_out[kind : kind + 1, part:width] = sums_mine[4, row : row + 1, lanes(core, part)]
        grad_norm_out[kind : kind + 1, width:] = sums_mine[3, row : row + 1, lanes(core, half)]

    drain(grad_first_out, channels // group)
    for copy in to_mate + head_moves:
        copy.wait_send()
    if gather:
        spread.drain()


def client_pass(gather, classes, features, labels, flag, params, head_low, weights):
    pixels, half = features.shape
    images = labels.shape[0]
    count_rows, channels = pixels // 2, 2 * half
    width = params.shape[1] - half
    classes_wide = LANES
    mine_images = images // 2
    line = SIDE * mine_images
    middle = 9 * width
    blocks = 32
    group = channels // SPOTS[0]
    any_space = pl.BlockSpec(memory_space=pl.ANY)
    vmem = pl.BlockSpec(memory_space=pltpu.VMEM)
    smem = pl.BlockSpec(memory_space=pltpu.SMEM)
    spots = SPOTS + (2,)
    scratch = [
        pltpu.VMEM((count_rows, channels), low_type),
        pltpu.VMEM((2, count_rows, half), low_type),
        pltpu.VMEM(spots + (channels // blocks, width), low_type),
        pltpu.VMEM(spots + (middle // blocks, width), low_type),
        pltpu.VMEM(spots + (channels // blocks, width), low_type),
        pltpu.VMEM((count_rows, width), wide),
        pltpu.VMEM((count_rows, width), wide),
        pltpu.VMEM((count_rows, channels), wide),
        pltpu.VMEM((count_rows + 2 * line, 3 * width), low_type),
        pltpu.VMEM((count_rows + 2 * line, 3 * width), low_type),
        pltpu.VMEM((count_rows, width), low_type),
        pltpu.VMEM((count_rows, LANES), wide),
        pltpu.VMEM((2, group, width), low_type),
        pltpu.VMEM((2,) + params.shape, wide),
        pltpu.VMEM((2, half, classes_wide), low_type),
        pltpu.VMEM((mine_images, channels), wide),
        pltpu.VMEM((mine_images, channels), wide),
        pltpu.VMEM((mine_images, channels), wide),
        pltpu.VMEM((mine_images, channels), wide),
        pltpu.VMEM((mine_images, half), low_type),
        pltpu.VMEM((2, mine_images, half), low_type),
        pltpu.VMEM((2, mine_images, classes_wide), low_type),
        pltpu.VMEM((6, 8, channels), wide),
        pltpu.VMEM((6, 8, channels), wide),
        pltpu.VMEM((24, max(width, group)), wide),
        pltpu.VMEM((3, 8, channels), wide),
        pltpu.SemaphoreType.DMA((6,)),
        pltpu.SemaphoreType.DMA((2, 6)),
        pltpu.SemaphoreType.DMA((2, 5)),
    ]
    if gather:
        scratch += [pltpu.SemaphoreType.DMA((2, 3, 3))]
        scratch += [pltpu.SemaphoreType.DMA((2, 4, 3)) for _ in range(3)]
    return pl.pallas_call(
        functools.partial(client_kernel, gather, images, classes),
        out_shape=(
            jax.ShapeDtypeStruct((channels, width), low_type),
            jax.ShapeDtypeStruct((middle, width), low_type),
            jax.ShapeDtypeStruct((channels, width), low_type),
            jax.ShapeDtypeStruct(params.shape, wide),
            jax.ShapeDtypeStruct((half, classes_wide), wide),
            jax.ShapeDtypeStruct((8, LANES), wide),
        ),
        in_specs=[any_space, vmem, smem, vmem, vmem] + ([vmem] if gather else [any_space] * 3),
        out_specs=(any_space, any_space, any_space, vmem, vmem, vmem),
        scratch_shapes=scratch,
        compiler_params=pltpu.CompilerParams(
            collective_id=0, has_side_effects=True, vmem_limit_bytes=VMEM_BYTES
        ),
    )(features, labels, flag, params, head_low, *weights)


def adam_update(param, grad, first, second, rate, decay):
    first = adam_first * first + (1.0 - adam_first) * grad
    second = adam_second * second + (1.0 - adam_second) * grad * grad
    first_hat = first / (1.0 - adam_first**STEP)
    second_hat = second / (1.0 - adam_second**STEP)
    return (
        param - rate * (first_hat / (jnp.sqrt(second_hat) + adam_epsilon) + decay * param),
        first,
        second,
    )


def gram_of(section):
    return lax.dot_general(section, section, (((0,), (0,)), ((), ())), precision=precise)


def square(gram):
    return jnp.dot(gram, gram, precision=precise)


def times_poly(left, mixed):
    return schulz_first * left + jnp.dot(left, mixed, precision=precise)


def schulz(sections):
    raw_grams = lax.psum(tuple(gram_of(section) for section in sections), ("client", "chan"))
    factors = [1.0 / (jnp.sqrt(jnp.trace(gram)) + 1e-07) for gram in raw_grams]
    current = [section * factor for section, factor in zip(sections, factors)]
    grams = [gram * (factor * factor) for gram, factor in zip(raw_grams, factors)]
    for turn in range(NS_STEPS):
        mixed = [schulz_second * gram + schulz_third * square(gram) for gram in grams]
        current = [times_poly(current[slot], mixed[slot]) for slot in range(3)]
        if turn + 1 < NS_STEPS:
            grams = [
                times_poly(times_poly(grams[slot], mixed[slot]), mixed[slot]) for slot in range(3)
            ]
    return current


def on_device(
    features,
    labels,
    mask,
    base_master,
    base_momentum,
    global_base,
    norm_params,
    norm_first,
    norm_second,
    head,
    head_first,
    head_second,
):
    halves = lax.axis_size("chan")
    blocks = lax.axis_size("client") * halves
    half = features.shape[2]
    width = base_master.shape[2]
    channels = half * halves
    images = labels.shape[1]
    classes = head.shape[2]
    rows_first = channels // blocks
    rows_mid = 9 * width // blocks
    bounds = (0, rows_first, rows_first + rows_mid, base_master.shape[1])
    master = base_master[0]
    head_low = jnp.pad(head[0].astype(low_type), ((0, 0), (0, LANES - classes)))
    low_master = master.astype(low_type)
    weights = [
        lax.all_gather(low_master[bounds[slot] : bounds[slot + 1]], ("client", "chan"), axis=0, tiled=True)
        for slot in range(3)
    ]
    weights = [weight.reshape(SPOTS + (2, weight.shape[0] // 32, width)) for weight in weights]
    grad_first, grad_middle, grad_last, grad_norm, grad_head, loss_tile = client_pass(
        False, classes, features[0], labels.reshape(images, 1), mask, norm_params[0, :, 0, :], head_low, weights
    )
    loss_sum, count = lax.psum(
        (loss_tile[0, 0], mask[0].astype(wide) * (images / halves)), ("client", "chan")
    )
    loss = jnp.stack([loss_sum, count])
    sums = [
        lax.psum_scatter(grad.astype(wide), ("client", "chan"), scatter_dimension=0, tiled=True)
        for grad in (grad_first, grad_middle, grad_last)
    ]
    grad_base = jnp.concatenate(sums, axis=0) + prox_weight * (master - global_base[0])
    momentum_new = momentum_decay * base_momentum[0] + grad_base
    current = schulz([momentum_new[bounds[slot] : bounds[slot + 1]] for slot in range(3)])
    ratio = (channels / width) ** 0.5
    ortho = jnp.concatenate([current[0] * ratio, current[1] * 3.0, current[2] * ratio], axis=0)
    base_new = master - muon_rate * (ortho + muon_decay * master)
    norm_new, norm_first_new, norm_second_new = adam_update(
        norm_params, grad_norm[None, :, None, :], norm_first, norm_second, norm_rate, 0.0
    )
    head_new, head_first_new, head_second_new = adam_update(
        head, grad_head[None, :, :classes], head_first, head_second, head_rate, head_decay
    )
    return (
        loss,
        base_new[None],
        momentum_new[None],
        base_new.astype(low_type)[None],
        norm_new,
        norm_first_new,
        norm_second_new,
        head_new,
        head_first_new,
        head_second_new,
    )


def solution(mesh):
    wide_block = P(("client", "chan"), None, None)
    norm_block = P("client", None, "chan", None)
    head_block = P("client", "chan", None)
    return jax.shard_map(
        on_device,
        mesh=mesh,
        in_specs=(P("client", None, "chan"), P("client", None), P("client"))
        + (wide_block,) * 3
        + (norm_block,) * 3
        + (head_block,) * 3,
        out_specs=(P(),) + (wide_block,) * 3 + (norm_block,) * 3 + (head_block,) * 3,
        check_vma=False,
    )
```

```python
import functools

import jax
import jax.numpy as jnp
from jax import lax
from jax.experimental import pallas as pl
from jax.experimental.pallas import tpu as pltpu
from jax.sharding import PartitionSpec as P

NS_STEPS = 5
STEP = 10

low_type = jnp.bfloat16
wide = jnp.float32
MESH = pl.DeviceIdType.MESH
precise = lax.Precision.HIGHEST
norm_epsilon = 1e-05
prox_weight = 0.05
momentum_decay = 0.95
muon_rate = 0.3
muon_decay = 0.1
schulz_first = 3.4445
schulz_second = -4.775
schulz_third = 2.0315
adam_first = 0.9
adam_second = 0.95
adam_epsilon = 1e-08
head_rate = 0.01
head_decay = 0.05
norm_rate = 0.5

SIDE = 7
PIXELS = SIDE * SIDE
LANES = 128
SPOTS = (4, 2, 2)
VMEM_BYTES = 62 * 2**20


def dot_nn(left, right):
    return jnp.dot(left, right, preferred_element_type=wide)


def dot_nt(left, right):
    return lax.dot_general(left, right, (((1,), (1,)), ((), ())), preferred_element_type=wide)


def dot_tn(left, right):
    return lax.dot_general(left, right, (((0,), (0,)), ((), ())), preferred_element_type=wide)


def flat_rows(block):
    return block.reshape(-1, block.shape[-1])


def sigmoid(value):
    return 0.5 * jnp.tanh(0.5 * value) + 0.5


def fold_rows(value):
    return jnp.sum(value.reshape(value.shape[0] // 8, 8, value.shape[1]), axis=0)


def column_sum(value):
    return jnp.sum(value, axis=0, keepdims=True)


def remote(src, dst, send_sem, recv_sem, client, core):
    return pltpu.make_async_remote_copy(
        src_ref=src,
        dst_ref=dst,
        send_sem=send_sem,
        recv_sem=recv_sem,
        device_id=(client, core),
        device_id_type=MESH,
    )


class Place:
    def __init__(self):
        self.client = lax.axis_index("client")
        self.core = lax.axis_index("chan")
        self.z = self.client // 4
        self.y = (self.client // 2) % 2
        self.x = self.client % 2
        self.others = [
            self.z + 1 - 2 * (self.z % 2),
            (self.z + 2) % 4,
            3 - self.z,
        ]

    def at(self, z, y, x):
        return z * 4 + y * 2 + x

    def along_x(self):
        return self.at(self.z, self.y, 1 - self.x)

    def along_y(self):
        return self.at(self.z, 1 - self.y, self.x)

    def along_z(self, step):
        return self.at(self.others[step], self.y, self.x)

    def greet(self, whole):
        barrier = pltpu.get_barrier_semaphore()
        pairs = [(self.client, 1 - self.core)]
        if whole:
            pairs += [(self.along_x(), self.core), (self.along_y(), self.core)]
            pairs += [(self.along_z(step), self.core) for step in range(3)]
        for pair in pairs:
            pl.semaphore_signal(barrier, inc=1, device_id=pair, device_id_type=MESH)
        pl.semaphore_wait(barrier, len(pairs))


class Spread:
    def __init__(self, place, weights, sems):
        self.place = place
        self.weights = weights
        self.z_sems, self.near_sems, self.far_sems, self.core_sems = sems
        self.order = [place.z] + place.others
        self.copies = []

    def z_copy(self, step, slot):
        p = self.place
        ref = self.weights[slot].at[p.z, p.y, p.x, p.core]
        sems = self.z_sems
        return remote(ref, ref, sems.at[0, step, slot], sems.at[1, step, slot], p.along_z(step), p.core)

    def near_copy(self, turn, slot):
        p = self.place
        ref = self.weights[slot].at[self.order[turn], p.y, p.x, p.core]
        to = p.along_y() if slot == 1 else p.along_x()
        sems = self.near_sems
        return remote(ref, ref, sems.at[0, turn, slot], sems.at[1, turn, slot], to, p.core)

    def far_copy(self, turn, slot):
        p = self.place
        if slot == 1:
            ref, to = self.weights[slot].at[self.order[turn], :, p.x, p.core], p.along_x()
        else:
            ref, to = self.weights[slot].at[self.order[turn], p.y, :, p.core], p.along_y()
        sems = self.far_sems
        return remote(ref, ref, sems.at[0, turn, slot], sems.at[1, turn, slot], to, p.core)

    def core_copy(self, turn, slot):
        p = self.place
        ref = self.weights[slot].at[self.order[turn], :, :, p.core]
        sems = self.core_sems
        return remote(ref, ref, sems.at[0, turn, slot], sems.at[1, turn, slot], p.client, 1 - p.core)

    def launch(self, copy):
        copy.start()
        self.copies.append(copy)

    def begin(self, master):
        p = self.place
        start = 0
        for slot in range(3):
            rows = self.weights[slot].shape[-2]
            self.weights[slot][p.z, p.y, p.x, p.core] = master[start : start + rows, :].astype(low_type)
            start += rows
        for slot in range(3):
            self.launch(self.near_copy(0, slot))
            for step in range(3):
                self.launch(self.z_copy(step, slot))

    def steps(self):
        listed = []
        for turn in range(6):
            for slot in range(3):
                if 1 <= turn < 4:
                    listed.append(functools.partial(self.near_step, turn, slot))
                if 1 <= turn < 5:
                    listed.append(functools.partial(self.far_step, turn - 1, slot))
                if 2 <= turn:
                    listed.append(functools.partial(self.core_step, turn - 2, slot))
        return listed

    def near_step(self, turn, slot):
        self.z_copy(turn - 1, slot).wait_recv()
        self.launch(self.near_copy(turn, slot))

    def far_step(self, turn, slot):
        self.near_copy(turn, slot).wait_recv()
        self.launch(self.far_copy(turn, slot))

    def core_step(self, turn, slot):
        self.far_copy(turn, slot).wait_recv()
        self.launch(self.core_copy(turn, slot))

    def arrive(self, slot):
        for turn in range(4):
            self.core_copy(turn, slot).wait_recv()

    def drain(self):
        for copy in self.copies:
            copy.wait_send()


def norm_stats(mine, theirs, count):
    gap = mine[0:1] - theirs[0:1]
    mean = 0.5 * (mine[0:1] + theirs[0:1])
    spread = mine[1:2] + theirs[1:2] + gap * gap * (0.5 * count)
    return mean, lax.rsqrt(spread / (2.0 * count) + norm_epsilon)


def client_kernel(
    gather,
    images,
    classes,
    features,
    labels,
    flag,
    params,
    head,
    *rest,
):
    if gather:
        master, *rest = rest
    else:
        first_in, middle_in, last_in, *rest = rest
    (
        grad_first_out,
        grad_middle_out,
        grad_last_out,
        grad_norm_out,
        grad_head_out,
        loss_out,
        x_all,
        mid_wide,
        w_first,
        w_middle,
        w_last,
        act_one,
        act_two,
        act_three,
        taps_one,
        taps_two,
        hidden_two,
        stage,
        outgoing,
        params_all,
        head_all,
        pool_acc,
        slope_acc,
        slope_normed_acc,
        grad_pool,
        pool_send,
        pool_all,
        logit_grads,
        sums_mine,
        sums_theirs,
        shift,
        fwd_stats,
        sem_local,
        sem_swap,
        sem_misc,
        *gather_sems,
    ) = rest
    place = Place()
    core = place.core
    mate = (place.client, 1 - core)
    count_rows, channels = x_all.shape
    half = channels // 2
    width = act_one.shape[1]
    part = width // 2
    mine_images = images // 2
    line = SIDE * mine_images
    total_rows = 2.0 * count_rows

    def tile(index):
        return pl.ds(pl.multiple_of(index * line, line), line)

    def lanes(index, size):
        return pl.ds(pl.multiple_of(index * size, size), size)

    place.greet(gather)

    own_rows = pl.ds(pl.multiple_of(core * count_rows, count_rows), count_rows)
    mate_rows = pl.ds(pl.multiple_of((1 - core) * count_rows, count_rows), count_rows)
    copy_own = pltpu.make_async_copy(features.at[own_rows, :], mid_wide.at[core], sem_local.at[0])
    copy_own.start()
    to_mate = [
        remote(params, params_all.at[core], sem_misc.at[0, 0], sem_misc.at[1, 0], *mate),
        remote(head, head_all.at[core], sem_misc.at[0, 1], sem_misc.at[1, 1], *mate),
        remote(features.at[mate_rows, :], mid_wide.at[core], sem_misc.at[0, 2], sem_misc.at[1, 2], *mate),
    ]
    for copy in to_mate:
        copy.start()
    params_all[core] = params[...]
    head_all[core] = head[...]

    weights = (w_first, w_middle, w_last)
    if gather:
        spread = Spread(place, weights, gather_sems)
        spread.begin(master)
    else:
        loads = [
            pltpu.make_async_copy(src, dst, sem_local.at[1 + slot])
            for slot, (src, dst) in enumerate(zip((first_in, middle_in, last_in), weights))
        ]
        for load in loads:
            load.start()

    taps_one[...] = jnp.zeros_like(taps_one)
    taps_two[...] = jnp.zeros_like(taps_two)

    copy_own.wait()
    for copy in to_mate:
        copy.wait_recv()

    def turn(index, carry):
        per_half = half // LANES
        stage[...] = mid_wide[index // per_half, :, lanes(index % per_half, LANES)].astype(wide)

        def pixel(spot, inner):
            x_all[
                pl.ds(pl.multiple_of(spot * mine_images, mine_images), mine_images),
                lanes(index, LANES),
            ] = stage[pl.ds(spot, mine_images, stride=PIXELS), :].astype(low_type)
            return inner

        return lax.fori_loop(0, PIXELS, pixel, carry, unroll=7)

    chunks = channels // LANES
    if gather:
        steps = spread.steps()
        for spot, step in enumerate(steps):
            step()
            lower, upper = spot * chunks // len(steps), (spot + 1) * chunks // len(steps)
            if upper > lower:
                lax.fori_loop(lower, upper, turn, 0)
        for slot in range(3):
            spread.arrive(slot)
    else:
        lax.fori_loop(0, chunks, turn, 0)
        for load in loads:
            load.wait()

    def swap(slot, size):
        return remote(
            sums_mine.at[slot, :, pl.ds(0, size)],
            sums_theirs.at[slot, :, pl.ds(0, size)],
            sem_swap.at[0, slot],
            sem_swap.at[1, slot],
            *mate,
        )

    def gain_bias(lower, upper):
        rows = []
        for kind in range(2):
            pieces = [params_all[side, kind : kind + 1, lower:upper] for side in range(2)]
            rows.append(jnp.concatenate(pieces, axis=1))
        return rows

    def collect(index, value, columns, size):
        @pl.when(index == 0)
        def _():
            shift[0:1, pl.ds(0, size)] = column_sum(fold_rows(value)) / value.shape[0]
            shift[8:24, pl.ds(0, size)] = jnp.zeros((16, size), wide)

        gap = value - shift[0:1, pl.ds(0, size)]
        shift[8:16, pl.ds(0, size)] += fold_rows(gap)
        shift[16:24, pl.ds(0, size)] += fold_rows(gap * gap)

    def close_stats(slot, columns, size):
        sum_gap = column_sum(shift[8:16, pl.ds(0, size)])
        sum_square = column_sum(shift[16:24, pl.ds(0, size)])
        sums_mine[slot, 0:1, columns] = shift[0:1, pl.ds(0, size)] + sum_gap / count_rows
        sums_mine[slot, 1:2, columns] = sum_square - sum_gap * sum_gap / count_rows

    def settle(slot, size):
        mean, scale = norm_stats(
            sums_mine[slot, 0:2, pl.ds(0, size)], sums_theirs[slot, 0:2, pl.ds(0, size)], float(count_rows)
        )
        fwd_stats[slot, 0:1, pl.ds(0, size)] = mean
        fwd_stats[slot, 1:2, pl.ds(0, size)] = scale

    whole_width = pl.ds(0, width)

    def first_tile(index, carry):
        value = dot_nn(x_all[tile(index), :], flat_rows(w_first[...]))
        act_one[tile(index), :] = value
        collect(index, value, whole_width, width)
        return carry

    lax.fori_loop(0, SIDE, first_tile, 0)
    close_stats(0, whole_width, width)
    move = swap(0, width)
    move.start()
    move.wait()
    settle(0, width)

    gain_one, bias_one = gain_bias(0, part)
    gain_two, bias_two = gain_bias(part, width)
    gain_three, bias_three = gain_bias(width, width + half)

    def spread_taps(buffer, index, value):
        base = pl.multiple_of((index + 1) * line, line)
        step = mine_images
        buffer[pl.ds(base, line), width : 2 * width] = value
        buffer[pl.ds(pl.multiple_of(base + step, step), line - step), 0:width] = value[: line - step]
        buffer[pl.ds(base, line - step), 2 * width : 3 * width] = value[step:]

    def normal(act, slot, index):
        mean = fwd_stats[slot, 0:1, pl.ds(0, width)]
        return (act[tile(index), :] - mean) * fwd_stats[slot, 1:2, pl.ds(0, width)]

    def hide_one(index, carry):
        value = normal(act_one, 0, index) * gain_one + bias_one
        spread_taps(taps_one, index, (value * sigmoid(value)).astype(low_type))
        return carry

    lax.fori_loop(0, SIDE, hide_one, 0)

    def shifted(buffer, index, down):
        return buffer[pl.ds(pl.multiple_of((index + down) * line, line), line), :]

    def second_tile(index, carry):
        kernel = flat_rows(w_middle[...])
        value = dot_nn(shifted(taps_one, index, 0), kernel[0 : 3 * width])
        value += dot_nn(shifted(taps_one, index, 1), kernel[3 * width : 6 * width])
        value += dot_nn(shifted(taps_one, index, 2), kernel[6 * width :])
        act_two[tile(index), :] = value
        collect(index, value, whole_width, width)
        return carry

    lax.fori_loop(0, SIDE, second_tile, 0)
    close_stats(1, whole_width, width)
    move_two = swap(1, width)
    move_two.start()
    move_two.wait()
    settle(1, width)

    def hide_two(index, carry):
        value = normal(act_two, 1, index) * gain_two + bias_two
        hidden_two[tile(index), :] = (value * sigmoid(value)).astype(low_type)
        return carry

    lax.fori_loop(0, SIDE, hide_two, 0)

    groups = w_last.shape[0]
    group = channels // groups

    def third_group(which, carry):
        columns = lanes(which, group)

        def third_tile(index, inner):
            value = dot_nt(hidden_two[tile(index), :], flat_rows(w_last[which]))
            act_three[tile(index), columns] = value
            collect(index, value, columns, group)
            return inner

        lax.fori_loop(0, SIDE, third_tile, 0)
        close_stats(2, columns, group)
        return carry

    lax.fori_loop(0, groups, third_group, 0)
    move_three = swap(2, channels)
    move_three.start()
    move_three.wait()
    settle(2, channels)
    fwd_stats[2, 2:3, :] = gain_three
    fwd_stats[2, 3:4, :] = bias_three

    per_half = half // LANES

    def block_of(spot):
        return pl.ds(pl.multiple_of(spot * mine_images, mine_images), mine_images)

    def emit(index, carry):
        columns = lanes(index, LANES)
        mean, scale = fwd_stats[2, 0:1, columns], fwd_stats[2, 1:2, columns]
        gain, bias = fwd_stats[2, 2:3, columns], fwd_stats[2, 3:4, columns]

        def pixel(spot, sums):
            pooled, slopes, slopes_normed = sums
            normed = (act_three[block_of(spot), columns] - mean) * scale
            total = normed * gain + bias + x_all[block_of(spot), columns].astype(wide)
            sig = sigmoid(total)
            out = total * sig
            slope = sig + out * (1.0 - sig)
            mid_wide[index // per_half, block_of(spot), lanes(index % per_half, LANES)] = slope.astype(low_type)
            return pooled + out, slopes + slope, slopes_normed + slope * normed

        zero = jnp.zeros((mine_images, LANES), wide)
        pooled, slopes, slopes_normed = lax.fori_loop(0, PIXELS, pixel, (zero, zero, zero), unroll=7)
        pool_acc[:, columns] = pooled
        slope_acc[:, columns] = slopes
        slope_normed_acc[:, columns] = slopes_normed
        return carry

    lax.fori_loop(0, channels // LANES, emit, 0)

    pooled = (pool_acc[...] / PIXELS).astype(low_type)
    head_full = flat_rows(head_all[...])
    logits = dot_nn(pooled, head_full)
    spots = lax.broadcasted_iota(jnp.int32, logits.shape, 1)
    inside = spots < classes
    onehot = (spots == labels[pl.ds(pl.multiple_of(core * mine_images, mine_images), mine_images), :]).astype(wide)
    top = jnp.max(jnp.where(inside, logits, -jnp.inf), axis=1, keepdims=True)
    powers = jnp.where(inside, jnp.exp(logits - top), 0.0)
    power_sum = jnp.sum(powers, axis=1, keepdims=True)
    picked = jnp.sum(logits * onehot, axis=1, keepdims=True)
    each_loss = top + jnp.log(power_sum) - picked
    taking = flag[0].astype(wide)
    tile_spots = lax.broadcasted_iota(jnp.int32, loss_out.shape, 1)
    loss_out[...] = jnp.where(tile_spots == 0, taking * jnp.sum(each_loss), taking * mine_images)
    grads = (taking / images * (powers / power_sum - onehot)).astype(low_type)
    grad_pool[...] = dot_nt(grads, head_full) / PIXELS
    logit_grads[core] = grads
    pool_all[core] = pooled[:, 0:half]
    pool_send[...] = pooled[:, half:]

    @pl.when(core == 1)
    def _():
        pool_all[core] = pooled[:, half:]
        pool_send[...] = pooled[:, 0:half]

    head_moves = [
        remote(pool_send, pool_all.at[core], sem_misc.at[0, 3], sem_misc.at[1, 3], *mate),
        remote(logit_grads.at[core], logit_grads.at[core], sem_misc.at[0, 4], sem_misc.at[1, 4], *mate),
    ]

    sums_mine[3, 0:1, :] = column_sum(grad_pool[...] * slope_acc[...])
    sums_mine[3, 1:2, :] = column_sum(grad_pool[...] * slope_normed_acc[...])
    move_back = swap(3, channels)
    move_back.start()
    for copy in head_moves:
        copy.start()
    move_back.wait()

    def back_terms(slot, layer, size, gain):
        columns = pl.ds(0, size)
        sums = sums_mine[slot, 0:2, columns] + sums_theirs[slot, 0:2, columns]
        sums_mine[slot, 2:4, columns] = sums
        scale = fwd_stats[layer, 1:2, columns]
        return (
            scale * gain,
            scale * gain * sums[0:1] / total_rows,
            scale * scale * gain * sums[1:2] / total_rows,
        )

    first, second, third = back_terms(3, 2, channels, gain_three)
    fwd_stats[2, 4:5, :] = first
    fwd_stats[2, 5:6, :] = second
    fwd_stats[2, 6:7, :] = third

    def pull(index, carry):
        columns = lanes(index, LANES)
        mean = fwd_stats[2, 0:1, columns]
        first, second = fwd_stats[2, 4:5, columns], fwd_stats[2, 5:6, columns]
        third = fwd_stats[2, 6:7, columns]
        reach = grad_pool[:, columns] * first

        def pixel(spot, inner):
            where = (index // per_half, block_of(spot), lanes(index % per_half, LANES))
            slope = mid_wide[where].astype(wide)
            gap = act_three[block_of(spot), columns] - mean
            mid_wide[where] = (reach * slope - second - third * gap).astype(low_type)
            return inner

        return lax.fori_loop(0, PIXELS, pixel, carry, unroll=7)

    lax.fori_loop(0, channels // LANES, pull, 0)
    for copy in head_moves:
        copy.wait_recv()
    grad_head_out[...] = dot_tn(flat_rows(pool_all[...]), flat_rows(logit_grads[...]))

    def drop_into(index, value, act, slot, gain, bias, columns):
        normed = normal(act, slot, index)
        norm = normed * gain + bias
        sig = sigmoid(norm)
        grad = value * (sig + norm * sig * (1.0 - sig))
        act_three[tile(index), columns] = grad
        size = pl.ds(0, width)

        @pl.when(index == 0)
        def _():
            shift[8:24, size] = jnp.zeros((16, width), wide)

        shift[8:16, size] += fold_rows(grad)
        shift[16:24, size] += fold_rows(grad * normed)

    def close_back(slot):
        size = pl.ds(0, width)
        sums_mine[slot, 0:1, size] = column_sum(shift[8:16, size])
        sums_mine[slot, 1:2, size] = column_sum(shift[16:24, size])

    space_two, space_one = pl.ds(0, width), pl.ds(width, width)

    def back_two(index, carry):
        kernel = flat_rows(w_last[...])
        value = dot_nn(mid_wide[0, tile(index), :], kernel[:half])
        value += dot_nn(mid_wide[1, tile(index), :], kernel[half:])
        drop_into(index, value, act_two, 1, gain_two, bias_two, space_two)
        return carry

    lax.fori_loop(0, SIDE, back_two, 0)
    close_back(4)
    move_back_two = swap(4, width)
    move_back_two.start()

    def put(out, block, value):
        slot = block % 2
        rows = lanes(block, group)

        @pl.when(block >= 2)
        def _():
            pltpu.make_async_copy(outgoing.at[slot], out.at[rows, :], sem_local.at[4 + slot]).wait()

        outgoing[slot] = value.astype(low_type)
        pltpu.make_async_copy(outgoing.at[slot], out.at[rows, :], sem_local.at[4 + slot]).start()

    def drain(out, blocks):
        for block in (blocks - 2, blocks - 1):
            slot = block % 2
            pltpu.make_async_copy(
                outgoing.at[slot], out.at[pl.ds(block * group, group), :], sem_local.at[4 + slot]
            ).wait()

    per_side = half // group

    def expand_block(block, carry):
        left = mid_wide[block // per_side, :, lanes(block % per_side, group)]
        put(grad_last_out, block, dot_tn(left, hidden_two[...]))
        return carry

    lax.fori_loop(0, channels // group, expand_block, 0)
    drain(grad_last_out, channels // group)
    move_back_two.wait()
    terms_two = back_terms(4, 1, width, gain_two)

    def back_act(terms, act, layer, index, columns):
        first, second, third = terms
        gap = act[tile(index), :] - fwd_stats[layer, 0:1, pl.ds(0, width)]
        return (first * act_three[tile(index), columns] - second - third * gap).astype(low_type)

    def grad_two(index, carry):
        spread_taps(taps_two, index, back_act(terms_two, act_two, 1, index, space_two))
        return carry

    lax.fori_loop(0, SIDE, grad_two, 0)

    def back_one(index, carry):
        kernel = flat_rows(w_middle[...])
        value = jnp.zeros((line, width), wide)
        for down in range(3):
            rows = shifted(taps_two, index, 2 - down)
            for over in range(3):
                tap = 3 * down + over
                value += dot_nt(
                    rows[:, (2 - over) * width : (3 - over) * width],
                    kernel[tap * width : (tap + 1) * width],
                )
        drop_into(index, value, act_one, 0, gain_one, bias_one, space_one)
        return carry

    lax.fori_loop(0, SIDE, back_one, 0)
    close_back(5)
    move_back_one = swap(5, width)
    move_back_one.start()

    def middle_block(block, carry):
        rows = pl.ds(pl.multiple_of((block // 3) * line, line), count_rows)
        left = taps_one[rows, lanes(block % 3, width)]
        put(grad_middle_out, block, dot_tn(left, taps_two[line : line + count_rows, width : 2 * width]))
        return carry

    lax.fori_loop(0, 9, middle_block, 0)
    drain(grad_middle_out, 9)
    move_back_one.wait()
    terms_one = back_terms(5, 0, width, gain_one)

    def grad_one(index, carry):
        hidden_two[tile(index), :] = back_act(terms_one, act_one, 0, index, space_one)
        return carry

    lax.fori_loop(0, SIDE, grad_one, 0)

    def reduce_block(block, carry):
        put(grad_first_out, block, dot_tn(x_all[:, lanes(block, group)], hidden_two[...]))
        return carry

    lax.fori_loop(0, channels // group, reduce_block, 0)

    for kind in range(2):
        row = 3 - kind
        grad_norm_out[kind : kind + 1, 0:part] = sums_mine[5, row : row + 1, lanes(core, part)]
        grad_norm_out[kind : kind + 1, part:width] = sums_mine[4, row : row + 1, lanes(core, part)]
        grad_norm_out[kind : kind + 1, width:] = sums_mine[3, row : row + 1, lanes(core, half)]

    drain(grad_first_out, channels // group)
    for copy in to_mate + head_moves:
        copy.wait_send()
    if gather:
        spread.drain()


def client_pass(gather, classes, features, labels, flag, params, head_low, weights):
    pixels, half = features.shape
    images = labels.shape[0]
    count_rows, channels = pixels // 2, 2 * half
    width = params.shape[1] - half
    classes_wide = LANES
    mine_images = images // 2
    line = SIDE * mine_images
    middle = 9 * width
    blocks = 32
    group = channels // SPOTS[0]
    any_space = pl.BlockSpec(memory_space=pl.ANY)
    vmem = pl.BlockSpec(memory_space=pltpu.VMEM)
    smem = pl.BlockSpec(memory_space=pltpu.SMEM)
    spots = SPOTS + (2,)
    scratch = [
        pltpu.VMEM((count_rows, channels), low_type),
        pltpu.VMEM((2, count_rows, half), low_type),
        pltpu.VMEM(spots + (channels // blocks, width), low_type),
        pltpu.VMEM(spots + (middle // blocks, width), low_type),
        pltpu.VMEM(spots + (channels // blocks, width), low_type),
        pltpu.VMEM((count_rows, width), wide),
        pltpu.VMEM((count_rows, width), wide),
        pltpu.VMEM((count_rows, channels), wide),
        pltpu.VMEM((count_rows + 2 * line, 3 * width), low_type),
        pltpu.VMEM((count_rows + 2 * line, 3 * width), low_type),
        pltpu.VMEM((count_rows, width), low_type),
        pltpu.VMEM((count_rows, LANES), wide),
        pltpu.VMEM((2, group, width), low_type),
        pltpu.VMEM((2,) + params.shape, wide),
        pltpu.VMEM((2, half, classes_wide), low_type),
        pltpu.VMEM((mine_images, channels), wide),
        pltpu.VMEM((mine_images, channels), wide),
        pltpu.VMEM((mine_images, channels), wide),
        pltpu.VMEM((mine_images, channels), wide),
        pltpu.VMEM((mine_images, half), low_type),
        pltpu.VMEM((2, mine_images, half), low_type),
        pltpu.VMEM((2, mine_images, classes_wide), low_type),
        pltpu.VMEM((6, 8, channels), wide),
        pltpu.VMEM((6, 8, channels), wide),
        pltpu.VMEM((24, max(width, group)), wide),
        pltpu.VMEM((3, 8, channels), wide),
        pltpu.SemaphoreType.DMA((6,)),
        pltpu.SemaphoreType.DMA((2, 6)),
        pltpu.SemaphoreType.DMA((2, 5)),
    ]
    if gather:
        scratch += [pltpu.SemaphoreType.DMA((2, 3, 3))]
        scratch += [pltpu.SemaphoreType.DMA((2, 4, 3)) for _ in range(3)]
    return pl.pallas_call(
        functools.partial(client_kernel, gather, images, classes),
        out_shape=(
            jax.ShapeDtypeStruct((channels, width), low_type),
            jax.ShapeDtypeStruct((middle, width), low_type),
            jax.ShapeDtypeStruct((channels, width), low_type),
            jax.ShapeDtypeStruct(params.shape, wide),
            jax.ShapeDtypeStruct((half, classes_wide), wide),
            jax.ShapeDtypeStruct((8, LANES), wide),
        ),
        in_specs=[any_space, vmem, smem, vmem, vmem] + ([vmem] if gather else [any_space] * 3),
        out_specs=(any_space, any_space, any_space, vmem, vmem, vmem),
        scratch_shapes=scratch,
        compiler_params=pltpu.CompilerParams(
            collective_id=0, has_side_effects=True, vmem_limit_bytes=VMEM_BYTES
        ),
    )(features, labels, flag, params, head_low, *weights)


class Fold:
    def __init__(self, place, sources, sums, boxes, sems):
        self.place = place
        self.sources = sources
        self.sums = sums
        self.core_boxes, self.near_boxes, self.far_boxes, self.z_boxes = boxes
        self.core_sems, self.near_sems, self.far_sems, self.z_sems = sems
        self.order = place.others[::-1] + [place.z]
        self.copies = []

    def core_copy(self, turn, slot):
        p = self.place
        sems = self.core_sems
        return remote(
            self.sources[slot].at[self.order[turn], :, :, 1 - p.core],
            self.core_boxes[slot].at[turn],
            sems.at[0, turn, slot],
            sems.at[1, turn, slot],
            p.client,
            1 - p.core,
        )

    def near_copy(self, turn, slot):
        p = self.place
        spot = self.order[turn]
        if slot == 1:
            ref, to = self.sums[slot].at[spot, 1 - p.y], p.along_y()
        else:
            ref, to = self.sums[slot].at[spot, :, 1 - p.x], p.along_x()
        sems = self.near_sems
        return remote(
            ref, self.near_boxes[slot].at[turn], sems.at[0, turn, slot], sems.at[1, turn, slot], to, p.core
        )

    def far_copy(self, turn, slot):
        p = self.place
        spot = self.order[turn]
        if slot == 1:
            ref, to = self.sums[slot].at[spot, p.y, 1 - p.x], p.along_x()
        else:
            ref, to = self.sums[slot].at[spot, 1 - p.y, p.x], p.along_y()
        sems = self.far_sems
        return remote(
            ref, self.far_boxes[slot].at[turn], sems.at[0, turn, slot], sems.at[1, turn, slot], to, p.core
        )

    def z_copy(self, turn, slot):
        p = self.place
        step = 2 - turn
        sems = self.z_sems
        return remote(
            self.sums[slot].at[self.order[turn], p.y, p.x],
            self.z_boxes[slot].at[step],
            sems.at[0, step, slot],
            sems.at[1, step, slot],
            p.along_z(step),
            p.core,
        )

    def launch(self, copy):
        copy.start()
        self.copies.append(copy)

    def core_step(self, turn, slot):
        spot = self.order[turn]
        self.core_copy(turn, slot).wait_recv()
        both = self.local[slot][spot].astype(wide)
        both += self.core_boxes[slot][turn].astype(wide)
        self.sums[slot][spot] = both.astype(low_type)
        self.launch(self.near_copy(turn, slot))

    def near_step(self, turn, slot):
        p = self.place
        spot = self.order[turn]
        self.near_copy(turn, slot).wait_recv()
        where = (spot, p.y) if slot == 1 else (spot, slice(None), p.x)
        both = self.sums[slot][where].astype(wide) + self.near_boxes[slot][turn].astype(wide)
        self.sums[slot][where] = both.astype(low_type)
        self.launch(self.far_copy(turn, slot))

    def far_step(self, turn, slot):
        p = self.place
        where = (self.order[turn], p.y, p.x)
        self.far_copy(turn, slot).wait_recv()
        both = self.sums[slot][where].astype(wide) + self.far_boxes[slot][turn].astype(wide)
        self.sums[slot][where] = both.astype(low_type)
        if turn < 3:
            self.launch(self.z_copy(turn, slot))

    def begin(self, slot):
        for turn in range(4):
            self.launch(self.core_copy(turn, slot))

    def steps(self):
        listed = []
        for turn in range(6):
            for slot in range(3):
                if turn < 4:
                    listed.append(functools.partial(self.core_step, turn, slot))
                if 1 <= turn < 5:
                    listed.append(functools.partial(self.near_step, turn - 1, slot))
                if 2 <= turn:
                    listed.append(functools.partial(self.far_step, turn - 2, slot))
        return listed

    def result(self, slot):
        p = self.place
        total = self.sums[slot][p.z, p.y, p.x].astype(wide)
        for step in range(3):
            self.z_copy(2 - step, slot).wait_recv()
            total += self.z_boxes[slot][step].astype(wide)
        return total

    def drain(self):
        for copy in self.copies:
            copy.wait_send()


class GramSum:
    def __init__(self, place, data, total, boxes, sems):
        self.place = place
        self.data = data
        self.total = total
        self.core_box, self.near_box, self.far_box, self.z_box = boxes
        self.sems = sems
        self.copies = []
        self.sizes = (data.shape[0] // 72 * 40 // 32, data.shape[0] // 72 * 32 // 32)

    def rows(self, kind, core, z=None, first=None, second=None):
        size = self.sizes[kind]
        start = core * (16 * (self.sizes[0] + self.sizes[1])) + kind * 16 * self.sizes[0]
        count = 16 * size
        for number, spot, parts in ((4 * size, z, 4), (2 * size, first, 2), (size, second, 2)):
            if spot is None:
                break
            start, count = start + spot * number, number
        return pl.ds(pl.multiple_of(start, 8), count)

    def ways(self, kind):
        p = self.place
        x_way, y_way = (p.x, p.along_x()), (p.y, p.along_y())
        return (x_way, y_way) if kind == 0 else (y_way, x_way)

    def copy(self, phase, kind, turn, src, dst, client, core):
        sems = self.sems
        return remote(
            src, dst, sems.at[0, phase, kind, turn], sems.at[1, phase, kind, turn], client, core
        )

    def launch(self, copy):
        copy.start()
        self.copies.append(copy)

    def down(self, phase, kind, turn):
        p = self.place
        z = (p.others[::-1] + [p.z])[turn]
        (first, first_to), (second, second_to) = self.ways(kind)
        base = self.sizes[0] * kind
        if phase == 0:
            src = self.data.at[self.rows(kind, 1 - p.core, z), :]
            box = self.core_box.at[turn, pl.ds(4 * base, 4 * self.sizes[kind]), :]
            return self.copy(0, kind, turn, src, box, p.client, 1 - p.core)
        if phase == 1:
            src = self.data.at[self.rows(kind, p.core, z, 1 - first), :]
            box = self.near_box.at[turn, pl.ds(2 * base, 2 * self.sizes[kind]), :]
            return self.copy(1, kind, turn, src, box, first_to, p.core)
        if phase == 2:
            src = self.data.at[self.rows(kind, p.core, z, first, 1 - second), :]
            box = self.far_box.at[turn, pl.ds(base, self.sizes[kind]), :]
            return self.copy(2, kind, turn, src, box, second_to, p.core)
        src = self.data.at[self.rows(kind, p.core, z, first, second), :]
        box = self.z_box.at[turn, pl.ds(base, self.sizes[kind]), :]
        return self.copy(3, kind, turn, src, box, p.along_z(2 - turn), p.core)

    def down_step(self, phase, kind, turn):
        p = self.place
        z = (p.others[::-1] + [p.z])[turn]
        (first, _), (second, _) = self.ways(kind)
        self.down(phase, kind, turn).wait_recv()
        spots = (z, first, second)[: phase + 1]
        where = self.rows(kind, p.core, *spots)
        scale = (4, 2, 1)[phase]
        box = (self.core_box, self.near_box, self.far_box)[phase]
        self.data[where, :] += box[turn, pl.ds(scale * self.sizes[0] * kind, scale * self.sizes[kind]), :]
        if phase < 2 or turn < 3:
            self.launch(self.down(phase + 1, kind, turn))

    def up(self, phase, kind, turn):
        p = self.place
        z = ([p.z] + p.others)[turn]
        (first, first_to), (second, second_to) = self.ways(kind)
        if phase == 0:
            ref, to = self.total.at[self.rows(kind, p.core, p.z, first, second), :], p.along_z(turn)
        elif phase == 1:
            ref, to = self.total.at[self.rows(kind, p.core, z, first, second), :], second_to
        elif phase == 2:
            ref, to = self.total.at[self.rows(kind, p.core, z, first), :], first_to
        else:
            ref, to = self.total.at[self.rows(kind, p.core, z), :], p.client
        return self.copy(4 + phase, kind, turn, ref, ref, to, 1 - p.core if phase == 3 else p.core)

    def run(self):
        kinds = (0, 1)
        for turn in range(4):
            for kind in kinds:
                self.launch(self.down(0, kind, turn))
        for turn in range(6):
            for kind in kinds:
                for phase in range(3):
                    if 0 <= turn - phase < 4:
                        self.down_step(phase, kind, turn - phase)
        p = self.place
        for kind in kinds:
            (first, _), (second, _) = self.ways(kind)
            where = self.rows(kind, p.core, p.z, first, second)
            value = self.data[where, :]
            for turn in range(3):
                self.down(3, kind, turn).wait_recv()
                value += self.z_box[turn, pl.ds(self.sizes[0] * kind, self.sizes[kind]), :]
            self.total[where, :] = value
            self.launch(self.up(1, kind, 0))
            for turn in range(3):
                self.launch(self.up(0, kind, turn))
        for turn in range(6):
            for kind in kinds:
                if 1 <= turn < 4:
                    self.up(0, kind, turn - 1).wait_recv()
                    self.launch(self.up(1, kind, turn))
                if 1 <= turn < 5:
                    self.up(1, kind, turn - 1).wait_recv()
                    self.launch(self.up(2, kind, turn - 1))
                if 2 <= turn:
                    self.up(2, kind, turn - 2).wait_recv()
                    self.launch(self.up(3, kind, turn - 2))
        for turn in range(4):
            for kind in kinds:
                self.up(3, kind, turn).wait_recv()

    def drain(self):
        for copy in self.copies:
            copy.wait_send()


class TileSum:
    def __init__(self, place, tiles, boxes, sems):
        self.place = place
        self.tiles = tiles
        self.boxes = boxes
        self.sems = sems

    def copy(self, stage, box):
        p = self.place
        to = (p.client, p.along_x(), p.along_y()) + tuple(p.along_z(step) for step in range(3))
        core = 1 - p.core if box == 0 else p.core
        return remote(
            self.tiles.at[stage], self.boxes.at[box], self.sems.at[0, box], self.sems.at[1, box], to[box], core
        )

    def steps(self):
        def start():
            self.copy(0, 0).start()

        def pair(stage):
            self.copy(stage, stage).wait_recv()
            self.tiles[stage + 1] = self.tiles[stage] + self.boxes[stage]
            if stage < 2:
                self.copy(stage + 1, stage + 1).start()
            else:
                for step in range(3):
                    self.copy(3, 3 + step).start()

        return [start] + [functools.partial(pair, stage) for stage in range(3)]

    def result(self):
        for step in range(3):
            self.copy(3, 3 + step).wait_recv()
        return (self.tiles[3] + self.boxes[3]) + (self.boxes[4] + self.boxes[5])

    def drain(self):
        for stage in range(3):
            self.copy(stage, stage).wait_send()
        for step in range(3):
            self.copy(3, 3 + step).wait_send()


def dot_high(left, right):
    return jnp.dot(left, right, precision=lax.Precision.HIGH, preferred_element_type=wide)


def base_kernel(
    ratios,
    master,
    momentum,
    anchor,
    loss_in,
    first_in,
    middle_in,
    last_in,
    base_new,
    momentum_new,
    base_low,
    loss_out,
    *rest,
):
    place = Place()
    rest = list(rest)

    def take(count):
        taken = rest[:count]
        del rest[:count]
        return taken

    sources, sums = take(3), take(3)
    fold_boxes = [take(3) for _ in range(4)]
    gram, gram_total = take(2)
    gram_boxes = take(4)
    grams, iterate, tiles, tile_boxes = take(4)
    (local_sems,) = take(1)
    fold_sems = take(4)
    gram_sems, tile_sems = take(2)

    place.greet(True)
    incoming = (first_in, middle_in, last_in)
    fold = Fold(place, incoming, sums, fold_boxes, fold_sems)
    for slot in (2, 1, 0):
        fold.begin(slot)
    loads = [
        pltpu.make_async_copy(incoming[slot].at[:, :, :, place.core], sources[slot], local_sems.at[slot])
        for slot in range(3)
    ]
    for load in loads:
        load.start()
    tiles[0] = loss_in[...]
    tile_sum = TileSum(place, tiles, tile_boxes, tile_sems)
    extra = tile_sum.steps()
    extra.pop(0)()
    for load in loads:
        load.wait()
    fold.local = sources
    steps = fold.steps()
    for spot, step in enumerate(steps):
        step()
        if extra and spot % 9 == 8:
            extra.pop(0)()
    for step in extra:
        step()

    bounds = [0]
    for slot in range(3):
        bounds.append(bounds[-1] + sums[slot].shape[-2])
    width = master.shape[1]
    part = width // 2
    for slot in range(3):
        rows = slice(bounds[slot], bounds[slot + 1])
        grad = fold.result(slot) + prox_weight * (master[rows, :] - anchor[rows, :])
        fresh = momentum_decay * momentum[rows, :] + grad
        momentum_new[rows, :] = fresh
        partial = lax.dot_general(
            fresh, fresh, (((0,), (0,)), ((), ())), precision=precise, preferred_element_type=wide
        )
        start = 3 * part * slot
        gram[start : start + part, :] = partial[:part, :part]
        gram[start + part : start + 2 * part, :] = partial[:part, part:]
        gram[start + 2 * part : start + 3 * part, :] = partial[part:, part:]
    loss_out[...] = tile_sum.result()

    gram_sum = GramSum(place, gram, gram_total, gram_boxes, gram_sems)
    gram_sum.run()

    spots = lax.broadcasted_iota(jnp.int32, (part, part), 0)
    diagonal = spots == lax.broadcasted_iota(jnp.int32, (part, part), 1)
    iterate[...] = jnp.zeros_like(iterate)
    for slot in range(3):
        start = 3 * part * slot
        corner = gram_total[start : start + part, :]
        side = gram_total[start + part : start + 2 * part, :]
        end = gram_total[start + 2 * part : start + 3 * part, :]
        trace = jnp.sum(jnp.where(diagonal, corner + end, 0.0))
        factor = 1.0 / (jnp.sqrt(trace) + 1e-07)
        square = factor * factor
        grams[slot, :part, :part] = corner * square
        grams[slot, :part, part:] = side * square
        grams[slot, part:, :part] = side.T * square
        grams[slot, part:, part:] = end * square
        rows = slice(bounds[slot], bounds[slot + 1])
        iterate[slot, : bounds[slot + 1] - bounds[slot], :] = momentum_new[rows, :] * factor

    def turn(slot, last):
        current = grams[slot]
        mixed = schulz_second * current + schulz_third * dot_high(current, current)
        held = iterate[slot]
        iterate[slot] = schulz_first * held + dot_high(held, mixed)
        if not last:
            once = schulz_first * current + dot_high(current, mixed)
            grams[slot] = schulz_first * once + dot_high(once, mixed)

    def one(count, carry):
        turn(lax.rem(count, 3), False)
        return carry

    lax.fori_loop(0, 3 * (NS_STEPS - 1), one, 0)

    def final(slot, carry):
        turn(slot, True)
        return carry

    lax.fori_loop(0, 3, final, 0)
    for slot in range(3):
        rows = slice(bounds[slot], bounds[slot + 1])
        held = master[rows, :]
        ortho = iterate[slot, : bounds[slot + 1] - bounds[slot], :] * ratios[slot]
        fresh = held - muon_rate * (ortho + muon_decay * held)
        base_new[rows, :] = fresh
        base_low[rows, :] = fresh.astype(low_type)
    fold.drain()
    gram_sum.drain()
    tile_sum.drain()


def base_pass(ratios, master, momentum, anchor, loss_tile, grads):
    rows, width = master.shape
    part = width // 2
    any_space = pl.BlockSpec(memory_space=pl.ANY)
    vmem = pl.BlockSpec(memory_space=pltpu.VMEM)
    sizes = [grad.shape[0] // 32 for grad in grads]
    grads = [grad.reshape(SPOTS + (2, size, width)) for grad, size in zip(grads, sizes)]
    shares = [4, 4, 4, 3]

    def boxes(lead):
        return [pltpu.VMEM(lead + (size, width), low_type) for size in sizes]

    scratch = boxes(SPOTS) + boxes(SPOTS)
    scratch += boxes(SPOTS) + boxes((4, 2)) + boxes((4,)) + boxes((3,))
    scratch += [pltpu.VMEM((9 * part, part), wide)] * 2
    share = 9 * part // 32
    scratch += [pltpu.VMEM((4, size, part), wide) for size in (4 * share, 2 * share, share)]
    scratch += [pltpu.VMEM((3, share, part), wide)]
    scratch += [
        pltpu.VMEM((3, width, width), wide),
        pltpu.VMEM((3, max(sizes), width), wide),
        pltpu.VMEM((4, 8, LANES), wide),
        pltpu.VMEM((6, 8, LANES), wide),
        pltpu.SemaphoreType.DMA((3,)),
    ]
    scratch += [pltpu.SemaphoreType.DMA((2, 4, 3))] * 3 + [pltpu.SemaphoreType.DMA((2, 3, 3))]
    scratch += [pltpu.SemaphoreType.DMA((2, 8, 2, 4)), pltpu.SemaphoreType.DMA((2, 6))]
    return pl.pallas_call(
        functools.partial(base_kernel, ratios),
        out_shape=(
            jax.ShapeDtypeStruct((rows, width), wide),
            jax.ShapeDtypeStruct((rows, width), wide),
            jax.ShapeDtypeStruct((rows, width), low_type),
            jax.ShapeDtypeStruct((8, LANES), wide),
        ),
        in_specs=[vmem] * 4 + [any_space] * 3,
        out_specs=(vmem,) * 4,
        scratch_shapes=scratch,
        compiler_params=pltpu.CompilerParams(
            collective_id=1, has_side_effects=True, vmem_limit_bytes=VMEM_BYTES
        ),
    )(master, momentum, anchor, loss_tile, *grads)


def adam_update(param, grad, first, second, rate, decay):
    first = adam_first * first + (1.0 - adam_first) * grad
    second = adam_second * second + (1.0 - adam_second) * grad * grad
    first_hat = first / (1.0 - adam_first**STEP)
    second_hat = second / (1.0 - adam_second**STEP)
    return (
        param - rate * (first_hat / (jnp.sqrt(second_hat) + adam_epsilon) + decay * param),
        first,
        second,
    )


def gram_of(section):
    return lax.dot_general(section, section, (((0,), (0,)), ((), ())), precision=precise)


def square(gram):
    return jnp.dot(gram, gram, precision=precise)


def times_poly(left, mixed):
    return schulz_first * left + jnp.dot(left, mixed, precision=precise)


def schulz(sections):
    raw_grams = lax.psum(tuple(gram_of(section) for section in sections), ("client", "chan"))
    factors = [1.0 / (jnp.sqrt(jnp.trace(gram)) + 1e-07) for gram in raw_grams]
    current = [section * factor for section, factor in zip(sections, factors)]
    grams = [gram * (factor * factor) for gram, factor in zip(raw_grams, factors)]
    for turn in range(NS_STEPS):
        mixed = [schulz_second * gram + schulz_third * square(gram) for gram in grams]
        current = [times_poly(current[slot], mixed[slot]) for slot in range(3)]
        if turn + 1 < NS_STEPS:
            grams = [
                times_poly(times_poly(grams[slot], mixed[slot]), mixed[slot]) for slot in range(3)
            ]
    return current


def base_far(ratios, bounds, master, momentum, anchor, loss_tile, grads):
    sums = [
        lax.psum_scatter(grad.astype(wide), ("client", "chan"), scatter_dimension=0, tiled=True)
        for grad in grads
    ]
    grad_base = jnp.concatenate(sums, axis=0) + prox_weight * (master - anchor)
    momentum_new = momentum_decay * momentum + grad_base
    current = schulz([momentum_new[bounds[slot] : bounds[slot + 1]] for slot in range(3)])
    ortho = jnp.concatenate([current[slot] * ratios[slot] for slot in range(3)], axis=0)
    base_new = master - muon_rate * (ortho + muon_decay * master)
    return base_new, momentum_new, base_new.astype(low_type), lax.psum(loss_tile, ("client", "chan"))


def on_device(
    features,
    labels,
    mask,
    base_master,
    base_momentum,
    global_base,
    norm_params,
    norm_first,
    norm_second,
    head,
    head_first,
    head_second,
):
    halves = lax.axis_size("chan")
    blocks = lax.axis_size("client") * halves
    half = features.shape[2]
    width = base_master.shape[2]
    channels = half * halves
    images = labels.shape[1]
    classes = head.shape[2]
    rows_first = channels // blocks
    rows_mid = 9 * width // blocks
    bounds = (0, rows_first, rows_first + rows_mid, base_master.shape[1])
    master = base_master[0]
    head_low = jnp.pad(head[0].astype(low_type), ((0, 0), (0, LANES - classes)))
    near = lax.axis_size("client") == SPOTS[0] * SPOTS[1] * SPOTS[2]
    if near:
        weights = [master]
    else:
        low_master = master.astype(low_type)
        weights = [
            lax.all_gather(low_master[bounds[slot] : bounds[slot + 1]], ("client", "chan"), axis=0, tiled=True)
            for slot in range(3)
        ]
        weights = [weight.reshape(SPOTS + (2, weight.shape[0] // 32, width)) for weight in weights]
    grad_first, grad_middle, grad_last, grad_norm, grad_head, loss_tile = client_pass(
        near, classes, features[0], labels.reshape(images, 1), mask, norm_params[0, :, 0, :], head_low, weights
    )
    ratio = (channels / width) ** 0.5
    ratios = (ratio, 3.0, ratio)
    if near:
        base_new, momentum_new, base_low, loss_tile = base_pass(
            ratios, master, base_momentum[0], global_base[0], loss_tile, (grad_first, grad_middle, grad_last)
        )
    else:
        base_new, momentum_new, base_low, loss_tile = base_far(
            ratios,
            bounds,
            master,
            base_momentum[0],
            global_base[0],
            loss_tile,
            (grad_first, grad_middle, grad_last),
        )
    norm_new, norm_first_new, norm_second_new = adam_update(
        norm_params, grad_norm[None, :, None, :], norm_first, norm_second, norm_rate, 0.0
    )
    head_new, head_first_new, head_second_new = adam_update(
        head, grad_head[None, :, :classes], head_first, head_second, head_rate, head_decay
    )
    return (
        loss_tile[0, 0:2],
        base_new[None],
        momentum_new[None],
        base_low[None],
        norm_new,
        norm_first_new,
        norm_second_new,
        head_new,
        head_first_new,
        head_second_new,
    )


def solution(mesh):
    wide_block = P(("client", "chan"), None, None)
    norm_block = P("client", None, "chan", None)
    head_block = P("client", "chan", None)
    return jax.shard_map(
        on_device,
        mesh=mesh,
        in_specs=(P("client", None, "chan"), P("client", None), P("client"))
        + (wide_block,) * 3
        + (norm_block,) * 3
        + (head_block,) * 3,
        out_specs=(P(),) + (wide_block,) * 3 + (norm_block,) * 3 + (head_block,) * 3,
        check_vma=False,
    )
```

```python
import functools

import jax
import jax.numpy as jnp
from jax import lax
from jax.experimental import pallas as pl
from jax.experimental.pallas import tpu as pltpu
from jax.sharding import PartitionSpec as P

NS_STEPS = 5
STEP = 10

low_type = jnp.bfloat16
wide = jnp.float32
MESH = pl.DeviceIdType.MESH
precise = lax.Precision.HIGHEST
norm_epsilon = 1e-05
prox_weight = 0.05
momentum_decay = 0.95
muon_rate = 0.3
muon_decay = 0.1
schulz_first = 3.4445
schulz_second = -4.775
schulz_third = 2.0315
adam_first = 0.9
adam_second = 0.95
adam_epsilon = 1e-08
head_rate = 0.01
head_decay = 0.05
norm_rate = 0.5

SIDE = 7
PIXELS = SIDE * SIDE
LANES = 128
SPOTS = (4, 2, 2)
VMEM_BYTES = 62 * 2**20


def dot_nn(left, right):
    return jnp.dot(left, right, preferred_element_type=wide)


def dot_nt(left, right):
    return lax.dot_general(left, right, (((1,), (1,)), ((), ())), preferred_element_type=wide)


def dot_tn(left, right):
    return lax.dot_general(left, right, (((0,), (0,)), ((), ())), preferred_element_type=wide)


def flat_rows(block):
    return block.reshape(-1, block.shape[-1])


def sigmoid(value):
    return 0.5 * jnp.tanh(0.5 * value) + 0.5


def fold_rows(value):
    return jnp.sum(value.reshape(value.shape[0] // 8, 8, value.shape[1]), axis=0)


def column_sum(value):
    return jnp.sum(value, axis=0, keepdims=True)


def remote(src, dst, send_sem, recv_sem, client, core):
    return pltpu.make_async_remote_copy(
        src_ref=src,
        dst_ref=dst,
        send_sem=send_sem,
        recv_sem=recv_sem,
        device_id=(client, core),
        device_id_type=MESH,
    )


class Place:
    def __init__(self):
        self.client = lax.axis_index("client")
        self.core = lax.axis_index("chan")
        self.z = self.client // 4
        self.y = (self.client // 2) % 2
        self.x = self.client % 2
        self.others = [
            self.z + 1 - 2 * (self.z % 2),
            (self.z + 2) % 4,
            3 - self.z,
        ]

    def at(self, z, y, x):
        return z * 4 + y * 2 + x

    def along_x(self):
        return self.at(self.z, self.y, 1 - self.x)

    def along_y(self):
        return self.at(self.z, 1 - self.y, self.x)

    def along_z(self, step):
        return self.at(self.others[step], self.y, self.x)

    def greet(self, whole):
        barrier = pltpu.get_barrier_semaphore()
        pairs = [(self.client, 1 - self.core)]
        if whole:
            pairs += [(self.along_x(), self.core), (self.along_y(), self.core)]
            pairs += [(self.along_z(step), self.core) for step in range(3)]
        for pair in pairs:
            pl.semaphore_signal(barrier, inc=1, device_id=pair, device_id_type=MESH)
        pl.semaphore_wait(barrier, len(pairs))


def cut_rows(counts):
    pieces = []
    for slot, rows in enumerate(counts):
        middle = (rows // 16 + 1) // 2 * 16
        pieces.append((slot, 0, middle, 0))
        pieces.append((slot, middle, rows - middle, 1))
    return pieces


class Spread:
    def __init__(self, place, weights, sems):
        self.place = place
        self.weights = weights
        self.pieces = cut_rows([weight.shape[-2] for weight in weights])
        self.z_sems, self.near_sems, self.far_sems, self.core_sems = sems
        self.order = [place.z] + place.others
        self.copies = []

    def z_copy(self, step, slot):
        p = self.place
        ref = self.weights[slot].at[p.z, p.y, p.x, p.core]
        sems = self.z_sems
        return remote(ref, ref, sems.at[0, step, slot], sems.at[1, step, slot], p.along_z(step), p.core)

    def near_copy(self, turn, number):
        p = self.place
        slot, start, count, way = self.pieces[number]
        ref = self.weights[slot].at[self.order[turn], p.y, p.x, p.core, pl.ds(start, count), :]
        sems = self.near_sems
        return remote(
            ref, ref, sems.at[0, turn, number], sems.at[1, turn, number], (p.along_x, p.along_y)[way](), p.core
        )

    def far_copy(self, turn, number):
        p = self.place
        slot, start, count, way = self.pieces[number]
        rows = pl.ds(start, count)
        spot = self.order[turn]
        if way == 0:
            ref = self.weights[slot].at[spot, p.y, :, p.core, rows, :]
        else:
            ref = self.weights[slot].at[spot, :, p.x, p.core, rows, :]
        sems = self.far_sems
        return remote(
            ref, ref, sems.at[0, turn, number], sems.at[1, turn, number], (p.along_y, p.along_x)[way](), p.core
        )

    def core_copy(self, turn, slot):
        p = self.place
        ref = self.weights[slot].at[self.order[turn], :, :, p.core]
        sems = self.core_sems
        return remote(ref, ref, sems.at[0, turn, slot], sems.at[1, turn, slot], p.client, 1 - p.core)

    def launch(self, copy):
        copy.start()
        self.copies.append(copy)

    def begin(self, master):
        p = self.place
        start = 0
        for slot in range(3):
            rows = self.weights[slot].shape[-2]
            self.weights[slot][p.z, p.y, p.x, p.core] = master[start : start + rows, :].astype(low_type)
            start += rows
        for slot in range(3):
            for number in (2 * slot, 2 * slot + 1):
                self.launch(self.near_copy(0, number))
            for step in range(3):
                self.launch(self.z_copy(step, slot))

    def steps(self):
        timed = []
        for slot, (start, pace) in enumerate(((0.0, 1.5), (4.0, 4.0), (20.0, 2.5))):
            for turn in range(4):
                base = start + turn * pace
                if turn > 0:
                    timed.append((base, functools.partial(self.near_step, turn, slot)))
                timed.append((base + 1.3 * pace, functools.partial(self.far_step, turn, slot)))
                timed.append((base + 2.6 * pace, functools.partial(self.core_step, turn, slot)))
        timed.sort(key=lambda pair: pair[0])
        return [step for _, step in timed]

    def near_step(self, turn, slot):
        self.z_copy(turn - 1, slot).wait_recv()
        for number in (2 * slot, 2 * slot + 1):
            self.launch(self.near_copy(turn, number))

    def far_step(self, turn, slot):
        for number in (2 * slot, 2 * slot + 1):
            self.near_copy(turn, number).wait_recv()
            self.launch(self.far_copy(turn, number))

    def core_step(self, turn, slot):
        for number in (2 * slot, 2 * slot + 1):
            self.far_copy(turn, number).wait_recv()
        self.launch(self.core_copy(turn, slot))

    def arrive(self, slot):
        for turn in range(4):
            self.core_copy(turn, slot).wait_recv()

    def drain(self):
        for copy in self.copies:
            copy.wait_send()


class Fold:
    def __init__(self, place, grads, counts, parts):
        self.place = place
        self.grads = grads
        self.counts = counts
        self.pieces = cut_rows(counts)
        self.core_boxes = [parts[1], parts[0], parts[1]]
        self.near_boxes, self.far_boxes, self.z_boxes = [parts[3 * k + 2 : 3 * k + 5] for k in range(3)]
        self.core_sems, self.near_sems, self.far_sems, self.z_sems = parts[11:]
        self.copies = []
        self.begun = set()

    def core_copy(self, which, slot):
        p = self.place
        sems = self.core_sems
        return remote(
            self.grads[slot].at[which, :, :, 1 - p.core, pl.ds(0, self.counts[slot]), :],
            self.core_boxes[slot].at[which],
            sems.at[0, which, slot],
            sems.at[1, which, slot],
            p.client,
            1 - p.core,
        )

    def near_copy(self, which, number):
        p = self.place
        slot, start, count, way = self.pieces[number]
        rows = pl.ds(start, count)
        if way == 0:
            ref = self.grads[slot].at[which, :, 1 - p.x, p.core, rows, :]
        else:
            ref = self.grads[slot].at[which, 1 - p.y, :, p.core, rows, :]
        box = self.near_boxes[slot].at[which, :, rows, :]
        sems = self.near_sems
        return remote(
            ref, box, sems.at[0, which, number], sems.at[1, which, number], (p.along_x, p.along_y)[way](), p.core
        )

    def far_copy(self, which, number):
        p = self.place
        slot, start, count, way = self.pieces[number]
        rows = pl.ds(start, count)
        if way == 0:
            ref = self.grads[slot].at[which, 1 - p.y, p.x, p.core, rows, :]
        else:
            ref = self.grads[slot].at[which, p.y, 1 - p.x, p.core, rows, :]
        box = self.far_boxes[slot].at[which, rows, :]
        sems = self.far_sems
        return remote(
            ref, box, sems.at[0, which, number], sems.at[1, which, number], (p.along_y, p.along_x)[way](), p.core
        )

    def z_copy(self, which, sender, number):
        p = self.place
        slot, start, count, _ = self.pieces[number]
        rows = pl.ds(start, count)
        sems = self.z_sems
        return remote(
            self.grads[slot].at[which, p.y, p.x, p.core, rows, :],
            self.z_boxes[slot].at[sender, rows, :],
            sems.at[0, which, number],
            sems.at[1, sender, number],
            p.at(which, p.y, p.x),
            p.core,
        )

    def launch(self, copy):
        copy.start()
        self.copies.append(copy)

    def begin(self, which, slot):
        self.begun.add((which, slot))
        self.launch(self.core_copy(which, slot))

    def steps(self):
        listed = []
        for slot in (2, 1, 0):
            for turn in range(6):
                for lag, step in ((0, self.core_step), (1, self.near_step), (2, self.far_step)):
                    if 0 <= turn - lag < 4:
                        listed.append(functools.partial(step, turn - lag, slot))
        return listed

    def ready(self, step):
        return step.args in self.begun

    def core_step(self, which, slot):
        p = self.place
        rows = pl.ds(0, self.counts[slot])
        self.core_copy(which, slot).wait_recv()
        where = (which, slice(None), slice(None), p.core, rows, slice(None))
        both = self.grads[slot][where].astype(wide) + self.core_boxes[slot][which].astype(wide)
        self.grads[slot][where] = both.astype(low_type)
        for number in (2 * slot, 2 * slot + 1):
            self.launch(self.near_copy(which, number))

    def near_step(self, which, slot):
        p = self.place
        for number in (2 * slot, 2 * slot + 1):
            _, start, count, way = self.pieces[number]
            rows = pl.ds(start, count)
            self.near_copy(which, number).wait_recv()
            if way == 0:
                where = (which, slice(None), p.x, p.core, rows, slice(None))
            else:
                where = (which, p.y, slice(None), p.core, rows, slice(None))
            both = self.grads[slot][where].astype(wide) + self.near_boxes[slot][which, :, rows, :].astype(wide)
            self.grads[slot][where] = both.astype(low_type)
            self.launch(self.far_copy(which, number))

    def far_step(self, which, slot):
        p = self.place
        for number in (2 * slot, 2 * slot + 1):
            _, start, count, way = self.pieces[number]
            rows = pl.ds(start, count)
            self.far_copy(which, number).wait_recv()
            where = (which, p.y, p.x, p.core, rows, slice(None))
            both = self.grads[slot][where].astype(wide) + self.far_boxes[slot][which, rows, :].astype(wide)
            self.grads[slot][where] = both.astype(low_type)

            @pl.when(p.z != which)
            def _():
                self.z_copy(which, p.z, number).start()

    def result(self, slot):
        p = self.place
        rows = pl.ds(0, self.counts[slot])
        self.z_boxes[slot][p.z] = self.grads[slot][p.z, p.y, p.x, p.core, rows, :]
        for sender in range(4):

            @pl.when(p.z != sender)
            def _():
                for number in (2 * slot, 2 * slot + 1):
                    self.z_copy(sender, sender, number).wait_recv()

        total = self.z_boxes[slot][0].astype(wide)
        for sender in range(1, 4):
            total += self.z_boxes[slot][sender].astype(wide)
        return total

    def drain(self):
        for copy in self.copies:
            copy.wait_send()
        for which in range(4):

            @pl.when(self.place.z != which)
            def _():
                for number in range(6):
                    self.z_copy(which, self.place.z, number).wait_send()


def norm_stats(mine, theirs, count):
    gap = mine[0:1] - theirs[0:1]
    mean = 0.5 * (mine[0:1] + theirs[0:1])
    spread = mine[1:2] + theirs[1:2] + gap * gap * (0.5 * count)
    return mean, lax.rsqrt(spread / (2.0 * count) + norm_epsilon)


def client_kernel(
    gather,
    images,
    classes,
    features,
    labels,
    flag,
    params,
    head,
    *rest,
):
    if gather:
        master, *rest = rest
    else:
        first_in, middle_in, last_in, *rest = rest
    if gather:
        grads_out, *rest = rest
    else:
        grads_out, rest = rest[:3], rest[3:]
    (
        grad_norm_out,
        grad_head_out,
        loss_out,
        x_all,
        mid_wide,
        w_first,
        w_middle,
        w_last,
        act_one,
        act_two,
        act_three,
        taps_one,
        taps_two,
        hidden_two,
        stage,
        params_all,
        head_all,
        grad_pool,
        pool_send,
        pool_all,
        logit_grads,
        sums_mine,
        sums_theirs,
        shift,
        fwd_stats,
        sem_local,
        sem_swap,
        sem_misc,
        *near_parts,
    ) = rest
    place = Place()
    core = place.core
    mate = (place.client, 1 - core)
    count_rows, channels = x_all.shape
    half = channels // 2
    width = act_one.shape[1]
    part = width // 2
    mine_images = images // 2
    line = SIDE * mine_images
    total_rows = 2.0 * count_rows

    def tile(index):
        return pl.ds(pl.multiple_of(index * line, line), line)

    def lanes(index, size):
        return pl.ds(pl.multiple_of(index * size, size), size)

    place.greet(gather)

    quarter = half // 2
    own_rows = pl.ds(pl.multiple_of(core * count_rows, count_rows), count_rows)
    mate_rows = pl.ds(pl.multiple_of((1 - core) * count_rows, count_rows), count_rows)
    top_rows = pl.ds(0, count_rows)
    own_copies = [
        pltpu.make_async_copy(
            features.at[own_rows, pl.ds(0, quarter)], hidden_two, sem_local.at[0]
        )
    ]
    for index in range(SIDE):
        rows = pl.ds(pl.multiple_of(core * count_rows + index * line, line), line)
        own_copies.append(
            pltpu.make_async_copy(
                features.at[rows, pl.ds(quarter, quarter)],
                mid_wide.at[0, index // 4, (index // 2) % 2, index % 2],
                sem_local.at[1 + index],
            )
        )
    to_mate = [
        remote(params, params_all.at[core], sem_misc.at[0, 0], sem_misc.at[1, 0], *mate),
        remote(head, head_all.at[core], sem_misc.at[0, 1], sem_misc.at[1, 1], *mate),
    ]
    for side, buffer in enumerate((taps_one, taps_two)):
        to_mate.append(
            remote(
                features.at[mate_rows, pl.ds(side * quarter, quarter)],
                buffer.at[top_rows, :],
                sem_misc.at[0, 5 + side],
                sem_misc.at[1, 5 + side],
                *mate,
            )
        )
    for copy in to_mate + own_copies:
        copy.start()
    params_all[core] = params[...]
    head_all[core] = head[...]

    weights = (w_first, w_middle, w_last)
    if gather:
        spread = Spread(place, weights, near_parts[:4])
        held = act_three.at[pl.ds(0, master.shape[0]), pl.ds(0, width)]
        load = pltpu.make_async_copy(master, held, sem_local.at[8])
        load.start()
        load.wait()
        spread.begin(held)
        counts = [weight.shape[-2] for weight in weights]
        fold = Fold(place, (w_first, mid_wide, w_last), counts, near_parts[4:])
        due = spread.steps()
    else:
        loads = [
            pltpu.make_async_copy(src, dst, sem_local.at[8 + slot])
            for slot, (src, dst) in enumerate(zip((first_in, middle_in, last_in), weights))
        ]
        for load in loads:
            load.start()
        due = []

    def advance(count):
        while count > 0 and due and (not fold.begun or fold.ready(due[0])):
            due.pop(0)()
            count -= 1

    def arrive(slot):
        if gather:
            while any(step.args[1] <= slot for step in due):
                advance(1)
            spread.arrive(slot)
        else:
            loads[slot].wait()

    def zero_edges(buffer):
        edge = jnp.zeros((line,) + buffer.shape[1:], low_type)
        buffer[0:line, :] = edge
        buffer[line + count_rows : 2 * line + count_rows, :] = edge

    advance(6)
    for copy in own_copies:
        copy.wait()

    def turn_from(source, base):
        def turn(index, carry):
            stage[...] = source(lanes(index, LANES)).astype(wide)

            def pixel(spot, inner):
                x_all[
                    pl.ds(pl.multiple_of(spot * mine_images, mine_images), mine_images),
                    pl.ds(pl.multiple_of(base + index * LANES, LANES), LANES),
                ] = stage[pl.ds(spot, mine_images, stride=PIXELS), :].astype(low_type)
                return inner

            return lax.fori_loop(0, PIXELS, pixel, carry, unroll=7)

        return turn

    quarters = quarter // LANES
    own_base, mate_base = core * half, (1 - core) * half
    lax.fori_loop(0, quarters, turn_from(lambda columns: hidden_two[:, columns], own_base), 0)
    advance(4)
    lax.fori_loop(
        0,
        quarters,
        turn_from(lambda columns: mid_wide[0, :, :, :, :, columns].reshape(8 * line, LANES)[:count_rows], own_base + quarter),
        0,
    )
    advance(4)
    for copy in to_mate:
        copy.wait_recv()
    lax.fori_loop(0, quarters, turn_from(lambda columns: taps_one[0:count_rows, columns], mate_base), 0)
    advance(4)
    lax.fori_loop(0, quarters, turn_from(lambda columns: taps_two[0:count_rows, columns], mate_base + quarter), 0)
    zero_edges(taps_one)
    zero_edges(taps_two)
    arrive(0)

    def swap(slot, size):
        return remote(
            sums_mine.at[slot, :, pl.ds(0, size)],
            sums_theirs.at[slot, :, pl.ds(0, size)],
            sem_swap.at[0, slot],
            sem_swap.at[1, slot],
            *mate,
        )

    def gain_bias(lower, upper):
        rows = []
        for kind in range(2):
            pieces = [params_all[side, kind : kind + 1, lower:upper] for side in range(2)]
            rows.append(jnp.concatenate(pieces, axis=1))
        return rows

    def collect(index, value, columns, size):
        @pl.when(index == 0)
        def _():
            shift[0:1, pl.ds(0, size)] = column_sum(fold_rows(value)) / value.shape[0]
            shift[8:24, pl.ds(0, size)] = jnp.zeros((16, size), wide)

        gap = value - shift[0:1, pl.ds(0, size)]
        shift[8:16, pl.ds(0, size)] += fold_rows(gap)
        shift[16:24, pl.ds(0, size)] += fold_rows(gap * gap)

    def close_stats(slot, columns, size):
        sum_gap = column_sum(shift[8:16, pl.ds(0, size)])
        sum_square = column_sum(shift[16:24, pl.ds(0, size)])
        sums_mine[slot, 0:1, columns] = shift[0:1, pl.ds(0, size)] + sum_gap / count_rows
        sums_mine[slot, 1:2, columns] = sum_square - sum_gap * sum_gap / count_rows

    def settle(slot, size):
        mean, scale = norm_stats(
            sums_mine[slot, 0:2, pl.ds(0, size)], sums_theirs[slot, 0:2, pl.ds(0, size)], float(count_rows)
        )
        fwd_stats[slot, 0:1, pl.ds(0, size)] = mean
        fwd_stats[slot, 1:2, pl.ds(0, size)] = scale

    whole_width = pl.ds(0, width)

    def first_tile(index, carry):
        value = dot_nn(x_all[tile(index), :], flat_rows(w_first[...]))
        act_one[tile(index), :] = value
        collect(index, value, whole_width, width)
        return carry

    for lower, upper in ((0, 2), (2, 4), (4, SIDE)):
        lax.fori_loop(lower, upper, first_tile, 0)
        advance(3)
    close_stats(0, whole_width, width)
    move = swap(0, width)
    move.start()
    move.wait()
    settle(0, width)

    gain_one, bias_one = gain_bias(0, part)
    gain_two, bias_two = gain_bias(part, width)
    gain_three, bias_three = gain_bias(width, width + half)

    def normal(act, slot, index):
        mean = fwd_stats[slot, 0:1, pl.ds(0, width)]
        return (act[tile(index), :] - mean) * fwd_stats[slot, 1:2, pl.ds(0, width)]

    def hide_one(index, carry):
        value = normal(act_one, 0, index) * gain_one + bias_one
        taps_one[pl.ds(pl.multiple_of((index + 1) * line, line), line), :] = (value * sigmoid(value)).astype(low_type)
        return carry

    lax.fori_loop(0, SIDE, hide_one, 0)
    arrive(1)

    def shifted(buffer, index, down):
        return buffer[pl.ds(pl.multiple_of((index + down) * line, line), line), :]

    step = mine_images
    edge_rows = jnp.zeros((step, width), wide)

    def over_lines(lines, tap_of, multiply, axis):
        left = jnp.concatenate(lines, axis=1)
        value = multiply(left, jnp.concatenate([tap_of(down, 1) for down in range(3)], axis=axis))
        lower = multiply(left[: line - step], jnp.concatenate([tap_of(down, 0) for down in range(3)], axis=axis))
        upper = multiply(left[step:], jnp.concatenate([tap_of(down, 2) for down in range(3)], axis=axis))
        value += jnp.concatenate([edge_rows, lower], axis=0)
        return value + jnp.concatenate([upper, edge_rows], axis=0)

    def second_tile(index, carry):
        kernel = flat_rows(w_middle[...])

        def tap_of(down, over):
            tap = 3 * down + over
            return kernel[tap * width : (tap + 1) * width]

        value = over_lines([shifted(taps_one, index, down) for down in range(3)], tap_of, dot_nn, 0)
        act_two[tile(index), :] = value
        collect(index, value, whole_width, width)
        return carry

    for lower, upper in ((0, 2), (2, 4), (4, SIDE)):
        lax.fori_loop(lower, upper, second_tile, 0)
        advance(4)
    close_stats(1, whole_width, width)
    move_two = swap(1, width)
    move_two.start()
    move_two.wait()
    settle(1, width)

    def hide_two(index, carry):
        value = normal(act_two, 1, index) * gain_two + bias_two
        hidden_two[tile(index), :] = (value * sigmoid(value)).astype(low_type)
        return carry

    lax.fori_loop(0, SIDE, hide_two, 0)

    arrive(2)
    groups = w_last.shape[0]
    group = channels // groups

    def third_group(which, carry):
        columns = lanes(which, group)

        def third_tile(index, inner):
            value = dot_nt(hidden_two[tile(index), :], flat_rows(w_last[which]))
            act_three[tile(index), columns] = value
            collect(index, value, columns, group)
            return inner

        lax.fori_loop(0, SIDE, third_tile, 0)
        close_stats(2, columns, group)
        return carry

    lax.fori_loop(0, groups, third_group, 0)
    move_three = swap(2, channels)
    move_three.start()
    move_three.wait()
    settle(2, channels)
    fwd_stats[2, 2:3, :] = gain_three
    fwd_stats[2, 3:4, :] = bias_three

    per_group = group // LANES

    def block_of(spot):
        return pl.ds(pl.multiple_of(spot * mine_images, mine_images), mine_images)

    def mid_line(which, index):
        return which, index // 4, (index // 2) % 2, index % 2, pl.ds(0, line)

    kept = channels // LANES * mine_images

    def gathered(kind):
        starts = range(kind * kept, (kind + 1) * kept, mine_images)
        return jnp.concatenate([stage[start : start + mine_images, :] for start in starts], axis=1)

    def emit(index, carry):
        columns = lanes(index, LANES)
        mean, scale = fwd_stats[2, 0:1, columns], fwd_stats[2, 1:2, columns]
        gain, bias = fwd_stats[2, 2:3, columns], fwd_stats[2, 3:4, columns]

        def pixels(row, sums):
            pooled, slopes, slopes_normed = sums
            found = []
            for spot in range(SIDE):
                where = block_of(row * SIDE + spot)
                normed = (act_three[where, columns] - mean) * scale
                total = normed * gain + bias + x_all[where, columns].astype(wide)
                sig = sigmoid(total)
                out = total * sig
                slope = sig + out * (1.0 - sig)
                found.append(slope.astype(low_type))
                pooled, slopes, slopes_normed = pooled + out, slopes + slope, slopes_normed + slope * normed
            mid_wide[mid_line(index // per_group, row) + (lanes(index % per_group, LANES),)] = jnp.concatenate(
                found, axis=0
            )
            return pooled, slopes, slopes_normed

        zero = jnp.zeros((mine_images, LANES), wide)
        pooled, slopes, slopes_normed = lax.fori_loop(0, SIDE, pixels, (zero, zero, zero))
        for kind, value in enumerate((pooled, slopes, slopes_normed)):
            stage[pl.ds(pl.multiple_of(kind * kept + index * mine_images, mine_images), mine_images), :] = value
        return carry

    lax.fori_loop(0, channels // LANES, emit, 0)

    pooled = (gathered(0) / PIXELS).astype(low_type)
    head_full = jnp.concatenate([head_all[0], head_all[1]], axis=1)
    logits = dot_nt(head_full, pooled)
    spots = lax.broadcasted_iota(jnp.int32, logits.shape, 0)
    inside = spots < classes
    first_labels, second_labels = labels[0:1, 0:mine_images], labels[0:1, mine_images:]
    onehot = (spots == jnp.where(core == 0, first_labels, second_labels)).astype(wide)
    top = jnp.max(jnp.where(inside, logits, -jnp.inf), axis=0, keepdims=True)
    powers = jnp.where(inside, jnp.exp(logits - top), 0.0)
    power_sum = jnp.sum(powers, axis=0, keepdims=True)
    picked = jnp.sum(logits * onehot, axis=0, keepdims=True)
    each_loss = top + jnp.log(power_sum) - picked
    taking = flag[0].astype(wide)
    tile_spots = lax.broadcasted_iota(jnp.int32, loss_out.shape, 1)
    loss_out[...] = jnp.where(tile_spots == 0, taking * jnp.sum(each_loss), taking * mine_images)
    grads = (taking / images * (powers / power_sum - onehot)).astype(low_type)
    grad_pool[...] = dot_tn(grads, head_full) / PIXELS
    logit_grads[core] = grads
    pool_all[core] = pooled[:, 0:half]
    pool_send[...] = pooled[:, half:]

    @pl.when(core == 1)
    def _():
        pool_all[core] = pooled[:, half:]
        pool_send[...] = pooled[:, 0:half]

    head_moves = [
        remote(pool_send, pool_all.at[core], sem_misc.at[0, 3], sem_misc.at[1, 3], *mate),
        remote(logit_grads.at[core], logit_grads.at[core], sem_misc.at[0, 4], sem_misc.at[1, 4], *mate),
    ]

    sums_mine[3, 0:1, :] = column_sum(grad_pool[...] * gathered(1))
    sums_mine[3, 1:2, :] = column_sum(grad_pool[...] * gathered(2))
    move_back = swap(3, channels)
    move_back.start()
    for copy in head_moves:
        copy.start()
    move_back.wait()

    def back_terms(slot, layer, size, gain):
        columns = pl.ds(0, size)
        sums = sums_mine[slot, 0:2, columns] + sums_theirs[slot, 0:2, columns]
        sums_mine[slot, 2:4, columns] = sums
        scale = fwd_stats[layer, 1:2, columns]
        return (
            scale * gain,
            scale * gain * sums[0:1] / total_rows,
            scale * scale * gain * sums[1:2] / total_rows,
        )

    first, second, third = back_terms(3, 2, channels, gain_three)
    fwd_stats[2, 4:5, :] = first
    fwd_stats[2, 5:6, :] = second
    fwd_stats[2, 6:7, :] = third

    def pull(index, carry):
        columns = lanes(index, LANES)
        mean = fwd_stats[2, 0:1, columns]
        first, second = fwd_stats[2, 4:5, columns], fwd_stats[2, 5:6, columns]
        third = fwd_stats[2, 6:7, columns]
        reach = grad_pool[:, columns] * first

        def pixels(row, inner):
            where = mid_line(index // per_group, row) + (lanes(index % per_group, LANES),)
            slopes = mid_wide[where].astype(wide)
            found = []
            for spot in range(SIDE):
                slope = slopes[spot * mine_images : (spot + 1) * mine_images]
                gap = act_three[block_of(row * SIDE + spot), columns] - mean
                found.append((reach * slope - second - third * gap).astype(low_type))
            mid_wide[where] = jnp.concatenate(found, axis=0)
            return inner

        return lax.fori_loop(0, SIDE, pixels, carry)

    lax.fori_loop(0, channels // LANES, pull, 0)
    for copy in head_moves:
        copy.wait_recv()
    head_space = act_three.at[pl.ds(0, grad_head_out.shape[0]), pl.ds(half, half)]
    head_space[...] = dot_nn(logit_grads[0], pool_all[0]) + dot_nn(logit_grads[1], pool_all[1])
    head_leave = pltpu.make_async_copy(head_space, grad_head_out, sem_local.at[0])
    head_leave.start()

    def drop_into(index, value, act, slot, gain, bias, columns):
        normed = normal(act, slot, index)
        norm = normed * gain + bias
        sig = sigmoid(norm)
        grad = value * (sig + norm * sig * (1.0 - sig))
        act_three[tile(index), columns] = grad
        size = pl.ds(0, width)

        @pl.when(index == 0)
        def _():
            shift[8:24, size] = jnp.zeros((16, width), wide)

        shift[8:16, size] += fold_rows(grad)
        shift[16:24, size] += fold_rows(grad * normed)

    def close_back(slot):
        size = pl.ds(0, width)
        sums_mine[slot, 0:1, size] = column_sum(shift[8:16, size])
        sums_mine[slot, 1:2, size] = column_sum(shift[16:24, size])

    space_two, space_one = pl.ds(0, width), pl.ds(width, width)

    def back_two(index, carry):
        kernel = flat_rows(w_last[...])
        left = jnp.concatenate([mid_wide[mid_line(which, index)] for which in range(groups)], axis=1)
        value = dot_nn(left, kernel)
        drop_into(index, value, act_two, 1, gain_two, bias_two, space_two)
        return carry

    lax.fori_loop(0, SIDE, back_two, 0)
    close_back(4)
    move_back_two = swap(4, width)
    move_back_two.start()

    if gather:
        spread.drain()

    def weight_rows(ref, which, rows):
        return ref.at[which, :, :, :, pl.ds(0, rows), :]

    def put(ref, which, value):
        rows = value.shape[0] // 8
        ref[which, :, :, :, pl.ds(0, rows), :] = value.astype(low_type).reshape(2, 2, 2, rows, width)

    def expand_group(which, carry):
        left = mid_wide[which].reshape(8 * line, group)[:count_rows]
        put(w_last, which, dot_tn(left, hidden_two[...]))
        return carry

    for which in range(groups):
        expand_group(which, 0)
        if gather:
            fold.begin(which, 2)
    move_back_two.wait()
    terms_two = back_terms(4, 1, width, gain_two)

    def back_act(terms, act, layer, index, columns):
        first, second, third = terms
        gap = act[tile(index), :] - fwd_stats[layer, 0:1, pl.ds(0, width)]
        return (first * act_three[tile(index), columns] - second - third * gap).astype(low_type)

    def grad_two(index, carry):
        taps_two[pl.ds(pl.multiple_of((index + 1) * line, line), line), :] = back_act(
            terms_two, act_two, 1, index, space_two
        )
        return carry

    lax.fori_loop(0, SIDE, grad_two, 0)
    if gather:
        due = fold.steps()

    middle_rows = 9 * width // groups
    for which in range(groups):
        pieces = []
        start = which * middle_rows
        while start < (which + 1) * middle_rows:
            tap, spot = start // width, start % width
            size = min(width - spot, (which + 1) * middle_rows - start)
            down, over = tap // 3, tap % 3
            left_start, right_start = (0, 0, step)[over], (step, 0, 0)[over]
            reach = line if over == 1 else line - step
            left = jnp.concatenate(
                [
                    taps_one[row + left_start : row + left_start + reach, spot : spot + size]
                    for row in range(down * line, (down + SIDE) * line, line)
                ],
                axis=0,
            )
            right = jnp.concatenate(
                [
                    taps_two[row + right_start : row + right_start + reach, :]
                    for row in range(line, (1 + SIDE) * line, line)
                ],
                axis=0,
            )
            pieces.append(dot_tn(left, right).astype(low_type))
            start += size
        put(mid_wide, which, jnp.concatenate(pieces, axis=0))
        if gather:
            fold.begin(which, 1)
        advance(5)

    def back_one(index, carry):
        kernel = flat_rows(w_middle[...])

        def tap_of(down, over):
            tap = 3 * down + 2 - over
            return kernel[tap * width : (tap + 1) * width]

        value = over_lines([shifted(taps_two, index, 2 - down) for down in range(3)], tap_of, dot_nt, 1)
        drop_into(index, value, act_one, 0, gain_one, bias_one, space_one)
        return carry

    for lower, upper in ((0, 1), (1, 2), (2, 3), (3, 4), (4, 5), (5, SIDE)):
        lax.fori_loop(lower, upper, back_one, 0)
        advance(5)
    close_back(5)
    while any(step.args[1] == 2 for step in due):
        advance(1)
    move_back_one = swap(5, width)
    move_back_one.start()

    move_back_one.wait()
    terms_one = back_terms(5, 0, width, gain_one)

    def grad_one(index, carry):
        hidden_two[tile(index), :] = back_act(terms_one, act_one, 0, index, space_one)
        return carry

    lax.fori_loop(0, SIDE, grad_one, 0)

    for which in range(groups):
        put(w_first, which, dot_tn(x_all[:, which * group : (which + 1) * group], hidden_two[...]))
        if gather:
            fold.begin(which, 0)
        advance(4)

    for kind in range(2):
        row = 3 - kind
        grad_norm_out[kind : kind + 1, 0:part] = sums_mine[5, row : row + 1, lanes(core, part)]
        grad_norm_out[kind : kind + 1, part:width] = sums_mine[4, row : row + 1, lanes(core, part)]
        grad_norm_out[kind : kind + 1, width:] = sums_mine[3, row : row + 1, lanes(core, half)]
    advance(len(due))
    if gather:
        start = 0
        for slot in range(3):
            rows = fold.counts[slot]
            act_three[kept + start : kept + start + rows, half : half + width] = fold.result(slot)
            start += rows
        leave = pltpu.make_async_copy(
            act_three.at[pl.ds(kept, start), pl.ds(half, width)], grads_out, sem_local.at[3]
        )
        leave.start()
        leave.wait()
        fold.drain()
    else:
        outs = [
            pltpu.make_async_copy(weight_rows(ref, slice(None), rows), out, sem_local.at[slot])
            for slot, (ref, rows, out) in enumerate(
                zip((w_first, mid_wide, w_last), [weight.shape[-2] for weight in weights], grads_out)
            )
        ]
        for copy in outs:
            copy.start()
        for copy in outs:
            copy.wait()
    head_leave.wait()
    for copy in to_mate + head_moves:
        copy.wait_send()


def client_pass(gather, classes, features, labels, flag, params, head_low, weights):
    pixels, half = features.shape
    images = labels.shape[1]
    count_rows, channels = pixels // 2, 2 * half
    width = params.shape[1] - half
    head_rows = head_low.shape[0]
    mine_images = images // 2
    line = SIDE * mine_images
    middle = 9 * width
    blocks = 32
    group = channels // SPOTS[0]
    vmem = pl.BlockSpec(memory_space=pltpu.VMEM)
    smem = pl.BlockSpec(memory_space=pltpu.SMEM)
    spots = SPOTS + (2,)
    scratch = [
        pltpu.VMEM((count_rows, channels), low_type),
        pltpu.VMEM(spots + (line, group), low_type),
        pltpu.VMEM(spots + (channels // blocks, width), low_type),
        pltpu.VMEM(spots + (middle // blocks, width), low_type),
        pltpu.VMEM(spots + (channels // blocks, width), low_type),
        pltpu.VMEM((count_rows, width), wide),
        pltpu.VMEM((count_rows, width), wide),
        pltpu.VMEM((count_rows, channels), wide),
        pltpu.VMEM((count_rows + 2 * line, width), low_type),
        pltpu.VMEM((count_rows + 2 * line, width), low_type),
        pltpu.VMEM((count_rows, width), low_type),
        pltpu.VMEM((count_rows, LANES), wide),
        pltpu.VMEM((2,) + params.shape, wide),
        pltpu.VMEM((2, head_rows, half), low_type),
        pltpu.VMEM((mine_images, channels), wide),
        pltpu.VMEM((mine_images, half), low_type),
        pltpu.VMEM((2, mine_images, half), low_type),
        pltpu.VMEM((2, head_rows, mine_images), low_type),
        pltpu.VMEM((6, 8, channels), wide),
        pltpu.VMEM((6, 8, channels), wide),
        pltpu.VMEM((24, max(width, group)), wide),
        pltpu.VMEM((3, 8, channels), wide),
        pltpu.SemaphoreType.DMA((11,)),
        pltpu.SemaphoreType.DMA((2, 6)),
        pltpu.SemaphoreType.DMA((2, 7)),
    ]
    any_space = pl.BlockSpec(memory_space=pl.ANY)
    if gather:
        counts = (channels // blocks, middle // blocks, channels // blocks)
        scratch += [pltpu.SemaphoreType.DMA((2, 3, 3))]
        scratch += [pltpu.SemaphoreType.DMA((2, 4, 6)) for _ in range(2)]
        scratch += [pltpu.SemaphoreType.DMA((2, 4, 3))]
        scratch += [pltpu.VMEM((4, 2, 2, rows, width), low_type) for rows in counts[1:]]
        for lead in ((4, 2), (4,), (4,)):
            scratch += [pltpu.VMEM(lead + (rows, width), low_type) for rows in counts]
        scratch += [pltpu.SemaphoreType.DMA((2, 4, 3))]
        scratch += [pltpu.SemaphoreType.DMA((2, 4, 6)) for _ in range(3)]
        grads_shape = [jax.ShapeDtypeStruct((sum(counts), width), wide)]
        grads_specs = [any_space]
    else:
        grads_shape = [jax.ShapeDtypeStruct(weight.shape, low_type) for weight in weights]
        grads_specs = [any_space] * 3
    return pl.pallas_call(
        functools.partial(client_kernel, gather, images, classes),
        out_shape=grads_shape
        + [
            jax.ShapeDtypeStruct(params.shape, wide),
            jax.ShapeDtypeStruct((head_rows, half), wide),
            jax.ShapeDtypeStruct((8, LANES), wide),
        ],
        in_specs=[any_space, vmem, smem, vmem, vmem] + [any_space] * len(weights),
        out_specs=grads_specs + [vmem, any_space, vmem],
        scratch_shapes=scratch,
        compiler_params=pltpu.CompilerParams(
            collective_id=0, has_side_effects=True, vmem_limit_bytes=VMEM_BYTES
        ),
    )(features, labels, flag, params, head_low, *weights)


def adam_update(param, grad, first, second, rate, decay):
    first = adam_first * first + (1.0 - adam_first) * grad
    second = adam_second * second + (1.0 - adam_second) * grad * grad
    first_hat = first / (1.0 - adam_first**STEP)
    second_hat = second / (1.0 - adam_second**STEP)
    return (
        param - rate * (first_hat / (jnp.sqrt(second_hat) + adam_epsilon) + decay * param),
        first,
        second,
    )
class GramSum:
    def __init__(self, place, data, total, boxes, sems):
        self.place = place
        self.data = data
        self.total = total
        self.core_box, self.near_box, self.far_box, self.z_box = boxes
        self.sems = sems
        self.copies = []
        self.sizes = (data.shape[0] // 72 * 40 // 32, data.shape[0] // 72 * 32 // 32)

    def rows(self, kind, core, z=None, first=None, second=None):
        size = self.sizes[kind]
        start = core * (16 * (self.sizes[0] + self.sizes[1])) + kind * 16 * self.sizes[0]
        count = 16 * size
        for number, spot, parts in ((4 * size, z, 4), (2 * size, first, 2), (size, second, 2)):
            if spot is None:
                break
            start, count = start + spot * number, number
        return pl.ds(pl.multiple_of(start, 8), count)

    def ways(self, kind):
        p = self.place
        x_way, y_way = (p.x, p.along_x()), (p.y, p.along_y())
        return (x_way, y_way) if kind == 0 else (y_way, x_way)

    def copy(self, phase, kind, turn, src, dst, client, core):
        sems = self.sems
        return remote(
            src, dst, sems.at[0, phase, kind, turn], sems.at[1, phase, kind, turn], client, core
        )

    def launch(self, copy):
        copy.start()
        self.copies.append(copy)

    def down(self, phase, kind, turn):
        p = self.place
        z = (p.others[::-1] + [p.z])[turn]
        (first, first_to), (second, second_to) = self.ways(kind)
        base = self.sizes[0] * kind
        if phase == 0:
            src = self.data.at[self.rows(kind, 1 - p.core, z), :]
            box = self.core_box.at[turn, pl.ds(4 * base, 4 * self.sizes[kind]), :]
            return self.copy(0, kind, turn, src, box, p.client, 1 - p.core)
        if phase == 1:
            src = self.data.at[self.rows(kind, p.core, z, 1 - first), :]
            box = self.near_box.at[turn, pl.ds(2 * base, 2 * self.sizes[kind]), :]
            return self.copy(1, kind, turn, src, box, first_to, p.core)
        if phase == 2:
            src = self.data.at[self.rows(kind, p.core, z, first, 1 - second), :]
            box = self.far_box.at[turn, pl.ds(base, self.sizes[kind]), :]
            return self.copy(2, kind, turn, src, box, second_to, p.core)
        src = self.data.at[self.rows(kind, p.core, z, first, second), :]
        box = self.z_box.at[turn, pl.ds(base, self.sizes[kind]), :]
        return self.copy(3, kind, turn, src, box, p.along_z(2 - turn), p.core)

    def down_step(self, phase, kind, turn):
        p = self.place
        z = (p.others[::-1] + [p.z])[turn]
        (first, _), (second, _) = self.ways(kind)
        self.down(phase, kind, turn).wait_recv()
        spots = (z, first, second)[: phase + 1]
        where = self.rows(kind, p.core, *spots)
        scale = (4, 2, 1)[phase]
        box = (self.core_box, self.near_box, self.far_box)[phase]
        self.data[where, :] += box[turn, pl.ds(scale * self.sizes[0] * kind, scale * self.sizes[kind]), :]
        if phase < 2 or turn < 3:
            self.launch(self.down(phase + 1, kind, turn))

    def up(self, phase, kind, turn):
        p = self.place
        z = ([p.z] + p.others)[turn]
        (first, first_to), (second, second_to) = self.ways(kind)
        if phase == 0:
            ref, to = self.total.at[self.rows(kind, p.core, p.z, first, second), :], p.along_z(turn)
        elif phase == 1:
            ref, to = self.total.at[self.rows(kind, p.core, z, first, second), :], second_to
        elif phase == 2:
            ref, to = self.total.at[self.rows(kind, p.core, z, first), :], first_to
        else:
            ref, to = self.total.at[self.rows(kind, p.core, z), :], p.client
        return self.copy(4 + phase, kind, turn, ref, ref, to, 1 - p.core if phase == 3 else p.core)

    def run(self, extra):
        extra = list(extra)
        kinds = (0, 1)
        for turn in range(4):
            for kind in kinds:
                self.launch(self.down(0, kind, turn))
        for turn in range(6):
            if extra:
                extra.pop(0)()
            for kind in kinds:
                for phase in range(3):
                    if 0 <= turn - phase < 4:
                        self.down_step(phase, kind, turn - phase)
        p = self.place
        for kind in kinds:
            (first, _), (second, _) = self.ways(kind)
            where = self.rows(kind, p.core, p.z, first, second)
            value = self.data[where, :]
            for turn in range(3):
                self.down(3, kind, turn).wait_recv()
                value += self.z_box[turn, pl.ds(self.sizes[0] * kind, self.sizes[kind]), :]
            self.total[where, :] = value
            self.launch(self.up(1, kind, 0))
            for turn in range(3):
                self.launch(self.up(0, kind, turn))
        for turn in range(6):
            for kind in kinds:
                if 1 <= turn < 4:
                    self.up(0, kind, turn - 1).wait_recv()
                    self.launch(self.up(1, kind, turn))
                if 1 <= turn < 5:
                    self.up(1, kind, turn - 1).wait_recv()
                    self.launch(self.up(2, kind, turn - 1))
                if 2 <= turn:
                    self.up(2, kind, turn - 2).wait_recv()
                    self.launch(self.up(3, kind, turn - 2))
        for turn in range(4):
            for kind in kinds:
                self.up(3, kind, turn).wait_recv()

    def drain(self):
        for copy in self.copies:
            copy.wait_send()


class TileSum:
    def __init__(self, place, tiles, boxes, sems):
        self.place = place
        self.tiles = tiles
        self.boxes = boxes
        self.sems = sems

    def copy(self, stage, box):
        p = self.place
        to = (p.client, p.along_x(), p.along_y()) + tuple(p.along_z(step) for step in range(3))
        core = 1 - p.core if box == 0 else p.core
        return remote(
            self.tiles.at[stage], self.boxes.at[box], self.sems.at[0, box], self.sems.at[1, box], to[box], core
        )

    def steps(self):
        def start():
            self.copy(0, 0).start()

        def pair(stage):
            self.copy(stage, stage).wait_recv()
            self.tiles[stage + 1] = self.tiles[stage] + self.boxes[stage]
            if stage < 2:
                self.copy(stage + 1, stage + 1).start()
            else:
                for step in range(3):
                    self.copy(3, 3 + step).start()

        return [start] + [functools.partial(pair, stage) for stage in range(3)]

    def result(self):
        for step in range(3):
            self.copy(3, 3 + step).wait_recv()
        return (self.tiles[3] + self.boxes[3]) + (self.boxes[4] + self.boxes[5])

    def drain(self):
        for stage in range(3):
            self.copy(stage, stage).wait_send()
        for step in range(3):
            self.copy(3, 3 + step).wait_send()


def dot_high(left, right):
    return jnp.dot(left, right, precision=lax.Precision.HIGH, preferred_element_type=wide)


def base_kernel(
    ratios,
    sizes,
    master,
    momentum,
    anchor,
    loss_in,
    grads,
    grad_norm,
    grad_head,
    *rest,
):
    place = Place()
    rest = list(rest)

    def take(count):
        taken = rest[:count]
        del rest[:count]
        return taken

    norms, heads = take(3), take(3)
    base_new, momentum_new, base_low, loss_out = take(4)
    norms_new, heads_new = take(3), take(3)
    gram, gram_total = take(2)
    gram_boxes = take(4)
    grams, iterate, tiles, tile_boxes = take(4)
    gram_sems, tile_sems = take(2)

    place.greet(True)
    tiles[0] = loss_in[...]
    tile_sum = TileSum(place, tiles, tile_boxes, tile_sems)
    extra = tile_sum.steps()
    extra.pop(0)()

    bounds = [0]
    for size in sizes:
        bounds.append(bounds[-1] + size)
    width = master.shape[1]
    part = width // 2
    for slot in range(3):
        rows = slice(bounds[slot], bounds[slot + 1])
        grad = grads[rows, :] + prox_weight * (master[rows, :] - anchor[rows, :])
        fresh = momentum_decay * momentum[rows, :] + grad
        momentum_new[rows, :] = fresh
        partial = lax.dot_general(
            fresh, fresh, (((0,), (0,)), ((), ())), precision=precise, preferred_element_type=wide
        )
        start = 3 * part * slot
        gram[start : start + part, :] = partial[:part, :part]
        gram[start + part : start + 2 * part, :] = partial[:part, part:]
        gram[start + 2 * part : start + 3 * part, :] = partial[part:, part:]

    gram_sum = GramSum(place, gram, gram_total, gram_boxes, gram_sems)

    def spare():
        head_rows = heads[0].shape[0]
        fresh = adam_update(
            heads[0][...], grad_head[0:head_rows, :], heads[1][...], heads[2][...], head_rate, head_decay
        )
        for out, value in zip(heads_new, fresh):
            out[...] = value
        fresh = adam_update(norms[0][...], grad_norm[...], norms[1][...], norms[2][...], norm_rate, 0.0)
        for out, value in zip(norms_new, fresh):
            out[...] = value

    gram_sum.run([spare] + extra)
    loss_out[...] = tile_sum.result()

    spots = lax.broadcasted_iota(jnp.int32, (part, part), 0)
    diagonal = spots == lax.broadcasted_iota(jnp.int32, (part, part), 1)
    iterate[...] = jnp.zeros_like(iterate)
    for slot in range(3):
        start = 3 * part * slot
        corner = gram_total[start : start + part, :]
        side = gram_total[start + part : start + 2 * part, :]
        end = gram_total[start + 2 * part : start + 3 * part, :]
        trace = jnp.sum(jnp.where(diagonal, corner + end, 0.0))
        factor = 1.0 / (jnp.sqrt(trace) + 1e-07)
        square = factor * factor
        grams[slot, :part, :part] = corner * square
        grams[slot, :part, part:] = side * square
        grams[slot, part:, :part] = side.T * square
        grams[slot, part:, part:] = end * square
        rows = slice(bounds[slot], bounds[slot + 1])
        iterate[slot, : bounds[slot + 1] - bounds[slot], :] = momentum_new[rows, :] * factor

    def turn(slot, last):
        current = grams[slot]
        mixed = schulz_second * current + schulz_third * dot_high(current, current)
        held = iterate[slot]
        iterate[slot] = schulz_first * held + dot_high(held, mixed)
        if not last:
            once = schulz_first * current + dot_high(current, mixed)
            grams[slot] = schulz_first * once + dot_high(once, mixed)

    def one(count, carry):
        turn(lax.rem(count, 3), False)
        return carry

    lax.fori_loop(0, 3 * (NS_STEPS - 1), one, 0)

    def final(slot, carry):
        turn(slot, True)
        return carry

    lax.fori_loop(0, 3, final, 0)
    for slot in range(3):
        rows = slice(bounds[slot], bounds[slot + 1])
        held = master[rows, :]
        ortho = iterate[slot, : bounds[slot + 1] - bounds[slot], :] * ratios[slot]
        fresh = held - muon_rate * (ortho + muon_decay * held)
        base_new[rows, :] = fresh
        base_low[rows, :] = fresh.astype(low_type)
    gram_sum.drain()
    tile_sum.drain()


def base_pass(ratios, sizes, master, momentum, anchor, loss_tile, grads, grad_norm, grad_head, norms, heads):
    rows, width = master.shape
    part = width // 2
    vmem = pl.BlockSpec(memory_space=pltpu.VMEM)
    share = 9 * part // 32
    scratch = [pltpu.VMEM((9 * part, part), wide)] * 2
    scratch += [pltpu.VMEM((4, size, part), wide) for size in (4 * share, 2 * share, share)]
    scratch += [pltpu.VMEM((3, share, part), wide)]
    scratch += [
        pltpu.VMEM((3, width, width), wide),
        pltpu.VMEM((3, max(sizes), width), wide),
        pltpu.VMEM((4, 8, LANES), wide),
        pltpu.VMEM((6, 8, LANES), wide),
        pltpu.SemaphoreType.DMA((2, 8, 2, 4)),
        pltpu.SemaphoreType.DMA((2, 6)),
    ]
    block = jax.ShapeDtypeStruct((rows, width), wide)
    outs = [block, block, jax.ShapeDtypeStruct((rows, width), low_type), jax.ShapeDtypeStruct((8, LANES), wide)]
    outs += [jax.ShapeDtypeStruct(value.shape, wide) for value in norms + heads]
    operands = [master, momentum, anchor, loss_tile, grads, grad_norm, grad_head] + norms + heads
    return pl.pallas_call(
        functools.partial(base_kernel, ratios, sizes),
        out_shape=outs,
        in_specs=[vmem] * len(operands),
        out_specs=[vmem] * len(outs),
        scratch_shapes=scratch,
        compiler_params=pltpu.CompilerParams(
            collective_id=1, has_side_effects=True, vmem_limit_bytes=VMEM_BYTES
        ),
    )(*operands)


def gram_of(section):
    return lax.dot_general(section, section, (((0,), (0,)), ((), ())), precision=precise)


def square(gram):
    return jnp.dot(gram, gram, precision=precise)


def times_poly(left, mixed):
    return schulz_first * left + jnp.dot(left, mixed, precision=precise)


def schulz(sections):
    raw_grams = lax.psum(tuple(gram_of(section) for section in sections), ("client", "chan"))
    factors = [1.0 / (jnp.sqrt(jnp.trace(gram)) + 1e-07) for gram in raw_grams]
    current = [section * factor for section, factor in zip(sections, factors)]
    grams = [gram * (factor * factor) for gram, factor in zip(raw_grams, factors)]
    for turn in range(NS_STEPS):
        mixed = [schulz_second * gram + schulz_third * square(gram) for gram in grams]
        current = [times_poly(current[slot], mixed[slot]) for slot in range(3)]
        if turn + 1 < NS_STEPS:
            grams = [
                times_poly(times_poly(grams[slot], mixed[slot]), mixed[slot]) for slot in range(3)
            ]
    return current


def base_far(ratios, bounds, master, momentum, anchor, loss_tile, grads):
    sums = [
        lax.psum_scatter(flat_rows(grad).astype(wide), ("client", "chan"), scatter_dimension=0, tiled=True)
        for grad in grads
    ]
    grad_base = jnp.concatenate(sums, axis=0) + prox_weight * (master - anchor)
    momentum_new = momentum_decay * momentum + grad_base
    current = schulz([momentum_new[bounds[slot] : bounds[slot + 1]] for slot in range(3)])
    ortho = jnp.concatenate([current[slot] * ratios[slot] for slot in range(3)], axis=0)
    base_new = master - muon_rate * (ortho + muon_decay * master)
    return base_new, momentum_new, base_new.astype(low_type), lax.psum(loss_tile, ("client", "chan"))


def on_device(
    features,
    labels,
    mask,
    base_master,
    base_momentum,
    global_base,
    norm_params,
    norm_first,
    norm_second,
    head,
    head_first,
    head_second,
):
    halves = lax.axis_size("chan")
    blocks = lax.axis_size("client") * halves
    half = features.shape[2]
    width = base_master.shape[2]
    channels = half * halves
    classes = head.shape[2]
    rows_first = channels // blocks
    rows_mid = 9 * width // blocks
    sizes = (rows_first, rows_mid, rows_first)
    bounds = (0, rows_first, rows_first + rows_mid, base_master.shape[1])
    ratio = (channels / width) ** 0.5
    ratios = (ratio, 3.0, ratio)
    master, momentum, anchor = base_master[0], base_momentum[0], global_base[0]
    norms = [value[0, :, 0, :] for value in (norm_params, norm_first, norm_second)]
    heads = [value[0].T for value in (head, head_first, head_second)]
    head_low = jnp.pad(heads[0].astype(low_type), ((0, -classes % 16), (0, 0)))
    near = lax.axis_size("client") == SPOTS[0] * SPOTS[1] * SPOTS[2]
    if near:
        weights = [master]
    else:
        low_master = master.astype(low_type)
        weights = [
            lax.all_gather(low_master[bounds[slot] : bounds[slot + 1]], ("client", "chan"), axis=0, tiled=True)
            for slot in range(3)
        ]
        weights = [weight.reshape(SPOTS + (2, weight.shape[0] // 32, width)) for weight in weights]
    *grads, grad_norm, grad_head, loss_tile = client_pass(
        near, classes, features[0], labels, mask, norms[0], head_low, weights
    )
    if near:
        base_new, momentum_new, base_low, loss_tile, *fresh = base_pass(
            ratios, sizes, master, momentum, anchor, loss_tile, grads[0], grad_norm, grad_head, norms, heads
        )
        norms, heads = fresh[:3], fresh[3:]
    else:
        base_new, momentum_new, base_low, loss_tile = base_far(
            ratios, bounds, master, momentum, anchor, loss_tile, grads
        )
        norms = adam_update(norms[0], grad_norm, norms[1], norms[2], norm_rate, 0.0)
        heads = adam_update(heads[0], grad_head[:classes], heads[1], heads[2], head_rate, head_decay)
    return (
        loss_tile[0, 0:2],
        base_new[None],
        momentum_new[None],
        base_low[None],
        *[value[None, :, None, :] for value in norms],
        *[value.T[None] for value in heads],
    )


def solution(mesh):
    wide_block = P(("client", "chan"), None, None)
    norm_block = P("client", None, "chan", None)
    head_block = P("client", "chan", None)
    return jax.shard_map(
        on_device,
        mesh=mesh,
        in_specs=(P("client", None, "chan"), P("client", None), P("client"))
        + (wide_block,) * 3
        + (norm_block,) * 3
        + (head_block,) * 3,
        out_specs=(P(),) + (wide_block,) * 3 + (norm_block,) * 3 + (head_block,) * 3,
        check_vma=False,
    )
```

```python
import functools

import jax
import jax.numpy as jnp
from jax import lax
from jax.experimental import pallas as pl
from jax.experimental.layout import Layout, with_layout_constraint
from jax.experimental.pallas import tpu as pltpu
from jax.sharding import PartitionSpec as P

NS_STEPS = 5
STEP = 10

low_type = jnp.bfloat16
wide = jnp.float32
MESH = pl.DeviceIdType.MESH
precise = lax.Precision.HIGHEST
norm_epsilon = 1e-05
prox_weight = 0.05
momentum_decay = 0.95
muon_rate = 0.3
muon_decay = 0.1
schulz_first = 3.4445
schulz_second = -4.775
schulz_third = 2.0315
adam_first = 0.9
adam_second = 0.95
adam_epsilon = 1e-08
head_rate = 0.01
head_decay = 0.05
norm_rate = 0.5

SIDE = 7
PIXELS = SIDE * SIDE
LANES = 128
SPOTS = (4, 2, 2)
VMEM_BYTES = 62 * 2**20


def dot_nn(left, right):
    return jnp.dot(left, right, preferred_element_type=wide)


def dot_nt(left, right):
    return lax.dot_general(left, right, (((1,), (1,)), ((), ())), preferred_element_type=wide)


def dot_tn(left, right):
    return lax.dot_general(left, right, (((0,), (0,)), ((), ())), preferred_element_type=wide)


def flat_rows(block):
    return block.reshape(-1, block.shape[-1])


def sigmoid(value):
    return 0.5 * jnp.tanh(0.5 * value) + 0.5


def fold_rows(value):
    return jnp.sum(value.reshape(value.shape[0] // 8, 8, value.shape[1]), axis=0)


def column_sum(value):
    return jnp.sum(value, axis=0, keepdims=True)


def remote(src, dst, send_sem, recv_sem, client, core):
    return pltpu.make_async_remote_copy(
        src_ref=src,
        dst_ref=dst,
        send_sem=send_sem,
        recv_sem=recv_sem,
        device_id=(client, core),
        device_id_type=MESH,
    )


class Place:
    def __init__(self):
        self.client = lax.axis_index("client")
        self.core = lax.axis_index("chan")
        self.z = self.client // 4
        self.y = (self.client // 2) % 2
        self.x = self.client % 2
        self.others = [
            self.z + 1 - 2 * (self.z % 2),
            (self.z + 2) % 4,
            3 - self.z,
        ]

    def at(self, z, y, x):
        return z * 4 + y * 2 + x

    def along_x(self):
        return self.at(self.z, self.y, 1 - self.x)

    def along_y(self):
        return self.at(self.z, 1 - self.y, self.x)

    def along_z(self, step):
        return self.at(self.others[step], self.y, self.x)

    def greet(self, whole):
        barrier = pltpu.get_barrier_semaphore()
        pairs = [(self.client, 1 - self.core)]
        if whole:
            pairs += [(self.along_x(), self.core), (self.along_y(), self.core)]
            pairs += [(self.along_z(step), self.core) for step in range(3)]
        for pair in pairs:
            pl.semaphore_signal(barrier, inc=1, device_id=pair, device_id_type=MESH)
        pl.semaphore_wait(barrier, len(pairs))


def cut_rows(counts):
    pieces = []
    for slot, rows in enumerate(counts):
        middle = (rows // 16 + 1) // 2 * 16
        pieces.append((slot, 0, middle, 0))
        pieces.append((slot, middle, rows - middle, 1))
    return pieces


class Spread:
    def __init__(self, place, weights, sems):
        self.place = place
        self.weights = weights
        self.pieces = cut_rows([weight.shape[-2] for weight in weights])
        self.z_sems, self.near_sems, self.far_sems, self.core_sems = sems
        self.order = [place.z] + place.others
        self.copies = []

    def z_copy(self, step, slot):
        p = self.place
        ref = self.weights[slot].at[p.z, p.y, p.x, p.core]
        sems = self.z_sems
        return remote(ref, ref, sems.at[0, step, slot], sems.at[1, step, slot], p.along_z(step), p.core)

    def near_copy(self, turn, number):
        p = self.place
        slot, start, count, way = self.pieces[number]
        ref = self.weights[slot].at[self.order[turn], p.y, p.x, p.core, pl.ds(start, count), :]
        sems = self.near_sems
        return remote(
            ref, ref, sems.at[0, turn, number], sems.at[1, turn, number], (p.along_x, p.along_y)[way](), p.core
        )

    def far_copy(self, turn, number):
        p = self.place
        slot, start, count, way = self.pieces[number]
        rows = pl.ds(start, count)
        spot = self.order[turn]
        if way == 0:
            ref = self.weights[slot].at[spot, p.y, :, p.core, rows, :]
        else:
            ref = self.weights[slot].at[spot, :, p.x, p.core, rows, :]
        sems = self.far_sems
        return remote(
            ref, ref, sems.at[0, turn, number], sems.at[1, turn, number], (p.along_y, p.along_x)[way](), p.core
        )

    def core_copy(self, turn, slot):
        p = self.place
        ref = self.weights[slot].at[self.order[turn], :, :, p.core]
        sems = self.core_sems
        return remote(ref, ref, sems.at[0, turn, slot], sems.at[1, turn, slot], p.client, 1 - p.core)

    def launch(self, copy):
        copy.start()
        self.copies.append(copy)

    def begin(self, master):
        p = self.place
        start = 0
        for slot in range(3):
            rows = self.weights[slot].shape[-2]
            self.weights[slot][p.z, p.y, p.x, p.core] = master[start : start + rows, :].astype(low_type)
            start += rows
        for step in range(3):
            self.launch(self.z_copy(step, 0))
        self.near_start(0)

    def near_start(self, slot):
        for number in (2 * slot, 2 * slot + 1):
            self.launch(self.near_copy(0, number))

    def steps(self):
        near, far, core, start = self.near_step, self.far_step, self.core_step, self.near_start
        groups = [
            [(far, 0, 0), (start, 1)],
            [(near, 1, 0)],
            [(near, 2, 0), (near, 3, 0)],
            [(far, 1, 0), (core, 0, 0), (far, 0, 1)],
            [(far, 2, 0), (far, 3, 0), (core, 1, 0)],
            [(core, 2, 0), (core, 3, 0), (near, 1, 1), (start, 2)],
            [(core, 0, 1), (near, 2, 1)],
            [(far, 1, 1), (near, 3, 1)],
            [(core, 1, 1), (far, 2, 1), (far, 0, 2)],
            [(far, 3, 1), (core, 2, 1), (near, 1, 2)],
            [(core, 3, 1), (core, 0, 2), (near, 2, 2)],
            [(far, 1, 2), (near, 3, 2)],
            [(core, 1, 2), (far, 2, 2)],
            [(far, 3, 2), (core, 2, 2)],
            [(core, 3, 2)],
        ]
        return [[functools.partial(*step) for step in group] for group in groups]

    def near_step(self, turn, slot):
        self.z_copy(turn - 1, slot).wait_recv()
        for number in (2 * slot, 2 * slot + 1):
            self.launch(self.near_copy(turn, number))
        if slot < 2:
            self.launch(self.z_copy(turn - 1, slot + 1))

    def far_step(self, turn, slot):
        for number in (2 * slot, 2 * slot + 1):
            self.near_copy(turn, number).wait_recv()
            self.launch(self.far_copy(turn, number))

    def core_step(self, turn, slot):
        for number in (2 * slot, 2 * slot + 1):
            self.far_copy(turn, number).wait_recv()
        self.launch(self.core_copy(turn, slot))

    def arrive(self, slot):
        for turn in range(4):
            self.core_copy(turn, slot).wait_recv()

    def drain(self):
        for copy in self.copies:
            copy.wait_send()


class Fold:
    def __init__(self, place, grads, counts, parts):
        self.place = place
        self.grads = grads
        self.counts = counts
        self.pieces = cut_rows(counts)
        self.core_boxes = [parts[1], parts[0], parts[1]]
        self.near_boxes, self.far_boxes, self.z_boxes = [parts[3 * k + 2 : 3 * k + 5] for k in range(3)]
        self.core_sems, self.near_sems, self.far_sems, self.z_sems = parts[11:]
        self.copies = []

    def core_copy(self, which, slot):
        p = self.place
        sems = self.core_sems
        return remote(
            self.grads[slot].at[which, :, :, 1 - p.core, pl.ds(0, self.counts[slot]), :],
            self.core_boxes[slot].at[which],
            sems.at[0, which, slot],
            sems.at[1, which, slot],
            p.client,
            1 - p.core,
        )

    def near_copy(self, which, number):
        p = self.place
        slot, start, count, way = self.pieces[number]
        rows = pl.ds(start, count)
        if way == 0:
            ref = self.grads[slot].at[which, :, 1 - p.x, p.core, rows, :]
        else:
            ref = self.grads[slot].at[which, 1 - p.y, :, p.core, rows, :]
        box = self.near_boxes[slot].at[which, :, rows, :]
        sems = self.near_sems
        return remote(
            ref, box, sems.at[0, which, number], sems.at[1, which, number], (p.along_x, p.along_y)[way](), p.core
        )

    def far_copy(self, which, number):
        p = self.place
        slot, start, count, way = self.pieces[number]
        rows = pl.ds(start, count)
        if way == 0:
            ref = self.grads[slot].at[which, 1 - p.y, p.x, p.core, rows, :]
        else:
            ref = self.grads[slot].at[which, p.y, 1 - p.x, p.core, rows, :]
        box = self.far_boxes[slot].at[which, rows, :]
        sems = self.far_sems
        return remote(
            ref, box, sems.at[0, which, number], sems.at[1, which, number], (p.along_y, p.along_x)[way](), p.core
        )

    def z_copy(self, which, sender, number):
        p = self.place
        slot, start, count, _ = self.pieces[number]
        rows = pl.ds(start, count)
        sems = self.z_sems
        return remote(
            self.grads[slot].at[which, p.y, p.x, p.core, rows, :],
            self.z_boxes[slot].at[sender, rows, :],
            sems.at[0, which, number],
            sems.at[1, sender, number],
            p.at(which, p.y, p.x),
            p.core,
        )

    def launch(self, copy):
        copy.start()
        self.copies.append(copy)

    def begin(self, which, slot):
        self.launch(self.core_copy(which, slot))

    def turn(self, slot, turn):
        for lag, step in ((2, self.far_step), (1, self.near_step), (0, self.core_step)):
            if 0 <= turn - lag < 4:
                step(turn - lag, slot)

    def core_step(self, which, slot):
        p = self.place
        rows = pl.ds(0, self.counts[slot])
        self.core_copy(which, slot).wait_recv()
        where = (which, slice(None), slice(None), p.core, rows, slice(None))
        both = self.grads[slot][where].astype(wide) + self.core_boxes[slot][which].astype(wide)
        self.grads[slot][where] = both.astype(low_type)
        for number in (2 * slot, 2 * slot + 1):
            self.launch(self.near_copy(which, number))

    def near_step(self, which, slot):
        p = self.place
        for number in (2 * slot, 2 * slot + 1):
            _, start, count, way = self.pieces[number]
            rows = pl.ds(start, count)
            self.near_copy(which, number).wait_recv()
            if way == 0:
                where = (which, slice(None), p.x, p.core, rows, slice(None))
            else:
                where = (which, p.y, slice(None), p.core, rows, slice(None))
            both = self.grads[slot][where].astype(wide) + self.near_boxes[slot][which, :, rows, :].astype(wide)
            self.grads[slot][where] = both.astype(low_type)
            self.launch(self.far_copy(which, number))

    def far_step(self, which, slot):
        p = self.place
        for number in (2 * slot, 2 * slot + 1):
            _, start, count, way = self.pieces[number]
            rows = pl.ds(start, count)
            self.far_copy(which, number).wait_recv()
            where = (which, p.y, p.x, p.core, rows, slice(None))
            both = self.grads[slot][where].astype(wide) + self.far_boxes[slot][which, rows, :].astype(wide)
            self.grads[slot][where] = both.astype(low_type)

            @pl.when(p.z != which)
            def _():
                self.z_copy(which, p.z, number).start()

    def result(self, slot):
        p = self.place
        rows = pl.ds(0, self.counts[slot])
        self.z_boxes[slot][p.z] = self.grads[slot][p.z, p.y, p.x, p.core, rows, :]
        for sender in range(4):

            @pl.when(p.z != sender)
            def _():
                for number in (2 * slot, 2 * slot + 1):
                    self.z_copy(sender, sender, number).wait_recv()

        total = self.z_boxes[slot][0].astype(wide)
        for sender in range(1, 4):
            total += self.z_boxes[slot][sender].astype(wide)
        return total

    def drain(self):
        for copy in self.copies:
            copy.wait_send()
        for which in range(4):

            @pl.when(self.place.z != which)
            def _():
                for number in range(6):
                    self.z_copy(which, self.place.z, number).wait_send()


def norm_stats(mine, theirs, count):
    gap = mine[0:1] - theirs[0:1]
    mean = 0.5 * (mine[0:1] + theirs[0:1])
    spread = mine[1:2] + theirs[1:2] + gap * gap * (0.5 * count)
    return mean, lax.rsqrt(spread / (2.0 * count) + norm_epsilon)


def client_kernel(
    gather,
    images,
    classes,
    features,
    labels,
    flag,
    params,
    head,
    *rest,
):
    if gather:
        master, *rest = rest
    else:
        first_in, middle_in, last_in, *rest = rest
    if gather:
        grads_out, *rest = rest
    else:
        grads_out, rest = rest[:3], rest[3:]
    (
        grad_norm_out,
        grad_head_out,
        loss_out,
        x_all,
        mid_wide,
        w_first,
        w_middle,
        w_last,
        act_one,
        act_two,
        act_three,
        taps_one,
        taps_two,
        hidden_two,
        stage,
        params_all,
        head_all,
        grad_pool,
        pool_send,
        pool_all,
        logit_grads,
        sums_mine,
        sums_theirs,
        shift,
        fwd_stats,
        sem_local,
        sem_swap,
        sem_misc,
        *near_parts,
    ) = rest
    place = Place()
    core = place.core
    mate = (place.client, 1 - core)
    count_rows, channels = x_all.shape
    half = channels // 2
    width = act_one.shape[1]
    part = width // 2
    mine_images = images // 2
    line = SIDE * mine_images
    total_rows = 2.0 * count_rows

    def tile(index):
        return pl.ds(pl.multiple_of(index * line, line), line)

    def lanes(index, size):
        return pl.ds(pl.multiple_of(index * size, size), size)

    place.greet(gather)

    quarter = half // 2
    own_rows = pl.ds(pl.multiple_of(core * count_rows, count_rows), count_rows)
    mate_rows = pl.ds(pl.multiple_of((1 - core) * count_rows, count_rows), count_rows)
    top_rows = pl.ds(0, count_rows)
    own_copies = [
        pltpu.make_async_copy(
            features.at[own_rows, pl.ds(0, quarter)], hidden_two, sem_local.at[0]
        )
    ]
    for index in range(SIDE):
        rows = pl.ds(pl.multiple_of(core * count_rows + index * line, line), line)
        own_copies.append(
            pltpu.make_async_copy(
                features.at[rows, pl.ds(quarter, quarter)],
                mid_wide.at[0, index // 4, (index // 2) % 2, index % 2],
                sem_local.at[1 + index],
            )
        )
    per_kind = params.shape[0] // 2
    for kind in range(2):
        rows = [params[kind * per_kind + spot : kind * per_kind + spot + 1, :] for spot in range(per_kind)]
        params_all[core, kind : kind + 1, :] = jnp.concatenate(rows, axis=1)
    head_all[core] = jnp.zeros(head_all.shape[1:], low_type)
    for spot in range(half // LANES):
        head_all[core, 0:classes, spot * LANES : (spot + 1) * LANES] = head[
            pl.ds(spot, classes, stride=half // LANES), :
        ].astype(low_type)
    to_mate = [
        remote(params_all.at[core], params_all.at[core], sem_misc.at[0, 0], sem_misc.at[1, 0], *mate),
        remote(head_all.at[core], head_all.at[core], sem_misc.at[0, 1], sem_misc.at[1, 1], *mate),
    ]
    for side, buffer in enumerate((taps_one, taps_two)):
        to_mate.append(
            remote(
                features.at[mate_rows, pl.ds(side * quarter, quarter)],
                buffer.at[top_rows, :],
                sem_misc.at[0, 5 + side],
                sem_misc.at[1, 5 + side],
                *mate,
            )
        )
    for copy in to_mate + own_copies:
        copy.start()

    weights = (w_first, w_middle, w_last)
    if gather:
        spread = Spread(place, weights, near_parts[:4])
        held = act_three.at[pl.ds(0, master.shape[0]), pl.ds(0, width)]
        load = pltpu.make_async_copy(master, held, sem_local.at[8])
        load.start()
        load.wait()
        spread.begin(held)
        counts = [weight.shape[-2] for weight in weights]
        fold = Fold(place, (w_first, mid_wide, w_last), counts, near_parts[4:])
        due = spread.steps()
    else:
        loads = [
            pltpu.make_async_copy(src, dst, sem_local.at[8 + slot])
            for slot, (src, dst) in enumerate(zip((first_in, middle_in, last_in), weights))
        ]
        for load in loads:
            load.start()
        due = []

    def advance(count):
        for group in due[:count]:
            for step in group:
                step()
        del due[:count]

    def arrive(slot, left):
        if gather:
            advance(len(due) - left)
            spread.arrive(slot)
        else:
            loads[slot].wait()

    def fold_turn(slot, turn):
        if gather:
            fold.turn(slot, turn)

    def fold_begin(which, slot):
        if gather:
            fold.begin(which, slot)

    def zero_edges(buffer):
        edge = jnp.zeros((line,) + buffer.shape[1:], low_type)
        buffer[0:line, :] = edge
        buffer[line + count_rows : 2 * line + count_rows, :] = edge

    advance(3)
    for copy in own_copies:
        copy.wait()

    def turn_from(source, base):
        def turn(index, carry):
            stage[...] = source(lanes(index, LANES)).astype(wide)

            def pixel(spot, inner):
                x_all[
                    pl.ds(pl.multiple_of(spot * mine_images, mine_images), mine_images),
                    pl.ds(pl.multiple_of(base + index * LANES, LANES), LANES),
                ] = stage[pl.ds(spot, mine_images, stride=PIXELS), :].astype(low_type)
                return inner

            return lax.fori_loop(0, PIXELS, pixel, carry, unroll=7)

        return turn

    quarters = quarter // LANES
    own_base, mate_base = core * half, (1 - core) * half
    lax.fori_loop(0, quarters, turn_from(lambda columns: hidden_two[:, columns], own_base), 0)
    advance(1)
    lax.fori_loop(
        0,
        quarters,
        turn_from(lambda columns: mid_wide[0, :, :, :, :, columns].reshape(8 * line, LANES)[:count_rows], own_base + quarter),
        0,
    )
    advance(1)
    for copy in to_mate:
        copy.wait_recv()
    lax.fori_loop(0, quarters, turn_from(lambda columns: taps_one[0:count_rows, columns], mate_base), 0)
    advance(1)
    lax.fori_loop(0, quarters, turn_from(lambda columns: taps_two[0:count_rows, columns], mate_base + quarter), 0)
    zero_edges(taps_one)
    zero_edges(taps_two)
    arrive(0, 9)

    def swap(slot, size):
        return remote(
            sums_mine.at[slot, :, pl.ds(0, size)],
            sums_theirs.at[slot, :, pl.ds(0, size)],
            sem_swap.at[0, slot],
            sem_swap.at[1, slot],
            *mate,
        )

    def gain_bias(lower, upper):
        rows = []
        for kind in range(2):
            pieces = [params_all[side, kind : kind + 1, lower:upper] for side in range(2)]
            rows.append(jnp.concatenate(pieces, axis=1))
        return rows

    def collect(index, value, columns, size):
        @pl.when(index == 0)
        def _():
            shift[0:1, pl.ds(0, size)] = column_sum(fold_rows(value)) / value.shape[0]
            shift[8:24, pl.ds(0, size)] = jnp.zeros((16, size), wide)

        gap = value - shift[0:1, pl.ds(0, size)]
        shift[8:16, pl.ds(0, size)] += fold_rows(gap)
        shift[16:24, pl.ds(0, size)] += fold_rows(gap * gap)

    def close_stats(slot, columns, size):
        sum_gap = column_sum(shift[8:16, pl.ds(0, size)])
        sum_square = column_sum(shift[16:24, pl.ds(0, size)])
        sums_mine[slot, 0:1, columns] = shift[0:1, pl.ds(0, size)] + sum_gap / count_rows
        sums_mine[slot, 1:2, columns] = sum_square - sum_gap * sum_gap / count_rows

    def settle(slot, size):
        mean, scale = norm_stats(
            sums_mine[slot, 0:2, pl.ds(0, size)], sums_theirs[slot, 0:2, pl.ds(0, size)], float(count_rows)
        )
        fwd_stats[slot, 0:1, pl.ds(0, size)] = mean
        fwd_stats[slot, 1:2, pl.ds(0, size)] = scale

    whole_width = pl.ds(0, width)

    def first_tile(index, carry):
        value = dot_nn(x_all[tile(index), :], flat_rows(w_first[...]))
        act_one[tile(index), :] = value
        collect(index, value, whole_width, width)
        return carry

    for lower, upper in ((0, 2), (2, 4), (4, SIDE)):
        lax.fori_loop(lower, upper, first_tile, 0)
        advance(1)
    close_stats(0, whole_width, width)
    move = swap(0, width)
    move.start()
    move.wait()
    settle(0, width)

    gain_one, bias_one = gain_bias(0, part)
    gain_two, bias_two = gain_bias(part, width)
    gain_three, bias_three = gain_bias(width, width + half)

    def normal(act, slot, index):
        mean = fwd_stats[slot, 0:1, pl.ds(0, width)]
        return (act[tile(index), :] - mean) * fwd_stats[slot, 1:2, pl.ds(0, width)]

    def hide_one(index, carry):
        value = normal(act_one, 0, index) * gain_one + bias_one
        taps_one[pl.ds(pl.multiple_of((index + 1) * line, line), line), :] = (value * sigmoid(value)).astype(low_type)
        return carry

    lax.fori_loop(0, SIDE, hide_one, 0)
    arrive(1, 4)

    def shifted(buffer, index, down):
        return buffer[pl.ds(pl.multiple_of((index + down) * line, line), line), :]

    step = mine_images
    edge_rows = jnp.zeros((step, width), wide)

    def over_lines(lines, tap_of, multiply, axis):
        left = jnp.concatenate(lines, axis=1)
        value = multiply(left, jnp.concatenate([tap_of(down, 1) for down in range(3)], axis=axis))
        lower = multiply(left[: line - step], jnp.concatenate([tap_of(down, 0) for down in range(3)], axis=axis))
        upper = multiply(left[step:], jnp.concatenate([tap_of(down, 2) for down in range(3)], axis=axis))
        value += jnp.concatenate([edge_rows, lower], axis=0)
        return value + jnp.concatenate([upper, edge_rows], axis=0)

    def second_tile(index, carry):
        kernel = flat_rows(w_middle[...])

        def tap_of(down, over):
            tap = 3 * down + over
            return kernel[tap * width : (tap + 1) * width]

        value = over_lines([shifted(taps_one, index, down) for down in range(3)], tap_of, dot_nn, 0)
        act_two[tile(index), :] = value
        collect(index, value, whole_width, width)
        return carry

    for lower, upper in ((0, 2), (2, 4), (4, SIDE)):
        lax.fori_loop(lower, upper, second_tile, 0)
        advance(1)
    close_stats(1, whole_width, width)
    move_two = swap(1, width)
    move_two.start()
    move_two.wait()
    settle(1, width)

    def hide_two(index, carry):
        value = normal(act_two, 1, index) * gain_two + bias_two
        hidden_two[tile(index), :] = (value * sigmoid(value)).astype(low_type)
        return carry

    lax.fori_loop(0, SIDE, hide_two, 0)

    arrive(2, 0)
    groups = w_last.shape[0]
    group = channels // groups

    def third_group(which, carry):
        columns = lanes(which, group)

        def third_tile(index, inner):
            value = dot_nt(hidden_two[tile(index), :], flat_rows(w_last[which]))
            act_three[tile(index), columns] = value
            collect(index, value, columns, group)
            return inner

        lax.fori_loop(0, SIDE, third_tile, 0)
        close_stats(2, columns, group)
        return carry

    lax.fori_loop(0, groups, third_group, 0)
    move_three = swap(2, channels)
    move_three.start()
    move_three.wait()
    settle(2, channels)
    fwd_stats[2, 2:3, :] = gain_three
    fwd_stats[2, 3:4, :] = bias_three

    per_group = group // LANES

    def block_of(spot):
        return pl.ds(pl.multiple_of(spot * mine_images, mine_images), mine_images)

    def mid_line(which, index):
        return which, index // 4, (index // 2) % 2, index % 2, pl.ds(0, line)

    kept = channels // LANES * mine_images

    def gathered(kind):
        starts = range(kind * kept, (kind + 1) * kept, mine_images)
        return jnp.concatenate([stage[start : start + mine_images, :] for start in starts], axis=1)

    def emit(index, carry):
        columns = lanes(index, LANES)
        mean, scale = fwd_stats[2, 0:1, columns], fwd_stats[2, 1:2, columns]
        gain, bias = fwd_stats[2, 2:3, columns], fwd_stats[2, 3:4, columns]

        def pixels(row, sums):
            pooled, slopes, slopes_normed = sums
            found = []
            for spot in range(SIDE):
                where = block_of(row * SIDE + spot)
                normed = (act_three[where, columns] - mean) * scale
                total = normed * gain + bias + x_all[where, columns].astype(wide)
                sig = sigmoid(total)
                out = total * sig
                slope = sig + out * (1.0 - sig)
                found.append(slope.astype(low_type))
                pooled, slopes, slopes_normed = pooled + out, slopes + slope, slopes_normed + slope * normed
            mid_wide[mid_line(index // per_group, row) + (lanes(index % per_group, LANES),)] = jnp.concatenate(
                found, axis=0
            )
            return pooled, slopes, slopes_normed

        zero = jnp.zeros((mine_images, LANES), wide)
        pooled, slopes, slopes_normed = lax.fori_loop(0, SIDE, pixels, (zero, zero, zero))
        for kind, value in enumerate((pooled, slopes, slopes_normed)):
            stage[pl.ds(pl.multiple_of(kind * kept + index * mine_images, mine_images), mine_images), :] = value
        return carry

    lax.fori_loop(0, channels // LANES, emit, 0)

    pooled = (gathered(0) / PIXELS).astype(low_type)
    head_full = jnp.concatenate([head_all[0], head_all[1]], axis=1)
    logits = dot_nt(head_full, pooled)
    spots = lax.broadcasted_iota(jnp.int32, logits.shape, 0)
    inside = spots < classes
    first_labels, second_labels = labels[0:1, 0:mine_images], labels[0:1, mine_images:]
    onehot = (spots == jnp.where(core == 0, first_labels, second_labels)).astype(wide)
    top = jnp.max(jnp.where(inside, logits, -jnp.inf), axis=0, keepdims=True)
    powers = jnp.where(inside, jnp.exp(logits - top), 0.0)
    power_sum = jnp.sum(powers, axis=0, keepdims=True)
    picked = jnp.sum(logits * onehot, axis=0, keepdims=True)
    each_loss = top + jnp.log(power_sum) - picked
    taking = flag[0].astype(wide)
    tile_spots = lax.broadcasted_iota(jnp.int32, loss_out.shape, 1)
    loss_out[...] = jnp.where(tile_spots == 0, taking * jnp.sum(each_loss), taking * mine_images)
    grads = (taking / images * (powers / power_sum - onehot)).astype(low_type)
    grad_pool[...] = dot_tn(grads, head_full) / PIXELS
    logit_grads[core] = grads
    pool_all[core] = pooled[:, 0:half]
    pool_send[...] = pooled[:, half:]

    @pl.when(core == 1)
    def _():
        pool_all[core] = pooled[:, half:]
        pool_send[...] = pooled[:, 0:half]

    head_moves = [
        remote(pool_send, pool_all.at[core], sem_misc.at[0, 3], sem_misc.at[1, 3], *mate),
        remote(logit_grads.at[core], logit_grads.at[core], sem_misc.at[0, 4], sem_misc.at[1, 4], *mate),
    ]

    sums_mine[3, 0:1, :] = column_sum(grad_pool[...] * gathered(1))
    sums_mine[3, 1:2, :] = column_sum(grad_pool[...] * gathered(2))
    move_back = swap(3, channels)
    move_back.start()
    for copy in head_moves:
        copy.start()
    move_back.wait()

    def back_terms(slot, layer, size, gain):
        columns = pl.ds(0, size)
        sums = sums_mine[slot, 0:2, columns] + sums_theirs[slot, 0:2, columns]
        sums_mine[slot, 2:4, columns] = sums
        scale = fwd_stats[layer, 1:2, columns]
        return (
            scale * gain,
            scale * gain * sums[0:1] / total_rows,
            scale * scale * gain * sums[1:2] / total_rows,
        )

    first, second, third = back_terms(3, 2, channels, gain_three)
    fwd_stats[2, 4:5, :] = first
    fwd_stats[2, 5:6, :] = second
    fwd_stats[2, 6:7, :] = third

    def pull(index, carry):
        columns = lanes(index, LANES)
        mean = fwd_stats[2, 0:1, columns]
        first, second = fwd_stats[2, 4:5, columns], fwd_stats[2, 5:6, columns]
        third = fwd_stats[2, 6:7, columns]
        reach = grad_pool[:, columns] * first

        def pixels(row, inner):
            where = mid_line(index // per_group, row) + (lanes(index % per_group, LANES),)
            slopes = mid_wide[where].astype(wide)
            found = []
            for spot in range(SIDE):
                slope = slopes[spot * mine_images : (spot + 1) * mine_images]
                gap = act_three[block_of(row * SIDE + spot), columns] - mean
                found.append((reach * slope - second - third * gap).astype(low_type))
            mid_wide[where] = jnp.concatenate(found, axis=0)
            return inner

        return lax.fori_loop(0, SIDE, pixels, carry)

    lax.fori_loop(0, channels // LANES, pull, 0)
    for copy in head_moves:
        copy.wait_recv()
    head_grad = dot_nn(logit_grads[0], pool_all[0]) + dot_nn(logit_grads[1], pool_all[1])
    for spot in range(half // LANES):
        stage[pl.ds(spot, classes, stride=half // LANES), :] = head_grad[
            0:classes, spot * LANES : (spot + 1) * LANES
        ]
    head_space = stage.at[pl.ds(0, grad_head_out.shape[0]), :]
    head_leave = pltpu.make_async_copy(head_space, grad_head_out, sem_local.at[0])
    head_leave.start()

    def drop_into(index, value, act, slot, gain, bias, columns):
        normed = normal(act, slot, index)
        norm = normed * gain + bias
        sig = sigmoid(norm)
        grad = value * (sig + norm * sig * (1.0 - sig))
        act_three[tile(index), columns] = grad
        size = pl.ds(0, width)

        @pl.when(index == 0)
        def _():
            shift[8:24, size] = jnp.zeros((16, width), wide)

        shift[8:16, size] += fold_rows(grad)
        shift[16:24, size] += fold_rows(grad * normed)

    def close_back(slot):
        size = pl.ds(0, width)
        sums_mine[slot, 0:1, size] = column_sum(shift[8:16, size])
        sums_mine[slot, 1:2, size] = column_sum(shift[16:24, size])

    space_two, space_one = pl.ds(0, width), pl.ds(width, width)

    def back_two(index, carry):
        kernel = flat_rows(w_last[...])
        left = jnp.concatenate([mid_wide[mid_line(which, index)] for which in range(groups)], axis=1)
        value = dot_nn(left, kernel)
        drop_into(index, value, act_two, 1, gain_two, bias_two, space_two)
        return carry

    lax.fori_loop(0, SIDE, back_two, 0)
    close_back(4)
    move_back_two = swap(4, width)
    move_back_two.start()

    if gather:
        spread.drain()

    def weight_rows(ref, which, rows):
        return ref.at[which, :, :, :, pl.ds(0, rows), :]

    def put(ref, which, value):
        rows = value.shape[0] // 8
        ref[which, :, :, :, pl.ds(0, rows), :] = value.astype(low_type).reshape(2, 2, 2, rows, width)

    def expand_group(which, carry):
        left = mid_wide[which].reshape(8 * line, group)[:count_rows]
        put(w_last, which, dot_tn(left, hidden_two[...]))
        return carry

    for which in range(groups):
        expand_group(which, 0)
        fold_begin(which, 2)
        if which > 0:
            fold_turn(2, which - 1)
    move_back_two.wait()
    terms_two = back_terms(4, 1, width, gain_two)

    def back_act(terms, act, layer, index, columns):
        first, second, third = terms
        gap = act[tile(index), :] - fwd_stats[layer, 0:1, pl.ds(0, width)]
        return (first * act_three[tile(index), columns] - second - third * gap).astype(low_type)

    def grad_two(index, carry):
        taps_two[pl.ds(pl.multiple_of((index + 1) * line, line), line), :] = back_act(
            terms_two, act_two, 1, index, space_two
        )
        return carry

    lax.fori_loop(0, SIDE, grad_two, 0)
    fold_turn(2, groups - 1)
    middle_rows = 9 * width // groups
    for which in range(groups):
        pieces = []
        start = which * middle_rows
        if which > 0:
            fold_turn(1, which - 1)
        while start < (which + 1) * middle_rows:
            tap, spot = start // width, start % width
            size = min(width - spot, (which + 1) * middle_rows - start)
            down, over = tap // 3, tap % 3
            left_start, right_start = (0, 0, step)[over], (step, 0, 0)[over]
            reach = line if over == 1 else line - step
            left = jnp.concatenate(
                [
                    taps_one[row + left_start : row + left_start + reach, spot : spot + size]
                    for row in range(down * line, (down + SIDE) * line, line)
                ],
                axis=0,
            )
            right = jnp.concatenate(
                [
                    taps_two[row + right_start : row + right_start + reach, :]
                    for row in range(line, (1 + SIDE) * line, line)
                ],
                axis=0,
            )
            pieces.append(dot_tn(left, right).astype(low_type))
            start += size
        put(mid_wide, which, jnp.concatenate(pieces, axis=0))
        fold_begin(which, 1)
        if which < 2:
            fold_turn(2, groups + which)

    def back_one(index, carry):
        kernel = flat_rows(w_middle[...])

        def tap_of(down, over):
            tap = 3 * down + 2 - over
            return kernel[tap * width : (tap + 1) * width]

        value = over_lines([shifted(taps_two, index, 2 - down) for down in range(3)], tap_of, dot_nt, 1)
        drop_into(index, value, act_one, 0, gain_one, bias_one, space_one)
        return carry

    for turn, (lower, upper) in enumerate(((0, 1), (1, 3), (3, 5), (5, SIDE))):
        lax.fori_loop(lower, upper, back_one, 0)
        if turn < 3:
            fold_turn(1, 3 + turn)
    close_back(5)
    move_back_one = swap(5, width)
    move_back_one.start()

    move_back_one.wait()
    terms_one = back_terms(5, 0, width, gain_one)

    def grad_one(index, carry):
        hidden_two[tile(index), :] = back_act(terms_one, act_one, 0, index, space_one)
        return carry

    lax.fori_loop(0, SIDE, grad_one, 0)

    for which in range(groups):
        put(w_first, which, dot_tn(x_all[:, which * group : (which + 1) * group], hidden_two[...]))
        fold_begin(which, 0)
        if which > 0:
            fold_turn(0, which - 1)

    for kind in range(2):
        row = 3 - kind
        pieces = [
            sums_mine[5, row : row + 1, lanes(core, part)],
            sums_mine[4, row : row + 1, lanes(core, part)],
            sums_mine[3, row : row + 1, lanes(core, half)],
        ]
        whole = jnp.concatenate(pieces, axis=1)
        per_kind = whole.shape[1] // LANES
        for spot in range(per_kind):
            grad_norm_out[kind * per_kind + spot : kind * per_kind + spot + 1, :] = whole[
                :, spot * LANES : (spot + 1) * LANES
            ]
    for turn in range(groups - 1, groups + 2):
        fold_turn(0, turn)
    if gather:
        start = 0
        for slot in range(3):
            rows = fold.counts[slot]
            act_three[kept + start : kept + start + rows, half : half + width] = fold.result(slot)
            start += rows
        leave = pltpu.make_async_copy(
            act_three.at[pl.ds(kept, start), pl.ds(half, width)], grads_out, sem_local.at[3]
        )
        leave.start()
        leave.wait()
        fold.drain()
    else:
        outs = [
            pltpu.make_async_copy(weight_rows(ref, slice(None), rows), out, sem_local.at[slot])
            for slot, (ref, rows, out) in enumerate(
                zip((w_first, mid_wide, w_last), [weight.shape[-2] for weight in weights], grads_out)
            )
        ]
        for copy in outs:
            copy.start()
        for copy in outs:
            copy.wait()
    head_leave.wait()
    for copy in to_mate + head_moves:
        copy.wait_send()


def client_pass(gather, classes, features, labels, flag, params, head, weights):
    pixels, half = features.shape
    images = labels.shape[1]
    count_rows, channels = pixels // 2, 2 * half
    width = params.shape[0] // 2 * LANES - half
    head_rows = classes + -classes % 16
    mine_images = images // 2
    line = SIDE * mine_images
    middle = 9 * width
    blocks = 32
    group = channels // SPOTS[0]
    vmem = pl.BlockSpec(memory_space=pltpu.VMEM)
    smem = pl.BlockSpec(memory_space=pltpu.SMEM)
    spots = SPOTS + (2,)
    scratch = [
        pltpu.VMEM((count_rows, channels), low_type),
        pltpu.VMEM(spots + (line, group), low_type),
        pltpu.VMEM(spots + (channels // blocks, width), low_type),
        pltpu.VMEM(spots + (middle // blocks, width), low_type),
        pltpu.VMEM(spots + (channels // blocks, width), low_type),
        pltpu.VMEM((count_rows, width), wide),
        pltpu.VMEM((count_rows, width), wide),
        pltpu.VMEM((count_rows, channels), wide),
        pltpu.VMEM((count_rows + 2 * line, width), low_type),
        pltpu.VMEM((count_rows + 2 * line, width), low_type),
        pltpu.VMEM((count_rows, width), low_type),
        pltpu.VMEM((count_rows, LANES), wide),
        pltpu.VMEM((2, 2, half + width), wide),
        pltpu.VMEM((2, head_rows, half), low_type),
        pltpu.VMEM((mine_images, channels), wide),
        pltpu.VMEM((mine_images, half), low_type),
        pltpu.VMEM((2, mine_images, half), low_type),
        pltpu.VMEM((2, head_rows, mine_images), low_type),
        pltpu.VMEM((6, 8, channels), wide),
        pltpu.VMEM((6, 8, channels), wide),
        pltpu.VMEM((24, max(width, group)), wide),
        pltpu.VMEM((3, 8, channels), wide),
        pltpu.SemaphoreType.DMA((11,)),
        pltpu.SemaphoreType.DMA((2, 6)),
        pltpu.SemaphoreType.DMA((2, 7)),
    ]
    any_space = pl.BlockSpec(memory_space=pl.ANY)
    if gather:
        counts = (channels // blocks, middle // blocks, channels // blocks)
        scratch += [pltpu.SemaphoreType.DMA((2, 3, 3))]
        scratch += [pltpu.SemaphoreType.DMA((2, 4, 6)) for _ in range(2)]
        scratch += [pltpu.SemaphoreType.DMA((2, 4, 3))]
        scratch += [pltpu.VMEM((4, 2, 2, rows, width), low_type) for rows in counts[1:]]
        for lead in ((4, 2), (4,), (4,)):
            scratch += [pltpu.VMEM(lead + (rows, width), low_type) for rows in counts]
        scratch += [pltpu.SemaphoreType.DMA((2, 4, 3))]
        scratch += [pltpu.SemaphoreType.DMA((2, 4, 6)) for _ in range(3)]
        grads_shape = [jax.ShapeDtypeStruct((sum(counts), width), wide)]
        grads_specs = [any_space]
    else:
        grads_shape = [jax.ShapeDtypeStruct(weight.shape, low_type) for weight in weights]
        grads_specs = [any_space] * 3
    return pl.pallas_call(
        functools.partial(client_kernel, gather, images, classes),
        out_shape=grads_shape
        + [
            jax.ShapeDtypeStruct(params.shape, wide),
            jax.ShapeDtypeStruct((classes * half // LANES, LANES), wide),
            jax.ShapeDtypeStruct((8, LANES), wide),
        ],
        in_specs=[any_space, vmem, smem, vmem, vmem] + [any_space] * len(weights),
        out_specs=grads_specs + [vmem, any_space, vmem],
        scratch_shapes=scratch,
        compiler_params=pltpu.CompilerParams(
            collective_id=0, has_side_effects=True, vmem_limit_bytes=VMEM_BYTES
        ),
    )(features, labels, flag, params, head, *weights)


def adam_update(param, grad, first, second, rate, decay):
    first = adam_first * first + (1.0 - adam_first) * grad
    second = adam_second * second + (1.0 - adam_second) * grad * grad
    first_hat = first / (1.0 - adam_first**STEP)
    second_hat = second / (1.0 - adam_second**STEP)
    return (
        param - rate * (first_hat / (jnp.sqrt(second_hat) + adam_epsilon) + decay * param),
        first,
        second,
    )
class GramSum:
    def __init__(self, place, data, total, boxes, sems):
        self.place = place
        self.data = data
        self.total = total
        self.core_box, self.near_box, self.far_box, self.z_box = boxes
        self.sems = sems
        self.copies = []
        self.sizes = (data.shape[0] // 72 * 40 // 32, data.shape[0] // 72 * 32 // 32)

    def rows(self, kind, core, z=None, first=None, second=None):
        size = self.sizes[kind]
        start = core * (16 * (self.sizes[0] + self.sizes[1])) + kind * 16 * self.sizes[0]
        count = 16 * size
        for number, spot, parts in ((4 * size, z, 4), (2 * size, first, 2), (size, second, 2)):
            if spot is None:
                break
            start, count = start + spot * number, number
        return pl.ds(pl.multiple_of(start, 8), count)

    def ways(self, kind):
        p = self.place
        x_way, y_way = (p.x, p.along_x()), (p.y, p.along_y())
        return (x_way, y_way) if kind == 0 else (y_way, x_way)

    def copy(self, phase, kind, turn, src, dst, client, core):
        sems = self.sems
        return remote(
            src, dst, sems.at[0, phase, kind, turn], sems.at[1, phase, kind, turn], client, core
        )

    def launch(self, copy):
        copy.start()
        self.copies.append(copy)

    def down(self, phase, kind, turn):
        p = self.place
        z = (p.others[::-1] + [p.z])[turn]
        (first, first_to), (second, second_to) = self.ways(kind)
        base = self.sizes[0] * kind
        if phase == 0:
            src = self.data.at[self.rows(kind, 1 - p.core, z), :]
            box = self.core_box.at[turn, pl.ds(4 * base, 4 * self.sizes[kind]), :]
            return self.copy(0, kind, turn, src, box, p.client, 1 - p.core)
        if phase == 1:
            src = self.data.at[self.rows(kind, p.core, z, 1 - first), :]
            box = self.near_box.at[turn, pl.ds(2 * base, 2 * self.sizes[kind]), :]
            return self.copy(1, kind, turn, src, box, first_to, p.core)
        if phase == 2:
            src = self.data.at[self.rows(kind, p.core, z, first, 1 - second), :]
            box = self.far_box.at[turn, pl.ds(base, self.sizes[kind]), :]
            return self.copy(2, kind, turn, src, box, second_to, p.core)
        src = self.data.at[self.rows(kind, p.core, z, first, second), :]
        box = self.z_box.at[turn, pl.ds(base, self.sizes[kind]), :]
        return self.copy(3, kind, turn, src, box, p.along_z(2 - turn), p.core)

    def down_step(self, phase, kind, turn):
        p = self.place
        z = (p.others[::-1] + [p.z])[turn]
        (first, _), (second, _) = self.ways(kind)
        self.down(phase, kind, turn).wait_recv()
        spots = (z, first, second)[: phase + 1]
        where = self.rows(kind, p.core, *spots)
        scale = (4, 2, 1)[phase]
        box = (self.core_box, self.near_box, self.far_box)[phase]
        self.data[where, :] += box[turn, pl.ds(scale * self.sizes[0] * kind, scale * self.sizes[kind]), :]
        if phase < 2 or turn < 3:
            self.launch(self.down(phase + 1, kind, turn))

    def up(self, phase, kind, turn):
        p = self.place
        z = ([p.z] + p.others)[turn]
        (first, first_to), (second, second_to) = self.ways(kind)
        if phase == 0:
            ref, to = self.total.at[self.rows(kind, p.core, p.z, first, second), :], p.along_z(turn)
        elif phase == 1:
            ref, to = self.total.at[self.rows(kind, p.core, z, first, second), :], second_to
        elif phase == 2:
            ref, to = self.total.at[self.rows(kind, p.core, z, first), :], first_to
        else:
            ref, to = self.total.at[self.rows(kind, p.core, z), :], p.client
        return self.copy(4 + phase, kind, turn, ref, ref, to, 1 - p.core if phase == 3 else p.core)

    def run(self, extra):
        extra = list(extra)
        kinds = (0, 1)
        for turn in range(4):
            for kind in kinds:
                self.launch(self.down(0, kind, turn))
        for turn in range(6):
            if extra:
                extra.pop(0)()
            for kind in kinds:
                for phase in range(3):
                    if 0 <= turn - phase < 4:
                        self.down_step(phase, kind, turn - phase)
        p = self.place
        for kind in kinds:
            (first, _), (second, _) = self.ways(kind)
            where = self.rows(kind, p.core, p.z, first, second)
            value = self.data[where, :]
            for turn in range(3):
                self.down(3, kind, turn).wait_recv()
                value += self.z_box[turn, pl.ds(self.sizes[0] * kind, self.sizes[kind]), :]
            self.total[where, :] = value
            self.launch(self.up(1, kind, 0))
            for turn in range(3):
                self.launch(self.up(0, kind, turn))
        for turn in range(6):
            for kind in kinds:
                if 1 <= turn < 4:
                    self.up(0, kind, turn - 1).wait_recv()
                    self.launch(self.up(1, kind, turn))
                if 1 <= turn < 5:
                    self.up(1, kind, turn - 1).wait_recv()
                    self.launch(self.up(2, kind, turn - 1))
                if 2 <= turn:
                    self.up(2, kind, turn - 2).wait_recv()
                    self.launch(self.up(3, kind, turn - 2))
        for turn in range(4):
            for kind in kinds:
                self.up(3, kind, turn).wait_recv()

    def drain(self):
        for copy in self.copies:
            copy.wait_send()


class TileSum:
    def __init__(self, place, tiles, boxes, sems):
        self.place = place
        self.tiles = tiles
        self.boxes = boxes
        self.sems = sems

    def copy(self, stage, box):
        p = self.place
        to = (p.client, p.along_x(), p.along_y()) + tuple(p.along_z(step) for step in range(3))
        core = 1 - p.core if box == 0 else p.core
        return remote(
            self.tiles.at[stage], self.boxes.at[box], self.sems.at[0, box], self.sems.at[1, box], to[box], core
        )

    def steps(self):
        def start():
            self.copy(0, 0).start()

        def pair(stage):
            self.copy(stage, stage).wait_recv()
            self.tiles[stage + 1] = self.tiles[stage] + self.boxes[stage]
            if stage < 2:
                self.copy(stage + 1, stage + 1).start()
            else:
                for step in range(3):
                    self.copy(3, 3 + step).start()

        return [start] + [functools.partial(pair, stage) for stage in range(3)]

    def result(self):
        for step in range(3):
            self.copy(3, 3 + step).wait_recv()
        return (self.tiles[3] + self.boxes[3]) + (self.boxes[4] + self.boxes[5])

    def drain(self):
        for stage in range(3):
            self.copy(stage, stage).wait_send()
        for step in range(3):
            self.copy(3, 3 + step).wait_send()


def dot_high(left, right):
    return jnp.dot(left, right, precision=lax.Precision.HIGH, preferred_element_type=wide)


def base_kernel(
    ratios,
    sizes,
    master,
    momentum,
    anchor,
    loss_in,
    grads,
    *rest,
):
    place = Place()
    rest = list(rest)

    def take(count):
        taken = rest[:count]
        del rest[:count]
        return taken

    base_new, momentum_new, base_low, loss_out = take(4)
    gram, gram_total = take(2)
    gram_boxes = take(4)
    grams, iterate, tiles, tile_boxes = take(4)
    gram_sems, tile_sems = take(2)

    place.greet(True)
    tiles[0] = loss_in[...]
    tile_sum = TileSum(place, tiles, tile_boxes, tile_sems)
    extra = tile_sum.steps()
    extra.pop(0)()

    bounds = [0]
    for size in sizes:
        bounds.append(bounds[-1] + size)
    width = master.shape[1]
    part = width // 2
    for slot in range(3):
        rows = slice(bounds[slot], bounds[slot + 1])
        grad = grads[rows, :] + prox_weight * (master[rows, :] - anchor[rows, :])
        fresh = momentum_decay * momentum[rows, :] + grad
        momentum_new[rows, :] = fresh
        partial = lax.dot_general(
            fresh, fresh, (((0,), (0,)), ((), ())), precision=precise, preferred_element_type=wide
        )
        start = 3 * part * slot
        gram[start : start + part, :] = partial[:part, :part]
        gram[start + part : start + 2 * part, :] = partial[:part, part:]
        gram[start + 2 * part : start + 3 * part, :] = partial[part:, part:]

    gram_sum = GramSum(place, gram, gram_total, gram_boxes, gram_sems)

    gram_sum.run(extra)
    loss_out[...] = tile_sum.result()

    spots = lax.broadcasted_iota(jnp.int32, (part, part), 0)
    diagonal = spots == lax.broadcasted_iota(jnp.int32, (part, part), 1)
    iterate[...] = jnp.zeros_like(iterate)
    for slot in range(3):
        start = 3 * part * slot
        corner = gram_total[start : start + part, :]
        side = gram_total[start + part : start + 2 * part, :]
        end = gram_total[start + 2 * part : start + 3 * part, :]
        trace = jnp.sum(jnp.where(diagonal, corner + end, 0.0))
        factor = 1.0 / (jnp.sqrt(trace) + 1e-07)
        square = factor * factor
        grams[slot, :part, :part] = corner * square
        grams[slot, :part, part:] = side * square
        grams[slot, part:, :part] = side.T * square
        grams[slot, part:, part:] = end * square
        rows = slice(bounds[slot], bounds[slot + 1])
        iterate[slot, : bounds[slot + 1] - bounds[slot], :] = momentum_new[rows, :] * factor

    def turn(slot, last):
        current = grams[slot]
        mixed = schulz_second * current + schulz_third * dot_high(current, current)
        held = iterate[slot]
        iterate[slot] = schulz_first * held + dot_high(held, mixed)
        if not last:
            once = schulz_first * current + dot_high(current, mixed)
            grams[slot] = schulz_first * once + dot_high(once, mixed)

    def one(count, carry):
        turn(lax.rem(count, 3), False)
        return carry

    lax.fori_loop(0, 3 * (NS_STEPS - 1), one, 0)

    def final(slot, carry):
        turn(slot, True)
        return carry

    lax.fori_loop(0, 3, final, 0)
    for slot in range(3):
        rows = slice(bounds[slot], bounds[slot + 1])
        held = master[rows, :]
        ortho = iterate[slot, : bounds[slot + 1] - bounds[slot], :] * ratios[slot]
        fresh = held - muon_rate * (ortho + muon_decay * held)
        base_new[rows, :] = fresh
        base_low[rows, :] = fresh.astype(low_type)
    gram_sum.drain()
    tile_sum.drain()


def base_pass(ratios, sizes, master, momentum, anchor, loss_tile, grads):
    rows, width = master.shape
    part = width // 2
    vmem = pl.BlockSpec(memory_space=pltpu.VMEM)
    share = 9 * part // 32
    scratch = [pltpu.VMEM((9 * part, part), wide)] * 2
    scratch += [pltpu.VMEM((4, size, part), wide) for size in (4 * share, 2 * share, share)]
    scratch += [pltpu.VMEM((3, share, part), wide)]
    scratch += [
        pltpu.VMEM((3, width, width), wide),
        pltpu.VMEM((3, max(sizes), width), wide),
        pltpu.VMEM((4, 8, LANES), wide),
        pltpu.VMEM((6, 8, LANES), wide),
        pltpu.SemaphoreType.DMA((2, 8, 2, 4)),
        pltpu.SemaphoreType.DMA((2, 6)),
    ]
    block = jax.ShapeDtypeStruct((rows, width), wide)
    outs = [block, block, jax.ShapeDtypeStruct((rows, width), low_type), jax.ShapeDtypeStruct((8, LANES), wide)]
    operands = [master, momentum, anchor, loss_tile, grads]
    return pl.pallas_call(
        functools.partial(base_kernel, ratios, sizes),
        out_shape=outs,
        in_specs=[vmem] * len(operands),
        out_specs=[vmem] * len(outs),
        scratch_shapes=scratch,
        compiler_params=pltpu.CompilerParams(
            collective_id=1, has_side_effects=True, vmem_limit_bytes=VMEM_BYTES
        ),
    )(*operands)


def gram_of(section):
    return lax.dot_general(section, section, (((0,), (0,)), ((), ())), precision=precise)


def square(gram):
    return jnp.dot(gram, gram, precision=precise)


def times_poly(left, mixed):
    return schulz_first * left + jnp.dot(left, mixed, precision=precise)


def schulz(sections):
    raw_grams = lax.psum(tuple(gram_of(section) for section in sections), ("client", "chan"))
    factors = [1.0 / (jnp.sqrt(jnp.trace(gram)) + 1e-07) for gram in raw_grams]
    current = [section * factor for section, factor in zip(sections, factors)]
    grams = [gram * (factor * factor) for gram, factor in zip(raw_grams, factors)]
    for turn in range(NS_STEPS):
        mixed = [schulz_second * gram + schulz_third * square(gram) for gram in grams]
        current = [times_poly(current[slot], mixed[slot]) for slot in range(3)]
        if turn + 1 < NS_STEPS:
            grams = [
                times_poly(times_poly(grams[slot], mixed[slot]), mixed[slot]) for slot in range(3)
            ]
    return current


def base_far(ratios, bounds, master, momentum, anchor, loss_tile, grads):
    sums = [
        lax.psum_scatter(flat_rows(grad).astype(wide), ("client", "chan"), scatter_dimension=0, tiled=True)
        for grad in grads
    ]
    grad_base = jnp.concatenate(sums, axis=0) + prox_weight * (master - anchor)
    momentum_new = momentum_decay * momentum + grad_base
    current = schulz([momentum_new[bounds[slot] : bounds[slot + 1]] for slot in range(3)])
    ortho = jnp.concatenate([current[slot] * ratios[slot] for slot in range(3)], axis=0)
    base_new = master - muon_rate * (ortho + muon_decay * master)
    return base_new, momentum_new, base_new.astype(low_type), lax.psum(loss_tile, ("client", "chan"))


def as_stored(rows, shape):
    return with_layout_constraint(rows.reshape(shape), Layout(major_to_minor=tuple(range(len(shape)))))


def on_device(
    features,
    labels,
    mask,
    base_master,
    base_momentum,
    global_base,
    norm_params,
    norm_first,
    norm_second,
    head,
    head_first,
    head_second,
):
    halves = lax.axis_size("chan")
    blocks = lax.axis_size("client") * halves
    half = features.shape[2]
    width = base_master.shape[2]
    channels = half * halves
    classes = head.shape[2]
    rows_first = channels // blocks
    rows_mid = 9 * width // blocks
    sizes = (rows_first, rows_mid, rows_first)
    bounds = (0, rows_first, rows_first + rows_mid, base_master.shape[1])
    ratio = (channels / width) ** 0.5
    ratios = (ratio, 3.0, ratio)
    master, momentum, anchor = base_master[0], base_momentum[0], global_base[0]
    norm_rows = norm_params.reshape(-1, LANES)
    head_rows = jnp.transpose(head, (2, 0, 1)).reshape(-1, LANES)
    near = lax.axis_size("client") == SPOTS[0] * SPOTS[1] * SPOTS[2]
    if near:
        weights = [master]
    else:
        low_master = master.astype(low_type)
        weights = [
            lax.all_gather(low_master[bounds[slot] : bounds[slot + 1]], ("client", "chan"), axis=0, tiled=True)
            for slot in range(3)
        ]
        weights = [weight.reshape(SPOTS + (2, weight.shape[0] // 32, width)) for weight in weights]
    *grads, grad_norm, grad_head, loss_tile = client_pass(
        near, classes, features[0], labels, mask, norm_rows, head_rows, weights
    )
    grad_norm = as_stored(grad_norm, norm_params.shape)
    grad_head = jnp.transpose(as_stored(grad_head, (classes, 1, half)), (1, 2, 0))
    norm_new, norm_first_new, norm_second_new = adam_update(
        norm_params, grad_norm, norm_first, norm_second, norm_rate, 0.0
    )
    head_new, head_first_new, head_second_new = adam_update(
        head, grad_head, head_first, head_second, head_rate, head_decay
    )
    if near:
        base_new, momentum_new, base_low, loss_tile = base_pass(
            ratios, sizes, master, momentum, anchor, loss_tile, grads[0]
        )
    else:
        base_new, momentum_new, base_low, loss_tile = base_far(
            ratios, bounds, master, momentum, anchor, loss_tile, grads
        )
    return (
        loss_tile[0, 0:2],
        base_new[None],
        momentum_new[None],
        base_low[None],
        norm_new,
        norm_first_new,
        norm_second_new,
        head_new,
        head_first_new,
        head_second_new,
    )


def solution(mesh):
    wide_block = P(("client", "chan"), None, None)
    norm_block = P("client", None, "chan", None)
    head_block = P("client", "chan", None)
    return jax.shard_map(
        on_device,
        mesh=mesh,
        in_specs=(P("client", None, "chan"), P("client", None), P("client"))
        + (wide_block,) * 3
        + (norm_block,) * 3
        + (head_block,) * 3,
        out_specs=(P(),) + (wide_block,) * 3 + (norm_block,) * 3 + (head_block,) * 3,
        check_vma=False,
    )
```

```python
import functools

import jax
import jax.numpy as jnp
from jax import lax
from jax.experimental import pallas as pl
from jax.experimental.layout import Layout, with_layout_constraint
from jax.experimental.pallas import tpu as pltpu
from jax.sharding import PartitionSpec as P

NS_STEPS = 5
STEP = 10

low_type = jnp.bfloat16
wide = jnp.float32
MESH = pl.DeviceIdType.MESH
precise = lax.Precision.HIGHEST
norm_epsilon = 1e-05
prox_weight = 0.05
momentum_decay = 0.95
muon_rate = 0.3
muon_decay = 0.1
schulz_first = 3.4445
schulz_second = -4.775
schulz_third = 2.0315
adam_first = 0.9
adam_second = 0.95
adam_epsilon = 1e-08
head_rate = 0.01
head_decay = 0.05
norm_rate = 0.5

SIDE = 7
PIXELS = SIDE * SIDE
LANES = 128
SPOTS = (4, 2, 2)
VMEM_BYTES = 62 * 2**20


def when(condition, call):
    if isinstance(condition, bool):
        if condition:
            call()
    else:
        pl.when(condition)(call)


def dot_nn(left, right):
    return jnp.dot(left, right, preferred_element_type=wide)


def dot_nt(left, right):
    return lax.dot_general(left, right, (((1,), (1,)), ((), ())), preferred_element_type=wide)


def dot_tn(left, right):
    return lax.dot_general(left, right, (((0,), (0,)), ((), ())), preferred_element_type=wide)


def flat_rows(block):
    return block.reshape(-1, block.shape[-1])


def sigmoid(value):
    return 0.5 * jnp.tanh(0.5 * value) + 0.5


def fold_rows(value):
    return jnp.sum(value.reshape(value.shape[0] // 8, 8, value.shape[1]), axis=0)


def column_sum(value):
    return jnp.sum(value, axis=0, keepdims=True)


def remote(src, dst, send_sem, recv_sem, client, core):
    return pltpu.make_async_remote_copy(
        src_ref=src,
        dst_ref=dst,
        send_sem=send_sem,
        recv_sem=recv_sem,
        device_id=(client, core),
        device_id_type=MESH,
    )


class Place:
    def __init__(self):
        self.client = lax.axis_index("client")
        self.core = lax.axis_index("chan")
        self.z = self.client // 4
        self.y = (self.client // 2) % 2
        self.x = self.client % 2
        self.others = [
            self.z + 1 - 2 * (self.z % 2),
            (self.z + 2) % 4,
            3 - self.z,
        ]

    def at(self, z, y, x):
        return z * 4 + y * 2 + x

    def along_x(self):
        return self.at(self.z, self.y, 1 - self.x)

    def along_y(self):
        return self.at(self.z, 1 - self.y, self.x)

    def along_z(self, step):
        return self.at(self.others[step], self.y, self.x)

    def greet(self, whole):
        barrier = pltpu.get_barrier_semaphore()
        pairs = [(self.client, 1 - self.core)]
        if whole:
            pairs += [(self.along_x(), self.core), (self.along_y(), self.core)]
            pairs += [(self.along_z(step), self.core) for step in range(3)]
        for pair in pairs:
            pl.semaphore_signal(barrier, inc=1, device_id=pair, device_id_type=MESH)
        pl.semaphore_wait(barrier, len(pairs))


def cut_rows(counts):
    pieces = []
    for slot, rows in enumerate(counts):
        middle = (rows // 16 + 1) // 2 * 16
        pieces.append((slot, 0, middle, 0))
        pieces.append((slot, middle, rows - middle, 1))
    return pieces


class Spread:
    def __init__(self, place, weights, sems):
        self.place = place
        self.weights = weights
        self.pieces = cut_rows([weight.shape[-2] for weight in weights])
        self.z_sems, self.near_sems, self.far_sems, self.core_sems = sems
        self.order = [place.z] + place.others

    def z_copy(self, step, slot):
        p = self.place
        ref = self.weights[slot].at[p.z, p.y, p.x, p.core]
        sems = self.z_sems
        return remote(ref, ref, sems.at[0, step, slot], sems.at[1, step, slot], p.along_z(step), p.core)

    def near_copy(self, turn, number):
        p = self.place
        slot, start, count, way = self.pieces[number]
        ref = self.weights[slot].at[self.order[turn], p.y, p.x, p.core, pl.ds(start, count), :]
        sems = self.near_sems
        return remote(
            ref, ref, sems.at[0, turn, number], sems.at[1, turn, number], (p.along_x, p.along_y)[way](), p.core
        )

    def far_copy(self, turn, number):
        p = self.place
        slot, start, count, way = self.pieces[number]
        rows = pl.ds(start, count)
        spot = self.order[turn]
        if way == 0:
            ref = self.weights[slot].at[spot, p.y, :, p.core, rows, :]
        else:
            ref = self.weights[slot].at[spot, :, p.x, p.core, rows, :]
        sems = self.far_sems
        return remote(
            ref, ref, sems.at[0, turn, number], sems.at[1, turn, number], (p.along_y, p.along_x)[way](), p.core
        )

    def core_copy(self, turn, slot):
        p = self.place
        ref = self.weights[slot].at[self.order[turn], :, :, p.core]
        sems = self.core_sems
        return remote(ref, ref, sems.at[0, turn, slot], sems.at[1, turn, slot], p.client, 1 - p.core)

    def begin(self, master):
        p = self.place
        start = 0
        for slot in range(3):
            rows = self.weights[slot].shape[-2]
            self.weights[slot][p.z, p.y, p.x, p.core] = master[start : start + rows, :].astype(low_type)
            start += rows
        for step in range(3):
            self.z_copy(step, 0).start()
        self.near_start(0)

    def near_start(self, slot):
        for number in (2 * slot, 2 * slot + 1):
            self.near_copy(0, number).start()

    def steps(self):
        near, far, core, start = self.near_step, self.far_step, self.core_step, self.near_start
        groups = [
            [(far, 0, 0), (start, 1)],
            [(near, 1, 0)],
            [(near, 2, 0), (near, 3, 0)],
            [(far, 1, 0), (core, 0, 0), (far, 0, 1)],
            [(far, 2, 0), (far, 3, 0), (core, 1, 0)],
            [(core, 2, 0), (core, 3, 0), (near, 1, 1), (start, 2)],
            [(core, 0, 1), (near, 2, 1)],
            [(far, 1, 1), (near, 3, 1)],
            [(core, 1, 1), (far, 2, 1), (far, 0, 2)],
            [(far, 3, 1), (core, 2, 1), (near, 1, 2)],
            [(core, 3, 1), (core, 0, 2), (near, 2, 2)],
            [(far, 1, 2), (near, 3, 2)],
            [(core, 1, 2), (far, 2, 2)],
            [(far, 3, 2), (core, 2, 2)],
            [(core, 3, 2)],
        ]
        return [[functools.partial(*step) for step in group] for group in groups]

    def near_step(self, turn, slot):
        self.z_copy(turn - 1, slot).wait_recv()
        for number in (2 * slot, 2 * slot + 1):
            self.near_copy(turn, number).start()
        if slot < 2:
            self.z_copy(turn - 1, slot + 1).start()

    def far_step(self, turn, slot):
        for number in (2 * slot, 2 * slot + 1):
            self.near_copy(turn, number).wait_recv()
            self.far_copy(turn, number).start()

    def core_step(self, turn, slot):
        for number in (2 * slot, 2 * slot + 1):
            self.far_copy(turn, number).wait_recv()
        self.core_copy(turn, slot).start()

    def arrive(self, slot):
        for turn in range(4):
            self.core_copy(turn, slot).wait_recv()

    def drain(self):
        for slot in range(3):
            for step in range(3):
                self.z_copy(step, slot).wait_send()
            for turn in range(4):
                self.core_copy(turn, slot).wait_send()
        for number in range(6):
            for turn in range(4):
                self.near_copy(turn, number).wait_send()
                self.far_copy(turn, number).wait_send()


class Fold:
    def __init__(self, place, grads, counts, parts):
        self.place = place
        self.grads = grads
        self.counts = counts
        self.pieces = cut_rows(counts)
        self.core_boxes = [parts[1], parts[0], parts[1]]
        self.near_boxes, self.far_boxes, self.z_boxes = [parts[3 * k + 2 : 3 * k + 5] for k in range(3)]
        self.core_sems, self.near_sems, self.far_sems, self.z_sems = parts[11:]

    def core_copy(self, which, slot):
        p = self.place
        sems = self.core_sems
        return remote(
            self.grads[slot].at[which, :, :, 1 - p.core, pl.ds(0, self.counts[slot]), :],
            self.core_boxes[slot].at[which],
            sems.at[0, which, slot],
            sems.at[1, which, slot],
            p.client,
            1 - p.core,
        )

    def near_copy(self, which, number):
        p = self.place
        slot, start, count, way = self.pieces[number]
        rows = pl.ds(start, count)
        if way == 0:
            ref = self.grads[slot].at[which, :, 1 - p.x, p.core, rows, :]
        else:
            ref = self.grads[slot].at[which, 1 - p.y, :, p.core, rows, :]
        box = self.near_boxes[slot].at[which, :, rows, :]
        sems = self.near_sems
        return remote(
            ref, box, sems.at[0, which, number], sems.at[1, which, number], (p.along_x, p.along_y)[way](), p.core
        )

    def far_copy(self, which, number):
        p = self.place
        slot, start, count, way = self.pieces[number]
        rows = pl.ds(start, count)
        if way == 0:
            ref = self.grads[slot].at[which, 1 - p.y, p.x, p.core, rows, :]
        else:
            ref = self.grads[slot].at[which, p.y, 1 - p.x, p.core, rows, :]
        box = self.far_boxes[slot].at[which, rows, :]
        sems = self.far_sems
        return remote(
            ref, box, sems.at[0, which, number], sems.at[1, which, number], (p.along_y, p.along_x)[way](), p.core
        )

    def z_copy(self, which, sender, number):
        p = self.place
        slot, start, count, _ = self.pieces[number]
        rows = pl.ds(start, count)
        sems = self.z_sems
        return remote(
            self.grads[slot].at[which, p.y, p.x, p.core, rows, :],
            self.z_boxes[slot].at[sender, rows, :],
            sems.at[0, which, number],
            sems.at[1, sender, number],
            p.at(which, p.y, p.x),
            p.core,
        )

    def begin(self, which, slot):
        self.core_copy(which, slot).start()

    def turn(self, slot, turn):
        for lag, step in ((2, self.far_step), (1, self.near_step), (0, self.core_step)):
            when((turn >= lag) & (turn < lag + 4), functools.partial(step, turn - lag, slot))

    def core_step(self, which, slot):
        p = self.place
        rows = pl.ds(0, self.counts[slot])
        self.core_copy(which, slot).wait_recv()
        where = (which, slice(None), slice(None), p.core, rows, slice(None))
        both = self.grads[slot][where].astype(wide) + self.core_boxes[slot][which].astype(wide)
        self.grads[slot][where] = both.astype(low_type)
        for number in (2 * slot, 2 * slot + 1):
            self.near_copy(which, number).start()

    def near_step(self, which, slot):
        p = self.place
        for number in (2 * slot, 2 * slot + 1):
            _, start, count, way = self.pieces[number]
            rows = pl.ds(start, count)
            self.near_copy(which, number).wait_recv()
            if way == 0:
                where = (which, slice(None), p.x, p.core, rows, slice(None))
            else:
                where = (which, p.y, slice(None), p.core, rows, slice(None))
            both = self.grads[slot][where].astype(wide) + self.near_boxes[slot][which, :, rows, :].astype(wide)
            self.grads[slot][where] = both.astype(low_type)
            self.far_copy(which, number).start()

    def far_step(self, which, slot):
        p = self.place
        for number in (2 * slot, 2 * slot + 1):
            _, start, count, way = self.pieces[number]
            rows = pl.ds(start, count)
            self.far_copy(which, number).wait_recv()
            where = (which, p.y, p.x, p.core, rows, slice(None))
            both = self.grads[slot][where].astype(wide) + self.far_boxes[slot][which, rows, :].astype(wide)
            self.grads[slot][where] = both.astype(low_type)

            @pl.when(p.z != which)
            def _():
                self.z_copy(which, p.z, number).start()

    def result(self, slot):
        p = self.place
        rows = pl.ds(0, self.counts[slot])
        self.z_boxes[slot][p.z] = self.grads[slot][p.z, p.y, p.x, p.core, rows, :]
        for sender in range(4):

            @pl.when(p.z != sender)
            def _():
                for number in (2 * slot, 2 * slot + 1):
                    self.z_copy(sender, sender, number).wait_recv()

        total = self.z_boxes[slot][0].astype(wide)
        for sender in range(1, 4):
            total += self.z_boxes[slot][sender].astype(wide)
        return total

    def drain(self):
        for which in range(4):
            for slot in range(3):
                self.core_copy(which, slot).wait_send()
            for number in range(6):
                self.near_copy(which, number).wait_send()
                self.far_copy(which, number).wait_send()

            @pl.when(self.place.z != which)
            def _():
                for number in range(6):
                    self.z_copy(which, self.place.z, number).wait_send()


def norm_stats(mine, theirs, count):
    gap = mine[0:1] - theirs[0:1]
    mean = 0.5 * (mine[0:1] + theirs[0:1])
    spread = mine[1:2] + theirs[1:2] + gap * gap * (0.5 * count)
    return mean, lax.rsqrt(spread / (2.0 * count) + norm_epsilon)


def client_kernel(
    gather,
    images,
    classes,
    features,
    labels,
    flag,
    params,
    head,
    *rest,
):
    if gather:
        master, *rest = rest
    else:
        first_in, middle_in, last_in, *rest = rest
    if gather:
        grads_out, *rest = rest
    else:
        grads_out, rest = rest[:3], rest[3:]
    (
        grad_norm_out,
        grad_head_out,
        loss_out,
        x_all,
        mid_wide,
        w_first,
        w_middle,
        w_last,
        act_one,
        act_two,
        act_three,
        taps_one,
        taps_two,
        hidden_two,
        stage,
        params_all,
        head_all,
        grad_pool,
        pool_send,
        pool_all,
        logit_grads,
        sums_mine,
        sums_theirs,
        shift,
        fwd_stats,
        sem_local,
        sem_swap,
        sem_misc,
        *near_parts,
    ) = rest
    place = Place()
    core = place.core
    mate = (place.client, 1 - core)
    count_rows, channels = x_all.shape
    half = channels // 2
    width = act_one.shape[1]
    part = width // 2
    mine_images = images // 2
    line = SIDE * mine_images
    total_rows = 2.0 * count_rows

    def tile(index):
        return pl.ds(pl.multiple_of(index * line, line), line)

    def lanes(index, size):
        return pl.ds(pl.multiple_of(index * size, size), size)

    place.greet(gather)

    quarter = half // 2
    own_rows = pl.ds(pl.multiple_of(core * count_rows, count_rows), count_rows)
    mate_rows = pl.ds(pl.multiple_of((1 - core) * count_rows, count_rows), count_rows)
    top_rows = pl.ds(0, count_rows)
    own_copies = [
        pltpu.make_async_copy(
            features.at[own_rows, pl.ds(0, quarter)], hidden_two, sem_local.at[0]
        )
    ]
    for index in range(SIDE):
        rows = pl.ds(pl.multiple_of(core * count_rows + index * line, line), line)
        own_copies.append(
            pltpu.make_async_copy(
                features.at[rows, pl.ds(quarter, quarter)],
                mid_wide.at[0, index // 4, (index // 2) % 2, index % 2],
                sem_local.at[1 + index],
            )
        )
    per_kind = params.shape[0] // 2
    for kind in range(2):
        rows = [params[kind * per_kind + spot : kind * per_kind + spot + 1, :] for spot in range(per_kind)]
        params_all[core, kind : kind + 1, :] = jnp.concatenate(rows, axis=1)
    head_all[core] = jnp.zeros(head_all.shape[1:], low_type)
    for spot in range(half // LANES):
        head_all[core, 0:classes, spot * LANES : (spot + 1) * LANES] = head[
            pl.ds(spot, classes, stride=half // LANES), :
        ].astype(low_type)
    to_mate = [
        remote(params_all.at[core], params_all.at[core], sem_misc.at[0, 0], sem_misc.at[1, 0], *mate),
        remote(head_all.at[core], head_all.at[core], sem_misc.at[0, 1], sem_misc.at[1, 1], *mate),
    ]
    for side, buffer in enumerate((taps_one, taps_two)):
        to_mate.append(
            remote(
                features.at[mate_rows, pl.ds(side * quarter, quarter)],
                buffer.at[top_rows, :],
                sem_misc.at[0, 5 + side],
                sem_misc.at[1, 5 + side],
                *mate,
            )
        )
    for copy in to_mate + own_copies:
        copy.start()

    weights = (w_first, w_middle, w_last)
    if gather:
        spread = Spread(place, weights, near_parts[:4])
        held = act_three.at[pl.ds(0, master.shape[0]), pl.ds(0, width)]
        load = pltpu.make_async_copy(master, held, sem_local.at[8])
        load.start()
        load.wait()
        spread.begin(held)
        counts = [weight.shape[-2] for weight in weights]
        fold = Fold(place, (w_first, mid_wide, w_last), counts, near_parts[4:])
        due = spread.steps()
    else:
        loads = [
            pltpu.make_async_copy(src, dst, sem_local.at[8 + slot])
            for slot, (src, dst) in enumerate(zip((first_in, middle_in, last_in), weights))
        ]
        for load in loads:
            load.start()
        due = []

    def advance(count):
        for group in due[:count]:
            for step in group:
                step()
        del due[:count]

    def advance_at(index, spots):
        for spot, group in zip(spots, due):

            @pl.when(index == spot)
            def _():
                for step in group:
                    step()

    def arrive(slot, left):
        if gather:
            advance(len(due) - left)
            spread.arrive(slot)
        else:
            loads[slot].wait()

    def fold_turn(slot, turn):
        if gather:
            fold.turn(slot, turn)

    def fold_begin(which, slot):
        if gather:
            fold.begin(which, slot)

    def zero_edges(buffer):
        edge = jnp.zeros((line,) + buffer.shape[1:], low_type)
        buffer[0:line, :] = edge
        buffer[line + count_rows : 2 * line + count_rows, :] = edge

    advance(3)
    for copy in own_copies:
        copy.wait()

    def turn_from(source, base):
        def turn(index, carry):
            stage[...] = source(lanes(index, LANES)).astype(wide)

            def pixel(spot, inner):
                x_all[
                    pl.ds(pl.multiple_of(spot * mine_images, mine_images), mine_images),
                    pl.ds(pl.multiple_of(base + index * LANES, LANES), LANES),
                ] = stage[pl.ds(spot, mine_images, stride=PIXELS), :].astype(low_type)
                return inner

            return lax.fori_loop(0, PIXELS, pixel, carry, unroll=7)

        return turn

    quarters = quarter // LANES
    own_base, mate_base = core * half, (1 - core) * half
    lax.fori_loop(0, quarters, turn_from(lambda columns: hidden_two[:, columns], own_base), 0)
    advance(1)
    lax.fori_loop(
        0,
        quarters,
        turn_from(lambda columns: mid_wide[0, :, :, :, :, columns].reshape(8 * line, LANES)[:count_rows], own_base + quarter),
        0,
    )
    advance(1)
    for copy in to_mate:
        copy.wait_recv()
    lax.fori_loop(0, quarters, turn_from(lambda columns: taps_one[0:count_rows, columns], mate_base), 0)
    advance(1)
    lax.fori_loop(0, quarters, turn_from(lambda columns: taps_two[0:count_rows, columns], mate_base + quarter), 0)
    zero_edges(taps_one)
    zero_edges(taps_two)
    arrive(0, 9)

    def swap(slot, size):
        return remote(
            sums_mine.at[slot, :, pl.ds(0, size)],
            sums_theirs.at[slot, :, pl.ds(0, size)],
            sem_swap.at[0, slot],
            sem_swap.at[1, slot],
            *mate,
        )

    def gain_bias(lower, upper):
        rows = []
        for kind in range(2):
            pieces = [params_all[side, kind : kind + 1, lower:upper] for side in range(2)]
            rows.append(jnp.concatenate(pieces, axis=1))
        return rows

    def collect(index, value, columns, size):
        @pl.when(index == 0)
        def _():
            shift[0:1, pl.ds(0, size)] = column_sum(fold_rows(value)) / value.shape[0]
            shift[8:24, pl.ds(0, size)] = jnp.zeros((16, size), wide)

        gap = value - shift[0:1, pl.ds(0, size)]
        shift[8:16, pl.ds(0, size)] += fold_rows(gap)
        shift[16:24, pl.ds(0, size)] += fold_rows(gap * gap)

    def close_stats(slot, columns, size):
        sum_gap = column_sum(shift[8:16, pl.ds(0, size)])
        sum_square = column_sum(shift[16:24, pl.ds(0, size)])
        sums_mine[slot, 0:1, columns] = shift[0:1, pl.ds(0, size)] + sum_gap / count_rows
        sums_mine[slot, 1:2, columns] = sum_square - sum_gap * sum_gap / count_rows

    def settle(slot, size):
        mean, scale = norm_stats(
            sums_mine[slot, 0:2, pl.ds(0, size)], sums_theirs[slot, 0:2, pl.ds(0, size)], float(count_rows)
        )
        fwd_stats[slot, 0:1, pl.ds(0, size)] = mean
        fwd_stats[slot, 1:2, pl.ds(0, size)] = scale

    whole_width = pl.ds(0, width)

    def first_tile(index, carry):
        value = dot_nn(x_all[tile(index), :], flat_rows(w_first[...]))
        act_one[tile(index), :] = value
        collect(index, value, whole_width, width)
        advance_at(index, (1, 3, 5))
        return carry

    lax.fori_loop(0, SIDE, first_tile, 0)
    del due[:3]
    close_stats(0, whole_width, width)
    move = swap(0, width)
    move.start()
    move.wait()
    settle(0, width)

    gain_one, bias_one = gain_bias(0, part)
    gain_two, bias_two = gain_bias(part, width)
    gain_three, bias_three = gain_bias(width, width + half)

    def normal(act, slot, index):
        mean = fwd_stats[slot, 0:1, pl.ds(0, width)]
        return (act[tile(index), :] - mean) * fwd_stats[slot, 1:2, pl.ds(0, width)]

    def hide_one(index, carry):
        value = normal(act_one, 0, index) * gain_one + bias_one
        taps_one[pl.ds(pl.multiple_of((index + 1) * line, line), line), :] = (value * sigmoid(value)).astype(low_type)
        return carry

    lax.fori_loop(0, SIDE, hide_one, 0)
    arrive(1, 4)

    def shifted(buffer, index, down):
        return buffer[pl.ds(pl.multiple_of((index + down) * line, line), line), :]

    step = mine_images
    edge_rows = jnp.zeros((step, width), wide)

    def over_lines(lines, tap_of, multiply, axis):
        left = jnp.concatenate(lines, axis=1)
        value = multiply(left, jnp.concatenate([tap_of(down, 1) for down in range(3)], axis=axis))
        lower = multiply(left[: line - step], jnp.concatenate([tap_of(down, 0) for down in range(3)], axis=axis))
        upper = multiply(left[step:], jnp.concatenate([tap_of(down, 2) for down in range(3)], axis=axis))
        value += jnp.concatenate([edge_rows, lower], axis=0)
        return value + jnp.concatenate([upper, edge_rows], axis=0)

    def second_tile(index, carry):
        kernel = flat_rows(w_middle[...])

        def tap_of(down, over):
            tap = 3 * down + over
            return kernel[tap * width : (tap + 1) * width]

        value = over_lines([shifted(taps_one, index, down) for down in range(3)], tap_of, dot_nn, 0)
        act_two[tile(index), :] = value
        collect(index, value, whole_width, width)
        advance_at(index, (1, 3, 5))
        return carry

    lax.fori_loop(0, SIDE, second_tile, 0)
    del due[:3]
    close_stats(1, whole_width, width)
    move_two = swap(1, width)
    move_two.start()
    move_two.wait()
    settle(1, width)

    def hide_two(index, carry):
        value = normal(act_two, 1, index) * gain_two + bias_two
        hidden_two[tile(index), :] = (value * sigmoid(value)).astype(low_type)
        return carry

    lax.fori_loop(0, SIDE, hide_two, 0)

    arrive(2, 0)
    groups = w_last.shape[0]
    group = channels // groups

    def third_group(which, carry):
        columns = lanes(which, group)

        def third_tile(index, inner):
            value = dot_nt(hidden_two[tile(index), :], flat_rows(w_last[which]))
            act_three[tile(index), columns] = value
            collect(index, value, columns, group)
            return inner

        lax.fori_loop(0, SIDE, third_tile, 0)
        close_stats(2, columns, group)
        return carry

    lax.fori_loop(0, groups, third_group, 0)
    move_three = swap(2, channels)
    move_three.start()
    move_three.wait()
    settle(2, channels)
    fwd_stats[2, 2:3, :] = gain_three
    fwd_stats[2, 3:4, :] = bias_three

    per_group = group // LANES

    def block_of(spot):
        return pl.ds(pl.multiple_of(spot * mine_images, mine_images), mine_images)

    def mid_line(which, index):
        return which, index // 4, (index // 2) % 2, index % 2, pl.ds(0, line)

    kept = channels // LANES * mine_images

    def gathered(kind):
        starts = range(kind * kept, (kind + 1) * kept, mine_images)
        return jnp.concatenate([stage[start : start + mine_images, :] for start in starts], axis=1)

    def emit(index, carry):
        columns = lanes(index, LANES)
        mean, scale = fwd_stats[2, 0:1, columns], fwd_stats[2, 1:2, columns]
        gain, bias = fwd_stats[2, 2:3, columns], fwd_stats[2, 3:4, columns]

        def pixels(row, sums):
            pooled, slopes, slopes_normed = sums
            found = []
            for spot in range(SIDE):
                where = block_of(row * SIDE + spot)
                normed = (act_three[where, columns] - mean) * scale
                total = normed * gain + bias + x_all[where, columns].astype(wide)
                sig = sigmoid(total)
                out = total * sig
                slope = sig + out * (1.0 - sig)
                found.append(slope.astype(low_type))
                pooled, slopes, slopes_normed = pooled + out, slopes + slope, slopes_normed + slope * normed
            mid_wide[mid_line(index // per_group, row) + (lanes(index % per_group, LANES),)] = jnp.concatenate(
                found, axis=0
            )
            return pooled, slopes, slopes_normed

        zero = jnp.zeros((mine_images, LANES), wide)
        pooled, slopes, slopes_normed = lax.fori_loop(0, SIDE, pixels, (zero, zero, zero))
        for kind, value in enumerate((pooled, slopes, slopes_normed)):
            stage[pl.ds(pl.multiple_of(kind * kept + index * mine_images, mine_images), mine_images), :] = value
        return carry

    lax.fori_loop(0, channels // LANES, emit, 0)

    pooled = (gathered(0) / PIXELS).astype(low_type)
    head_full = jnp.concatenate([head_all[0], head_all[1]], axis=1)
    logits = dot_nt(head_full, pooled)
    spots = lax.broadcasted_iota(jnp.int32, logits.shape, 0)
    inside = spots < classes
    first_labels, second_labels = labels[0:1, 0:mine_images], labels[0:1, mine_images:]
    onehot = (spots == jnp.where(core == 0, first_labels, second_labels)).astype(wide)
    top = jnp.max(jnp.where(inside, logits, -jnp.inf), axis=0, keepdims=True)
    powers = jnp.where(inside, jnp.exp(logits - top), 0.0)
    power_sum = jnp.sum(powers, axis=0, keepdims=True)
    picked = jnp.sum(logits * onehot, axis=0, keepdims=True)
    each_loss = top + jnp.log(power_sum) - picked
    taking = flag[0].astype(wide)
    tile_spots = lax.broadcasted_iota(jnp.int32, loss_out.shape, 1)
    loss_out[...] = jnp.where(tile_spots == 0, taking * jnp.sum(each_loss), taking * mine_images)
    grads = (taking / images * (powers / power_sum - onehot)).astype(low_type)
    grad_pool[...] = dot_tn(grads, head_full) / PIXELS
    logit_grads[core] = grads
    pool_all[core] = pooled[:, 0:half]
    pool_send[...] = pooled[:, half:]

    @pl.when(core == 1)
    def _():
        pool_all[core] = pooled[:, half:]
        pool_send[...] = pooled[:, 0:half]

    head_moves = [
        remote(pool_send, pool_all.at[core], sem_misc.at[0, 3], sem_misc.at[1, 3], *mate),
        remote(logit_grads.at[core], logit_grads.at[core], sem_misc.at[0, 4], sem_misc.at[1, 4], *mate),
    ]

    sums_mine[3, 0:1, :] = column_sum(grad_pool[...] * gathered(1))
    sums_mine[3, 1:2, :] = column_sum(grad_pool[...] * gathered(2))
    move_back = swap(3, channels)
    move_back.start()
    for copy in head_moves:
        copy.start()
    move_back.wait()

    def back_terms(slot, layer, size, gain):
        columns = pl.ds(0, size)
        sums = sums_mine[slot, 0:2, columns] + sums_theirs[slot, 0:2, columns]
        sums_mine[slot, 2:4, columns] = sums
        scale = fwd_stats[layer, 1:2, columns]
        return (
            scale * gain,
            scale * gain * sums[0:1] / total_rows,
            scale * scale * gain * sums[1:2] / total_rows,
        )

    first, second, third = back_terms(3, 2, channels, gain_three)
    fwd_stats[2, 4:5, :] = first
    fwd_stats[2, 5:6, :] = second
    fwd_stats[2, 6:7, :] = third

    def pull(index, carry):
        columns = lanes(index, LANES)
        mean = fwd_stats[2, 0:1, columns]
        first, second = fwd_stats[2, 4:5, columns], fwd_stats[2, 5:6, columns]
        third = fwd_stats[2, 6:7, columns]
        reach = grad_pool[:, columns] * first

        def pixels(row, inner):
            where = mid_line(index // per_group, row) + (lanes(index % per_group, LANES),)
            slopes = mid_wide[where].astype(wide)
            found = []
            for spot in range(SIDE):
                slope = slopes[spot * mine_images : (spot + 1) * mine_images]
                gap = act_three[block_of(row * SIDE + spot), columns] - mean
                found.append((reach * slope - second - third * gap).astype(low_type))
            mid_wide[where] = jnp.concatenate(found, axis=0)
            return inner

        return lax.fori_loop(0, SIDE, pixels, carry)

    lax.fori_loop(0, channels // LANES, pull, 0)
    for copy in head_moves:
        copy.wait_recv()
    head_grad = dot_nn(logit_grads[0], pool_all[0]) + dot_nn(logit_grads[1], pool_all[1])
    for spot in range(half // LANES):
        stage[pl.ds(spot, classes, stride=half // LANES), :] = head_grad[
            0:classes, spot * LANES : (spot + 1) * LANES
        ]
    head_space = stage.at[pl.ds(0, grad_head_out.shape[0]), :]
    head_leave = pltpu.make_async_copy(head_space, grad_head_out, sem_local.at[0])
    head_leave.start()

    def drop_into(index, value, act, slot, gain, bias, columns):
        normed = normal(act, slot, index)
        norm = normed * gain + bias
        sig = sigmoid(norm)
        grad = value * (sig + norm * sig * (1.0 - sig))
        act_three[tile(index), columns] = grad
        size = pl.ds(0, width)

        @pl.when(index == 0)
        def _():
            shift[8:24, size] = jnp.zeros((16, width), wide)

        shift[8:16, size] += fold_rows(grad)
        shift[16:24, size] += fold_rows(grad * normed)

    def close_back(slot):
        size = pl.ds(0, width)
        sums_mine[slot, 0:1, size] = column_sum(shift[8:16, size])
        sums_mine[slot, 1:2, size] = column_sum(shift[16:24, size])

    space_two, space_one = pl.ds(0, width), pl.ds(width, width)

    def back_two(index, carry):
        kernel = flat_rows(w_last[...])
        left = jnp.concatenate([mid_wide[mid_line(which, index)] for which in range(groups)], axis=1)
        value = dot_nn(left, kernel)
        drop_into(index, value, act_two, 1, gain_two, bias_two, space_two)
        return carry

    lax.fori_loop(0, SIDE, back_two, 0)
    close_back(4)
    move_back_two = swap(4, width)
    move_back_two.start()

    if gather:
        spread.drain()

    def weight_rows(ref, which, rows):
        return ref.at[which, :, :, :, pl.ds(0, rows), :]

    def put(ref, which, value):
        rows = value.shape[0] // 8
        ref[which, :, :, :, pl.ds(0, rows), :] = value.astype(low_type).reshape(2, 2, 2, rows, width)

    def expand_group(which, carry):
        left = mid_wide[which].reshape(8 * line, group)[:count_rows]
        put(w_last, which, dot_tn(left, hidden_two[...]))
        fold_begin(which, 2)
        fold_turn(2, which - 1)
        return carry

    lax.fori_loop(0, groups, expand_group, 0)
    move_back_two.wait()
    terms_two = back_terms(4, 1, width, gain_two)

    def back_act(terms, act, layer, index, columns):
        first, second, third = terms
        gap = act[tile(index), :] - fwd_stats[layer, 0:1, pl.ds(0, width)]
        return (first * act_three[tile(index), columns] - second - third * gap).astype(low_type)

    def grad_two(index, carry):
        taps_two[pl.ds(pl.multiple_of((index + 1) * line, line), line), :] = back_act(
            terms_two, act_two, 1, index, space_two
        )
        return carry

    lax.fori_loop(0, SIDE, grad_two, 0)
    fold_turn(2, groups - 1)
    piece = width // 2
    middle_rows = 9 * width // groups
    grain = 48

    def middle_row(down, carry):
        def middle_piece(spot, inner):
            for over in range(3):
                left_start, right_start = (0, 0, step)[over], (step, 0, 0)[over]
                reach = line if over == 1 else line - step
                left = [
                    taps_one[
                        pl.ds(pl.multiple_of((down + row) * line + left_start, step), reach), lanes(spot, piece)
                    ]
                    for row in range(SIDE)
                ]
                right = [
                    taps_two[(row + 1) * line + right_start : (row + 1) * line + right_start + reach, :]
                    for row in range(SIDE)
                ]
                value = dot_tn(jnp.concatenate(left, axis=0), jnp.concatenate(right, axis=0))
                start = pl.multiple_of(over * width + spot * piece, piece)
                hidden_two[pl.ds(start, piece), :] = value.astype(low_type)
            return inner

        lax.fori_loop(0, 2, middle_piece, 0)
        grains = 3 * width // grain
        per_block = middle_rows // 8 // grain

        def lay_out(spot, inner):
            place_of = down * grains + spot
            block = place_of // per_block
            rows = pl.ds(pl.multiple_of((place_of % per_block) * grain, 16), grain)
            mid_wide[block // 8, (block // 4) % 2, (block // 2) % 2, block % 2, rows, :] = hidden_two[
                pl.ds(pl.multiple_of(spot * grain, 16), grain), :
            ]
            return inner

        lax.fori_loop(0, grains, lay_out, 0, unroll=4)
        fold_begin(down, 1)

        @pl.when(down == 2)
        def _():
            fold_begin(3, 1)

        fold_turn(2, groups + down)
        fold_turn(1, down - 1)
        return carry

    lax.fori_loop(0, 3, middle_row, 0)

    def back_one(index, carry):
        kernel = flat_rows(w_middle[...])

        def tap_of(down, over):
            tap = 3 * down + 2 - over
            return kernel[tap * width : (tap + 1) * width]

        value = over_lines([shifted(taps_two, index, 2 - down) for down in range(3)], tap_of, dot_nt, 1)
        drop_into(index, value, act_one, 0, gain_one, bias_one, space_one)

        @pl.when(index % 2 == 0)
        def _():
            fold_turn(1, 2 + index // 2)

        return carry

    lax.fori_loop(0, SIDE, back_one, 0)
    close_back(5)
    move_back_one = swap(5, width)
    move_back_one.start()

    move_back_one.wait()
    terms_one = back_terms(5, 0, width, gain_one)

    def grad_one(index, carry):
        hidden_two[tile(index), :] = back_act(terms_one, act_one, 0, index, space_one)
        return carry

    lax.fori_loop(0, SIDE, grad_one, 0)

    def reduce_group(which, carry):
        put(w_first, which, dot_tn(x_all[:, lanes(which, group)], hidden_two[...]))
        fold_begin(which, 0)
        fold_turn(0, which - 1)
        return carry

    lax.fori_loop(0, groups, reduce_group, 0)

    for kind in range(2):
        row = 3 - kind
        pieces = [
            sums_mine[5, row : row + 1, lanes(core, part)],
            sums_mine[4, row : row + 1, lanes(core, part)],
            sums_mine[3, row : row + 1, lanes(core, half)],
        ]
        whole = jnp.concatenate(pieces, axis=1)
        per_kind = whole.shape[1] // LANES
        for spot in range(per_kind):
            grad_norm_out[kind * per_kind + spot : kind * per_kind + spot + 1, :] = whole[
                :, spot * LANES : (spot + 1) * LANES
            ]
    for turn in range(groups - 1, groups + 2):
        fold_turn(0, turn)
    if gather:
        start = 0
        for slot in range(3):
            rows = fold.counts[slot]
            act_three[kept + start : kept + start + rows, half : half + width] = fold.result(slot)
            start += rows
        leave = pltpu.make_async_copy(
            act_three.at[pl.ds(kept, start), pl.ds(half, width)], grads_out, sem_local.at[3]
        )
        leave.start()
        leave.wait()
        fold.drain()
    else:
        outs = [
            pltpu.make_async_copy(weight_rows(ref, slice(None), rows), out, sem_local.at[slot])
            for slot, (ref, rows, out) in enumerate(
                zip((w_first, mid_wide, w_last), [weight.shape[-2] for weight in weights], grads_out)
            )
        ]
        for copy in outs:
            copy.start()
        for copy in outs:
            copy.wait()
    head_leave.wait()
    for copy in to_mate + head_moves:
        copy.wait_send()


def client_pass(gather, classes, features, labels, flag, params, head, weights):
    pixels, half = features.shape
    images = labels.shape[1]
    count_rows, channels = pixels // 2, 2 * half
    width = params.shape[0] // 2 * LANES - half
    head_rows = classes + -classes % 16
    mine_images = images // 2
    line = SIDE * mine_images
    middle = 9 * width
    blocks = 32
    group = channels // SPOTS[0]
    vmem = pl.BlockSpec(memory_space=pltpu.VMEM)
    smem = pl.BlockSpec(memory_space=pltpu.SMEM)
    spots = SPOTS + (2,)
    scratch = [
        pltpu.VMEM((count_rows, channels), low_type),
        pltpu.VMEM(spots + (line, group), low_type),
        pltpu.VMEM(spots + (channels // blocks, width), low_type),
        pltpu.VMEM(spots + (middle // blocks, width), low_type),
        pltpu.VMEM(spots + (channels // blocks, width), low_type),
        pltpu.VMEM((count_rows, width), wide),
        pltpu.VMEM((count_rows, width), wide),
        pltpu.VMEM((count_rows, channels), wide),
        pltpu.VMEM((count_rows + 2 * line, width), low_type),
        pltpu.VMEM((count_rows + 2 * line, width), low_type),
        pltpu.VMEM((count_rows, width), low_type),
        pltpu.VMEM((count_rows, LANES), wide),
        pltpu.VMEM((2, 2, half + width), wide),
        pltpu.VMEM((2, head_rows, half), low_type),
        pltpu.VMEM((mine_images, channels), wide),
        pltpu.VMEM((mine_images, half), low_type),
        pltpu.VMEM((2, mine_images, half), low_type),
        pltpu.VMEM((2, head_rows, mine_images), low_type),
        pltpu.VMEM((6, 8, channels), wide),
        pltpu.VMEM((6, 8, channels), wide),
        pltpu.VMEM((24, max(width, group)), wide),
        pltpu.VMEM((3, 8, channels), wide),
        pltpu.SemaphoreType.DMA((11,)),
        pltpu.SemaphoreType.DMA((2, 6)),
        pltpu.SemaphoreType.DMA((2, 7)),
    ]
    any_space = pl.BlockSpec(memory_space=pl.ANY)
    if gather:
        counts = (channels // blocks, middle // blocks, channels // blocks)
        scratch += [pltpu.SemaphoreType.DMA((2, 3, 3))]
        scratch += [pltpu.SemaphoreType.DMA((2, 4, 6)) for _ in range(2)]
        scratch += [pltpu.SemaphoreType.DMA((2, 4, 3))]
        scratch += [pltpu.VMEM((4, 2, 2, rows, width), low_type) for rows in counts[1:]]
        for lead in ((4, 2), (4,), (4,)):
            scratch += [pltpu.VMEM(lead + (rows, width), low_type) for rows in counts]
        scratch += [pltpu.SemaphoreType.DMA((2, 4, 3))]
        scratch += [pltpu.SemaphoreType.DMA((2, 4, 6)) for _ in range(3)]
        grads_shape = [jax.ShapeDtypeStruct((sum(counts), width), wide)]
        grads_specs = [any_space]
    else:
        grads_shape = [jax.ShapeDtypeStruct(weight.shape, low_type) for weight in weights]
        grads_specs = [any_space] * 3
    return pl.pallas_call(
        functools.partial(client_kernel, gather, images, classes),
        out_shape=grads_shape
        + [
            jax.ShapeDtypeStruct(params.shape, wide),
            jax.ShapeDtypeStruct((classes * half // LANES, LANES), wide),
            jax.ShapeDtypeStruct((8, LANES), wide),
        ],
        in_specs=[any_space, vmem, smem, vmem, vmem] + [any_space] * len(weights),
        out_specs=grads_specs + [vmem, any_space, vmem],
        scratch_shapes=scratch,
        compiler_params=pltpu.CompilerParams(
            collective_id=0, has_side_effects=True, vmem_limit_bytes=VMEM_BYTES
        ),
    )(features, labels, flag, params, head, *weights)


def adam_update(param, grad, first, second, rate, decay):
    first = adam_first * first + (1.0 - adam_first) * grad
    second = adam_second * second + (1.0 - adam_second) * grad * grad
    first_hat = first / (1.0 - adam_first**STEP)
    second_hat = second / (1.0 - adam_second**STEP)
    return (
        param - rate * (first_hat / (jnp.sqrt(second_hat) + adam_epsilon) + decay * param),
        first,
        second,
    )
class GramSum:
    def __init__(self, place, data, total, boxes, sems):
        self.place = place
        self.data = data
        self.total = total
        self.core_box, self.near_box, self.far_box, self.z_box = boxes
        self.sems = sems
        self.copies = []
        self.sizes = (data.shape[0] // 72 * 40 // 32, data.shape[0] // 72 * 32 // 32)

    def rows(self, kind, core, z=None, first=None, second=None):
        size = self.sizes[kind]
        start = core * (16 * (self.sizes[0] + self.sizes[1])) + kind * 16 * self.sizes[0]
        count = 16 * size
        for number, spot, parts in ((4 * size, z, 4), (2 * size, first, 2), (size, second, 2)):
            if spot is None:
                break
            start, count = start + spot * number, number
        return pl.ds(pl.multiple_of(start, 8), count)

    def ways(self, kind):
        p = self.place
        x_way, y_way = (p.x, p.along_x()), (p.y, p.along_y())
        return (x_way, y_way) if kind == 0 else (y_way, x_way)

    def copy(self, phase, kind, turn, src, dst, client, core):
        sems = self.sems
        return remote(
            src, dst, sems.at[0, phase, kind, turn], sems.at[1, phase, kind, turn], client, core
        )

    def launch(self, copy):
        copy.start()
        self.copies.append(copy)

    def down(self, phase, kind, turn):
        p = self.place
        z = (p.others[::-1] + [p.z])[turn]
        (first, first_to), (second, second_to) = self.ways(kind)
        base = self.sizes[0] * kind
        if phase == 0:
            src = self.data.at[self.rows(kind, 1 - p.core, z), :]
            box = self.core_box.at[turn, pl.ds(4 * base, 4 * self.sizes[kind]), :]
            return self.copy(0, kind, turn, src, box, p.client, 1 - p.core)
        if phase == 1:
            src = self.data.at[self.rows(kind, p.core, z, 1 - first), :]
            box = self.near_box.at[turn, pl.ds(2 * base, 2 * self.sizes[kind]), :]
            return self.copy(1, kind, turn, src, box, first_to, p.core)
        if phase == 2:
            src = self.data.at[self.rows(kind, p.core, z, first, 1 - second), :]
            box = self.far_box.at[turn, pl.ds(base, self.sizes[kind]), :]
            return self.copy(2, kind, turn, src, box, second_to, p.core)
        src = self.data.at[self.rows(kind, p.core, z, first, second), :]
        box = self.z_box.at[turn, pl.ds(base, self.sizes[kind]), :]
        return self.copy(3, kind, turn, src, box, p.along_z(2 - turn), p.core)

    def down_step(self, phase, kind, turn):
        p = self.place
        z = (p.others[::-1] + [p.z])[turn]
        (first, _), (second, _) = self.ways(kind)
        self.down(phase, kind, turn).wait_recv()
        spots = (z, first, second)[: phase + 1]
        where = self.rows(kind, p.core, *spots)
        scale = (4, 2, 1)[phase]
        box = (self.core_box, self.near_box, self.far_box)[phase]
        self.data[where, :] += box[turn, pl.ds(scale * self.sizes[0] * kind, scale * self.sizes[kind]), :]
        if phase < 2 or turn < 3:
            self.launch(self.down(phase + 1, kind, turn))

    def up(self, phase, kind, turn):
        p = self.place
        z = ([p.z] + p.others)[turn]
        (first, first_to), (second, second_to) = self.ways(kind)
        if phase == 0:
            ref, to = self.total.at[self.rows(kind, p.core, p.z, first, second), :], p.along_z(turn)
        elif phase == 1:
            ref, to = self.total.at[self.rows(kind, p.core, z, first, second), :], second_to
        elif phase == 2:
            ref, to = self.total.at[self.rows(kind, p.core, z, first), :], first_to
        else:
            ref, to = self.total.at[self.rows(kind, p.core, z), :], p.client
        return self.copy(4 + phase, kind, turn, ref, ref, to, 1 - p.core if phase == 3 else p.core)

    def run(self, extra):
        extra = list(extra)
        kinds = (0, 1)
        for turn in range(4):
            for kind in kinds:
                self.launch(self.down(0, kind, turn))
        for turn in range(6):
            if extra:
                extra.pop(0)()
            for kind in kinds:
                for phase in range(3):
                    if 0 <= turn - phase < 4:
                        self.down_step(phase, kind, turn - phase)
        p = self.place
        for kind in kinds:
            (first, _), (second, _) = self.ways(kind)
            where = self.rows(kind, p.core, p.z, first, second)
            value = self.data[where, :]
            for turn in range(3):
                self.down(3, kind, turn).wait_recv()
                value += self.z_box[turn, pl.ds(self.sizes[0] * kind, self.sizes[kind]), :]
            self.total[where, :] = value
            self.launch(self.up(1, kind, 0))
            for turn in range(3):
                self.launch(self.up(0, kind, turn))
        for turn in range(6):
            for kind in kinds:
                if 1 <= turn < 4:
                    self.up(0, kind, turn - 1).wait_recv()
                    self.launch(self.up(1, kind, turn))
                if 1 <= turn < 5:
                    self.up(1, kind, turn - 1).wait_recv()
                    self.launch(self.up(2, kind, turn - 1))
                if 2 <= turn:
                    self.up(2, kind, turn - 2).wait_recv()
                    self.launch(self.up(3, kind, turn - 2))
        for turn in range(4):
            for kind in kinds:
                self.up(3, kind, turn).wait_recv()

    def drain(self):
        for copy in self.copies:
            copy.wait_send()


class TileSum:
    def __init__(self, place, tiles, boxes, sems):
        self.place = place
        self.tiles = tiles
        self.boxes = boxes
        self.sems = sems

    def copy(self, stage, box):
        p = self.place
        to = (p.client, p.along_x(), p.along_y()) + tuple(p.along_z(step) for step in range(3))
        core = 1 - p.core if box == 0 else p.core
        return remote(
            self.tiles.at[stage], self.boxes.at[box], self.sems.at[0, box], self.sems.at[1, box], to[box], core
        )

    def steps(self):
        def start():
            self.copy(0, 0).start()

        def pair(stage):
            self.copy(stage, stage).wait_recv()
            self.tiles[stage + 1] = self.tiles[stage] + self.boxes[stage]
            if stage < 2:
                self.copy(stage + 1, stage + 1).start()
            else:
                for step in range(3):
                    self.copy(3, 3 + step).start()

        return [start] + [functools.partial(pair, stage) for stage in range(3)]

    def result(self):
        for step in range(3):
            self.copy(3, 3 + step).wait_recv()
        return (self.tiles[3] + self.boxes[3]) + (self.boxes[4] + self.boxes[5])

    def drain(self):
        for stage in range(3):
            self.copy(stage, stage).wait_send()
        for step in range(3):
            self.copy(3, 3 + step).wait_send()


def dot_high(left, right):
    return jnp.dot(left, right, precision=lax.Precision.HIGH, preferred_element_type=wide)


def base_kernel(
    ratios,
    sizes,
    master,
    momentum,
    anchor,
    loss_in,
    grads,
    *rest,
):
    place = Place()
    rest = list(rest)

    def take(count):
        taken = rest[:count]
        del rest[:count]
        return taken

    ortho_out, loss_out = take(2)
    gram, gram_total = take(2)
    gram_boxes = take(4)
    grams, iterate, tiles, tile_boxes = take(4)
    gram_sems, tile_sems = take(2)

    place.greet(True)
    tiles[0] = loss_in[...]
    tile_sum = TileSum(place, tiles, tile_boxes, tile_sems)
    extra = tile_sum.steps()
    extra.pop(0)()

    bounds = [0]
    for size in sizes:
        bounds.append(bounds[-1] + size)
    width = master.shape[1]
    part = width // 2
    for slot in range(3):
        rows = slice(bounds[slot], bounds[slot + 1])
        grad = grads[rows, :] + prox_weight * (master[rows, :] - anchor[rows, :])
        fresh = momentum_decay * momentum[rows, :] + grad
        ortho_out[rows, :] = fresh
        partial = lax.dot_general(
            fresh, fresh, (((0,), (0,)), ((), ())), precision=precise, preferred_element_type=wide
        )
        start = 3 * part * slot
        gram[start : start + part, :] = partial[:part, :part]
        gram[start + part : start + 2 * part, :] = partial[:part, part:]
        gram[start + 2 * part : start + 3 * part, :] = partial[part:, part:]

    gram_sum = GramSum(place, gram, gram_total, gram_boxes, gram_sems)

    gram_sum.run(extra)
    loss_out[...] = tile_sum.result()

    spots = lax.broadcasted_iota(jnp.int32, (part, part), 0)
    diagonal = spots == lax.broadcasted_iota(jnp.int32, (part, part), 1)
    iterate[...] = jnp.zeros_like(iterate)
    for slot in range(3):
        start = 3 * part * slot
        corner = gram_total[start : start + part, :]
        side = gram_total[start + part : start + 2 * part, :]
        end = gram_total[start + 2 * part : start + 3 * part, :]
        trace = jnp.sum(jnp.where(diagonal, corner + end, 0.0))
        factor = 1.0 / (jnp.sqrt(trace) + 1e-07)
        square = factor * factor
        grams[slot, :part, :part] = corner * square
        grams[slot, :part, part:] = side * square
        grams[slot, part:, :part] = side.T * square
        grams[slot, part:, part:] = end * square
        rows = slice(bounds[slot], bounds[slot + 1])
        iterate[slot, : bounds[slot + 1] - bounds[slot], :] = ortho_out[rows, :] * factor

    def turn(count, carry):
        slot = lax.rem(count, 3)
        current = grams[slot]
        mixed = schulz_second * current + schulz_third * dot_high(current, current)
        held = iterate[slot]
        iterate[slot] = schulz_first * held + dot_high(held, mixed)

        @pl.when(count < 3 * (NS_STEPS - 1))
        def _():
            once = schulz_first * current + dot_high(current, mixed)
            grams[slot] = schulz_first * once + dot_high(once, mixed)

        return carry

    lax.fori_loop(0, 3 * NS_STEPS, turn, 0)
    for slot in range(3):
        ortho_out[bounds[slot] : bounds[slot + 1], :] = (
            iterate[slot, : bounds[slot + 1] - bounds[slot], :] * ratios[slot]
        )
    gram_sum.drain()
    tile_sum.drain()


def base_pass(ratios, sizes, master, momentum, anchor, loss_tile, grads):
    rows, width = master.shape
    part = width // 2
    vmem = pl.BlockSpec(memory_space=pltpu.VMEM)
    share = 9 * part // 32
    scratch = [pltpu.VMEM((9 * part, part), wide)] * 2
    scratch += [pltpu.VMEM((4, size, part), wide) for size in (4 * share, 2 * share, share)]
    scratch += [pltpu.VMEM((3, share, part), wide)]
    scratch += [
        pltpu.VMEM((3, width, width), wide),
        pltpu.VMEM((3, max(sizes), width), wide),
        pltpu.VMEM((4, 8, LANES), wide),
        pltpu.VMEM((6, 8, LANES), wide),
        pltpu.SemaphoreType.DMA((2, 8, 2, 4)),
        pltpu.SemaphoreType.DMA((2, 6)),
    ]
    block = jax.ShapeDtypeStruct((rows, width), wide)
    outs = [block, jax.ShapeDtypeStruct((8, LANES), wide)]
    operands = [master, momentum, anchor, loss_tile, grads]
    return pl.pallas_call(
        functools.partial(base_kernel, ratios, sizes),
        out_shape=outs,
        in_specs=[vmem] * len(operands),
        out_specs=[vmem] * len(outs),
        scratch_shapes=scratch,
        compiler_params=pltpu.CompilerParams(
            collective_id=1, has_side_effects=True, vmem_limit_bytes=VMEM_BYTES
        ),
    )(*operands)


def update_kernel(master, momentum, anchor, grads, ortho, *rest):
    norms, grad_norm, heads, grad_head, outs = rest[0:3], rest[3], rest[4:7], rest[7], rest[8:]
    momentum_out, base_out, low_out = outs[0:3]
    held = master[...]
    momentum_out[...] = momentum_decay * momentum[...] + (grads[...] + prox_weight * (held - anchor[...]))
    fresh = held - muon_rate * (ortho[...] + muon_decay * held)
    base_out[...] = fresh
    low_out[...] = fresh.astype(low_type)
    for targets, values, grad, rate, decay in (
        (outs[3:6], norms, grad_norm, norm_rate, 0.0),
        (outs[6:9], heads, grad_head, head_rate, head_decay),
    ):
        updates = adam_update(values[0][...], grad[...], values[1][...], values[2][...], rate, decay)
        for target, value in zip(targets, updates):
            target[...] = value


def update_pass(master, momentum, anchor, grads, ortho, norms, grad_norm, heads, grad_head):
    vmem = pl.BlockSpec(memory_space=pltpu.VMEM)
    operands = [master, momentum, anchor, grads, ortho, *norms, grad_norm, *heads, grad_head]
    outs = [master.shape, master.shape, master.shape] + [grad_norm.shape] * 3 + [grad_head.shape] * 3
    types = [wide, wide, low_type] + [wide] * 6
    return pl.pallas_call(
        update_kernel,
        out_shape=[jax.ShapeDtypeStruct(shape, kind) for shape, kind in zip(outs, types)],
        in_specs=[vmem] * len(operands),
        out_specs=[vmem] * len(outs),
        compiler_params=pltpu.CompilerParams(vmem_limit_bytes=VMEM_BYTES),
    )(*operands)


def gram_of(section):
    return lax.dot_general(section, section, (((0,), (0,)), ((), ())), precision=precise)


def square(gram):
    return jnp.dot(gram, gram, precision=precise)


def times_poly(left, mixed):
    return schulz_first * left + jnp.dot(left, mixed, precision=precise)


def schulz(sections):
    raw_grams = lax.psum(tuple(gram_of(section) for section in sections), ("client", "chan"))
    factors = [1.0 / (jnp.sqrt(jnp.trace(gram)) + 1e-07) for gram in raw_grams]
    current = [section * factor for section, factor in zip(sections, factors)]
    grams = [gram * (factor * factor) for gram, factor in zip(raw_grams, factors)]
    for turn in range(NS_STEPS):
        mixed = [schulz_second * gram + schulz_third * square(gram) for gram in grams]
        current = [times_poly(current[slot], mixed[slot]) for slot in range(3)]
        if turn + 1 < NS_STEPS:
            grams = [
                times_poly(times_poly(grams[slot], mixed[slot]), mixed[slot]) for slot in range(3)
            ]
    return current


def base_far(ratios, bounds, master, momentum, anchor, loss_tile, grads):
    sums = [
        lax.psum_scatter(flat_rows(grad).astype(wide), ("client", "chan"), scatter_dimension=0, tiled=True)
        for grad in grads
    ]
    grad_base = jnp.concatenate(sums, axis=0)
    momentum_new = momentum_decay * momentum + (grad_base + prox_weight * (master - anchor))
    current = schulz([momentum_new[bounds[slot] : bounds[slot + 1]] for slot in range(3)])
    ortho = jnp.concatenate([current[slot] * ratios[slot] for slot in range(3)], axis=0)
    return grad_base, ortho, lax.psum(loss_tile, ("client", "chan"))


def as_stored(rows, shape):
    return with_layout_constraint(rows.reshape(shape), Layout(major_to_minor=tuple(range(len(shape)))))


def on_device(
    features,
    labels,
    mask,
    base_master,
    base_momentum,
    global_base,
    norm_params,
    norm_first,
    norm_second,
    head,
    head_first,
    head_second,
):
    halves = lax.axis_size("chan")
    blocks = lax.axis_size("client") * halves
    half = features.shape[2]
    width = base_master.shape[2]
    channels = half * halves
    classes = head.shape[2]
    rows_first = channels // blocks
    rows_mid = 9 * width // blocks
    sizes = (rows_first, rows_mid, rows_first)
    bounds = (0, rows_first, rows_first + rows_mid, base_master.shape[1])
    ratio = (channels / width) ** 0.5
    ratios = (ratio, 3.0, ratio)
    master, momentum, anchor = base_master[0], base_momentum[0], global_base[0]
    norms = [value.reshape(-1, LANES) for value in (norm_params, norm_first, norm_second)]
    heads = [jnp.transpose(value, (2, 0, 1)).reshape(-1, LANES) for value in (head, head_first, head_second)]
    near = lax.axis_size("client") == SPOTS[0] * SPOTS[1] * SPOTS[2]
    if near:
        weights = [master]
    else:
        low_master = master.astype(low_type)
        weights = [
            lax.all_gather(low_master[bounds[slot] : bounds[slot + 1]], ("client", "chan"), axis=0, tiled=True)
            for slot in range(3)
        ]
        weights = [weight.reshape(SPOTS + (2, weight.shape[0] // 32, width)) for weight in weights]
    *grads, grad_norm, grad_head, loss_tile = client_pass(
        near, classes, features[0], labels, mask, norms[0], heads[0], weights
    )
    if near:
        (grad_base,) = grads
        ortho, loss_tile = base_pass(ratios, sizes, master, momentum, anchor, loss_tile, grad_base)
    else:
        grad_base, ortho, loss_tile = base_far(ratios, bounds, master, momentum, anchor, loss_tile, grads)
    momentum_new, base_new, base_low, *fresh = update_pass(
        master, momentum, anchor, grad_base, ortho, norms, grad_norm, heads, grad_head
    )
    fresh_norms = [as_stored(value, norm_params.shape) for value in fresh[:3]]
    fresh_heads = [jnp.transpose(as_stored(value, (classes, 1, half)), (1, 2, 0)) for value in fresh[3:]]
    return (
        loss_tile[0, 0:2],
        base_new[None],
        momentum_new[None],
        base_low[None],
        *fresh_norms,
        *fresh_heads,
    )


def solution(mesh):
    wide_block = P(("client", "chan"), None, None)
    norm_block = P("client", None, "chan", None)
    head_block = P("client", "chan", None)
    return jax.shard_map(
        on_device,
        mesh=mesh,
        in_specs=(P("client", None, "chan"), P("client", None), P("client"))
        + (wide_block,) * 3
        + (norm_block,) * 3
        + (head_block,) * 3,
        out_specs=(P(),) + (wide_block,) * 3 + (norm_block,) * 3 + (head_block,) * 3,
        check_vma=False,
    )
```

```python
import functools

import jax
import jax.numpy as jnp
from jax import lax
from jax.experimental import pallas as pl
from jax.experimental.layout import Layout, with_layout_constraint
from jax.experimental.pallas import tpu as pltpu
from jax.sharding import PartitionSpec as P

NS_STEPS = 5
STEP = 10

low_type = jnp.bfloat16
wide = jnp.float32
MESH = pl.DeviceIdType.MESH
precise = lax.Precision.HIGHEST
norm_epsilon = 1e-05
prox_weight = 0.05
momentum_decay = 0.95
muon_rate = 0.3
muon_decay = 0.1
schulz_first = 3.4445
schulz_second = -4.775
schulz_third = 2.0315
adam_first = 0.9
adam_second = 0.95
adam_epsilon = 1e-08
head_rate = 0.01
head_decay = 0.05
norm_rate = 0.5

SIDE = 7
PIXELS = SIDE * SIDE
LANES = 128
SPOTS = (4, 2, 2)
VMEM_BYTES = 62 * 2**20


def when(condition, call):
    if isinstance(condition, bool):
        if condition:
            call()
    else:
        pl.when(condition)(call)


def dot_nn(left, right):
    return jnp.dot(left, right, preferred_element_type=wide)


def dot_nt(left, right):
    return lax.dot_general(left, right, (((1,), (1,)), ((), ())), preferred_element_type=wide)


def dot_tn(left, right):
    return lax.dot_general(left, right, (((0,), (0,)), ((), ())), preferred_element_type=wide)


def flat_rows(block):
    return block.reshape(-1, block.shape[-1])


def sigmoid(value):
    return 0.5 * jnp.tanh(0.5 * value) + 0.5


def fold_rows(value):
    return jnp.sum(value.reshape(value.shape[0] // 8, 8, value.shape[1]), axis=0)


def column_sum(value):
    return jnp.sum(value, axis=0, keepdims=True)


def remote(src, dst, send_sem, recv_sem, client, core):
    return pltpu.make_async_remote_copy(
        src_ref=src,
        dst_ref=dst,
        send_sem=send_sem,
        recv_sem=recv_sem,
        device_id=(client, core),
        device_id_type=MESH,
    )


class Place:
    def __init__(self):
        self.client = lax.axis_index("client")
        self.core = lax.axis_index("chan")
        self.z = self.client // 4
        self.y = (self.client // 2) % 2
        self.x = self.client % 2
        self.others = [
            self.z + 1 - 2 * (self.z % 2),
            (self.z + 2) % 4,
            3 - self.z,
        ]

    def at(self, z, y, x):
        return z * 4 + y * 2 + x

    def along_x(self):
        return self.at(self.z, self.y, 1 - self.x)

    def along_y(self):
        return self.at(self.z, 1 - self.y, self.x)

    def along_z(self, step):
        return self.at(self.others[step], self.y, self.x)

    def greet(self, whole):
        barrier = pltpu.get_barrier_semaphore()
        pairs = [(self.client, 1 - self.core)]
        if whole:
            pairs += [(self.along_x(), self.core), (self.along_y(), self.core)]
            pairs += [(self.along_z(step), self.core) for step in range(3)]
        for pair in pairs:
            pl.semaphore_signal(barrier, inc=1, device_id=pair, device_id_type=MESH)
        pl.semaphore_wait(barrier, len(pairs))


def cut_rows(counts):
    pieces = []
    for slot, rows in enumerate(counts):
        middle = (rows // 16 + 1) // 2 * 16
        pieces.append((slot, 0, middle, 0))
        pieces.append((slot, middle, rows - middle, 1))
    return pieces


def block_ref(ref, size, z, y, x, core, start, count):
    if len(ref.shape) == 2:
        first = (((z * 2 + y) * 2 + x) * 2 + core) * size + start
        return ref.at[pl.ds(pl.multiple_of(first, 16), count), :]
    return ref.at[z, y, x, core, pl.ds(start, count), :]


class Spread:
    def __init__(self, place, weights, counts, sems):
        self.place = place
        self.weights = weights
        self.counts = counts
        self.pieces = cut_rows(counts)
        self.z_sems, self.near_sems, self.far_sems, self.core_sems = sems
        self.order = [place.z] + place.others

    def z_copy(self, step, slot):
        p = self.place
        ref = block_ref(self.weights[slot], self.counts[slot], p.z, p.y, p.x, p.core, 0, self.counts[slot])
        sems = self.z_sems
        return remote(ref, ref, sems.at[0, step, slot], sems.at[1, step, slot], p.along_z(step), p.core)

    def near_copy(self, turn, number):
        p = self.place
        slot, start, count, way = self.pieces[number]
        ref = block_ref(self.weights[slot], self.counts[slot], self.order[turn], p.y, p.x, p.core, start, count)
        sems = self.near_sems
        return remote(
            ref, ref, sems.at[0, turn, number], sems.at[1, turn, number], (p.along_x, p.along_y)[way](), p.core
        )

    def far_copies(self, turn, number):
        p = self.place
        slot, start, count, way = self.pieces[number]
        spot = self.order[turn]
        sems = self.far_sems
        copies = []
        for part, other in enumerate((0, 1) if slot == 1 else (slice(None),)):
            y, x = (p.y, other) if way == 0 else (other, p.x)
            ref = block_ref(self.weights[slot], self.counts[slot], spot, y, x, p.core, start, count)
            sem = number + 4 * part
            to = (p.along_y, p.along_x)[way]()
            copies.append(remote(ref, ref, sems.at[0, turn, sem], sems.at[1, turn, sem], to, p.core))
        return copies

    def core_copies(self, turn, slot):
        p = self.place
        sems = self.core_sems
        copies = []
        pairs = [(y, x) for y in (0, 1) for x in (0, 1)] if slot == 1 else [(slice(None), slice(None))]
        for part, (y, x) in enumerate(pairs):
            ref = block_ref(self.weights[slot], self.counts[slot], self.order[turn], y, x, p.core, 0, self.counts[slot])
            sem = (0, 2 + part, 1)[slot]
            copies.append(remote(ref, ref, sems.at[0, turn, sem], sems.at[1, turn, sem], p.client, 1 - p.core))
        return copies

    def begin(self, master):
        p = self.place
        start = 0
        for slot in range(3):
            rows = self.counts[slot]
            own = block_ref(self.weights[slot], self.counts[slot], p.z, p.y, p.x, p.core, 0, rows)
            own[...] = master[start : start + rows, :].astype(low_type)
            start += rows
        for step in range(3):
            self.z_copy(step, 0).start()
        self.near_start(0)

    def near_start(self, slot):
        for number in (2 * slot, 2 * slot + 1):
            self.near_copy(0, number).start()

    def steps(self):
        near, far, core, start = self.near_step, self.far_step, self.core_step, self.near_start
        groups = [
            [(far, 0, 0), (start, 1)],
            [(near, 1, 0)],
            [(near, 2, 0), (near, 3, 0)],
            [(far, 1, 0), (core, 0, 0), (far, 0, 1)],
            [(far, 2, 0), (far, 3, 0), (core, 1, 0)],
            [(core, 2, 0), (core, 3, 0), (near, 1, 1), (start, 2)],
            [(core, 0, 1), (near, 2, 1)],
            [(far, 1, 1), (near, 3, 1)],
            [(core, 1, 1), (far, 2, 1), (far, 0, 2)],
            [(far, 3, 1), (core, 2, 1), (near, 1, 2)],
            [(core, 3, 1), (core, 0, 2), (near, 2, 2)],
            [(far, 1, 2), (near, 3, 2)],
            [(core, 1, 2), (far, 2, 2)],
            [(far, 3, 2), (core, 2, 2)],
            [(core, 3, 2)],
        ]
        return [[functools.partial(*step) for step in group] for group in groups]

    def near_step(self, turn, slot):
        self.z_copy(turn - 1, slot).wait_recv()
        for number in (2 * slot, 2 * slot + 1):
            self.near_copy(turn, number).start()
        if slot < 2:
            self.z_copy(turn - 1, slot + 1).start()

    def far_step(self, turn, slot):
        for number in (2 * slot, 2 * slot + 1):
            self.near_copy(turn, number).wait_recv()
            for copy in self.far_copies(turn, number):
                copy.start()

    def core_step(self, turn, slot):
        for number in (2 * slot, 2 * slot + 1):
            for copy in self.far_copies(turn, number):
                copy.wait_recv()
        for copy in self.core_copies(turn, slot):
            copy.start()

    def arrive(self, slot):
        for turn in range(4):
            for copy in self.core_copies(turn, slot):
                copy.wait_recv()

    def drain(self):
        for slot in range(3):
            for step in range(3):
                self.z_copy(step, slot).wait_send()
            for turn in range(4):
                for copy in self.core_copies(turn, slot):
                    copy.wait_send()
        for number in range(6):
            for turn in range(4):
                self.near_copy(turn, number).wait_send()
                for copy in self.far_copies(turn, number):
                    copy.wait_send()


class Fold:
    def __init__(self, place, grads, counts, parts):
        self.place = place
        self.grads = grads
        self.counts = counts
        self.pieces = cut_rows(counts)
        self.core_boxes = [parts[1], parts[0], parts[1]]
        self.near_boxes, self.far_boxes, self.z_boxes = [parts[3 * k + 2 : 3 * k + 5] for k in range(3)]
        self.core_sems, self.near_sems, self.far_sems, self.z_sems = parts[11:]

    def core_copies(self, which, slot):
        p = self.place
        sems = self.core_sems
        copies = []
        pairs = [(y, x) for y in (0, 1) for x in (0, 1)] if slot == 1 else [(slice(None), slice(None))]
        for part, (y, x) in enumerate(pairs):
            ref = block_ref(self.grads[slot], self.counts[slot], which, y, x, 1 - p.core, 0, self.counts[slot])
            box = self.core_boxes[slot].at[which, y, x]
            sem = (0, 2 + part, 1)[slot]
            copies.append(remote(ref, box, sems.at[0, which, sem], sems.at[1, which, sem], p.client, 1 - p.core))
        return copies

    def near_copies(self, which, number):
        p = self.place
        slot, start, count, way = self.pieces[number]
        sems = self.near_sems
        copies = []
        for part, other in enumerate((0, 1) if slot == 1 else (slice(None),)):
            y, x = (other, 1 - p.x) if way == 0 else (1 - p.y, other)
            ref = block_ref(self.grads[slot], self.counts[slot], which, y, x, p.core, start, count)
            box = self.near_boxes[slot].at[which, other, pl.ds(start, count), :]
            sem = number + 4 * part
            to = (p.along_x, p.along_y)[way]()
            copies.append(remote(ref, box, sems.at[0, which, sem], sems.at[1, which, sem], to, p.core))
        return copies

    def far_copy(self, which, number):
        p = self.place
        slot, start, count, way = self.pieces[number]
        y, x = (1 - p.y, p.x) if way == 0 else (p.y, 1 - p.x)
        ref = block_ref(self.grads[slot], self.counts[slot], which, y, x, p.core, start, count)
        box = self.far_boxes[slot].at[which, pl.ds(start, count), :]
        sems = self.far_sems
        return remote(
            ref, box, sems.at[0, which, number], sems.at[1, which, number], (p.along_y, p.along_x)[way](), p.core
        )

    def z_copy(self, which, sender, number):
        p = self.place
        slot, start, count, _ = self.pieces[number]
        rows = pl.ds(start, count)
        sems = self.z_sems
        return remote(
            block_ref(self.grads[slot], self.counts[slot], which, p.y, p.x, p.core, start, count),
            self.z_boxes[slot].at[sender, rows, :],
            sems.at[0, which, number],
            sems.at[1, sender, number],
            p.at(which, p.y, p.x),
            p.core,
        )

    def begin(self, which, slot):
        for copy in self.core_copies(which, slot):
            copy.start()

    def add(self, slot, spots, start, count, box):
        ref = block_ref(self.grads[slot], self.counts[slot], *spots, self.place.core, start, count)
        ref[...] = (ref[...].astype(wide) + box.astype(wide)).astype(low_type)

    def turn(self, slot, turn):
        for lag, step in ((2, self.far_step), (1, self.near_step), (0, self.core_step)):
            when((turn >= lag) & (turn < lag + 4), functools.partial(step, turn - lag, slot))

    def core_step(self, which, slot):
        for copy in self.core_copies(which, slot):
            copy.wait_recv()
        pairs = [(y, x) for y in (0, 1) for x in (0, 1)] if slot == 1 else [(slice(None), slice(None))]
        for y, x in pairs:
            self.add(slot, (which, y, x), 0, self.counts[slot], self.core_boxes[slot][which, y, x])
        for number in (2 * slot, 2 * slot + 1):
            for copy in self.near_copies(which, number):
                copy.start()

    def near_step(self, which, slot):
        p = self.place
        for number in (2 * slot, 2 * slot + 1):
            _, start, count, way = self.pieces[number]
            for copy in self.near_copies(which, number):
                copy.wait_recv()
            for other in (0, 1) if slot == 1 else (slice(None),):
                y, x = (other, p.x) if way == 0 else (p.y, other)
                box = self.near_boxes[slot][which, other, pl.ds(start, count), :]
                self.add(slot, (which, y, x), start, count, box)
            self.far_copy(which, number).start()

    def far_step(self, which, slot):
        p = self.place
        for number in (2 * slot, 2 * slot + 1):
            _, start, count, way = self.pieces[number]
            self.far_copy(which, number).wait_recv()
            box = self.far_boxes[slot][which, pl.ds(start, count), :]
            self.add(slot, (which, p.y, p.x), start, count, box)

            @pl.when(p.z != which)
            def _():
                self.z_copy(which, p.z, number).start()

    def result(self, slot):
        p = self.place
        self.z_boxes[slot][p.z] = block_ref(self.grads[slot], self.counts[slot], p.z, p.y, p.x, p.core, 0, self.counts[slot])[...]
        for sender in range(4):

            @pl.when(p.z != sender)
            def _():
                for number in (2 * slot, 2 * slot + 1):
                    self.z_copy(sender, sender, number).wait_recv()

        total = self.z_boxes[slot][0].astype(wide)
        for sender in range(1, 4):
            total += self.z_boxes[slot][sender].astype(wide)
        return total

    def drain(self):
        for which in range(4):
            for slot in range(3):
                for copy in self.core_copies(which, slot):
                    copy.wait_send()
            for number in range(6):
                for copy in self.near_copies(which, number):
                    copy.wait_send()
                self.far_copy(which, number).wait_send()

            @pl.when(self.place.z != which)
            def _():
                for number in range(6):
                    self.z_copy(which, self.place.z, number).wait_send()


def norm_stats(mine, theirs, count):
    gap = mine[0:1] - theirs[0:1]
    mean = 0.5 * (mine[0:1] + theirs[0:1])
    spread = mine[1:2] + theirs[1:2] + gap * gap * (0.5 * count)
    return mean, lax.rsqrt(spread / (2.0 * count) + norm_epsilon)


def client_kernel(
    gather,
    images,
    classes,
    features,
    labels,
    flag,
    params,
    head,
    *rest,
):
    if gather:
        master, *rest = rest
    else:
        first_in, middle_in, last_in, *rest = rest
    if gather:
        grads_out, *rest = rest
    else:
        grads_out, rest = rest[:3], rest[3:]
    (
        grad_norm_out,
        grad_head_out,
        loss_out,
        x_all,
        mid_wide,
        w_first,
        w_middle,
        w_last,
        act_one,
        act_two,
        act_three,
        taps_one,
        taps_two,
        hidden_two,
        stage,
        params_all,
        head_all,
        grad_pool,
        pool_send,
        pool_all,
        logit_grads,
        sums_mine,
        sums_theirs,
        shift,
        fwd_stats,
        sem_local,
        sem_swap,
        sem_misc,
        *near_parts,
    ) = rest
    place = Place()
    core = place.core
    mate = (place.client, 1 - core)
    count_rows, channels = x_all.shape
    half = channels // 2
    width = act_one.shape[1]
    part = width // 2
    mine_images = images // 2
    line = SIDE * mine_images
    total_rows = 2.0 * count_rows

    def tile(index):
        return pl.ds(pl.multiple_of(index * line, line), line)

    def lanes(index, size):
        return pl.ds(pl.multiple_of(index * size, size), size)

    place.greet(gather)

    quarter = half // 2
    own_rows = pl.ds(pl.multiple_of(core * count_rows, count_rows), count_rows)
    mate_rows = pl.ds(pl.multiple_of((1 - core) * count_rows, count_rows), count_rows)
    top_rows = pl.ds(0, count_rows)
    own_copies = [
        pltpu.make_async_copy(
            features.at[own_rows, pl.ds(side * quarter, quarter)], buffer, sem_local.at[side]
        )
        for side, buffer in enumerate((hidden_two, mid_wide.at[top_rows, :]))
    ]
    per_kind = params.shape[0] // 2
    for kind in range(2):
        rows = [params[kind * per_kind + spot : kind * per_kind + spot + 1, :] for spot in range(per_kind)]
        params_all[core, kind : kind + 1, :] = jnp.concatenate(rows, axis=1)
    head_all[core] = jnp.zeros(head_all.shape[1:], low_type)
    for spot in range(half // LANES):
        head_all[core, 0:classes, spot * LANES : (spot + 1) * LANES] = head[
            pl.ds(spot, classes, stride=half // LANES), :
        ].astype(low_type)
    to_mate = [
        remote(params_all.at[core], params_all.at[core], sem_misc.at[0, 0], sem_misc.at[1, 0], *mate),
        remote(head_all.at[core], head_all.at[core], sem_misc.at[0, 1], sem_misc.at[1, 1], *mate),
    ]
    for side, buffer in enumerate((taps_one, taps_two)):
        to_mate.append(
            remote(
                features.at[mate_rows, pl.ds(side * quarter, quarter)],
                buffer.at[top_rows, :],
                sem_misc.at[0, 5 + side],
                sem_misc.at[1, 5 + side],
                *mate,
            )
        )
    for copy in to_mate + own_copies:
        copy.start()

    weights = (w_first, w_middle, w_last)
    if gather:
        counts = [channels // 32, 9 * width // 32, channels // 32]
        spread = Spread(place, weights, counts, near_parts[:4])
        held = act_three.at[pl.ds(0, master.shape[0]), pl.ds(0, width)]
        load = pltpu.make_async_copy(master, held, sem_local.at[8])
        load.start()
        load.wait()
        spread.begin(held)
        fold = Fold(place, (w_first, mid_wide, w_last), counts, near_parts[4:])
        due = spread.steps()
    else:
        loads = [
            pltpu.make_async_copy(src, dst, sem_local.at[8 + slot])
            for slot, (src, dst) in enumerate(zip((first_in, middle_in, last_in), weights))
        ]
        for load in loads:
            load.start()
        due = []

    def advance(count):
        for group in due[:count]:
            for step in group:
                step()
        del due[:count]

    def advance_at(index, spots):
        for spot, group in zip(spots, due):

            @pl.when(index == spot)
            def _():
                for step in group:
                    step()

    def arrive(slot, left):
        if gather:
            advance(len(due) - left)
            spread.arrive(slot)
        else:
            loads[slot].wait()

    def fold_turn(slot, turn):
        if gather:
            fold.turn(slot, turn)

    def fold_begin(which, slot):
        if gather:
            fold.begin(which, slot)

    def zero_edges(buffer):
        edge = jnp.zeros((line,) + buffer.shape[1:], low_type)
        buffer[0:line, :] = edge
        buffer[line + count_rows : 2 * line + count_rows, :] = edge

    advance(3)
    for copy in own_copies:
        copy.wait()

    def turn_from(source, base):
        def turn(index, carry):
            stage[...] = source(lanes(index, LANES)).astype(wide)

            def pixel(spot, inner):
                x_all[
                    pl.ds(pl.multiple_of(spot * mine_images, mine_images), mine_images),
                    pl.ds(pl.multiple_of(base + index * LANES, LANES), LANES),
                ] = stage[pl.ds(spot, mine_images, stride=PIXELS), :].astype(low_type)
                return inner

            return lax.fori_loop(0, PIXELS, pixel, carry, unroll=7)

        return turn

    quarters = quarter // LANES
    own_base, mate_base = core * half, (1 - core) * half
    lax.fori_loop(0, quarters, turn_from(lambda columns: hidden_two[:, columns], own_base), 0)
    advance(1)
    lax.fori_loop(
        0,
        quarters,
        turn_from(lambda columns: mid_wide[0:count_rows, columns], own_base + quarter),
        0,
    )
    advance(1)
    for copy in to_mate:
        copy.wait_recv()
    lax.fori_loop(0, quarters, turn_from(lambda columns: taps_one[0:count_rows, columns], mate_base), 0)
    advance(1)
    lax.fori_loop(0, quarters, turn_from(lambda columns: taps_two[0:count_rows, columns], mate_base + quarter), 0)
    zero_edges(taps_one)
    zero_edges(taps_two)
    arrive(0, 9)

    def swap(slot, size):
        return remote(
            sums_mine.at[slot, :, pl.ds(0, size)],
            sums_theirs.at[slot, :, pl.ds(0, size)],
            sem_swap.at[0, slot],
            sem_swap.at[1, slot],
            *mate,
        )

    def gain_bias(lower, upper):
        rows = []
        for kind in range(2):
            pieces = [params_all[side, kind : kind + 1, lower:upper] for side in range(2)]
            rows.append(jnp.concatenate(pieces, axis=1))
        return rows

    def collect(index, value, columns, size):
        @pl.when(index == 0)
        def _():
            shift[0:1, pl.ds(0, size)] = column_sum(fold_rows(value)) / value.shape[0]
            shift[8:24, pl.ds(0, size)] = jnp.zeros((16, size), wide)

        gap = value - shift[0:1, pl.ds(0, size)]
        shift[8:16, pl.ds(0, size)] += fold_rows(gap)
        shift[16:24, pl.ds(0, size)] += fold_rows(gap * gap)

    def close_stats(slot, columns, size):
        sum_gap = column_sum(shift[8:16, pl.ds(0, size)])
        sum_square = column_sum(shift[16:24, pl.ds(0, size)])
        sums_mine[slot, 0:1, columns] = shift[0:1, pl.ds(0, size)] + sum_gap / count_rows
        sums_mine[slot, 1:2, columns] = sum_square - sum_gap * sum_gap / count_rows

    def look_over(act, columns):
        def look(index, carry):
            collect(index, act[tile(index), columns], None, width)
            return carry

        lax.fori_loop(0, SIDE, look, 0)

    groups = SPOTS[0]
    group = channels // groups

    def settle(slot, size):
        mean, scale = norm_stats(
            sums_mine[slot, 0:2, pl.ds(0, size)], sums_theirs[slot, 0:2, pl.ds(0, size)], float(count_rows)
        )
        fwd_stats[slot, 0:1, pl.ds(0, size)] = mean
        fwd_stats[slot, 1:2, pl.ds(0, size)] = scale

    whole_width = pl.ds(0, width)

    def first_part(index, carry):
        act_one[...] += dot_nn(x_all[:, lanes(index, group)], flat_rows(w_first[index]))
        advance_at(index, (0, 1, 2))
        return carry

    act_one[...] = jnp.zeros_like(act_one)
    lax.fori_loop(0, groups, first_part, 0)
    del due[:3]
    look_over(act_one, whole_width)
    close_stats(0, whole_width, width)
    move = swap(0, width)
    move.start()
    move.wait()
    settle(0, width)

    gain_one, bias_one = gain_bias(0, part)
    gain_two, bias_two = gain_bias(part, width)
    gain_three, bias_three = gain_bias(width, width + half)

    def normal(act, slot, index):
        mean = fwd_stats[slot, 0:1, pl.ds(0, width)]
        return (act[tile(index), :] - mean) * fwd_stats[slot, 1:2, pl.ds(0, width)]

    def hide_one(index, carry):
        value = normal(act_one, 0, index) * gain_one + bias_one
        taps_one[pl.ds(pl.multiple_of((index + 1) * line, line), line), :] = (value * sigmoid(value)).astype(low_type)
        return carry

    lax.fori_loop(0, SIDE, hide_one, 0)
    arrive(1, 4)

    step = mine_images
    piece = width // 2

    def row_windows(buffer, down, start, reach):
        if reach == line:
            return buffer[pl.ds(pl.multiple_of(down * line, line), count_rows), :]
        windows = [
            buffer[pl.ds(pl.multiple_of((down + row) * line + start, step), reach), :] for row in range(SIDE)
        ]
        return jnp.concatenate(windows, axis=0)

    def add_windows(target, columns, value, start, reach):
        for row in range(SIDE):
            rows = slice(row * line + start, row * line + start + reach)
            target[rows, columns] += value[row * reach : (row + 1) * reach]

    low_start, high_start, reaches = (0, 0, step), (step, 0, 0), (line - step, line, line - step)

    def second_part(index, carry):
        down, columns = index // 2, lanes(index % 2, piece)
        for over in range(3):
            left = row_windows(taps_one, down, low_start[over], reaches[over])
            kernel = w_middle[pl.ds(pl.multiple_of((3 * down + over) * width, width), width), columns]
            add_windows(act_two, columns, dot_nn(left, kernel), high_start[over], reaches[over])
        advance_at(index, (1, 3, 5))
        return carry

    act_two[...] = jnp.zeros_like(act_two)
    lax.fori_loop(0, 6, second_part, 0)
    del due[:3]
    look_over(act_two, whole_width)
    close_stats(1, whole_width, width)
    move_two = swap(1, width)
    move_two.start()
    move_two.wait()
    settle(1, width)

    def hide_two(index, carry):
        value = normal(act_two, 1, index) * gain_two + bias_two
        hidden_two[tile(index), :] = (value * sigmoid(value)).astype(low_type)
        return carry

    lax.fori_loop(0, SIDE, hide_two, 0)

    arrive(2, 0)

    def third_group(which, carry):
        columns = lanes(which, group)
        act_three[:, columns] = dot_nt(hidden_two[...], flat_rows(w_last[which]))
        look_over(act_three, columns)
        close_stats(2, columns, group)
        return carry

    lax.fori_loop(0, groups, third_group, 0)
    move_three = swap(2, channels)
    move_three.start()
    move_three.wait()
    settle(2, channels)
    fwd_stats[2, 2:3, :] = gain_three
    fwd_stats[2, 3:4, :] = bias_three

    per_group = group // LANES

    def block_of(spot):
        return pl.ds(pl.multiple_of(spot * mine_images, mine_images), mine_images)

    def mid_line(which, index):
        return pl.ds(pl.multiple_of(which * count_rows + index * line, line), line)

    kept = channels // LANES * mine_images

    def gathered(kind):
        starts = range(kind * kept, (kind + 1) * kept, mine_images)
        return jnp.concatenate([stage[start : start + mine_images, :] for start in starts], axis=1)

    def emit(index, carry):
        columns = lanes(index, LANES)
        mean, scale = fwd_stats[2, 0:1, columns], fwd_stats[2, 1:2, columns]
        gain, bias = fwd_stats[2, 2:3, columns], fwd_stats[2, 3:4, columns]

        def pixels(row, sums):
            pooled, slopes, slopes_normed = sums
            found = []
            for spot in range(SIDE):
                where = block_of(row * SIDE + spot)
                normed = (act_three[where, columns] - mean) * scale
                total = normed * gain + bias + x_all[where, columns].astype(wide)
                sig = sigmoid(total)
                out = total * sig
                slope = sig + out * (1.0 - sig)
                found.append(slope.astype(low_type))
                pooled, slopes, slopes_normed = pooled + out, slopes + slope, slopes_normed + slope * normed
            mid_wide[mid_line(index // per_group, row), lanes(index % per_group, LANES)] = jnp.concatenate(
                found, axis=0
            )
            return pooled, slopes, slopes_normed

        zero = jnp.zeros((mine_images, LANES), wide)
        pooled, slopes, slopes_normed = lax.fori_loop(0, SIDE, pixels, (zero, zero, zero))
        for kind, value in enumerate((pooled, slopes, slopes_normed)):
            stage[pl.ds(pl.multiple_of(kind * kept + index * mine_images, mine_images), mine_images), :] = value
        return carry

    lax.fori_loop(0, channels // LANES, emit, 0)

    pooled = (gathered(0) / PIXELS).astype(low_type)
    head_full = jnp.concatenate([head_all[0], head_all[1]], axis=1)
    logits = dot_nt(head_full, pooled)
    spots = lax.broadcasted_iota(jnp.int32, logits.shape, 0)
    inside = spots < classes
    first_labels, second_labels = labels[0:1, 0:mine_images], labels[0:1, mine_images:]
    onehot = (spots == jnp.where(core == 0, first_labels, second_labels)).astype(wide)
    top = jnp.max(jnp.where(inside, logits, -jnp.inf), axis=0, keepdims=True)
    powers = jnp.where(inside, jnp.exp(logits - top), 0.0)
    power_sum = jnp.sum(powers, axis=0, keepdims=True)
    picked = jnp.sum(logits * onehot, axis=0, keepdims=True)
    each_loss = top + jnp.log(power_sum) - picked
    taking = flag[0].astype(wide)
    tile_spots = lax.broadcasted_iota(jnp.int32, loss_out.shape, 1)
    loss_out[...] = jnp.where(tile_spots == 0, taking * jnp.sum(each_loss), taking * mine_images)
    grads = (taking / images * (powers / power_sum - onehot)).astype(low_type)
    grad_pool[...] = dot_tn(grads, head_full) / PIXELS
    logit_grads[core] = grads
    pool_all[core] = pooled[:, 0:half]
    pool_send[...] = pooled[:, half:]

    @pl.when(core == 1)
    def _():
        pool_all[core] = pooled[:, half:]
        pool_send[...] = pooled[:, 0:half]

    head_moves = [
        remote(pool_send, pool_all.at[core], sem_misc.at[0, 3], sem_misc.at[1, 3], *mate),
        remote(logit_grads.at[core], logit_grads.at[core], sem_misc.at[0, 4], sem_misc.at[1, 4], *mate),
    ]

    sums_mine[3, 0:1, :] = column_sum(grad_pool[...] * gathered(1))
    sums_mine[3, 1:2, :] = column_sum(grad_pool[...] * gathered(2))
    move_back = swap(3, channels)
    move_back.start()
    for copy in head_moves:
        copy.start()
    move_back.wait()

    def back_terms(slot, layer, size, gain):
        columns = pl.ds(0, size)
        sums = sums_mine[slot, 0:2, columns] + sums_theirs[slot, 0:2, columns]
        sums_mine[slot, 2:4, columns] = sums
        scale = fwd_stats[layer, 1:2, columns]
        return (
            scale * gain,
            scale * gain * sums[0:1] / total_rows,
            scale * scale * gain * sums[1:2] / total_rows,
        )

    first, second, third = back_terms(3, 2, channels, gain_three)
    fwd_stats[2, 4:5, :] = first
    fwd_stats[2, 5:6, :] = second
    fwd_stats[2, 6:7, :] = third

    def pull(index, carry):
        columns = lanes(index, LANES)
        mean = fwd_stats[2, 0:1, columns]
        first, second = fwd_stats[2, 4:5, columns], fwd_stats[2, 5:6, columns]
        third = fwd_stats[2, 6:7, columns]
        reach = grad_pool[:, columns] * first

        def pixels(row, inner):
            where = (mid_line(index // per_group, row), lanes(index % per_group, LANES))
            slopes = mid_wide[where].astype(wide)
            found = []
            for spot in range(SIDE):
                slope = slopes[spot * mine_images : (spot + 1) * mine_images]
                gap = act_three[block_of(row * SIDE + spot), columns] - mean
                found.append((reach * slope - second - third * gap).astype(low_type))
            mid_wide[where] = jnp.concatenate(found, axis=0)
            return inner

        return lax.fori_loop(0, SIDE, pixels, carry)

    lax.fori_loop(0, channels // LANES, pull, 0)
    for copy in head_moves:
        copy.wait_recv()
    head_grad = dot_nn(logit_grads[0], pool_all[0]) + dot_nn(logit_grads[1], pool_all[1])
    for spot in range(half // LANES):
        stage[pl.ds(spot, classes, stride=half // LANES), :] = head_grad[
            0:classes, spot * LANES : (spot + 1) * LANES
        ]
    head_space = stage.at[pl.ds(0, grad_head_out.shape[0]), :]
    head_leave = pltpu.make_async_copy(head_space, grad_head_out, sem_local.at[0])
    head_leave.start()

    def drop_into(act, slot, gain, bias, columns):
        size = pl.ds(0, width)
        shift[8:24, size] = jnp.zeros((16, width), wide)

        def drop(index, carry):
            normed = normal(act, slot, index)
            norm = normed * gain + bias
            sig = sigmoid(norm)
            grad = act_three[tile(index), columns] * (sig + norm * sig * (1.0 - sig))
            act_three[tile(index), columns] = grad
            shift[8:16, size] += fold_rows(grad)
            shift[16:24, size] += fold_rows(grad * normed)
            return carry

        lax.fori_loop(0, SIDE, drop, 0)

    def close_back(slot):
        size = pl.ds(0, width)
        sums_mine[slot, 0:1, size] = column_sum(shift[8:16, size])
        sums_mine[slot, 1:2, size] = column_sum(shift[16:24, size])

    space_two, space_one = pl.ds(0, width), pl.ds(width, width)

    def mid_group(which):
        return mid_wide[pl.ds(pl.multiple_of(which * count_rows, count_rows), count_rows), :]

    def back_two(which, carry):
        act_three[:, space_two] += dot_nn(mid_group(which), flat_rows(w_last[which]))
        return carry

    act_three[:, space_two] = jnp.zeros((count_rows, width), wide)
    lax.fori_loop(0, groups, back_two, 0)
    drop_into(act_two, 1, gain_two, bias_two, space_two)
    close_back(4)
    move_back_two = swap(4, width)
    move_back_two.start()

    if gather:
        spread.drain()

    def put(ref, which, value):
        ref[which] = value.astype(low_type).reshape(ref.shape[1:])

    def expand_group(which, carry):
        put(w_last, which, dot_tn(mid_group(which), hidden_two[...]))
        fold_begin(which, 2)
        fold_turn(2, which - 1)
        return carry

    lax.fori_loop(0, groups, expand_group, 0)
    move_back_two.wait()
    terms_two = back_terms(4, 1, width, gain_two)

    def back_act(terms, act, layer, index, columns):
        first, second, third = terms
        gap = act[tile(index), :] - fwd_stats[layer, 0:1, pl.ds(0, width)]
        return (first * act_three[tile(index), columns] - second - third * gap).astype(low_type)

    def grad_two(index, carry):
        taps_two[pl.ds(pl.multiple_of((index + 1) * line, line), line), :] = back_act(
            terms_two, act_two, 1, index, space_two
        )
        return carry

    lax.fori_loop(0, SIDE, grad_two, 0)
    fold_turn(2, groups - 1)
    def middle_row(down, carry):
        for over in range(3):
            left = row_windows(taps_one, down, low_start[over], reaches[over])
            right = row_windows(taps_two, 1, high_start[over], reaches[over])
            rows = pl.ds(pl.multiple_of((3 * down + over) * width, width), width)
            mid_wide[rows, :] = dot_tn(left, right).astype(low_type)
        fold_begin(down, 1)

        @pl.when(down == 2)
        def _():
            fold_begin(3, 1)

        fold_turn(2, groups + down)
        fold_turn(1, down - 1)
        return carry

    lax.fori_loop(0, 3, middle_row, 0)

    def back_one(index, carry):
        down, side = index // 2, index % 2
        columns = lanes(2 + side, piece)
        for over in range(3):
            left = row_windows(taps_two, 2 - down, high_start[over], reaches[over])
            start = pl.multiple_of((3 * down + over) * width + side * piece, piece)
            value = dot_nt(left, w_middle[pl.ds(start, piece), :])
            add_windows(act_three, columns, value, low_start[over], reaches[over])
        when(index < 4, functools.partial(fold_turn, 1, 2 + index))
        return carry

    act_three[:, space_one] = jnp.zeros((count_rows, width), wide)
    lax.fori_loop(0, 6, back_one, 0)
    drop_into(act_one, 0, gain_one, bias_one, space_one)
    close_back(5)
    move_back_one = swap(5, width)
    move_back_one.start()

    move_back_one.wait()
    terms_one = back_terms(5, 0, width, gain_one)

    def grad_one(index, carry):
        hidden_two[tile(index), :] = back_act(terms_one, act_one, 0, index, space_one)
        return carry

    lax.fori_loop(0, SIDE, grad_one, 0)

    def reduce_group(which, carry):
        put(w_first, which, dot_tn(x_all[:, lanes(which, group)], hidden_two[...]))
        fold_begin(which, 0)
        fold_turn(0, which - 1)
        return carry

    lax.fori_loop(0, groups, reduce_group, 0)

    for kind in range(2):
        row = 3 - kind
        pieces = [
            sums_mine[5, row : row + 1, lanes(core, part)],
            sums_mine[4, row : row + 1, lanes(core, part)],
            sums_mine[3, row : row + 1, lanes(core, half)],
        ]
        whole = jnp.concatenate(pieces, axis=1)
        per_kind = whole.shape[1] // LANES
        for spot in range(per_kind):
            grad_norm_out[kind * per_kind + spot : kind * per_kind + spot + 1, :] = whole[
                :, spot * LANES : (spot + 1) * LANES
            ]
    for turn in range(groups - 1, groups + 2):
        fold_turn(0, turn)
    if gather:
        start = 0
        for slot in range(3):
            rows = fold.counts[slot]
            act_three[kept + start : kept + start + rows, half : half + width] = fold.result(slot)
            start += rows
        leave = pltpu.make_async_copy(
            act_three.at[pl.ds(kept, start), pl.ds(half, width)], grads_out, sem_local.at[3]
        )
        leave.start()
        leave.wait()
        fold.drain()
    else:
        outs = [
            pltpu.make_async_copy(ref, out, sem_local.at[slot])
            for slot, (ref, out) in enumerate(zip((w_first, mid_wide.at[pl.ds(0, 9 * width), :], w_last), grads_out))
        ]
        for copy in outs:
            copy.start()
        for copy in outs:
            copy.wait()
    head_leave.wait()
    for copy in to_mate + head_moves:
        copy.wait_send()


def client_pass(gather, classes, features, labels, flag, params, head, weights):
    pixels, half = features.shape
    images = labels.shape[1]
    count_rows, channels = pixels // 2, 2 * half
    width = params.shape[0] // 2 * LANES - half
    head_rows = classes + -classes % 16
    mine_images = images // 2
    line = SIDE * mine_images
    middle = 9 * width
    blocks = 32
    group = channels // SPOTS[0]
    vmem = pl.BlockSpec(memory_space=pltpu.VMEM)
    smem = pl.BlockSpec(memory_space=pltpu.SMEM)
    spots = SPOTS + (2,)
    scratch = [
        pltpu.VMEM((count_rows, channels), low_type),
        pltpu.VMEM((SPOTS[0] * count_rows, group), low_type),
        pltpu.VMEM(spots + (channels // blocks, width), low_type),
        pltpu.VMEM((middle, width), low_type),
        pltpu.VMEM(spots + (channels // blocks, width), low_type),
        pltpu.VMEM((count_rows, width), wide),
        pltpu.VMEM((count_rows, width), wide),
        pltpu.VMEM((count_rows, channels), wide),
        pltpu.VMEM((count_rows + 2 * line, width), low_type),
        pltpu.VMEM((count_rows + 2 * line, width), low_type),
        pltpu.VMEM((count_rows, width), low_type),
        pltpu.VMEM((count_rows, LANES), wide),
        pltpu.VMEM((2, 2, half + width), wide),
        pltpu.VMEM((2, head_rows, half), low_type),
        pltpu.VMEM((mine_images, channels), wide),
        pltpu.VMEM((mine_images, half), low_type),
        pltpu.VMEM((2, mine_images, half), low_type),
        pltpu.VMEM((2, head_rows, mine_images), low_type),
        pltpu.VMEM((6, 8, channels), wide),
        pltpu.VMEM((6, 8, channels), wide),
        pltpu.VMEM((24, max(width, group)), wide),
        pltpu.VMEM((3, 8, channels), wide),
        pltpu.SemaphoreType.DMA((11,)),
        pltpu.SemaphoreType.DMA((2, 6)),
        pltpu.SemaphoreType.DMA((2, 7)),
    ]
    any_space = pl.BlockSpec(memory_space=pl.ANY)
    if gather:
        counts = (channels // blocks, middle // blocks, channels // blocks)
        scratch += [pltpu.SemaphoreType.DMA((2, 3, 3))]
        scratch += [pltpu.SemaphoreType.DMA((2, 4, size)) for size in (6, 8, 6)]
        scratch += [pltpu.VMEM((4, 2, 2, rows, width), low_type) for rows in counts[1:]]
        for lead in ((4, 2), (4,), (4,)):
            scratch += [pltpu.VMEM(lead + (rows, width), low_type) for rows in counts]
        scratch += [pltpu.SemaphoreType.DMA((2, 4, size)) for size in (6, 8, 6, 6)]
        grads_shape = [jax.ShapeDtypeStruct((sum(counts), width), wide)]
        grads_specs = [any_space]
    else:
        grads_shape = [jax.ShapeDtypeStruct(weight.shape, low_type) for weight in weights]
        grads_specs = [any_space] * 3
    return pl.pallas_call(
        functools.partial(client_kernel, gather, images, classes),
        out_shape=grads_shape
        + [
            jax.ShapeDtypeStruct(params.shape, wide),
            jax.ShapeDtypeStruct((classes * half // LANES, LANES), wide),
            jax.ShapeDtypeStruct((8, LANES), wide),
        ],
        in_specs=[any_space, vmem, smem, vmem, vmem] + [any_space] * len(weights),
        out_specs=grads_specs + [vmem, any_space, vmem],
        scratch_shapes=scratch,
        compiler_params=pltpu.CompilerParams(
            collective_id=0, has_side_effects=True, vmem_limit_bytes=VMEM_BYTES
        ),
    )(features, labels, flag, params, head, *weights)


def adam_update(param, grad, first, second, rate, decay):
    first = adam_first * first + (1.0 - adam_first) * grad
    second = adam_second * second + (1.0 - adam_second) * grad * grad
    first_hat = first / (1.0 - adam_first**STEP)
    second_hat = second / (1.0 - adam_second**STEP)
    return (
        param - rate * (first_hat / (jnp.sqrt(second_hat) + adam_epsilon) + decay * param),
        first,
        second,
    )
class GramSum:
    def __init__(self, place, data, total, boxes, sems):
        self.place = place
        self.data = data
        self.total = total
        self.core_box, self.near_box, self.far_box, self.z_box = boxes
        self.sems = sems
        self.copies = []
        self.sizes = (data.shape[0] // 72 * 40 // 32, data.shape[0] // 72 * 32 // 32)

    def rows(self, kind, core, z=None, first=None, second=None):
        size = self.sizes[kind]
        start = core * (16 * (self.sizes[0] + self.sizes[1])) + kind * 16 * self.sizes[0]
        count = 16 * size
        for number, spot, parts in ((4 * size, z, 4), (2 * size, first, 2), (size, second, 2)):
            if spot is None:
                break
            start, count = start + spot * number, number
        return pl.ds(pl.multiple_of(start, 8), count)

    def ways(self, kind):
        p = self.place
        x_way, y_way = (p.x, p.along_x()), (p.y, p.along_y())
        return (x_way, y_way) if kind == 0 else (y_way, x_way)

    def copy(self, phase, kind, turn, src, dst, client, core):
        sems = self.sems
        return remote(
            src, dst, sems.at[0, phase, kind, turn], sems.at[1, phase, kind, turn], client, core
        )

    def launch(self, copy):
        copy.start()
        self.copies.append(copy)

    def down(self, phase, kind, turn):
        p = self.place
        z = (p.others[::-1] + [p.z])[turn]
        (first, first_to), (second, second_to) = self.ways(kind)
        base = self.sizes[0] * kind
        if phase == 0:
            src = self.data.at[self.rows(kind, 1 - p.core, z), :]
            box = self.core_box.at[turn, pl.ds(4 * base, 4 * self.sizes[kind]), :]
            return self.copy(0, kind, turn, src, box, p.client, 1 - p.core)
        if phase == 1:
            src = self.data.at[self.rows(kind, p.core, z, 1 - first), :]
            box = self.near_box.at[turn, pl.ds(2 * base, 2 * self.sizes[kind]), :]
            return self.copy(1, kind, turn, src, box, first_to, p.core)
        if phase == 2:
            src = self.data.at[self.rows(kind, p.core, z, first, 1 - second), :]
            box = self.far_box.at[turn, pl.ds(base, self.sizes[kind]), :]
            return self.copy(2, kind, turn, src, box, second_to, p.core)
        src = self.data.at[self.rows(kind, p.core, z, first, second), :]
        box = self.z_box.at[turn, pl.ds(base, self.sizes[kind]), :]
        return self.copy(3, kind, turn, src, box, p.along_z(2 - turn), p.core)

    def down_step(self, phase, kind, turn):
        p = self.place
        z = (p.others[::-1] + [p.z])[turn]
        (first, _), (second, _) = self.ways(kind)
        self.down(phase, kind, turn).wait_recv()
        spots = (z, first, second)[: phase + 1]
        where = self.rows(kind, p.core, *spots)
        scale = (4, 2, 1)[phase]
        box = (self.core_box, self.near_box, self.far_box)[phase]
        self.data[where, :] += box[turn, pl.ds(scale * self.sizes[0] * kind, scale * self.sizes[kind]), :]
        if phase < 2 or turn < 3:
            self.launch(self.down(phase + 1, kind, turn))

    def up(self, phase, kind, turn):
        p = self.place
        z = ([p.z] + p.others)[turn]
        (first, first_to), (second, second_to) = self.ways(kind)
        if phase == 0:
            ref, to = self.total.at[self.rows(kind, p.core, p.z, first, second), :], p.along_z(turn)
        elif phase == 1:
            ref, to = self.total.at[self.rows(kind, p.core, z, first, second), :], second_to
        elif phase == 2:
            ref, to = self.total.at[self.rows(kind, p.core, z, first), :], first_to
        else:
            ref, to = self.total.at[self.rows(kind, p.core, z), :], p.client
        return self.copy(4 + phase, kind, turn, ref, ref, to, 1 - p.core if phase == 3 else p.core)

    def run(self, extra):
        extra = list(extra)
        kinds = (0, 1)
        for turn in range(4):
            for kind in kinds:
                self.launch(self.down(0, kind, turn))
        for turn in range(6):
            if extra:
                extra.pop(0)()
            for kind in kinds:
                for phase in range(3):
                    if 0 <= turn - phase < 4:
                        self.down_step(phase, kind, turn - phase)
        p = self.place
        for kind in kinds:
            (first, _), (second, _) = self.ways(kind)
            where = self.rows(kind, p.core, p.z, first, second)
            value = self.data[where, :]
            for turn in range(3):
                self.down(3, kind, turn).wait_recv()
                value += self.z_box[turn, pl.ds(self.sizes[0] * kind, self.sizes[kind]), :]
            self.total[where, :] = value
            self.launch(self.up(1, kind, 0))
            for turn in range(3):
                self.launch(self.up(0, kind, turn))
        for turn in range(6):
            for kind in kinds:
                if 1 <= turn < 4:
                    self.up(0, kind, turn - 1).wait_recv()
                    self.launch(self.up(1, kind, turn))
                if 1 <= turn < 5:
                    self.up(1, kind, turn - 1).wait_recv()
                    self.launch(self.up(2, kind, turn - 1))
                if 2 <= turn:
                    self.up(2, kind, turn - 2).wait_recv()
                    self.launch(self.up(3, kind, turn - 2))
        for turn in range(4):
            for kind in kinds:
                self.up(3, kind, turn).wait_recv()

    def drain(self):
        for copy in self.copies:
            copy.wait_send()


class TileSum:
    def __init__(self, place, tiles, boxes, sems):
        self.place = place
        self.tiles = tiles
        self.boxes = boxes
        self.sems = sems

    def copy(self, stage, box):
        p = self.place
        to = (p.client, p.along_x(), p.along_y()) + tuple(p.along_z(step) for step in range(3))
        core = 1 - p.core if box == 0 else p.core
        return remote(
            self.tiles.at[stage], self.boxes.at[box], self.sems.at[0, box], self.sems.at[1, box], to[box], core
        )

    def steps(self):
        def start():
            self.copy(0, 0).start()

        def pair(stage):
            self.copy(stage, stage).wait_recv()
            self.tiles[stage + 1] = self.tiles[stage] + self.boxes[stage]
            if stage < 2:
                self.copy(stage + 1, stage + 1).start()
            else:
                for step in range(3):
                    self.copy(3, 3 + step).start()

        return [start] + [functools.partial(pair, stage) for stage in range(3)]

    def result(self):
        for step in range(3):
            self.copy(3, 3 + step).wait_recv()
        return (self.tiles[3] + self.boxes[3]) + (self.boxes[4] + self.boxes[5])

    def drain(self):
        for stage in range(3):
            self.copy(stage, stage).wait_send()
        for step in range(3):
            self.copy(3, 3 + step).wait_send()


def dot_high(left, right):
    return jnp.dot(left, right, precision=lax.Precision.HIGH, preferred_element_type=wide)


def base_kernel(
    ratios,
    sizes,
    master,
    momentum,
    anchor,
    loss_in,
    grads,
    *rest,
):
    place = Place()
    rest = list(rest)

    def take(count):
        taken = rest[:count]
        del rest[:count]
        return taken

    ortho_out, loss_out = take(2)
    gram, gram_total = take(2)
    gram_boxes = take(4)
    grams, iterate, tiles, tile_boxes = take(4)
    gram_sems, tile_sems = take(2)

    place.greet(True)
    tiles[0] = loss_in[...]
    tile_sum = TileSum(place, tiles, tile_boxes, tile_sems)
    extra = tile_sum.steps()
    extra.pop(0)()

    bounds = [0]
    for size in sizes:
        bounds.append(bounds[-1] + size)
    width = master.shape[1]
    part = width // 2
    for slot in range(3):
        rows = slice(bounds[slot], bounds[slot + 1])
        grad = grads[rows, :] + prox_weight * (master[rows, :] - anchor[rows, :])
        fresh = momentum_decay * momentum[rows, :] + grad
        ortho_out[rows, :] = fresh
        partial = lax.dot_general(
            fresh, fresh, (((0,), (0,)), ((), ())), precision=precise, preferred_element_type=wide
        )
        start = 3 * part * slot
        gram[start : start + part, :] = partial[:part, :part]
        gram[start + part : start + 2 * part, :] = partial[:part, part:]
        gram[start + 2 * part : start + 3 * part, :] = partial[part:, part:]

    gram_sum = GramSum(place, gram, gram_total, gram_boxes, gram_sems)

    gram_sum.run(extra)
    loss_out[...] = tile_sum.result()

    spots = lax.broadcasted_iota(jnp.int32, (part, part), 0)
    diagonal = spots == lax.broadcasted_iota(jnp.int32, (part, part), 1)
    iterate[...] = jnp.zeros_like(iterate)
    for slot in range(3):
        start = 3 * part * slot
        corner = gram_total[start : start + part, :]
        side = gram_total[start + part : start + 2 * part, :]
        end = gram_total[start + 2 * part : start + 3 * part, :]
        trace = jnp.sum(jnp.where(diagonal, corner + end, 0.0))
        factor = 1.0 / (jnp.sqrt(trace) + 1e-07)
        square = factor * factor
        grams[slot, :part, :part] = corner * square
        grams[slot, :part, part:] = side * square
        grams[slot, part:, :part] = side.T * square
        grams[slot, part:, part:] = end * square
        rows = slice(bounds[slot], bounds[slot + 1])
        iterate[slot, : bounds[slot + 1] - bounds[slot], :] = ortho_out[rows, :] * factor

    def turn(count, carry):
        slot = lax.rem(count, 3)
        current = grams[slot]
        mixed = schulz_second * current + schulz_third * dot_high(current, current)
        held = iterate[slot]
        iterate[slot] = schulz_first * held + dot_high(held, mixed)

        @pl.when(count < 3 * (NS_STEPS - 1))
        def _():
            once = schulz_first * current + dot_high(current, mixed)
            grams[slot] = schulz_first * once + dot_high(once, mixed)

        return carry

    lax.fori_loop(0, 3 * NS_STEPS, turn, 0)
    for slot in range(3):
        ortho_out[bounds[slot] : bounds[slot + 1], :] = (
            iterate[slot, : bounds[slot + 1] - bounds[slot], :] * ratios[slot]
        )
    gram_sum.drain()
    tile_sum.drain()


def base_pass(ratios, sizes, master, momentum, anchor, loss_tile, grads):
    rows, width = master.shape
    part = width // 2
    vmem = pl.BlockSpec(memory_space=pltpu.VMEM)
    share = 9 * part // 32
    scratch = [pltpu.VMEM((9 * part, part), wide)] * 2
    scratch += [pltpu.VMEM((4, size, part), wide) for size in (4 * share, 2 * share, share)]
    scratch += [pltpu.VMEM((3, share, part), wide)]
    scratch += [
        pltpu.VMEM((3, width, width), wide),
        pltpu.VMEM((3, max(sizes), width), wide),
        pltpu.VMEM((4, 8, LANES), wide),
        pltpu.VMEM((6, 8, LANES), wide),
        pltpu.SemaphoreType.DMA((2, 8, 2, 4)),
        pltpu.SemaphoreType.DMA((2, 6)),
    ]
    block = jax.ShapeDtypeStruct((rows, width), wide)
    outs = [block, jax.ShapeDtypeStruct((8, LANES), wide)]
    operands = [master, momentum, anchor, loss_tile, grads]
    return pl.pallas_call(
        functools.partial(base_kernel, ratios, sizes),
        out_shape=outs,
        in_specs=[vmem] * len(operands),
        out_specs=[vmem] * len(outs),
        scratch_shapes=scratch,
        compiler_params=pltpu.CompilerParams(
            collective_id=1, has_side_effects=True, vmem_limit_bytes=VMEM_BYTES
        ),
    )(*operands)


def update_kernel(master, momentum, anchor, grads, ortho, *rest):
    norms, grad_norm, heads, grad_head, outs = rest[0:3], rest[3], rest[4:7], rest[7], rest[8:]
    momentum_out, base_out, low_out = outs[0:3]
    held = master[...]
    momentum_out[...] = momentum_decay * momentum[...] + (grads[...] + prox_weight * (held - anchor[...]))
    fresh = held - muon_rate * (ortho[...] + muon_decay * held)
    base_out[...] = fresh
    low_out[...] = fresh.astype(low_type)
    for targets, values, grad, rate, decay in (
        (outs[3:6], norms, grad_norm, norm_rate, 0.0),
        (outs[6:9], heads, grad_head, head_rate, head_decay),
    ):
        updates = adam_update(values[0][...], grad[...], values[1][...], values[2][...], rate, decay)
        for target, value in zip(targets, updates):
            target[...] = value


def update_pass(master, momentum, anchor, grads, ortho, norms, grad_norm, heads, grad_head):
    vmem = pl.BlockSpec(memory_space=pltpu.VMEM)
    operands = [master, momentum, anchor, grads, ortho, *norms, grad_norm, *heads, grad_head]
    outs = [master.shape, master.shape, master.shape] + [grad_norm.shape] * 3 + [grad_head.shape] * 3
    types = [wide, wide, low_type] + [wide] * 6
    return pl.pallas_call(
        update_kernel,
        out_shape=[jax.ShapeDtypeStruct(shape, kind) for shape, kind in zip(outs, types)],
        in_specs=[vmem] * len(operands),
        out_specs=[vmem] * len(outs),
        compiler_params=pltpu.CompilerParams(vmem_limit_bytes=VMEM_BYTES),
    )(*operands)


def gram_of(section):
    return lax.dot_general(section, section, (((0,), (0,)), ((), ())), precision=precise)


def square(gram):
    return jnp.dot(gram, gram, precision=precise)


def times_poly(left, mixed):
    return schulz_first * left + jnp.dot(left, mixed, precision=precise)


def schulz(sections):
    raw_grams = lax.psum(tuple(gram_of(section) for section in sections), ("client", "chan"))
    factors = [1.0 / (jnp.sqrt(jnp.trace(gram)) + 1e-07) for gram in raw_grams]
    current = [section * factor for section, factor in zip(sections, factors)]
    grams = [gram * (factor * factor) for gram, factor in zip(raw_grams, factors)]
    for turn in range(NS_STEPS):
        mixed = [schulz_second * gram + schulz_third * square(gram) for gram in grams]
        current = [times_poly(current[slot], mixed[slot]) for slot in range(3)]
        if turn + 1 < NS_STEPS:
            grams = [
                times_poly(times_poly(grams[slot], mixed[slot]), mixed[slot]) for slot in range(3)
            ]
    return current


def base_far(ratios, bounds, master, momentum, anchor, loss_tile, grads):
    sums = [
        lax.psum_scatter(flat_rows(grad).astype(wide), ("client", "chan"), scatter_dimension=0, tiled=True)
        for grad in grads
    ]
    grad_base = jnp.concatenate(sums, axis=0)
    momentum_new = momentum_decay * momentum + (grad_base + prox_weight * (master - anchor))
    current = schulz([momentum_new[bounds[slot] : bounds[slot + 1]] for slot in range(3)])
    ortho = jnp.concatenate([current[slot] * ratios[slot] for slot in range(3)], axis=0)
    return grad_base, ortho, lax.psum(loss_tile, ("client", "chan"))


def as_stored(rows, shape):
    return with_layout_constraint(rows.reshape(shape), Layout(major_to_minor=tuple(range(len(shape)))))


def on_device(
    features,
    labels,
    mask,
    base_master,
    base_momentum,
    global_base,
    norm_params,
    norm_first,
    norm_second,
    head,
    head_first,
    head_second,
):
    halves = lax.axis_size("chan")
    blocks = lax.axis_size("client") * halves
    half = features.shape[2]
    width = base_master.shape[2]
    channels = half * halves
    classes = head.shape[2]
    rows_first = channels // blocks
    rows_mid = 9 * width // blocks
    sizes = (rows_first, rows_mid, rows_first)
    bounds = (0, rows_first, rows_first + rows_mid, base_master.shape[1])
    ratio = (channels / width) ** 0.5
    ratios = (ratio, 3.0, ratio)
    master, momentum, anchor = base_master[0], base_momentum[0], global_base[0]
    norms = [value.reshape(-1, LANES) for value in (norm_params, norm_first, norm_second)]
    heads = [jnp.transpose(value, (2, 0, 1)).reshape(-1, LANES) for value in (head, head_first, head_second)]
    near = lax.axis_size("client") == SPOTS[0] * SPOTS[1] * SPOTS[2]
    if near:
        weights = [master]
    else:
        low_master = master.astype(low_type)
        weights = [
            lax.all_gather(low_master[bounds[slot] : bounds[slot + 1]], ("client", "chan"), axis=0, tiled=True)
            for slot in range(3)
        ]
        split = SPOTS + (2, channels // 32, width)
        weights = [weights[0].reshape(split), weights[1], weights[2].reshape(split)]
    *grads, grad_norm, grad_head, loss_tile = client_pass(
        near, classes, features[0], labels, mask, norms[0], heads[0], weights
    )
    if near:
        (grad_base,) = grads
        ortho, loss_tile = base_pass(ratios, sizes, master, momentum, anchor, loss_tile, grad_base)
    else:
        grad_base, ortho, loss_tile = base_far(ratios, bounds, master, momentum, anchor, loss_tile, grads)
    momentum_new, base_new, base_low, *fresh = update_pass(
        master, momentum, anchor, grad_base, ortho, norms, grad_norm, heads, grad_head
    )
    fresh_norms = [as_stored(value, norm_params.shape) for value in fresh[:3]]
    fresh_heads = [jnp.transpose(as_stored(value, (classes, 1, half)), (1, 2, 0)) for value in fresh[3:]]
    return (
        loss_tile[0, 0:2],
        base_new[None],
        momentum_new[None],
        base_low[None],
        *fresh_norms,
        *fresh_heads,
    )


def solution(mesh):
    wide_block = P(("client", "chan"), None, None)
    norm_block = P("client", None, "chan", None)
    head_block = P("client", "chan", None)
    return jax.shard_map(
        on_device,
        mesh=mesh,
        in_specs=(P("client", None, "chan"), P("client", None), P("client"))
        + (wide_block,) * 3
        + (norm_block,) * 3
        + (head_block,) * 3,
        out_specs=(P(),) + (wide_block,) * 3 + (norm_block,) * 3 + (head_block,) * 3,
        check_vma=False,
    )
```

```python
import functools

import jax
import jax.numpy as jnp
from jax import lax
from jax.experimental import pallas as pl
from jax.experimental.layout import Layout, with_layout_constraint
from jax.experimental.pallas import tpu as pltpu
from jax.sharding import PartitionSpec as P

NS_STEPS = 5
STEP = 10

low_type = jnp.bfloat16
wide = jnp.float32
MESH = pl.DeviceIdType.MESH
precise = lax.Precision.HIGHEST
norm_epsilon = 1e-05
prox_weight = 0.05
momentum_decay = 0.95
muon_rate = 0.3
muon_decay = 0.1
schulz_first = 3.4445
schulz_second = -4.775
schulz_third = 2.0315
adam_first = 0.9
adam_second = 0.95
adam_epsilon = 1e-08
head_rate = 0.01
head_decay = 0.05
norm_rate = 0.5

SIDE = 7
PIXELS = SIDE * SIDE
LANES = 128
SPOTS = (4, 2, 2)
VMEM_BYTES = 62 * 2**20


def when(condition, call):
    if isinstance(condition, bool):
        if condition:
            call()
    else:
        pl.when(condition)(call)


def dot_nn(left, right):
    return jnp.dot(left, right, preferred_element_type=wide)


def dot_nt(left, right):
    return lax.dot_general(left, right, (((1,), (1,)), ((), ())), preferred_element_type=wide)


def dot_tn(left, right):
    return lax.dot_general(left, right, (((0,), (0,)), ((), ())), preferred_element_type=wide)


def flat_rows(block):
    return block.reshape(-1, block.shape[-1])


def sigmoid(value):
    return 0.5 * jnp.tanh(0.5 * value) + 0.5


def fold_rows(value):
    return jnp.sum(value.reshape(value.shape[0] // 8, 8, value.shape[1]), axis=0)


def column_sum(value):
    return jnp.sum(value, axis=0, keepdims=True)


def remote(src, dst, send_sem, recv_sem, client, core):
    return pltpu.make_async_remote_copy(
        src_ref=src,
        dst_ref=dst,
        send_sem=send_sem,
        recv_sem=recv_sem,
        device_id=(client, core),
        device_id_type=MESH,
    )


class Place:
    def __init__(self):
        self.client = lax.axis_index("client")
        self.core = lax.axis_index("chan")
        self.z = self.client // 4
        self.y = (self.client // 2) % 2
        self.x = self.client % 2
        self.others = [
            self.z + 1 - 2 * (self.z % 2),
            (self.z + 2) % 4,
            3 - self.z,
        ]

    def at(self, z, y, x):
        return z * 4 + y * 2 + x

    def along_x(self):
        return self.at(self.z, self.y, 1 - self.x)

    def along_y(self):
        return self.at(self.z, 1 - self.y, self.x)

    def along_z(self, step):
        return self.at(self.others[step], self.y, self.x)

    def greet(self, whole, across=False):
        barrier = pltpu.get_barrier_semaphore()
        pairs = [(self.client, 1 - self.core)]
        if whole:
            pairs += [(self.along_x(), self.core), (self.along_y(), self.core)]
            pairs += [(self.along_z(step), self.core) for step in range(3)]
        if across:
            pairs += [(self.along_x(), 1 - self.core)]
        for pair in pairs:
            pl.semaphore_signal(barrier, inc=1, device_id=pair, device_id_type=MESH)
        pl.semaphore_wait(barrier, len(pairs))


def cut_rows(counts):
    pieces = []
    for slot, rows in enumerate(counts):
        middle = (rows // 16 + 1) // 2 * 16
        pieces.append((slot, 0, middle, 0))
        pieces.append((slot, middle, rows - middle, 1))
    return pieces


def block_ref(ref, size, z, y, x, core, start, count):
    if len(ref.shape) == 2:
        first = (((z * 2 + y) * 2 + x) * 2 + core) * size + start
        return ref.at[pl.ds(pl.multiple_of(first, 16), count), :]
    return ref.at[z, y, x, core, pl.ds(start, count), :]


class Spread:
    def __init__(self, place, weights, counts, sems):
        self.place = place
        self.weights = weights
        self.counts = counts
        self.pieces = cut_rows(counts)
        self.z_sems, self.near_sems, self.far_sems, self.core_sems = sems
        self.order = [place.z] + place.others

    def z_copy(self, step, slot):
        p = self.place
        ref = block_ref(self.weights[slot], self.counts[slot], p.z, p.y, p.x, p.core, 0, self.counts[slot])
        sems = self.z_sems
        return remote(ref, ref, sems.at[0, step, slot], sems.at[1, step, slot], p.along_z(step), p.core)

    def near_copy(self, turn, number):
        p = self.place
        slot, start, count, way = self.pieces[number]
        ref = block_ref(self.weights[slot], self.counts[slot], self.order[turn], p.y, p.x, p.core, start, count)
        sems = self.near_sems
        return remote(
            ref, ref, sems.at[0, turn, number], sems.at[1, turn, number], (p.along_x, p.along_y)[way](), p.core
        )

    def far_copies(self, turn, number):
        p = self.place
        slot, start, count, way = self.pieces[number]
        spot = self.order[turn]
        sems = self.far_sems
        copies = []
        for part, other in enumerate((0, 1) if slot == 1 else (slice(None),)):
            y, x = (p.y, other) if way == 0 else (other, p.x)
            ref = block_ref(self.weights[slot], self.counts[slot], spot, y, x, p.core, start, count)
            sem = number + 4 * part
            to = (p.along_y, p.along_x)[way]()
            copies.append(remote(ref, ref, sems.at[0, turn, sem], sems.at[1, turn, sem], to, p.core))
        return copies

    def core_copies(self, turn, slot):
        p = self.place
        sems = self.core_sems
        copies = []
        pairs = [(y, x) for y in (0, 1) for x in (0, 1)] if slot == 1 else [(slice(None), slice(None))]
        for part, (y, x) in enumerate(pairs):
            ref = block_ref(self.weights[slot], self.counts[slot], self.order[turn], y, x, p.core, 0, self.counts[slot])
            sem = (0, 2 + part, 1)[slot]
            copies.append(remote(ref, ref, sems.at[0, turn, sem], sems.at[1, turn, sem], p.client, 1 - p.core))
        return copies

    def begin(self, master):
        p = self.place
        start = 0
        for slot in range(3):
            rows = self.counts[slot]
            own = block_ref(self.weights[slot], self.counts[slot], p.z, p.y, p.x, p.core, 0, rows)
            own[...] = master[start : start + rows, :].astype(low_type)
            start += rows
        for step in range(3):
            self.z_copy(step, 0).start()
        self.near_start(0)

    def near_start(self, slot):
        for number in (2 * slot, 2 * slot + 1):
            self.near_copy(0, number).start()

    def steps(self):
        near, far, core, start = self.near_step, self.far_step, self.core_step, self.near_start
        groups = [
            [(far, 0, 0), (start, 1)],
            [(near, 1, 0)],
            [(near, 2, 0), (near, 3, 0)],
            [(far, 1, 0), (core, 0, 0), (far, 0, 1)],
            [(far, 2, 0), (far, 3, 0), (core, 1, 0)],
            [(core, 2, 0), (core, 3, 0), (near, 1, 1), (start, 2)],
            [(core, 0, 1), (near, 2, 1)],
            [(far, 1, 1), (near, 3, 1)],
            [(core, 1, 1), (far, 2, 1), (far, 0, 2)],
            [(far, 3, 1), (core, 2, 1), (near, 1, 2)],
            [(core, 3, 1), (core, 0, 2), (near, 2, 2)],
            [(far, 1, 2), (near, 3, 2)],
            [(core, 1, 2), (far, 2, 2)],
            [(far, 3, 2), (core, 2, 2)],
            [(core, 3, 2)],
        ]
        return [[functools.partial(*step) for step in group] for group in groups]

    def near_step(self, turn, slot):
        self.z_copy(turn - 1, slot).wait_recv()
        for number in (2 * slot, 2 * slot + 1):
            self.near_copy(turn, number).start()
        if slot < 2:
            self.z_copy(turn - 1, slot + 1).start()

    def far_step(self, turn, slot):
        for number in (2 * slot, 2 * slot + 1):
            self.near_copy(turn, number).wait_recv()
            for copy in self.far_copies(turn, number):
                copy.start()

    def core_step(self, turn, slot):
        for number in (2 * slot, 2 * slot + 1):
            for copy in self.far_copies(turn, number):
                copy.wait_recv()
        for copy in self.core_copies(turn, slot):
            copy.start()

    def arrive(self, slot):
        for turn in range(4):
            for copy in self.core_copies(turn, slot):
                copy.wait_recv()

    def drain(self):
        for slot in range(3):
            for step in range(3):
                self.z_copy(step, slot).wait_send()
            for turn in range(4):
                for copy in self.core_copies(turn, slot):
                    copy.wait_send()
        for number in range(6):
            for turn in range(4):
                self.near_copy(turn, number).wait_send()
                for copy in self.far_copies(turn, number):
                    copy.wait_send()


class Fold:
    def __init__(self, place, grads, counts, parts):
        self.place = place
        self.grads = grads
        self.counts = counts
        self.pieces = cut_rows(counts)
        self.core_boxes = [parts[1], parts[0], parts[1]]
        self.near_boxes, self.far_boxes, self.z_boxes = [parts[3 * k + 2 : 3 * k + 5] for k in range(3)]
        self.core_sems, self.near_sems, self.far_sems, self.z_sems = parts[11:]

    def core_copies(self, which, slot):
        p = self.place
        sems = self.core_sems
        copies = []
        pairs = [(y, x) for y in (0, 1) for x in (0, 1)] if slot == 1 else [(slice(None), slice(None))]
        for part, (y, x) in enumerate(pairs):
            ref = block_ref(self.grads[slot], self.counts[slot], which, y, x, 1 - p.core, 0, self.counts[slot])
            box = self.core_boxes[slot].at[which, y, x]
            sem = (0, 2 + part, 1)[slot]
            copies.append(remote(ref, box, sems.at[0, which, sem], sems.at[1, which, sem], p.client, 1 - p.core))
        return copies

    def near_copies(self, which, number):
        p = self.place
        slot, start, count, way = self.pieces[number]
        sems = self.near_sems
        copies = []
        for part, other in enumerate((0, 1) if slot == 1 else (slice(None),)):
            y, x = (other, 1 - p.x) if way == 0 else (1 - p.y, other)
            ref = block_ref(self.grads[slot], self.counts[slot], which, y, x, p.core, start, count)
            box = self.near_boxes[slot].at[which, other, pl.ds(start, count), :]
            sem = number + 4 * part
            to = (p.along_x, p.along_y)[way]()
            copies.append(remote(ref, box, sems.at[0, which, sem], sems.at[1, which, sem], to, p.core))
        return copies

    def far_copy(self, which, number):
        p = self.place
        slot, start, count, way = self.pieces[number]
        y, x = (1 - p.y, p.x) if way == 0 else (p.y, 1 - p.x)
        ref = block_ref(self.grads[slot], self.counts[slot], which, y, x, p.core, start, count)
        box = self.far_boxes[slot].at[which, pl.ds(start, count), :]
        sems = self.far_sems
        return remote(
            ref, box, sems.at[0, which, number], sems.at[1, which, number], (p.along_y, p.along_x)[way](), p.core
        )

    def z_copy(self, which, sender, number):
        p = self.place
        slot, start, count, _ = self.pieces[number]
        rows = pl.ds(start, count)
        sems = self.z_sems
        return remote(
            block_ref(self.grads[slot], self.counts[slot], which, p.y, p.x, p.core, start, count),
            self.z_boxes[slot].at[sender, rows, :],
            sems.at[0, which, number],
            sems.at[1, sender, number],
            p.at(which, p.y, p.x),
            p.core,
        )

    def begin(self, which, slot):
        for copy in self.core_copies(which, slot):
            copy.start()

    def add(self, slot, spots, start, count, box):
        ref = block_ref(self.grads[slot], self.counts[slot], *spots, self.place.core, start, count)
        ref[...] = (ref[...].astype(wide) + box.astype(wide)).astype(low_type)

    def turn(self, slot, turn):
        for lag, step in ((2, self.far_step), (1, self.near_step), (0, self.core_step)):
            when((turn >= lag) & (turn < lag + 4), functools.partial(step, turn - lag, slot))

    def core_step(self, which, slot):
        for copy in self.core_copies(which, slot):
            copy.wait_recv()
        pairs = [(y, x) for y in (0, 1) for x in (0, 1)] if slot == 1 else [(slice(None), slice(None))]
        for y, x in pairs:
            self.add(slot, (which, y, x), 0, self.counts[slot], self.core_boxes[slot][which, y, x])
        for number in (2 * slot, 2 * slot + 1):
            for copy in self.near_copies(which, number):
                copy.start()

    def near_step(self, which, slot):
        p = self.place
        for number in (2 * slot, 2 * slot + 1):
            _, start, count, way = self.pieces[number]
            for copy in self.near_copies(which, number):
                copy.wait_recv()
            for other in (0, 1) if slot == 1 else (slice(None),):
                y, x = (other, p.x) if way == 0 else (p.y, other)
                box = self.near_boxes[slot][which, other, pl.ds(start, count), :]
                self.add(slot, (which, y, x), start, count, box)
            self.far_copy(which, number).start()

    def far_step(self, which, slot):
        p = self.place
        for number in (2 * slot, 2 * slot + 1):
            _, start, count, way = self.pieces[number]
            self.far_copy(which, number).wait_recv()
            box = self.far_boxes[slot][which, pl.ds(start, count), :]
            self.add(slot, (which, p.y, p.x), start, count, box)

            @pl.when(p.z != which)
            def _():
                self.z_copy(which, p.z, number).start()

    def result(self, slot):
        p = self.place
        self.z_boxes[slot][p.z] = block_ref(self.grads[slot], self.counts[slot], p.z, p.y, p.x, p.core, 0, self.counts[slot])[...]
        for sender in range(4):

            @pl.when(p.z != sender)
            def _():
                for number in (2 * slot, 2 * slot + 1):
                    self.z_copy(sender, sender, number).wait_recv()

        total = self.z_boxes[slot][0].astype(wide)
        for sender in range(1, 4):
            total += self.z_boxes[slot][sender].astype(wide)
        return total

    def drain(self):
        for which in range(4):
            for slot in range(3):
                for copy in self.core_copies(which, slot):
                    copy.wait_send()
            for number in range(6):
                for copy in self.near_copies(which, number):
                    copy.wait_send()
                self.far_copy(which, number).wait_send()

            @pl.when(self.place.z != which)
            def _():
                for number in range(6):
                    self.z_copy(which, self.place.z, number).wait_send()


def norm_stats(mine, theirs, count):
    gap = mine[0:1] - theirs[0:1]
    mean = 0.5 * (mine[0:1] + theirs[0:1])
    spread = mine[1:2] + theirs[1:2] + gap * gap * (0.5 * count)
    return mean, lax.rsqrt(spread / (2.0 * count) + norm_epsilon)


def client_kernel(
    gather,
    images,
    classes,
    features,
    labels,
    flag,
    params,
    head,
    *rest,
):
    if gather:
        master, *rest = rest
    else:
        first_in, middle_in, last_in, *rest = rest
    if gather:
        grads_out, *rest = rest
    else:
        grads_out, rest = rest[:3], rest[3:]
    (
        grad_norm_out,
        grad_head_out,
        loss_out,
        x_all,
        mid_wide,
        w_first,
        w_middle,
        w_last,
        act_one,
        act_two,
        act_three,
        taps_one,
        taps_two,
        hidden_two,
        stage,
        params_all,
        head_all,
        grad_pool,
        pool_send,
        pool_all,
        logit_grads,
        sums_mine,
        sums_theirs,
        shift,
        fwd_stats,
        sem_local,
        sem_swap,
        sem_misc,
        *near_parts,
    ) = rest
    place = Place()
    core = place.core
    mate = (place.client, 1 - core)
    count_rows, channels = x_all.shape
    half = channels // 2
    width = act_one.shape[1]
    part = width // 2
    mine_images = images // 2
    line = SIDE * mine_images
    total_rows = 2.0 * count_rows

    def tile(index):
        return pl.ds(pl.multiple_of(index * line, line), line)

    def lanes(index, size):
        return pl.ds(pl.multiple_of(index * size, size), size)

    place.greet(gather)

    quarter = half // 2
    own_rows = pl.ds(pl.multiple_of(core * count_rows, count_rows), count_rows)
    mate_rows = pl.ds(pl.multiple_of((1 - core) * count_rows, count_rows), count_rows)
    top_rows = pl.ds(0, count_rows)
    own_copies = [
        pltpu.make_async_copy(
            features.at[own_rows, pl.ds(side * quarter, quarter)], buffer, sem_local.at[side]
        )
        for side, buffer in enumerate((hidden_two, mid_wide.at[top_rows, :]))
    ]
    per_kind = params.shape[0] // 2
    for kind in range(2):
        rows = [params[kind * per_kind + spot : kind * per_kind + spot + 1, :] for spot in range(per_kind)]
        params_all[core, kind : kind + 1, :] = jnp.concatenate(rows, axis=1)
    head_all[core] = jnp.zeros(head_all.shape[1:], low_type)
    for spot in range(half // LANES):
        head_all[core, 0:classes, spot * LANES : (spot + 1) * LANES] = head[
            pl.ds(spot, classes, stride=half // LANES), :
        ].astype(low_type)
    to_mate = [
        remote(params_all.at[core], params_all.at[core], sem_misc.at[0, 0], sem_misc.at[1, 0], *mate),
        remote(head_all.at[core], head_all.at[core], sem_misc.at[0, 1], sem_misc.at[1, 1], *mate),
    ]
    for side, buffer in enumerate((taps_one, taps_two)):
        to_mate.append(
            remote(
                features.at[mate_rows, pl.ds(side * quarter, quarter)],
                buffer.at[top_rows, :],
                sem_misc.at[0, 5 + side],
                sem_misc.at[1, 5 + side],
                *mate,
            )
        )
    for copy in to_mate + own_copies:
        copy.start()

    weights = (w_first, w_middle, w_last)
    if gather:
        counts = [channels // 32, 9 * width // 32, channels // 32]
        spread = Spread(place, weights, counts, near_parts[:4])
        held = act_three.at[pl.ds(0, master.shape[0]), pl.ds(0, width)]
        load = pltpu.make_async_copy(master, held, sem_local.at[8])
        load.start()
        load.wait()
        spread.begin(held)
        fold = Fold(place, (w_first, mid_wide, w_last), counts, near_parts[4:])
        due = spread.steps()
    else:
        loads = [
            pltpu.make_async_copy(src, dst, sem_local.at[8 + slot])
            for slot, (src, dst) in enumerate(zip((first_in, middle_in, last_in), weights))
        ]
        for load in loads:
            load.start()
        due = []

    def advance(count):
        for group in due[:count]:
            for step in group:
                step()
        del due[:count]

    def advance_at(index, spots):
        for spot, group in zip(spots, due):

            @pl.when(index == spot)
            def _():
                for step in group:
                    step()

    def arrive(slot, left):
        if gather:
            advance(len(due) - left)
            spread.arrive(slot)
        else:
            loads[slot].wait()

    def fold_turn(slot, turn):
        if gather:
            fold.turn(slot, turn)

    def fold_step(kind, slot, which):
        if gather:
            (fold.core_step, fold.near_step, fold.far_step)[kind](which, slot)

    def fold_at(index, spot, *steps):
        @pl.when(index == spot)
        def _():
            for step in steps:
                fold_step(*step)

    def fold_begin(which, slot):
        if gather:
            fold.begin(which, slot)

    def zero_edges(buffer):
        edge = jnp.zeros((line,) + buffer.shape[1:], low_type)
        buffer[0:line, :] = edge
        buffer[line + count_rows : 2 * line + count_rows, :] = edge

    advance(3)
    for copy in own_copies:
        copy.wait()

    def turn_from(source, base):
        def turn(index, carry):
            stage[...] = source(lanes(index, LANES)).astype(wide)

            def pixel(spot, inner):
                x_all[
                    pl.ds(pl.multiple_of(spot * mine_images, mine_images), mine_images),
                    pl.ds(pl.multiple_of(base + index * LANES, LANES), LANES),
                ] = stage[pl.ds(spot, mine_images, stride=PIXELS), :].astype(low_type)
                return inner

            return lax.fori_loop(0, PIXELS, pixel, carry, unroll=7)

        return turn

    quarters = quarter // LANES
    own_base, mate_base = core * half, (1 - core) * half
    lax.fori_loop(0, quarters, turn_from(lambda columns: hidden_two[:, columns], own_base), 0)
    advance(1)
    lax.fori_loop(
        0,
        quarters,
        turn_from(lambda columns: mid_wide[0:count_rows, columns], own_base + quarter),
        0,
    )
    advance(1)
    for copy in to_mate:
        copy.wait_recv()
    lax.fori_loop(0, quarters, turn_from(lambda columns: taps_one[0:count_rows, columns], mate_base), 0)
    advance(1)
    lax.fori_loop(0, quarters, turn_from(lambda columns: taps_two[0:count_rows, columns], mate_base + quarter), 0)
    zero_edges(taps_one)
    zero_edges(taps_two)
    arrive(0, 9)

    def swap(slot, size):
        return remote(
            sums_mine.at[slot, :, pl.ds(0, size)],
            sums_theirs.at[slot, :, pl.ds(0, size)],
            sem_swap.at[0, slot],
            sem_swap.at[1, slot],
            *mate,
        )

    def gain_bias(lower, upper):
        rows = []
        for kind in range(2):
            pieces = [params_all[side, kind : kind + 1, lower:upper] for side in range(2)]
            rows.append(jnp.concatenate(pieces, axis=1))
        return rows

    def collect(index, value, columns, size):
        @pl.when(index == 0)
        def _():
            shift[0:1, pl.ds(0, size)] = column_sum(fold_rows(value)) / value.shape[0]
            shift[8:24, pl.ds(0, size)] = jnp.zeros((16, size), wide)

        gap = value - shift[0:1, pl.ds(0, size)]
        shift[8:16, pl.ds(0, size)] += fold_rows(gap)
        shift[16:24, pl.ds(0, size)] += fold_rows(gap * gap)

    def close_stats(slot, columns, size):
        sum_gap = column_sum(shift[8:16, pl.ds(0, size)])
        sum_square = column_sum(shift[16:24, pl.ds(0, size)])
        sums_mine[slot, 0:1, columns] = shift[0:1, pl.ds(0, size)] + sum_gap / count_rows
        sums_mine[slot, 1:2, columns] = sum_square - sum_gap * sum_gap / count_rows

    def look_over(act, columns):
        def look(index, carry):
            collect(index, act[tile(index), columns], None, width)
            return carry

        lax.fori_loop(0, SIDE, look, 0)

    groups = SPOTS[0]
    group = channels // groups

    def settle(slot, size):
        mean, scale = norm_stats(
            sums_mine[slot, 0:2, pl.ds(0, size)], sums_theirs[slot, 0:2, pl.ds(0, size)], float(count_rows)
        )
        fwd_stats[slot, 0:1, pl.ds(0, size)] = mean
        fwd_stats[slot, 1:2, pl.ds(0, size)] = scale

    whole_width = pl.ds(0, width)

    def first_part(index, carry):
        act_one[...] += dot_nn(x_all[:, lanes(index, group)], flat_rows(w_first[index]))
        advance_at(index, (0, 1, 2))
        return carry

    act_one[...] = jnp.zeros_like(act_one)
    lax.fori_loop(0, groups, first_part, 0)
    del due[:3]
    look_over(act_one, whole_width)
    close_stats(0, whole_width, width)
    move = swap(0, width)
    move.start()
    advance(1)
    move.wait()
    settle(0, width)

    gain_one, bias_one = gain_bias(0, part)
    gain_two, bias_two = gain_bias(part, width)
    gain_three, bias_three = gain_bias(width, width + half)

    def normal(act, slot, index):
        mean = fwd_stats[slot, 0:1, pl.ds(0, width)]
        return (act[tile(index), :] - mean) * fwd_stats[slot, 1:2, pl.ds(0, width)]

    def hide_one(index, carry):
        value = normal(act_one, 0, index) * gain_one + bias_one
        taps_one[pl.ds(pl.multiple_of((index + 1) * line, line), line), :] = (value * sigmoid(value)).astype(low_type)
        return carry

    lax.fori_loop(0, SIDE, hide_one, 0)
    arrive(1, 4)

    step = mine_images
    piece = width // 2

    def row_windows(buffer, down, start, reach):
        if reach == line:
            return buffer[pl.ds(pl.multiple_of(down * line, line), count_rows), :]
        windows = [
            buffer[pl.ds(pl.multiple_of((down + row) * line + start, step), reach), :] for row in range(SIDE)
        ]
        return jnp.concatenate(windows, axis=0)

    def add_windows(target, columns, value, start, reach):
        for row in range(SIDE):
            rows = slice(row * line + start, row * line + start + reach)
            target[rows, columns] += value[row * reach : (row + 1) * reach]

    low_start, high_start, reaches = (0, 0, step), (step, 0, 0), (line - step, line, line - step)

    def second_part(index, carry):
        down, columns = index // 2, lanes(index % 2, piece)
        for over in range(3):
            left = row_windows(taps_one, down, low_start[over], reaches[over])
            kernel = w_middle[pl.ds(pl.multiple_of((3 * down + over) * width, width), width), columns]
            add_windows(act_two, columns, dot_nn(left, kernel), high_start[over], reaches[over])
        advance_at(index, (1, 3, 5))
        return carry

    act_two[...] = jnp.zeros_like(act_two)
    lax.fori_loop(0, 6, second_part, 0)
    del due[:3]
    look_over(act_two, whole_width)
    close_stats(1, whole_width, width)
    move_two = swap(1, width)
    move_two.start()
    move_two.wait()
    settle(1, width)

    def hide_two(index, carry):
        value = normal(act_two, 1, index) * gain_two + bias_two
        hidden_two[tile(index), :] = (value * sigmoid(value)).astype(low_type)
        return carry

    lax.fori_loop(0, SIDE, hide_two, 0)

    arrive(2, 0)

    def third_group(which, carry):
        columns = lanes(which, group)
        act_three[:, columns] = dot_nt(hidden_two[...], flat_rows(w_last[which]))
        look_over(act_three, columns)
        close_stats(2, columns, group)
        return carry

    lax.fori_loop(0, groups, third_group, 0)
    move_three = swap(2, channels)
    move_three.start()
    move_three.wait()
    settle(2, channels)
    fwd_stats[2, 2:3, :] = gain_three
    fwd_stats[2, 3:4, :] = bias_three

    per_group = group // LANES

    def block_of(spot):
        return pl.ds(pl.multiple_of(spot * mine_images, mine_images), mine_images)

    def mid_line(which, index):
        return pl.ds(pl.multiple_of(which * count_rows + index * line, line), line)

    kept = channels // LANES * mine_images

    def gathered(kind):
        starts = range(kind * kept, (kind + 1) * kept, mine_images)
        return jnp.concatenate([stage[start : start + mine_images, :] for start in starts], axis=1)

    def emit(index, carry):
        columns = lanes(index, LANES)
        mean, scale = fwd_stats[2, 0:1, columns], fwd_stats[2, 1:2, columns]
        gain, bias = fwd_stats[2, 2:3, columns], fwd_stats[2, 3:4, columns]

        def pixels(row, sums):
            pooled, slopes, slopes_normed = sums
            found = []
            for spot in range(SIDE):
                where = block_of(row * SIDE + spot)
                normed = (act_three[where, columns] - mean) * scale
                total = normed * gain + bias + x_all[where, columns].astype(wide)
                sig = sigmoid(total)
                out = total * sig
                slope = sig + out * (1.0 - sig)
                found.append(slope.astype(low_type))
                pooled, slopes, slopes_normed = pooled + out, slopes + slope, slopes_normed + slope * normed
            mid_wide[mid_line(index // per_group, row), lanes(index % per_group, LANES)] = jnp.concatenate(
                found, axis=0
            )
            return pooled, slopes, slopes_normed

        zero = jnp.zeros((mine_images, LANES), wide)
        pooled, slopes, slopes_normed = lax.fori_loop(0, SIDE, pixels, (zero, zero, zero))
        for kind, value in enumerate((pooled, slopes, slopes_normed)):
            stage[pl.ds(pl.multiple_of(kind * kept + index * mine_images, mine_images), mine_images), :] = value
        return carry

    lax.fori_loop(0, channels // LANES, emit, 0)

    pooled = (gathered(0) / PIXELS).astype(low_type)
    head_full = jnp.concatenate([head_all[0], head_all[1]], axis=1)
    logits = dot_nt(head_full, pooled)
    spots = lax.broadcasted_iota(jnp.int32, logits.shape, 0)
    inside = spots < classes
    first_labels, second_labels = labels[0:1, 0:mine_images], labels[0:1, mine_images:]
    onehot = (spots == jnp.where(core == 0, first_labels, second_labels)).astype(wide)
    top = jnp.max(jnp.where(inside, logits, -jnp.inf), axis=0, keepdims=True)
    powers = jnp.where(inside, jnp.exp(logits - top), 0.0)
    power_sum = jnp.sum(powers, axis=0, keepdims=True)
    picked = jnp.sum(logits * onehot, axis=0, keepdims=True)
    each_loss = top + jnp.log(power_sum) - picked
    taking = flag[0].astype(wide)
    tile_spots = lax.broadcasted_iota(jnp.int32, loss_out.shape, 1)
    loss_out[...] = jnp.where(tile_spots == 0, taking * jnp.sum(each_loss), taking * mine_images)
    grads = (taking / images * (powers / power_sum - onehot)).astype(low_type)
    grad_pool[...] = dot_tn(grads, head_full) / PIXELS
    logit_grads[core] = grads
    pool_all[core] = pooled[:, 0:half]
    pool_send[...] = pooled[:, half:]

    @pl.when(core == 1)
    def _():
        pool_all[core] = pooled[:, half:]
        pool_send[...] = pooled[:, 0:half]

    head_moves = [
        remote(pool_send, pool_all.at[core], sem_misc.at[0, 3], sem_misc.at[1, 3], *mate),
        remote(logit_grads.at[core], logit_grads.at[core], sem_misc.at[0, 4], sem_misc.at[1, 4], *mate),
    ]

    sums_mine[3, 0:1, :] = column_sum(grad_pool[...] * gathered(1))
    sums_mine[3, 1:2, :] = column_sum(grad_pool[...] * gathered(2))
    move_back = swap(3, channels)
    move_back.start()
    for copy in head_moves:
        copy.start()
    move_back.wait()

    def back_terms(slot, layer, size, gain):
        columns = pl.ds(0, size)
        sums = sums_mine[slot, 0:2, columns] + sums_theirs[slot, 0:2, columns]
        sums_mine[slot, 2:4, columns] = sums
        scale = fwd_stats[layer, 1:2, columns]
        return (
            scale * gain,
            scale * gain * sums[0:1] / total_rows,
            scale * scale * gain * sums[1:2] / total_rows,
        )

    first, second, third = back_terms(3, 2, channels, gain_three)
    fwd_stats[2, 4:5, :] = first
    fwd_stats[2, 5:6, :] = second
    fwd_stats[2, 6:7, :] = third

    def pull(index, carry):
        columns = lanes(index, LANES)
        mean = fwd_stats[2, 0:1, columns]
        first, second = fwd_stats[2, 4:5, columns], fwd_stats[2, 5:6, columns]
        third = fwd_stats[2, 6:7, columns]
        reach = grad_pool[:, columns] * first

        def pixels(row, inner):
            where = (mid_line(index // per_group, row), lanes(index % per_group, LANES))
            slopes = mid_wide[where].astype(wide)
            found = []
            for spot in range(SIDE):
                slope = slopes[spot * mine_images : (spot + 1) * mine_images]
                gap = act_three[block_of(row * SIDE + spot), columns] - mean
                found.append((reach * slope - second - third * gap).astype(low_type))
            mid_wide[where] = jnp.concatenate(found, axis=0)
            return inner

        return lax.fori_loop(0, SIDE, pixels, carry)

    lax.fori_loop(0, channels // LANES, pull, 0)
    for copy in head_moves:
        copy.wait_recv()
    head_grad = dot_nn(logit_grads[0], pool_all[0]) + dot_nn(logit_grads[1], pool_all[1])
    for spot in range(half // LANES):
        stage[pl.ds(spot, classes, stride=half // LANES), :] = head_grad[
            0:classes, spot * LANES : (spot + 1) * LANES
        ]
    head_space = stage.at[pl.ds(0, grad_head_out.shape[0]), :]
    head_leave = pltpu.make_async_copy(head_space, grad_head_out, sem_local.at[0])
    head_leave.start()

    def drop_into(act, slot, gain, bias, columns):
        size = pl.ds(0, width)
        shift[8:24, size] = jnp.zeros((16, width), wide)

        def drop(index, carry):
            normed = normal(act, slot, index)
            norm = normed * gain + bias
            sig = sigmoid(norm)
            grad = act_three[tile(index), columns] * (sig + norm * sig * (1.0 - sig))
            act_three[tile(index), columns] = grad
            shift[8:16, size] += fold_rows(grad)
            shift[16:24, size] += fold_rows(grad * normed)
            return carry

        lax.fori_loop(0, SIDE, drop, 0)

    def close_back(slot):
        size = pl.ds(0, width)
        sums_mine[slot, 0:1, size] = column_sum(shift[8:16, size])
        sums_mine[slot, 1:2, size] = column_sum(shift[16:24, size])

    space_two, space_one = pl.ds(0, width), pl.ds(width, width)

    def mid_group(which):
        return mid_wide[pl.ds(pl.multiple_of(which * count_rows, count_rows), count_rows), :]

    def back_two(which, carry):
        act_three[:, space_two] += dot_nn(mid_group(which), flat_rows(w_last[which]))
        return carry

    act_three[:, space_two] = jnp.zeros((count_rows, width), wide)
    lax.fori_loop(0, groups, back_two, 0)
    drop_into(act_two, 1, gain_two, bias_two, space_two)
    close_back(4)
    move_back_two = swap(4, width)
    move_back_two.start()

    if gather:
        spread.drain()

    def put(ref, which, value):
        ref[which] = value.astype(low_type).reshape(ref.shape[1:])

    def expand_group(which, carry):
        put(w_last, which, dot_tn(mid_group(which), hidden_two[...]))
        fold_begin(which, 2)
        fold_turn(2, which - 1)
        return carry

    lax.fori_loop(0, groups, expand_group, 0)
    move_back_two.wait()
    terms_two = back_terms(4, 1, width, gain_two)

    def back_act(terms, act, layer, index, columns):
        first, second, third = terms
        gap = act[tile(index), :] - fwd_stats[layer, 0:1, pl.ds(0, width)]
        return (first * act_three[tile(index), columns] - second - third * gap).astype(low_type)

    def grad_two(index, carry):
        taps_two[pl.ds(pl.multiple_of((index + 1) * line, line), line), :] = back_act(
            terms_two, act_two, 1, index, space_two
        )
        return carry

    lax.fori_loop(0, SIDE, grad_two, 0)
    fold_turn(2, groups - 1)
    def middle_row(down, carry):
        for over in range(3):
            left = row_windows(taps_one, down, low_start[over], reaches[over])
            right = row_windows(taps_two, 1, high_start[over], reaches[over])
            rows = pl.ds(pl.multiple_of((3 * down + over) * width, width), width)
            mid_wide[rows, :] = dot_tn(left, right).astype(low_type)
        fold_begin(down, 1)

        @pl.when(down == 2)
        def _():
            fold_begin(3, 1)

        fold_turn(2, groups + down)
        fold_at(down, 1, (0, 1, 0))
        fold_at(down, 2, (1, 1, 0), (0, 1, 1))
        return carry

    lax.fori_loop(0, 3, middle_row, 0)

    def back_one(index, carry):
        down, side = index // 2, index % 2
        columns = lanes(2 + side, piece)
        for over in range(3):
            left = row_windows(taps_two, 2 - down, high_start[over], reaches[over])
            start = pl.multiple_of((3 * down + over) * width + side * piece, piece)
            value = dot_nt(left, w_middle[pl.ds(start, piece), :])
            add_windows(act_three, columns, value, low_start[over], reaches[over])
        fold_at(index, 0, (0, 1, 2))
        fold_at(index, 1, (0, 1, 3))
        fold_at(index, 2, (1, 1, 1))
        fold_at(index, 3, (2, 1, 0))
        fold_at(index, 4, (1, 1, 2))
        fold_at(index, 5, (2, 1, 1))
        return carry

    act_three[:, space_one] = jnp.zeros((count_rows, width), wide)
    lax.fori_loop(0, 6, back_one, 0)
    drop_into(act_one, 0, gain_one, bias_one, space_one)
    fold_step(1, 1, 3)
    close_back(5)
    move_back_one = swap(5, width)
    move_back_one.start()

    move_back_one.wait()
    terms_one = back_terms(5, 0, width, gain_one)

    def grad_one(index, carry):
        hidden_two[tile(index), :] = back_act(terms_one, act_one, 0, index, space_one)
        return carry

    lax.fori_loop(0, SIDE, grad_one, 0)
    fold_step(2, 1, 2)

    def reduce_group(which, carry):
        put(w_first, which, dot_tn(x_all[:, lanes(which, group)], hidden_two[...]))
        fold_begin(which, 0)
        fold_turn(0, which - 1)
        fold_at(which, 1, (2, 1, 3))
        return carry

    lax.fori_loop(0, groups, reduce_group, 0)

    for kind in range(2):
        row = 3 - kind
        pieces = [
            sums_mine[5, row : row + 1, lanes(core, part)],
            sums_mine[4, row : row + 1, lanes(core, part)],
            sums_mine[3, row : row + 1, lanes(core, half)],
        ]
        whole = jnp.concatenate(pieces, axis=1)
        per_kind = whole.shape[1] // LANES
        for spot in range(per_kind):
            grad_norm_out[kind * per_kind + spot : kind * per_kind + spot + 1, :] = whole[
                :, spot * LANES : (spot + 1) * LANES
            ]
    for turn in range(groups - 1, groups + 2):
        fold_turn(0, turn)
    if gather:
        start = 0
        for slot in range(3):
            rows = fold.counts[slot]
            act_three[kept + start : kept + start + rows, half : half + width] = fold.result(slot)
            start += rows
        leave = pltpu.make_async_copy(
            act_three.at[pl.ds(kept, start), pl.ds(half, width)], grads_out, sem_local.at[3]
        )
        leave.start()
        leave.wait()
        fold.drain()
    else:
        outs = [
            pltpu.make_async_copy(ref, out, sem_local.at[slot])
            for slot, (ref, out) in enumerate(zip((w_first, mid_wide.at[pl.ds(0, 9 * width), :], w_last), grads_out))
        ]
        for copy in outs:
            copy.start()
        for copy in outs:
            copy.wait()
    head_leave.wait()
    for copy in to_mate + head_moves:
        copy.wait_send()


def client_pass(gather, classes, features, labels, flag, params, head, weights):
    pixels, half = features.shape
    images = labels.shape[1]
    count_rows, channels = pixels // 2, 2 * half
    width = params.shape[0] // 2 * LANES - half
    head_rows = classes + -classes % 16
    mine_images = images // 2
    line = SIDE * mine_images
    middle = 9 * width
    blocks = 32
    group = channels // SPOTS[0]
    vmem = pl.BlockSpec(memory_space=pltpu.VMEM)
    smem = pl.BlockSpec(memory_space=pltpu.SMEM)
    spots = SPOTS + (2,)
    scratch = [
        pltpu.VMEM((count_rows, channels), low_type),
        pltpu.VMEM((SPOTS[0] * count_rows, group), low_type),
        pltpu.VMEM(spots + (channels // blocks, width), low_type),
        pltpu.VMEM((middle, width), low_type),
        pltpu.VMEM(spots + (channels // blocks, width), low_type),
        pltpu.VMEM((count_rows, width), wide),
        pltpu.VMEM((count_rows, width), wide),
        pltpu.VMEM((count_rows, channels), wide),
        pltpu.VMEM((count_rows + 2 * line, width), low_type),
        pltpu.VMEM((count_rows + 2 * line, width), low_type),
        pltpu.VMEM((count_rows, width), low_type),
        pltpu.VMEM((count_rows, LANES), wide),
        pltpu.VMEM((2, 2, half + width), wide),
        pltpu.VMEM((2, head_rows, half), low_type),
        pltpu.VMEM((mine_images, channels), wide),
        pltpu.VMEM((mine_images, half), low_type),
        pltpu.VMEM((2, mine_images, half), low_type),
        pltpu.VMEM((2, head_rows, mine_images), low_type),
        pltpu.VMEM((6, 8, channels), wide),
        pltpu.VMEM((6, 8, channels), wide),
        pltpu.VMEM((24, max(width, group)), wide),
        pltpu.VMEM((3, 8, channels), wide),
        pltpu.SemaphoreType.DMA((11,)),
        pltpu.SemaphoreType.DMA((2, 6)),
        pltpu.SemaphoreType.DMA((2, 7)),
    ]
    any_space = pl.BlockSpec(memory_space=pl.ANY)
    if gather:
        counts = (channels // blocks, middle // blocks, channels // blocks)
        scratch += [pltpu.SemaphoreType.DMA((2, 3, 3))]
        scratch += [pltpu.SemaphoreType.DMA((2, 4, size)) for size in (6, 8, 6)]
        scratch += [pltpu.VMEM((4, 2, 2, rows, width), low_type) for rows in counts[1:]]
        for lead in ((4, 2), (4,), (4,)):
            scratch += [pltpu.VMEM(lead + (rows, width), low_type) for rows in counts]
        scratch += [pltpu.SemaphoreType.DMA((2, 4, size)) for size in (6, 8, 6, 6)]
        grads_shape = [jax.ShapeDtypeStruct((sum(counts), width), wide)]
        grads_specs = [any_space]
    else:
        grads_shape = [jax.ShapeDtypeStruct(weight.shape, low_type) for weight in weights]
        grads_specs = [any_space] * 3
    return pl.pallas_call(
        functools.partial(client_kernel, gather, images, classes),
        out_shape=grads_shape
        + [
            jax.ShapeDtypeStruct(params.shape, wide),
            jax.ShapeDtypeStruct((classes * half // LANES, LANES), wide),
            jax.ShapeDtypeStruct((8, LANES), wide),
        ],
        in_specs=[any_space, vmem, smem, vmem, vmem] + [any_space] * len(weights),
        out_specs=grads_specs + [vmem, any_space, vmem],
        scratch_shapes=scratch,
        compiler_params=pltpu.CompilerParams(
            collective_id=0, has_side_effects=True, vmem_limit_bytes=VMEM_BYTES
        ),
    )(features, labels, flag, params, head, *weights)


def adam_update(param, grad, first, second, rate, decay):
    first = adam_first * first + (1.0 - adam_first) * grad
    second = adam_second * second + (1.0 - adam_second) * grad * grad
    first_hat = first / (1.0 - adam_first**STEP)
    second_hat = second / (1.0 - adam_second**STEP)
    return (
        param - rate * (first_hat / (jnp.sqrt(second_hat) + adam_epsilon) + decay * param),
        first,
        second,
    )
class GramSum:
    def __init__(self, place, data, total, boxes, sems):
        self.place = place
        self.data = data
        self.total = total
        self.core_box, self.near_box, self.far_box, self.z_box = boxes
        self.sems = sems
        self.copies = []
        self.sizes = (data.shape[0] // 72 * 40 // 32, data.shape[0] // 72 * 32 // 32)

    def rows(self, kind, core, z=None, first=None, second=None):
        size = self.sizes[kind]
        start = core * (16 * (self.sizes[0] + self.sizes[1])) + kind * 16 * self.sizes[0]
        count = 16 * size
        for number, spot, parts in ((4 * size, z, 4), (2 * size, first, 2), (size, second, 2)):
            if spot is None:
                break
            start, count = start + spot * number, number
        return pl.ds(pl.multiple_of(start, 8), count)

    def ways(self, kind):
        p = self.place
        x_way, y_way = (p.x, p.along_x()), (p.y, p.along_y())
        return (x_way, y_way) if kind == 0 else (y_way, x_way)

    def copy(self, phase, kind, turn, src, dst, client, core):
        sems = self.sems
        return remote(
            src, dst, sems.at[0, phase, kind, turn], sems.at[1, phase, kind, turn], client, core
        )

    def launch(self, copy):
        copy.start()
        self.copies.append(copy)

    def down(self, phase, kind, turn):
        p = self.place
        z = (p.others[::-1] + [p.z])[turn]
        (first, first_to), (second, second_to) = self.ways(kind)
        base = self.sizes[0] * kind
        if phase == 0:
            src = self.data.at[self.rows(kind, 1 - p.core, z), :]
            box = self.core_box.at[turn, pl.ds(4 * base, 4 * self.sizes[kind]), :]
            return self.copy(0, kind, turn, src, box, p.client, 1 - p.core)
        if phase == 1:
            src = self.data.at[self.rows(kind, p.core, z, 1 - first), :]
            box = self.near_box.at[turn, pl.ds(2 * base, 2 * self.sizes[kind]), :]
            return self.copy(1, kind, turn, src, box, first_to, p.core)
        if phase == 2:
            src = self.data.at[self.rows(kind, p.core, z, first, 1 - second), :]
            box = self.far_box.at[turn, pl.ds(base, self.sizes[kind]), :]
            return self.copy(2, kind, turn, src, box, second_to, p.core)
        src = self.data.at[self.rows(kind, p.core, z, first, second), :]
        box = self.z_box.at[turn, pl.ds(base, self.sizes[kind]), :]
        return self.copy(3, kind, turn, src, box, p.along_z(2 - turn), p.core)

    def down_step(self, phase, kind, turn):
        p = self.place
        z = (p.others[::-1] + [p.z])[turn]
        (first, _), (second, _) = self.ways(kind)
        self.down(phase, kind, turn).wait_recv()
        spots = (z, first, second)[: phase + 1]
        where = self.rows(kind, p.core, *spots)
        scale = (4, 2, 1)[phase]
        box = (self.core_box, self.near_box, self.far_box)[phase]
        self.data[where, :] += box[turn, pl.ds(scale * self.sizes[0] * kind, scale * self.sizes[kind]), :]
        if phase < 2 or turn < 3:
            self.launch(self.down(phase + 1, kind, turn))

    def up(self, phase, kind, turn):
        p = self.place
        z = ([p.z] + p.others)[turn]
        (first, first_to), (second, second_to) = self.ways(kind)
        if phase == 0:
            ref, to = self.total.at[self.rows(kind, p.core, p.z, first, second), :], p.along_z(turn)
        elif phase == 1:
            ref, to = self.total.at[self.rows(kind, p.core, z, first, second), :], second_to
        elif phase == 2:
            ref, to = self.total.at[self.rows(kind, p.core, z, first), :], first_to
        else:
            ref, to = self.total.at[self.rows(kind, p.core, z), :], p.client
        return self.copy(4 + phase, kind, turn, ref, ref, to, 1 - p.core if phase == 3 else p.core)

    def run(self, extra):
        extra = list(extra)
        kinds = (0, 1)
        for turn in range(4):
            for kind in kinds:
                self.launch(self.down(0, kind, turn))
        for turn in range(6):
            if extra:
                extra.pop(0)()
            for kind in kinds:
                for phase in range(3):
                    if 0 <= turn - phase < 4:
                        self.down_step(phase, kind, turn - phase)
        p = self.place
        for kind in kinds:
            (first, _), (second, _) = self.ways(kind)
            where = self.rows(kind, p.core, p.z, first, second)
            value = self.data[where, :]
            for turn in range(3):
                self.down(3, kind, turn).wait_recv()
                value += self.z_box[turn, pl.ds(self.sizes[0] * kind, self.sizes[kind]), :]
            self.total[where, :] = value
            self.launch(self.up(1, kind, 0))
            for turn in range(3):
                self.launch(self.up(0, kind, turn))
        for turn in range(6):
            for kind in kinds:
                if 1 <= turn < 4:
                    self.up(0, kind, turn - 1).wait_recv()
                    self.launch(self.up(1, kind, turn))
                if 1 <= turn < 5:
                    self.up(1, kind, turn - 1).wait_recv()
                    self.launch(self.up(2, kind, turn - 1))
                if 2 <= turn:
                    self.up(2, kind, turn - 2).wait_recv()
                    self.launch(self.up(3, kind, turn - 2))
        for turn in range(4):
            for kind in kinds:
                self.up(3, kind, turn).wait_recv()

    def drain(self):
        for copy in self.copies:
            copy.wait_send()


class TileSum:
    def __init__(self, place, tiles, boxes, sems):
        self.place = place
        self.tiles = tiles
        self.boxes = boxes
        self.sems = sems

    def copy(self, stage, box):
        p = self.place
        to = (p.client, p.along_x(), p.along_y()) + tuple(p.along_z(step) for step in range(3))
        core = 1 - p.core if box == 0 else p.core
        return remote(
            self.tiles.at[stage], self.boxes.at[box], self.sems.at[0, box], self.sems.at[1, box], to[box], core
        )

    def steps(self):
        def start():
            self.copy(0, 0).start()

        def pair(stage):
            self.copy(stage, stage).wait_recv()
            self.tiles[stage + 1] = self.tiles[stage] + self.boxes[stage]
            if stage < 2:
                self.copy(stage + 1, stage + 1).start()
            else:
                for step in range(3):
                    self.copy(3, 3 + step).start()

        return [start] + [functools.partial(pair, stage) for stage in range(3)]

    def result(self):
        for step in range(3):
            self.copy(3, 3 + step).wait_recv()
        return (self.tiles[3] + self.boxes[3]) + (self.boxes[4] + self.boxes[5])

    def drain(self):
        for stage in range(3):
            self.copy(stage, stage).wait_send()
        for step in range(3):
            self.copy(3, 3 + step).wait_send()


def dot_high(left, right):
    return jnp.dot(left, right, precision=lax.Precision.HIGH, preferred_element_type=wide)


class Share:
    def __init__(self, place, sizes, buffers, sems):
        self.place = place
        self.sizes = sizes
        self.fresh, self.rows_in, self.rows_out, self.back = buffers
        self.sems = sems
        self.bounds = [0, sizes[0], sizes[0] + sizes[1], sum(sizes)]
        p = place
        self.duty = jnp.where(p.x == 1, 1, 2 * p.core)
        self.mine = p.x * 2 + p.core

    def section(self, slot):
        return pl.ds(self.bounds[slot], self.sizes[slot])

    def spot(self, slot, x, core):
        number = x if slot == 1 else x * 2 + core
        return pl.ds(pl.multiple_of(number * self.sizes[slot], 16), self.sizes[slot])

    def doer(self, slot):
        return (0, 0) if slot == 0 else (0, 1) if slot == 2 else (1, self.place.core)

    def out_copy(self, slot):
        p = self.place
        x, core = self.doer(slot)
        return remote(
            self.fresh.at[self.section(slot), :],
            self.rows_in.at[self.spot(slot, p.x, p.core), :],
            self.sems.at[0, slot],
            self.sems.at[1, self.mine],
            p.at(p.z, p.y, x),
            core,
        )

    def in_copy(self, slot, x, core):
        p = self.place
        return remote(
            self.fresh.at[self.section(slot), :],
            self.rows_in.at[self.spot(slot, x, core), :],
            self.sems.at[0, slot],
            self.sems.at[1, x * 2 + core],
            p.at(p.z, p.y, x),
            core,
        )

    def back_copy(self, slot, x, core):
        p = self.place
        return remote(
            self.rows_out.at[self.spot(slot, x, core), :],
            self.back.at[self.section(slot), :],
            self.sems.at[0, 3 + x * 2 + core],
            self.sems.at[1, 4 + slot],
            p.at(p.z, p.y, x),
            core,
        )

    def users(self, slot):
        p = self.place
        if slot == 1:
            return [(0, p.core), (1, p.core)]
        return [(x, core) for x in (0, 1) for core in (0, 1)]

    def send(self):
        for slot in range(3):

            @pl.when(self.duty != slot)
            def _():
                self.out_copy(slot).start()

            @pl.when(self.duty == slot)
            def _():
                self.rows_in[self.spot(slot, self.place.x, self.place.core), :] = self.fresh[self.section(slot), :]

    def gather(self):
        p = self.place
        for slot in range(3):

            @pl.when(self.duty == slot)
            def _():
                for x, core in self.users(slot):

                    @pl.when((p.x != x) | (p.core != core))
                    def _():
                        self.in_copy(slot, x, core).wait_recv()

    def give_back(self):
        p = self.place
        for slot in range(3):

            @pl.when(self.duty == slot)
            def _():
                for x, core in self.users(slot):

                    @pl.when((p.x != x) | (p.core != core))
                    def _():
                        self.back_copy(slot, x, core).start()

                self.back[self.section(slot), :] = self.rows_out[self.spot(slot, p.x, p.core), :]

    def finish(self):
        p = self.place
        for slot in range(3):

            @pl.when(self.duty != slot)
            def _():
                self.back_copy(slot, p.x, p.core).wait_recv()
                self.out_copy(slot).wait_send()

            @pl.when(self.duty == slot)
            def _():
                for x, core in self.users(slot):

                    @pl.when((p.x != x) | (p.core != core))
                    def _():
                        self.back_copy(slot, x, core).wait_send()


def base_kernel(
    ratios,
    sizes,
    master,
    momentum,
    anchor,
    loss_in,
    grads,
    *rest,
):
    place = Place()
    rest = list(rest)

    def take(count):
        taken = rest[:count]
        del rest[:count]
        return taken

    ortho_out, loss_out = take(2)
    gram, gram_total = take(2)
    gram_boxes = take(4)
    grams, fresh, rows_in, rows_out, back, tiles, tile_boxes = take(7)
    gram_sems, tile_sems, share_sems = take(3)

    rows_in[...] = jnp.zeros_like(rows_in)
    place.greet(True, True)
    fresh[...] = momentum_decay * momentum[...] + (grads[...] + prox_weight * (master[...] - anchor[...]))
    share = Share(place, sizes, (fresh, rows_in, rows_out, back), share_sems)
    share.send()
    tiles[0] = loss_in[...]
    tile_sum = TileSum(place, tiles, tile_boxes, tile_sems)
    extra = tile_sum.steps()
    extra.pop(0)()

    width = master.shape[1]
    part = width // 2
    for slot in range(3):
        section = fresh[share.section(slot), :]
        partial = lax.dot_general(
            section, section, (((0,), (0,)), ((), ())), precision=precise, preferred_element_type=wide
        )
        start = 3 * part * slot
        gram[start : start + part, :] = partial[:part, :part]
        gram[start + part : start + 2 * part, :] = partial[:part, part:]
        gram[start + 2 * part : start + 3 * part, :] = partial[part:, part:]

    gram_sum = GramSum(place, gram, gram_total, gram_boxes, gram_sems)
    gram_sum.run(extra)
    loss_out[...] = tile_sum.result()

    spots = lax.broadcasted_iota(jnp.int32, (part, part), 0)
    diagonal = spots == lax.broadcasted_iota(jnp.int32, (part, part), 1)
    start = 3 * part * share.duty
    corner = gram_total[pl.ds(pl.multiple_of(start, part), part), :]
    side = gram_total[pl.ds(pl.multiple_of(start + part, part), part), :]
    end = gram_total[pl.ds(pl.multiple_of(start + 2 * part, part), part), :]
    trace = jnp.sum(jnp.where(diagonal, corner + end, 0.0))
    factor = 1.0 / (jnp.sqrt(trace) + 1e-07)
    square = factor * factor
    grams[:part, :part] = corner * square
    grams[:part, part:] = side * square
    grams[part:, :part] = side.T * square
    grams[part:, part:] = end * square
    share.gather()
    rows_in[...] = rows_in[...] * factor

    def turn(count, carry):
        current = grams[...]
        mixed = schulz_second * current + schulz_third * dot_high(current, current)
        held = rows_in[...]
        rows_in[...] = schulz_first * held + dot_high(held, mixed)

        @pl.when(count < NS_STEPS - 1)
        def _():
            once = schulz_first * current + dot_high(current, mixed)
            grams[...] = schulz_first * once + dot_high(once, mixed)

        return carry

    lax.fori_loop(0, NS_STEPS, turn, 0)
    ratio = jnp.where(share.duty == 1, ratios[1], ratios[0])
    rows_out[...] = (rows_in[...] * ratio).astype(low_type)
    share.give_back()
    share.finish()
    ortho_out[...] = back[...].astype(wide)
    gram_sum.drain()
    tile_sum.drain()


def base_pass(ratios, sizes, master, momentum, anchor, loss_tile, grads):
    rows, width = master.shape
    part = width // 2
    vmem = pl.BlockSpec(memory_space=pltpu.VMEM)
    share = 9 * part // 32
    scratch = [pltpu.VMEM((9 * part, part), wide)] * 2
    scratch += [pltpu.VMEM((4, size, part), wide) for size in (4 * share, 2 * share, share)]
    scratch += [pltpu.VMEM((3, share, part), wide)]
    scratch += [
        pltpu.VMEM((width, width), wide),
        pltpu.VMEM((rows, width), wide),
        pltpu.VMEM((max(4 * sizes[0], 2 * sizes[1]), width), wide),
        pltpu.VMEM((max(4 * sizes[0], 2 * sizes[1]), width), low_type),
        pltpu.VMEM((rows, width), low_type),
        pltpu.VMEM((4, 8, LANES), wide),
        pltpu.VMEM((6, 8, LANES), wide),
        pltpu.SemaphoreType.DMA((2, 8, 2, 4)),
        pltpu.SemaphoreType.DMA((2, 6)),
        pltpu.SemaphoreType.DMA((2, 7)),
    ]
    block = jax.ShapeDtypeStruct((rows, width), wide)
    outs = [block, jax.ShapeDtypeStruct((8, LANES), wide)]
    operands = [master, momentum, anchor, loss_tile, grads]
    return pl.pallas_call(
        functools.partial(base_kernel, ratios, sizes),
        out_shape=outs,
        in_specs=[vmem] * len(operands),
        out_specs=[vmem] * len(outs),
        scratch_shapes=scratch,
        compiler_params=pltpu.CompilerParams(
            collective_id=1, has_side_effects=True, vmem_limit_bytes=VMEM_BYTES
        ),
    )(*operands)


def update_kernel(master, momentum, anchor, grads, ortho, *rest):
    norms, grad_norm, heads, grad_head, outs = rest[0:3], rest[3], rest[4:7], rest[7], rest[8:]
    momentum_out, base_out, low_out = outs[0:3]
    held = master[...]
    momentum_out[...] = momentum_decay * momentum[...] + (grads[...] + prox_weight * (held - anchor[...]))
    fresh = held - muon_rate * (ortho[...] + muon_decay * held)
    base_out[...] = fresh
    low_out[...] = fresh.astype(low_type)
    for targets, values, grad, rate, decay in (
        (outs[3:6], norms, grad_norm, norm_rate, 0.0),
        (outs[6:9], heads, grad_head, head_rate, head_decay),
    ):
        updates = adam_update(values[0][...], grad[...], values[1][...], values[2][...], rate, decay)
        for target, value in zip(targets, updates):
            target[...] = value


def update_pass(master, momentum, anchor, grads, ortho, norms, grad_norm, heads, grad_head):
    vmem = pl.BlockSpec(memory_space=pltpu.VMEM)
    operands = [master, momentum, anchor, grads, ortho, *norms, grad_norm, *heads, grad_head]
    outs = [master.shape, master.shape, master.shape] + [grad_norm.shape] * 3 + [grad_head.shape] * 3
    types = [wide, wide, low_type] + [wide] * 6
    return pl.pallas_call(
        update_kernel,
        out_shape=[jax.ShapeDtypeStruct(shape, kind) for shape, kind in zip(outs, types)],
        in_specs=[vmem] * len(operands),
        out_specs=[vmem] * len(outs),
        compiler_params=pltpu.CompilerParams(vmem_limit_bytes=VMEM_BYTES),
    )(*operands)


def gram_of(section):
    return lax.dot_general(section, section, (((0,), (0,)), ((), ())), precision=precise)


def square(gram):
    return jnp.dot(gram, gram, precision=precise)


def times_poly(left, mixed):
    return schulz_first * left + jnp.dot(left, mixed, precision=precise)


def schulz(sections):
    raw_grams = lax.psum(tuple(gram_of(section) for section in sections), ("client", "chan"))
    factors = [1.0 / (jnp.sqrt(jnp.trace(gram)) + 1e-07) for gram in raw_grams]
    current = [section * factor for section, factor in zip(sections, factors)]
    grams = [gram * (factor * factor) for gram, factor in zip(raw_grams, factors)]
    for turn in range(NS_STEPS):
        mixed = [schulz_second * gram + schulz_third * square(gram) for gram in grams]
        current = [times_poly(current[slot], mixed[slot]) for slot in range(3)]
        if turn + 1 < NS_STEPS:
            grams = [
                times_poly(times_poly(grams[slot], mixed[slot]), mixed[slot]) for slot in range(3)
            ]
    return current


def base_far(ratios, bounds, master, momentum, anchor, loss_tile, grads):
    sums = [
        lax.psum_scatter(flat_rows(grad).astype(wide), ("client", "chan"), scatter_dimension=0, tiled=True)
        for grad in grads
    ]
    grad_base = jnp.concatenate(sums, axis=0)
    momentum_new = momentum_decay * momentum + (grad_base + prox_weight * (master - anchor))
    current = schulz([momentum_new[bounds[slot] : bounds[slot + 1]] for slot in range(3)])
    ortho = jnp.concatenate([current[slot] * ratios[slot] for slot in range(3)], axis=0)
    return grad_base, ortho, lax.psum(loss_tile, ("client", "chan"))


def as_stored(rows, shape):
    return with_layout_constraint(rows.reshape(shape), Layout(major_to_minor=tuple(range(len(shape)))))


def on_device(
    features,
    labels,
    mask,
    base_master,
    base_momentum,
    global_base,
    norm_params,
    norm_first,
    norm_second,
    head,
    head_first,
    head_second,
):
    halves = lax.axis_size("chan")
    blocks = lax.axis_size("client") * halves
    half = features.shape[2]
    width = base_master.shape[2]
    channels = half * halves
    classes = head.shape[2]
    rows_first = channels // blocks
    rows_mid = 9 * width // blocks
    sizes = (rows_first, rows_mid, rows_first)
    bounds = (0, rows_first, rows_first + rows_mid, base_master.shape[1])
    ratio = (channels / width) ** 0.5
    ratios = (ratio, 3.0, ratio)
    master, momentum, anchor = base_master[0], base_momentum[0], global_base[0]
    norms = [value.reshape(-1, LANES) for value in (norm_params, norm_first, norm_second)]
    heads = [jnp.transpose(value, (2, 0, 1)).reshape(-1, LANES) for value in (head, head_first, head_second)]
    near = lax.axis_size("client") == SPOTS[0] * SPOTS[1] * SPOTS[2]
    if near:
        weights = [master]
    else:
        low_master = master.astype(low_type)
        weights = [
            lax.all_gather(low_master[bounds[slot] : bounds[slot + 1]], ("client", "chan"), axis=0, tiled=True)
            for slot in range(3)
        ]
        split = SPOTS + (2, channels // 32, width)
        weights = [weights[0].reshape(split), weights[1], weights[2].reshape(split)]
    *grads, grad_norm, grad_head, loss_tile = client_pass(
        near, classes, features[0], labels, mask, norms[0], heads[0], weights
    )
    if near:
        (grad_base,) = grads
        ortho, loss_tile = base_pass(ratios, sizes, master, momentum, anchor, loss_tile, grad_base)
    else:
        grad_base, ortho, loss_tile = base_far(ratios, bounds, master, momentum, anchor, loss_tile, grads)
    momentum_new, base_new, base_low, *fresh = update_pass(
        master, momentum, anchor, grad_base, ortho, norms, grad_norm, heads, grad_head
    )
    fresh_norms = [as_stored(value, norm_params.shape) for value in fresh[:3]]
    fresh_heads = [jnp.transpose(as_stored(value, (classes, 1, half)), (1, 2, 0)) for value in fresh[3:]]
    return (
        loss_tile[0, 0:2],
        base_new[None],
        momentum_new[None],
        base_low[None],
        *fresh_norms,
        *fresh_heads,
    )


def solution(mesh):
    wide_block = P(("client", "chan"), None, None)
    norm_block = P("client", None, "chan", None)
    head_block = P("client", "chan", None)
    return jax.shard_map(
        on_device,
        mesh=mesh,
        in_specs=(P("client", None, "chan"), P("client", None), P("client"))
        + (wide_block,) * 3
        + (norm_block,) * 3
        + (head_block,) * 3,
        out_specs=(P(),) + (wide_block,) * 3 + (norm_block,) * 3 + (head_block,) * 3,
        check_vma=False,
    )
```

```python
import functools

import jax
import jax.numpy as jnp
from jax import lax
from jax.experimental import pallas as pl
from jax.experimental.layout import Layout, with_layout_constraint
from jax.experimental.pallas import tpu as pltpu
from jax.sharding import PartitionSpec as P

NS_STEPS = 5
STEP = 10

low_type = jnp.bfloat16
wide = jnp.float32
MESH = pl.DeviceIdType.MESH
precise = lax.Precision.HIGHEST
norm_epsilon = 1e-05
prox_weight = 0.05
momentum_decay = 0.95
muon_rate = 0.3
muon_decay = 0.1
schulz_first = 3.4445
schulz_second = -4.775
schulz_third = 2.0315
adam_first = 0.9
adam_second = 0.95
adam_epsilon = 1e-08
head_rate = 0.01
head_decay = 0.05
norm_rate = 0.5

SIDE = 7
PIXELS = SIDE * SIDE
LANES = 128
SPOTS = (4, 2, 2)
VMEM_BYTES = 62 * 2**20


def when(condition, call):
    if isinstance(condition, bool):
        if condition:
            call()
    else:
        pl.when(condition)(call)


def dot_nn(left, right):
    return jnp.dot(left, right, preferred_element_type=wide)


def dot_nt(left, right):
    return lax.dot_general(left, right, (((1,), (1,)), ((), ())), preferred_element_type=wide)


def dot_tn(left, right):
    return lax.dot_general(left, right, (((0,), (0,)), ((), ())), preferred_element_type=wide)


def flat_rows(block):
    return block.reshape(-1, block.shape[-1])


def sigmoid(value):
    return 0.5 * jnp.tanh(0.5 * value) + 0.5


def fold_rows(value):
    return jnp.sum(value.reshape(value.shape[0] // 8, 8, value.shape[1]), axis=0)


def column_sum(value):
    return jnp.sum(value, axis=0, keepdims=True)


def remote(src, dst, send_sem, recv_sem, client, core):
    return pltpu.make_async_remote_copy(
        src_ref=src,
        dst_ref=dst,
        send_sem=send_sem,
        recv_sem=recv_sem,
        device_id=(client, core),
        device_id_type=MESH,
    )


class Place:
    def __init__(self):
        self.client = lax.axis_index("client")
        self.core = lax.axis_index("chan")
        self.z = self.client // 4
        self.y = (self.client // 2) % 2
        self.x = self.client % 2
        self.others = [
            self.z + 1 - 2 * (self.z % 2),
            (self.z + 2) % 4,
            3 - self.z,
        ]

    def at(self, z, y, x):
        return z * 4 + y * 2 + x

    def along_x(self):
        return self.at(self.z, self.y, 1 - self.x)

    def along_y(self):
        return self.at(self.z, 1 - self.y, self.x)

    def along_z(self, step):
        return self.at(self.others[step], self.y, self.x)

    def greet(self, whole, across=False):
        barrier = pltpu.get_barrier_semaphore()
        pairs = [(self.client, 1 - self.core)]
        if whole:
            pairs += [(self.along_x(), self.core), (self.along_y(), self.core)]
            pairs += [(self.along_z(step), self.core) for step in range(3)]
        if across:
            pairs += [(self.along_x(), 1 - self.core)]
        for pair in pairs:
            pl.semaphore_signal(barrier, inc=1, device_id=pair, device_id_type=MESH)
        pl.semaphore_wait(barrier, len(pairs))


def cut_rows(counts):
    pieces = []
    for slot, rows in enumerate(counts):
        middle = (rows // 16 + 1) // 2 * 16
        pieces.append((slot, 0, middle, 0))
        pieces.append((slot, middle, rows - middle, 1))
    return pieces


def block_ref(ref, size, z, y, x, core, start, count):
    if len(ref.shape) == 2:
        first = (((z * 2 + y) * 2 + x) * 2 + core) * size + start
        return ref.at[pl.ds(pl.multiple_of(first, 16), count), :]
    return ref.at[z, y, x, core, pl.ds(start, count), :]


class Spread:
    def __init__(self, place, weights, counts, sems):
        self.place = place
        self.weights = weights
        self.counts = counts
        self.pieces = cut_rows(counts)
        self.z_sems, self.near_sems, self.far_sems, self.core_sems = sems
        self.order = [place.z] + place.others

    def z_copy(self, step, slot):
        p = self.place
        ref = block_ref(self.weights[slot], self.counts[slot], p.z, p.y, p.x, p.core, 0, self.counts[slot])
        sems = self.z_sems
        return remote(ref, ref, sems.at[0, step, slot], sems.at[1, step, slot], p.along_z(step), p.core)

    def near_copy(self, turn, number):
        p = self.place
        slot, start, count, way = self.pieces[number]
        ref = block_ref(self.weights[slot], self.counts[slot], self.order[turn], p.y, p.x, p.core, start, count)
        sems = self.near_sems
        return remote(
            ref, ref, sems.at[0, turn, number], sems.at[1, turn, number], (p.along_x, p.along_y)[way](), p.core
        )

    def far_copies(self, turn, number):
        p = self.place
        slot, start, count, way = self.pieces[number]
        spot = self.order[turn]
        sems = self.far_sems
        copies = []
        for part, other in enumerate((0, 1) if slot == 1 else (slice(None),)):
            y, x = (p.y, other) if way == 0 else (other, p.x)
            ref = block_ref(self.weights[slot], self.counts[slot], spot, y, x, p.core, start, count)
            sem = number + 4 * part
            to = (p.along_y, p.along_x)[way]()
            copies.append(remote(ref, ref, sems.at[0, turn, sem], sems.at[1, turn, sem], to, p.core))
        return copies

    def core_copies(self, turn, slot):
        p = self.place
        sems = self.core_sems
        copies = []
        pairs = [(y, x) for y in (0, 1) for x in (0, 1)] if slot == 1 else [(slice(None), slice(None))]
        for part, (y, x) in enumerate(pairs):
            ref = block_ref(self.weights[slot], self.counts[slot], self.order[turn], y, x, p.core, 0, self.counts[slot])
            sem = (0, 2 + part, 1)[slot]
            copies.append(remote(ref, ref, sems.at[0, turn, sem], sems.at[1, turn, sem], p.client, 1 - p.core))
        return copies

    def begin(self, master):
        p = self.place
        start = 0
        for slot in range(3):
            rows = self.counts[slot]
            own = block_ref(self.weights[slot], self.counts[slot], p.z, p.y, p.x, p.core, 0, rows)
            own[...] = master[start : start + rows, :].astype(low_type)
            start += rows
        for step in range(3):
            self.z_copy(step, 0).start()
        self.near_start(0)

    def near_start(self, slot):
        for number in (2 * slot, 2 * slot + 1):
            self.near_copy(0, number).start()

    def steps(self):
        near, far, core, start = self.near_step, self.far_step, self.core_step, self.near_start
        groups = [
            [(far, 0, 0), (start, 1)],
            [(near, 1, 0)],
            [(near, 2, 0), (near, 3, 0)],
            [(far, 1, 0), (core, 0, 0), (far, 0, 1)],
            [(far, 2, 0), (far, 3, 0), (core, 1, 0)],
            [(core, 2, 0), (core, 3, 0), (near, 1, 1), (start, 2)],
            [(core, 0, 1), (near, 2, 1)],
            [(far, 1, 1), (near, 3, 1)],
            [(core, 1, 1), (far, 2, 1), (far, 0, 2)],
            [(far, 3, 1), (core, 2, 1), (near, 1, 2)],
            [(core, 3, 1), (core, 0, 2), (near, 2, 2)],
            [(far, 1, 2), (near, 3, 2)],
            [(core, 1, 2), (far, 2, 2)],
            [(far, 3, 2), (core, 2, 2)],
            [(core, 3, 2)],
        ]
        return [[functools.partial(*step) for step in group] for group in groups]

    def near_step(self, turn, slot):
        self.z_copy(turn - 1, slot).wait_recv()
        for number in (2 * slot, 2 * slot + 1):
            self.near_copy(turn, number).start()
        if slot < 2:
            self.z_copy(turn - 1, slot + 1).start()

    def far_step(self, turn, slot):
        for number in (2 * slot, 2 * slot + 1):
            self.near_copy(turn, number).wait_recv()
            for copy in self.far_copies(turn, number):
                copy.start()

    def core_step(self, turn, slot):
        for number in (2 * slot, 2 * slot + 1):
            for copy in self.far_copies(turn, number):
                copy.wait_recv()
        for copy in self.core_copies(turn, slot):
            copy.start()

    def arrive(self, slot):
        for turn in range(4):
            for copy in self.core_copies(turn, slot):
                copy.wait_recv()

    def drain(self):
        for slot in range(3):
            for step in range(3):
                self.z_copy(step, slot).wait_send()
            for turn in range(4):
                for copy in self.core_copies(turn, slot):
                    copy.wait_send()
        for number in range(6):
            for turn in range(4):
                self.near_copy(turn, number).wait_send()
                for copy in self.far_copies(turn, number):
                    copy.wait_send()


class Fold:
    def __init__(self, place, grads, counts, parts):
        self.place = place
        self.grads = grads
        self.counts = counts
        self.pieces = cut_rows(counts)
        self.core_boxes = [parts[1], parts[0], parts[1]]
        self.near_boxes, self.far_boxes, self.z_boxes = [parts[3 * k + 2 : 3 * k + 5] for k in range(3)]
        self.core_sems, self.near_sems, self.far_sems, self.z_sems = parts[11:]

    def core_copies(self, which, slot):
        p = self.place
        sems = self.core_sems
        copies = []
        pairs = [(y, x) for y in (0, 1) for x in (0, 1)] if slot == 1 else [(slice(None), slice(None))]
        for part, (y, x) in enumerate(pairs):
            ref = block_ref(self.grads[slot], self.counts[slot], which, y, x, 1 - p.core, 0, self.counts[slot])
            box = self.core_boxes[slot].at[which, y, x]
            sem = (0, 2 + part, 1)[slot]
            copies.append(remote(ref, box, sems.at[0, which, sem], sems.at[1, which, sem], p.client, 1 - p.core))
        return copies

    def near_copies(self, which, number):
        p = self.place
        slot, start, count, way = self.pieces[number]
        sems = self.near_sems
        copies = []
        for part, other in enumerate((0, 1) if slot == 1 else (slice(None),)):
            y, x = (other, 1 - p.x) if way == 0 else (1 - p.y, other)
            ref = block_ref(self.grads[slot], self.counts[slot], which, y, x, p.core, start, count)
            box = self.near_boxes[slot].at[which, other, pl.ds(start, count), :]
            sem = number + 4 * part
            to = (p.along_x, p.along_y)[way]()
            copies.append(remote(ref, box, sems.at[0, which, sem], sems.at[1, which, sem], to, p.core))
        return copies

    def far_copy(self, which, number):
        p = self.place
        slot, start, count, way = self.pieces[number]
        y, x = (1 - p.y, p.x) if way == 0 else (p.y, 1 - p.x)
        ref = block_ref(self.grads[slot], self.counts[slot], which, y, x, p.core, start, count)
        box = self.far_boxes[slot].at[which, pl.ds(start, count), :]
        sems = self.far_sems
        return remote(
            ref, box, sems.at[0, which, number], sems.at[1, which, number], (p.along_y, p.along_x)[way](), p.core
        )

    def z_copy(self, which, sender, number):
        p = self.place
        slot, start, count, _ = self.pieces[number]
        rows = pl.ds(start, count)
        sems = self.z_sems
        return remote(
            block_ref(self.grads[slot], self.counts[slot], which, p.y, p.x, p.core, start, count),
            self.z_boxes[slot].at[sender, rows, :],
            sems.at[0, which, number],
            sems.at[1, sender, number],
            p.at(which, p.y, p.x),
            p.core,
        )

    def begin(self, which, slot):
        for copy in self.core_copies(which, slot):
            copy.start()

    def add(self, slot, spots, start, count, box):
        ref = block_ref(self.grads[slot], self.counts[slot], *spots, self.place.core, start, count)
        ref[...] = (ref[...].astype(wide) + box.astype(wide)).astype(low_type)

    def turn(self, slot, turn):
        for lag, step in ((2, self.far_step), (1, self.near_step), (0, self.core_step)):
            when((turn >= lag) & (turn < lag + 4), functools.partial(step, turn - lag, slot))

    def core_step(self, which, slot):
        for copy in self.core_copies(which, slot):
            copy.wait_recv()
        pairs = [(y, x) for y in (0, 1) for x in (0, 1)] if slot == 1 else [(slice(None), slice(None))]
        for y, x in pairs:
            self.add(slot, (which, y, x), 0, self.counts[slot], self.core_boxes[slot][which, y, x])
        for number in (2 * slot, 2 * slot + 1):
            for copy in self.near_copies(which, number):
                copy.start()

    def near_step(self, which, slot):
        p = self.place
        for number in (2 * slot, 2 * slot + 1):
            _, start, count, way = self.pieces[number]
            for copy in self.near_copies(which, number):
                copy.wait_recv()
            for other in (0, 1) if slot == 1 else (slice(None),):
                y, x = (other, p.x) if way == 0 else (p.y, other)
                box = self.near_boxes[slot][which, other, pl.ds(start, count), :]
                self.add(slot, (which, y, x), start, count, box)
            self.far_copy(which, number).start()

    def far_step(self, which, slot):
        p = self.place
        for number in (2 * slot, 2 * slot + 1):
            _, start, count, way = self.pieces[number]
            self.far_copy(which, number).wait_recv()
            box = self.far_boxes[slot][which, pl.ds(start, count), :]
            self.add(slot, (which, p.y, p.x), start, count, box)

            @pl.when(p.z != which)
            def _():
                self.z_copy(which, p.z, number).start()

    def result(self, slot):
        p = self.place
        self.z_boxes[slot][p.z] = block_ref(self.grads[slot], self.counts[slot], p.z, p.y, p.x, p.core, 0, self.counts[slot])[...]
        for sender in range(4):

            @pl.when(p.z != sender)
            def _():
                for number in (2 * slot, 2 * slot + 1):
                    self.z_copy(sender, sender, number).wait_recv()

        total = self.z_boxes[slot][0].astype(wide)
        for sender in range(1, 4):
            total += self.z_boxes[slot][sender].astype(wide)
        return total

    def drain(self):
        for which in range(4):
            for slot in range(3):
                for copy in self.core_copies(which, slot):
                    copy.wait_send()
            for number in range(6):
                for copy in self.near_copies(which, number):
                    copy.wait_send()
                self.far_copy(which, number).wait_send()

            @pl.when(self.place.z != which)
            def _():
                for number in range(6):
                    self.z_copy(which, self.place.z, number).wait_send()


def norm_stats(mine, theirs, count):
    gap = mine[0:1] - theirs[0:1]
    mean = 0.5 * (mine[0:1] + theirs[0:1])
    spread = mine[1:2] + theirs[1:2] + gap * gap * (0.5 * count)
    return mean, lax.rsqrt(spread / (2.0 * count) + norm_epsilon)


def client_kernel(
    gather,
    images,
    classes,
    features,
    labels,
    flag,
    params,
    head,
    *rest,
):
    if gather:
        master, *rest = rest
    else:
        first_in, middle_in, last_in, *rest = rest
    if gather:
        grads_out, *rest = rest
    else:
        grads_out, rest = rest[:3], rest[3:]
    (
        grad_norm_out,
        grad_head_out,
        loss_out,
        x_all,
        mid_wide,
        w_first,
        w_middle,
        w_last,
        act_one,
        act_two,
        act_three,
        taps_one,
        taps_two,
        hidden_two,
        stage,
        params_all,
        head_all,
        grad_pool,
        pool_send,
        pool_all,
        logit_grads,
        sums_mine,
        sums_theirs,
        shift,
        fwd_stats,
        sem_local,
        sem_swap,
        sem_misc,
        *near_parts,
    ) = rest
    place = Place()
    core = place.core
    mate = (place.client, 1 - core)
    count_rows, channels = x_all.shape
    half = channels // 2
    width = act_one.shape[1]
    part = width // 2
    mine_images = images // 2
    line = SIDE * mine_images
    total_rows = 2.0 * count_rows

    def tile(index):
        return pl.ds(pl.multiple_of(index * line, line), line)

    def lanes(index, size):
        return pl.ds(pl.multiple_of(index * size, size), size)

    place.greet(gather)

    quarter = half // 2
    own_rows = pl.ds(pl.multiple_of(core * count_rows, count_rows), count_rows)
    mate_rows = pl.ds(pl.multiple_of((1 - core) * count_rows, count_rows), count_rows)
    top_rows = pl.ds(0, count_rows)
    own_copies = [
        pltpu.make_async_copy(
            features.at[own_rows, pl.ds(side * quarter, quarter)], buffer, sem_local.at[side]
        )
        for side, buffer in enumerate((hidden_two, mid_wide.at[top_rows, :]))
    ]
    per_kind = params.shape[0] // 2
    for kind in range(2):
        rows = [params[kind * per_kind + spot : kind * per_kind + spot + 1, :] for spot in range(per_kind)]
        params_all[core, kind : kind + 1, :] = jnp.concatenate(rows, axis=1)
    head_all[core] = jnp.zeros(head_all.shape[1:], low_type)
    for spot in range(half // LANES):
        head_all[core, 0:classes, spot * LANES : (spot + 1) * LANES] = head[
            pl.ds(spot, classes, stride=half // LANES), :
        ].astype(low_type)
    to_mate = [
        remote(params_all.at[core], params_all.at[core], sem_misc.at[0, 0], sem_misc.at[1, 0], *mate),
        remote(head_all.at[core], head_all.at[core], sem_misc.at[0, 1], sem_misc.at[1, 1], *mate),
    ]
    for side, buffer in enumerate((taps_one, taps_two)):
        to_mate.append(
            remote(
                features.at[mate_rows, pl.ds(side * quarter, quarter)],
                buffer.at[top_rows, :],
                sem_misc.at[0, 5 + side],
                sem_misc.at[1, 5 + side],
                *mate,
            )
        )
    for copy in to_mate + own_copies:
        copy.start()

    weights = (w_first, w_middle, w_last)
    if gather:
        counts = [channels // 32, 9 * width // 32, channels // 32]
        spread = Spread(place, weights, counts, near_parts[:4])
        held = act_three.at[pl.ds(0, master.shape[0]), pl.ds(0, width)]
        load = pltpu.make_async_copy(master, held, sem_local.at[8])
        load.start()
        load.wait()
        spread.begin(held)
        fold = Fold(place, (w_first, mid_wide, w_last), counts, near_parts[4:])
        due = spread.steps()
    else:
        loads = [
            pltpu.make_async_copy(src, dst, sem_local.at[8 + slot])
            for slot, (src, dst) in enumerate(zip((first_in, middle_in, last_in), weights))
        ]
        for load in loads:
            load.start()
        due = []

    def advance(count):
        for group in due[:count]:
            for step in group:
                step()
        del due[:count]

    def advance_at(index, spots):
        for spot, group in zip(spots, due):

            @pl.when(index == spot)
            def _():
                for step in group:
                    step()

    def arrive(slot, left):
        if gather:
            advance(len(due) - left)
            spread.arrive(slot)
        else:
            loads[slot].wait()

    def fold_turn(slot, turn):
        if gather:
            fold.turn(slot, turn)

    def fold_step(kind, slot, which):
        if gather:
            (fold.core_step, fold.near_step, fold.far_step)[kind](which, slot)

    def fold_at(index, spot, *steps):
        @pl.when(index == spot)
        def _():
            for step in steps:
                fold_step(*step)

    def fold_begin(which, slot):
        if gather:
            fold.begin(which, slot)

    def zero_edges(buffer):
        edge = jnp.zeros((line,) + buffer.shape[1:], low_type)
        buffer[0:line, :] = edge
        buffer[line + count_rows : 2 * line + count_rows, :] = edge

    advance(3)
    for copy in own_copies:
        copy.wait()

    def turn_from(source, base):
        def turn(index, carry):
            stage[...] = source(lanes(index, LANES)).astype(wide)

            def pixel(spot, inner):
                x_all[
                    pl.ds(pl.multiple_of(spot * mine_images, mine_images), mine_images),
                    pl.ds(pl.multiple_of(base + index * LANES, LANES), LANES),
                ] = stage[pl.ds(spot, mine_images, stride=PIXELS), :].astype(low_type)
                return inner

            return lax.fori_loop(0, PIXELS, pixel, carry, unroll=7)

        return turn

    quarters = quarter // LANES
    own_base, mate_base = core * half, (1 - core) * half
    lax.fori_loop(0, quarters, turn_from(lambda columns: hidden_two[:, columns], own_base), 0)
    advance(1)
    lax.fori_loop(
        0,
        quarters,
        turn_from(lambda columns: mid_wide[0:count_rows, columns], own_base + quarter),
        0,
    )
    advance(1)
    for copy in to_mate:
        copy.wait_recv()
    lax.fori_loop(0, quarters, turn_from(lambda columns: taps_one[0:count_rows, columns], mate_base), 0)
    advance(1)
    lax.fori_loop(0, quarters, turn_from(lambda columns: taps_two[0:count_rows, columns], mate_base + quarter), 0)
    zero_edges(taps_one)
    zero_edges(taps_two)
    arrive(0, 9)

    def swap(slot, size):
        return remote(
            sums_mine.at[slot, :, pl.ds(0, size)],
            sums_theirs.at[slot, :, pl.ds(0, size)],
            sem_swap.at[0, slot],
            sem_swap.at[1, slot],
            *mate,
        )

    def gain_bias(lower, upper):
        rows = []
        for kind in range(2):
            pieces = [params_all[side, kind : kind + 1, lower:upper] for side in range(2)]
            rows.append(jnp.concatenate(pieces, axis=1))
        return rows

    def collect(index, value, columns, size):
        @pl.when(index == 0)
        def _():
            shift[0:1, pl.ds(0, size)] = column_sum(fold_rows(value)) / value.shape[0]
            shift[8:24, pl.ds(0, size)] = jnp.zeros((16, size), wide)

        gap = value - shift[0:1, pl.ds(0, size)]
        shift[8:16, pl.ds(0, size)] += fold_rows(gap)
        shift[16:24, pl.ds(0, size)] += fold_rows(gap * gap)

    def close_stats(slot, columns, size):
        sum_gap = column_sum(shift[8:16, pl.ds(0, size)])
        sum_square = column_sum(shift[16:24, pl.ds(0, size)])
        sums_mine[slot, 0:1, columns] = shift[0:1, pl.ds(0, size)] + sum_gap / count_rows
        sums_mine[slot, 1:2, columns] = sum_square - sum_gap * sum_gap / count_rows

    def look_over(act, columns):
        def look(index, carry):
            collect(index, act[tile(index), columns], None, width)
            return carry

        lax.fori_loop(0, SIDE, look, 0)

    groups = SPOTS[0]
    group = channels // groups

    def settle(slot, size):
        mean, scale = norm_stats(
            sums_mine[slot, 0:2, pl.ds(0, size)], sums_theirs[slot, 0:2, pl.ds(0, size)], float(count_rows)
        )
        fwd_stats[slot, 0:1, pl.ds(0, size)] = mean
        fwd_stats[slot, 1:2, pl.ds(0, size)] = scale

    whole_width = pl.ds(0, width)

    def first_part(index, carry):
        act_one[...] += dot_nn(x_all[:, lanes(index, group)], flat_rows(w_first[index]))
        advance_at(index, (0, 1, 2))
        return carry

    act_one[...] = jnp.zeros_like(act_one)
    lax.fori_loop(0, groups, first_part, 0)
    del due[:3]
    look_over(act_one, whole_width)
    close_stats(0, whole_width, width)
    move = swap(0, width)
    move.start()
    advance(1)
    move.wait()
    settle(0, width)

    gain_one, bias_one = gain_bias(0, part)
    gain_two, bias_two = gain_bias(part, width)
    gain_three, bias_three = gain_bias(width, width + half)

    def normal(act, slot, index):
        mean = fwd_stats[slot, 0:1, pl.ds(0, width)]
        return (act[tile(index), :] - mean) * fwd_stats[slot, 1:2, pl.ds(0, width)]

    def hide_one(index, carry):
        value = normal(act_one, 0, index) * gain_one + bias_one
        taps_one[pl.ds(pl.multiple_of((index + 1) * line, line), line), :] = (value * sigmoid(value)).astype(low_type)
        return carry

    lax.fori_loop(0, SIDE, hide_one, 0)
    arrive(1, 4)

    step = mine_images
    piece = width // 2

    def row_windows(buffer, down, start, reach):
        if reach == line:
            return buffer[pl.ds(pl.multiple_of(down * line, line), count_rows), :]
        windows = [
            buffer[pl.ds(pl.multiple_of((down + row) * line + start, step), reach), :] for row in range(SIDE)
        ]
        return jnp.concatenate(windows, axis=0)

    def add_windows(target, columns, value, start, reach):
        for row in range(SIDE):
            rows = slice(row * line + start, row * line + start + reach)
            target[rows, columns] += value[row * reach : (row + 1) * reach]

    low_start, high_start, reaches = (0, 0, step), (step, 0, 0), (line - step, line, line - step)

    def second_part(index, carry):
        down, columns = index // 2, lanes(index % 2, piece)
        for over in range(3):
            left = row_windows(taps_one, down, low_start[over], reaches[over])
            kernel = w_middle[pl.ds(pl.multiple_of((3 * down + over) * width, width), width), columns]
            add_windows(act_two, columns, dot_nn(left, kernel), high_start[over], reaches[over])
        advance_at(index, (1, 3, 5))
        return carry

    act_two[...] = jnp.zeros_like(act_two)
    lax.fori_loop(0, 6, second_part, 0)
    del due[:3]
    look_over(act_two, whole_width)
    close_stats(1, whole_width, width)
    move_two = swap(1, width)
    move_two.start()
    move_two.wait()
    settle(1, width)

    arrive(2, 0)

    def third_line(index, carry):
        value = normal(act_two, 1, index) * gain_two + bias_two
        hidden = (value * sigmoid(value)).astype(low_type)
        hidden_two[tile(index), :] = hidden
        value = dot_nt(hidden, flat_rows(w_last[...]))
        act_three[tile(index), :] = value
        start = jnp.where(index == 0, column_sum(value[0:8]) / 8.0, shift[0:1, :])
        gap = value - start
        kept_sums = jnp.where(index == 0, 0.0, shift[8:24, :])
        shift[0:1, :] = start
        shift[8:16, :] = kept_sums[0:8] + fold_rows(gap)
        shift[16:24, :] = kept_sums[8:16] + fold_rows(gap * gap)
        return carry

    lax.fori_loop(0, SIDE, third_line, 0)
    close_stats(2, pl.ds(0, channels), channels)
    move_three = swap(2, channels)
    move_three.start()
    move_three.wait()
    settle(2, channels)

    per_group = group // LANES

    def block_of(spot):
        return pl.ds(pl.multiple_of(spot * mine_images, mine_images), mine_images)

    def mid_line(which, index):
        return pl.ds(pl.multiple_of(which * count_rows + index * line, line), line)

    kept = channels // LANES * mine_images

    def gathered(kind):
        starts = range(kind * kept, (kind + 1) * kept, mine_images)
        return jnp.concatenate([stage[start : start + mine_images, :] for start in starts], axis=1)

    fwd_stats[2, 4:5, :] = fwd_stats[2, 1:2, :] * gain_three
    fwd_stats[2, 5:6, :] = bias_three - fwd_stats[2, 0:1, :] * fwd_stats[2, 4:5, :]

    def emit(index, carry):
        columns = lanes(index, LANES)
        slant, level = fwd_stats[2, 4:5, columns], fwd_stats[2, 5:6, columns]

        def pixels(row, sums):
            pooled, steeps, steeps_act = sums
            found = []
            for spot in range(SIDE):
                where = block_of(row * SIDE + spot)
                act = act_three[where, columns]
                half_total = 0.5 * (act * slant + level + x_all[where, columns].astype(wide))
                rise = 1.0 + jnp.tanh(half_total)
                out = half_total * rise
                steep = rise + out * (2.0 - rise)
                found.append(steep.astype(low_type))
                pooled, steeps, steeps_act = pooled + out, steeps + steep, steeps_act + steep * act
            mid_wide[mid_line(index // per_group, row), lanes(index % per_group, LANES)] = jnp.concatenate(
                found, axis=0
            )
            return pooled, steeps, steeps_act

        zero = jnp.zeros((mine_images, LANES), wide)
        sums = lax.fori_loop(0, SIDE, pixels, (zero, zero, zero))
        for kind, value in enumerate(sums):
            stage[pl.ds(pl.multiple_of(kind * kept + index * mine_images, mine_images), mine_images), :] = value
        return carry

    lax.fori_loop(0, channels // LANES, emit, 0)

    pooled = (gathered(0) / PIXELS).astype(low_type)
    head_full = jnp.concatenate([head_all[0], head_all[1]], axis=1)
    logits = dot_nt(head_full, pooled)
    spots = lax.broadcasted_iota(jnp.int32, logits.shape, 0)
    inside = spots < classes
    first_labels, second_labels = labels[0:1, 0:mine_images], labels[0:1, mine_images:]
    onehot = (spots == jnp.where(core == 0, first_labels, second_labels)).astype(wide)
    top = jnp.max(jnp.where(inside, logits, -jnp.inf), axis=0, keepdims=True)
    powers = jnp.where(inside, jnp.exp(logits - top), 0.0)
    power_sum = jnp.sum(powers, axis=0, keepdims=True)
    picked = jnp.sum(logits * onehot, axis=0, keepdims=True)
    each_loss = top + jnp.log(power_sum) - picked
    taking = flag[0].astype(wide)
    tile_spots = lax.broadcasted_iota(jnp.int32, loss_out.shape, 1)
    loss_out[...] = jnp.where(tile_spots == 0, taking * jnp.sum(each_loss), taking * mine_images)
    grads = (taking / images * (powers / power_sum - onehot)).astype(low_type)
    grad_pool[...] = dot_tn(grads, head_full) * (0.5 / PIXELS)
    logit_grads[core] = grads
    pool_all[core] = pooled[:, 0:half]
    pool_send[...] = pooled[:, half:]

    @pl.when(core == 1)
    def _():
        pool_all[core] = pooled[:, half:]
        pool_send[...] = pooled[:, 0:half]

    head_moves = [
        remote(pool_send, pool_all.at[core], sem_misc.at[0, 3], sem_misc.at[1, 3], *mate),
        remote(logit_grads.at[core], logit_grads.at[core], sem_misc.at[0, 4], sem_misc.at[1, 4], *mate),
    ]

    steeps = gathered(1)
    steeps_normed = (gathered(2) - fwd_stats[2, 0:1, :] * steeps) * fwd_stats[2, 1:2, :]
    sums_mine[3, 0:1, :] = column_sum(grad_pool[...] * steeps)
    sums_mine[3, 1:2, :] = column_sum(grad_pool[...] * steeps_normed)
    move_back = swap(3, channels)
    move_back.start()
    for copy in head_moves:
        copy.start()
    move_back.wait()

    def back_terms(slot, layer, size, gain):
        columns = pl.ds(0, size)
        sums = sums_mine[slot, 0:2, columns] + sums_theirs[slot, 0:2, columns]
        sums_mine[slot, 2:4, columns] = sums
        scale = fwd_stats[layer, 1:2, columns]
        return (
            scale * gain,
            scale * gain * sums[0:1] / total_rows,
            scale * scale * gain * sums[1:2] / total_rows,
        )

    first, second, third = back_terms(3, 2, channels, gain_three)
    fwd_stats[2, 4:5, :] = second - third * fwd_stats[2, 0:1, :]
    fwd_stats[2, 5:6, :] = third
    grad_pool[...] = grad_pool[...] * first

    def pull(index):
        for which in range(groups):
            columns = slice(which * group, (which + 1) * group)
            reach = grad_pool[:, columns]
            steep = mid_wide[mid_line(which, index), :].astype(wide)
            value = jnp.concatenate([reach] * SIDE, axis=0) * steep
            value = value - fwd_stats[2, 4:5, columns] - fwd_stats[2, 5:6, columns] * act_three[tile(index), columns]
            mid_wide[mid_line(which, index), :] = value.astype(low_type)

    pull(0)
    for copy in head_moves:
        copy.wait_recv()
    head_grad = dot_nn(logit_grads[0], pool_all[0]) + dot_nn(logit_grads[1], pool_all[1])
    for spot in range(half // LANES):
        stage[pl.ds(spot, classes, stride=half // LANES), :] = head_grad[
            0:classes, spot * LANES : (spot + 1) * LANES
        ]
    head_space = stage.at[pl.ds(0, grad_head_out.shape[0]), :]
    head_leave = pltpu.make_async_copy(head_space, grad_head_out, sem_local.at[0])
    head_leave.start()

    def drop_into(act, slot, gain, bias, columns):
        size = pl.ds(0, width)
        shift[8:24, size] = jnp.zeros((16, width), wide)

        def drop(index, carry):
            normed = normal(act, slot, index)
            norm = normed * gain + bias
            sig = sigmoid(norm)
            grad = act_three[tile(index), columns] * (sig + norm * sig * (1.0 - sig))
            act_three[tile(index), columns] = grad
            shift[8:16, size] += fold_rows(grad)
            shift[16:24, size] += fold_rows(grad * normed)
            return carry

        lax.fori_loop(0, SIDE, drop, 0)

    def close_back(slot):
        size = pl.ds(0, width)
        sums_mine[slot, 0:1, size] = column_sum(shift[8:16, size])
        sums_mine[slot, 1:2, size] = column_sum(shift[16:24, size])

    space_two, space_one = pl.ds(0, width), pl.ds(width, width)

    def mid_group(which):
        return mid_wide[pl.ds(pl.multiple_of(which * count_rows, count_rows), count_rows), :]

    def back_two(index):
        left = jnp.concatenate([mid_wide[mid_line(which, index), :] for which in range(groups)], axis=1)
        value = dot_nn(left, flat_rows(w_last[...]))
        normed = normal(act_two, 1, index)
        norm = normed * gain_two + bias_two
        sig = sigmoid(norm)
        grad = value * (sig + norm * sig * (1.0 - sig))
        act_three[tile(index), space_two] = grad
        size = pl.ds(0, width)
        shift[8:16, size] += fold_rows(grad)
        shift[16:24, size] += fold_rows(grad * normed)

    def back_two_line(index, carry):
        pull(index + 1)
        back_two(index)
        return carry

    shift[8:24, :] = jnp.zeros((16, channels), wide)
    lax.fori_loop(0, SIDE - 1, back_two_line, 0)
    back_two(SIDE - 1)
    close_back(4)
    move_back_two = swap(4, width)
    move_back_two.start()

    if gather:
        spread.drain()

    def put(ref, which, value):
        ref[which] = value.astype(low_type).reshape(ref.shape[1:])

    def expand_group(which, carry):
        put(w_last, which, dot_tn(mid_group(which), hidden_two[...]))
        fold_begin(which, 2)
        fold_turn(2, which - 1)
        return carry

    lax.fori_loop(0, groups, expand_group, 0)
    move_back_two.wait()
    terms_two = back_terms(4, 1, width, gain_two)

    def back_act(terms, act, layer, index, columns):
        first, second, third = terms
        gap = act[tile(index), :] - fwd_stats[layer, 0:1, pl.ds(0, width)]
        return (first * act_three[tile(index), columns] - second - third * gap).astype(low_type)

    def grad_two(index, carry):
        taps_two[pl.ds(pl.multiple_of((index + 1) * line, line), line), :] = back_act(
            terms_two, act_two, 1, index, space_two
        )
        return carry

    lax.fori_loop(0, SIDE, grad_two, 0)
    fold_turn(2, groups - 1)
    def middle_row(down, carry):
        for over in range(3):
            left = row_windows(taps_one, down, low_start[over], reaches[over])
            right = row_windows(taps_two, 1, high_start[over], reaches[over])
            rows = pl.ds(pl.multiple_of((3 * down + over) * width, width), width)
            mid_wide[rows, :] = dot_tn(left, right).astype(low_type)
        fold_begin(down, 1)

        @pl.when(down == 2)
        def _():
            fold_begin(3, 1)

        fold_turn(2, groups + down)
        fold_at(down, 1, (0, 1, 0))
        fold_at(down, 2, (1, 1, 0), (0, 1, 1))
        return carry

    lax.fori_loop(0, 3, middle_row, 0)

    def back_one(index, carry):
        down, side = index // 2, index % 2
        columns = lanes(2 + side, piece)
        for over in range(3):
            left = row_windows(taps_two, 2 - down, high_start[over], reaches[over])
            start = pl.multiple_of((3 * down + over) * width + side * piece, piece)
            value = dot_nt(left, w_middle[pl.ds(start, piece), :])
            add_windows(act_three, columns, value, low_start[over], reaches[over])
        fold_at(index, 0, (0, 1, 2))
        fold_at(index, 1, (0, 1, 3))
        fold_at(index, 2, (1, 1, 1))
        fold_at(index, 3, (2, 1, 0))
        fold_at(index, 4, (1, 1, 2))
        fold_at(index, 5, (2, 1, 1))
        return carry

    act_three[:, space_one] = jnp.zeros((count_rows, width), wide)
    lax.fori_loop(0, 6, back_one, 0)
    drop_into(act_one, 0, gain_one, bias_one, space_one)
    fold_step(1, 1, 3)
    close_back(5)
    move_back_one = swap(5, width)
    move_back_one.start()

    move_back_one.wait()
    terms_one = back_terms(5, 0, width, gain_one)

    def grad_one(index, carry):
        hidden_two[tile(index), :] = back_act(terms_one, act_one, 0, index, space_one)
        return carry

    lax.fori_loop(0, SIDE, grad_one, 0)
    fold_step(2, 1, 2)

    def reduce_group(which, carry):
        put(w_first, which, dot_tn(x_all[:, lanes(which, group)], hidden_two[...]))
        fold_begin(which, 0)
        fold_turn(0, which - 1)
        fold_at(which, 1, (2, 1, 3))
        return carry

    lax.fori_loop(0, groups, reduce_group, 0)

    for kind in range(2):
        row = 3 - kind
        pieces = [
            sums_mine[5, row : row + 1, lanes(core, part)],
            sums_mine[4, row : row + 1, lanes(core, part)],
            sums_mine[3, row : row + 1, lanes(core, half)],
        ]
        whole = jnp.concatenate(pieces, axis=1)
        per_kind = whole.shape[1] // LANES
        for spot in range(per_kind):
            grad_norm_out[kind * per_kind + spot : kind * per_kind + spot + 1, :] = whole[
                :, spot * LANES : (spot + 1) * LANES
            ]
    for turn in range(groups - 1, groups + 2):
        fold_turn(0, turn)
    if gather:
        start = 0
        for slot in range(3):
            rows = fold.counts[slot]
            act_three[kept + start : kept + start + rows, half : half + width] = fold.result(slot)
            start += rows
        leave = pltpu.make_async_copy(
            act_three.at[pl.ds(kept, start), pl.ds(half, width)], grads_out, sem_local.at[3]
        )
        leave.start()
        leave.wait()
        fold.drain()
    else:
        outs = [
            pltpu.make_async_copy(ref, out, sem_local.at[slot])
            for slot, (ref, out) in enumerate(zip((w_first, mid_wide.at[pl.ds(0, 9 * width), :], w_last), grads_out))
        ]
        for copy in outs:
            copy.start()
        for copy in outs:
            copy.wait()
    head_leave.wait()
    for copy in to_mate + head_moves:
        copy.wait_send()


def client_pass(gather, classes, features, labels, flag, params, head, weights):
    pixels, half = features.shape
    images = labels.shape[1]
    count_rows, channels = pixels // 2, 2 * half
    width = params.shape[0] // 2 * LANES - half
    head_rows = classes + -classes % 16
    mine_images = images // 2
    line = SIDE * mine_images
    middle = 9 * width
    blocks = 32
    group = channels // SPOTS[0]
    vmem = pl.BlockSpec(memory_space=pltpu.VMEM)
    smem = pl.BlockSpec(memory_space=pltpu.SMEM)
    spots = SPOTS + (2,)
    scratch = [
        pltpu.VMEM((count_rows, channels), low_type),
        pltpu.VMEM((SPOTS[0] * count_rows, group), low_type),
        pltpu.VMEM(spots + (channels // blocks, width), low_type),
        pltpu.VMEM((middle, width), low_type),
        pltpu.VMEM(spots + (channels // blocks, width), low_type),
        pltpu.VMEM((count_rows, width), wide),
        pltpu.VMEM((count_rows, width), wide),
        pltpu.VMEM((count_rows, channels), wide),
        pltpu.VMEM((count_rows + 2 * line, width), low_type),
        pltpu.VMEM((count_rows + 2 * line, width), low_type),
        pltpu.VMEM((count_rows, width), low_type),
        pltpu.VMEM((count_rows, LANES), wide),
        pltpu.VMEM((2, 2, half + width), wide),
        pltpu.VMEM((2, head_rows, half), low_type),
        pltpu.VMEM((mine_images, channels), wide),
        pltpu.VMEM((mine_images, half), low_type),
        pltpu.VMEM((2, mine_images, half), low_type),
        pltpu.VMEM((2, head_rows, mine_images), low_type),
        pltpu.VMEM((6, 8, channels), wide),
        pltpu.VMEM((6, 8, channels), wide),
        pltpu.VMEM((24, channels), wide),
        pltpu.VMEM((3, 8, channels), wide),
        pltpu.SemaphoreType.DMA((11,)),
        pltpu.SemaphoreType.DMA((2, 6)),
        pltpu.SemaphoreType.DMA((2, 7)),
    ]
    any_space = pl.BlockSpec(memory_space=pl.ANY)
    if gather:
        counts = (channels // blocks, middle // blocks, channels // blocks)
        scratch += [pltpu.SemaphoreType.DMA((2, 3, 3))]
        scratch += [pltpu.SemaphoreType.DMA((2, 4, size)) for size in (6, 8, 6)]
        scratch += [pltpu.VMEM((4, 2, 2, rows, width), low_type) for rows in counts[1:]]
        for lead in ((4, 2), (4,), (4,)):
            scratch += [pltpu.VMEM(lead + (rows, width), low_type) for rows in counts]
        scratch += [pltpu.SemaphoreType.DMA((2, 4, size)) for size in (6, 8, 6, 6)]
        grads_shape = [jax.ShapeDtypeStruct((sum(counts), width), wide)]
        grads_specs = [any_space]
    else:
        grads_shape = [jax.ShapeDtypeStruct(weight.shape, low_type) for weight in weights]
        grads_specs = [any_space] * 3
    return pl.pallas_call(
        functools.partial(client_kernel, gather, images, classes),
        out_shape=grads_shape
        + [
            jax.ShapeDtypeStruct(params.shape, wide),
            jax.ShapeDtypeStruct((classes * half // LANES, LANES), wide),
            jax.ShapeDtypeStruct((8, LANES), wide),
        ],
        in_specs=[any_space, vmem, smem, vmem, vmem] + [any_space] * len(weights),
        out_specs=grads_specs + [vmem, any_space, vmem],
        scratch_shapes=scratch,
        compiler_params=pltpu.CompilerParams(
            collective_id=0, has_side_effects=True, vmem_limit_bytes=VMEM_BYTES
        ),
    )(features, labels, flag, params, head, *weights)


def adam_update(param, grad, first, second, rate, decay):
    first = adam_first * first + (1.0 - adam_first) * grad
    second = adam_second * second + (1.0 - adam_second) * grad * grad
    first_hat = first / (1.0 - adam_first**STEP)
    second_hat = second / (1.0 - adam_second**STEP)
    return (
        param - rate * (first_hat / (jnp.sqrt(second_hat) + adam_epsilon) + decay * param),
        first,
        second,
    )
class GramSum:
    def __init__(self, place, data, total, boxes, sems):
        self.place = place
        self.data = data
        self.total = total
        self.core_box, self.near_box, self.far_box, self.z_box = boxes
        self.sems = sems
        self.copies = []
        self.sizes = (data.shape[0] // 72 * 40 // 32, data.shape[0] // 72 * 32 // 32)

    def rows(self, kind, core, z=None, first=None, second=None):
        size = self.sizes[kind]
        start = core * (16 * (self.sizes[0] + self.sizes[1])) + kind * 16 * self.sizes[0]
        count = 16 * size
        for number, spot, parts in ((4 * size, z, 4), (2 * size, first, 2), (size, second, 2)):
            if spot is None:
                break
            start, count = start + spot * number, number
        return pl.ds(pl.multiple_of(start, 8), count)

    def ways(self, kind):
        p = self.place
        x_way, y_way = (p.x, p.along_x()), (p.y, p.along_y())
        return (x_way, y_way) if kind == 0 else (y_way, x_way)

    def copy(self, phase, kind, turn, src, dst, client, core):
        sems = self.sems
        return remote(
            src, dst, sems.at[0, phase, kind, turn], sems.at[1, phase, kind, turn], client, core
        )

    def launch(self, copy):
        copy.start()
        self.copies.append(copy)

    def down(self, phase, kind, turn):
        p = self.place
        z = (p.others[::-1] + [p.z])[turn]
        (first, first_to), (second, second_to) = self.ways(kind)
        base = self.sizes[0] * kind
        if phase == 0:
            src = self.data.at[self.rows(kind, 1 - p.core, z), :]
            box = self.core_box.at[turn, pl.ds(4 * base, 4 * self.sizes[kind]), :]
            return self.copy(0, kind, turn, src, box, p.client, 1 - p.core)
        if phase == 1:
            src = self.data.at[self.rows(kind, p.core, z, 1 - first), :]
            box = self.near_box.at[turn, pl.ds(2 * base, 2 * self.sizes[kind]), :]
            return self.copy(1, kind, turn, src, box, first_to, p.core)
        if phase == 2:
            src = self.data.at[self.rows(kind, p.core, z, first, 1 - second), :]
            box = self.far_box.at[turn, pl.ds(base, self.sizes[kind]), :]
            return self.copy(2, kind, turn, src, box, second_to, p.core)
        src = self.data.at[self.rows(kind, p.core, z, first, second), :]
        box = self.z_box.at[turn, pl.ds(base, self.sizes[kind]), :]
        return self.copy(3, kind, turn, src, box, p.along_z(2 - turn), p.core)

    def down_step(self, phase, kind, turn):
        p = self.place
        z = (p.others[::-1] + [p.z])[turn]
        (first, _), (second, _) = self.ways(kind)
        self.down(phase, kind, turn).wait_recv()
        spots = (z, first, second)[: phase + 1]
        where = self.rows(kind, p.core, *spots)
        scale = (4, 2, 1)[phase]
        box = (self.core_box, self.near_box, self.far_box)[phase]
        self.data[where, :] += box[turn, pl.ds(scale * self.sizes[0] * kind, scale * self.sizes[kind]), :]
        if phase < 2 or turn < 3:
            self.launch(self.down(phase + 1, kind, turn))

    def up(self, phase, kind, turn):
        p = self.place
        z = ([p.z] + p.others)[turn]
        (first, first_to), (second, second_to) = self.ways(kind)
        if phase == 0:
            ref, to = self.total.at[self.rows(kind, p.core, p.z, first, second), :], p.along_z(turn)
        elif phase == 1:
            ref, to = self.total.at[self.rows(kind, p.core, z, first, second), :], second_to
        elif phase == 2:
            ref, to = self.total.at[self.rows(kind, p.core, z, first), :], first_to
        else:
            ref, to = self.total.at[self.rows(kind, p.core, z), :], p.client
        return self.copy(4 + phase, kind, turn, ref, ref, to, 1 - p.core if phase == 3 else p.core)

    def run(self, extra):
        extra = list(extra)
        kinds = (0, 1)
        for turn in range(4):
            for kind in kinds:
                self.launch(self.down(0, kind, turn))
        for turn in range(6):
            if extra:
                extra.pop(0)()
            for kind in kinds:
                for phase in range(3):
                    if 0 <= turn - phase < 4:
                        self.down_step(phase, kind, turn - phase)
        p = self.place
        for kind in kinds:
            (first, _), (second, _) = self.ways(kind)
            where = self.rows(kind, p.core, p.z, first, second)
            value = self.data[where, :]
            for turn in range(3):
                self.down(3, kind, turn).wait_recv()
                value += self.z_box[turn, pl.ds(self.sizes[0] * kind, self.sizes[kind]), :]
            self.total[where, :] = value
            self.launch(self.up(1, kind, 0))
            for turn in range(3):
                self.launch(self.up(0, kind, turn))
        for turn in range(6):
            for kind in kinds:
                if 1 <= turn < 4:
                    self.up(0, kind, turn - 1).wait_recv()
                    self.launch(self.up(1, kind, turn))
                if 1 <= turn < 5:
                    self.up(1, kind, turn - 1).wait_recv()
                    self.launch(self.up(2, kind, turn - 1))
                if 2 <= turn:
                    self.up(2, kind, turn - 2).wait_recv()
                    self.launch(self.up(3, kind, turn - 2))
        for turn in range(4):
            for kind in kinds:
                self.up(3, kind, turn).wait_recv()

    def drain(self):
        for copy in self.copies:
            copy.wait_send()


class TileSum:
    def __init__(self, place, tiles, boxes, sems):
        self.place = place
        self.tiles = tiles
        self.boxes = boxes
        self.sems = sems

    def copy(self, stage, box):
        p = self.place
        to = (p.client, p.along_x(), p.along_y()) + tuple(p.along_z(step) for step in range(3))
        core = 1 - p.core if box == 0 else p.core
        return remote(
            self.tiles.at[stage], self.boxes.at[box], self.sems.at[0, box], self.sems.at[1, box], to[box], core
        )

    def steps(self):
        def start():
            self.copy(0, 0).start()

        def pair(stage):
            self.copy(stage, stage).wait_recv()
            self.tiles[stage + 1] = self.tiles[stage] + self.boxes[stage]
            if stage < 2:
                self.copy(stage + 1, stage + 1).start()
            else:
                for step in range(3):
                    self.copy(3, 3 + step).start()

        return [start] + [functools.partial(pair, stage) for stage in range(3)]

    def result(self):
        for step in range(3):
            self.copy(3, 3 + step).wait_recv()
        return (self.tiles[3] + self.boxes[3]) + (self.boxes[4] + self.boxes[5])

    def drain(self):
        for stage in range(3):
            self.copy(stage, stage).wait_send()
        for step in range(3):
            self.copy(3, 3 + step).wait_send()


def dot_high(left, right):
    return jnp.dot(left, right, precision=lax.Precision.HIGH, preferred_element_type=wide)


class Share:
    def __init__(self, place, sizes, buffers, sems):
        self.place = place
        self.sizes = sizes
        self.fresh, self.rows_in, self.rows_out, self.back = buffers
        self.sems = sems
        self.bounds = [0, sizes[0], sizes[0] + sizes[1], sum(sizes)]
        p = place
        self.duty = jnp.where(p.x == 1, 1, 2 * p.core)
        self.mine = p.x * 2 + p.core

    def section(self, slot):
        return pl.ds(self.bounds[slot], self.sizes[slot])

    def spot(self, slot, x, core):
        number = x if slot == 1 else x * 2 + core
        return pl.ds(pl.multiple_of(number * self.sizes[slot], 16), self.sizes[slot])

    def doer(self, slot):
        return (0, 0) if slot == 0 else (0, 1) if slot == 2 else (1, self.place.core)

    def out_copy(self, slot):
        p = self.place
        x, core = self.doer(slot)
        return remote(
            self.fresh.at[self.section(slot), :],
            self.rows_in.at[self.spot(slot, p.x, p.core), :],
            self.sems.at[0, slot],
            self.sems.at[1, self.mine],
            p.at(p.z, p.y, x),
            core,
        )

    def in_copy(self, slot, x, core):
        p = self.place
        return remote(
            self.fresh.at[self.section(slot), :],
            self.rows_in.at[self.spot(slot, x, core), :],
            self.sems.at[0, slot],
            self.sems.at[1, x * 2 + core],
            p.at(p.z, p.y, x),
            core,
        )

    def back_copy(self, slot, x, core):
        p = self.place
        return remote(
            self.rows_out.at[self.spot(slot, x, core), :],
            self.back.at[self.section(slot), :],
            self.sems.at[0, 3 + x * 2 + core],
            self.sems.at[1, 4 + slot],
            p.at(p.z, p.y, x),
            core,
        )

    def users(self, slot):
        p = self.place
        if slot == 1:
            return [(0, p.core), (1, p.core)]
        return [(x, core) for x in (0, 1) for core in (0, 1)]

    def send(self):
        for slot in range(3):

            @pl.when(self.duty != slot)
            def _():
                self.out_copy(slot).start()

            @pl.when(self.duty == slot)
            def _():
                self.rows_in[self.spot(slot, self.place.x, self.place.core), :] = self.fresh[self.section(slot), :]

    def gather(self):
        p = self.place
        for slot in range(3):

            @pl.when(self.duty == slot)
            def _():
                for x, core in self.users(slot):

                    @pl.when((p.x != x) | (p.core != core))
                    def _():
                        self.in_copy(slot, x, core).wait_recv()

    def give_back(self):
        p = self.place
        for slot in range(3):

            @pl.when(self.duty == slot)
            def _():
                for x, core in self.users(slot):

                    @pl.when((p.x != x) | (p.core != core))
                    def _():
                        self.back_copy(slot, x, core).start()

                self.back[self.section(slot), :] = self.rows_out[self.spot(slot, p.x, p.core), :]

    def finish(self):
        p = self.place
        for slot in range(3):

            @pl.when(self.duty != slot)
            def _():
                self.back_copy(slot, p.x, p.core).wait_recv()
                self.out_copy(slot).wait_send()

            @pl.when(self.duty == slot)
            def _():
                for x, core in self.users(slot):

                    @pl.when((p.x != x) | (p.core != core))
                    def _():
                        self.back_copy(slot, x, core).wait_send()


def base_kernel(
    ratios,
    sizes,
    master,
    momentum,
    anchor,
    loss_in,
    grads,
    *rest,
):
    place = Place()
    rest = list(rest)

    def take(count):
        taken = rest[:count]
        del rest[:count]
        return taken

    ortho_out, loss_out = take(2)
    gram, gram_total = take(2)
    gram_boxes = take(4)
    grams, fresh, rows_in, rows_out, back, tiles, tile_boxes = take(7)
    gram_sems, tile_sems, share_sems = take(3)

    rows_in[...] = jnp.zeros_like(rows_in)
    place.greet(True, True)
    fresh[...] = momentum_decay * momentum[...] + (grads[...] + prox_weight * (master[...] - anchor[...]))
    share = Share(place, sizes, (fresh, rows_in, rows_out, back), share_sems)
    share.send()
    tiles[0] = loss_in[...]
    tile_sum = TileSum(place, tiles, tile_boxes, tile_sems)
    extra = tile_sum.steps()
    extra.pop(0)()

    width = master.shape[1]
    part = width // 2
    for slot in range(3):
        section = fresh[share.section(slot), :]
        partial = lax.dot_general(
            section, section, (((0,), (0,)), ((), ())), precision=precise, preferred_element_type=wide
        )
        start = 3 * part * slot
        gram[start : start + part, :] = partial[:part, :part]
        gram[start + part : start + 2 * part, :] = partial[:part, part:]
        gram[start + 2 * part : start + 3 * part, :] = partial[part:, part:]

    gram_sum = GramSum(place, gram, gram_total, gram_boxes, gram_sems)
    gram_sum.run(extra)
    loss_out[...] = tile_sum.result()

    spots = lax.broadcasted_iota(jnp.int32, (part, part), 0)
    diagonal = spots == lax.broadcasted_iota(jnp.int32, (part, part), 1)
    start = 3 * part * share.duty
    corner = gram_total[pl.ds(pl.multiple_of(start, part), part), :]
    side = gram_total[pl.ds(pl.multiple_of(start + part, part), part), :]
    end = gram_total[pl.ds(pl.multiple_of(start + 2 * part, part), part), :]
    trace = jnp.sum(jnp.where(diagonal, corner + end, 0.0))
    factor = 1.0 / (jnp.sqrt(trace) + 1e-07)
    square = factor * factor
    grams[:part, :part] = corner * square
    grams[:part, part:] = side * square
    grams[part:, :part] = side.T * square
    grams[part:, part:] = end * square
    share.gather()
    rows_in[...] = rows_in[...] * factor

    def turn(count, carry):
        current = grams[...]
        mixed = schulz_second * current + schulz_third * dot_high(current, current)
        held = rows_in[...]
        rows_in[...] = schulz_first * held + dot_high(held, mixed)

        @pl.when(count < NS_STEPS - 1)
        def _():
            once = schulz_first * current + dot_high(current, mixed)
            grams[...] = schulz_first * once + dot_high(once, mixed)

        return carry

    lax.fori_loop(0, NS_STEPS, turn, 0)
    ratio = jnp.where(share.duty == 1, ratios[1], ratios[0])
    rows_out[...] = (rows_in[...] * ratio).astype(low_type)
    share.give_back()
    share.finish()
    ortho_out[...] = back[...].astype(wide)
    gram_sum.drain()
    tile_sum.drain()


def base_pass(ratios, sizes, master, momentum, anchor, loss_tile, grads):
    rows, width = master.shape
    part = width // 2
    vmem = pl.BlockSpec(memory_space=pltpu.VMEM)
    share = 9 * part // 32
    scratch = [pltpu.VMEM((9 * part, part), wide)] * 2
    scratch += [pltpu.VMEM((4, size, part), wide) for size in (4 * share, 2 * share, share)]
    scratch += [pltpu.VMEM((3, share, part), wide)]
    scratch += [
        pltpu.VMEM((width, width), wide),
        pltpu.VMEM((rows, width), wide),
        pltpu.VMEM((max(4 * sizes[0], 2 * sizes[1]), width), wide),
        pltpu.VMEM((max(4 * sizes[0], 2 * sizes[1]), width), low_type),
        pltpu.VMEM((rows, width), low_type),
        pltpu.VMEM((4, 8, LANES), wide),
        pltpu.VMEM((6, 8, LANES), wide),
        pltpu.SemaphoreType.DMA((2, 8, 2, 4)),
        pltpu.SemaphoreType.DMA((2, 6)),
        pltpu.SemaphoreType.DMA((2, 7)),
    ]
    block = jax.ShapeDtypeStruct((rows, width), wide)
    outs = [block, jax.ShapeDtypeStruct((8, LANES), wide)]
    operands = [master, momentum, anchor, loss_tile, grads]
    return pl.pallas_call(
        functools.partial(base_kernel, ratios, sizes),
        out_shape=outs,
        in_specs=[vmem] * len(operands),
        out_specs=[vmem] * len(outs),
        scratch_shapes=scratch,
        compiler_params=pltpu.CompilerParams(
            collective_id=1, has_side_effects=True, vmem_limit_bytes=VMEM_BYTES // 2
        ),
    )(*operands)


def update_kernel(loss_tile, master, momentum, anchor, grads, ortho, *rest):
    norms, grad_norm, heads, grad_head, outs = rest[0:3], rest[3], rest[4:7], rest[7], rest[8:]
    loss_out, *outs = outs
    loss_out[0] = loss_tile[0, 0]
    loss_out[1] = loss_tile[0, 1]
    momentum_out, base_out, low_out = outs[0:3]
    held = master[...]
    momentum_out[...] = momentum_decay * momentum[...] + (grads[...] + prox_weight * (held - anchor[...]))
    fresh = held - muon_rate * (ortho[...] + muon_decay * held)
    base_out[...] = fresh
    low_out[...] = fresh.astype(low_type)
    for targets, values, grad, rate, decay in (
        (outs[3:6], norms, grad_norm, norm_rate, 0.0),
        (outs[6:9], heads, grad_head, head_rate, head_decay),
    ):
        updates = adam_update(values[0][...], grad[...], values[1][...], values[2][...], rate, decay)
        for target, value in zip(targets, updates):
            target[...] = value


def update_pass(loss_tile, master, momentum, anchor, grads, ortho, norms, grad_norm, heads, grad_head):
    vmem = pl.BlockSpec(memory_space=pltpu.VMEM)
    smem = pl.BlockSpec(memory_space=pltpu.SMEM)
    operands = [loss_tile, master, momentum, anchor, grads, ortho, *norms, grad_norm, *heads, grad_head]
    outs = [(2,), master.shape, master.shape, master.shape] + [grad_norm.shape] * 3 + [grad_head.shape] * 3
    types = [wide, wide, wide, low_type] + [wide] * 6
    return pl.pallas_call(
        update_kernel,
        out_shape=[jax.ShapeDtypeStruct(shape, kind) for shape, kind in zip(outs, types)],
        in_specs=[smem] + [vmem] * (len(operands) - 1),
        out_specs=[smem] + [vmem] * (len(outs) - 1),
        compiler_params=pltpu.CompilerParams(vmem_limit_bytes=VMEM_BYTES // 4),
    )(*operands)


def gram_of(section):
    return lax.dot_general(section, section, (((0,), (0,)), ((), ())), precision=precise)


def square(gram):
    return jnp.dot(gram, gram, precision=precise)


def times_poly(left, mixed):
    return schulz_first * left + jnp.dot(left, mixed, precision=precise)


def schulz(sections):
    raw_grams = lax.psum(tuple(gram_of(section) for section in sections), ("client", "chan"))
    factors = [1.0 / (jnp.sqrt(jnp.trace(gram)) + 1e-07) for gram in raw_grams]
    current = [section * factor for section, factor in zip(sections, factors)]
    grams = [gram * (factor * factor) for gram, factor in zip(raw_grams, factors)]
    for turn in range(NS_STEPS):
        mixed = [schulz_second * gram + schulz_third * square(gram) for gram in grams]
        current = [times_poly(current[slot], mixed[slot]) for slot in range(3)]
        if turn + 1 < NS_STEPS:
            grams = [
                times_poly(times_poly(grams[slot], mixed[slot]), mixed[slot]) for slot in range(3)
            ]
    return current


def base_far(ratios, bounds, master, momentum, anchor, loss_tile, grads):
    sums = [
        lax.psum_scatter(flat_rows(grad).astype(wide), ("client", "chan"), scatter_dimension=0, tiled=True)
        for grad in grads
    ]
    grad_base = jnp.concatenate(sums, axis=0)
    momentum_new = momentum_decay * momentum + (grad_base + prox_weight * (master - anchor))
    current = schulz([momentum_new[bounds[slot] : bounds[slot + 1]] for slot in range(3)])
    ortho = jnp.concatenate([current[slot] * ratios[slot] for slot in range(3)], axis=0)
    return grad_base, ortho, lax.psum(loss_tile, ("client", "chan"))


def as_stored(rows, shape):
    return with_layout_constraint(rows.reshape(shape), Layout(major_to_minor=tuple(range(len(shape)))))


def on_device(
    features,
    labels,
    mask,
    base_master,
    base_momentum,
    global_base,
    norm_params,
    norm_first,
    norm_second,
    head,
    head_first,
    head_second,
):
    halves = lax.axis_size("chan")
    blocks = lax.axis_size("client") * halves
    half = features.shape[2]
    width = base_master.shape[2]
    channels = half * halves
    classes = head.shape[2]
    rows_first = channels // blocks
    rows_mid = 9 * width // blocks
    sizes = (rows_first, rows_mid, rows_first)
    bounds = (0, rows_first, rows_first + rows_mid, base_master.shape[1])
    ratio = (channels / width) ** 0.5
    ratios = (ratio, 3.0, ratio)
    master, momentum, anchor = base_master[0], base_momentum[0], global_base[0]
    norms = [value.reshape(-1, LANES) for value in (norm_params, norm_first, norm_second)]
    heads = [jnp.transpose(value, (2, 0, 1)).reshape(-1, LANES) for value in (head, head_first, head_second)]
    near = lax.axis_size("client") == SPOTS[0] * SPOTS[1] * SPOTS[2]
    if near:
        weights = [master]
    else:
        low_master = master.astype(low_type)
        weights = [
            lax.all_gather(low_master[bounds[slot] : bounds[slot + 1]], ("client", "chan"), axis=0, tiled=True)
            for slot in range(3)
        ]
        split = SPOTS + (2, channels // 32, width)
        weights = [weights[0].reshape(split), weights[1], weights[2].reshape(split)]
    *grads, grad_norm, grad_head, loss_tile = client_pass(
        near, classes, features[0], labels, mask, norms[0], heads[0], weights
    )
    if near:
        (grad_base,) = grads
        ortho, loss_tile = base_pass(ratios, sizes, master, momentum, anchor, loss_tile, grad_base)
    else:
        grad_base, ortho, loss_tile = base_far(ratios, bounds, master, momentum, anchor, loss_tile, grads)
    loss, momentum_new, base_new, base_low, *fresh = update_pass(
        loss_tile, master, momentum, anchor, grad_base, ortho, norms, grad_norm, heads, grad_head
    )
    fresh_norms = [as_stored(value, norm_params.shape) for value in fresh[:3]]
    fresh_heads = [jnp.transpose(as_stored(value, (classes, 1, half)), (1, 2, 0)) for value in fresh[3:]]
    return (
        loss,
        base_new[None],
        momentum_new[None],
        base_low[None],
        *fresh_norms,
        *fresh_heads,
    )


def solution(mesh):
    wide_block = P(("client", "chan"), None, None)
    norm_block = P("client", None, "chan", None)
    head_block = P("client", "chan", None)
    return jax.shard_map(
        on_device,
        mesh=mesh,
        in_specs=(P("client", None, "chan"), P("client", None), P("client"))
        + (wide_block,) * 3
        + (norm_block,) * 3
        + (head_block,) * 3,
        out_specs=(P(),) + (wide_block,) * 3 + (norm_block,) * 3 + (head_block,) * 3,
        check_vma=False,
    )
```

```python
import functools

import jax
import jax.numpy as jnp
from jax import lax
from jax.experimental import pallas as pl
from jax.experimental.layout import Layout, with_layout_constraint
from jax.experimental.pallas import tpu as pltpu
from jax.sharding import PartitionSpec as P

NS_STEPS = 5
STEP = 10

low_type = jnp.bfloat16
wide = jnp.float32
MESH = pl.DeviceIdType.MESH
precise = lax.Precision.HIGHEST
norm_epsilon = 1e-05
prox_weight = 0.05
momentum_decay = 0.95
muon_rate = 0.3
muon_decay = 0.1
schulz_first = 3.4445
schulz_second = -4.775
schulz_third = 2.0315
adam_first = 0.9
adam_second = 0.95
adam_epsilon = 1e-08
head_rate = 0.01
head_decay = 0.05
norm_rate = 0.5

SIDE = 7
PIXELS = SIDE * SIDE
LANES = 128
SPOTS = (4, 2, 2)
VMEM_BYTES = 62 * 2**20


def when(condition, call):
    if isinstance(condition, bool):
        if condition:
            call()
    else:
        pl.when(condition)(call)


def dot_nn(left, right):
    return jnp.dot(left, right, preferred_element_type=wide)


def dot_nt(left, right):
    return lax.dot_general(left, right, (((1,), (1,)), ((), ())), preferred_element_type=wide)


def dot_tn(left, right):
    return lax.dot_general(left, right, (((0,), (0,)), ((), ())), preferred_element_type=wide)


def flat_rows(block):
    return block.reshape(-1, block.shape[-1])


def sigmoid(value):
    return 0.5 * jnp.tanh(0.5 * value) + 0.5


def fold_rows(value):
    return jnp.sum(value.reshape(value.shape[0] // 8, 8, value.shape[1]), axis=0)


def column_sum(value):
    return jnp.sum(value, axis=0, keepdims=True)


def remote(src, dst, send_sem, recv_sem, client, core):
    return pltpu.make_async_remote_copy(
        src_ref=src,
        dst_ref=dst,
        send_sem=send_sem,
        recv_sem=recv_sem,
        device_id=(client, core),
        device_id_type=MESH,
    )


class Place:
    def __init__(self):
        self.client = lax.axis_index("client")
        self.core = lax.axis_index("chan")
        self.z = self.client // 4
        self.y = (self.client // 2) % 2
        self.x = self.client % 2
        self.others = [
            self.z + 1 - 2 * (self.z % 2),
            (self.z + 2) % 4,
            3 - self.z,
        ]

    def at(self, z, y, x):
        return z * 4 + y * 2 + x

    def along_x(self):
        return self.at(self.z, self.y, 1 - self.x)

    def along_y(self):
        return self.at(self.z, 1 - self.y, self.x)

    def along_z(self, step):
        return self.at(self.others[step], self.y, self.x)

    def greet(self, whole, across=False):
        barrier = pltpu.get_barrier_semaphore()
        pairs = [(self.client, 1 - self.core)]
        if whole:
            pairs += [(self.along_x(), self.core), (self.along_y(), self.core)]
            pairs += [(self.along_z(step), self.core) for step in range(3)]
        if across:
            pairs += [(self.along_x(), 1 - self.core)]
        for pair in pairs:
            pl.semaphore_signal(barrier, inc=1, device_id=pair, device_id_type=MESH)
        pl.semaphore_wait(barrier, len(pairs))


def cut_rows(counts):
    pieces = []
    for slot, rows in enumerate(counts):
        middle = (rows // 16 + 1) // 2 * 16
        pieces.append((slot, 0, middle, 0))
        pieces.append((slot, middle, rows - middle, 1))
    return pieces


def block_ref(ref, size, z, y, x, core, start, count):
    if len(ref.shape) == 2:
        first = (((z * 2 + y) * 2 + x) * 2 + core) * size + start
        return ref.at[pl.ds(pl.multiple_of(first, 16), count), :]
    return ref.at[z, y, x, core, pl.ds(start, count), :]


class Spread:
    def __init__(self, place, weights, counts, sems):
        self.place = place
        self.weights = weights
        self.counts = counts
        self.pieces = cut_rows(counts)
        self.z_sems, self.near_sems, self.far_sems, self.core_sems = sems
        self.order = [place.z] + place.others

    def z_copy(self, step, slot):
        p = self.place
        ref = block_ref(self.weights[slot], self.counts[slot], p.z, p.y, p.x, p.core, 0, self.counts[slot])
        sems = self.z_sems
        return remote(ref, ref, sems.at[0, step, slot], sems.at[1, step, slot], p.along_z(step), p.core)

    def near_copy(self, turn, number):
        p = self.place
        slot, start, count, way = self.pieces[number]
        ref = block_ref(self.weights[slot], self.counts[slot], self.order[turn], p.y, p.x, p.core, start, count)
        sems = self.near_sems
        return remote(
            ref, ref, sems.at[0, turn, number], sems.at[1, turn, number], (p.along_x, p.along_y)[way](), p.core
        )

    def far_copies(self, turn, number):
        p = self.place
        slot, start, count, way = self.pieces[number]
        spot = self.order[turn]
        sems = self.far_sems
        copies = []
        for part, other in enumerate((0, 1) if slot == 1 else (slice(None),)):
            y, x = (p.y, other) if way == 0 else (other, p.x)
            ref = block_ref(self.weights[slot], self.counts[slot], spot, y, x, p.core, start, count)
            sem = number + 4 * part
            to = (p.along_y, p.along_x)[way]()
            copies.append(remote(ref, ref, sems.at[0, turn, sem], sems.at[1, turn, sem], to, p.core))
        return copies

    def core_copies(self, turn, slot):
        p = self.place
        sems = self.core_sems
        copies = []
        pairs = [(y, x) for y in (0, 1) for x in (0, 1)] if slot == 1 else [(slice(None), slice(None))]
        for part, (y, x) in enumerate(pairs):
            ref = block_ref(self.weights[slot], self.counts[slot], self.order[turn], y, x, p.core, 0, self.counts[slot])
            sem = (0, 2 + part, 1)[slot]
            copies.append(remote(ref, ref, sems.at[0, turn, sem], sems.at[1, turn, sem], p.client, 1 - p.core))
        return copies

    def begin(self, master):
        p = self.place
        start = 0
        for slot in range(3):
            rows = self.counts[slot]
            own = block_ref(self.weights[slot], self.counts[slot], p.z, p.y, p.x, p.core, 0, rows)
            own[...] = master[start : start + rows, :].astype(low_type)
            start += rows
        for step in range(3):
            self.z_copy(step, 0).start()
        self.near_start(0)

    def near_start(self, slot):
        for number in (2 * slot, 2 * slot + 1):
            self.near_copy(0, number).start()

    def steps(self):
        near, far, core, start = self.near_step, self.far_step, self.core_step, self.near_start
        groups = [
            [(far, 0, 0), (start, 1)],
            [(near, 1, 0)],
            [(near, 2, 0), (near, 3, 0)],
            [(far, 1, 0), (core, 0, 0), (far, 0, 1)],
            [(far, 2, 0), (far, 3, 0), (core, 1, 0)],
            [(core, 2, 0), (core, 3, 0), (near, 1, 1), (start, 2)],
            [(core, 0, 1), (near, 2, 1)],
            [(far, 1, 1), (near, 3, 1)],
            [(core, 1, 1), (far, 2, 1), (far, 0, 2)],
            [(far, 3, 1), (core, 2, 1), (near, 1, 2)],
            [(core, 3, 1), (core, 0, 2), (near, 2, 2)],
            [(far, 1, 2), (near, 3, 2)],
            [(core, 1, 2), (far, 2, 2)],
            [(far, 3, 2), (core, 2, 2)],
            [(core, 3, 2)],
        ]
        return [[functools.partial(*step) for step in group] for group in groups]

    def near_step(self, turn, slot):
        self.z_copy(turn - 1, slot).wait_recv()
        for number in (2 * slot, 2 * slot + 1):
            self.near_copy(turn, number).start()
        if slot < 2:
            self.z_copy(turn - 1, slot + 1).start()

    def far_step(self, turn, slot):
        for number in (2 * slot, 2 * slot + 1):
            self.near_copy(turn, number).wait_recv()
            for copy in self.far_copies(turn, number):
                copy.start()

    def core_step(self, turn, slot):
        for number in (2 * slot, 2 * slot + 1):
            for copy in self.far_copies(turn, number):
                copy.wait_recv()
        for copy in self.core_copies(turn, slot):
            copy.start()

    def arrive(self, slot):
        for turn in range(4):
            for copy in self.core_copies(turn, slot):
                copy.wait_recv()

    def drain(self):
        for slot in range(3):
            for step in range(3):
                self.z_copy(step, slot).wait_send()
            for turn in range(4):
                for copy in self.core_copies(turn, slot):
                    copy.wait_send()
        for number in range(6):
            for turn in range(4):
                self.near_copy(turn, number).wait_send()
                for copy in self.far_copies(turn, number):
                    copy.wait_send()


class Fold:
    def __init__(self, place, grads, counts, parts):
        self.place = place
        self.grads = grads
        self.counts = counts
        self.pieces = cut_rows(counts)
        self.core_boxes = [parts[1], parts[0], parts[1]]
        self.near_boxes, self.far_boxes, self.z_boxes = [parts[3 * k + 2 : 3 * k + 5] for k in range(3)]
        self.core_sems, self.near_sems, self.far_sems, self.z_sems = parts[11:]

    def core_copies(self, which, slot):
        p = self.place
        sems = self.core_sems
        copies = []
        pairs = [(y, x) for y in (0, 1) for x in (0, 1)] if slot == 1 else [(slice(None), slice(None))]
        for part, (y, x) in enumerate(pairs):
            ref = block_ref(self.grads[slot], self.counts[slot], which, y, x, 1 - p.core, 0, self.counts[slot])
            box = self.core_boxes[slot].at[which, y, x]
            sem = (0, 2 + part, 1)[slot]
            copies.append(remote(ref, box, sems.at[0, which, sem], sems.at[1, which, sem], p.client, 1 - p.core))
        return copies

    def near_copies(self, which, number):
        p = self.place
        slot, start, count, way = self.pieces[number]
        sems = self.near_sems
        copies = []
        for part, other in enumerate((0, 1) if slot == 1 else (slice(None),)):
            y, x = (other, 1 - p.x) if way == 0 else (1 - p.y, other)
            ref = block_ref(self.grads[slot], self.counts[slot], which, y, x, p.core, start, count)
            box = self.near_boxes[slot].at[which, other, pl.ds(start, count), :]
            sem = number + 4 * part
            to = (p.along_x, p.along_y)[way]()
            copies.append(remote(ref, box, sems.at[0, which, sem], sems.at[1, which, sem], to, p.core))
        return copies

    def far_copy(self, which, number):
        p = self.place
        slot, start, count, way = self.pieces[number]
        y, x = (1 - p.y, p.x) if way == 0 else (p.y, 1 - p.x)
        ref = block_ref(self.grads[slot], self.counts[slot], which, y, x, p.core, start, count)
        box = self.far_boxes[slot].at[which, pl.ds(start, count), :]
        sems = self.far_sems
        return remote(
            ref, box, sems.at[0, which, number], sems.at[1, which, number], (p.along_y, p.along_x)[way](), p.core
        )

    def z_copy(self, which, sender, number):
        p = self.place
        slot, start, count, _ = self.pieces[number]
        rows = pl.ds(start, count)
        sems = self.z_sems
        return remote(
            block_ref(self.grads[slot], self.counts[slot], which, p.y, p.x, p.core, start, count),
            self.z_boxes[slot].at[sender, rows, :],
            sems.at[0, which, number],
            sems.at[1, sender, number],
            p.at(which, p.y, p.x),
            p.core,
        )

    def begin(self, which, slot):
        for copy in self.core_copies(which, slot):
            copy.start()

    def add(self, slot, spots, start, count, box):
        ref = block_ref(self.grads[slot], self.counts[slot], *spots, self.place.core, start, count)
        ref[...] = (ref[...].astype(wide) + box.astype(wide)).astype(low_type)

    def turn(self, slot, turn):
        for lag, step in ((2, self.far_step), (1, self.near_step), (0, self.core_step)):
            when((turn >= lag) & (turn < lag + 4), functools.partial(step, turn - lag, slot))

    def core_step(self, which, slot):
        for copy in self.core_copies(which, slot):
            copy.wait_recv()
        pairs = [(y, x) for y in (0, 1) for x in (0, 1)] if slot == 1 else [(slice(None), slice(None))]
        for y, x in pairs:
            self.add(slot, (which, y, x), 0, self.counts[slot], self.core_boxes[slot][which, y, x])
        for number in (2 * slot, 2 * slot + 1):
            for copy in self.near_copies(which, number):
                copy.start()

    def near_step(self, which, slot):
        p = self.place
        for number in (2 * slot, 2 * slot + 1):
            _, start, count, way = self.pieces[number]
            for copy in self.near_copies(which, number):
                copy.wait_recv()
            for other in (0, 1) if slot == 1 else (slice(None),):
                y, x = (other, p.x) if way == 0 else (p.y, other)
                box = self.near_boxes[slot][which, other, pl.ds(start, count), :]
                self.add(slot, (which, y, x), start, count, box)
            self.far_copy(which, number).start()

    def far_step(self, which, slot):
        p = self.place
        for number in (2 * slot, 2 * slot + 1):
            _, start, count, way = self.pieces[number]
            self.far_copy(which, number).wait_recv()
            box = self.far_boxes[slot][which, pl.ds(start, count), :]
            self.add(slot, (which, p.y, p.x), start, count, box)

            @pl.when(p.z != which)
            def _():
                self.z_copy(which, p.z, number).start()

    def result(self, slot):
        p = self.place
        self.z_boxes[slot][p.z] = block_ref(self.grads[slot], self.counts[slot], p.z, p.y, p.x, p.core, 0, self.counts[slot])[...]
        for sender in range(4):

            @pl.when(p.z != sender)
            def _():
                for number in (2 * slot, 2 * slot + 1):
                    self.z_copy(sender, sender, number).wait_recv()

        total = self.z_boxes[slot][0].astype(wide)
        for sender in range(1, 4):
            total += self.z_boxes[slot][sender].astype(wide)
        return total

    def drain(self):
        for which in range(4):
            for slot in range(3):
                for copy in self.core_copies(which, slot):
                    copy.wait_send()
            for number in range(6):
                for copy in self.near_copies(which, number):
                    copy.wait_send()
                self.far_copy(which, number).wait_send()

            @pl.when(self.place.z != which)
            def _():
                for number in range(6):
                    self.z_copy(which, self.place.z, number).wait_send()


def norm_stats(mine, theirs, count):
    gap = mine[0:1] - theirs[0:1]
    mean = 0.5 * (mine[0:1] + theirs[0:1])
    spread = mine[1:2] + theirs[1:2] + gap * gap * (0.5 * count)
    return mean, lax.rsqrt(spread / (2.0 * count) + norm_epsilon)


def client_kernel(
    gather,
    images,
    classes,
    features,
    labels,
    flag,
    params,
    head,
    *rest,
):
    if gather:
        master, *rest = rest
    else:
        first_in, middle_in, last_in, *rest = rest
    if gather:
        grads_out, *rest = rest
    else:
        grads_out, rest = rest[:3], rest[3:]
    (
        grad_norm_out,
        grad_head_out,
        loss_out,
        x_all,
        mid_wide,
        w_first,
        w_middle,
        w_last,
        act_one,
        act_two,
        act_three,
        taps_one,
        taps_two,
        hidden_two,
        stage,
        params_all,
        head_all,
        grad_pool,
        pool_send,
        pool_all,
        logit_grads,
        sums_mine,
        sums_theirs,
        shift,
        fwd_stats,
        sem_local,
        sem_swap,
        sem_misc,
        *near_parts,
    ) = rest
    place = Place()
    core = place.core
    mate = (place.client, 1 - core)
    count_rows, channels = x_all.shape
    half = channels // 2
    width = act_one.shape[1]
    part = width // 2
    mine_images = images // 2
    line = SIDE * mine_images
    total_rows = 2.0 * count_rows

    def tile(index):
        return pl.ds(pl.multiple_of(index * line, line), line)

    def lanes(index, size):
        return pl.ds(pl.multiple_of(index * size, size), size)

    place.greet(gather)

    quarter = half // 2
    own_rows = pl.ds(pl.multiple_of(core * count_rows, count_rows), count_rows)
    mate_rows = pl.ds(pl.multiple_of((1 - core) * count_rows, count_rows), count_rows)
    top_rows = pl.ds(0, count_rows)
    own_copies = [
        pltpu.make_async_copy(
            features.at[own_rows, pl.ds(side * quarter, quarter)], buffer, sem_local.at[side]
        )
        for side, buffer in enumerate((hidden_two, mid_wide.at[top_rows, :]))
    ]
    per_kind = params.shape[0] // 2
    for kind in range(2):
        rows = [params[kind * per_kind + spot : kind * per_kind + spot + 1, :] for spot in range(per_kind)]
        params_all[core, kind : kind + 1, :] = jnp.concatenate(rows, axis=1)
    head_all[core] = jnp.zeros(head_all.shape[1:], low_type)
    for spot in range(half // LANES):
        head_all[core, 0:classes, spot * LANES : (spot + 1) * LANES] = head[
            pl.ds(spot, classes, stride=half // LANES), :
        ].astype(low_type)
    to_mate = [
        remote(params_all.at[core], params_all.at[core], sem_misc.at[0, 0], sem_misc.at[1, 0], *mate),
        remote(head_all.at[core], head_all.at[core], sem_misc.at[0, 1], sem_misc.at[1, 1], *mate),
    ]
    for side, buffer in enumerate((taps_one, taps_two)):
        to_mate.append(
            remote(
                features.at[mate_rows, pl.ds(side * quarter, quarter)],
                buffer.at[top_rows, :],
                sem_misc.at[0, 5 + side],
                sem_misc.at[1, 5 + side],
                *mate,
            )
        )
    for copy in to_mate + own_copies:
        copy.start()

    weights = (w_first, w_middle, w_last)
    if gather:
        counts = [channels // 32, 9 * width // 32, channels // 32]
        spread = Spread(place, weights, counts, near_parts[:4])
        held = act_three.at[pl.ds(0, master.shape[0]), pl.ds(0, width)]
        load = pltpu.make_async_copy(master, held, sem_local.at[8])
        load.start()
        load.wait()
        spread.begin(held)
        fold = Fold(place, (w_first, mid_wide, w_last), counts, near_parts[4:])
        due = spread.steps()
    else:
        loads = [
            pltpu.make_async_copy(src, dst, sem_local.at[8 + slot])
            for slot, (src, dst) in enumerate(zip((first_in, middle_in, last_in), weights))
        ]
        for load in loads:
            load.start()
        due = []

    def advance(count):
        for group in due[:count]:
            for step in group:
                step()
        del due[:count]

    def advance_at(index, spots):
        for spot, group in zip(spots, due):

            @pl.when(index == spot)
            def _():
                for step in group:
                    step()

    def arrive(slot, left):
        if gather:
            advance(len(due) - left)
            spread.arrive(slot)
        else:
            loads[slot].wait()

    def fold_turn(slot, turn):
        if gather:
            fold.turn(slot, turn)

    def fold_step(kind, slot, which):
        if gather:
            (fold.core_step, fold.near_step, fold.far_step)[kind](which, slot)

    def fold_at(index, spot, *steps):
        @pl.when(index == spot)
        def _():
            for step in steps:
                fold_step(*step)

    def fold_begin(which, slot):
        if gather:
            fold.begin(which, slot)

    def zero_edges(buffer):
        edge = jnp.zeros((line,) + buffer.shape[1:], low_type)
        buffer[0:line, :] = edge
        buffer[line + count_rows : 2 * line + count_rows, :] = edge

    advance(3)
    for copy in own_copies:
        copy.wait()

    def turn_from(source, base):
        def turn(index, carry):
            stage[...] = source(lanes(index, LANES)).astype(wide)

            def pixel(spot, inner):
                x_all[
                    pl.ds(pl.multiple_of(spot * mine_images, mine_images), mine_images),
                    pl.ds(pl.multiple_of(base + index * LANES, LANES), LANES),
                ] = stage[pl.ds(spot, mine_images, stride=PIXELS), :].astype(low_type)
                return inner

            return lax.fori_loop(0, PIXELS, pixel, carry, unroll=7)

        return turn

    quarters = quarter // LANES
    own_base, mate_base = core * half, (1 - core) * half
    lax.fori_loop(0, quarters, turn_from(lambda columns: hidden_two[:, columns], own_base), 0)
    advance(1)
    lax.fori_loop(
        0,
        quarters,
        turn_from(lambda columns: mid_wide[0:count_rows, columns], own_base + quarter),
        0,
    )
    advance(1)
    for copy in to_mate:
        copy.wait_recv()
    lax.fori_loop(0, quarters, turn_from(lambda columns: taps_one[0:count_rows, columns], mate_base), 0)
    advance(1)
    lax.fori_loop(0, quarters, turn_from(lambda columns: taps_two[0:count_rows, columns], mate_base + quarter), 0)
    zero_edges(taps_one)
    zero_edges(taps_two)
    arrive(0, 9)

    def swap(slot, size):
        return remote(
            sums_mine.at[slot, :, pl.ds(0, size)],
            sums_theirs.at[slot, :, pl.ds(0, size)],
            sem_swap.at[0, slot],
            sem_swap.at[1, slot],
            *mate,
        )

    def gain_bias(lower, upper):
        rows = []
        for kind in range(2):
            pieces = [params_all[side, kind : kind + 1, lower:upper] for side in range(2)]
            rows.append(jnp.concatenate(pieces, axis=1))
        return rows

    def collect(index, value, columns, size):
        @pl.when(index == 0)
        def _():
            shift[0:1, pl.ds(0, size)] = column_sum(fold_rows(value)) / value.shape[0]
            shift[8:24, pl.ds(0, size)] = jnp.zeros((16, size), wide)

        gap = value - shift[0:1, pl.ds(0, size)]
        shift[8:16, pl.ds(0, size)] += fold_rows(gap)
        shift[16:24, pl.ds(0, size)] += fold_rows(gap * gap)

    def close_stats(slot, columns, size):
        sum_gap = column_sum(shift[8:16, pl.ds(0, size)])
        sum_square = column_sum(shift[16:24, pl.ds(0, size)])
        sums_mine[slot, 0:1, columns] = shift[0:1, pl.ds(0, size)] + sum_gap / count_rows
        sums_mine[slot, 1:2, columns] = sum_square - sum_gap * sum_gap / count_rows

    def look_over(act, columns):
        def look(index, carry):
            collect(index, act[tile(index), columns], None, width)
            return carry

        lax.fori_loop(0, SIDE, look, 0)

    groups = SPOTS[0]
    group = channels // groups

    def settle(slot, size):
        mean, scale = norm_stats(
            sums_mine[slot, 0:2, pl.ds(0, size)], sums_theirs[slot, 0:2, pl.ds(0, size)], float(count_rows)
        )
        fwd_stats[slot, 0:1, pl.ds(0, size)] = mean
        fwd_stats[slot, 1:2, pl.ds(0, size)] = scale

    whole_width = pl.ds(0, width)

    def first_part(index, carry):
        act_one[...] += dot_nn(x_all[:, lanes(index, group)], flat_rows(w_first[index]))
        advance_at(index, (0, 1, 2))
        return carry

    act_one[...] = jnp.zeros_like(act_one)
    lax.fori_loop(0, groups, first_part, 0)
    del due[:3]
    look_over(act_one, whole_width)
    close_stats(0, whole_width, width)
    move = swap(0, width)
    move.start()
    advance(1)
    move.wait()
    settle(0, width)

    gain_one, bias_one = gain_bias(0, part)
    gain_two, bias_two = gain_bias(part, width)
    gain_three, bias_three = gain_bias(width, width + half)

    def normal(act, slot, index):
        mean = fwd_stats[slot, 0:1, pl.ds(0, width)]
        return (act[tile(index), :] - mean) * fwd_stats[slot, 1:2, pl.ds(0, width)]

    def hide_one(index, carry):
        value = normal(act_one, 0, index) * gain_one + bias_one
        taps_one[pl.ds(pl.multiple_of((index + 1) * line, line), line), :] = (value * sigmoid(value)).astype(low_type)
        return carry

    lax.fori_loop(0, SIDE, hide_one, 0)
    arrive(1, 4)

    step = mine_images
    piece = width // 2

    def row_windows(buffer, down, start, reach):
        if reach == line:
            return buffer[pl.ds(pl.multiple_of(down * line, line), count_rows), :]
        windows = [
            buffer[pl.ds(pl.multiple_of((down + row) * line + start, step), reach), :] for row in range(SIDE)
        ]
        return jnp.concatenate(windows, axis=0)

    def add_windows(target, columns, value, start, reach):
        for row in range(SIDE):
            rows = slice(row * line + start, row * line + start + reach)
            target[rows, columns] += value[row * reach : (row + 1) * reach]

    low_start, high_start, reaches = (0, 0, step), (step, 0, 0), (line - step, line, line - step)

    def second_part(index, carry):
        down, columns = index // 2, lanes(index % 2, piece)
        for over in range(3):
            left = row_windows(taps_one, down, low_start[over], reaches[over])
            kernel = w_middle[pl.ds(pl.multiple_of((3 * down + over) * width, width), width), columns]
            add_windows(act_two, columns, dot_nn(left, kernel), high_start[over], reaches[over])
        advance_at(index, (1, 3, 5))
        return carry

    act_two[...] = jnp.zeros_like(act_two)
    lax.fori_loop(0, 6, second_part, 0)
    del due[:3]
    look_over(act_two, whole_width)
    close_stats(1, whole_width, width)
    move_two = swap(1, width)
    move_two.start()
    move_two.wait()
    settle(1, width)

    arrive(2, 0)

    def third_line(index, carry):
        value = normal(act_two, 1, index) * gain_two + bias_two
        hidden = (value * sigmoid(value)).astype(low_type)
        hidden_two[tile(index), :] = hidden
        value = dot_nt(hidden, flat_rows(w_last[...]))
        act_three[tile(index), :] = value
        start = jnp.where(index == 0, column_sum(value[0:8]) / 8.0, shift[0:1, :])
        gap = value - start
        kept_sums = jnp.where(index == 0, 0.0, shift[8:24, :])
        shift[0:1, :] = start
        shift[8:16, :] = kept_sums[0:8] + fold_rows(gap)
        shift[16:24, :] = kept_sums[8:16] + fold_rows(gap * gap)
        return carry

    lax.fori_loop(0, SIDE, third_line, 0)
    close_stats(2, pl.ds(0, channels), channels)
    move_three = swap(2, channels)
    move_three.start()
    move_three.wait()
    settle(2, channels)

    per_group = group // LANES

    def block_of(spot):
        return pl.ds(pl.multiple_of(spot * mine_images, mine_images), mine_images)

    def mid_line(which, index):
        return pl.ds(pl.multiple_of(which * count_rows + index * line, line), line)

    kept = channels // LANES * mine_images

    def gathered(kind):
        starts = range(kind * kept, (kind + 1) * kept, mine_images)
        return jnp.concatenate([stage[start : start + mine_images, :] for start in starts], axis=1)

    fwd_stats[2, 4:5, :] = fwd_stats[2, 1:2, :] * gain_three
    fwd_stats[2, 5:6, :] = bias_three - fwd_stats[2, 0:1, :] * fwd_stats[2, 4:5, :]

    def emit(index, carry):
        columns = lanes(index, LANES)
        slant, level = fwd_stats[2, 4:5, columns], fwd_stats[2, 5:6, columns]

        def pixels(row, sums):
            pooled, steeps, steeps_act = sums
            found = []
            for spot in range(SIDE):
                where = block_of(row * SIDE + spot)
                act = act_three[where, columns]
                half_total = 0.5 * (act * slant + level + x_all[where, columns].astype(wide))
                rise = 1.0 + jnp.tanh(half_total)
                out = half_total * rise
                steep = rise + out * (2.0 - rise)
                found.append(steep.astype(low_type))
                pooled, steeps, steeps_act = pooled + out, steeps + steep, steeps_act + steep * act
            mid_wide[mid_line(index // per_group, row), lanes(index % per_group, LANES)] = jnp.concatenate(
                found, axis=0
            )
            return pooled, steeps, steeps_act

        zero = jnp.zeros((mine_images, LANES), wide)
        sums = lax.fori_loop(0, SIDE, pixels, (zero, zero, zero))
        for kind, value in enumerate(sums):
            stage[pl.ds(pl.multiple_of(kind * kept + index * mine_images, mine_images), mine_images), :] = value
        return carry

    lax.fori_loop(0, channels // LANES, emit, 0)

    pooled = (gathered(0) / PIXELS).astype(low_type)
    head_full = jnp.concatenate([head_all[0], head_all[1]], axis=1)
    logits = dot_nt(head_full, pooled)
    spots = lax.broadcasted_iota(jnp.int32, logits.shape, 0)
    inside = spots < classes
    first_labels, second_labels = labels[0:1, 0:mine_images], labels[0:1, mine_images:]
    onehot = (spots == jnp.where(core == 0, first_labels, second_labels)).astype(wide)
    top = jnp.max(jnp.where(inside, logits, -jnp.inf), axis=0, keepdims=True)
    powers = jnp.where(inside, jnp.exp(logits - top), 0.0)
    power_sum = jnp.sum(powers, axis=0, keepdims=True)
    picked = jnp.sum(logits * onehot, axis=0, keepdims=True)
    each_loss = top + jnp.log(power_sum) - picked
    taking = flag[0].astype(wide)
    tile_spots = lax.broadcasted_iota(jnp.int32, loss_out.shape, 1)
    loss_out[...] = jnp.where(tile_spots == 0, taking * jnp.sum(each_loss), taking * mine_images)
    grads = (taking / images * (powers / power_sum - onehot)).astype(low_type)
    grad_pool[...] = dot_tn(grads, head_full) * (0.5 / PIXELS)
    logit_grads[core] = grads
    pool_all[core] = pooled[:, 0:half]
    pool_send[...] = pooled[:, half:]

    @pl.when(core == 1)
    def _():
        pool_all[core] = pooled[:, half:]
        pool_send[...] = pooled[:, 0:half]

    head_moves = [
        remote(pool_send, pool_all.at[core], sem_misc.at[0, 3], sem_misc.at[1, 3], *mate),
        remote(logit_grads.at[core], logit_grads.at[core], sem_misc.at[0, 4], sem_misc.at[1, 4], *mate),
    ]

    steeps = gathered(1)
    steeps_normed = (gathered(2) - fwd_stats[2, 0:1, :] * steeps) * fwd_stats[2, 1:2, :]
    sums_mine[3, 0:1, :] = column_sum(grad_pool[...] * steeps)
    sums_mine[3, 1:2, :] = column_sum(grad_pool[...] * steeps_normed)
    move_back = swap(3, channels)
    move_back.start()
    for copy in head_moves:
        copy.start()
    move_back.wait()

    def back_terms(slot, layer, size, gain):
        columns = pl.ds(0, size)
        sums = sums_mine[slot, 0:2, columns] + sums_theirs[slot, 0:2, columns]
        sums_mine[slot, 2:4, columns] = sums
        scale = fwd_stats[layer, 1:2, columns]
        return (
            scale * gain,
            scale * gain * sums[0:1] / total_rows,
            scale * scale * gain * sums[1:2] / total_rows,
        )

    first, second, third = back_terms(3, 2, channels, gain_three)
    fwd_stats[2, 4:5, :] = second - third * fwd_stats[2, 0:1, :]
    fwd_stats[2, 5:6, :] = third
    grad_pool[...] = grad_pool[...] * first

    def pull(index):
        for which in range(groups):
            columns = slice(which * group, (which + 1) * group)
            reach = grad_pool[:, columns]
            steep = mid_wide[mid_line(which, index), :].astype(wide)
            value = jnp.concatenate([reach] * SIDE, axis=0) * steep
            value = value - fwd_stats[2, 4:5, columns] - fwd_stats[2, 5:6, columns] * act_three[tile(index), columns]
            mid_wide[mid_line(which, index), :] = value.astype(low_type)

    pull(0)
    for copy in head_moves:
        copy.wait_recv()
    head_grad = dot_nn(logit_grads[0], pool_all[0]) + dot_nn(logit_grads[1], pool_all[1])
    for spot in range(half // LANES):
        stage[pl.ds(spot, classes, stride=half // LANES), :] = head_grad[
            0:classes, spot * LANES : (spot + 1) * LANES
        ]
    head_space = stage.at[pl.ds(0, grad_head_out.shape[0]), :]
    head_leave = pltpu.make_async_copy(head_space, grad_head_out, sem_local.at[0])
    head_leave.start()

    def drop_into(act, slot, gain, bias, columns):
        size = pl.ds(0, width)
        shift[8:24, size] = jnp.zeros((16, width), wide)

        def drop(index, carry):
            normed = normal(act, slot, index)
            norm = normed * gain + bias
            sig = sigmoid(norm)
            grad = act_three[tile(index), columns] * (sig + norm * sig * (1.0 - sig))
            act_three[tile(index), columns] = grad
            shift[8:16, size] += fold_rows(grad)
            shift[16:24, size] += fold_rows(grad * normed)
            return carry

        lax.fori_loop(0, SIDE, drop, 0)

    def close_back(slot):
        size = pl.ds(0, width)
        sums_mine[slot, 0:1, size] = column_sum(shift[8:16, size])
        sums_mine[slot, 1:2, size] = column_sum(shift[16:24, size])

    space_two, space_one = pl.ds(0, width), pl.ds(width, width)

    def mid_group(which):
        return mid_wide[pl.ds(pl.multiple_of(which * count_rows, count_rows), count_rows), :]

    def back_two(index):
        left = jnp.concatenate([mid_wide[mid_line(which, index), :] for which in range(groups)], axis=1)
        value = dot_nn(left, flat_rows(w_last[...]))
        normed = normal(act_two, 1, index)
        norm = normed * gain_two + bias_two
        sig = sigmoid(norm)
        grad = value * (sig + norm * sig * (1.0 - sig))
        act_three[tile(index), space_two] = grad
        size = pl.ds(0, width)
        shift[8:16, size] += fold_rows(grad)
        shift[16:24, size] += fold_rows(grad * normed)

    def back_two_line(index, carry):
        pull(index + 1)
        back_two(index)
        return carry

    shift[8:24, :] = jnp.zeros((16, channels), wide)
    lax.fori_loop(0, SIDE - 1, back_two_line, 0)
    back_two(SIDE - 1)
    close_back(4)
    move_back_two = swap(4, width)
    move_back_two.start()

    if gather:
        spread.drain()

    def put(ref, which, value):
        ref[which] = value.astype(low_type).reshape(ref.shape[1:])

    def expand_group(which, carry):
        put(w_last, which, dot_tn(mid_group(which), hidden_two[...]))
        fold_begin(which, 2)
        fold_turn(2, which - 1)
        return carry

    lax.fori_loop(0, groups, expand_group, 0)
    move_back_two.wait()
    terms_two = back_terms(4, 1, width, gain_two)

    def back_act(terms, act, layer, index, columns):
        first, second, third = terms
        gap = act[tile(index), :] - fwd_stats[layer, 0:1, pl.ds(0, width)]
        return (first * act_three[tile(index), columns] - second - third * gap).astype(low_type)

    def grad_two(index, carry):
        taps_two[pl.ds(pl.multiple_of((index + 1) * line, line), line), :] = back_act(
            terms_two, act_two, 1, index, space_two
        )
        return carry

    lax.fori_loop(0, SIDE, grad_two, 0)
    fold_turn(2, groups - 1)
    def middle_row(down, carry):
        for over in range(3):
            left = row_windows(taps_one, down, low_start[over], reaches[over])
            right = row_windows(taps_two, 1, high_start[over], reaches[over])
            rows = pl.ds(pl.multiple_of((3 * down + over) * width, width), width)
            mid_wide[rows, :] = dot_tn(left, right).astype(low_type)
        fold_begin(down, 1)

        @pl.when(down == 2)
        def _():
            fold_begin(3, 1)

        fold_turn(2, groups + down)
        fold_at(down, 1, (0, 1, 0))
        fold_at(down, 2, (1, 1, 0), (0, 1, 1))
        return carry

    lax.fori_loop(0, 3, middle_row, 0)

    def back_one(index, carry):
        down, side = index // 2, index % 2
        columns = lanes(2 + side, piece)
        for over in range(3):
            left = row_windows(taps_two, 2 - down, high_start[over], reaches[over])
            start = pl.multiple_of((3 * down + over) * width + side * piece, piece)
            value = dot_nt(left, w_middle[pl.ds(start, piece), :])
            add_windows(act_three, columns, value, low_start[over], reaches[over])
        fold_at(index, 0, (0, 1, 2))
        fold_at(index, 1, (0, 1, 3))
        fold_at(index, 2, (1, 1, 1))
        fold_at(index, 3, (2, 1, 0))
        fold_at(index, 4, (1, 1, 2))
        fold_at(index, 5, (2, 1, 1))
        return carry

    act_three[:, space_one] = jnp.zeros((count_rows, width), wide)
    lax.fori_loop(0, 6, back_one, 0)
    drop_into(act_one, 0, gain_one, bias_one, space_one)
    fold_step(1, 1, 3)
    close_back(5)
    move_back_one = swap(5, width)
    move_back_one.start()

    move_back_one.wait()
    terms_one = back_terms(5, 0, width, gain_one)

    def grad_one(index, carry):
        hidden_two[tile(index), :] = back_act(terms_one, act_one, 0, index, space_one)
        return carry

    lax.fori_loop(0, SIDE, grad_one, 0)
    fold_step(2, 1, 2)

    def reduce_group(which, carry):
        put(w_first, which, dot_tn(x_all[:, lanes(which, group)], hidden_two[...]))
        fold_begin(which, 0)
        fold_turn(0, which - 1)
        fold_at(which, 1, (2, 1, 3))
        return carry

    lax.fori_loop(0, groups, reduce_group, 0)

    for kind in range(2):
        row = 3 - kind
        pieces = [
            sums_mine[5, row : row + 1, lanes(core, part)],
            sums_mine[4, row : row + 1, lanes(core, part)],
            sums_mine[3, row : row + 1, lanes(core, half)],
        ]
        whole = jnp.concatenate(pieces, axis=1)
        per_kind = whole.shape[1] // LANES
        for spot in range(per_kind):
            grad_norm_out[kind * per_kind + spot : kind * per_kind + spot + 1, :] = whole[
                :, spot * LANES : (spot + 1) * LANES
            ]
    for turn in range(groups - 1, groups + 2):
        fold_turn(0, turn)
    if gather:
        start = 0
        for slot in range(3):
            rows = fold.counts[slot]
            act_three[kept + start : kept + start + rows, half : half + width] = fold.result(slot)
            start += rows
        leave = pltpu.make_async_copy(
            act_three.at[pl.ds(kept, start), pl.ds(half, width)], grads_out, sem_local.at[3]
        )
        leave.start()
        leave.wait()
        fold.drain()
    else:
        outs = [
            pltpu.make_async_copy(ref, out, sem_local.at[slot])
            for slot, (ref, out) in enumerate(zip((w_first, mid_wide.at[pl.ds(0, 9 * width), :], w_last), grads_out))
        ]
        for copy in outs:
            copy.start()
        for copy in outs:
            copy.wait()
    head_leave.wait()
    for copy in to_mate + head_moves:
        copy.wait_send()


def client_pass(gather, classes, features, labels, flag, params, head, weights):
    pixels, half = features.shape
    images = labels.shape[1]
    count_rows, channels = pixels // 2, 2 * half
    width = params.shape[0] // 2 * LANES - half
    head_rows = classes + -classes % 16
    mine_images = images // 2
    line = SIDE * mine_images
    middle = 9 * width
    blocks = 32
    group = channels // SPOTS[0]
    vmem = pl.BlockSpec(memory_space=pltpu.VMEM)
    smem = pl.BlockSpec(memory_space=pltpu.SMEM)
    spots = SPOTS + (2,)
    scratch = [
        pltpu.VMEM((count_rows, channels), low_type),
        pltpu.VMEM((SPOTS[0] * count_rows, group), low_type),
        pltpu.VMEM(spots + (channels // blocks, width), low_type),
        pltpu.VMEM((middle, width), low_type),
        pltpu.VMEM(spots + (channels // blocks, width), low_type),
        pltpu.VMEM((count_rows, width), wide),
        pltpu.VMEM((count_rows, width), wide),
        pltpu.VMEM((count_rows, channels), wide),
        pltpu.VMEM((count_rows + 2 * line, width), low_type),
        pltpu.VMEM((count_rows + 2 * line, width), low_type),
        pltpu.VMEM((count_rows, width), low_type),
        pltpu.VMEM((count_rows, LANES), wide),
        pltpu.VMEM((2, 2, half + width), wide),
        pltpu.VMEM((2, head_rows, half), low_type),
        pltpu.VMEM((mine_images, channels), wide),
        pltpu.VMEM((mine_images, half), low_type),
        pltpu.VMEM((2, mine_images, half), low_type),
        pltpu.VMEM((2, head_rows, mine_images), low_type),
        pltpu.VMEM((6, 8, channels), wide),
        pltpu.VMEM((6, 8, channels), wide),
        pltpu.VMEM((24, channels), wide),
        pltpu.VMEM((3, 8, channels), wide),
        pltpu.SemaphoreType.DMA((11,)),
        pltpu.SemaphoreType.DMA((2, 6)),
        pltpu.SemaphoreType.DMA((2, 7)),
    ]
    any_space = pl.BlockSpec(memory_space=pl.ANY)
    if gather:
        counts = (channels // blocks, middle // blocks, channels // blocks)
        scratch += [pltpu.SemaphoreType.DMA((2, 3, 3))]
        scratch += [pltpu.SemaphoreType.DMA((2, 4, size)) for size in (6, 8, 6)]
        scratch += [pltpu.VMEM((4, 2, 2, rows, width), low_type) for rows in counts[1:]]
        for lead in ((4, 2), (4,), (4,)):
            scratch += [pltpu.VMEM(lead + (rows, width), low_type) for rows in counts]
        scratch += [pltpu.SemaphoreType.DMA((2, 4, size)) for size in (6, 8, 6, 6)]
        grads_shape = [jax.ShapeDtypeStruct((sum(counts), width), wide)]
        grads_specs = [any_space]
    else:
        grads_shape = [jax.ShapeDtypeStruct(weight.shape, low_type) for weight in weights]
        grads_specs = [any_space] * 3
    return pl.pallas_call(
        functools.partial(client_kernel, gather, images, classes),
        out_shape=grads_shape
        + [
            jax.ShapeDtypeStruct(params.shape, wide),
            jax.ShapeDtypeStruct((classes * half // LANES, LANES), wide),
            jax.ShapeDtypeStruct((8, LANES), wide),
        ],
        in_specs=[any_space, vmem, smem, vmem, vmem] + [any_space] * len(weights),
        out_specs=grads_specs + [vmem, any_space, vmem],
        scratch_shapes=scratch,
        compiler_params=pltpu.CompilerParams(
            collective_id=0, has_side_effects=True, vmem_limit_bytes=VMEM_BYTES
        ),
    )(features, labels, flag, params, head, *weights)


def adam_update(param, grad, first, second, rate, decay):
    first = adam_first * first + (1.0 - adam_first) * grad
    second = adam_second * second + (1.0 - adam_second) * grad * grad
    first_hat = first / (1.0 - adam_first**STEP)
    second_hat = second / (1.0 - adam_second**STEP)
    return (
        param - rate * (first_hat / (jnp.sqrt(second_hat) + adam_epsilon) + decay * param),
        first,
        second,
    )
class GramSum:
    def __init__(self, place, data, total, boxes, sems):
        self.place = place
        self.data = data
        self.total = total
        self.y_box, self.z_box = boxes
        self.sems = sems
        self.share = data.shape[0] // 8
        self.down_order = place.others[::-1] + [place.z]

    def rows(self, z, y):
        return pl.ds(pl.multiple_of((z * 2 + y) * self.share, 8), self.share)

    def copy(self, number, src, dst, to):
        sems = self.sems
        return remote(src, dst, sems.at[0, number], sems.at[1, number], to, self.place.core)

    def y_down(self, turn):
        p = self.place
        src = self.data.at[self.rows(self.down_order[turn], 1 - p.y), :]
        return self.copy(turn, src, self.y_box.at[turn], p.along_y())

    def z_down(self, step):
        p = self.place
        src = self.data.at[self.rows(p.others[step], p.y), :]
        return self.copy(4 + step, src, self.z_box.at[step], p.along_z(step))

    def z_up(self, step):
        p = self.place
        ref = self.total.at[self.rows(p.z, p.y), :]
        return self.copy(7 + step, ref, ref, p.along_z(step))

    def y_up(self, turn):
        p = self.place
        ref = self.total.at[self.rows(([p.z] + p.others)[turn], p.y), :]
        return self.copy(10 + turn, ref, ref, p.along_y())

    def run(self, extra):
        extra = list(extra)
        p = self.place
        for turn in range(4):
            self.y_down(turn).start()
        for turn in range(4):
            self.y_down(turn).wait_recv()
            self.data[self.rows(self.down_order[turn], p.y), :] += self.y_box[turn]
            if turn < 3:
                self.z_down(2 - turn).start()
            if extra:
                extra.pop(0)()
        mine = self.rows(p.z, p.y)
        value = self.data[mine, :]
        for step in (2, 1, 0):
            self.z_down(step).wait_recv()
            value += self.z_box[step]
        self.total[mine, :] = value
        for step in range(3):
            self.z_up(step).start()
        self.y_up(0).start()
        for step in range(3):
            self.z_up(step).wait_recv()
            self.y_up(1 + step).start()
        for turn in range(4):
            self.y_up(turn).wait_recv()

    def drain(self):
        for turn in range(4):
            self.y_down(turn).wait_send()
            self.y_up(turn).wait_send()
        for step in range(3):
            self.z_down(step).wait_send()
            self.z_up(step).wait_send()


class TileSum:
    def __init__(self, place, tiles, boxes, sems):
        self.place = place
        self.tiles = tiles
        self.boxes = boxes
        self.sems = sems

    def copy(self, stage, box):
        p = self.place
        to = (p.client, p.along_x(), p.along_y()) + tuple(p.along_z(step) for step in range(3))
        core = 1 - p.core if box == 0 else p.core
        return remote(
            self.tiles.at[stage], self.boxes.at[box], self.sems.at[0, box], self.sems.at[1, box], to[box], core
        )

    def steps(self):
        def start():
            self.copy(0, 0).start()

        def pair(stage):
            self.copy(stage, stage).wait_recv()
            self.tiles[stage + 1] = self.tiles[stage] + self.boxes[stage]
            if stage < 2:
                self.copy(stage + 1, stage + 1).start()
            else:
                for step in range(3):
                    self.copy(3, 3 + step).start()

        return [start] + [functools.partial(pair, stage) for stage in range(3)]

    def result(self):
        for step in range(3):
            self.copy(3, 3 + step).wait_recv()
        return (self.tiles[3] + self.boxes[3]) + (self.boxes[4] + self.boxes[5])

    def drain(self):
        for stage in range(3):
            self.copy(stage, stage).wait_send()
        for step in range(3):
            self.copy(3, 3 + step).wait_send()


def dot_high(left, right):
    return jnp.dot(left, right, precision=lax.Precision.HIGH, preferred_element_type=wide)


class Share:
    def __init__(self, place, sizes, buffers, sems):
        self.place = place
        self.sizes = sizes
        self.fresh, self.rows_in, self.rows_out, self.back = buffers
        self.sems = sems
        self.bounds = [0, sizes[0], sizes[0] + sizes[1], sum(sizes)]
        p = place
        self.duty = jnp.where(p.x == 1, 1, 2 * p.core)
        self.mine = p.x * 2 + p.core

    def section(self, slot):
        return pl.ds(self.bounds[slot], self.sizes[slot])

    def spot(self, slot, x, core):
        number = x if slot == 1 else x * 2 + core
        return pl.ds(pl.multiple_of(number * self.sizes[slot], 16), self.sizes[slot])

    def doer(self, slot):
        return (0, 0) if slot == 0 else (0, 1) if slot == 2 else (1, self.place.core)

    def out_copy(self, slot):
        p = self.place
        x, core = self.doer(slot)
        return remote(
            self.fresh.at[self.section(slot), :],
            self.rows_in.at[self.spot(slot, p.x, p.core), :],
            self.sems.at[0, slot],
            self.sems.at[1, self.mine],
            p.at(p.z, p.y, x),
            core,
        )

    def in_copy(self, slot, x, core):
        p = self.place
        return remote(
            self.fresh.at[self.section(slot), :],
            self.rows_in.at[self.spot(slot, x, core), :],
            self.sems.at[0, slot],
            self.sems.at[1, x * 2 + core],
            p.at(p.z, p.y, x),
            core,
        )

    def back_copy(self, slot, x, core):
        p = self.place
        return remote(
            self.rows_out.at[self.spot(slot, x, core), :],
            self.back.at[self.section(slot), :],
            self.sems.at[0, 3 + x * 2 + core],
            self.sems.at[1, 4 + slot],
            p.at(p.z, p.y, x),
            core,
        )

    def users(self, slot):
        p = self.place
        if slot == 1:
            return [(0, p.core), (1, p.core)]
        return [(x, core) for x in (0, 1) for core in (0, 1)]

    def send(self):
        for slot in range(3):

            @pl.when(self.duty != slot)
            def _():
                self.out_copy(slot).start()

            @pl.when(self.duty == slot)
            def _():
                self.rows_in[self.spot(slot, self.place.x, self.place.core), :] = self.fresh[self.section(slot), :]

    def gather(self):
        p = self.place
        for slot in range(3):

            @pl.when(self.duty == slot)
            def _():
                for x, core in self.users(slot):

                    @pl.when((p.x != x) | (p.core != core))
                    def _():
                        self.in_copy(slot, x, core).wait_recv()

    def give_back(self):
        p = self.place
        for slot in range(3):

            @pl.when(self.duty == slot)
            def _():
                for x, core in self.users(slot):

                    @pl.when((p.x != x) | (p.core != core))
                    def _():
                        self.back_copy(slot, x, core).start()

                self.back[self.section(slot), :] = self.rows_out[self.spot(slot, p.x, p.core), :]

    def finish(self):
        p = self.place
        for slot in range(3):

            @pl.when(self.duty != slot)
            def _():
                self.back_copy(slot, p.x, p.core).wait_recv()
                self.out_copy(slot).wait_send()

            @pl.when(self.duty == slot)
            def _():
                for x, core in self.users(slot):

                    @pl.when((p.x != x) | (p.core != core))
                    def _():
                        self.back_copy(slot, x, core).wait_send()


def base_kernel(
    ratios,
    sizes,
    master,
    momentum,
    anchor,
    loss_in,
    grads,
    *rest,
):
    place = Place()
    rest = list(rest)

    def take(count):
        taken = rest[:count]
        del rest[:count]
        return taken

    ortho_out, loss_out = take(2)
    gram, gram_total = take(2)
    gram_boxes = take(2)
    (mate_gram,) = take(1)
    grams, fresh, rows_in, rows_out, back, tiles, tile_boxes = take(7)
    gram_sems, tile_sems, share_sems = take(3)

    rows_in[...] = jnp.zeros_like(rows_in)
    place.greet(True, True)
    fresh[...] = momentum_decay * momentum[...] + (grads[...] + prox_weight * (master[...] - anchor[...]))
    share = Share(place, sizes, (fresh, rows_in, rows_out, back), share_sems)
    share.send()
    tiles[0] = loss_in[...]
    tile_sum = TileSum(place, tiles, tile_boxes, tile_sems)
    extra = tile_sum.steps()
    extra.pop(0)()

    width = master.shape[1]
    part = width // 2
    share.gather()
    held = rows_in[...]
    partial = lax.dot_general(
        held, held, (((0,), (0,)), ((), ())), precision=precise, preferred_element_type=wide
    )
    gram[0:part, :] = partial[:part, :part]
    gram[part : 2 * part, :] = partial[:part, part:]
    gram[2 * part :, :] = partial[part:, part:]

    @pl.when(place.x == 1)
    def _():
        swap = remote(gram, mate_gram, share_sems.at[0, 7], share_sems.at[1, 7], place.client, 1 - place.core)
        swap.start()
        swap.wait()
        gram[...] += mate_gram[...]

    gram_sum = GramSum(place, gram, gram_total, gram_boxes, gram_sems)
    gram_sum.run(extra)
    loss_out[...] = tile_sum.result()

    spots = lax.broadcasted_iota(jnp.int32, (part, part), 0)
    diagonal = spots == lax.broadcasted_iota(jnp.int32, (part, part), 1)
    corner, side, end = [gram_total[start * part : (start + 1) * part, :] for start in range(3)]
    trace = jnp.sum(jnp.where(diagonal, corner + end, 0.0))
    factor = 1.0 / (jnp.sqrt(trace) + 1e-07)
    square = factor * factor
    grams[:part, :part] = corner * square
    grams[:part, part:] = side * square
    grams[part:, :part] = side.T * square
    grams[part:, part:] = end * square
    rows_in[...] = rows_in[...] * factor

    def turn(count, carry):
        current = grams[...]
        mixed = schulz_second * current + schulz_third * dot_high(current, current)
        held = rows_in[...]
        rows_in[...] = schulz_first * held + dot_high(held, mixed)

        @pl.when(count < NS_STEPS - 1)
        def _():
            once = schulz_first * current + dot_high(current, mixed)
            grams[...] = schulz_first * once + dot_high(once, mixed)

        return carry

    lax.fori_loop(0, NS_STEPS, turn, 0)
    ratio = jnp.where(share.duty == 1, ratios[1], ratios[0])
    rows_out[...] = (rows_in[...] * ratio).astype(low_type)
    share.give_back()
    share.finish()
    ortho_out[...] = back[...].astype(wide)
    gram_sum.drain()
    tile_sum.drain()


def base_pass(ratios, sizes, master, momentum, anchor, loss_tile, grads):
    rows, width = master.shape
    part = width // 2
    vmem = pl.BlockSpec(memory_space=pltpu.VMEM)
    scratch = [pltpu.VMEM((3 * part, part), wide)] * 2
    scratch += [pltpu.VMEM((count, 3 * part // 8, part), wide) for count in (4, 3)]
    scratch += [pltpu.VMEM((3 * part, part), wide)]
    scratch += [
        pltpu.VMEM((width, width), wide),
        pltpu.VMEM((rows, width), wide),
        pltpu.VMEM((max(4 * sizes[0], 2 * sizes[1]), width), wide),
        pltpu.VMEM((max(4 * sizes[0], 2 * sizes[1]), width), low_type),
        pltpu.VMEM((rows, width), low_type),
        pltpu.VMEM((4, 8, LANES), wide),
        pltpu.VMEM((6, 8, LANES), wide),
        pltpu.SemaphoreType.DMA((2, 14)),
        pltpu.SemaphoreType.DMA((2, 6)),
        pltpu.SemaphoreType.DMA((2, 8)),
    ]
    block = jax.ShapeDtypeStruct((rows, width), wide)
    outs = [block, jax.ShapeDtypeStruct((8, LANES), wide)]
    operands = [master, momentum, anchor, loss_tile, grads]
    return pl.pallas_call(
        functools.partial(base_kernel, ratios, sizes),
        out_shape=outs,
        in_specs=[vmem] * len(operands),
        out_specs=[vmem] * len(outs),
        scratch_shapes=scratch,
        compiler_params=pltpu.CompilerParams(
            collective_id=1, has_side_effects=True, vmem_limit_bytes=VMEM_BYTES
        ),
    )(*operands)


def update_kernel(loss_tile, master, momentum, anchor, grads, ortho, *rest):
    norms, grad_norm, heads, grad_head, outs = rest[0:3], rest[3], rest[4:7], rest[7], rest[8:]
    loss_out, *outs = outs
    loss_out[0] = loss_tile[0, 0]
    loss_out[1] = loss_tile[0, 1]
    momentum_out, base_out, low_out = outs[0:3]
    held = master[...]
    momentum_out[...] = momentum_decay * momentum[...] + (grads[...] + prox_weight * (held - anchor[...]))
    fresh = held - muon_rate * (ortho[...] + muon_decay * held)
    base_out[...] = fresh
    low_out[...] = fresh.astype(low_type)
    for targets, values, grad, rate, decay in (
        (outs[3:6], norms, grad_norm, norm_rate, 0.0),
        (outs[6:9], heads, grad_head, head_rate, head_decay),
    ):
        updates = adam_update(values[0][...], grad[...], values[1][...], values[2][...], rate, decay)
        for target, value in zip(targets, updates):
            target[...] = value


def update_pass(loss_tile, master, momentum, anchor, grads, ortho, norms, grad_norm, heads, grad_head):
    vmem = pl.BlockSpec(memory_space=pltpu.VMEM)
    smem = pl.BlockSpec(memory_space=pltpu.SMEM)
    operands = [loss_tile, master, momentum, anchor, grads, ortho, *norms, grad_norm, *heads, grad_head]
    outs = [(2,), master.shape, master.shape, master.shape] + [grad_norm.shape] * 3 + [grad_head.shape] * 3
    types = [wide, wide, wide, low_type] + [wide] * 6
    return pl.pallas_call(
        update_kernel,
        out_shape=[jax.ShapeDtypeStruct(shape, kind) for shape, kind in zip(outs, types)],
        in_specs=[smem] + [vmem] * (len(operands) - 1),
        out_specs=[smem] + [vmem] * (len(outs) - 1),
        compiler_params=pltpu.CompilerParams(vmem_limit_bytes=VMEM_BYTES),
    )(*operands)


def gram_of(section):
    return lax.dot_general(section, section, (((0,), (0,)), ((), ())), precision=precise)


def square(gram):
    return jnp.dot(gram, gram, precision=precise)


def times_poly(left, mixed):
    return schulz_first * left + jnp.dot(left, mixed, precision=precise)


def schulz(sections):
    raw_grams = lax.psum(tuple(gram_of(section) for section in sections), ("client", "chan"))
    factors = [1.0 / (jnp.sqrt(jnp.trace(gram)) + 1e-07) for gram in raw_grams]
    current = [section * factor for section, factor in zip(sections, factors)]
    grams = [gram * (factor * factor) for gram, factor in zip(raw_grams, factors)]
    for turn in range(NS_STEPS):
        mixed = [schulz_second * gram + schulz_third * square(gram) for gram in grams]
        current = [times_poly(current[slot], mixed[slot]) for slot in range(3)]
        if turn + 1 < NS_STEPS:
            grams = [
                times_poly(times_poly(grams[slot], mixed[slot]), mixed[slot]) for slot in range(3)
            ]
    return current


def base_far(ratios, bounds, master, momentum, anchor, loss_tile, grads):
    sums = [
        lax.psum_scatter(flat_rows(grad).astype(wide), ("client", "chan"), scatter_dimension=0, tiled=True)
        for grad in grads
    ]
    grad_base = jnp.concatenate(sums, axis=0)
    momentum_new = momentum_decay * momentum + (grad_base + prox_weight * (master - anchor))
    current = schulz([momentum_new[bounds[slot] : bounds[slot + 1]] for slot in range(3)])
    ortho = jnp.concatenate([current[slot] * ratios[slot] for slot in range(3)], axis=0)
    return grad_base, ortho, lax.psum(loss_tile, ("client", "chan"))


def as_stored(rows, shape):
    return with_layout_constraint(rows.reshape(shape), Layout(major_to_minor=tuple(range(len(shape)))))


def on_device(
    features,
    labels,
    mask,
    base_master,
    base_momentum,
    global_base,
    norm_params,
    norm_first,
    norm_second,
    head,
    head_first,
    head_second,
):
    halves = lax.axis_size("chan")
    blocks = lax.axis_size("client") * halves
    half = features.shape[2]
    width = base_master.shape[2]
    channels = half * halves
    classes = head.shape[2]
    rows_first = channels // blocks
    rows_mid = 9 * width // blocks
    sizes = (rows_first, rows_mid, rows_first)
    bounds = (0, rows_first, rows_first + rows_mid, base_master.shape[1])
    ratio = (channels / width) ** 0.5
    ratios = (ratio, 3.0, ratio)
    master, momentum, anchor = base_master[0], base_momentum[0], global_base[0]
    norms = [value.reshape(-1, LANES) for value in (norm_params, norm_first, norm_second)]
    heads = [jnp.transpose(value, (2, 0, 1)).reshape(-1, LANES) for value in (head, head_first, head_second)]
    near = lax.axis_size("client") == SPOTS[0] * SPOTS[1] * SPOTS[2]
    if near:
        weights = [master]
    else:
        low_master = master.astype(low_type)
        weights = [
            lax.all_gather(low_master[bounds[slot] : bounds[slot + 1]], ("client", "chan"), axis=0, tiled=True)
            for slot in range(3)
        ]
        split = SPOTS + (2, channels // 32, width)
        weights = [weights[0].reshape(split), weights[1], weights[2].reshape(split)]
    *grads, grad_norm, grad_head, loss_tile = client_pass(
        near, classes, features[0], labels, mask, norms[0], heads[0], weights
    )
    if near:
        (grad_base,) = grads
        ortho, loss_tile = base_pass(ratios, sizes, master, momentum, anchor, loss_tile, grad_base)
    else:
        grad_base, ortho, loss_tile = base_far(ratios, bounds, master, momentum, anchor, loss_tile, grads)
    loss, momentum_new, base_new, base_low, *fresh = update_pass(
        loss_tile, master, momentum, anchor, grad_base, ortho, norms, grad_norm, heads, grad_head
    )
    fresh_norms = [as_stored(value, norm_params.shape) for value in fresh[:3]]
    fresh_heads = [jnp.transpose(as_stored(value, (classes, 1, half)), (1, 2, 0)) for value in fresh[3:]]
    return (
        loss,
        base_new[None],
        momentum_new[None],
        base_low[None],
        *fresh_norms,
        *fresh_heads,
    )


def solution(mesh):
    wide_block = P(("client", "chan"), None, None)
    norm_block = P("client", None, "chan", None)
    head_block = P("client", "chan", None)
    return jax.shard_map(
        on_device,
        mesh=mesh,
        in_specs=(P("client", None, "chan"), P("client", None), P("client"))
        + (wide_block,) * 3
        + (norm_block,) * 3
        + (head_block,) * 3,
        out_specs=(P(),) + (wide_block,) * 3 + (norm_block,) * 3 + (head_block,) * 3,
        check_vma=False,
    )
```

```python
import functools

import jax
import jax.numpy as jnp
from jax import lax
from jax.experimental import pallas as pl
from jax.experimental.layout import Layout, with_layout_constraint
from jax.experimental.pallas import tpu as pltpu
from jax.sharding import PartitionSpec as P

NS_STEPS = 5
STEP = 10

low_type = jnp.bfloat16
wide = jnp.float32
MESH = pl.DeviceIdType.MESH
precise = lax.Precision.HIGHEST
norm_epsilon = 1e-05
prox_weight = 0.05
momentum_decay = 0.95
muon_rate = 0.3
muon_decay = 0.1
schulz_first = 3.4445
schulz_second = -4.775
schulz_third = 2.0315
adam_first = 0.9
adam_second = 0.95
adam_epsilon = 1e-08
head_rate = 0.01
head_decay = 0.05
norm_rate = 0.5

SIDE = 7
PIXELS = SIDE * SIDE
LANES = 128
SPOTS = (4, 2, 2)
CUTS = 4
VMEM_BYTES = 62 * 2**20


def dot_nn(left, right):
    return jnp.dot(left, right, preferred_element_type=wide)


def dot_nt(left, right):
    return lax.dot_general(left, right, (((1,), (1,)), ((), ())), preferred_element_type=wide)


def dot_tn(left, right):
    return lax.dot_general(left, right, (((0,), (0,)), ((), ())), preferred_element_type=wide)


def flat_rows(block):
    return block.reshape(-1, block.shape[-1])


def sigmoid(value):
    return 0.5 * jnp.tanh(0.5 * value) + 0.5


def fold_rows(value):
    return jnp.sum(value.reshape(value.shape[0] // 8, 8, value.shape[1]), axis=0)


def column_sum(value):
    return jnp.sum(value, axis=0, keepdims=True)


def remote(src, dst, send_sem, recv_sem, client, core):
    return pltpu.make_async_remote_copy(
        src_ref=src,
        dst_ref=dst,
        send_sem=send_sem,
        recv_sem=recv_sem,
        device_id=(client, core),
        device_id_type=MESH,
    )


class Place:
    def __init__(self):
        self.client = lax.axis_index("client")
        self.core = lax.axis_index("chan")
        self.z = self.client // 4
        self.y = (self.client // 2) % 2
        self.x = self.client % 2
        self.others = [
            self.z + 1 - 2 * (self.z % 2),
            (self.z + 2) % 4,
            3 - self.z,
        ]

    def at(self, z, y, x):
        return z * 4 + y * 2 + x

    def along_x(self):
        return self.at(self.z, self.y, 1 - self.x)

    def along_y(self):
        return self.at(self.z, 1 - self.y, self.x)

    def along_z(self, step):
        return self.at(self.others[step], self.y, self.x)

    def greet(self, whole, across=False):
        barrier = pltpu.get_barrier_semaphore()
        pairs = [(self.client, 1 - self.core)]
        if whole:
            pairs += [(self.along_x(), self.core), (self.along_y(), self.core)]
            pairs += [(self.along_z(step), self.core) for step in range(3)]
        if across:
            pairs += [(self.along_x(), 1 - self.core)]
        for pair in pairs:
            pl.semaphore_signal(barrier, inc=1, device_id=pair, device_id_type=MESH)
        pl.semaphore_wait(barrier, len(pairs))


def cut_rows(counts):
    pieces = []
    for slot, rows in enumerate(counts):
        middle = (rows // 16 + 1) // 2 * 16
        pieces.append((slot, 0, middle, 0))
        pieces.append((slot, middle, rows - middle, 1))
    return pieces


def block_ref(ref, size, z, y, x, core, start, count):
    if len(ref.shape) == 2:
        first = (((z * 2 + y) * 2 + x) * 2 + core) * size + start
        return ref.at[pl.ds(pl.multiple_of(first, 16), count), :]
    return ref.at[z, y, x, core, pl.ds(start, count), :]


class Spread:
    def __init__(self, place, weights, counts, sems):
        self.place = place
        self.weights = weights
        self.counts = counts
        self.pieces = cut_rows(counts)
        self.z_sems, self.near_sems, self.far_sems, self.core_sems = sems
        self.order = [place.z] + place.others

    def z_copy(self, step, slot):
        p = self.place
        ref = block_ref(self.weights[slot], self.counts[slot], p.z, p.y, p.x, p.core, 0, self.counts[slot])
        sems = self.z_sems
        return remote(ref, ref, sems.at[0, step, slot], sems.at[1, step, slot], p.along_z(step), p.core)

    def near_copy(self, turn, number):
        p = self.place
        slot, start, count, way = self.pieces[number]
        ref = block_ref(self.weights[slot], self.counts[slot], self.order[turn], p.y, p.x, p.core, start, count)
        sems = self.near_sems
        return remote(
            ref, ref, sems.at[0, turn, number], sems.at[1, turn, number], (p.along_x, p.along_y)[way](), p.core
        )

    def far_copies(self, turn, number):
        p = self.place
        slot, start, count, way = self.pieces[number]
        spot = self.order[turn]
        sems = self.far_sems
        copies = []
        for part, other in enumerate((0, 1) if slot == 1 else (slice(None),)):
            y, x = (p.y, other) if way == 0 else (other, p.x)
            ref = block_ref(self.weights[slot], self.counts[slot], spot, y, x, p.core, start, count)
            sem = number + 4 * part
            to = (p.along_y, p.along_x)[way]()
            copies.append(remote(ref, ref, sems.at[0, turn, sem], sems.at[1, turn, sem], to, p.core))
        return copies

    def core_copies(self, turn, slot):
        p = self.place
        sems = self.core_sems
        copies = []
        pairs = [(y, x) for y in (0, 1) for x in (0, 1)] if slot == 1 else [(slice(None), slice(None))]
        for part, (y, x) in enumerate(pairs):
            ref = block_ref(self.weights[slot], self.counts[slot], self.order[turn], y, x, p.core, 0, self.counts[slot])
            sem = (0, 2 + part, 1)[slot]
            copies.append(remote(ref, ref, sems.at[0, turn, sem], sems.at[1, turn, sem], p.client, 1 - p.core))
        return copies

    def fill(self, master):
        p = self.place
        start = 0
        for slot in range(3):
            rows = self.counts[slot]
            own = block_ref(self.weights[slot], self.counts[slot], p.z, p.y, p.x, p.core, 0, rows)
            own[...] = master[start : start + rows, :].astype(low_type)
            start += rows

    def begin(self):
        for step in range(3):
            self.z_copy(step, 0).start()
        self.near_start(0)

    def near_start(self, slot):
        for number in (2 * slot, 2 * slot + 1):
            self.near_copy(0, number).start()

    def steps(self):
        near, far, core, start = self.near_step, self.far_step, self.core_step, self.near_start
        groups = [
            [(far, 0, 0), (start, 1)],
            [(near, 1, 0)],
            [(near, 2, 0), (near, 3, 0)],
            [(far, 1, 0), (core, 0, 0), (far, 0, 1)],
            [(far, 2, 0), (far, 3, 0), (core, 1, 0)],
            [(core, 2, 0), (core, 3, 0), (near, 1, 1), (start, 2)],
            [(core, 0, 1), (near, 2, 1)],
            [(far, 1, 1), (near, 3, 1)],
            [(core, 1, 1), (far, 2, 1), (far, 0, 2)],
            [(far, 3, 1), (core, 2, 1), (near, 1, 2)],
            [(core, 3, 1), (core, 0, 2), (near, 2, 2)],
            [(far, 1, 2), (near, 3, 2)],
            [(core, 1, 2), (far, 2, 2)],
            [(far, 3, 2), (core, 2, 2)],
            [(core, 3, 2)],
        ]
        return [[functools.partial(*step) for step in group] for group in groups]

    def near_step(self, turn, slot):
        self.z_copy(turn - 1, slot).wait_recv()
        for number in (2 * slot, 2 * slot + 1):
            self.near_copy(turn, number).start()
        if slot < 2:
            self.z_copy(turn - 1, slot + 1).start()

    def far_step(self, turn, slot):
        for number in (2 * slot, 2 * slot + 1):
            self.near_copy(turn, number).wait_recv()
            for copy in self.far_copies(turn, number):
                copy.start()

    def core_step(self, turn, slot):
        for number in (2 * slot, 2 * slot + 1):
            for copy in self.far_copies(turn, number):
                copy.wait_recv()
        for copy in self.core_copies(turn, slot):
            copy.start()

    def arrive(self, slot):
        for turn in range(4):
            for copy in self.core_copies(turn, slot):
                copy.wait_recv()

    def drain(self):
        for slot in range(3):
            for step in range(3):
                self.z_copy(step, slot).wait_send()
            for turn in range(4):
                for copy in self.core_copies(turn, slot):
                    copy.wait_send()
        for number in range(6):
            for turn in range(4):
                self.near_copy(turn, number).wait_send()
                for copy in self.far_copies(turn, number):
                    copy.wait_send()


class Fold:
    def __init__(self, place, grads, counts, parts):
        self.place = place
        self.grads = grads
        self.counts = counts
        self.pieces = cut_rows(counts)
        self.core_boxes = [parts[1], parts[0], parts[1]]
        self.near_boxes, self.far_boxes, self.z_boxes = [parts[3 * k + 2 : 3 * k + 5] for k in range(3)]
        self.core_sems, self.near_sems, self.far_sems, self.z_sems = parts[11:]

    def core_copies(self, which, slot):
        p = self.place
        sems = self.core_sems
        copies = []
        pairs = [(y, x) for y in (0, 1) for x in (0, 1)] if slot == 1 else [(slice(None), slice(None))]
        for part, (y, x) in enumerate(pairs):
            ref = block_ref(self.grads[slot], self.counts[slot], which, y, x, 1 - p.core, 0, self.counts[slot])
            box = self.core_boxes[slot].at[which, y, x]
            sem = (0, 2 + part, 1)[slot]
            copies.append(remote(ref, box, sems.at[0, which, sem], sems.at[1, which, sem], p.client, 1 - p.core))
        return copies

    def near_copies(self, which, number):
        p = self.place
        slot, start, count, way = self.pieces[number]
        sems = self.near_sems
        copies = []
        for part, other in enumerate((0, 1) if slot == 1 else (slice(None),)):
            y, x = (other, 1 - p.x) if way == 0 else (1 - p.y, other)
            ref = block_ref(self.grads[slot], self.counts[slot], which, y, x, p.core, start, count)
            box = self.near_boxes[slot].at[which, other, pl.ds(start, count), :]
            sem = number + 4 * part
            to = (p.along_x, p.along_y)[way]()
            copies.append(remote(ref, box, sems.at[0, which, sem], sems.at[1, which, sem], to, p.core))
        return copies

    def far_copy(self, which, number):
        p = self.place
        slot, start, count, way = self.pieces[number]
        y, x = (1 - p.y, p.x) if way == 0 else (p.y, 1 - p.x)
        ref = block_ref(self.grads[slot], self.counts[slot], which, y, x, p.core, start, count)
        box = self.far_boxes[slot].at[which, pl.ds(start, count), :]
        sems = self.far_sems
        return remote(
            ref, box, sems.at[0, which, number], sems.at[1, which, number], (p.along_y, p.along_x)[way](), p.core
        )

    def z_copy(self, which, sender, number):
        p = self.place
        slot, start, count, _ = self.pieces[number]
        rows = pl.ds(start, count)
        sems = self.z_sems
        return remote(
            block_ref(self.grads[slot], self.counts[slot], which, p.y, p.x, p.core, start, count),
            self.z_boxes[slot].at[sender, rows, :],
            sems.at[0, which, number],
            sems.at[1, sender, number],
            p.at(which, p.y, p.x),
            p.core,
        )

    def begin(self, which, slot):
        for copy in self.core_copies(which, slot):
            copy.start()

    def add(self, slot, spots, start, count, box):
        ref = block_ref(self.grads[slot], self.counts[slot], *spots, self.place.core, start, count)
        ref[...] = (ref[...].astype(wide) + box.astype(wide)).astype(low_type)

    def core_step(self, which, slot):
        for copy in self.core_copies(which, slot):
            copy.wait_recv()
        pairs = [(y, x) for y in (0, 1) for x in (0, 1)] if slot == 1 else [(slice(None), slice(None))]
        for y, x in pairs:
            self.add(slot, (which, y, x), 0, self.counts[slot], self.core_boxes[slot][which, y, x])
        for number in (2 * slot, 2 * slot + 1):
            for copy in self.near_copies(which, number):
                copy.start()

    def near_step(self, which, slot):
        p = self.place
        for number in (2 * slot, 2 * slot + 1):
            _, start, count, way = self.pieces[number]
            for copy in self.near_copies(which, number):
                copy.wait_recv()
            for other in (0, 1) if slot == 1 else (slice(None),):
                y, x = (other, p.x) if way == 0 else (p.y, other)
                box = self.near_boxes[slot][which, other, pl.ds(start, count), :]
                self.add(slot, (which, y, x), start, count, box)
            self.far_copy(which, number).start()

    def far_step(self, which, slot):
        p = self.place
        for number in (2 * slot, 2 * slot + 1):
            _, start, count, way = self.pieces[number]
            self.far_copy(which, number).wait_recv()
            box = self.far_boxes[slot][which, pl.ds(start, count), :]
            self.add(slot, (which, p.y, p.x), start, count, box)

            @pl.when(p.z != which)
            def _():
                self.z_copy(which, p.z, number).start()

    def result(self, slot):
        p = self.place
        self.z_boxes[slot][p.z] = block_ref(self.grads[slot], self.counts[slot], p.z, p.y, p.x, p.core, 0, self.counts[slot])[...]
        for sender in range(4):

            @pl.when(p.z != sender)
            def _():
                for number in (2 * slot, 2 * slot + 1):
                    self.z_copy(sender, sender, number).wait_recv()

        total = self.z_boxes[slot][0].astype(wide)
        for sender in range(1, 4):
            total += self.z_boxes[slot][sender].astype(wide)
        return total

    def drain(self):
        for which in range(4):
            for slot in range(3):
                for copy in self.core_copies(which, slot):
                    copy.wait_send()
            for number in range(6):
                for copy in self.near_copies(which, number):
                    copy.wait_send()
                self.far_copy(which, number).wait_send()

            @pl.when(self.place.z != which)
            def _():
                for number in range(6):
                    self.z_copy(which, self.place.z, number).wait_send()


def norm_stats(mine, theirs, count):
    gap = mine[0:1] - theirs[0:1]
    mean = 0.5 * (mine[0:1] + theirs[0:1])
    spread = mine[1:2] + theirs[1:2] + gap * gap * (0.5 * count)
    return mean, lax.rsqrt(spread / (2.0 * count) + norm_epsilon)


def client_kernel(
    gather,
    images,
    classes,
    features,
    labels,
    flag,
    params,
    head,
    *rest,
):
    if gather:
        master, *rest = rest
    else:
        first_in, middle_in, last_in, *rest = rest
    if gather:
        grads_out, *rest = rest
    else:
        grads_out, rest = rest[:3], rest[3:]
    (
        grad_norm_out,
        grad_head_out,
        loss_out,
        x_all,
        mid_wide,
        w_first,
        w_middle,
        w_last,
        act_one,
        act_two,
        act_three,
        taps_one,
        taps_two,
        hidden_two,
        stage,
        params_all,
        head_all,
        grad_pool,
        pool_send,
        pool_all,
        logit_grads,
        sums_mine,
        sums_theirs,
        shift,
        fwd_stats,
        sem_local,
        sem_swap,
        sem_misc,
        *near_parts,
    ) = rest
    place = Place()
    core = place.core
    mate = (place.client, 1 - core)
    count_rows, channels = x_all.shape
    half = channels // 2
    width = act_one.shape[1]
    part = width // 2
    mine_images = images // 2
    line = SIDE * mine_images
    total_rows = 2.0 * count_rows

    def tile(index):
        return pl.ds(pl.multiple_of(index * line, line), line)

    def lanes(index, size):
        return pl.ds(pl.multiple_of(index * size, size), size)

    weights = (w_first, w_middle, w_last)
    if gather:
        held = act_three.at[pl.ds(0, master.shape[0]), pl.ds(0, width)]
        load = pltpu.make_async_copy(master, held, sem_local.at[8])
        load.start()
        counts = [channels // 32, 9 * width // 32, channels // 32]
        spread = Spread(place, weights, counts, near_parts[:4])
        fold = Fold(place, (w_first, mid_wide, w_last), counts, near_parts[4:])
        due = spread.steps()
        load.wait()
        spread.fill(held)
        place.greet(True)
        spread.begin()
    else:
        place.greet(False)
        loads = [
            pltpu.make_async_copy(src, dst, sem_local.at[8 + slot])
            for slot, (src, dst) in enumerate(zip((first_in, middle_in, last_in), weights))
        ]
        for load in loads:
            load.start()
        due = []

    quarter = half // 2
    own_rows = pl.ds(pl.multiple_of(core * count_rows, count_rows), count_rows)
    mate_rows = pl.ds(pl.multiple_of((1 - core) * count_rows, count_rows), count_rows)
    top_rows = pl.ds(0, count_rows)
    own_copies = [
        pltpu.make_async_copy(
            features.at[own_rows, pl.ds(side * quarter, quarter)], buffer, sem_local.at[side]
        )
        for side, buffer in enumerate((hidden_two, mid_wide.at[top_rows, :]))
    ]
    per_kind = params.shape[0] // 2
    for kind in range(2):
        rows = [params[kind * per_kind + spot : kind * per_kind + spot + 1, :] for spot in range(per_kind)]
        params_all[core, kind : kind + 1, :] = jnp.concatenate(rows, axis=1)
    head_all[core] = jnp.zeros(head_all.shape[1:], low_type)
    for spot in range(half // LANES):
        head_all[core, 0:classes, spot * LANES : (spot + 1) * LANES] = head[
            pl.ds(spot, classes, stride=half // LANES), :
        ].astype(low_type)
    to_mate = [
        remote(params_all.at[core], params_all.at[core], sem_misc.at[0, 0], sem_misc.at[1, 0], *mate),
        remote(head_all.at[core], head_all.at[core], sem_misc.at[0, 1], sem_misc.at[1, 1], *mate),
    ]
    for side, buffer in enumerate((taps_one, taps_two)):
        to_mate.append(
            remote(
                features.at[mate_rows, pl.ds(side * quarter, quarter)],
                buffer.at[top_rows, :],
                sem_misc.at[0, 5 + side],
                sem_misc.at[1, 5 + side],
                *mate,
            )
        )
    for copy in to_mate + own_copies:
        copy.start()

    def advance(count):
        for group in due[:count]:
            for step in group:
                step()
        del due[:count]

    def advance_at(index, spots):
        for spot, group in zip(spots, due):

            @pl.when(index == spot)
            def _():
                for step in group:
                    step()

    def arrive(slot, left):
        if gather:
            advance(len(due) - left)
            spread.arrive(slot)
        else:
            loads[slot].wait()

    def arrive_turns(slot, turns):
        if gather:
            for turn in turns:
                for copy in spread.core_copies(turn, slot):
                    copy.wait_recv()

    def fold_step(kind, slot, which):
        if gather:
            (fold.core_step, fold.near_step, fold.far_step)[kind](which, slot)

    def fold_at(index, spot, *steps):
        @pl.when(index == spot)
        def _():
            for step in steps:
                fold_step(*step)

    def fold_begin(which, slot):
        if gather:
            fold.begin(which, slot)

    def zero_edges(buffer):
        edge = jnp.zeros((line,) + buffer.shape[1:], low_type)
        buffer[0:line, :] = edge
        buffer[line + count_rows : 2 * line + count_rows, :] = edge

    advance(3)
    for copy in own_copies:
        copy.wait()

    def turn_from(source, base):
        def turn(index, carry):
            stage[...] = source(lanes(index, LANES)).astype(wide)

            def pixel(spot, inner):
                x_all[
                    pl.ds(pl.multiple_of(spot * mine_images, mine_images), mine_images),
                    pl.ds(pl.multiple_of(base + index * LANES, LANES), LANES),
                ] = stage[pl.ds(spot, mine_images, stride=PIXELS), :].astype(low_type)
                return inner

            return lax.fori_loop(0, PIXELS, pixel, carry, unroll=7)

        return turn

    quarters = quarter // LANES
    own_base, mate_base = core * half, (1 - core) * half
    lax.fori_loop(0, quarters, turn_from(lambda columns: hidden_two[:, columns], own_base), 0)
    advance(1)
    lax.fori_loop(
        0,
        quarters,
        turn_from(lambda columns: mid_wide[0:count_rows, columns], own_base + quarter),
        0,
    )
    advance(1)
    for copy in to_mate:
        copy.wait_recv()
    lax.fori_loop(0, quarters, turn_from(lambda columns: taps_one[0:count_rows, columns], mate_base), 0)
    advance(1)
    lax.fori_loop(0, quarters, turn_from(lambda columns: taps_two[0:count_rows, columns], mate_base + quarter), 0)
    zero_edges(taps_one)
    zero_edges(taps_two)
    arrive(0, 9)

    def swap(slot, size):
        return remote(
            sums_mine.at[slot, :, pl.ds(0, size)],
            sums_theirs.at[slot, :, pl.ds(0, size)],
            sem_swap.at[0, slot],
            sem_swap.at[1, slot],
            *mate,
        )

    def gain_bias(lower, upper):
        rows = []
        for kind in range(2):
            pieces = [params_all[side, kind : kind + 1, lower:upper] for side in range(2)]
            rows.append(jnp.concatenate(pieces, axis=1))
        return rows

    def collect(index, value, columns, size):
        @pl.when(index == 0)
        def _():
            shift[0:1, pl.ds(0, size)] = column_sum(fold_rows(value)) / value.shape[0]
            shift[8:24, pl.ds(0, size)] = jnp.zeros((16, size), wide)

        gap = value - shift[0:1, pl.ds(0, size)]
        shift[8:16, pl.ds(0, size)] += fold_rows(gap)
        shift[16:24, pl.ds(0, size)] += fold_rows(gap * gap)

    def close_stats(slot, columns, size):
        sum_gap = column_sum(shift[8:16, pl.ds(0, size)])
        sum_square = column_sum(shift[16:24, pl.ds(0, size)])
        sums_mine[slot, 0:1, columns] = shift[0:1, pl.ds(0, size)] + sum_gap / count_rows
        sums_mine[slot, 1:2, columns] = sum_square - sum_gap * sum_gap / count_rows

    def look_over(act, columns):
        def look(index, carry):
            collect(index, act[tile(index), columns], None, width)
            return carry

        lax.fori_loop(0, SIDE, look, 0)

    groups = SPOTS[0]
    group = channels // groups

    def settle(slot, size):
        mean, scale = norm_stats(
            sums_mine[slot, 0:2, pl.ds(0, size)], sums_theirs[slot, 0:2, pl.ds(0, size)], float(count_rows)
        )
        fwd_stats[slot, 0:1, pl.ds(0, size)] = mean
        fwd_stats[slot, 1:2, pl.ds(0, size)] = scale

    whole_width = pl.ds(0, width)

    def first_part(index, carry):
        act_one[...] += dot_nn(x_all[:, lanes(index, group)], flat_rows(w_first[index]))
        advance_at(index, (0, 1, 2))
        return carry

    act_one[...] = jnp.zeros_like(act_one)
    lax.fori_loop(0, groups, first_part, 0)
    del due[:3]
    look_over(act_one, whole_width)
    close_stats(0, whole_width, width)
    move = swap(0, width)
    move.start()
    advance(1)
    move.wait()
    settle(0, width)

    gain_one, bias_one = gain_bias(0, part)
    gain_two, bias_two = gain_bias(part, width)
    gain_three, bias_three = gain_bias(width, width + half)

    def normal(act, slot, index):
        mean = fwd_stats[slot, 0:1, pl.ds(0, width)]
        return (act[tile(index), :] - mean) * fwd_stats[slot, 1:2, pl.ds(0, width)]

    def hide_one(index, carry):
        value = normal(act_one, 0, index) * gain_one + bias_one
        taps_one[pl.ds(pl.multiple_of((index + 1) * line, line), line), :] = (value * sigmoid(value)).astype(low_type)
        return carry

    lax.fori_loop(0, SIDE, hide_one, 0)
    if gather:
        arrive_turns(1, (0, 1))
    else:
        arrive(1, 0)

    step = mine_images
    piece = width // 2

    def row_windows(buffer, down, start, reach):
        if reach == line:
            return buffer[pl.ds(pl.multiple_of(down * line, line), count_rows), :]
        windows = [
            buffer[pl.ds(pl.multiple_of((down + row) * line + start, step), reach), :] for row in range(SIDE)
        ]
        return jnp.concatenate(windows, axis=0)

    def add_windows(target, columns, value, start, reach):
        for row in range(SIDE):
            rows = slice(row * line + start, row * line + start + reach)
            target[rows, columns] += value[row * reach : (row + 1) * reach]

    low_start, high_start, reaches = (0, 0, step), (step, 0, 0), (line - step, line, line - step)

    early, taps = 4, 9

    def second_part(index, carry):
        tap = jnp.where(place.z < 2, index, (index + taps - early) % taps) if gather else index

        @pl.when(index == early)
        def _():
            arrive_turns(1, (2, 3))

        down = tap // 3
        for over in range(3):

            @pl.when(tap % 3 == over)
            def _():
                left = row_windows(taps_one, down, low_start[over], reaches[over])
                kernel = w_middle[pl.ds(pl.multiple_of(tap * width, width), width), :]
                add_windows(act_two, slice(None), dot_nn(left, kernel), high_start[over], reaches[over])

        advance_at(index, (2, 5, 6, 8))
        return carry

    act_two[...] = jnp.zeros_like(act_two)
    lax.fori_loop(0, taps, second_part, 0)
    del due[:4]
    look_over(act_two, whole_width)
    close_stats(1, whole_width, width)
    move_two = swap(1, width)
    move_two.start()
    move_two.wait()
    settle(1, width)

    arrive(2, 0)

    def third_line(index, carry):
        value = normal(act_two, 1, index) * gain_two + bias_two
        hidden = (value * sigmoid(value)).astype(low_type)
        hidden_two[tile(index), :] = hidden
        value = dot_nt(hidden, flat_rows(w_last[...]))
        act_three[tile(index), :] = value
        start = jnp.where(index == 0, column_sum(value[0:8]) / 8.0, shift[0:1, :])
        gap = value - start
        kept_sums = jnp.where(index == 0, 0.0, shift[8:24, :])
        shift[0:1, :] = start
        shift[8:16, :] = kept_sums[0:8] + fold_rows(gap)
        shift[16:24, :] = kept_sums[8:16] + fold_rows(gap * gap)
        return carry

    lax.fori_loop(0, SIDE, third_line, 0)
    close_stats(2, pl.ds(0, channels), channels)
    move_three = swap(2, channels)
    move_three.start()
    move_three.wait()
    settle(2, channels)

    per_group = group // LANES

    def block_of(spot):
        return pl.ds(pl.multiple_of(spot * mine_images, mine_images), mine_images)

    def mid_line(which, index):
        return pl.ds(pl.multiple_of(which * count_rows + index * line, line), line)

    kept = channels // LANES * mine_images

    def gathered(kind):
        starts = range(kind * kept, (kind + 1) * kept, mine_images)
        return jnp.concatenate([stage[start : start + mine_images, :] for start in starts], axis=1)

    fwd_stats[2, 4:5, :] = fwd_stats[2, 1:2, :] * gain_three
    fwd_stats[2, 5:6, :] = bias_three - fwd_stats[2, 0:1, :] * fwd_stats[2, 4:5, :]

    def emit(index, carry):
        columns = lanes(index, LANES)
        slant, level = fwd_stats[2, 4:5, columns], fwd_stats[2, 5:6, columns]

        def pixels(row, sums):
            pooled, steeps, steeps_act = sums
            found = []
            for spot in range(SIDE):
                where = block_of(row * SIDE + spot)
                act = act_three[where, columns]
                half_total = 0.5 * (act * slant + level + x_all[where, columns].astype(wide))
                rise = 1.0 + jnp.tanh(half_total)
                out = half_total * rise
                steep = rise + out * (2.0 - rise)
                found.append(steep.astype(low_type))
                pooled, steeps, steeps_act = pooled + out, steeps + steep, steeps_act + steep * act
            mid_wide[mid_line(index // per_group, row), lanes(index % per_group, LANES)] = jnp.concatenate(
                found, axis=0
            )
            return pooled, steeps, steeps_act

        zero = jnp.zeros((mine_images, LANES), wide)
        sums = lax.fori_loop(0, SIDE, pixels, (zero, zero, zero))
        for kind, value in enumerate(sums):
            stage[pl.ds(pl.multiple_of(kind * kept + index * mine_images, mine_images), mine_images), :] = value
        return carry

    lax.fori_loop(0, channels // LANES, emit, 0)

    pooled = (gathered(0) / PIXELS).astype(low_type)
    head_full = jnp.concatenate([head_all[0], head_all[1]], axis=1)
    logits = dot_nt(head_full, pooled)
    spots = lax.broadcasted_iota(jnp.int32, logits.shape, 0)
    inside = spots < classes
    first_labels, second_labels = labels[0:1, 0:mine_images], labels[0:1, mine_images:]
    onehot = (spots == jnp.where(core == 0, first_labels, second_labels)).astype(wide)
    top = jnp.max(jnp.where(inside, logits, -jnp.inf), axis=0, keepdims=True)
    powers = jnp.where(inside, jnp.exp(logits - top), 0.0)
    power_sum = jnp.sum(powers, axis=0, keepdims=True)
    picked = jnp.sum(logits * onehot, axis=0, keepdims=True)
    each_loss = top + jnp.log(power_sum) - picked
    taking = flag[0].astype(wide)
    tile_spots = lax.broadcasted_iota(jnp.int32, loss_out.shape, 1)
    loss_out[...] = jnp.where(tile_spots == 0, taking * jnp.sum(each_loss), taking * mine_images)
    grads = (taking / images * (powers / power_sum - onehot)).astype(low_type)
    grad_pool[...] = dot_tn(grads, head_full) * (0.5 / PIXELS)
    logit_grads[core] = grads
    pool_all[core] = pooled[:, 0:half]
    pool_send[...] = pooled[:, half:]

    @pl.when(core == 1)
    def _():
        pool_all[core] = pooled[:, half:]
        pool_send[...] = pooled[:, 0:half]

    head_moves = [
        remote(pool_send, pool_all.at[core], sem_misc.at[0, 3], sem_misc.at[1, 3], *mate),
        remote(logit_grads.at[core], logit_grads.at[core], sem_misc.at[0, 4], sem_misc.at[1, 4], *mate),
    ]

    steeps = gathered(1)
    steeps_normed = (gathered(2) - fwd_stats[2, 0:1, :] * steeps) * fwd_stats[2, 1:2, :]
    sums_mine[3, 0:1, :] = column_sum(grad_pool[...] * steeps)
    sums_mine[3, 1:2, :] = column_sum(grad_pool[...] * steeps_normed)
    move_back = swap(3, channels)
    move_back.start()
    for copy in head_moves:
        copy.start()
    move_back.wait()

    def back_terms(slot, layer, size, gain):
        columns = pl.ds(0, size)
        sums = sums_mine[slot, 0:2, columns] + sums_theirs[slot, 0:2, columns]
        sums_mine[slot, 2:4, columns] = sums
        scale = fwd_stats[layer, 1:2, columns]
        return (
            scale * gain,
            scale * gain * sums[0:1] / total_rows,
            scale * scale * gain * sums[1:2] / total_rows,
        )

    first, second, third = back_terms(3, 2, channels, gain_three)
    fwd_stats[2, 4:5, :] = second - third * fwd_stats[2, 0:1, :]
    fwd_stats[2, 5:6, :] = third
    grad_pool[...] = grad_pool[...] * first

    def pull(index):
        for which in range(groups):
            columns = slice(which * group, (which + 1) * group)
            reach = grad_pool[:, columns]
            steep = mid_wide[mid_line(which, index), :].astype(wide)
            value = jnp.concatenate([reach] * SIDE, axis=0) * steep
            value = value - fwd_stats[2, 4:5, columns] - fwd_stats[2, 5:6, columns] * act_three[tile(index), columns]
            mid_wide[mid_line(which, index), :] = value.astype(low_type)

    pull(0)
    for copy in head_moves:
        copy.wait_recv()
    head_grad = dot_nn(logit_grads[0], pool_all[0]) + dot_nn(logit_grads[1], pool_all[1])
    for spot in range(half // LANES):
        stage[pl.ds(spot, classes, stride=half // LANES), :] = head_grad[
            0:classes, spot * LANES : (spot + 1) * LANES
        ]
    head_space = stage.at[pl.ds(0, grad_head_out.shape[0]), :]
    head_leave = pltpu.make_async_copy(head_space, grad_head_out, sem_local.at[0])
    head_leave.start()

    def drop_into(act, slot, gain, bias, columns):
        size = pl.ds(0, width)
        shift[8:24, size] = jnp.zeros((16, width), wide)

        def drop(index, carry):
            normed = normal(act, slot, index)
            norm = normed * gain + bias
            sig = sigmoid(norm)
            grad = act_three[tile(index), columns] * (sig + norm * sig * (1.0 - sig))
            act_three[tile(index), columns] = grad
            shift[8:16, size] += fold_rows(grad)
            shift[16:24, size] += fold_rows(grad * normed)
            return carry

        lax.fori_loop(0, SIDE, drop, 0)

    def close_back(slot):
        size = pl.ds(0, width)
        sums_mine[slot, 0:1, size] = column_sum(shift[8:16, size])
        sums_mine[slot, 1:2, size] = column_sum(shift[16:24, size])

    space_two, space_one = pl.ds(0, width), pl.ds(width, width)

    def mid_group(which):
        return mid_wide[pl.ds(pl.multiple_of(which * count_rows, count_rows), count_rows), :]

    def back_two(index):
        left = jnp.concatenate([mid_wide[mid_line(which, index), :] for which in range(groups)], axis=1)
        value = dot_nn(left, flat_rows(w_last[...]))
        normed = normal(act_two, 1, index)
        norm = normed * gain_two + bias_two
        sig = sigmoid(norm)
        grad = value * (sig + norm * sig * (1.0 - sig))
        act_three[tile(index), space_two] = grad
        size = pl.ds(0, width)
        shift[8:16, size] += fold_rows(grad)
        shift[16:24, size] += fold_rows(grad * normed)

    def back_two_line(index, carry):
        pull(index + 1)
        back_two(index)
        return carry

    shift[8:24, :] = jnp.zeros((16, channels), wide)
    lax.fori_loop(0, SIDE - 1, back_two_line, 0)
    back_two(SIDE - 1)
    close_back(4)
    move_back_two = swap(4, width)
    move_back_two.start()

    if gather:
        spread.drain()

    def put(ref, which, value):
        ref[which] = value.astype(low_type).reshape(ref.shape[1:])

    def expand_group(which, carry):
        put(w_last, which, dot_tn(mid_group(which), hidden_two[...]))
        fold_begin(which, 2)
        fold_at(which, 2, (0, 2, 0))
        fold_at(which, 3, (0, 2, 1))
        return carry

    lax.fori_loop(0, groups, expand_group, 0)
    move_back_two.wait()
    terms_two = back_terms(4, 1, width, gain_two)

    def back_act(terms, act, layer, index, columns):
        first, second, third = terms
        gap = act[tile(index), :] - fwd_stats[layer, 0:1, pl.ds(0, width)]
        return (first * act_three[tile(index), columns] - second - third * gap).astype(low_type)

    def grad_two(index, carry):
        taps_two[pl.ds(pl.multiple_of((index + 1) * line, line), line), :] = back_act(
            terms_two, act_two, 1, index, space_two
        )
        return carry

    lax.fori_loop(0, SIDE, grad_two, 0)
    fold_step(0, 2, 2)
    fold_step(1, 2, 0)
    core_step, near_step, far_step = 0, 1, 2
    plan = {
        0: [(core_step, 2, 3)],
        1: [(near_step, 2, 1)],
        2: [(far_step, 2, 0), (near_step, 2, 2)],
        3: [(far_step, 2, 1), (near_step, 2, 3)],
        4: [(far_step, 2, 2)],
        5: [(far_step, 2, 3), (core_step, 1, 0)],
        7: [(core_step, 1, 1)],
    }

    def middle_row(down, carry):
        for over in range(3):
            left = row_windows(taps_one, down, low_start[over], reaches[over])
            right = row_windows(taps_two, 1, high_start[over], reaches[over])
            rows = pl.ds(pl.multiple_of((3 * down + over) * width, width), width)
            mid_wide[rows, :] = dot_tn(left, right).astype(low_type)
            for row in range(3):
                tap = 3 * row + over

                @pl.when(down == row)
                def _():
                    if tap >= 2 and tap % 2 == 0:
                        fold_begin(tap // 2 - 1, 1)
                    for step in plan.get(tap, ()):
                        fold_step(*step)

        return carry

    lax.fori_loop(0, 3, middle_row, 0)

    def back_one(index, carry):
        down, side = index // 2, index % 2
        columns = lanes(2 + side, piece)
        for over in range(3):
            left = row_windows(taps_two, 2 - down, high_start[over], reaches[over])
            start = pl.multiple_of((3 * down + over) * width + side * piece, piece)
            value = dot_nt(left, w_middle[pl.ds(start, piece), :])
            add_windows(act_three, columns, value, low_start[over], reaches[over])
        fold_at(index, 0, (core_step, 1, 2), (near_step, 1, 0))
        fold_at(index, 1, (core_step, 1, 3))
        fold_at(index, 2, (near_step, 1, 1), (far_step, 1, 0))
        fold_at(index, 4, (far_step, 1, 1))
        fold_at(index, 5, (near_step, 1, 2))
        return carry

    act_three[:, space_one] = jnp.zeros((count_rows, width), wide)
    lax.fori_loop(0, 6, back_one, 0)
    drop_into(act_one, 0, gain_one, bias_one, space_one)
    fold_step(near_step, 1, 3)
    close_back(5)
    move_back_one = swap(5, width)
    move_back_one.start()

    move_back_one.wait()
    terms_one = back_terms(5, 0, width, gain_one)

    def grad_one(index, carry):
        hidden_two[tile(index), :] = back_act(terms_one, act_one, 0, index, space_one)
        return carry

    lax.fori_loop(0, SIDE, grad_one, 0)
    fold_step(far_step, 1, 2)

    def reduce_group(which, carry):
        put(w_first, which, dot_tn(x_all[:, lanes(which, group)], hidden_two[...]))
        fold_begin(which, 0)
        fold_at(which, 0, (far_step, 1, 3))
        fold_at(which, 2, (core_step, 0, 0))
        fold_at(which, 3, (core_step, 0, 1), (near_step, 0, 0))
        return carry

    lax.fori_loop(0, groups, reduce_group, 0)

    for kind in range(2):
        row = 3 - kind
        pieces = [
            sums_mine[5, row : row + 1, lanes(core, part)],
            sums_mine[4, row : row + 1, lanes(core, part)],
            sums_mine[3, row : row + 1, lanes(core, half)],
        ]
        whole = jnp.concatenate(pieces, axis=1)
        per_kind = whole.shape[1] // LANES
        for spot in range(per_kind):
            grad_norm_out[kind * per_kind + spot : kind * per_kind + spot + 1, :] = whole[
                :, spot * LANES : (spot + 1) * LANES
            ]
    for step in (
        (core_step, 0, 2),
        (core_step, 0, 3),
        (far_step, 0, 0),
        (near_step, 0, 1),
        (near_step, 0, 2),
        (far_step, 0, 1),
        (near_step, 0, 3),
        (far_step, 0, 2),
        (far_step, 0, 3),
    ):
        fold_step(*step)
    if gather:
        start = 0
        for slot in range(3):
            rows = fold.counts[slot]
            act_three[kept + start : kept + start + rows, half : half + width] = fold.result(slot)
            start += rows
        leave = pltpu.make_async_copy(
            act_three.at[pl.ds(kept, start), pl.ds(half, width)], grads_out, sem_local.at[3]
        )
        leave.start()
        leave.wait()
        fold.drain()
    else:
        outs = [
            pltpu.make_async_copy(ref, out, sem_local.at[slot])
            for slot, (ref, out) in enumerate(zip((w_first, mid_wide.at[pl.ds(0, 9 * width), :], w_last), grads_out))
        ]
        for copy in outs:
            copy.start()
        for copy in outs:
            copy.wait()
    head_leave.wait()
    for copy in to_mate + head_moves:
        copy.wait_send()


def client_pass(gather, classes, features, labels, flag, params, head, weights):
    pixels, half = features.shape
    images = labels.shape[1]
    count_rows, channels = pixels // 2, 2 * half
    width = params.shape[0] // 2 * LANES - half
    head_rows = classes + -classes % 16
    mine_images = images // 2
    line = SIDE * mine_images
    middle = 9 * width
    blocks = 32
    group = channels // SPOTS[0]
    vmem = pl.BlockSpec(memory_space=pltpu.VMEM)
    smem = pl.BlockSpec(memory_space=pltpu.SMEM)
    spots = SPOTS + (2,)
    scratch = [
        pltpu.VMEM((count_rows, channels), low_type),
        pltpu.VMEM((SPOTS[0] * count_rows, group), low_type),
        pltpu.VMEM(spots + (channels // blocks, width), low_type),
        pltpu.VMEM((middle, width), low_type),
        pltpu.VMEM(spots + (channels // blocks, width), low_type),
        pltpu.VMEM((count_rows, width), wide),
        pltpu.VMEM((count_rows, width), wide),
        pltpu.VMEM((count_rows, channels), wide),
        pltpu.VMEM((count_rows + 2 * line, width), low_type),
        pltpu.VMEM((count_rows + 2 * line, width), low_type),
        pltpu.VMEM((count_rows, width), low_type),
        pltpu.VMEM((count_rows, LANES), wide),
        pltpu.VMEM((2, 2, half + width), wide),
        pltpu.VMEM((2, head_rows, half), low_type),
        pltpu.VMEM((mine_images, channels), wide),
        pltpu.VMEM((mine_images, half), low_type),
        pltpu.VMEM((2, mine_images, half), low_type),
        pltpu.VMEM((2, head_rows, mine_images), low_type),
        pltpu.VMEM((6, 8, channels), wide),
        pltpu.VMEM((6, 8, channels), wide),
        pltpu.VMEM((24, channels), wide),
        pltpu.VMEM((3, 8, channels), wide),
        pltpu.SemaphoreType.DMA((11,)),
        pltpu.SemaphoreType.DMA((2, 6)),
        pltpu.SemaphoreType.DMA((2, 7)),
    ]
    any_space = pl.BlockSpec(memory_space=pl.ANY)
    if gather:
        counts = (channels // blocks, middle // blocks, channels // blocks)
        scratch += [pltpu.SemaphoreType.DMA((2, 3, 3))]
        scratch += [pltpu.SemaphoreType.DMA((2, 4, size)) for size in (6, 8, 6)]
        scratch += [pltpu.VMEM((4, 2, 2, rows, width), low_type) for rows in counts[1:]]
        for lead in ((4, 2), (4,), (4,)):
            scratch += [pltpu.VMEM(lead + (rows, width), low_type) for rows in counts]
        scratch += [pltpu.SemaphoreType.DMA((2, 4, size)) for size in (6, 8, 6, 6)]
        grads_shape = [jax.ShapeDtypeStruct((sum(counts), width), wide)]
        grads_specs = [any_space]
    else:
        grads_shape = [jax.ShapeDtypeStruct(weight.shape, low_type) for weight in weights]
        grads_specs = [any_space] * 3
    return pl.pallas_call(
        functools.partial(client_kernel, gather, images, classes),
        out_shape=grads_shape
        + [
            jax.ShapeDtypeStruct(params.shape, wide),
            jax.ShapeDtypeStruct((classes * half // LANES, LANES), wide),
            jax.ShapeDtypeStruct((8, LANES), wide),
        ],
        in_specs=[any_space, vmem, smem, vmem, vmem] + [any_space] * len(weights),
        out_specs=grads_specs + [vmem, any_space, vmem],
        scratch_shapes=scratch,
        compiler_params=pltpu.CompilerParams(
            collective_id=0, has_side_effects=True, vmem_limit_bytes=VMEM_BYTES
        ),
    )(features, labels, flag, params, head, *weights)


def adam_update(param, grad, first, second, rate, decay):
    first = adam_first * first + (1.0 - adam_first) * grad
    second = adam_second * second + (1.0 - adam_second) * grad * grad
    first_hat = first / (1.0 - adam_first**STEP)
    second_hat = second / (1.0 - adam_second**STEP)
    return (
        param - rate * (first_hat / (jnp.sqrt(second_hat) + adam_epsilon) + decay * param),
        first,
        second,
    )
class GramSum:
    def __init__(self, place, data, total, boxes, sems):
        self.place = place
        self.data = data
        self.total = total
        self.y_box, self.z_box = boxes
        self.sems = sems
        self.share = data.shape[0] // 8
        self.down_order = place.others[::-1] + [place.z]

    def rows(self, z, y):
        return pl.ds(pl.multiple_of((z * 2 + y) * self.share, 8), self.share)

    def copy(self, number, src, dst, to):
        sems = self.sems
        return remote(src, dst, sems.at[0, number], sems.at[1, number], to, self.place.core)

    def y_down(self, turn):
        p = self.place
        src = self.data.at[self.rows(self.down_order[turn], 1 - p.y), :]
        return self.copy(turn, src, self.y_box.at[turn], p.along_y())

    def z_down(self, step):
        p = self.place
        src = self.data.at[self.rows(p.others[step], p.y), :]
        return self.copy(4 + step, src, self.z_box.at[step], p.along_z(step))

    def z_up(self, step):
        p = self.place
        ref = self.total.at[self.rows(p.z, p.y), :]
        return self.copy(7 + step, ref, ref, p.along_z(step))

    def y_up(self, turn):
        p = self.place
        ref = self.total.at[self.rows(([p.z] + p.others)[turn], p.y), :]
        return self.copy(10 + turn, ref, ref, p.along_y())

    def run(self, extra):
        extra = list(extra)
        p = self.place
        for turn in range(4):
            self.y_down(turn).start()
        for turn in range(4):
            self.y_down(turn).wait_recv()
            self.data[self.rows(self.down_order[turn], p.y), :] += self.y_box[turn]
            if turn < 3:
                self.z_down(2 - turn).start()
            if extra:
                extra.pop(0)()
        mine = self.rows(p.z, p.y)
        value = self.data[mine, :]
        for step in (2, 1, 0):
            self.z_down(step).wait_recv()
            value += self.z_box[step]
        self.total[mine, :] = value
        for step in range(3):
            self.z_up(step).start()
        self.y_up(0).start()
        for step in range(3):
            self.z_up(step).wait_recv()
            self.y_up(1 + step).start()
        for turn in range(4):
            self.y_up(turn).wait_recv()

    def drain(self):
        for turn in range(4):
            self.y_down(turn).wait_send()
            self.y_up(turn).wait_send()
        for step in range(3):
            self.z_down(step).wait_send()
            self.z_up(step).wait_send()


class TileSum:
    def __init__(self, place, tiles, boxes, sems):
        self.place = place
        self.tiles = tiles
        self.boxes = boxes
        self.sems = sems

    def copy(self, stage, box):
        p = self.place
        to = (p.client, p.along_x(), p.along_y()) + tuple(p.along_z(step) for step in range(3))
        core = 1 - p.core if box == 0 else p.core
        return remote(
            self.tiles.at[stage], self.boxes.at[box], self.sems.at[0, box], self.sems.at[1, box], to[box], core
        )

    def steps(self):
        def start():
            self.copy(0, 0).start()

        def pair(stage):
            self.copy(stage, stage).wait_recv()
            self.tiles[stage + 1] = self.tiles[stage] + self.boxes[stage]
            if stage < 2:
                self.copy(stage + 1, stage + 1).start()
            else:
                for step in range(3):
                    self.copy(3, 3 + step).start()

        return [start] + [functools.partial(pair, stage) for stage in range(3)]

    def result(self):
        for step in range(3):
            self.copy(3, 3 + step).wait_recv()
        return (self.tiles[3] + self.boxes[3]) + (self.boxes[4] + self.boxes[5])

    def drain(self):
        for stage in range(3):
            self.copy(stage, stage).wait_send()
        for step in range(3):
            self.copy(3, 3 + step).wait_send()


def dot_high(left, right):
    return jnp.dot(left, right, precision=lax.Precision.HIGH, preferred_element_type=wide)


class Share:
    def __init__(self, place, sizes, buffers, sems):
        self.place = place
        self.sizes = sizes
        self.fresh, self.rows_in, self.rows_out, self.back = buffers
        self.sems = sems
        self.bounds = [0, sizes[0], sizes[0] + sizes[1], sum(sizes)]
        p = place
        self.duty = jnp.where(p.x == 1, 1, 2 * p.core)
        self.mine = p.x * 2 + p.core

    def section(self, slot):
        return pl.ds(self.bounds[slot], self.sizes[slot])

    def spot(self, slot, x, core):
        number = x if slot == 1 else x * 2 + core
        return pl.ds(pl.multiple_of(number * self.sizes[slot], 16), self.sizes[slot])

    def doer(self, slot):
        return (0, 0) if slot == 0 else (0, 1) if slot == 2 else (1, self.place.core)

    def out_copy(self, slot):
        p = self.place
        x, core = self.doer(slot)
        return remote(
            self.fresh.at[self.section(slot), :],
            self.rows_in.at[self.spot(slot, p.x, p.core), :],
            self.sems.at[0, slot],
            self.sems.at[1, self.mine],
            p.at(p.z, p.y, x),
            core,
        )

    def in_copy(self, slot, x, core):
        p = self.place
        return remote(
            self.fresh.at[self.section(slot), :],
            self.rows_in.at[self.spot(slot, x, core), :],
            self.sems.at[0, slot],
            self.sems.at[1, x * 2 + core],
            p.at(p.z, p.y, x),
            core,
        )

    def back_copy(self, slot, x, core):
        p = self.place
        return remote(
            self.rows_out.at[self.spot(slot, x, core), :],
            self.back.at[self.section(slot), :],
            self.sems.at[0, 3 + x * 2 + core],
            self.sems.at[1, 4 + slot],
            p.at(p.z, p.y, x),
            core,
        )

    def users(self, slot):
        p = self.place
        if slot == 1:
            return [(0, p.core), (1, p.core)]
        return [(x, core) for x in (0, 1) for core in (0, 1)]

    def send(self):
        for slot in range(3):

            @pl.when(self.duty != slot)
            def _():
                self.out_copy(slot).start()

            @pl.when(self.duty == slot)
            def _():
                self.rows_in[self.spot(slot, self.place.x, self.place.core), :] = self.fresh[self.section(slot), :]

    def gather(self):
        p = self.place
        for slot in range(3):

            @pl.when(self.duty == slot)
            def _():
                for x, core in self.users(slot):

                    @pl.when((p.x != x) | (p.core != core))
                    def _():
                        self.in_copy(slot, x, core).wait_recv()

    def give_back(self):
        p = self.place
        for slot in range(3):

            @pl.when(self.duty == slot)
            def _():
                for x, core in self.users(slot):

                    @pl.when((p.x != x) | (p.core != core))
                    def _():
                        self.back_copy(slot, x, core).start()

                self.back[self.section(slot), :] = self.rows_out[self.spot(slot, p.x, p.core), :]

    def finish(self):
        p = self.place
        for slot in range(3):

            @pl.when(self.duty != slot)
            def _():
                self.back_copy(slot, p.x, p.core).wait_recv()
                self.out_copy(slot).wait_send()

            @pl.when(self.duty == slot)
            def _():
                for x, core in self.users(slot):

                    @pl.when((p.x != x) | (p.core != core))
                    def _():
                        self.back_copy(slot, x, core).wait_send()


def corner_spot(number, part):
    row, column = number // 2, number % 2
    return slice(row * part, (row + 1) * part), slice(column * part, (column + 1) * part)


def base_kernel(
    ratios,
    sizes,
    master,
    momentum,
    anchor,
    loss_in,
    grads,
    *rest,
):
    place = Place()
    rest = list(rest)

    def take(count):
        taken = rest[:count]
        del rest[:count]
        return taken

    ortho_out, loss_out = take(2)
    gram, gram_total = take(2)
    gram_boxes = take(2)
    (mate_gram,) = take(1)
    grams, fresh, rows_in, rows_out, back, tiles, tile_boxes = take(7)
    gram_sems, tile_sems, share_sems = take(3)

    rows_in[...] = jnp.zeros_like(rows_in)
    place.greet(True, True)
    fresh[...] = momentum_decay * momentum[...] + (grads[...] + prox_weight * (master[...] - anchor[...]))
    share = Share(place, sizes, (fresh, rows_in, rows_out, back), share_sems)
    share.send()
    tiles[0] = loss_in[...]
    tile_sum = TileSum(place, tiles, tile_boxes, tile_sems)
    extra = tile_sum.steps()
    extra.pop(0)()

    width = master.shape[1]
    part = width // CUTS
    corners = [(row, column) for row in range(CUTS) for column in range(row, CUTS)]
    share.gather()
    held = rows_in[...]
    partial = lax.dot_general(
        held, held, (((0,), (0,)), ((), ())), precision=precise, preferred_element_type=wide
    )
    for number, (row, column) in enumerate(corners):
        gram[corner_spot(number, part)] = partial[
            row * part : (row + 1) * part, column * part : (column + 1) * part
        ]

    @pl.when(place.x == 1)
    def _():
        swap = remote(gram, mate_gram, share_sems.at[0, 7], share_sems.at[1, 7], place.client, 1 - place.core)
        swap.start()
        swap.wait()
        gram[...] += mate_gram[...]

    gram_sum = GramSum(place, gram, gram_total, gram_boxes, gram_sems)
    gram_sum.run(extra)
    loss_out[...] = tile_sum.result()

    spots = lax.broadcasted_iota(jnp.int32, (part, part), 0)
    diagonal = spots == lax.broadcasted_iota(jnp.int32, (part, part), 1)
    blocks = [gram_total[corner_spot(number, part)] for number in range(len(corners))]
    trace = sum(
        jnp.sum(jnp.where(diagonal, block, 0.0)) for block, (row, column) in zip(blocks, corners) if row == column
    )
    factor = 1.0 / (jnp.sqrt(trace) + 1e-07)
    square = factor * factor
    for block, (row, column) in zip(blocks, corners):
        rows, columns = slice(row * part, (row + 1) * part), slice(column * part, (column + 1) * part)
        grams[rows, columns] = block * square
        if row < column:
            grams[columns, rows] = block.T * square
    rows_in[...] = rows_in[...] * factor

    def turn(count, carry):
        current = grams[...]
        mixed = schulz_second * current + schulz_third * dot_high(current, current)
        held = rows_in[...]
        rows_in[...] = schulz_first * held + dot_high(held, mixed)

        @pl.when(count < NS_STEPS - 1)
        def _():
            once = schulz_first * current + dot_high(current, mixed)
            grams[...] = schulz_first * once + dot_high(once, mixed)

        return carry

    lax.fori_loop(0, NS_STEPS, turn, 0)
    ratio = jnp.where(share.duty == 1, ratios[1], ratios[0])
    rows_out[...] = (rows_in[...] * ratio).astype(low_type)
    share.give_back()
    share.finish()
    ortho_out[...] = back[...].astype(wide)
    gram_sum.drain()
    tile_sum.drain()


def base_pass(ratios, sizes, master, momentum, anchor, loss_tile, grads):
    rows, width = master.shape
    part = width // CUTS
    gram_rows = CUTS * (CUTS + 1) // 4 * part
    vmem = pl.BlockSpec(memory_space=pltpu.VMEM)
    scratch = [pltpu.VMEM((gram_rows, 2 * part), wide)] * 2
    scratch += [pltpu.VMEM((count, gram_rows // 8, 2 * part), wide) for count in (4, 3)]
    scratch += [pltpu.VMEM((gram_rows, 2 * part), wide)]
    scratch += [
        pltpu.VMEM((width, width), wide),
        pltpu.VMEM((rows, width), wide),
        pltpu.VMEM((max(4 * sizes[0], 2 * sizes[1]), width), wide),
        pltpu.VMEM((max(4 * sizes[0], 2 * sizes[1]), width), low_type),
        pltpu.VMEM((rows, width), low_type),
        pltpu.VMEM((4, 8, LANES), wide),
        pltpu.VMEM((6, 8, LANES), wide),
        pltpu.SemaphoreType.DMA((2, 14)),
        pltpu.SemaphoreType.DMA((2, 6)),
        pltpu.SemaphoreType.DMA((2, 8)),
    ]
    block = jax.ShapeDtypeStruct((rows, width), wide)
    outs = [block, jax.ShapeDtypeStruct((8, LANES), wide)]
    operands = [master, momentum, anchor, loss_tile, grads]
    return pl.pallas_call(
        functools.partial(base_kernel, ratios, sizes),
        out_shape=outs,
        in_specs=[vmem] * len(operands),
        out_specs=[vmem] * len(outs),
        scratch_shapes=scratch,
        compiler_params=pltpu.CompilerParams(
            collective_id=1, has_side_effects=True, vmem_limit_bytes=VMEM_BYTES
        ),
    )(*operands)


def update_kernel(loss_tile, master, momentum, anchor, grads, ortho, *rest):
    norms, grad_norm, heads, grad_head, outs = rest[0:3], rest[3], rest[4:7], rest[7], rest[8:]
    loss_out, *outs = outs
    loss_out[0] = loss_tile[0, 0]
    loss_out[1] = loss_tile[0, 1]
    momentum_out, base_out, low_out = outs[0:3]
    held = master[...]
    momentum_out[...] = momentum_decay * momentum[...] + (grads[...] + prox_weight * (held - anchor[...]))
    fresh = held - muon_rate * (ortho[...] + muon_decay * held)
    base_out[...] = fresh
    low_out[...] = fresh.astype(low_type)
    for targets, values, grad, rate, decay in (
        (outs[3:6], norms, grad_norm, norm_rate, 0.0),
        (outs[6:9], heads, grad_head, head_rate, head_decay),
    ):
        updates = adam_update(values[0][...], grad[...], values[1][...], values[2][...], rate, decay)
        for target, value in zip(targets, updates):
            target[...] = value


def update_pass(loss_tile, master, momentum, anchor, grads, ortho, norms, grad_norm, heads, grad_head):
    vmem = pl.BlockSpec(memory_space=pltpu.VMEM)
    smem = pl.BlockSpec(memory_space=pltpu.SMEM)
    operands = [loss_tile, master, momentum, anchor, grads, ortho, *norms, grad_norm, *heads, grad_head]
    outs = [(2,), master.shape, master.shape, master.shape] + [grad_norm.shape] * 3 + [grad_head.shape] * 3
    types = [wide, wide, wide, low_type] + [wide] * 6
    return pl.pallas_call(
        update_kernel,
        out_shape=[jax.ShapeDtypeStruct(shape, kind) for shape, kind in zip(outs, types)],
        in_specs=[smem] + [vmem] * (len(operands) - 1),
        out_specs=[smem] + [vmem] * (len(outs) - 1),
        compiler_params=pltpu.CompilerParams(vmem_limit_bytes=VMEM_BYTES),
    )(*operands)


def gram_of(section):
    return lax.dot_general(section, section, (((0,), (0,)), ((), ())), precision=precise)


def square(gram):
    return jnp.dot(gram, gram, precision=precise)


def times_poly(left, mixed):
    return schulz_first * left + jnp.dot(left, mixed, precision=precise)


def schulz(sections):
    raw_grams = lax.psum(tuple(gram_of(section) for section in sections), ("client", "chan"))
    factors = [1.0 / (jnp.sqrt(jnp.trace(gram)) + 1e-07) for gram in raw_grams]
    current = [section * factor for section, factor in zip(sections, factors)]
    grams = [gram * (factor * factor) for gram, factor in zip(raw_grams, factors)]
    for turn in range(NS_STEPS):
        mixed = [schulz_second * gram + schulz_third * square(gram) for gram in grams]
        current = [times_poly(current[slot], mixed[slot]) for slot in range(3)]
        if turn + 1 < NS_STEPS:
            grams = [
                times_poly(times_poly(grams[slot], mixed[slot]), mixed[slot]) for slot in range(3)
            ]
    return current


def base_far(ratios, bounds, master, momentum, anchor, loss_tile, grads):
    sums = [
        lax.psum_scatter(flat_rows(grad).astype(wide), ("client", "chan"), scatter_dimension=0, tiled=True)
        for grad in grads
    ]
    grad_base = jnp.concatenate(sums, axis=0)
    momentum_new = momentum_decay * momentum + (grad_base + prox_weight * (master - anchor))
    current = schulz([momentum_new[bounds[slot] : bounds[slot + 1]] for slot in range(3)])
    ortho = jnp.concatenate([current[slot] * ratios[slot] for slot in range(3)], axis=0)
    return grad_base, ortho, lax.psum(loss_tile, ("client", "chan"))


def as_stored(rows, shape):
    return with_layout_constraint(rows.reshape(shape), Layout(major_to_minor=tuple(range(len(shape)))))


def on_device(
    features,
    labels,
    mask,
    base_master,
    base_momentum,
    global_base,
    norm_params,
    norm_first,
    norm_second,
    head,
    head_first,
    head_second,
):
    halves = lax.axis_size("chan")
    blocks = lax.axis_size("client") * halves
    half = features.shape[2]
    width = base_master.shape[2]
    channels = half * halves
    classes = head.shape[2]
    rows_first = channels // blocks
    rows_mid = 9 * width // blocks
    sizes = (rows_first, rows_mid, rows_first)
    bounds = (0, rows_first, rows_first + rows_mid, base_master.shape[1])
    ratio = (channels / width) ** 0.5
    ratios = (ratio, 3.0, ratio)
    master, momentum, anchor = base_master[0], base_momentum[0], global_base[0]
    norms = [value.reshape(-1, LANES) for value in (norm_params, norm_first, norm_second)]
    heads = [jnp.transpose(value, (2, 0, 1)).reshape(-1, LANES) for value in (head, head_first, head_second)]
    near = lax.axis_size("client") == SPOTS[0] * SPOTS[1] * SPOTS[2]
    if near:
        weights = [master]
    else:
        low_master = master.astype(low_type)
        weights = [
            lax.all_gather(low_master[bounds[slot] : bounds[slot + 1]], ("client", "chan"), axis=0, tiled=True)
            for slot in range(3)
        ]
        split = SPOTS + (2, channels // 32, width)
        weights = [weights[0].reshape(split), weights[1], weights[2].reshape(split)]
    *grads, grad_norm, grad_head, loss_tile = client_pass(
        near, classes, features[0], labels, mask, norms[0], heads[0], weights
    )
    if near:
        (grad_base,) = grads
        ortho, loss_tile = base_pass(ratios, sizes, master, momentum, anchor, loss_tile, grad_base)
    else:
        grad_base, ortho, loss_tile = base_far(ratios, bounds, master, momentum, anchor, loss_tile, grads)
    loss, momentum_new, base_new, base_low, *fresh = update_pass(
        loss_tile, master, momentum, anchor, grad_base, ortho, norms, grad_norm, heads, grad_head
    )
    fresh_norms = [as_stored(value, norm_params.shape) for value in fresh[:3]]
    fresh_heads = [jnp.transpose(as_stored(value, (classes, 1, half)), (1, 2, 0)) for value in fresh[3:]]
    return (
        loss,
        base_new[None],
        momentum_new[None],
        base_low[None],
        *fresh_norms,
        *fresh_heads,
    )


def solution(mesh):
    wide_block = P(("client", "chan"), None, None)
    norm_block = P("client", None, "chan", None)
    head_block = P("client", "chan", None)
    return jax.shard_map(
        on_device,
        mesh=mesh,
        in_specs=(P("client", None, "chan"), P("client", None), P("client"))
        + (wide_block,) * 3
        + (norm_block,) * 3
        + (head_block,) * 3,
        out_specs=(P(),) + (wide_block,) * 3 + (norm_block,) * 3 + (head_block,) * 3,
        check_vma=False,
    )
```

```python
import functools

import jax
import jax.numpy as jnp
from jax import lax
from jax.experimental import pallas as pl
from jax.experimental.layout import Layout, with_layout_constraint
from jax.experimental.pallas import tpu as pltpu
from jax.sharding import PartitionSpec as P

NS_STEPS = 5
STEP = 10

low_type = jnp.bfloat16
wide = jnp.float32
MESH = pl.DeviceIdType.MESH
precise = lax.Precision.HIGHEST
norm_epsilon = 1e-05
prox_weight = 0.05
momentum_decay = 0.95
muon_rate = 0.3
muon_decay = 0.1
schulz_first = 3.4445
schulz_second = -4.775
schulz_third = 2.0315
adam_first = 0.9
adam_second = 0.95
adam_epsilon = 1e-08
head_rate = 0.01
head_decay = 0.05
norm_rate = 0.5

SIDE = 7
PIXELS = SIDE * SIDE
LANES = 128
SPOTS = (4, 2, 2)
CUTS = 4
VMEM_BYTES = 62 * 2**20


def dot_nn(left, right):
    return jnp.dot(left, right, preferred_element_type=wide)


def dot_nt(left, right):
    return lax.dot_general(left, right, (((1,), (1,)), ((), ())), preferred_element_type=wide)


def dot_tn(left, right):
    return lax.dot_general(left, right, (((0,), (0,)), ((), ())), preferred_element_type=wide)


def flat_rows(block):
    return block.reshape(-1, block.shape[-1])


def sigmoid(value):
    return 0.5 * jnp.tanh(0.5 * value) + 0.5


def fold_rows(value):
    return jnp.sum(value.reshape(value.shape[0] // 8, 8, value.shape[1]), axis=0)


def column_sum(value):
    return jnp.sum(value, axis=0, keepdims=True)


def remote(src, dst, send_sem, recv_sem, client, core):
    return pltpu.make_async_remote_copy(
        src_ref=src,
        dst_ref=dst,
        send_sem=send_sem,
        recv_sem=recv_sem,
        device_id=(client, core),
        device_id_type=MESH,
    )


class Place:
    def __init__(self):
        self.client = lax.axis_index("client")
        self.core = lax.axis_index("chan")
        self.z = self.client // 4
        self.y = (self.client // 2) % 2
        self.x = self.client % 2
        self.others = [
            self.z + 1 - 2 * (self.z % 2),
            (self.z + 2) % 4,
            3 - self.z,
        ]

    def at(self, z, y, x):
        return z * 4 + y * 2 + x

    def along_x(self):
        return self.at(self.z, self.y, 1 - self.x)

    def along_y(self):
        return self.at(self.z, 1 - self.y, self.x)

    def along_z(self, step):
        return self.at(self.others[step], self.y, self.x)

    def greet(self, whole, across=False):
        barrier = pltpu.get_barrier_semaphore()
        pairs = [(self.client, 1 - self.core)]
        if whole:
            pairs += [(self.along_x(), self.core), (self.along_y(), self.core)]
            pairs += [(self.along_z(step), self.core) for step in range(3)]
        if across:
            pairs += [(self.along_x(), 1 - self.core)]
        for pair in pairs:
            pl.semaphore_signal(barrier, inc=1, device_id=pair, device_id_type=MESH)
        pl.semaphore_wait(barrier, len(pairs))


def cut_rows(counts):
    pieces = []
    for slot, rows in enumerate(counts):
        middle = (rows // 16 + 1) // 2 * 16
        pieces.append((slot, 0, middle, 0))
        pieces.append((slot, middle, rows - middle, 1))
    return pieces


def block_ref(ref, size, z, y, x, core, start, count):
    if len(ref.shape) == 2:
        first = (((z * 2 + y) * 2 + x) * 2 + core) * size + start
        return ref.at[pl.ds(pl.multiple_of(first, 16), count), :]
    return ref.at[z, y, x, core, pl.ds(start, count), :]


class Spread:
    def __init__(self, place, weights, counts, sems):
        self.place = place
        self.weights = weights
        self.counts = counts
        self.pieces = cut_rows(counts)
        self.z_sems, self.near_sems, self.far_sems, self.core_sems = sems
        self.order = [place.z] + place.others

    def z_copy(self, step, slot):
        p = self.place
        ref = block_ref(self.weights[slot], self.counts[slot], p.z, p.y, p.x, p.core, 0, self.counts[slot])
        sems = self.z_sems
        return remote(ref, ref, sems.at[0, step, slot], sems.at[1, step, slot], p.along_z(step), p.core)

    def near_copy(self, turn, number):
        p = self.place
        slot, start, count, way = self.pieces[number]
        ref = block_ref(self.weights[slot], self.counts[slot], self.order[turn], p.y, p.x, p.core, start, count)
        sems = self.near_sems
        return remote(
            ref, ref, sems.at[0, turn, number], sems.at[1, turn, number], (p.along_x, p.along_y)[way](), p.core
        )

    def far_copies(self, turn, number):
        p = self.place
        slot, start, count, way = self.pieces[number]
        spot = self.order[turn]
        sems = self.far_sems
        copies = []
        for part, other in enumerate((0, 1) if slot == 1 else (slice(None),)):
            y, x = (p.y, other) if way == 0 else (other, p.x)
            ref = block_ref(self.weights[slot], self.counts[slot], spot, y, x, p.core, start, count)
            sem = number + 4 * part
            to = (p.along_y, p.along_x)[way]()
            copies.append(remote(ref, ref, sems.at[0, turn, sem], sems.at[1, turn, sem], to, p.core))
        return copies

    def core_copies(self, turn, slot):
        p = self.place
        sems = self.core_sems
        copies = []
        pairs = [(y, x) for y in (0, 1) for x in (0, 1)] if slot == 1 else [(slice(None), slice(None))]
        for part, (y, x) in enumerate(pairs):
            ref = block_ref(self.weights[slot], self.counts[slot], self.order[turn], y, x, p.core, 0, self.counts[slot])
            sem = (0, 2 + part, 1)[slot]
            copies.append(remote(ref, ref, sems.at[0, turn, sem], sems.at[1, turn, sem], p.client, 1 - p.core))
        return copies

    def fill(self, master):
        p = self.place
        start = 0
        for slot in range(3):
            rows = self.counts[slot]
            own = block_ref(self.weights[slot], self.counts[slot], p.z, p.y, p.x, p.core, 0, rows)
            own[...] = master[start : start + rows, :].astype(low_type)
            start += rows

    def begin(self):
        for step in range(3):
            self.z_copy(step, 0).start()
        self.near_start(0)

    def near_start(self, slot):
        for number in (2 * slot, 2 * slot + 1):
            self.near_copy(0, number).start()

    def steps(self):
        near, far, core, start = self.near_step, self.far_step, self.core_step, self.near_start
        groups = [
            [(far, 0, 0), (start, 1)],
            [(near, 1, 0)],
            [(near, 2, 0), (near, 3, 0)],
            [(far, 1, 0), (core, 0, 0), (far, 0, 1)],
            [(far, 2, 0), (far, 3, 0), (core, 1, 0)],
            [(core, 2, 0), (core, 3, 0), (near, 1, 1), (start, 2)],
            [(core, 0, 1), (near, 2, 1)],
            [(far, 1, 1), (near, 3, 1)],
            [(core, 1, 1), (far, 2, 1), (far, 0, 2)],
            [(far, 3, 1), (core, 2, 1), (near, 1, 2)],
            [(core, 3, 1), (core, 0, 2), (near, 2, 2)],
            [(far, 1, 2), (near, 3, 2)],
            [(core, 1, 2), (far, 2, 2)],
            [(far, 3, 2), (core, 2, 2)],
            [(core, 3, 2)],
        ]
        return [[functools.partial(*step) for step in group] for group in groups]

    def near_step(self, turn, slot):
        self.z_copy(turn - 1, slot).wait_recv()
        for number in (2 * slot, 2 * slot + 1):
            self.near_copy(turn, number).start()
        if slot < 2:
            self.z_copy(turn - 1, slot + 1).start()

    def far_step(self, turn, slot):
        for number in (2 * slot, 2 * slot + 1):
            self.near_copy(turn, number).wait_recv()
            for copy in self.far_copies(turn, number):
                copy.start()

    def core_step(self, turn, slot):
        for number in (2 * slot, 2 * slot + 1):
            for copy in self.far_copies(turn, number):
                copy.wait_recv()
        for copy in self.core_copies(turn, slot):
            copy.start()

    def arrive(self, slot):
        for turn in range(4):
            for copy in self.core_copies(turn, slot):
                copy.wait_recv()

    def drain(self):
        for slot in range(3):
            for step in range(3):
                self.z_copy(step, slot).wait_send()
            for turn in range(4):
                for copy in self.core_copies(turn, slot):
                    copy.wait_send()
        for number in range(6):
            for turn in range(4):
                self.near_copy(turn, number).wait_send()
                for copy in self.far_copies(turn, number):
                    copy.wait_send()


class Fold:
    def __init__(self, place, grads, counts, parts):
        self.place = place
        self.grads = grads
        self.counts = counts
        self.pieces = cut_rows(counts)
        self.core_boxes = [parts[1], parts[0], parts[1]]
        self.near_boxes, self.far_boxes, self.z_boxes = [parts[3 * k + 2 : 3 * k + 5] for k in range(3)]
        self.core_sems, self.near_sems, self.far_sems, self.z_sems = parts[11:]

    def core_copies(self, which, slot):
        p = self.place
        sems = self.core_sems
        copies = []
        pairs = [(y, x) for y in (0, 1) for x in (0, 1)] if slot == 1 else [(slice(None), slice(None))]
        for part, (y, x) in enumerate(pairs):
            ref = block_ref(self.grads[slot], self.counts[slot], which, y, x, 1 - p.core, 0, self.counts[slot])
            box = self.core_boxes[slot].at[which, y, x]
            sem = (0, 2 + part, 1)[slot]
            copies.append(remote(ref, box, sems.at[0, which, sem], sems.at[1, which, sem], p.client, 1 - p.core))
        return copies

    def near_copies(self, which, number):
        p = self.place
        slot, start, count, way = self.pieces[number]
        sems = self.near_sems
        copies = []
        for part, other in enumerate((0, 1) if slot == 1 else (slice(None),)):
            y, x = (other, 1 - p.x) if way == 0 else (1 - p.y, other)
            ref = block_ref(self.grads[slot], self.counts[slot], which, y, x, p.core, start, count)
            box = self.near_boxes[slot].at[which, other, pl.ds(start, count), :]
            sem = number + 4 * part
            to = (p.along_x, p.along_y)[way]()
            copies.append(remote(ref, box, sems.at[0, which, sem], sems.at[1, which, sem], to, p.core))
        return copies

    def far_copy(self, which, number):
        p = self.place
        slot, start, count, way = self.pieces[number]
        y, x = (1 - p.y, p.x) if way == 0 else (p.y, 1 - p.x)
        ref = block_ref(self.grads[slot], self.counts[slot], which, y, x, p.core, start, count)
        box = self.far_boxes[slot].at[which, pl.ds(start, count), :]
        sems = self.far_sems
        return remote(
            ref, box, sems.at[0, which, number], sems.at[1, which, number], (p.along_y, p.along_x)[way](), p.core
        )

    def z_copy(self, which, sender, number):
        p = self.place
        slot, start, count, _ = self.pieces[number]
        rows = pl.ds(start, count)
        sems = self.z_sems
        return remote(
            block_ref(self.grads[slot], self.counts[slot], which, p.y, p.x, p.core, start, count),
            self.z_boxes[slot].at[sender, rows, :],
            sems.at[0, which, number],
            sems.at[1, sender, number],
            p.at(which, p.y, p.x),
            p.core,
        )

    def begin(self, which, slot):
        for copy in self.core_copies(which, slot):
            copy.start()

    def add(self, slot, spots, start, count, box):
        ref = block_ref(self.grads[slot], self.counts[slot], *spots, self.place.core, start, count)
        ref[...] = (ref[...].astype(wide) + box.astype(wide)).astype(low_type)

    def core_step(self, which, slot):
        for copy in self.core_copies(which, slot):
            copy.wait_recv()
        pairs = [(y, x) for y in (0, 1) for x in (0, 1)] if slot == 1 else [(slice(None), slice(None))]
        for y, x in pairs:
            self.add(slot, (which, y, x), 0, self.counts[slot], self.core_boxes[slot][which, y, x])
        for number in (2 * slot, 2 * slot + 1):
            for copy in self.near_copies(which, number):
                copy.start()

    def near_step(self, which, slot):
        p = self.place
        for number in (2 * slot, 2 * slot + 1):
            _, start, count, way = self.pieces[number]
            for copy in self.near_copies(which, number):
                copy.wait_recv()
            for other in (0, 1) if slot == 1 else (slice(None),):
                y, x = (other, p.x) if way == 0 else (p.y, other)
                box = self.near_boxes[slot][which, other, pl.ds(start, count), :]
                self.add(slot, (which, y, x), start, count, box)
            self.far_copy(which, number).start()

    def far_step(self, which, slot):
        p = self.place
        for number in (2 * slot, 2 * slot + 1):
            _, start, count, way = self.pieces[number]
            self.far_copy(which, number).wait_recv()
            box = self.far_boxes[slot][which, pl.ds(start, count), :]
            self.add(slot, (which, p.y, p.x), start, count, box)

            @pl.when(p.z != which)
            def _():
                self.z_copy(which, p.z, number).start()

    def result(self, slot):
        p = self.place
        self.z_boxes[slot][p.z] = block_ref(self.grads[slot], self.counts[slot], p.z, p.y, p.x, p.core, 0, self.counts[slot])[...]
        for sender in range(4):

            @pl.when(p.z != sender)
            def _():
                for number in (2 * slot, 2 * slot + 1):
                    self.z_copy(sender, sender, number).wait_recv()

        total = self.z_boxes[slot][0].astype(wide)
        for sender in range(1, 4):
            total += self.z_boxes[slot][sender].astype(wide)
        return total

    def drain(self):
        for which in range(4):
            for slot in range(3):
                for copy in self.core_copies(which, slot):
                    copy.wait_send()
            for number in range(6):
                for copy in self.near_copies(which, number):
                    copy.wait_send()
                self.far_copy(which, number).wait_send()

            @pl.when(self.place.z != which)
            def _():
                for number in range(6):
                    self.z_copy(which, self.place.z, number).wait_send()
class GramSum:
    def __init__(self, place, data, total, boxes, sems):
        self.place = place
        self.data = data
        self.total = total
        self.y_box, self.z_box = boxes
        self.sems = sems
        self.share = data.shape[0] // 8
        self.down_order = place.others[::-1] + [place.z]

    def rows(self, z, y):
        return pl.ds(pl.multiple_of((z * 2 + y) * self.share, 8), self.share)

    def copy(self, number, src, dst, to):
        sems = self.sems
        return remote(src, dst, sems.at[0, number], sems.at[1, number], to, self.place.core)

    def y_down(self, turn):
        p = self.place
        src = self.data.at[self.rows(self.down_order[turn], 1 - p.y), :]
        return self.copy(turn, src, self.y_box.at[turn], p.along_y())

    def z_down(self, step):
        p = self.place
        src = self.data.at[self.rows(p.others[step], p.y), :]
        return self.copy(4 + step, src, self.z_box.at[step], p.along_z(step))

    def z_up(self, step):
        p = self.place
        ref = self.total.at[self.rows(p.z, p.y), :]
        return self.copy(7 + step, ref, ref, p.along_z(step))

    def y_up(self, turn):
        p = self.place
        ref = self.total.at[self.rows(([p.z] + p.others)[turn], p.y), :]
        return self.copy(10 + turn, ref, ref, p.along_y())

    def run(self):
        p = self.place
        for turn in range(4):
            self.y_down(turn).start()
        for turn in range(4):
            self.y_down(turn).wait_recv()
            self.data[self.rows(self.down_order[turn], p.y), :] += self.y_box[turn]
            if turn < 3:
                self.z_down(2 - turn).start()
        mine = self.rows(p.z, p.y)
        value = self.data[mine, :]
        for step in (2, 1, 0):
            self.z_down(step).wait_recv()
            value += self.z_box[step]
        self.total[mine, :] = value
        for step in range(3):
            self.z_up(step).start()
        self.y_up(0).start()
        for step in range(3):
            self.z_up(step).wait_recv()
            self.y_up(1 + step).start()
        for turn in range(4):
            self.y_up(turn).wait_recv()

    def drain(self):
        for turn in range(4):
            self.y_down(turn).wait_send()
            self.y_up(turn).wait_send()
        for step in range(3):
            self.z_down(step).wait_send()
            self.z_up(step).wait_send()


class TileSum:
    def __init__(self, place, tiles, boxes, sems):
        self.place = place
        self.tiles = tiles
        self.boxes = boxes
        self.sems = sems

    def copy(self, stage, box):
        p = self.place
        to = (p.client, p.along_x(), p.along_y()) + tuple(p.along_z(step) for step in range(3))
        core = 1 - p.core if box == 0 else p.core
        return remote(
            self.tiles.at[stage], self.boxes.at[box], self.sems.at[0, box], self.sems.at[1, box], to[box], core
        )

    def start(self):
        self.copy(0, 0).start()

    def pair(self, stage):
        self.copy(stage, stage).wait_recv()
        self.tiles[stage + 1] = self.tiles[stage] + self.boxes[stage]
        if stage < 2:
            self.copy(stage + 1, stage + 1).start()
        else:
            for step in range(3):
                self.copy(3, 3 + step).start()

    def result(self):
        for step in range(3):
            self.copy(3, 3 + step).wait_recv()
        return (self.tiles[3] + self.boxes[3]) + (self.boxes[4] + self.boxes[5])

    def drain(self):
        for stage in range(3):
            self.copy(stage, stage).wait_send()
        for step in range(3):
            self.copy(3, 3 + step).wait_send()


def halves_of(value):
    high = value.astype(low_type)
    return high, (value - high.astype(wide)).astype(low_type)


class Share:
    def __init__(self, place, sizes, buffers, sems):
        self.place = place
        self.sizes = sizes
        self.fresh, self.rows_in, self.rows_out, self.back = buffers
        self.sems = sems
        self.bounds = [0, sizes[0], sizes[0] + sizes[1], sum(sizes)]
        p = place
        self.duty = jnp.where(p.x == 1, 1, 2 * p.core)
        self.mine = p.x * 2 + p.core

    def section(self, slot):
        return pl.ds(self.bounds[slot], self.sizes[slot])

    def spot(self, slot, x, core):
        number = x if slot == 1 else x * 2 + core
        return pl.ds(pl.multiple_of(number * self.sizes[slot], 16), self.sizes[slot])

    def doer(self, slot):
        return (0, 0) if slot == 0 else (0, 1) if slot == 2 else (1, self.place.core)

    def out_copy(self, slot):
        p = self.place
        x, core = self.doer(slot)
        return remote(
            self.fresh.at[self.section(slot), :],
            self.rows_in.at[self.spot(slot, p.x, p.core), :],
            self.sems.at[0, slot],
            self.sems.at[1, self.mine],
            p.at(p.z, p.y, x),
            core,
        )

    def in_copy(self, slot, x, core):
        p = self.place
        return remote(
            self.fresh.at[self.section(slot), :],
            self.rows_in.at[self.spot(slot, x, core), :],
            self.sems.at[0, slot],
            self.sems.at[1, x * 2 + core],
            p.at(p.z, p.y, x),
            core,
        )

    def back_copy(self, slot, x, core):
        p = self.place
        return remote(
            self.rows_out.at[self.spot(slot, x, core), :],
            self.back.at[self.section(slot), :],
            self.sems.at[0, 3 + x * 2 + core],
            self.sems.at[1, 4 + slot],
            p.at(p.z, p.y, x),
            core,
        )

    def users(self, slot):
        p = self.place
        if slot == 1:
            return [(0, p.core), (1, p.core)]
        return [(x, core) for x in (0, 1) for core in (0, 1)]

    def send(self, slot):
        @pl.when(self.duty != slot)
        def _():
            self.out_copy(slot).start()

        @pl.when(self.duty == slot)
        def _():
            self.rows_in[self.spot(slot, self.place.x, self.place.core), :] = self.fresh[self.section(slot), :]

    def gather(self):
        p = self.place
        for slot in range(3):

            @pl.when(self.duty == slot)
            def _():
                for x, core in self.users(slot):

                    @pl.when((p.x != x) | (p.core != core))
                    def _():
                        self.in_copy(slot, x, core).wait_recv()

    def give_back(self):
        p = self.place
        for slot in range(3):

            @pl.when(self.duty == slot)
            def _():
                for x, core in self.users(slot):

                    @pl.when((p.x != x) | (p.core != core))
                    def _():
                        self.back_copy(slot, x, core).start()

                self.back[self.section(slot), :] = self.rows_out[self.spot(slot, p.x, p.core), :]

    def finish(self):
        p = self.place
        for slot in range(3):

            @pl.when(self.duty != slot)
            def _():
                self.back_copy(slot, p.x, p.core).wait_recv()
                self.out_copy(slot).wait_send()

            @pl.when(self.duty == slot)
            def _():
                for x, core in self.users(slot):

                    @pl.when((p.x != x) | (p.core != core))
                    def _():
                        self.back_copy(slot, x, core).wait_send()


def corner_spot(number, part):
    row, column = number // 2, number % 2
    return slice(row * part, (row + 1) * part), slice(column * part, (column + 1) * part)


def orthogonal(place, ratios, share, share_sems, gram, gram_total, mate_gram, gram_sum, squares, rows_in, low_rows):
    grams, mixed, once = squares
    count, width = rows_in.shape
    part = width // CUTS
    corners = [(row, column) for row in range(CUTS) for column in range(row, CUTS)]
    right_high, right_low = [low_rows.at[pl.ds(count + spot * width, width), :] for spot in range(2)]

    def set_right(value_ref):
        for start in range(0, width, part):
            rows = slice(start, start + part)
            right_high[rows, :], right_low[rows, :] = halves_of(value_ref[rows, :])

    def times_right(value):
        high, low = halves_of(value)
        left = jnp.concatenate([high, high, low], axis=1)
        right = jnp.concatenate([right_high[...], right_low[...], right_high[...]], axis=0)
        return dot_nn(left, right)

    def by_rows(rows, step, call):
        def body(index, carry):
            call(pl.ds(pl.multiple_of(index * step, step), step))
            return carry

        lax.fori_loop(0, rows // step, body, 0)

    share.gather()
    high, low = halves_of(rows_in[...])
    left = jnp.concatenate([high, high, low], axis=0)
    right = jnp.concatenate([high, low, high], axis=0)
    for row in range(CUTS):
        strip = dot_tn(left[:, row * part : (row + 1) * part], right[:, row * part :])
        for column in range(row, CUTS):
            gram[corner_spot(corners.index((row, column)), part)] = strip[
                :, (column - row) * part : (column - row + 1) * part
            ]

    @pl.when(place.x == 1)
    def _():
        swap = remote(gram, mate_gram, share_sems.at[0, 7], share_sems.at[1, 7], place.client, 1 - place.core)
        swap.start()
        swap.wait()
        gram[...] += mate_gram[...]

    gram_sum.run()
    spots = lax.broadcasted_iota(jnp.int32, (part, part), 0)
    diagonal = spots == lax.broadcasted_iota(jnp.int32, (part, part), 1)
    trace = 0.0
    for number, (row, column) in enumerate(corners):
        if row == column:
            trace += jnp.sum(jnp.where(diagonal, gram_total[corner_spot(number, part)], 0.0))
    factor = 1.0 / (jnp.sqrt(trace) + 1e-07)
    square = factor * factor
    for number, (row, column) in enumerate(corners):
        rows, columns = slice(row * part, (row + 1) * part), slice(column * part, (column + 1) * part)
        block = gram_total[corner_spot(number, part)] * square
        grams[rows, columns] = block
        if row < column:
            grams[columns, rows] = block.T
    rows_in[...] = rows_in[...] * factor
    step = width // 2

    def turn(number, carry):
        set_right(grams)

        def mix(rows):
            current = grams[rows, :]
            mixed[rows, :] = schulz_second * current + schulz_third * times_right(current)

        by_rows(width, step, mix)
        set_right(mixed)

        def move(rows):
            held = rows_in[rows, :]
            rows_in[rows, :] = schulz_first * held + times_right(held)

        by_rows(count, count // 2, move)

        @pl.when(number < NS_STEPS - 1)
        def _():
            def first(rows):
                current = grams[rows, :]
                once[rows, :] = schulz_first * current + times_right(current)

            def second(rows):
                current = once[rows, :]
                grams[rows, :] = schulz_first * current + times_right(current)

            by_rows(width, step, first)
            by_rows(width, step, second)

        return carry

    lax.fori_loop(0, NS_STEPS, turn, 0)
    ratio = jnp.where(share.duty == 1, ratios[1], ratios[0])
    low_rows[0:count, :] = (rows_in[...] * ratio).astype(low_type)
    share.give_back()


def update_kernel(loss_tile, master, fresh_momentum, ortho, *rest):
    norms, grad_norm, heads, grad_head, outs = rest[0:3], rest[3], rest[4:7], rest[7], rest[8:]
    loss_out, *outs = outs
    loss_out[0] = loss_tile[0, 0]
    loss_out[1] = loss_tile[0, 1]
    momentum_out, base_out, low_out = outs[0:3]
    held = master[...]
    momentum_out[...] = fresh_momentum[...]
    fresh = held - muon_rate * (ortho[...].astype(wide) + muon_decay * held)
    base_out[...] = fresh
    low_out[...] = fresh.astype(low_type)
    for targets, values, grad, rate, decay in (
        (outs[3:6], norms, grad_norm, norm_rate, 0.0),
        (outs[6:9], heads, grad_head, head_rate, head_decay),
    ):
        updates = adam_update(values[0][...], grad[...], values[1][...], values[2][...], rate, decay)
        for target, value in zip(targets, updates):
            target[...] = value


def update_pass(loss_tile, master, fresh_momentum, ortho, norms, grad_norm, heads, grad_head):
    vmem = pl.BlockSpec(memory_space=pltpu.VMEM)
    smem = pl.BlockSpec(memory_space=pltpu.SMEM)
    operands = [loss_tile, master, fresh_momentum, ortho, *norms, grad_norm, *heads, grad_head]
    outs = [(2,), master.shape, master.shape, master.shape] + [grad_norm.shape] * 3 + [grad_head.shape] * 3
    types = [wide, wide, wide, low_type] + [wide] * 6
    return pl.pallas_call(
        update_kernel,
        out_shape=[jax.ShapeDtypeStruct(shape, kind) for shape, kind in zip(outs, types)],
        in_specs=[smem] + [vmem] * (len(operands) - 1),
        out_specs=[smem] + [vmem] * (len(outs) - 1),
        compiler_params=pltpu.CompilerParams(vmem_limit_bytes=VMEM_BYTES),
    )(*operands)


def norm_stats(mine, theirs, count):
    gap = mine[0:1] - theirs[0:1]
    mean = 0.5 * (mine[0:1] + theirs[0:1])
    spread = mine[1:2] + theirs[1:2] + gap * gap * (0.5 * count)
    return mean, lax.rsqrt(spread / (2.0 * count) + norm_epsilon)


def client_kernel(
    gather,
    ratios,
    images,
    classes,
    features,
    labels,
    flag,
    params,
    head,
    *rest,
):
    if gather:
        master, momentum, anchor, *rest = rest
    else:
        first_in, middle_in, last_in, *rest = rest
    if gather:
        fresh_out, ortho_out, *rest = rest
    else:
        grads_out, rest = rest[:3], rest[3:]
    (
        grad_norm_out,
        grad_head_out,
        loss_out,
        x_all,
        mid_wide,
        w_first,
        w_middle,
        w_last,
        act_one,
        act_two,
        act_three,
        taps_one,
        taps_two,
        hidden_two,
        stage,
        params_all,
        head_all,
        grad_pool,
        pool_send,
        pool_all,
        logit_grads,
        sums_mine,
        sums_theirs,
        shift,
        fwd_stats,
        sem_local,
        sem_swap,
        sem_misc,
        *near_parts,
    ) = rest
    place = Place()
    core = place.core
    mate = (place.client, 1 - core)
    count_rows, channels = x_all.shape
    half = channels // 2
    width = act_one.shape[1]
    part = width // 2
    mine_images = images // 2
    line = SIDE * mine_images
    total_rows = 2.0 * count_rows

    def tile(index):
        return pl.ds(pl.multiple_of(index * line, line), line)

    def lanes(index, size):
        return pl.ds(pl.multiple_of(index * size, size), size)

    weights = (w_first, w_middle, w_last)
    if gather:
        held = act_three.at[pl.ds(0, master.shape[0]), pl.ds(0, width)]
        load = pltpu.make_async_copy(master, held, sem_local.at[8])
        load.start()
        counts = [channels // 32, 9 * width // 32, channels // 32]
        spread = Spread(place, weights, counts, near_parts[:4])
        fold = Fold(place, (w_first, mid_wide, w_last), counts, near_parts[4:19])
        rows_in, back, tiles, tile_boxes, gram_total, y_box, z_box, mate_gram = near_parts[19:27]
        tile_sems, share_sems, gram_sems = near_parts[27:]
        block_rows = master.shape[0]
        side_space = pl.ds(half, width)
        held_base, held_momentum, held_anchor, fresh = [
            act_three.at[pl.ds(number * block_rows, block_rows), side_space] for number in range(4)
        ]
        rows_in[...] = jnp.zeros_like(rows_in)
        share = Share(place, counts, (fresh, rows_in, hidden_two, back), share_sems)
        tile_sum = TileSum(place, tiles, tile_boxes, tile_sems)
        due = spread.steps()
        load.wait()
        spread.fill(held)
        place.greet(True, True)
        spread.begin()
    else:
        place.greet(False)
        loads = [
            pltpu.make_async_copy(src, dst, sem_local.at[8 + slot])
            for slot, (src, dst) in enumerate(zip((first_in, middle_in, last_in), weights))
        ]
        for load in loads:
            load.start()
        due = []

    quarter = half // 2
    own_rows = pl.ds(pl.multiple_of(core * count_rows, count_rows), count_rows)
    mate_rows = pl.ds(pl.multiple_of((1 - core) * count_rows, count_rows), count_rows)
    top_rows = pl.ds(0, count_rows)
    own_copies = [
        pltpu.make_async_copy(
            features.at[own_rows, pl.ds(side * quarter, quarter)], buffer, sem_local.at[side]
        )
        for side, buffer in enumerate((hidden_two, mid_wide.at[top_rows, :]))
    ]
    per_kind = params.shape[0] // 2
    for kind in range(2):
        rows = [params[kind * per_kind + spot : kind * per_kind + spot + 1, :] for spot in range(per_kind)]
        params_all[core, kind : kind + 1, :] = jnp.concatenate(rows, axis=1)
    head_all[core] = jnp.zeros(head_all.shape[1:], low_type)
    for spot in range(half // LANES):
        head_all[core, 0:classes, spot * LANES : (spot + 1) * LANES] = head[
            pl.ds(spot, classes, stride=half // LANES), :
        ].astype(low_type)
    to_mate = [
        remote(params_all.at[core], params_all.at[core], sem_misc.at[0, 0], sem_misc.at[1, 0], *mate),
        remote(head_all.at[core], head_all.at[core], sem_misc.at[0, 1], sem_misc.at[1, 1], *mate),
    ]
    for side, buffer in enumerate((taps_one, taps_two)):
        to_mate.append(
            remote(
                features.at[mate_rows, pl.ds(side * quarter, quarter)],
                buffer.at[top_rows, :],
                sem_misc.at[0, 5 + side],
                sem_misc.at[1, 5 + side],
                *mate,
            )
        )
    for copy in to_mate + own_copies:
        copy.start()

    def advance(count):
        for group in due[:count]:
            for step in group:
                step()
        del due[:count]

    def advance_at(index, spots):
        for spot, group in zip(spots, due):

            @pl.when(index == spot)
            def _():
                for step in group:
                    step()

    def arrive(slot, left):
        if gather:
            advance(len(due) - left)
            spread.arrive(slot)
        else:
            loads[slot].wait()

    def arrive_turns(slot, turns):
        if gather:
            for turn in turns:
                for copy in spread.core_copies(turn, slot):
                    copy.wait_recv()

    def fold_step(kind, slot, which):
        if gather:
            (fold.core_step, fold.near_step, fold.far_step)[kind](which, slot)

    def fold_at(index, spot, *steps):
        @pl.when(index == spot)
        def _():
            for step in steps:
                fold_step(*step)

    def fold_begin(which, slot):
        if gather:
            fold.begin(which, slot)

    def zero_edges(buffer):
        edge = jnp.zeros((line,) + buffer.shape[1:], low_type)
        buffer[0:line, :] = edge
        buffer[line + count_rows : 2 * line + count_rows, :] = edge

    advance(3)
    for copy in own_copies:
        copy.wait()

    def turn_from(source, base):
        def turn(index, carry):
            stage[...] = source(lanes(index, LANES)).astype(wide)

            def pixel(spot, inner):
                x_all[
                    pl.ds(pl.multiple_of(spot * mine_images, mine_images), mine_images),
                    pl.ds(pl.multiple_of(base + index * LANES, LANES), LANES),
                ] = stage[pl.ds(spot, mine_images, stride=PIXELS), :].astype(low_type)
                return inner

            return lax.fori_loop(0, PIXELS, pixel, carry, unroll=7)

        return turn

    quarters = quarter // LANES
    own_base, mate_base = core * half, (1 - core) * half
    lax.fori_loop(0, quarters, turn_from(lambda columns: hidden_two[:, columns], own_base), 0)
    advance(1)
    lax.fori_loop(
        0,
        quarters,
        turn_from(lambda columns: mid_wide[0:count_rows, columns], own_base + quarter),
        0,
    )
    advance(1)
    for copy in to_mate:
        copy.wait_recv()
    lax.fori_loop(0, quarters, turn_from(lambda columns: taps_one[0:count_rows, columns], mate_base), 0)
    advance(1)
    lax.fori_loop(0, quarters, turn_from(lambda columns: taps_two[0:count_rows, columns], mate_base + quarter), 0)
    zero_edges(taps_one)
    zero_edges(taps_two)
    arrive(0, 9)

    def swap(slot, size):
        return remote(
            sums_mine.at[slot, :, pl.ds(0, size)],
            sums_theirs.at[slot, :, pl.ds(0, size)],
            sem_swap.at[0, slot],
            sem_swap.at[1, slot],
            *mate,
        )

    def gain_bias(lower, upper):
        rows = []
        for kind in range(2):
            pieces = [params_all[side, kind : kind + 1, lower:upper] for side in range(2)]
            rows.append(jnp.concatenate(pieces, axis=1))
        return rows

    def collect(index, value, columns, size):
        @pl.when(index == 0)
        def _():
            shift[0:1, pl.ds(0, size)] = column_sum(fold_rows(value)) / value.shape[0]
            shift[8:24, pl.ds(0, size)] = jnp.zeros((16, size), wide)

        gap = value - shift[0:1, pl.ds(0, size)]
        shift[8:16, pl.ds(0, size)] += fold_rows(gap)
        shift[16:24, pl.ds(0, size)] += fold_rows(gap * gap)

    def close_stats(slot, columns, size):
        sum_gap = column_sum(shift[8:16, pl.ds(0, size)])
        sum_square = column_sum(shift[16:24, pl.ds(0, size)])
        sums_mine[slot, 0:1, columns] = shift[0:1, pl.ds(0, size)] + sum_gap / count_rows
        sums_mine[slot, 1:2, columns] = sum_square - sum_gap * sum_gap / count_rows

    def look_over(act, columns):
        def look(index, carry):
            collect(index, act[tile(index), columns], None, width)
            return carry

        lax.fori_loop(0, SIDE, look, 0)

    groups = SPOTS[0]
    group = channels // groups

    def settle(slot, size):
        mean, scale = norm_stats(
            sums_mine[slot, 0:2, pl.ds(0, size)], sums_theirs[slot, 0:2, pl.ds(0, size)], float(count_rows)
        )
        fwd_stats[slot, 0:1, pl.ds(0, size)] = mean
        fwd_stats[slot, 1:2, pl.ds(0, size)] = scale

    whole_width = pl.ds(0, width)

    def first_part(index, carry):
        kernel = flat_rows(w_first[index])
        for side in range(2):
            columns = slice(side * width // 2, (side + 1) * width // 2)
            act_one[:, columns] += dot_nn(x_all[:, lanes(index, group)], kernel[:, columns])
        advance_at(index, (0, 1, 2))
        return carry

    act_one[...] = jnp.zeros_like(act_one)
    lax.fori_loop(0, groups, first_part, 0)
    del due[:3]
    look_over(act_one, whole_width)
    close_stats(0, whole_width, width)
    move = swap(0, width)
    move.start()
    advance(1)
    move.wait()
    settle(0, width)

    gain_one, bias_one = gain_bias(0, part)
    gain_two, bias_two = gain_bias(part, width)
    gain_three, bias_three = gain_bias(width, width + half)

    def normal(act, slot, index):
        mean = fwd_stats[slot, 0:1, pl.ds(0, width)]
        return (act[tile(index), :] - mean) * fwd_stats[slot, 1:2, pl.ds(0, width)]

    def hide_one(index, carry):
        value = normal(act_one, 0, index) * gain_one + bias_one
        taps_one[pl.ds(pl.multiple_of((index + 1) * line, line), line), :] = (value * sigmoid(value)).astype(low_type)
        return carry

    lax.fori_loop(0, SIDE, hide_one, 0)
    if gather:
        arrive_turns(1, (0, 1))
    else:
        arrive(1, 0)

    step = mine_images
    piece = width // 2

    def row_windows(buffer, down, start, reach):
        if reach == line:
            return buffer[pl.ds(pl.multiple_of(down * line, line), count_rows), :]
        windows = [
            buffer[pl.ds(pl.multiple_of((down + row) * line + start, step), reach), :] for row in range(SIDE)
        ]
        return jnp.concatenate(windows, axis=0)

    def add_windows(target, columns, value, start, reach):
        for row in range(SIDE):
            rows = slice(row * line + start, row * line + start + reach)
            target[rows, columns] += value[row * reach : (row + 1) * reach]

    low_start, high_start, reaches = (0, 0, step), (step, 0, 0), (line - step, line, line - step)

    early, taps = 4, 9

    def second_part(index, carry):
        tap = jnp.where(place.z < 2, index, (index + taps - early) % taps) if gather else index

        @pl.when(index == early)
        def _():
            arrive_turns(1, (2, 3))

        down = tap // 3
        for over in range(3):

            @pl.when(tap % 3 == over)
            def _():
                left = row_windows(taps_one, down, low_start[over], reaches[over])
                rows = pl.ds(pl.multiple_of(tap * width, width), width)
                for side in range(2):
                    columns = slice(side * piece, (side + 1) * piece)
                    value = dot_nn(left, w_middle[rows, columns])
                    add_windows(act_two, columns, value, high_start[over], reaches[over])

        advance_at(index, (2, 5, 6, 8))
        return carry

    act_two[...] = jnp.zeros_like(act_two)
    lax.fori_loop(0, taps, second_part, 0)
    del due[:4]
    look_over(act_two, whole_width)
    close_stats(1, whole_width, width)
    move_two = swap(1, width)
    move_two.start()
    move_two.wait()
    settle(1, width)

    arrive(2, 0)

    def third_line(index, carry):
        value = normal(act_two, 1, index) * gain_two + bias_two
        hidden = (value * sigmoid(value)).astype(low_type)
        hidden_two[tile(index), :] = hidden
        for which in range(groups):
            columns = slice(which * group, (which + 1) * group)
            value = dot_nt(hidden, flat_rows(w_last[which]))
            act_three[tile(index), columns] = value
            start = jnp.where(index == 0, column_sum(value[0:8]) / 8.0, shift[0:1, columns])
            gap = value - start
            kept_sums = jnp.where(index == 0, 0.0, shift[8:24, columns])
            shift[0:1, columns] = start
            shift[8:16, columns] = kept_sums[0:8] + fold_rows(gap)
            shift[16:24, columns] = kept_sums[8:16] + fold_rows(gap * gap)
        return carry

    lax.fori_loop(0, SIDE, third_line, 0)
    close_stats(2, pl.ds(0, channels), channels)
    move_three = swap(2, channels)
    move_three.start()
    move_three.wait()
    settle(2, channels)

    per_group = group // LANES

    def block_of(spot):
        return pl.ds(pl.multiple_of(spot * mine_images, mine_images), mine_images)

    def mid_line(which, index):
        return pl.ds(pl.multiple_of(which * count_rows + index * line, line), line)

    kept = channels // LANES * mine_images

    def gathered(kind):
        starts = range(kind * kept, (kind + 1) * kept, mine_images)
        return jnp.concatenate([stage[start : start + mine_images, :] for start in starts], axis=1)

    fwd_stats[2, 4:5, :] = fwd_stats[2, 1:2, :] * gain_three
    fwd_stats[2, 5:6, :] = bias_three - fwd_stats[2, 0:1, :] * fwd_stats[2, 4:5, :]

    def emit(index, carry):
        columns = lanes(index, LANES)
        slant, level = fwd_stats[2, 4:5, columns], fwd_stats[2, 5:6, columns]

        def pixels(row, sums):
            pooled, steeps, steeps_act = sums
            found = []
            for spot in range(SIDE):
                where = block_of(row * SIDE + spot)
                act = act_three[where, columns]
                half_total = 0.5 * (act * slant + level + x_all[where, columns].astype(wide))
                rise = 1.0 + jnp.tanh(half_total)
                out = half_total * rise
                steep = rise + out * (2.0 - rise)
                found.append(steep.astype(low_type))
                pooled, steeps, steeps_act = pooled + out, steeps + steep, steeps_act + steep * act
            mid_wide[mid_line(index // per_group, row), lanes(index % per_group, LANES)] = jnp.concatenate(
                found, axis=0
            )
            return pooled, steeps, steeps_act

        zero = jnp.zeros((mine_images, LANES), wide)
        sums = lax.fori_loop(0, SIDE, pixels, (zero, zero, zero))
        for kind, value in enumerate(sums):
            stage[pl.ds(pl.multiple_of(kind * kept + index * mine_images, mine_images), mine_images), :] = value
        return carry

    lax.fori_loop(0, channels // LANES, emit, 0)

    pooled = (gathered(0) / PIXELS).astype(low_type)
    head_full = jnp.concatenate([head_all[0], head_all[1]], axis=1)
    logits = dot_nt(head_full, pooled)
    spots = lax.broadcasted_iota(jnp.int32, logits.shape, 0)
    inside = spots < classes
    first_labels, second_labels = labels[0:1, 0:mine_images], labels[0:1, mine_images:]
    onehot = (spots == jnp.where(core == 0, first_labels, second_labels)).astype(wide)
    top = jnp.max(jnp.where(inside, logits, -jnp.inf), axis=0, keepdims=True)
    powers = jnp.where(inside, jnp.exp(logits - top), 0.0)
    power_sum = jnp.sum(powers, axis=0, keepdims=True)
    picked = jnp.sum(logits * onehot, axis=0, keepdims=True)
    each_loss = top + jnp.log(power_sum) - picked
    taking = flag[0].astype(wide)
    tile_spots = lax.broadcasted_iota(jnp.int32, loss_out.shape, 1)
    loss_out[...] = jnp.where(tile_spots == 0, taking * jnp.sum(each_loss), taking * mine_images)
    grads = (taking / images * (powers / power_sum - onehot)).astype(low_type)
    grad_pool[...] = dot_tn(grads, head_full) * (0.5 / PIXELS)
    logit_grads[core] = grads
    pool_all[core] = pooled[:, 0:half]
    pool_send[...] = pooled[:, half:]

    @pl.when(core == 1)
    def _():
        pool_all[core] = pooled[:, half:]
        pool_send[...] = pooled[:, 0:half]

    head_moves = [
        remote(pool_send, pool_all.at[core], sem_misc.at[0, 3], sem_misc.at[1, 3], *mate),
        remote(logit_grads.at[core], logit_grads.at[core], sem_misc.at[0, 4], sem_misc.at[1, 4], *mate),
    ]

    steeps = gathered(1)
    steeps_normed = (gathered(2) - fwd_stats[2, 0:1, :] * steeps) * fwd_stats[2, 1:2, :]
    sums_mine[3, 0:1, :] = column_sum(grad_pool[...] * steeps)
    sums_mine[3, 1:2, :] = column_sum(grad_pool[...] * steeps_normed)
    move_back = swap(3, channels)
    move_back.start()
    for copy in head_moves:
        copy.start()
    move_back.wait()

    def back_terms(slot, layer, size, gain):
        columns = pl.ds(0, size)
        sums = sums_mine[slot, 0:2, columns] + sums_theirs[slot, 0:2, columns]
        sums_mine[slot, 2:4, columns] = sums
        scale = fwd_stats[layer, 1:2, columns]
        return (
            scale * gain,
            scale * gain * sums[0:1] / total_rows,
            scale * scale * gain * sums[1:2] / total_rows,
        )

    first, second, third = back_terms(3, 2, channels, gain_three)
    fwd_stats[2, 4:5, :] = second - third * fwd_stats[2, 0:1, :]
    fwd_stats[2, 5:6, :] = third
    grad_pool[...] = grad_pool[...] * first

    def pull(index):
        for which in range(groups):
            columns = slice(which * group, (which + 1) * group)
            reach = grad_pool[:, columns]
            steep = mid_wide[mid_line(which, index), :].astype(wide)
            value = jnp.concatenate([reach] * SIDE, axis=0) * steep
            value = value - fwd_stats[2, 4:5, columns] - fwd_stats[2, 5:6, columns] * act_three[tile(index), columns]
            mid_wide[mid_line(which, index), :] = value.astype(low_type)

    pull(0)
    for copy in head_moves:
        copy.wait_recv()
    head_grad = dot_nn(logit_grads[0], pool_all[0]) + dot_nn(logit_grads[1], pool_all[1])
    for spot in range(half // LANES):
        stage[pl.ds(spot, classes, stride=half // LANES), :] = head_grad[
            0:classes, spot * LANES : (spot + 1) * LANES
        ]
    head_space = stage.at[pl.ds(0, grad_head_out.shape[0]), :]
    head_leave = pltpu.make_async_copy(head_space, grad_head_out, sem_local.at[0])
    head_leave.start()

    def drop_into(act, slot, gain, bias, columns):
        size = pl.ds(0, width)
        shift[8:24, size] = jnp.zeros((16, width), wide)

        def drop(index, carry):
            normed = normal(act, slot, index)
            norm = normed * gain + bias
            sig = sigmoid(norm)
            grad = act_three[tile(index), columns] * (sig + norm * sig * (1.0 - sig))
            act_three[tile(index), columns] = grad
            shift[8:16, size] += fold_rows(grad)
            shift[16:24, size] += fold_rows(grad * normed)
            return carry

        lax.fori_loop(0, SIDE, drop, 0)

    def close_back(slot):
        size = pl.ds(0, width)
        sums_mine[slot, 0:1, size] = column_sum(shift[8:16, size])
        sums_mine[slot, 1:2, size] = column_sum(shift[16:24, size])

    space_two, space_one = pl.ds(0, width), pl.ds(width, width)

    def mid_group(which):
        return mid_wide[pl.ds(pl.multiple_of(which * count_rows, count_rows), count_rows), :]

    def back_two(index):
        left = jnp.concatenate([mid_wide[mid_line(which, index), :] for which in range(groups)], axis=1)
        value = dot_nn(left, flat_rows(w_last[...]))
        normed = normal(act_two, 1, index)
        norm = normed * gain_two + bias_two
        sig = sigmoid(norm)
        grad = value * (sig + norm * sig * (1.0 - sig))
        act_three[tile(index), space_two] = grad
        size = pl.ds(0, width)
        shift[8:16, size] += fold_rows(grad)
        shift[16:24, size] += fold_rows(grad * normed)

    def back_two_line(index, carry):
        pull(index + 1)
        back_two(index)
        return carry

    shift[8:24, :] = jnp.zeros((16, channels), wide)
    lax.fori_loop(0, SIDE - 1, back_two_line, 0)
    back_two(SIDE - 1)
    close_back(4)
    move_back_two = swap(4, width)
    move_back_two.start()
    if gather:
        base_loads = [
            pltpu.make_async_copy(src, dst, sem_local.at[1 + number])
            for number, (src, dst) in enumerate(
                ((master, held_base), (momentum, held_momentum), (anchor, held_anchor))
            )
        ]
        for load in base_loads:
            load.start()
        tiles[0] = loss_out[...]
        tile_sum.start()

    def settle_section(slot):
        if gather:
            rows = share.section(slot)
            grad = fold.result(slot) + prox_weight * (held_base[rows, :] - held_anchor[rows, :])
            fresh[rows, :] = momentum_decay * held_momentum[rows, :] + grad
            share.send(slot)

    if gather:
        spread.drain()

    def put(ref, which, value):
        ref[which] = value.astype(low_type).reshape(ref.shape[1:])

    def expand_group(which, carry):
        put(w_last, which, dot_tn(mid_group(which), hidden_two[...]))
        fold_begin(which, 2)
        fold_at(which, 2, (0, 2, 0))
        fold_at(which, 3, (0, 2, 1))
        return carry

    lax.fori_loop(0, groups, expand_group, 0)
    move_back_two.wait()
    terms_two = back_terms(4, 1, width, gain_two)

    def back_act(terms, act, layer, index, columns):
        first, second, third = terms
        gap = act[tile(index), :] - fwd_stats[layer, 0:1, pl.ds(0, width)]
        return (first * act_three[tile(index), columns] - second - third * gap).astype(low_type)

    def grad_two(index, carry):
        taps_two[pl.ds(pl.multiple_of((index + 1) * line, line), line), :] = back_act(
            terms_two, act_two, 1, index, space_two
        )
        return carry

    lax.fori_loop(0, SIDE, grad_two, 0)
    fold_step(0, 2, 2)
    fold_step(1, 2, 0)
    core_step, near_step, far_step = 0, 1, 2
    plan = {
        0: [(core_step, 2, 3)],
        1: [(near_step, 2, 1)],
        2: [(far_step, 2, 0), (near_step, 2, 2)],
        3: [(far_step, 2, 1), (near_step, 2, 3)],
        4: [(far_step, 2, 2)],
        5: [(far_step, 2, 3), (core_step, 1, 0)],
        7: [(core_step, 1, 1)],
    }

    def middle_row(down, carry):
        for over in range(3):
            left = row_windows(taps_one, down, low_start[over], reaches[over])
            right = row_windows(taps_two, 1, high_start[over], reaches[over])
            rows = pl.ds(pl.multiple_of((3 * down + over) * width, width), width)
            mid_wide[rows, :] = dot_tn(left, right).astype(low_type)
            for row in range(3):
                tap = 3 * row + over

                @pl.when(down == row)
                def _():
                    if tap >= 2 and tap % 2 == 0:
                        fold_begin(tap // 2 - 1, 1)
                    for step in plan.get(tap, ()):
                        fold_step(*step)

        return carry

    lax.fori_loop(0, 3, middle_row, 0)
    if gather:
        tile_sum.pair(0)
        for load in base_loads:
            load.wait()

    def back_one(index, carry):
        down, side = index // 2, index % 2
        columns = lanes(2 + side, piece)
        for over in range(3):
            left = row_windows(taps_two, 2 - down, high_start[over], reaches[over])
            start = pl.multiple_of((3 * down + over) * width + side * piece, piece)
            value = dot_nt(left, w_middle[pl.ds(start, piece), :])
            add_windows(act_three, columns, value, low_start[over], reaches[over])
        fold_at(index, 0, (core_step, 1, 2), (near_step, 1, 0))
        fold_at(index, 1, (core_step, 1, 3))
        fold_at(index, 2, (near_step, 1, 1), (far_step, 1, 0))
        fold_at(index, 4, (far_step, 1, 1))
        fold_at(index, 5, (near_step, 1, 2))
        return carry

    act_three[:, space_one] = jnp.zeros((count_rows, width), wide)
    lax.fori_loop(0, 6, back_one, 0)
    drop_into(act_one, 0, gain_one, bias_one, space_one)
    fold_step(near_step, 1, 3)
    settle_section(2)
    close_back(5)
    move_back_one = swap(5, width)
    move_back_one.start()

    move_back_one.wait()
    terms_one = back_terms(5, 0, width, gain_one)

    def grad_one(index, carry):
        hidden_two[tile(index), :] = back_act(terms_one, act_one, 0, index, space_one)
        return carry

    lax.fori_loop(0, SIDE, grad_one, 0)
    fold_step(far_step, 1, 2)
    if gather:
        tile_sum.pair(1)

    def reduce_group(which, carry):
        put(w_first, which, dot_tn(x_all[:, lanes(which, group)], hidden_two[...]))
        fold_begin(which, 0)
        fold_at(which, 0, (far_step, 1, 3))
        fold_at(which, 2, (core_step, 0, 0))
        fold_at(which, 3, (core_step, 0, 1), (near_step, 0, 0))
        return carry

    lax.fori_loop(0, groups, reduce_group, 0)

    for kind in range(2):
        row = 3 - kind
        pieces = [
            sums_mine[5, row : row + 1, lanes(core, part)],
            sums_mine[4, row : row + 1, lanes(core, part)],
            sums_mine[3, row : row + 1, lanes(core, half)],
        ]
        whole = jnp.concatenate(pieces, axis=1)
        per_kind = whole.shape[1] // LANES
        for spot in range(per_kind):
            grad_norm_out[kind * per_kind + spot : kind * per_kind + spot + 1, :] = whole[
                :, spot * LANES : (spot + 1) * LANES
            ]
    for step in (
        (core_step, 0, 2),
        (core_step, 0, 3),
        (far_step, 0, 0),
        (near_step, 0, 1),
        (near_step, 0, 2),
        (far_step, 0, 1),
        (near_step, 0, 3),
        (far_step, 0, 2),
        (far_step, 0, 3),
    ):
        fold_step(*step)
        if step == (far_step, 0, 0):
            settle_section(1)
    if gather:
        settle_section(0)
        leave = pltpu.make_async_copy(fresh, fresh_out, sem_local.at[1])
        leave.start()
        tile_sum.pair(2)
        part = width // CUTS
        gram = act_three.at[pl.ds(0, gram_total.shape[0]), pl.ds(half + width, 2 * part)]
        corner_rows = pl.ds(gram_total.shape[0], width)
        squares = [act_three.at[corner_rows, pl.ds(spot * width, width)] for spot in (0, 1, 3)]
        gram_sum = GramSum(place, gram, gram_total, (y_box, z_box), gram_sems)
        orthogonal(place, ratios, share, share_sems, gram, gram_total, mate_gram, gram_sum, squares, rows_in, hidden_two)
        share.finish()
        loss_out[...] = tile_sum.result()
        ortho_leave = pltpu.make_async_copy(back, ortho_out, sem_local.at[2])
        ortho_leave.start()
        gram_sum.drain()
        tile_sum.drain()
        fold.drain()
        leave.wait()
        ortho_leave.wait()
    else:
        outs = [
            pltpu.make_async_copy(ref, out, sem_local.at[slot])
            for slot, (ref, out) in enumerate(zip((w_first, mid_wide.at[pl.ds(0, 9 * width), :], w_last), grads_out))
        ]
        for copy in outs:
            copy.start()
        for copy in outs:
            copy.wait()
    head_leave.wait()
    for copy in to_mate + head_moves:
        copy.wait_send()


def client_pass(gather, ratios, classes, features, labels, flag, params, head, weights):
    pixels, half = features.shape
    images = labels.shape[1]
    count_rows, channels = pixels // 2, 2 * half
    width = params.shape[0] // 2 * LANES - half
    head_rows = classes + -classes % 16
    mine_images = images // 2
    line = SIDE * mine_images
    middle = 9 * width
    blocks = 32
    group = channels // SPOTS[0]
    vmem = pl.BlockSpec(memory_space=pltpu.VMEM)
    smem = pl.BlockSpec(memory_space=pltpu.SMEM)
    spots = SPOTS + (2,)
    scratch = [
        pltpu.VMEM((count_rows, channels), low_type),
        pltpu.VMEM((SPOTS[0] * count_rows, group), low_type),
        pltpu.VMEM(spots + (channels // blocks, width), low_type),
        pltpu.VMEM((middle, width), low_type),
        pltpu.VMEM(spots + (channels // blocks, width), low_type),
        pltpu.VMEM((count_rows, width), wide),
        pltpu.VMEM((count_rows, width), wide),
        pltpu.VMEM((count_rows, channels), wide),
        pltpu.VMEM((count_rows + 2 * line, width), low_type),
        pltpu.VMEM((count_rows + 2 * line, width), low_type),
        pltpu.VMEM((count_rows, width), low_type),
        pltpu.VMEM((count_rows, LANES), wide),
        pltpu.VMEM((2, 2, half + width), wide),
        pltpu.VMEM((2, head_rows, half), low_type),
        pltpu.VMEM((mine_images, channels), wide),
        pltpu.VMEM((mine_images, half), low_type),
        pltpu.VMEM((2, mine_images, half), low_type),
        pltpu.VMEM((2, head_rows, mine_images), low_type),
        pltpu.VMEM((6, 8, channels), wide),
        pltpu.VMEM((6, 8, channels), wide),
        pltpu.VMEM((24, channels), wide),
        pltpu.VMEM((3, 8, channels), wide),
        pltpu.SemaphoreType.DMA((11,)),
        pltpu.SemaphoreType.DMA((2, 6)),
        pltpu.SemaphoreType.DMA((2, 7)),
    ]
    any_space = pl.BlockSpec(memory_space=pl.ANY)
    if gather:
        counts = (channels // blocks, middle // blocks, channels // blocks)
        scratch += [pltpu.SemaphoreType.DMA((2, 3, 3))]
        scratch += [pltpu.SemaphoreType.DMA((2, 4, size)) for size in (6, 8, 6)]
        scratch += [pltpu.VMEM((4, 2, 2, rows, width), low_type) for rows in counts[1:]]
        for lead in ((4, 2), (4,), (4,)):
            scratch += [pltpu.VMEM(lead + (rows, width), low_type) for rows in counts]
        scratch += [pltpu.SemaphoreType.DMA((2, 4, size)) for size in (6, 8, 6, 6)]
        part = width // CUTS
        gram_rows = CUTS * (CUTS + 1) // 4 * part
        many = max(4 * counts[0], 2 * counts[1])
        scratch += [
            pltpu.VMEM((many, width), wide),
            pltpu.VMEM((sum(counts), width), low_type),
            pltpu.VMEM((4, 8, LANES), wide),
            pltpu.VMEM((6, 8, LANES), wide),
            pltpu.VMEM((gram_rows, 2 * part), wide),
            pltpu.VMEM((4, gram_rows // 8, 2 * part), wide),
            pltpu.VMEM((3, gram_rows // 8, 2 * part), wide),
            pltpu.VMEM((gram_rows, 2 * part), wide),
            pltpu.SemaphoreType.DMA((2, 6)),
            pltpu.SemaphoreType.DMA((2, 8)),
            pltpu.SemaphoreType.DMA((2, 14)),
        ]
        grads_shape = [
            jax.ShapeDtypeStruct((sum(counts), width), wide),
            jax.ShapeDtypeStruct((sum(counts), width), low_type),
        ]
        grads_specs = [any_space] * 2
    else:
        grads_shape = [jax.ShapeDtypeStruct(weight.shape, low_type) for weight in weights]
        grads_specs = [any_space] * 3
    return pl.pallas_call(
        functools.partial(client_kernel, gather, ratios, images, classes),
        out_shape=grads_shape
        + [
            jax.ShapeDtypeStruct(params.shape, wide),
            jax.ShapeDtypeStruct((classes * half // LANES, LANES), wide),
            jax.ShapeDtypeStruct((8, LANES), wide),
        ],
        in_specs=[any_space, vmem, smem, vmem, vmem] + [any_space] * len(weights),
        out_specs=grads_specs + [vmem, any_space, vmem],
        scratch_shapes=scratch,
        compiler_params=pltpu.CompilerParams(
            collective_id=0, has_side_effects=True, vmem_limit_bytes=VMEM_BYTES
        ),
    )(features, labels, flag, params, head, *weights)


def adam_update(param, grad, first, second, rate, decay):
    first = adam_first * first + (1.0 - adam_first) * grad
    second = adam_second * second + (1.0 - adam_second) * grad * grad
    first_hat = first / (1.0 - adam_first**STEP)
    second_hat = second / (1.0 - adam_second**STEP)
    return (
        param - rate * (first_hat / (jnp.sqrt(second_hat) + adam_epsilon) + decay * param),
        first,
        second,
    )


def gram_of(section):
    return lax.dot_general(section, section, (((0,), (0,)), ((), ())), precision=precise)


def square(gram):
    return jnp.dot(gram, gram, precision=precise)


def times_poly(left, mixed):
    return schulz_first * left + jnp.dot(left, mixed, precision=precise)


def schulz(sections):
    raw_grams = lax.psum(tuple(gram_of(section) for section in sections), ("client", "chan"))
    factors = [1.0 / (jnp.sqrt(jnp.trace(gram)) + 1e-07) for gram in raw_grams]
    current = [section * factor for section, factor in zip(sections, factors)]
    grams = [gram * (factor * factor) for gram, factor in zip(raw_grams, factors)]
    for turn in range(NS_STEPS):
        mixed = [schulz_second * gram + schulz_third * square(gram) for gram in grams]
        current = [times_poly(current[slot], mixed[slot]) for slot in range(3)]
        if turn + 1 < NS_STEPS:
            grams = [
                times_poly(times_poly(grams[slot], mixed[slot]), mixed[slot]) for slot in range(3)
            ]
    return current


def base_far(ratios, bounds, master, momentum, anchor, loss_tile, grads):
    sums = [
        lax.psum_scatter(flat_rows(grad).astype(wide), ("client", "chan"), scatter_dimension=0, tiled=True)
        for grad in grads
    ]
    grad_base = jnp.concatenate(sums, axis=0)
    momentum_new = momentum_decay * momentum + (grad_base + prox_weight * (master - anchor))
    current = schulz([momentum_new[bounds[slot] : bounds[slot + 1]] for slot in range(3)])
    ortho = jnp.concatenate([current[slot] * ratios[slot] for slot in range(3)], axis=0)
    return momentum_new, ortho, lax.psum(loss_tile, ("client", "chan"))


def as_stored(rows, shape):
    return with_layout_constraint(rows.reshape(shape), Layout(major_to_minor=tuple(range(len(shape)))))


def on_device(
    features,
    labels,
    mask,
    base_master,
    base_momentum,
    global_base,
    norm_params,
    norm_first,
    norm_second,
    head,
    head_first,
    head_second,
):
    halves = lax.axis_size("chan")
    blocks = lax.axis_size("client") * halves
    half = features.shape[2]
    width = base_master.shape[2]
    channels = half * halves
    classes = head.shape[2]
    rows_first = channels // blocks
    rows_mid = 9 * width // blocks
    bounds = (0, rows_first, rows_first + rows_mid, base_master.shape[1])
    ratio = (channels / width) ** 0.5
    ratios = (ratio, 3.0, ratio)
    master, momentum, anchor = base_master[0], base_momentum[0], global_base[0]
    norms = [value.reshape(-1, LANES) for value in (norm_params, norm_first, norm_second)]
    heads = [jnp.transpose(value, (2, 0, 1)).reshape(-1, LANES) for value in (head, head_first, head_second)]
    near = lax.axis_size("client") == SPOTS[0] * SPOTS[1] * SPOTS[2]
    if near:
        weights = [master, momentum, anchor]
    else:
        low_master = master.astype(low_type)
        weights = [
            lax.all_gather(low_master[bounds[slot] : bounds[slot + 1]], ("client", "chan"), axis=0, tiled=True)
            for slot in range(3)
        ]
        split = SPOTS + (2, channels // 32, width)
        weights = [weights[0].reshape(split), weights[1], weights[2].reshape(split)]
    *grads, grad_norm, grad_head, loss_tile = client_pass(
        near, ratios, classes, features[0], labels, mask, norms[0], heads[0], weights
    )
    if near:
        fresh_momentum, ortho = grads
    else:
        fresh_momentum, ortho, loss_tile = base_far(ratios, bounds, master, momentum, anchor, loss_tile, grads)
    loss, momentum_new, base_new, base_low, *fresh = update_pass(
        loss_tile, master, fresh_momentum, ortho, norms, grad_norm, heads, grad_head
    )
    fresh_norms = [as_stored(value, norm_params.shape) for value in fresh[:3]]
    fresh_heads = [jnp.transpose(as_stored(value, (classes, 1, half)), (1, 2, 0)) for value in fresh[3:]]
    return (
        loss,
        base_new[None],
        momentum_new[None],
        base_low[None],
        *fresh_norms,
        *fresh_heads,
    )


def solution(mesh):
    wide_block = P(("client", "chan"), None, None)
    norm_block = P("client", None, "chan", None)
    head_block = P("client", "chan", None)
    return jax.shard_map(
        on_device,
        mesh=mesh,
        in_specs=(P("client", None, "chan"), P("client", None), P("client"))
        + (wide_block,) * 3
        + (norm_block,) * 3
        + (head_block,) * 3,
        out_specs=(P(),) + (wide_block,) * 3 + (norm_block,) * 3 + (head_block,) * 3,
        check_vma=False,
    )
```

```python
import functools

import jax
import jax.numpy as jnp
from jax import lax
from jax.experimental import pallas as pl
from jax.experimental.layout import Layout, with_layout_constraint
from jax.experimental.pallas import tpu as pltpu
from jax.sharding import PartitionSpec as P

NS_STEPS = 5
STEP = 10

low_type = jnp.bfloat16
wide = jnp.float32
MESH = pl.DeviceIdType.MESH
precise = lax.Precision.HIGHEST
norm_epsilon = 1e-05
prox_weight = 0.05
momentum_decay = 0.95
muon_rate = 0.3
muon_decay = 0.1
schulz_first = 3.4445
schulz_second = -4.775
schulz_third = 2.0315
adam_first = 0.9
adam_second = 0.95
adam_epsilon = 1e-08
head_rate = 0.01
head_decay = 0.05
norm_rate = 0.5

SIDE = 7
PIXELS = SIDE * SIDE
LANES = 128
SPOTS = (4, 2, 2)
CUTS = 4
VMEM_BYTES = 62 * 2**20


def dot_nn(left, right):
    return jnp.dot(left, right, preferred_element_type=wide)


def dot_nt(left, right):
    return lax.dot_general(left, right, (((1,), (1,)), ((), ())), preferred_element_type=wide)


def dot_tn(left, right):
    return lax.dot_general(left, right, (((0,), (0,)), ((), ())), preferred_element_type=wide)


def flat_rows(block):
    return block.reshape(-1, block.shape[-1])


def sigmoid(value):
    return 0.5 * jnp.tanh(0.5 * value) + 0.5


def fold_rows(value):
    return jnp.sum(value.reshape(value.shape[0] // 8, 8, value.shape[1]), axis=0)


def column_sum(value):
    return jnp.sum(value, axis=0, keepdims=True)


def remote(src, dst, send_sem, recv_sem, client, core):
    return pltpu.make_async_remote_copy(
        src_ref=src,
        dst_ref=dst,
        send_sem=send_sem,
        recv_sem=recv_sem,
        device_id=(client, core),
        device_id_type=MESH,
    )


class Place:
    def __init__(self):
        self.client = lax.axis_index("client")
        self.core = lax.axis_index("chan")
        self.z = self.client // 4
        self.y = (self.client // 2) % 2
        self.x = self.client % 2
        self.others = [
            self.z + 1 - 2 * (self.z % 2),
            (self.z + 2) % 4,
            3 - self.z,
        ]

    def at(self, z, y, x):
        return z * 4 + y * 2 + x

    def along_x(self):
        return self.at(self.z, self.y, 1 - self.x)

    def along_y(self):
        return self.at(self.z, 1 - self.y, self.x)

    def along_z(self, step):
        return self.at(self.others[step], self.y, self.x)

    def greet(self, whole, across=False):
        barrier = pltpu.get_barrier_semaphore()
        pairs = [(self.client, 1 - self.core)]
        if whole:
            pairs += [(self.along_x(), self.core), (self.along_y(), self.core)]
            pairs += [(self.along_z(step), self.core) for step in range(3)]
        if across:
            pairs += [(self.along_x(), 1 - self.core)]
        for pair in pairs:
            pl.semaphore_signal(barrier, inc=1, device_id=pair, device_id_type=MESH)
        pl.semaphore_wait(barrier, len(pairs))


def cut_rows(counts):
    pieces = []
    for slot, rows in enumerate(counts):
        middle = (rows // 16 + 1) // 2 * 16
        pieces.append((slot, 0, middle, 0))
        pieces.append((slot, middle, rows - middle, 1))
    return pieces


def block_ref(ref, size, z, y, x, core, start, count):
    if len(ref.shape) == 2:
        first = (((z * 2 + y) * 2 + x) * 2 + core) * size + start
        return ref.at[pl.ds(pl.multiple_of(first, 16), count), :]
    return ref.at[z, y, x, core, pl.ds(start, count), :]


class Spread:
    def __init__(self, place, weights, counts, sems):
        self.place = place
        self.weights = weights
        self.counts = counts
        self.pieces = cut_rows(counts)
        self.z_sems, self.near_sems, self.far_sems, self.core_sems = sems
        self.order = [place.z] + place.others

    def z_copy(self, step, slot):
        p = self.place
        ref = block_ref(self.weights[slot], self.counts[slot], p.z, p.y, p.x, p.core, 0, self.counts[slot])
        sems = self.z_sems
        return remote(ref, ref, sems.at[0, step, slot], sems.at[1, step, slot], p.along_z(step), p.core)

    def near_copy(self, turn, number):
        p = self.place
        slot, start, count, way = self.pieces[number]
        ref = block_ref(self.weights[slot], self.counts[slot], self.order[turn], p.y, p.x, p.core, start, count)
        sems = self.near_sems
        return remote(
            ref, ref, sems.at[0, turn, number], sems.at[1, turn, number], (p.along_x, p.along_y)[way](), p.core
        )

    def far_copies(self, turn, number):
        p = self.place
        slot, start, count, way = self.pieces[number]
        spot = self.order[turn]
        sems = self.far_sems
        copies = []
        for part, other in enumerate((0, 1) if slot == 1 else (slice(None),)):
            y, x = (p.y, other) if way == 0 else (other, p.x)
            ref = block_ref(self.weights[slot], self.counts[slot], spot, y, x, p.core, start, count)
            sem = number + 4 * part
            to = (p.along_y, p.along_x)[way]()
            copies.append(remote(ref, ref, sems.at[0, turn, sem], sems.at[1, turn, sem], to, p.core))
        return copies

    def core_copies(self, turn, slot):
        p = self.place
        sems = self.core_sems
        copies = []
        pairs = [(y, x) for y in (0, 1) for x in (0, 1)] if slot == 1 else [(slice(None), slice(None))]
        for part, (y, x) in enumerate(pairs):
            ref = block_ref(self.weights[slot], self.counts[slot], self.order[turn], y, x, p.core, 0, self.counts[slot])
            sem = (0, 2 + part, 1)[slot]
            copies.append(remote(ref, ref, sems.at[0, turn, sem], sems.at[1, turn, sem], p.client, 1 - p.core))
        return copies

    def fill(self, master):
        p = self.place
        start = 0
        for slot in range(3):
            rows = self.counts[slot]
            own = block_ref(self.weights[slot], self.counts[slot], p.z, p.y, p.x, p.core, 0, rows)
            own[...] = master[start : start + rows, :].astype(low_type)
            start += rows

    def begin(self):
        for step in range(3):
            self.z_copy(step, 0).start()
        self.near_start(0)

    def near_start(self, slot):
        for number in (2 * slot, 2 * slot + 1):
            self.near_copy(0, number).start()

    def steps(self):
        near, far, core, start = self.near_step, self.far_step, self.core_step, self.near_start
        groups = [
            [(far, 0, 0), (start, 1)],
            [(near, 1, 0)],
            [(near, 2, 0), (near, 3, 0)],
            [(far, 1, 0), (core, 0, 0), (far, 0, 1)],
            [(far, 2, 0), (far, 3, 0), (core, 1, 0)],
            [(core, 2, 0), (core, 3, 0), (near, 1, 1), (start, 2)],
            [(core, 0, 1), (near, 2, 1)],
            [(far, 1, 1), (near, 3, 1)],
            [(core, 1, 1), (far, 2, 1), (far, 0, 2)],
            [(far, 3, 1), (core, 2, 1), (near, 1, 2)],
            [(core, 3, 1), (core, 0, 2), (near, 2, 2)],
            [(far, 1, 2), (near, 3, 2)],
            [(core, 1, 2), (far, 2, 2)],
            [(far, 3, 2), (core, 2, 2)],
            [(core, 3, 2)],
        ]
        return [[functools.partial(*step) for step in group] for group in groups]

    def near_step(self, turn, slot):
        self.z_copy(turn - 1, slot).wait_recv()
        for number in (2 * slot, 2 * slot + 1):
            self.near_copy(turn, number).start()
        if slot < 2:
            self.z_copy(turn - 1, slot + 1).start()

    def far_step(self, turn, slot):
        for number in (2 * slot, 2 * slot + 1):
            self.near_copy(turn, number).wait_recv()
            for copy in self.far_copies(turn, number):
                copy.start()

    def core_step(self, turn, slot):
        for number in (2 * slot, 2 * slot + 1):
            for copy in self.far_copies(turn, number):
                copy.wait_recv()
        for copy in self.core_copies(turn, slot):
            copy.start()

    def arrive(self, slot):
        for turn in range(4):
            for copy in self.core_copies(turn, slot):
                copy.wait_recv()

    def drain(self, slot):
        for step in range(3):
            self.z_copy(step, slot).wait_send()
        for turn in range(4):
            for copy in self.core_copies(turn, slot):
                copy.wait_send()
            for number in (2 * slot, 2 * slot + 1):
                self.near_copy(turn, number).wait_send()
                for copy in self.far_copies(turn, number):
                    copy.wait_send()


class Fold:
    def __init__(self, place, grads, counts, parts):
        self.place = place
        self.grads = grads
        self.counts = counts
        self.pieces = cut_rows(counts)
        self.core_boxes = [parts[1], parts[0], parts[1]]
        self.near_boxes, self.far_boxes, self.z_boxes = [parts[3 * k + 2 : 3 * k + 5] for k in range(3)]
        self.core_sems, self.near_sems, self.far_sems, self.z_sems = parts[11:]

    def core_copies(self, which, slot):
        p = self.place
        sems = self.core_sems
        copies = []
        pairs = [(y, x) for y in (0, 1) for x in (0, 1)] if slot == 1 else [(slice(None), slice(None))]
        for part, (y, x) in enumerate(pairs):
            ref = block_ref(self.grads[slot], self.counts[slot], which, y, x, 1 - p.core, 0, self.counts[slot])
            box = self.core_boxes[slot].at[which, y, x]
            sem = (0, 2 + part, 1)[slot]
            copies.append(remote(ref, box, sems.at[0, which, sem], sems.at[1, which, sem], p.client, 1 - p.core))
        return copies

    def near_copies(self, which, number):
        p = self.place
        slot, start, count, way = self.pieces[number]
        sems = self.near_sems
        copies = []
        for part, other in enumerate((0, 1) if slot == 1 else (slice(None),)):
            y, x = (other, 1 - p.x) if way == 0 else (1 - p.y, other)
            ref = block_ref(self.grads[slot], self.counts[slot], which, y, x, p.core, start, count)
            box = self.near_boxes[slot].at[which, other, pl.ds(start, count), :]
            sem = number + 4 * part
            to = (p.along_x, p.along_y)[way]()
            copies.append(remote(ref, box, sems.at[0, which, sem], sems.at[1, which, sem], to, p.core))
        return copies

    def far_copy(self, which, number):
        p = self.place
        slot, start, count, way = self.pieces[number]
        y, x = (1 - p.y, p.x) if way == 0 else (p.y, 1 - p.x)
        ref = block_ref(self.grads[slot], self.counts[slot], which, y, x, p.core, start, count)
        box = self.far_boxes[slot].at[which, pl.ds(start, count), :]
        sems = self.far_sems
        return remote(
            ref, box, sems.at[0, which, number], sems.at[1, which, number], (p.along_y, p.along_x)[way](), p.core
        )

    def z_copy(self, which, sender, number):
        p = self.place
        slot, start, count, _ = self.pieces[number]
        rows = pl.ds(start, count)
        sems = self.z_sems
        return remote(
            block_ref(self.grads[slot], self.counts[slot], which, p.y, p.x, p.core, start, count),
            self.z_boxes[slot].at[sender, rows, :],
            sems.at[0, which, number],
            sems.at[1, sender, number],
            p.at(which, p.y, p.x),
            p.core,
        )

    def begin(self, which, slot):
        for copy in self.core_copies(which, slot):
            copy.start()

    def add(self, slot, spots, start, count, box):
        ref = block_ref(self.grads[slot], self.counts[slot], *spots, self.place.core, start, count)
        ref[...] = (ref[...].astype(wide) + box.astype(wide)).astype(low_type)

    def core_step(self, which, slot):
        for copy in self.core_copies(which, slot):
            copy.wait_recv()
        pairs = [(y, x) for y in (0, 1) for x in (0, 1)] if slot == 1 else [(slice(None), slice(None))]
        for y, x in pairs:
            self.add(slot, (which, y, x), 0, self.counts[slot], self.core_boxes[slot][which, y, x])
        for number in (2 * slot, 2 * slot + 1):
            for copy in self.near_copies(which, number):
                copy.start()

    def near_step(self, which, slot):
        p = self.place
        for number in (2 * slot, 2 * slot + 1):
            _, start, count, way = self.pieces[number]
            for copy in self.near_copies(which, number):
                copy.wait_recv()
            for other in (0, 1) if slot == 1 else (slice(None),):
                y, x = (other, p.x) if way == 0 else (p.y, other)
                box = self.near_boxes[slot][which, other, pl.ds(start, count), :]
                self.add(slot, (which, y, x), start, count, box)
            self.far_copy(which, number).start()

    def far_step(self, which, slot):
        p = self.place
        for number in (2 * slot, 2 * slot + 1):
            _, start, count, way = self.pieces[number]
            self.far_copy(which, number).wait_recv()
            box = self.far_boxes[slot][which, pl.ds(start, count), :]
            self.add(slot, (which, p.y, p.x), start, count, box)

            @pl.when(p.z != which)
            def _():
                self.z_copy(which, p.z, number).start()

    def result(self, slot):
        p = self.place
        self.z_boxes[slot][p.z] = block_ref(self.grads[slot], self.counts[slot], p.z, p.y, p.x, p.core, 0, self.counts[slot])[...]
        for sender in range(4):

            @pl.when(p.z != sender)
            def _():
                for number in (2 * slot, 2 * slot + 1):
                    self.z_copy(sender, sender, number).wait_recv()

        total = self.z_boxes[slot][0].astype(wide)
        for sender in range(1, 4):
            total += self.z_boxes[slot][sender].astype(wide)
        return total

    def drain(self):
        for which in range(4):
            for slot in range(3):
                for copy in self.core_copies(which, slot):
                    copy.wait_send()
            for number in range(6):
                for copy in self.near_copies(which, number):
                    copy.wait_send()
                self.far_copy(which, number).wait_send()

            @pl.when(self.place.z != which)
            def _():
                for number in range(6):
                    self.z_copy(which, self.place.z, number).wait_send()
class GramSum:
    def __init__(self, place, data, total, boxes, sems):
        self.place = place
        self.data = data
        self.total = total
        self.y_box, self.z_box = boxes
        self.sems = sems
        self.share = data.shape[0] // 8
        self.down_order = place.others[::-1] + [place.z]

    def rows(self, z, y):
        return pl.ds(pl.multiple_of((z * 2 + y) * self.share, 8), self.share)

    def copy(self, number, src, dst, to):
        sems = self.sems
        return remote(src, dst, sems.at[0, number], sems.at[1, number], to, self.place.core)

    def y_down(self, turn):
        p = self.place
        src = self.data.at[self.rows(self.down_order[turn], 1 - p.y), :]
        return self.copy(turn, src, self.y_box.at[turn], p.along_y())

    def z_down(self, step):
        p = self.place
        src = self.data.at[self.rows(p.others[step], p.y), :]
        return self.copy(4 + step, src, self.z_box.at[step], p.along_z(step))

    def z_up(self, step):
        p = self.place
        ref = self.total.at[self.rows(p.z, p.y), :]
        return self.copy(7 + step, ref, ref, p.along_z(step))

    def y_up(self, turn):
        p = self.place
        ref = self.total.at[self.rows(([p.z] + p.others)[turn], p.y), :]
        return self.copy(10 + turn, ref, ref, p.along_y())

    def run(self):
        p = self.place
        for turn in range(4):
            self.y_down(turn).start()
        for turn in range(4):
            self.y_down(turn).wait_recv()
            self.data[self.rows(self.down_order[turn], p.y), :] += self.y_box[turn]
            if turn < 3:
                self.z_down(2 - turn).start()
        mine = self.rows(p.z, p.y)
        value = self.data[mine, :]
        for step in (2, 1, 0):
            self.z_down(step).wait_recv()
            value += self.z_box[step]
        self.total[mine, :] = value
        for step in range(3):
            self.z_up(step).start()
        self.y_up(0).start()
        for step in range(3):
            self.z_up(step).wait_recv()
            self.y_up(1 + step).start()
        for turn in range(4):
            self.y_up(turn).wait_recv()

    def drain(self):
        for turn in range(4):
            self.y_down(turn).wait_send()
            self.y_up(turn).wait_send()
        for step in range(3):
            self.z_down(step).wait_send()
            self.z_up(step).wait_send()


class TileSum:
    def __init__(self, place, tiles, boxes, sems):
        self.place = place
        self.tiles = tiles
        self.boxes = boxes
        self.sems = sems

    def copy(self, stage, box):
        p = self.place
        to = (p.client, p.along_x(), p.along_y()) + tuple(p.along_z(step) for step in range(3))
        core = 1 - p.core if box == 0 else p.core
        return remote(
            self.tiles.at[stage], self.boxes.at[box], self.sems.at[0, box], self.sems.at[1, box], to[box], core
        )

    def start(self):
        self.copy(0, 0).start()

    def pair(self, stage):
        self.copy(stage, stage).wait_recv()
        self.tiles[stage + 1] = self.tiles[stage] + self.boxes[stage]
        if stage < 2:
            self.copy(stage + 1, stage + 1).start()
        else:
            for step in range(3):
                self.copy(3, 3 + step).start()

    def result(self):
        for step in range(3):
            self.copy(3, 3 + step).wait_recv()
        return (self.tiles[3] + self.boxes[3]) + (self.boxes[4] + self.boxes[5])

    def drain(self):
        for stage in range(3):
            self.copy(stage, stage).wait_send()
        for step in range(3):
            self.copy(3, 3 + step).wait_send()


def halves_of(value):
    high = value.astype(low_type)
    return high, (value - high.astype(wide)).astype(low_type)


class Share:
    def __init__(self, place, sizes, buffers, sems):
        self.place = place
        self.sizes = sizes
        self.fresh, self.rows_in, self.rows_out, self.back = buffers
        self.sems = sems
        self.bounds = [0, sizes[0], sizes[0] + sizes[1], sum(sizes)]
        p = place
        self.duty = jnp.where(p.x == 1, 1, 2 * p.core)
        self.mine = p.x * 2 + p.core

    def section(self, slot):
        return pl.ds(self.bounds[slot], self.sizes[slot])

    def spot(self, slot, x, core):
        number = x if slot == 1 else x * 2 + core
        return pl.ds(pl.multiple_of(number * self.sizes[slot], 16), self.sizes[slot])

    def doer(self, slot):
        return (0, 0) if slot == 0 else (0, 1) if slot == 2 else (1, self.place.core)

    def out_copy(self, slot):
        p = self.place
        x, core = self.doer(slot)
        return remote(
            self.fresh.at[self.section(slot), :],
            self.rows_in.at[self.spot(slot, p.x, p.core), :],
            self.sems.at[0, slot],
            self.sems.at[1, self.mine],
            p.at(p.z, p.y, x),
            core,
        )

    def in_copy(self, slot, x, core):
        p = self.place
        return remote(
            self.fresh.at[self.section(slot), :],
            self.rows_in.at[self.spot(slot, x, core), :],
            self.sems.at[0, slot],
            self.sems.at[1, x * 2 + core],
            p.at(p.z, p.y, x),
            core,
        )

    def back_copy(self, slot, x, core):
        p = self.place
        return remote(
            self.rows_out.at[self.spot(slot, x, core), :],
            self.back.at[self.section(slot), :],
            self.sems.at[0, 3 + x * 2 + core],
            self.sems.at[1, 4 + slot],
            p.at(p.z, p.y, x),
            core,
        )

    def users(self, slot):
        p = self.place
        if slot == 1:
            return [(0, p.core), (1, p.core)]
        return [(x, core) for x in (0, 1) for core in (0, 1)]

    def send(self, slot):
        @pl.when(self.duty != slot)
        def _():
            self.out_copy(slot).start()

        @pl.when(self.duty == slot)
        def _():
            self.rows_in[self.spot(slot, self.place.x, self.place.core), :] = self.fresh[self.section(slot), :]

    def gather(self):
        p = self.place
        for slot in range(3):

            @pl.when(self.duty == slot)
            def _():
                for x, core in self.users(slot):

                    @pl.when((p.x != x) | (p.core != core))
                    def _():
                        self.in_copy(slot, x, core).wait_recv()

    def give_back(self):
        p = self.place
        for slot in range(3):

            @pl.when(self.duty == slot)
            def _():
                for x, core in self.users(slot):

                    @pl.when((p.x != x) | (p.core != core))
                    def _():
                        self.back_copy(slot, x, core).start()

                self.back[self.section(slot), :] = self.rows_out[self.spot(slot, p.x, p.core), :]

    def finish(self):
        p = self.place
        for slot in range(3):

            @pl.when(self.duty != slot)
            def _():
                self.back_copy(slot, p.x, p.core).wait_recv()
                self.out_copy(slot).wait_send()

            @pl.when(self.duty == slot)
            def _():
                for x, core in self.users(slot):

                    @pl.when((p.x != x) | (p.core != core))
                    def _():
                        self.back_copy(slot, x, core).wait_send()


def corner_spot(number, part):
    row, column = number // 2, number % 2
    return slice(row * part, (row + 1) * part), slice(column * part, (column + 1) * part)


def orthogonal(place, ratios, share, share_sems, gram, gram_total, mate_gram, gram_sum, squares, rows_in, low_rows):
    grams, mixed, once = squares
    count, width = rows_in.shape
    part = width // CUTS
    corners = [(row, column) for row in range(CUTS) for column in range(row, CUTS)]
    right_high, right_low = [low_rows.at[pl.ds(count + spot * width, width), :] for spot in range(2)]

    def set_right(value_ref):
        for start in range(0, width, part):
            rows = slice(start, start + part)
            right_high[rows, :], right_low[rows, :] = halves_of(value_ref[rows, :])

    def times_right(value):
        high, low = halves_of(value)
        left = jnp.concatenate([high, high, low], axis=1)
        right = jnp.concatenate([right_high[...], right_low[...], right_high[...]], axis=0)
        return dot_nn(left, right)

    share.gather()
    high, low = halves_of(rows_in[...])
    left = jnp.concatenate([high, high, low], axis=0)
    right = jnp.concatenate([high, low, high], axis=0)
    for row in range(CUTS):
        strip = dot_tn(left[:, row * part : (row + 1) * part], right[:, row * part :])
        for column in range(row, CUTS):
            gram[corner_spot(corners.index((row, column)), part)] = strip[
                :, (column - row) * part : (column - row + 1) * part
            ]

    @pl.when(place.x == 1)
    def _():
        swap = remote(gram, mate_gram, share_sems.at[0, 7], share_sems.at[1, 7], place.client, 1 - place.core)
        swap.start()
        swap.wait()
        gram[...] += mate_gram[...]

    gram_sum.run()
    spots = lax.broadcasted_iota(jnp.int32, (part, part), 0)
    diagonal = spots == lax.broadcasted_iota(jnp.int32, (part, part), 1)
    trace = 0.0
    for number, (row, column) in enumerate(corners):
        if row == column:
            trace += jnp.sum(jnp.where(diagonal, gram_total[corner_spot(number, part)], 0.0))
    factor = 1.0 / (jnp.sqrt(trace) + 1e-07)
    square = factor * factor
    for number, (row, column) in enumerate(corners):
        rows, columns = slice(row * part, (row + 1) * part), slice(column * part, (column + 1) * part)
        block = gram_total[corner_spot(number, part)] * square
        grams[rows, columns] = block
        if row < column:
            grams[columns, rows] = block.T
    rows_in[...] = rows_in[...] * factor

    def turn(number, carry):
        set_right(grams)
        mixed[...] = schulz_second * grams[...] + schulz_third * times_right(grams[...])
        set_right(mixed)

        @pl.when(number < NS_STEPS - 1)
        def _():
            both = times_right(jnp.concatenate([grams[...], rows_in[...]], axis=0))
            once[...] = schulz_first * grams[...] + both[:width]
            rows_in[...] = schulz_first * rows_in[...] + both[width:]
            grams[...] = schulz_first * once[...] + times_right(once[...])

        @pl.when(number == NS_STEPS - 1)
        def _():
            rows_in[...] = schulz_first * rows_in[...] + times_right(rows_in[...])

        return carry

    lax.fori_loop(0, NS_STEPS, turn, 0)
    ratio = jnp.where(share.duty == 1, ratios[1], ratios[0])
    low_rows[0:count, :] = (rows_in[...] * ratio).astype(low_type)
    share.give_back()


def update_kernel(loss_tile, master, fresh_momentum, ortho, *rest):
    norms, grad_norm, heads, grad_head, outs = rest[0:3], rest[3], rest[4:7], rest[7], rest[8:]
    loss_out, *outs = outs
    loss_out[0] = loss_tile[0, 0]
    loss_out[1] = loss_tile[0, 1]
    momentum_out, base_out, low_out = outs[0:3]
    held = master[...]
    momentum_out[...] = fresh_momentum[...]
    fresh = held - muon_rate * (ortho[...].astype(wide) + muon_decay * held)
    base_out[...] = fresh
    low_out[...] = fresh.astype(low_type)
    for targets, values, grad, rate, decay in (
        (outs[3:6], norms, grad_norm, norm_rate, 0.0),
        (outs[6:9], heads, grad_head, head_rate, head_decay),
    ):
        updates = adam_update(values[0][...], grad[...], values[1][...], values[2][...], rate, decay)
        for target, value in zip(targets, updates):
            target[...] = value


def update_pass(loss_tile, master, fresh_momentum, ortho, norms, grad_norm, heads, grad_head):
    vmem = pl.BlockSpec(memory_space=pltpu.VMEM)
    smem = pl.BlockSpec(memory_space=pltpu.SMEM)
    operands = [loss_tile, master, fresh_momentum, ortho, *norms, grad_norm, *heads, grad_head]
    outs = [(2,), master.shape, master.shape, master.shape] + [grad_norm.shape] * 3 + [grad_head.shape] * 3
    types = [wide, wide, wide, low_type] + [wide] * 6
    return pl.pallas_call(
        update_kernel,
        out_shape=[jax.ShapeDtypeStruct(shape, kind) for shape, kind in zip(outs, types)],
        in_specs=[smem] + [vmem] * (len(operands) - 1),
        out_specs=[smem] + [vmem] * (len(outs) - 1),
        compiler_params=pltpu.CompilerParams(vmem_limit_bytes=VMEM_BYTES),
    )(*operands)


def norm_stats(mine, theirs, count):
    gap = mine[0:1] - theirs[0:1]
    mean = 0.5 * (mine[0:1] + theirs[0:1])
    spread = mine[1:2] + theirs[1:2] + gap * gap * (0.5 * count)
    return mean, lax.rsqrt(spread / (2.0 * count) + norm_epsilon)


def client_kernel(
    gather,
    ratios,
    images,
    classes,
    features,
    labels,
    flag,
    params,
    head,
    *rest,
):
    if gather:
        master, momentum, anchor, *rest = rest
    else:
        first_in, middle_in, last_in, *rest = rest
    if gather:
        fresh_out, ortho_out, *rest = rest
    else:
        grads_out, rest = rest[:3], rest[3:]
    (
        grad_norm_out,
        grad_head_out,
        loss_out,
        x_all,
        mid_wide,
        w_first,
        w_middle,
        w_last,
        act_one,
        act_two,
        act_three,
        taps_one,
        taps_two,
        hidden_two,
        stage,
        params_all,
        head_all,
        grad_pool,
        pool_send,
        pool_all,
        logit_grads,
        sums_mine,
        sums_theirs,
        shift,
        fwd_stats,
        sem_local,
        sem_swap,
        sem_misc,
        *near_parts,
    ) = rest
    place = Place()
    core = place.core
    mate = (place.client, 1 - core)
    count_rows, channels = x_all.shape
    half = channels // 2
    width = act_one.shape[1]
    part = width // 2
    mine_images = images // 2
    line = SIDE * mine_images
    total_rows = 2.0 * count_rows

    def tile(index):
        return pl.ds(pl.multiple_of(index * line, line), line)

    def lanes(index, size):
        return pl.ds(pl.multiple_of(index * size, size), size)

    weights = (w_first, w_middle, w_last)
    if gather:
        held = act_three.at[pl.ds(0, master.shape[0]), pl.ds(0, width)]
        load = pltpu.make_async_copy(master, held, sem_local.at[8])
        load.start()
        counts = [channels // 32, 9 * width // 32, channels // 32]
        spread = Spread(place, weights, counts, near_parts[:4])
        fold = Fold(place, (w_first, mid_wide, w_last), counts, near_parts[4:19])
        rows_in, back, tiles, tile_boxes, gram_total, y_box, z_box, mate_gram = near_parts[19:27]
        tile_sems, share_sems, gram_sems = near_parts[27:]
        block_rows = master.shape[0]
        side_space = pl.ds(half, width)
        held_base, held_momentum, held_anchor, fresh = [
            act_three.at[pl.ds(number * block_rows, block_rows), side_space] for number in range(4)
        ]
        rows_in[...] = jnp.zeros_like(rows_in)
        share = Share(place, counts, (fresh, rows_in, hidden_two, back), share_sems)
        tile_sum = TileSum(place, tiles, tile_boxes, tile_sems)
        due = spread.steps()
        load.wait()
        spread.fill(held)
        place.greet(True, True)
        spread.begin()
    else:
        place.greet(False)
        loads = [
            pltpu.make_async_copy(src, dst, sem_local.at[8 + slot])
            for slot, (src, dst) in enumerate(zip((first_in, middle_in, last_in), weights))
        ]
        for load in loads:
            load.start()
        due = []

    quarter = half // 2
    own_rows = pl.ds(pl.multiple_of(core * count_rows, count_rows), count_rows)
    mate_rows = pl.ds(pl.multiple_of((1 - core) * count_rows, count_rows), count_rows)
    top_rows = pl.ds(0, count_rows)
    own_copies = [
        pltpu.make_async_copy(
            features.at[own_rows, pl.ds(side * quarter, quarter)], buffer, sem_local.at[side]
        )
        for side, buffer in enumerate((hidden_two, mid_wide.at[top_rows, :]))
    ]
    per_kind = params.shape[0] // 2
    for kind in range(2):
        rows = [params[kind * per_kind + spot : kind * per_kind + spot + 1, :] for spot in range(per_kind)]
        params_all[core, kind : kind + 1, :] = jnp.concatenate(rows, axis=1)
    head_all[core] = jnp.zeros(head_all.shape[1:], low_type)
    for spot in range(half // LANES):
        head_all[core, 0:classes, spot * LANES : (spot + 1) * LANES] = head[
            pl.ds(spot, classes, stride=half // LANES), :
        ].astype(low_type)
    to_mate = [
        remote(params_all.at[core], params_all.at[core], sem_misc.at[0, 0], sem_misc.at[1, 0], *mate),
        remote(head_all.at[core], head_all.at[core], sem_misc.at[0, 1], sem_misc.at[1, 1], *mate),
    ]
    for side, buffer in enumerate((taps_one, taps_two)):
        to_mate.append(
            remote(
                features.at[mate_rows, pl.ds(side * quarter, quarter)],
                buffer.at[top_rows, :],
                sem_misc.at[0, 5 + side],
                sem_misc.at[1, 5 + side],
                *mate,
            )
        )
    for copy in to_mate + own_copies:
        copy.start()

    def advance(count):
        for group in due[:count]:
            for step in group:
                step()
        del due[:count]

    def advance_at(index, spots):
        for spot, group in zip(spots, due):

            @pl.when(index == spot)
            def _():
                for step in group:
                    step()

    def arrive(slot, left):
        if gather:
            advance(len(due) - left)
            spread.arrive(slot)
        else:
            loads[slot].wait()

    def arrive_turns(slot, turns):
        if gather:
            for turn in turns:
                for copy in spread.core_copies(turn, slot):
                    copy.wait_recv()

    def fold_step(kind, slot, which):
        if gather:
            (fold.core_step, fold.near_step, fold.far_step)[kind](which, slot)

    def fold_at(index, spot, *steps):
        @pl.when(index == spot)
        def _():
            for step in steps:
                fold_step(*step)

    def fold_begin(which, slot):
        if gather:
            fold.begin(which, slot)

    def zero_edges(buffer):
        edge = jnp.zeros((line,) + buffer.shape[1:], low_type)
        buffer[0:line, :] = edge
        buffer[line + count_rows : 2 * line + count_rows, :] = edge

    advance(3)
    for copy in own_copies:
        copy.wait()

    def turn_from(source, base):
        def turn(index, carry):
            stage[...] = source(lanes(index, LANES)).astype(wide)

            def pixel(spot, inner):
                x_all[
                    pl.ds(pl.multiple_of(spot * mine_images, mine_images), mine_images),
                    pl.ds(pl.multiple_of(base + index * LANES, LANES), LANES),
                ] = stage[pl.ds(spot, mine_images, stride=PIXELS), :].astype(low_type)
                return inner

            return lax.fori_loop(0, PIXELS, pixel, carry, unroll=7)

        return turn

    quarters = quarter // LANES
    own_base, mate_base = core * half, (1 - core) * half
    lax.fori_loop(0, quarters, turn_from(lambda columns: hidden_two[:, columns], own_base), 0)
    advance(1)
    lax.fori_loop(
        0,
        quarters,
        turn_from(lambda columns: mid_wide[0:count_rows, columns], own_base + quarter),
        0,
    )
    advance(1)
    for copy in to_mate:
        copy.wait_recv()
    lax.fori_loop(0, quarters, turn_from(lambda columns: taps_one[0:count_rows, columns], mate_base), 0)
    advance(1)
    lax.fori_loop(0, quarters, turn_from(lambda columns: taps_two[0:count_rows, columns], mate_base + quarter), 0)
    zero_edges(taps_one)
    zero_edges(taps_two)
    arrive(0, 9)

    def swap(slot, size):
        return remote(
            sums_mine.at[slot, :, pl.ds(0, size)],
            sums_theirs.at[slot, :, pl.ds(0, size)],
            sem_swap.at[0, slot],
            sem_swap.at[1, slot],
            *mate,
        )

    def gain_bias(lower, upper):
        rows = []
        for kind in range(2):
            pieces = [params_all[side, kind : kind + 1, lower:upper] for side in range(2)]
            rows.append(jnp.concatenate(pieces, axis=1))
        return rows

    def collect(index, value, columns, size):
        @pl.when(index == 0)
        def _():
            shift[0:1, pl.ds(0, size)] = column_sum(fold_rows(value)) / value.shape[0]
            shift[8:24, pl.ds(0, size)] = jnp.zeros((16, size), wide)

        gap = value - shift[0:1, pl.ds(0, size)]
        shift[8:16, pl.ds(0, size)] += fold_rows(gap)
        shift[16:24, pl.ds(0, size)] += fold_rows(gap * gap)

    def close_stats(slot, columns, size):
        sum_gap = column_sum(shift[8:16, pl.ds(0, size)])
        sum_square = column_sum(shift[16:24, pl.ds(0, size)])
        sums_mine[slot, 0:1, columns] = shift[0:1, pl.ds(0, size)] + sum_gap / count_rows
        sums_mine[slot, 1:2, columns] = sum_square - sum_gap * sum_gap / count_rows

    def look_over(act, columns):
        def look(index, carry):
            collect(index, act[tile(index), columns], None, width)
            return carry

        lax.fori_loop(0, SIDE, look, 0)

    groups = SPOTS[0]
    group = channels // groups

    def settle(slot, size):
        mean, scale = norm_stats(
            sums_mine[slot, 0:2, pl.ds(0, size)], sums_theirs[slot, 0:2, pl.ds(0, size)], float(count_rows)
        )
        fwd_stats[slot, 0:1, pl.ds(0, size)] = mean
        fwd_stats[slot, 1:2, pl.ds(0, size)] = scale

    whole_width = pl.ds(0, width)

    def first_part(index, carry):
        act_one[...] += dot_nn(x_all[:, lanes(index, group)], flat_rows(w_first[index]))
        advance_at(index, (0, 1, 2))
        return carry

    act_one[...] = jnp.zeros_like(act_one)
    lax.fori_loop(0, groups, first_part, 0)
    del due[:3]
    look_over(act_one, whole_width)
    close_stats(0, whole_width, width)
    move = swap(0, width)
    move.start()
    advance(1)
    move.wait()
    settle(0, width)

    gain_one, bias_one = gain_bias(0, part)
    gain_two, bias_two = gain_bias(part, width)
    gain_three, bias_three = gain_bias(width, width + half)

    def normal(act, slot, index):
        mean = fwd_stats[slot, 0:1, pl.ds(0, width)]
        return (act[tile(index), :] - mean) * fwd_stats[slot, 1:2, pl.ds(0, width)]

    def hide_one(index, carry):
        value = normal(act_one, 0, index) * gain_one + bias_one
        taps_one[pl.ds(pl.multiple_of((index + 1) * line, line), line), :] = (value * sigmoid(value)).astype(low_type)
        return carry

    lax.fori_loop(0, SIDE, hide_one, 0)
    if gather:
        arrive_turns(1, (0, 1))
    else:
        arrive(1, 0)

    step = mine_images
    piece = width // 2

    def row_windows(buffer, down, start, reach):
        if reach == line:
            return buffer[pl.ds(pl.multiple_of(down * line, line), count_rows), :]
        windows = [
            buffer[pl.ds(pl.multiple_of((down + row) * line + start, step), reach), :] for row in range(SIDE)
        ]
        return jnp.concatenate(windows, axis=0)

    def add_windows(target, columns, value, start, reach):
        for row in range(SIDE):
            rows = slice(row * line + start, row * line + start + reach)
            target[rows, columns] += value[row * reach : (row + 1) * reach]

    low_start, high_start, reaches = (0, 0, step), (step, 0, 0), (line - step, line, line - step)

    early, taps = 4, 9

    def second_part(index, carry):
        tap = jnp.where(place.z < 2, index, (index + taps - early) % taps) if gather else index

        @pl.when(index == early)
        def _():
            arrive_turns(1, (2, 3))

        down = tap // 3
        for over in range(3):

            @pl.when(tap % 3 == over)
            def _():
                left = row_windows(taps_one, down, low_start[over], reaches[over])
                kernel = w_middle[pl.ds(pl.multiple_of(tap * width, width), width), :]
                add_windows(act_two, slice(None), dot_nn(left, kernel), high_start[over], reaches[over])

        advance_at(index, (2, 5, 6, 8))
        return carry

    act_two[...] = jnp.zeros_like(act_two)
    lax.fori_loop(0, taps, second_part, 0)
    del due[:4]
    look_over(act_two, whole_width)
    close_stats(1, whole_width, width)
    move_two = swap(1, width)
    move_two.start()
    arrive(2, 0)
    if gather:
        spread.drain(0)

    def turn_weights(which, carry):
        w_first[which] = jnp.transpose(flat_rows(w_last[which])).reshape(w_first.shape[1:])
        return carry

    lax.fori_loop(0, groups, turn_weights, 0)
    move_two.wait()
    settle(1, width)

    def third_line(index, carry):
        value = normal(act_two, 1, index) * gain_two + bias_two
        hidden = (value * sigmoid(value)).astype(low_type)
        hidden_two[tile(index), :] = hidden
        for which in range(groups):
            columns = slice(which * group, (which + 1) * group)
            value = dot_nn(hidden, flat_rows(w_first[which]))
            act_three[tile(index), columns] = value
            start = jnp.where(index == 0, column_sum(value[0:8]) / 8.0, shift[0:1, columns])
            gap = value - start
            kept_sums = jnp.where(index == 0, 0.0, shift[8:24, columns])
            shift[0:1, columns] = start
            shift[8:16, columns] = kept_sums[0:8] + fold_rows(gap)
            shift[16:24, columns] = kept_sums[8:16] + fold_rows(gap * gap)
        return carry

    lax.fori_loop(0, SIDE, third_line, 0)
    close_stats(2, pl.ds(0, channels), channels)
    move_three = swap(2, channels)
    move_three.start()
    move_three.wait()
    settle(2, channels)

    per_group = group // LANES

    def block_of(spot):
        return pl.ds(pl.multiple_of(spot * mine_images, mine_images), mine_images)

    def mid_line(which, index):
        return pl.ds(pl.multiple_of(which * count_rows + index * line, line), line)

    kept = channels // LANES * mine_images

    def gathered(kind):
        starts = range(kind * kept, (kind + 1) * kept, mine_images)
        return jnp.concatenate([stage[start : start + mine_images, :] for start in starts], axis=1)

    fwd_stats[2, 4:5, :] = fwd_stats[2, 1:2, :] * gain_three
    fwd_stats[2, 5:6, :] = bias_three - fwd_stats[2, 0:1, :] * fwd_stats[2, 4:5, :]

    def emit(index, carry):
        columns = lanes(index, LANES)
        slant, level = fwd_stats[2, 4:5, columns], fwd_stats[2, 5:6, columns]

        def pixels(row, sums):
            pooled, steeps, steeps_act = sums
            found = []
            for spot in range(SIDE):
                where = block_of(row * SIDE + spot)
                act = act_three[where, columns]
                half_total = 0.5 * (act * slant + level + x_all[where, columns].astype(wide))
                rise = 1.0 + jnp.tanh(half_total)
                out = half_total * rise
                steep = rise + out * (2.0 - rise)
                found.append(steep.astype(low_type))
                pooled, steeps, steeps_act = pooled + out, steeps + steep, steeps_act + steep * act
            mid_wide[mid_line(index // per_group, row), lanes(index % per_group, LANES)] = jnp.concatenate(
                found, axis=0
            )
            return pooled, steeps, steeps_act

        zero = jnp.zeros((mine_images, LANES), wide)
        sums = lax.fori_loop(0, SIDE, pixels, (zero, zero, zero))
        for kind, value in enumerate(sums):
            stage[pl.ds(pl.multiple_of(kind * kept + index * mine_images, mine_images), mine_images), :] = value
        return carry

    lax.fori_loop(0, channels // LANES, emit, 0)

    pooled = (gathered(0) / PIXELS).astype(low_type)
    head_full = jnp.concatenate([head_all[0], head_all[1]], axis=1)
    logits = dot_nt(head_full, pooled)
    spots = lax.broadcasted_iota(jnp.int32, logits.shape, 0)
    inside = spots < classes
    first_labels, second_labels = labels[0:1, 0:mine_images], labels[0:1, mine_images:]
    onehot = (spots == jnp.where(core == 0, first_labels, second_labels)).astype(wide)
    top = jnp.max(jnp.where(inside, logits, -jnp.inf), axis=0, keepdims=True)
    powers = jnp.where(inside, jnp.exp(logits - top), 0.0)
    power_sum = jnp.sum(powers, axis=0, keepdims=True)
    picked = jnp.sum(logits * onehot, axis=0, keepdims=True)
    each_loss = top + jnp.log(power_sum) - picked
    taking = flag[0].astype(wide)
    tile_spots = lax.broadcasted_iota(jnp.int32, loss_out.shape, 1)
    loss_out[...] = jnp.where(tile_spots == 0, taking * jnp.sum(each_loss), taking * mine_images)
    grads = (taking / images * (powers / power_sum - onehot)).astype(low_type)
    grad_pool[...] = dot_tn(grads, head_full) * (0.5 / PIXELS)
    logit_grads[core] = grads
    pool_all[core] = pooled[:, 0:half]
    pool_send[...] = pooled[:, half:]

    @pl.when(core == 1)
    def _():
        pool_all[core] = pooled[:, half:]
        pool_send[...] = pooled[:, 0:half]

    head_moves = [
        remote(pool_send, pool_all.at[core], sem_misc.at[0, 3], sem_misc.at[1, 3], *mate),
        remote(logit_grads.at[core], logit_grads.at[core], sem_misc.at[0, 4], sem_misc.at[1, 4], *mate),
    ]

    steeps = gathered(1)
    steeps_normed = (gathered(2) - fwd_stats[2, 0:1, :] * steeps) * fwd_stats[2, 1:2, :]
    sums_mine[3, 0:1, :] = column_sum(grad_pool[...] * steeps)
    sums_mine[3, 1:2, :] = column_sum(grad_pool[...] * steeps_normed)
    move_back = swap(3, channels)
    move_back.start()
    for copy in head_moves:
        copy.start()
    move_back.wait()

    def back_terms(slot, layer, size, gain):
        columns = pl.ds(0, size)
        sums = sums_mine[slot, 0:2, columns] + sums_theirs[slot, 0:2, columns]
        sums_mine[slot, 2:4, columns] = sums
        scale = fwd_stats[layer, 1:2, columns]
        return (
            scale * gain,
            scale * gain * sums[0:1] / total_rows,
            scale * scale * gain * sums[1:2] / total_rows,
        )

    first, second, third = back_terms(3, 2, channels, gain_three)
    fwd_stats[2, 4:5, :] = second - third * fwd_stats[2, 0:1, :]
    fwd_stats[2, 5:6, :] = third
    grad_pool[...] = grad_pool[...] * first

    def pull(index):
        for which in range(groups):
            columns = slice(which * group, (which + 1) * group)
            reach = grad_pool[:, columns]
            steep = mid_wide[mid_line(which, index), :].astype(wide)
            value = jnp.concatenate([reach] * SIDE, axis=0) * steep
            value = value - fwd_stats[2, 4:5, columns] - fwd_stats[2, 5:6, columns] * act_three[tile(index), columns]
            mid_wide[mid_line(which, index), :] = value.astype(low_type)

    pull(0)

    def drop_into(act, slot, gain, bias, columns):
        size = pl.ds(0, width)
        shift[8:24, size] = jnp.zeros((16, width), wide)

        def drop(index, carry):
            normed = normal(act, slot, index)
            norm = normed * gain + bias
            sig = sigmoid(norm)
            grad = act_three[tile(index), columns] * (sig + norm * sig * (1.0 - sig))
            act_three[tile(index), columns] = grad
            shift[8:16, size] += fold_rows(grad)
            shift[16:24, size] += fold_rows(grad * normed)
            return carry

        lax.fori_loop(0, SIDE, drop, 0)

    def close_back(slot):
        size = pl.ds(0, width)
        sums_mine[slot, 0:1, size] = column_sum(shift[8:16, size])
        sums_mine[slot, 1:2, size] = column_sum(shift[16:24, size])

    space_two, space_one = pl.ds(0, width), pl.ds(width, width)

    def mid_group(which):
        return mid_wide[pl.ds(pl.multiple_of(which * count_rows, count_rows), count_rows), :]

    def back_two(index):
        left = jnp.concatenate([mid_wide[mid_line(which, index), :] for which in range(groups)], axis=1)
        value = dot_nn(left, flat_rows(w_last[...]))
        normed = normal(act_two, 1, index)
        norm = normed * gain_two + bias_two
        sig = sigmoid(norm)
        grad = value * (sig + norm * sig * (1.0 - sig))
        act_three[tile(index), space_two] = grad
        size = pl.ds(0, width)
        shift[8:16, size] += fold_rows(grad)
        shift[16:24, size] += fold_rows(grad * normed)

    def back_two_line(index, carry):
        pull(index + 1)
        back_two(index)
        return carry

    shift[8:24, :] = jnp.zeros((16, channels), wide)
    lax.fori_loop(0, SIDE - 1, back_two_line, 0)
    back_two(SIDE - 1)
    close_back(4)
    move_back_two = swap(4, width)
    move_back_two.start()
    if gather:
        base_loads = [
            pltpu.make_async_copy(src, dst, sem_local.at[1 + number])
            for number, (src, dst) in enumerate(
                ((master, held_base), (momentum, held_momentum), (anchor, held_anchor))
            )
        ]
        for load in base_loads:
            load.start()
        tiles[0] = loss_out[...]
        tile_sum.start()

    def settle_section(slot):
        if gather:
            rows = share.section(slot)
            grad = fold.result(slot) + prox_weight * (held_base[rows, :] - held_anchor[rows, :])
            fresh[rows, :] = momentum_decay * held_momentum[rows, :] + grad
            share.send(slot)

    if gather:
        spread.drain(1)
        spread.drain(2)

    def put(ref, which, value):
        ref[which] = value.astype(low_type).reshape(ref.shape[1:])

    def expand_group(which, carry):
        put(w_last, which, dot_tn(mid_group(which), hidden_two[...]))
        fold_begin(which, 2)
        fold_at(which, 2, (0, 2, 0))
        fold_at(which, 3, (0, 2, 1))
        return carry

    lax.fori_loop(0, groups, expand_group, 0)
    move_back_two.wait()
    terms_two = back_terms(4, 1, width, gain_two)

    def back_act(terms, act, layer, index, columns):
        first, second, third = terms
        gap = act[tile(index), :] - fwd_stats[layer, 0:1, pl.ds(0, width)]
        return (first * act_three[tile(index), columns] - second - third * gap).astype(low_type)

    def grad_two(index, carry):
        taps_two[pl.ds(pl.multiple_of((index + 1) * line, line), line), :] = back_act(
            terms_two, act_two, 1, index, space_two
        )
        return carry

    lax.fori_loop(0, SIDE, grad_two, 0)
    fold_step(0, 2, 2)
    fold_step(1, 2, 0)
    core_step, near_step, far_step = 0, 1, 2
    plan = {
        0: [(core_step, 2, 3)],
        1: [(near_step, 2, 1)],
        2: [(far_step, 2, 0), (near_step, 2, 2)],
        3: [(far_step, 2, 1), (near_step, 2, 3)],
        4: [(far_step, 2, 2)],
        5: [(far_step, 2, 3), (core_step, 1, 0)],
        7: [(core_step, 1, 1)],
    }

    def middle_row(down, carry):
        for over in range(3):
            left = row_windows(taps_one, down, low_start[over], reaches[over])
            right = row_windows(taps_two, 1, high_start[over], reaches[over])
            rows = pl.ds(pl.multiple_of((3 * down + over) * width, width), width)
            mid_wide[rows, :] = dot_tn(left, right).astype(low_type)
            for row in range(3):
                tap = 3 * row + over

                @pl.when(down == row)
                def _():
                    if tap >= 2 and tap % 2 == 0:
                        fold_begin(tap // 2 - 1, 1)
                    for step in plan.get(tap, ()):
                        fold_step(*step)

        return carry

    lax.fori_loop(0, 3, middle_row, 0)
    for copy in head_moves:
        copy.wait_recv()
    head_grad = dot_nn(logit_grads[0], pool_all[0]) + dot_nn(logit_grads[1], pool_all[1])
    for spot in range(half // LANES):
        stage[pl.ds(spot, classes, stride=half // LANES), :] = head_grad[
            0:classes, spot * LANES : (spot + 1) * LANES
        ]
    head_space = stage.at[pl.ds(0, grad_head_out.shape[0]), :]
    head_leave = pltpu.make_async_copy(head_space, grad_head_out, sem_local.at[0])
    head_leave.start()
    if gather:
        tile_sum.pair(0)
        for load in base_loads:
            load.wait()

    def back_one(index, carry):
        down, side = index // 2, index % 2
        columns = lanes(2 + side, piece)
        for over in range(3):
            left = row_windows(taps_two, 2 - down, high_start[over], reaches[over])
            start = pl.multiple_of((3 * down + over) * width + side * piece, piece)
            value = dot_nt(left, w_middle[pl.ds(start, piece), :])
            add_windows(act_three, columns, value, low_start[over], reaches[over])
        fold_at(index, 0, (core_step, 1, 2), (near_step, 1, 0))
        fold_at(index, 1, (core_step, 1, 3))
        fold_at(index, 2, (near_step, 1, 1), (far_step, 1, 0))
        fold_at(index, 4, (far_step, 1, 1))
        fold_at(index, 5, (near_step, 1, 2))
        return carry

    act_three[:, space_one] = jnp.zeros((count_rows, width), wide)
    lax.fori_loop(0, 6, back_one, 0)
    drop_into(act_one, 0, gain_one, bias_one, space_one)
    fold_step(near_step, 1, 3)
    settle_section(2)
    close_back(5)
    move_back_one = swap(5, width)
    move_back_one.start()

    move_back_one.wait()
    terms_one = back_terms(5, 0, width, gain_one)

    def grad_one(index, carry):
        hidden_two[tile(index), :] = back_act(terms_one, act_one, 0, index, space_one)
        return carry

    lax.fori_loop(0, SIDE, grad_one, 0)
    fold_step(far_step, 1, 2)
    if gather:
        tile_sum.pair(1)

    def reduce_group(which, carry):
        put(w_first, which, dot_tn(x_all[:, lanes(which, group)], hidden_two[...]))
        fold_begin(which, 0)
        fold_at(which, 0, (far_step, 1, 3))
        fold_at(which, 2, (core_step, 0, 0))
        fold_at(which, 3, (core_step, 0, 1), (near_step, 0, 0))
        return carry

    lax.fori_loop(0, groups, reduce_group, 0)

    for kind in range(2):
        row = 3 - kind
        pieces = [
            sums_mine[5, row : row + 1, lanes(core, part)],
            sums_mine[4, row : row + 1, lanes(core, part)],
            sums_mine[3, row : row + 1, lanes(core, half)],
        ]
        whole = jnp.concatenate(pieces, axis=1)
        per_kind = whole.shape[1] // LANES
        for spot in range(per_kind):
            grad_norm_out[kind * per_kind + spot : kind * per_kind + spot + 1, :] = whole[
                :, spot * LANES : (spot + 1) * LANES
            ]
    for step in (
        (core_step, 0, 2),
        (core_step, 0, 3),
        (far_step, 0, 0),
        (near_step, 0, 1),
        (near_step, 0, 2),
        (far_step, 0, 1),
        (near_step, 0, 3),
        (far_step, 0, 2),
        (far_step, 0, 3),
    ):
        fold_step(*step)
        if step == (far_step, 0, 0):
            settle_section(1)
    if gather:
        settle_section(0)
        leave = pltpu.make_async_copy(fresh, fresh_out, sem_local.at[1])
        leave.start()
        tile_sum.pair(2)
        part = width // CUTS
        gram = act_three.at[pl.ds(0, gram_total.shape[0]), pl.ds(half + width, 2 * part)]
        corner_rows = pl.ds(gram_total.shape[0], width)
        squares = [act_three.at[corner_rows, pl.ds(spot * width, width)] for spot in (0, 1, 3)]
        gram_sum = GramSum(place, gram, gram_total, (y_box, z_box), gram_sems)
        orthogonal(place, ratios, share, share_sems, gram, gram_total, mate_gram, gram_sum, squares, rows_in, hidden_two)
        share.finish()
        loss_out[...] = tile_sum.result()
        ortho_leave = pltpu.make_async_copy(back, ortho_out, sem_local.at[2])
        ortho_leave.start()
        gram_sum.drain()
        tile_sum.drain()
        fold.drain()
        leave.wait()
        ortho_leave.wait()
    else:
        outs = [
            pltpu.make_async_copy(ref, out, sem_local.at[slot])
            for slot, (ref, out) in enumerate(zip((w_first, mid_wide.at[pl.ds(0, 9 * width), :], w_last), grads_out))
        ]
        for copy in outs:
            copy.start()
        for copy in outs:
            copy.wait()
    head_leave.wait()
    for copy in to_mate + head_moves:
        copy.wait_send()


def client_pass(gather, ratios, classes, features, labels, flag, params, head, weights):
    pixels, half = features.shape
    images = labels.shape[1]
    count_rows, channels = pixels // 2, 2 * half
    width = params.shape[0] // 2 * LANES - half
    head_rows = classes + -classes % 16
    mine_images = images // 2
    line = SIDE * mine_images
    middle = 9 * width
    blocks = 32
    group = channels // SPOTS[0]
    vmem = pl.BlockSpec(memory_space=pltpu.VMEM)
    smem = pl.BlockSpec(memory_space=pltpu.SMEM)
    spots = SPOTS + (2,)
    scratch = [
        pltpu.VMEM((count_rows, channels), low_type),
        pltpu.VMEM((SPOTS[0] * count_rows, group), low_type),
        pltpu.VMEM(spots + (channels // blocks, width), low_type),
        pltpu.VMEM((middle, width), low_type),
        pltpu.VMEM(spots + (channels // blocks, width), low_type),
        pltpu.VMEM((count_rows, width), wide),
        pltpu.VMEM((count_rows, width), wide),
        pltpu.VMEM((count_rows, channels), wide),
        pltpu.VMEM((count_rows + 2 * line, width), low_type),
        pltpu.VMEM((count_rows + 2 * line, width), low_type),
        pltpu.VMEM((count_rows, width), low_type),
        pltpu.VMEM((count_rows, LANES), wide),
        pltpu.VMEM((2, 2, half + width), wide),
        pltpu.VMEM((2, head_rows, half), low_type),
        pltpu.VMEM((mine_images, channels), wide),
        pltpu.VMEM((mine_images, half), low_type),
        pltpu.VMEM((2, mine_images, half), low_type),
        pltpu.VMEM((2, head_rows, mine_images), low_type),
        pltpu.VMEM((6, 8, channels), wide),
        pltpu.VMEM((6, 8, channels), wide),
        pltpu.VMEM((24, channels), wide),
        pltpu.VMEM((3, 8, channels), wide),
        pltpu.SemaphoreType.DMA((11,)),
        pltpu.SemaphoreType.DMA((2, 6)),
        pltpu.SemaphoreType.DMA((2, 7)),
    ]
    any_space = pl.BlockSpec(memory_space=pl.ANY)
    if gather:
        counts = (channels // blocks, middle // blocks, channels // blocks)
        scratch += [pltpu.SemaphoreType.DMA((2, 3, 3))]
        scratch += [pltpu.SemaphoreType.DMA((2, 4, size)) for size in (6, 8, 6)]
        scratch += [pltpu.VMEM((4, 2, 2, rows, width), low_type) for rows in counts[1:]]
        for lead in ((4, 2), (4,), (4,)):
            scratch += [pltpu.VMEM(lead + (rows, width), low_type) for rows in counts]
        scratch += [pltpu.SemaphoreType.DMA((2, 4, size)) for size in (6, 8, 6, 6)]
        part = width // CUTS
        gram_rows = CUTS * (CUTS + 1) // 4 * part
        many = max(4 * counts[0], 2 * counts[1])
        scratch += [
            pltpu.VMEM((many, width), wide),
            pltpu.VMEM((sum(counts), width), low_type),
            pltpu.VMEM((4, 8, LANES), wide),
            pltpu.VMEM((6, 8, LANES), wide),
            pltpu.VMEM((gram_rows, 2 * part), wide),
            pltpu.VMEM((4, gram_rows // 8, 2 * part), wide),
            pltpu.VMEM((3, gram_rows // 8, 2 * part), wide),
            pltpu.VMEM((gram_rows, 2 * part), wide),
            pltpu.SemaphoreType.DMA((2, 6)),
            pltpu.SemaphoreType.DMA((2, 8)),
            pltpu.SemaphoreType.DMA((2, 14)),
        ]
        grads_shape = [
            jax.ShapeDtypeStruct((sum(counts), width), wide),
            jax.ShapeDtypeStruct((sum(counts), width), low_type),
        ]
        grads_specs = [any_space] * 2
    else:
        grads_shape = [jax.ShapeDtypeStruct(weight.shape, low_type) for weight in weights]
        grads_specs = [any_space] * 3
    return pl.pallas_call(
        functools.partial(client_kernel, gather, ratios, images, classes),
        out_shape=grads_shape
        + [
            jax.ShapeDtypeStruct(params.shape, wide),
            jax.ShapeDtypeStruct((classes * half // LANES, LANES), wide),
            jax.ShapeDtypeStruct((8, LANES), wide),
        ],
        in_specs=[any_space, vmem, smem, vmem, vmem] + [any_space] * len(weights),
        out_specs=grads_specs + [vmem, any_space, vmem],
        scratch_shapes=scratch,
        compiler_params=pltpu.CompilerParams(
            collective_id=0, has_side_effects=True, vmem_limit_bytes=VMEM_BYTES
        ),
    )(features, labels, flag, params, head, *weights)


def adam_update(param, grad, first, second, rate, decay):
    first = adam_first * first + (1.0 - adam_first) * grad
    second = adam_second * second + (1.0 - adam_second) * grad * grad
    first_hat = first / (1.0 - adam_first**STEP)
    second_hat = second / (1.0 - adam_second**STEP)
    return (
        param - rate * (first_hat / (jnp.sqrt(second_hat) + adam_epsilon) + decay * param),
        first,
        second,
    )


def gram_of(section):
    return lax.dot_general(section, section, (((0,), (0,)), ((), ())), precision=precise)


def square(gram):
    return jnp.dot(gram, gram, precision=precise)


def times_poly(left, mixed):
    return schulz_first * left + jnp.dot(left, mixed, precision=precise)


def schulz(sections):
    raw_grams = lax.psum(tuple(gram_of(section) for section in sections), ("client", "chan"))
    factors = [1.0 / (jnp.sqrt(jnp.trace(gram)) + 1e-07) for gram in raw_grams]
    current = [section * factor for section, factor in zip(sections, factors)]
    grams = [gram * (factor * factor) for gram, factor in zip(raw_grams, factors)]
    for turn in range(NS_STEPS):
        mixed = [schulz_second * gram + schulz_third * square(gram) for gram in grams]
        current = [times_poly(current[slot], mixed[slot]) for slot in range(3)]
        if turn + 1 < NS_STEPS:
            grams = [
                times_poly(times_poly(grams[slot], mixed[slot]), mixed[slot]) for slot in range(3)
            ]
    return current


def base_far(ratios, bounds, master, momentum, anchor, loss_tile, grads):
    sums = [
        lax.psum_scatter(flat_rows(grad).astype(wide), ("client", "chan"), scatter_dimension=0, tiled=True)
        for grad in grads
    ]
    grad_base = jnp.concatenate(sums, axis=0)
    momentum_new = momentum_decay * momentum + (grad_base + prox_weight * (master - anchor))
    current = schulz([momentum_new[bounds[slot] : bounds[slot + 1]] for slot in range(3)])
    ortho = jnp.concatenate([current[slot] * ratios[slot] for slot in range(3)], axis=0)
    return momentum_new, ortho, lax.psum(loss_tile, ("client", "chan"))


def as_stored(rows, shape):
    return with_layout_constraint(rows.reshape(shape), Layout(major_to_minor=tuple(range(len(shape)))))


def on_device(
    features,
    labels,
    mask,
    base_master,
    base_momentum,
    global_base,
    norm_params,
    norm_first,
    norm_second,
    head,
    head_first,
    head_second,
):
    halves = lax.axis_size("chan")
    blocks = lax.axis_size("client") * halves
    half = features.shape[2]
    width = base_master.shape[2]
    channels = half * halves
    classes = head.shape[2]
    rows_first = channels // blocks
    rows_mid = 9 * width // blocks
    bounds = (0, rows_first, rows_first + rows_mid, base_master.shape[1])
    ratio = (channels / width) ** 0.5
    ratios = (ratio, 3.0, ratio)
    master, momentum, anchor = base_master[0], base_momentum[0], global_base[0]
    norms = [value.reshape(-1, LANES) for value in (norm_params, norm_first, norm_second)]
    heads = [jnp.transpose(value, (2, 0, 1)).reshape(-1, LANES) for value in (head, head_first, head_second)]
    near = lax.axis_size("client") == SPOTS[0] * SPOTS[1] * SPOTS[2]
    if near:
        weights = [master, momentum, anchor]
    else:
        low_master = master.astype(low_type)
        weights = [
            lax.all_gather(low_master[bounds[slot] : bounds[slot + 1]], ("client", "chan"), axis=0, tiled=True)
            for slot in range(3)
        ]
        split = SPOTS + (2, channels // 32, width)
        weights = [weights[0].reshape(split), weights[1], weights[2].reshape(split)]
    *grads, grad_norm, grad_head, loss_tile = client_pass(
        near, ratios, classes, features[0], labels, mask, norms[0], heads[0], weights
    )
    if near:
        fresh_momentum, ortho = grads
    else:
        fresh_momentum, ortho, loss_tile = base_far(ratios, bounds, master, momentum, anchor, loss_tile, grads)
    loss, momentum_new, base_new, base_low, *fresh = update_pass(
        loss_tile, master, fresh_momentum, ortho, norms, grad_norm, heads, grad_head
    )
    fresh_norms = [as_stored(value, norm_params.shape) for value in fresh[:3]]
    fresh_heads = [jnp.transpose(as_stored(value, (classes, 1, half)), (1, 2, 0)) for value in fresh[3:]]
    return (
        loss,
        base_new[None],
        momentum_new[None],
        base_low[None],
        *fresh_norms,
        *fresh_heads,
    )


def solution(mesh):
    wide_block = P(("client", "chan"), None, None)
    norm_block = P("client", None, "chan", None)
    head_block = P("client", "chan", None)
    return jax.shard_map(
        on_device,
        mesh=mesh,
        in_specs=(P("client", None, "chan"), P("client", None), P("client"))
        + (wide_block,) * 3
        + (norm_block,) * 3
        + (head_block,) * 3,
        out_specs=(P(),) + (wide_block,) * 3 + (norm_block,) * 3 + (head_block,) * 3,
        check_vma=False,
    )
```

```python
import functools

import jax
import jax.numpy as jnp
from jax import lax
from jax.experimental import pallas as pl
from jax.experimental.layout import Layout, with_layout_constraint
from jax.experimental.pallas import tpu as pltpu
from jax.sharding import PartitionSpec as P

NS_STEPS = 5
STEP = 10

low_type = jnp.bfloat16
wide = jnp.float32
MESH = pl.DeviceIdType.MESH
precise = lax.Precision.HIGHEST
norm_epsilon = 1e-05
prox_weight = 0.05
momentum_decay = 0.95
muon_rate = 0.3
muon_decay = 0.1
schulz_first = 3.4445
schulz_second = -4.775
schulz_third = 2.0315
adam_first = 0.9
adam_second = 0.95
adam_epsilon = 1e-08
head_rate = 0.01
head_decay = 0.05
norm_rate = 0.5

SIDE = 7
PIXELS = SIDE * SIDE
LANES = 128
SPOTS = (4, 2, 2)
CUTS = 4
VMEM_BYTES = 62 * 2**20


def dot_nn(left, right):
    return jnp.dot(left, right, preferred_element_type=wide)


def dot_nt(left, right):
    return lax.dot_general(left, right, (((1,), (1,)), ((), ())), preferred_element_type=wide)


def dot_tn(left, right):
    return lax.dot_general(left, right, (((0,), (0,)), ((), ())), preferred_element_type=wide)


def flat_rows(block):
    return block.reshape(-1, block.shape[-1])


def sigmoid(value):
    return 0.5 * jnp.tanh(0.5 * value) + 0.5


def fold_rows(value):
    return jnp.sum(value.reshape(value.shape[0] // 8, 8, value.shape[1]), axis=0)


def column_sum(value):
    return jnp.sum(value, axis=0, keepdims=True)


def remote(src, dst, send_sem, recv_sem, client, core):
    return pltpu.make_async_remote_copy(
        src_ref=src,
        dst_ref=dst,
        send_sem=send_sem,
        recv_sem=recv_sem,
        device_id=(client, core),
        device_id_type=MESH,
    )


class Place:
    def __init__(self):
        self.client = lax.axis_index("client")
        self.core = lax.axis_index("chan")
        self.z = self.client // 4
        self.y = (self.client // 2) % 2
        self.x = self.client % 2
        self.others = [
            self.z + 1 - 2 * (self.z % 2),
            (self.z + 2) % 4,
            3 - self.z,
        ]

    def at(self, z, y, x):
        return z * 4 + y * 2 + x

    def along_x(self):
        return self.at(self.z, self.y, 1 - self.x)

    def along_y(self):
        return self.at(self.z, 1 - self.y, self.x)

    def along_z(self, step):
        return self.at(self.others[step], self.y, self.x)

    def greet(self, whole, across=False):
        barrier = pltpu.get_barrier_semaphore()
        pairs = [(self.client, 1 - self.core)]
        if whole:
            pairs += [(self.along_x(), self.core), (self.along_y(), self.core)]
            pairs += [(self.along_z(step), self.core) for step in range(3)]
        if across:
            pairs += [(self.along_x(), 1 - self.core)]
        for pair in pairs:
            pl.semaphore_signal(barrier, inc=1, device_id=pair, device_id_type=MESH)
        pl.semaphore_wait(barrier, len(pairs))


def cut_rows(counts):
    pieces = []
    for slot, rows in enumerate(counts):
        middle = (rows // 16 + 1) // 2 * 16
        pieces.append((slot, 0, middle, 0))
        pieces.append((slot, middle, rows - middle, 1))
    return pieces


def block_ref(ref, size, z, y, x, core, start, count):
    if len(ref.shape) == 2:
        first = (((z * 2 + y) * 2 + x) * 2 + core) * size + start
        return ref.at[pl.ds(pl.multiple_of(first, 16), count), :]
    return ref.at[z, y, x, core, pl.ds(start, count), :]


class Spread:
    def __init__(self, place, weights, counts, sems):
        self.place = place
        self.weights = weights
        self.counts = counts
        self.pieces = cut_rows(counts)
        self.z_sems, self.near_sems, self.far_sems, self.core_sems = sems
        self.order = [place.z] + place.others

    def z_copy(self, step, slot):
        p = self.place
        ref = block_ref(self.weights[slot], self.counts[slot], p.z, p.y, p.x, p.core, 0, self.counts[slot])
        sems = self.z_sems
        return remote(ref, ref, sems.at[0, step, slot], sems.at[1, step, slot], p.along_z(step), p.core)

    def near_copy(self, turn, number):
        p = self.place
        slot, start, count, way = self.pieces[number]
        ref = block_ref(self.weights[slot], self.counts[slot], self.order[turn], p.y, p.x, p.core, start, count)
        sems = self.near_sems
        return remote(
            ref, ref, sems.at[0, turn, number], sems.at[1, turn, number], (p.along_x, p.along_y)[way](), p.core
        )

    def far_copies(self, turn, number):
        p = self.place
        slot, start, count, way = self.pieces[number]
        spot = self.order[turn]
        sems = self.far_sems
        copies = []
        for part, other in enumerate((0, 1) if slot == 1 else (slice(None),)):
            y, x = (p.y, other) if way == 0 else (other, p.x)
            ref = block_ref(self.weights[slot], self.counts[slot], spot, y, x, p.core, start, count)
            sem = number + 4 * part
            to = (p.along_y, p.along_x)[way]()
            copies.append(remote(ref, ref, sems.at[0, turn, sem], sems.at[1, turn, sem], to, p.core))
        return copies

    def core_copies(self, turn, slot):
        p = self.place
        sems = self.core_sems
        copies = []
        pairs = [(y, x) for y in (0, 1) for x in (0, 1)] if slot == 1 else [(slice(None), slice(None))]
        for part, (y, x) in enumerate(pairs):
            ref = block_ref(self.weights[slot], self.counts[slot], self.order[turn], y, x, p.core, 0, self.counts[slot])
            sem = (0, 2 + part, 1)[slot]
            copies.append(remote(ref, ref, sems.at[0, turn, sem], sems.at[1, turn, sem], p.client, 1 - p.core))
        return copies

    def fill(self, master):
        p = self.place
        start = 0
        for slot in range(3):
            rows = self.counts[slot]
            own = block_ref(self.weights[slot], self.counts[slot], p.z, p.y, p.x, p.core, 0, rows)
            own[...] = master[start : start + rows, :].astype(low_type)
            start += rows

    def begin(self):
        for step in range(3):
            self.z_copy(step, 0).start()
        self.near_start(0)

    def near_start(self, slot):
        for number in (2 * slot, 2 * slot + 1):
            self.near_copy(0, number).start()

    def steps(self):
        near, far, core, start = self.near_step, self.far_step, self.core_step, self.near_start
        groups = [
            [(far, 0, 0), (start, 1)],
            [(near, 1, 0)],
            [(near, 2, 0), (near, 3, 0)],
            [(far, 1, 0), (core, 0, 0), (far, 0, 1)],
            [(far, 2, 0), (far, 3, 0), (core, 1, 0)],
            [(core, 2, 0), (core, 3, 0), (near, 1, 1), (start, 2)],
            [(core, 0, 1), (near, 2, 1)],
            [(far, 1, 1), (near, 3, 1)],
            [(core, 1, 1), (far, 2, 1), (far, 0, 2)],
            [(far, 3, 1), (core, 2, 1), (near, 1, 2)],
            [(core, 3, 1), (core, 0, 2), (near, 2, 2)],
            [(far, 1, 2), (near, 3, 2)],
            [(core, 1, 2), (far, 2, 2)],
            [(far, 3, 2), (core, 2, 2)],
            [(core, 3, 2)],
        ]
        return [[functools.partial(*step) for step in group] for group in groups]

    def near_step(self, turn, slot):
        self.z_copy(turn - 1, slot).wait_recv()
        for number in (2 * slot, 2 * slot + 1):
            self.near_copy(turn, number).start()
        if slot < 2:
            self.z_copy(turn - 1, slot + 1).start()

    def far_step(self, turn, slot):
        for number in (2 * slot, 2 * slot + 1):
            self.near_copy(turn, number).wait_recv()
            for copy in self.far_copies(turn, number):
                copy.start()

    def core_step(self, turn, slot):
        for number in (2 * slot, 2 * slot + 1):
            for copy in self.far_copies(turn, number):
                copy.wait_recv()
        for copy in self.core_copies(turn, slot):
            copy.start()

    def arrive(self, slot):
        for turn in range(4):
            for copy in self.core_copies(turn, slot):
                copy.wait_recv()

    def drain(self, slot):
        for step in range(3):
            self.z_copy(step, slot).wait_send()
        for turn in range(4):
            for copy in self.core_copies(turn, slot):
                copy.wait_send()
            for number in (2 * slot, 2 * slot + 1):
                self.near_copy(turn, number).wait_send()
                for copy in self.far_copies(turn, number):
                    copy.wait_send()


class Fold:
    def __init__(self, place, grads, counts, parts):
        self.place = place
        self.grads = grads
        self.counts = counts
        self.pieces = cut_rows(counts)
        self.core_boxes = [parts[1], parts[0], parts[1]]
        self.near_boxes, self.far_boxes, self.z_boxes = [parts[3 * k + 2 : 3 * k + 5] for k in range(3)]
        self.core_sems, self.near_sems, self.far_sems, self.z_sems = parts[11:]

    def core_copies(self, which, slot):
        p = self.place
        sems = self.core_sems
        copies = []
        pairs = [(y, x) for y in (0, 1) for x in (0, 1)] if slot == 1 else [(slice(None), slice(None))]
        for part, (y, x) in enumerate(pairs):
            ref = block_ref(self.grads[slot], self.counts[slot], which, y, x, 1 - p.core, 0, self.counts[slot])
            box = self.core_boxes[slot].at[which, y, x]
            sem = (0, 2 + part, 1)[slot]
            copies.append(remote(ref, box, sems.at[0, which, sem], sems.at[1, which, sem], p.client, 1 - p.core))
        return copies

    def near_copies(self, which, number):
        p = self.place
        slot, start, count, way = self.pieces[number]
        sems = self.near_sems
        copies = []
        for part, other in enumerate((0, 1) if slot == 1 else (slice(None),)):
            y, x = (other, 1 - p.x) if way == 0 else (1 - p.y, other)
            ref = block_ref(self.grads[slot], self.counts[slot], which, y, x, p.core, start, count)
            box = self.near_boxes[slot].at[which, other, pl.ds(start, count), :]
            sem = number + 4 * part
            to = (p.along_x, p.along_y)[way]()
            copies.append(remote(ref, box, sems.at[0, which, sem], sems.at[1, which, sem], to, p.core))
        return copies

    def far_copy(self, which, number):
        p = self.place
        slot, start, count, way = self.pieces[number]
        y, x = (1 - p.y, p.x) if way == 0 else (p.y, 1 - p.x)
        ref = block_ref(self.grads[slot], self.counts[slot], which, y, x, p.core, start, count)
        box = self.far_boxes[slot].at[which, pl.ds(start, count), :]
        sems = self.far_sems
        return remote(
            ref, box, sems.at[0, which, number], sems.at[1, which, number], (p.along_y, p.along_x)[way](), p.core
        )

    def z_copy(self, which, sender, number):
        p = self.place
        slot, start, count, _ = self.pieces[number]
        rows = pl.ds(start, count)
        sems = self.z_sems
        return remote(
            block_ref(self.grads[slot], self.counts[slot], which, p.y, p.x, p.core, start, count),
            self.z_boxes[slot].at[sender, rows, :],
            sems.at[0, which, number],
            sems.at[1, sender, number],
            p.at(which, p.y, p.x),
            p.core,
        )

    def begin(self, which, slot):
        for copy in self.core_copies(which, slot):
            copy.start()

    def add(self, slot, spots, start, count, box):
        ref = block_ref(self.grads[slot], self.counts[slot], *spots, self.place.core, start, count)
        ref[...] = (ref[...].astype(wide) + box.astype(wide)).astype(low_type)

    def core_step(self, which, slot):
        for copy in self.core_copies(which, slot):
            copy.wait_recv()
        pairs = [(y, x) for y in (0, 1) for x in (0, 1)] if slot == 1 else [(slice(None), slice(None))]
        for y, x in pairs:
            self.add(slot, (which, y, x), 0, self.counts[slot], self.core_boxes[slot][which, y, x])
        for number in (2 * slot, 2 * slot + 1):
            for copy in self.near_copies(which, number):
                copy.start()

    def near_step(self, which, slot):
        p = self.place
        for number in (2 * slot, 2 * slot + 1):
            _, start, count, way = self.pieces[number]
            for copy in self.near_copies(which, number):
                copy.wait_recv()
            for other in (0, 1) if slot == 1 else (slice(None),):
                y, x = (other, p.x) if way == 0 else (p.y, other)
                box = self.near_boxes[slot][which, other, pl.ds(start, count), :]
                self.add(slot, (which, y, x), start, count, box)
            self.far_copy(which, number).start()

    def far_step(self, which, slot):
        p = self.place
        for number in (2 * slot, 2 * slot + 1):
            _, start, count, way = self.pieces[number]
            self.far_copy(which, number).wait_recv()
            box = self.far_boxes[slot][which, pl.ds(start, count), :]
            self.add(slot, (which, p.y, p.x), start, count, box)

            @pl.when(p.z != which)
            def _():
                self.z_copy(which, p.z, number).start()

    def result(self, slot):
        p = self.place
        self.z_boxes[slot][p.z] = block_ref(self.grads[slot], self.counts[slot], p.z, p.y, p.x, p.core, 0, self.counts[slot])[...]
        for sender in range(4):

            @pl.when(p.z != sender)
            def _():
                for number in (2 * slot, 2 * slot + 1):
                    self.z_copy(sender, sender, number).wait_recv()

        total = self.z_boxes[slot][0].astype(wide)
        for sender in range(1, 4):
            total += self.z_boxes[slot][sender].astype(wide)
        return total

    def drain(self):
        for which in range(4):
            for slot in range(3):
                for copy in self.core_copies(which, slot):
                    copy.wait_send()
            for number in range(6):
                for copy in self.near_copies(which, number):
                    copy.wait_send()
                self.far_copy(which, number).wait_send()

            @pl.when(self.place.z != which)
            def _():
                for number in range(6):
                    self.z_copy(which, self.place.z, number).wait_send()
class GramSum:
    def __init__(self, place, data, total, boxes, sems):
        self.place = place
        self.data = data
        self.total = total
        self.y_box, self.z_box = boxes
        self.sems = sems
        self.share = data.shape[0] // 8
        self.down_order = place.others[::-1] + [place.z]

    def rows(self, z, y):
        return pl.ds(pl.multiple_of((z * 2 + y) * self.share, 8), self.share)

    def copy(self, number, src, dst, to):
        sems = self.sems
        return remote(src, dst, sems.at[0, number], sems.at[1, number], to, self.place.core)

    def y_down(self, turn):
        p = self.place
        src = self.data.at[self.rows(self.down_order[turn], 1 - p.y), :]
        return self.copy(turn, src, self.y_box.at[turn], p.along_y())

    def z_down(self, step):
        p = self.place
        src = self.data.at[self.rows(p.others[step], p.y), :]
        return self.copy(4 + step, src, self.z_box.at[step], p.along_z(step))

    def z_up(self, step):
        p = self.place
        ref = self.total.at[self.rows(p.z, p.y), :]
        return self.copy(7 + step, ref, ref, p.along_z(step))

    def y_up(self, turn):
        p = self.place
        ref = self.total.at[self.rows(([p.z] + p.others)[turn], p.y), :]
        return self.copy(10 + turn, ref, ref, p.along_y())

    def start(self):
        for turn in range(4):
            self.y_down(turn).start()

    def pass_down(self):
        for turn in range(4):
            self.y_down(turn).wait_recv()
            self.data[self.rows(self.down_order[turn], self.place.y), :] += self.y_box[turn]
            if turn < 3:
                self.z_down(2 - turn).start()

    def turn_up(self):
        p = self.place
        mine = self.rows(p.z, p.y)
        value = self.data[mine, :]
        for step in (2, 1, 0):
            self.z_down(step).wait_recv()
            value += self.z_box[step]
        self.total[mine, :] = value
        for step in range(3):
            self.z_up(step).start()
        self.y_up(0).start()

    def pass_up(self):
        for step in range(3):
            self.z_up(step).wait_recv()
            self.y_up(1 + step).start()

    def close(self):
        for turn in range(4):
            self.y_up(turn).wait_recv()

    def drain(self):
        for turn in range(4):
            self.y_down(turn).wait_send()
            self.y_up(turn).wait_send()
        for step in range(3):
            self.z_down(step).wait_send()
            self.z_up(step).wait_send()


class TileSum:
    def __init__(self, place, tiles, boxes, sems):
        self.place = place
        self.tiles = tiles
        self.boxes = boxes
        self.sems = sems

    def copy(self, stage, box):
        p = self.place
        to = (p.client, p.along_x(), p.along_y()) + tuple(p.along_z(step) for step in range(3))
        core = 1 - p.core if box == 0 else p.core
        return remote(
            self.tiles.at[stage], self.boxes.at[box], self.sems.at[0, box], self.sems.at[1, box], to[box], core
        )

    def start(self):
        self.copy(0, 0).start()

    def pair(self, stage):
        self.copy(stage, stage).wait_recv()
        self.tiles[stage + 1] = self.tiles[stage] + self.boxes[stage]
        if stage < 2:
            self.copy(stage + 1, stage + 1).start()
        else:
            for step in range(3):
                self.copy(3, 3 + step).start()

    def result(self):
        for step in range(3):
            self.copy(3, 3 + step).wait_recv()
        return (self.tiles[3] + self.boxes[3]) + (self.boxes[4] + self.boxes[5])

    def drain(self):
        for stage in range(3):
            self.copy(stage, stage).wait_send()
        for step in range(3):
            self.copy(3, 3 + step).wait_send()


def halves_of(value):
    high = value.astype(low_type)
    return high, (value - high.astype(wide)).astype(low_type)


class Share:
    def __init__(self, place, sizes, buffers, sems):
        self.place = place
        self.sizes = sizes
        self.fresh, self.rows_in, self.rows_out, self.back = buffers
        self.sems = sems
        self.bounds = [0, sizes[0], sizes[0] + sizes[1], sum(sizes)]
        p = place
        self.duty = jnp.where(p.x == 1, 1, 2 * p.core)
        self.mine = p.x * 2 + p.core

    def section(self, slot):
        return pl.ds(self.bounds[slot], self.sizes[slot])

    def spot(self, slot, x, core):
        number = x if slot == 1 else x * 2 + core
        return pl.ds(pl.multiple_of(number * self.sizes[slot], 16), self.sizes[slot])

    def doer(self, slot):
        return (0, 0) if slot == 0 else (0, 1) if slot == 2 else (1, self.place.core)

    def out_copy(self, slot):
        p = self.place
        x, core = self.doer(slot)
        return remote(
            self.fresh.at[self.section(slot), :],
            self.rows_in.at[self.spot(slot, p.x, p.core), :],
            self.sems.at[0, slot],
            self.sems.at[1, self.mine],
            p.at(p.z, p.y, x),
            core,
        )

    def in_copy(self, slot, x, core):
        p = self.place
        return remote(
            self.fresh.at[self.section(slot), :],
            self.rows_in.at[self.spot(slot, x, core), :],
            self.sems.at[0, slot],
            self.sems.at[1, x * 2 + core],
            p.at(p.z, p.y, x),
            core,
        )

    def back_copy(self, slot, x, core):
        p = self.place
        return remote(
            self.rows_out.at[self.spot(slot, x, core), :],
            self.back.at[self.section(slot), :],
            self.sems.at[0, 3 + x * 2 + core],
            self.sems.at[1, 4 + slot],
            p.at(p.z, p.y, x),
            core,
        )

    def users(self, slot):
        p = self.place
        if slot == 1:
            return [(0, p.core), (1, p.core)]
        return [(x, core) for x in (0, 1) for core in (0, 1)]

    def send(self, slot):
        @pl.when(self.duty != slot)
        def _():
            self.out_copy(slot).start()

        @pl.when(self.duty == slot)
        def _():
            self.rows_in[self.spot(slot, self.place.x, self.place.core), :] = self.fresh[self.section(slot), :]

    def gather(self, slot):
        p = self.place
        for x, core in self.users(slot):

            @pl.when((p.x != x) | (p.core != core))
            def _():
                self.in_copy(slot, x, core).wait_recv()

    def give_back(self):
        p = self.place
        for slot in range(3):

            @pl.when(self.duty == slot)
            def _():
                for x, core in self.users(slot):

                    @pl.when((p.x != x) | (p.core != core))
                    def _():
                        self.back_copy(slot, x, core).start()

                self.back[self.section(slot), :] = self.rows_out[self.spot(slot, p.x, p.core), :]

    def finish(self):
        p = self.place
        for slot in range(3):

            @pl.when(self.duty != slot)
            def _():
                self.back_copy(slot, p.x, p.core).wait_recv()
                self.out_copy(slot).wait_send()

            @pl.when(self.duty == slot)
            def _():
                for x, core in self.users(slot):

                    @pl.when((p.x != x) | (p.core != core))
                    def _():
                        self.back_copy(slot, x, core).wait_send()


def corner_spot(number, part):
    row, column = number // 2, number % 2
    return slice(row * part, (row + 1) * part), slice(column * part, (column + 1) * part)


def triangle(width):
    part = width // CUTS
    return part, [(row, column) for row in range(CUTS) for column in range(row, CUTS)]


def form_gram(place, slot, share, share_sems, gram, mate_gram, rows_in):
    part, corners = triangle(rows_in.shape[1])
    share.gather(slot)
    high, low = halves_of(rows_in[...])
    left = jnp.concatenate([high, high, low], axis=0)
    right = jnp.concatenate([high, low, high], axis=0)
    for row in range(CUTS):
        strip = dot_tn(left[:, row * part : (row + 1) * part], right[:, row * part :])
        for column in range(row, CUTS):
            gram[corner_spot(corners.index((row, column)), part)] = strip[
                :, (column - row) * part : (column - row + 1) * part
            ]

    if slot == 1:
        swap = remote(gram, mate_gram, share_sems.at[0, 7], share_sems.at[1, 7], place.client, 1 - place.core)
        swap.start()
        swap.wait()
        gram[...] += mate_gram[...]


def orthogonal(ratios, share, gram_total, squares, rows_in, low_rows):
    grams, mixed, once = squares
    count, width = rows_in.shape
    part, corners = triangle(width)
    right_high, right_low = [low_rows.at[pl.ds(count + spot * width, width), :] for spot in range(2)]

    def set_right(value_ref):
        for start in range(0, width, part):
            rows = slice(start, start + part)
            right_high[rows, :], right_low[rows, :] = halves_of(value_ref[rows, :])

    def times_right(value):
        high, low = halves_of(value)
        left = jnp.concatenate([high, high, low], axis=1)
        right = jnp.concatenate([right_high[...], right_low[...], right_high[...]], axis=0)
        return dot_nn(left, right)

    spots = lax.broadcasted_iota(jnp.int32, (part, part), 0)
    diagonal = spots == lax.broadcasted_iota(jnp.int32, (part, part), 1)
    trace = 0.0
    for number, (row, column) in enumerate(corners):
        if row == column:
            trace += jnp.sum(jnp.where(diagonal, gram_total[corner_spot(number, part)], 0.0))
    factor = 1.0 / (jnp.sqrt(trace) + 1e-07)
    square = factor * factor
    for number, (row, column) in enumerate(corners):
        rows, columns = slice(row * part, (row + 1) * part), slice(column * part, (column + 1) * part)
        block = gram_total[corner_spot(number, part)] * square
        grams[rows, columns] = block
        if row < column:
            grams[columns, rows] = block.T
    rows_in[...] = rows_in[...] * factor

    def turn(number, carry):
        set_right(grams)
        mixed[...] = schulz_second * grams[...] + schulz_third * times_right(grams[...])
        set_right(mixed)

        @pl.when(number < NS_STEPS - 1)
        def _():
            both = times_right(jnp.concatenate([grams[...], rows_in[...]], axis=0))
            once[...] = schulz_first * grams[...] + both[:width]
            rows_in[...] = schulz_first * rows_in[...] + both[width:]
            grams[...] = schulz_first * once[...] + times_right(once[...])

        @pl.when(number == NS_STEPS - 1)
        def _():
            rows_in[...] = schulz_first * rows_in[...] + times_right(rows_in[...])

        return carry

    lax.fori_loop(0, NS_STEPS, turn, 0)
    ratio = jnp.where(share.duty == 1, ratios[1], ratios[0])
    low_rows[0:count, :] = (rows_in[...] * ratio).astype(low_type)
    share.give_back()


def update_kernel(loss_tile, master, fresh_momentum, ortho, *rest):
    norms, grad_norm, heads, grad_head, outs = rest[0:3], rest[3], rest[4:7], rest[7], rest[8:]
    loss_out, *outs = outs
    loss_out[0] = loss_tile[0, 0]
    loss_out[1] = loss_tile[0, 1]
    momentum_out, base_out, low_out = outs[0:3]
    held = master[...]
    momentum_out[...] = fresh_momentum[...]
    fresh = held - muon_rate * (ortho[...].astype(wide) + muon_decay * held)
    base_out[...] = fresh
    low_out[...] = fresh.astype(low_type)
    for targets, values, grad, rate, decay in (
        (outs[3:6], norms, grad_norm, norm_rate, 0.0),
        (outs[6:9], heads, grad_head, head_rate, head_decay),
    ):
        updates = adam_update(values[0][...], grad[...], values[1][...], values[2][...], rate, decay)
        for target, value in zip(targets, updates):
            target[...] = value


def update_pass(loss_tile, master, fresh_momentum, ortho, norms, grad_norm, heads, grad_head):
    vmem = pl.BlockSpec(memory_space=pltpu.VMEM)
    smem = pl.BlockSpec(memory_space=pltpu.SMEM)
    operands = [loss_tile, master, fresh_momentum, ortho, *norms, grad_norm, *heads, grad_head]
    outs = [(2,), master.shape, master.shape, master.shape] + [grad_norm.shape] * 3 + [grad_head.shape] * 3
    types = [wide, wide, wide, low_type] + [wide] * 6
    return pl.pallas_call(
        update_kernel,
        out_shape=[jax.ShapeDtypeStruct(shape, kind) for shape, kind in zip(outs, types)],
        in_specs=[smem] + [vmem] * (len(operands) - 1),
        out_specs=[smem] + [vmem] * (len(outs) - 1),
        compiler_params=pltpu.CompilerParams(vmem_limit_bytes=VMEM_BYTES),
    )(*operands)


def norm_stats(mine, theirs, count):
    gap = mine[0:1] - theirs[0:1]
    mean = 0.5 * (mine[0:1] + theirs[0:1])
    spread = mine[1:2] + theirs[1:2] + gap * gap * (0.5 * count)
    return mean, lax.rsqrt(spread / (2.0 * count) + norm_epsilon)


def client_kernel(
    gather,
    ratios,
    images,
    classes,
    features,
    labels,
    flag,
    params,
    head,
    *rest,
):
    if gather:
        master, momentum, anchor, *rest = rest
    else:
        first_in, middle_in, last_in, *rest = rest
    if gather:
        fresh_out, ortho_out, *rest = rest
    else:
        grads_out, rest = rest[:3], rest[3:]
    (
        grad_norm_out,
        grad_head_out,
        loss_out,
        x_all,
        mid_wide,
        w_first,
        w_middle,
        w_last,
        act_one,
        act_two,
        act_three,
        taps_one,
        taps_two,
        hidden_two,
        stage,
        params_all,
        head_all,
        grad_pool,
        pool_send,
        pool_all,
        logit_grads,
        sums_mine,
        sums_theirs,
        shift,
        fwd_stats,
        sem_local,
        sem_swap,
        sem_misc,
        *near_parts,
    ) = rest
    place = Place()
    core = place.core
    mate = (place.client, 1 - core)
    count_rows, channels = x_all.shape
    half = channels // 2
    width = act_one.shape[1]
    part = width // 2
    mine_images = images // 2
    line = SIDE * mine_images
    total_rows = 2.0 * count_rows

    def tile(index):
        return pl.ds(pl.multiple_of(index * line, line), line)

    def lanes(index, size):
        return pl.ds(pl.multiple_of(index * size, size), size)

    weights = (w_first, w_middle, w_last)
    if gather:
        held = act_three.at[pl.ds(0, master.shape[0]), pl.ds(0, width)]
        load = pltpu.make_async_copy(master, held, sem_local.at[8])
        load.start()
        counts = [channels // 32, 9 * width // 32, channels // 32]
        spread = Spread(place, weights, counts, near_parts[:4])
        fold = Fold(place, (w_first, mid_wide, w_last), counts, near_parts[4:19])
        rows_in, back, tiles, tile_boxes, gram_total, y_box, z_box, mate_gram = near_parts[19:27]
        tile_sems, share_sems, gram_sems = near_parts[27:]
        block_rows = master.shape[0]
        side_space = pl.ds(half, width)
        held_base, held_momentum, held_anchor, fresh = [
            act_three.at[pl.ds(number * block_rows, block_rows), side_space] for number in range(4)
        ]
        rows_in[...] = jnp.zeros_like(rows_in)
        share = Share(place, counts, (fresh, rows_in, hidden_two, back), share_sems)
        tile_sum = TileSum(place, tiles, tile_boxes, tile_sems)
        due = spread.steps()
        load.wait()
        spread.fill(held)
        place.greet(True, True)
        spread.begin()
    else:
        place.greet(False)
        loads = [
            pltpu.make_async_copy(src, dst, sem_local.at[8 + slot])
            for slot, (src, dst) in enumerate(zip((first_in, middle_in, last_in), weights))
        ]
        for load in loads:
            load.start()
        due = []

    quarter = half // 2
    own_rows = pl.ds(pl.multiple_of(core * count_rows, count_rows), count_rows)
    mate_rows = pl.ds(pl.multiple_of((1 - core) * count_rows, count_rows), count_rows)
    top_rows = pl.ds(0, count_rows)
    own_copies = [
        pltpu.make_async_copy(
            features.at[own_rows, pl.ds(side * quarter, quarter)], buffer, sem_local.at[side]
        )
        for side, buffer in enumerate((hidden_two, mid_wide.at[top_rows, :]))
    ]
    per_kind = params.shape[0] // 2
    for kind in range(2):
        rows = [params[kind * per_kind + spot : kind * per_kind + spot + 1, :] for spot in range(per_kind)]
        params_all[core, kind : kind + 1, :] = jnp.concatenate(rows, axis=1)
    head_all[core] = jnp.zeros(head_all.shape[1:], low_type)
    for spot in range(half // LANES):
        head_all[core, 0:classes, spot * LANES : (spot + 1) * LANES] = head[
            pl.ds(spot, classes, stride=half // LANES), :
        ].astype(low_type)
    to_mate = [
        remote(params_all.at[core], params_all.at[core], sem_misc.at[0, 0], sem_misc.at[1, 0], *mate),
        remote(head_all.at[core], head_all.at[core], sem_misc.at[0, 1], sem_misc.at[1, 1], *mate),
    ]
    for side, buffer in enumerate((taps_one, taps_two)):
        to_mate.append(
            remote(
                features.at[mate_rows, pl.ds(side * quarter, quarter)],
                buffer.at[top_rows, :],
                sem_misc.at[0, 5 + side],
                sem_misc.at[1, 5 + side],
                *mate,
            )
        )
    for copy in to_mate + own_copies:
        copy.start()

    def advance(count):
        for group in due[:count]:
            for step in group:
                step()
        del due[:count]

    def advance_at(index, spots):
        for spot, group in zip(spots, due):

            @pl.when(index == spot)
            def _():
                for step in group:
                    step()

    def arrive(slot, left):
        if gather:
            advance(len(due) - left)
            spread.arrive(slot)
        else:
            loads[slot].wait()

    def arrive_turns(slot, turns):
        if gather:
            for turn in turns:
                for copy in spread.core_copies(turn, slot):
                    copy.wait_recv()

    def fold_step(kind, slot, which):
        if gather:
            (fold.core_step, fold.near_step, fold.far_step)[kind](which, slot)

    def fold_at(index, spot, *steps):
        @pl.when(index == spot)
        def _():
            for step in steps:
                fold_step(*step)

    def fold_begin(which, slot):
        if gather:
            fold.begin(which, slot)

    def zero_edges(buffer):
        edge = jnp.zeros((line,) + buffer.shape[1:], low_type)
        buffer[0:line, :] = edge
        buffer[line + count_rows : 2 * line + count_rows, :] = edge

    advance(3)
    for copy in own_copies:
        copy.wait()

    def turn_from(source, base):
        def turn(index, carry):
            stage[...] = source(lanes(index, LANES)).astype(wide)

            def pixel(spot, inner):
                x_all[
                    pl.ds(pl.multiple_of(spot * mine_images, mine_images), mine_images),
                    pl.ds(pl.multiple_of(base + index * LANES, LANES), LANES),
                ] = stage[pl.ds(spot, mine_images, stride=PIXELS), :].astype(low_type)
                return inner

            return lax.fori_loop(0, PIXELS, pixel, carry, unroll=7)

        return turn

    quarters = quarter // LANES
    own_base, mate_base = core * half, (1 - core) * half
    lax.fori_loop(0, quarters, turn_from(lambda columns: hidden_two[:, columns], own_base), 0)
    advance(1)
    lax.fori_loop(
        0,
        quarters,
        turn_from(lambda columns: mid_wide[0:count_rows, columns], own_base + quarter),
        0,
    )
    advance(1)
    for copy in to_mate:
        copy.wait_recv()
    lax.fori_loop(0, quarters, turn_from(lambda columns: taps_one[0:count_rows, columns], mate_base), 0)
    advance(1)
    lax.fori_loop(0, quarters, turn_from(lambda columns: taps_two[0:count_rows, columns], mate_base + quarter), 0)
    zero_edges(taps_one)
    zero_edges(taps_two)
    arrive(0, 9)

    def swap(slot, size):
        return remote(
            sums_mine.at[slot, :, pl.ds(0, size)],
            sums_theirs.at[slot, :, pl.ds(0, size)],
            sem_swap.at[0, slot],
            sem_swap.at[1, slot],
            *mate,
        )

    def gain_bias(lower, upper):
        rows = []
        for kind in range(2):
            pieces = [params_all[side, kind : kind + 1, lower:upper] for side in range(2)]
            rows.append(jnp.concatenate(pieces, axis=1))
        return rows

    def collect(index, value, columns, size):
        @pl.when(index == 0)
        def _():
            shift[0:1, pl.ds(0, size)] = column_sum(fold_rows(value)) / value.shape[0]
            shift[8:24, pl.ds(0, size)] = jnp.zeros((16, size), wide)

        gap = value - shift[0:1, pl.ds(0, size)]
        shift[8:16, pl.ds(0, size)] += fold_rows(gap)
        shift[16:24, pl.ds(0, size)] += fold_rows(gap * gap)

    def close_stats(slot, columns, size):
        sum_gap = column_sum(shift[8:16, pl.ds(0, size)])
        sum_square = column_sum(shift[16:24, pl.ds(0, size)])
        sums_mine[slot, 0:1, columns] = shift[0:1, pl.ds(0, size)] + sum_gap / count_rows
        sums_mine[slot, 1:2, columns] = sum_square - sum_gap * sum_gap / count_rows

    def look_over(act, columns):
        def look(index, carry):
            collect(index, act[tile(index), columns], None, width)
            return carry

        lax.fori_loop(0, SIDE, look, 0)

    groups = SPOTS[0]
    group = channels // groups

    def settle(slot, size):
        mean, scale = norm_stats(
            sums_mine[slot, 0:2, pl.ds(0, size)], sums_theirs[slot, 0:2, pl.ds(0, size)], float(count_rows)
        )
        fwd_stats[slot, 0:1, pl.ds(0, size)] = mean
        fwd_stats[slot, 1:2, pl.ds(0, size)] = scale

    whole_width = pl.ds(0, width)

    def first_part(index, carry):
        act_one[...] += dot_nn(x_all[:, lanes(index, group)], flat_rows(w_first[index]))
        advance_at(index, (0, 1, 2))
        return carry

    act_one[...] = jnp.zeros_like(act_one)
    lax.fori_loop(0, groups, first_part, 0)
    del due[:3]
    look_over(act_one, whole_width)
    close_stats(0, whole_width, width)
    move = swap(0, width)
    move.start()
    advance(1)
    move.wait()
    settle(0, width)

    gain_one, bias_one = gain_bias(0, part)
    gain_two, bias_two = gain_bias(part, width)
    gain_three, bias_three = gain_bias(width, width + half)

    def normal(act, slot, index):
        mean = fwd_stats[slot, 0:1, pl.ds(0, width)]
        return (act[tile(index), :] - mean) * fwd_stats[slot, 1:2, pl.ds(0, width)]

    def hide_one(index, carry):
        value = normal(act_one, 0, index) * gain_one + bias_one
        taps_one[pl.ds(pl.multiple_of((index + 1) * line, line), line), :] = (value * sigmoid(value)).astype(low_type)
        return carry

    lax.fori_loop(0, SIDE, hide_one, 0)
    if gather:
        arrive_turns(1, (0, 1))
    else:
        arrive(1, 0)

    step = mine_images
    piece = width // 2

    def row_windows(buffer, down, start, reach):
        if reach == line:
            return buffer[pl.ds(pl.multiple_of(down * line, line), count_rows), :]
        windows = [
            buffer[pl.ds(pl.multiple_of((down + row) * line + start, step), reach), :] for row in range(SIDE)
        ]
        return jnp.concatenate(windows, axis=0)

    def add_windows(target, columns, value, start, reach):
        for row in range(SIDE):
            rows = slice(row * line + start, row * line + start + reach)
            target[rows, columns] += value[row * reach : (row + 1) * reach]

    low_start, high_start, reaches = (0, 0, step), (step, 0, 0), (line - step, line, line - step)

    early, taps = 4, 9

    def second_part(index, carry):
        tap = jnp.where(place.z < 2, index, (index + taps - early) % taps) if gather else index

        @pl.when(index == early)
        def _():
            arrive_turns(1, (2, 3))

        down = tap // 3
        for over in range(3):

            @pl.when(tap % 3 == over)
            def _():
                left = row_windows(taps_one, down, low_start[over], reaches[over])
                kernel = w_middle[pl.ds(pl.multiple_of(tap * width, width), width), :]
                add_windows(act_two, slice(None), dot_nn(left, kernel), high_start[over], reaches[over])

        advance_at(index, (2, 5, 6, 8))
        return carry

    act_two[...] = jnp.zeros_like(act_two)
    lax.fori_loop(0, taps, second_part, 0)
    del due[:4]
    look_over(act_two, whole_width)
    close_stats(1, whole_width, width)
    move_two = swap(1, width)
    move_two.start()
    arrive(2, 0)
    if gather:
        spread.drain(0)

    def turn_weights(which, carry):
        w_first[which] = jnp.transpose(flat_rows(w_last[which])).reshape(w_first.shape[1:])
        return carry

    lax.fori_loop(0, groups, turn_weights, 0)
    move_two.wait()
    settle(1, width)

    def third_line(index, carry):
        value = normal(act_two, 1, index) * gain_two + bias_two
        hidden = (value * sigmoid(value)).astype(low_type)
        hidden_two[tile(index), :] = hidden
        for which in range(groups):
            columns = slice(which * group, (which + 1) * group)
            value = dot_nn(hidden, flat_rows(w_first[which]))
            act_three[tile(index), columns] = value
            start = jnp.where(index == 0, column_sum(value[0:8]) / 8.0, shift[0:1, columns])
            gap = value - start
            kept_sums = jnp.where(index == 0, 0.0, shift[8:24, columns])
            shift[0:1, columns] = start
            shift[8:16, columns] = kept_sums[0:8] + fold_rows(gap)
            shift[16:24, columns] = kept_sums[8:16] + fold_rows(gap * gap)
        return carry

    lax.fori_loop(0, SIDE, third_line, 0)
    close_stats(2, pl.ds(0, channels), channels)
    move_three = swap(2, channels)
    move_three.start()
    move_three.wait()
    settle(2, channels)

    per_group = group // LANES

    def block_of(spot):
        return pl.ds(pl.multiple_of(spot * mine_images, mine_images), mine_images)

    def mid_line(which, index):
        return pl.ds(pl.multiple_of(which * count_rows + index * line, line), line)

    kept = channels // LANES * mine_images

    def gathered(kind):
        starts = range(kind * kept, (kind + 1) * kept, mine_images)
        return jnp.concatenate([stage[start : start + mine_images, :] for start in starts], axis=1)

    fwd_stats[2, 4:5, :] = fwd_stats[2, 1:2, :] * gain_three
    fwd_stats[2, 5:6, :] = bias_three - fwd_stats[2, 0:1, :] * fwd_stats[2, 4:5, :]

    def emit(index, carry):
        columns = lanes(index, LANES)
        slant, level = fwd_stats[2, 4:5, columns], fwd_stats[2, 5:6, columns]

        def pixels(row, sums):
            pooled, steeps, steeps_act = sums
            found = []
            for spot in range(SIDE):
                where = block_of(row * SIDE + spot)
                act = act_three[where, columns]
                half_total = 0.5 * (act * slant + level + x_all[where, columns].astype(wide))
                rise = 1.0 + jnp.tanh(half_total)
                out = half_total * rise
                steep = rise + out * (2.0 - rise)
                found.append(steep.astype(low_type))
                pooled, steeps, steeps_act = pooled + out, steeps + steep, steeps_act + steep * act
            mid_wide[mid_line(index // per_group, row), lanes(index % per_group, LANES)] = jnp.concatenate(
                found, axis=0
            )
            return pooled, steeps, steeps_act

        zero = jnp.zeros((mine_images, LANES), wide)
        sums = lax.fori_loop(0, SIDE, pixels, (zero, zero, zero))
        for kind, value in enumerate(sums):
            stage[pl.ds(pl.multiple_of(kind * kept + index * mine_images, mine_images), mine_images), :] = value
        return carry

    lax.fori_loop(0, channels // LANES, emit, 0)

    pooled = (gathered(0) / PIXELS).astype(low_type)
    head_full = jnp.concatenate([head_all[0], head_all[1]], axis=1)
    logits = dot_nt(head_full, pooled)
    spots = lax.broadcasted_iota(jnp.int32, logits.shape, 0)
    inside = spots < classes
    first_labels, second_labels = labels[0:1, 0:mine_images], labels[0:1, mine_images:]
    onehot = (spots == jnp.where(core == 0, first_labels, second_labels)).astype(wide)
    top = jnp.max(jnp.where(inside, logits, -jnp.inf), axis=0, keepdims=True)
    powers = jnp.where(inside, jnp.exp(logits - top), 0.0)
    power_sum = jnp.sum(powers, axis=0, keepdims=True)
    picked = jnp.sum(logits * onehot, axis=0, keepdims=True)
    each_loss = top + jnp.log(power_sum) - picked
    taking = flag[0].astype(wide)
    tile_spots = lax.broadcasted_iota(jnp.int32, loss_out.shape, 1)
    loss_out[...] = jnp.where(tile_spots == 0, taking * jnp.sum(each_loss), taking * mine_images)
    grads = (taking / images * (powers / power_sum - onehot)).astype(low_type)
    grad_pool[...] = dot_tn(grads, head_full) * (0.5 / PIXELS)
    logit_grads[core] = grads
    pool_all[core] = pooled[:, 0:half]
    pool_send[...] = pooled[:, half:]

    @pl.when(core == 1)
    def _():
        pool_all[core] = pooled[:, half:]
        pool_send[...] = pooled[:, 0:half]

    head_moves = [
        remote(pool_send, pool_all.at[core], sem_misc.at[0, 3], sem_misc.at[1, 3], *mate),
        remote(logit_grads.at[core], logit_grads.at[core], sem_misc.at[0, 4], sem_misc.at[1, 4], *mate),
    ]

    steeps = gathered(1)
    steeps_normed = (gathered(2) - fwd_stats[2, 0:1, :] * steeps) * fwd_stats[2, 1:2, :]
    sums_mine[3, 0:1, :] = column_sum(grad_pool[...] * steeps)
    sums_mine[3, 1:2, :] = column_sum(grad_pool[...] * steeps_normed)
    move_back = swap(3, channels)
    move_back.start()
    for copy in head_moves:
        copy.start()
    move_back.wait()

    def back_terms(slot, layer, size, gain):
        columns = pl.ds(0, size)
        sums = sums_mine[slot, 0:2, columns] + sums_theirs[slot, 0:2, columns]
        sums_mine[slot, 2:4, columns] = sums
        scale = fwd_stats[layer, 1:2, columns]
        return (
            scale * gain,
            scale * gain * sums[0:1] / total_rows,
            scale * scale * gain * sums[1:2] / total_rows,
        )

    first, second, third = back_terms(3, 2, channels, gain_three)
    fwd_stats[2, 4:5, :] = second - third * fwd_stats[2, 0:1, :]
    fwd_stats[2, 5:6, :] = third
    grad_pool[...] = grad_pool[...] * first

    def pull(index):
        for which in range(groups):
            columns = slice(which * group, (which + 1) * group)
            reach = grad_pool[:, columns]
            steep = mid_wide[mid_line(which, index), :].astype(wide)
            value = jnp.concatenate([reach] * SIDE, axis=0) * steep
            value = value - fwd_stats[2, 4:5, columns] - fwd_stats[2, 5:6, columns] * act_three[tile(index), columns]
            mid_wide[mid_line(which, index), :] = value.astype(low_type)

    pull(0)

    def drop_into(act, slot, gain, bias, columns):
        size = pl.ds(0, width)
        shift[8:24, size] = jnp.zeros((16, width), wide)

        def drop(index, carry):
            normed = normal(act, slot, index)
            norm = normed * gain + bias
            sig = sigmoid(norm)
            grad = act_three[tile(index), columns] * (sig + norm * sig * (1.0 - sig))
            act_three[tile(index), columns] = grad
            shift[8:16, size] += fold_rows(grad)
            shift[16:24, size] += fold_rows(grad * normed)
            return carry

        lax.fori_loop(0, SIDE, drop, 0)

    def close_back(slot):
        size = pl.ds(0, width)
        sums_mine[slot, 0:1, size] = column_sum(shift[8:16, size])
        sums_mine[slot, 1:2, size] = column_sum(shift[16:24, size])

    space_two, space_one = pl.ds(0, width), pl.ds(width, width)

    def mid_group(which):
        return mid_wide[pl.ds(pl.multiple_of(which * count_rows, count_rows), count_rows), :]

    def back_two(index):
        left = jnp.concatenate([mid_wide[mid_line(which, index), :] for which in range(groups)], axis=1)
        value = dot_nn(left, flat_rows(w_last[...]))
        normed = normal(act_two, 1, index)
        norm = normed * gain_two + bias_two
        sig = sigmoid(norm)
        grad = value * (sig + norm * sig * (1.0 - sig))
        act_three[tile(index), space_two] = grad
        size = pl.ds(0, width)
        shift[8:16, size] += fold_rows(grad)
        shift[16:24, size] += fold_rows(grad * normed)

    def back_two_line(index, carry):
        pull(index + 1)
        back_two(index)
        return carry

    shift[8:24, :] = jnp.zeros((16, channels), wide)
    lax.fori_loop(0, SIDE - 1, back_two_line, 0)
    back_two(SIDE - 1)
    close_back(4)
    move_back_two = swap(4, width)
    move_back_two.start()
    if gather:
        base_loads = [
            pltpu.make_async_copy(src, dst, sem_local.at[1 + number])
            for number, (src, dst) in enumerate(
                ((master, held_base), (momentum, held_momentum), (anchor, held_anchor))
            )
        ]
        for load in base_loads:
            load.start()
        tiles[0] = loss_out[...]
        tile_sum.start()

    def settle_section(slot):
        if gather:
            rows = share.section(slot)
            grad = fold.result(slot) + prox_weight * (held_base[rows, :] - held_anchor[rows, :])
            fresh[rows, :] = momentum_decay * held_momentum[rows, :] + grad
            share.send(slot)

    if gather:
        spread.drain(1)
        spread.drain(2)

    def put(ref, which, value):
        ref[which] = value.astype(low_type).reshape(ref.shape[1:])

    def expand_group(which, carry):
        put(w_last, which, dot_tn(mid_group(which), hidden_two[...]))
        fold_begin(which, 2)
        fold_at(which, 2, (0, 2, 0))
        fold_at(which, 3, (0, 2, 1))
        return carry

    lax.fori_loop(0, groups, expand_group, 0)
    move_back_two.wait()
    terms_two = back_terms(4, 1, width, gain_two)

    def back_act(terms, act, layer, index, columns):
        first, second, third = terms
        gap = act[tile(index), :] - fwd_stats[layer, 0:1, pl.ds(0, width)]
        return (first * act_three[tile(index), columns] - second - third * gap).astype(low_type)

    def grad_two(index, carry):
        taps_two[pl.ds(pl.multiple_of((index + 1) * line, line), line), :] = back_act(
            terms_two, act_two, 1, index, space_two
        )
        return carry

    lax.fori_loop(0, SIDE, grad_two, 0)
    fold_step(0, 2, 2)
    fold_step(1, 2, 0)
    core_step, near_step, far_step = 0, 1, 2
    plan = {
        0: [(core_step, 2, 3)],
        1: [(near_step, 2, 1)],
        2: [(far_step, 2, 0), (near_step, 2, 2)],
        3: [(far_step, 2, 1), (near_step, 2, 3)],
        4: [(far_step, 2, 2)],
        5: [(far_step, 2, 3), (core_step, 1, 0)],
        7: [(core_step, 1, 1)],
    }

    def middle_row(down, carry):
        for over in range(3):
            left = row_windows(taps_one, down, low_start[over], reaches[over])
            right = row_windows(taps_two, 1, high_start[over], reaches[over])
            rows = pl.ds(pl.multiple_of((3 * down + over) * width, width), width)
            mid_wide[rows, :] = dot_tn(left, right).astype(low_type)
            for row in range(3):
                tap = 3 * row + over

                @pl.when(down == row)
                def _():
                    if tap >= 2 and tap % 2 == 0:
                        fold_begin(tap // 2 - 1, 1)
                    for step in plan.get(tap, ()):
                        fold_step(*step)

        return carry

    lax.fori_loop(0, 3, middle_row, 0)
    for copy in head_moves:
        copy.wait_recv()
    head_grad = dot_nn(logit_grads[0], pool_all[0]) + dot_nn(logit_grads[1], pool_all[1])
    for spot in range(half // LANES):
        stage[pl.ds(spot, classes, stride=half // LANES), :] = head_grad[
            0:classes, spot * LANES : (spot + 1) * LANES
        ]
    head_space = stage.at[pl.ds(0, grad_head_out.shape[0]), :]
    head_leave = pltpu.make_async_copy(head_space, grad_head_out, sem_local.at[0])
    head_leave.start()
    if gather:
        tile_sum.pair(0)
        for load in base_loads:
            load.wait()

    def back_one(index, carry):
        down, side = index // 2, index % 2
        columns = lanes(2 + side, piece)
        for over in range(3):
            left = row_windows(taps_two, 2 - down, high_start[over], reaches[over])
            start = pl.multiple_of((3 * down + over) * width + side * piece, piece)
            value = dot_nt(left, w_middle[pl.ds(start, piece), :])
            add_windows(act_three, columns, value, low_start[over], reaches[over])
        fold_at(index, 0, (core_step, 1, 2), (near_step, 1, 0))
        fold_at(index, 1, (core_step, 1, 3))
        fold_at(index, 2, (near_step, 1, 1), (far_step, 1, 0))
        fold_at(index, 4, (far_step, 1, 1))
        fold_at(index, 5, (near_step, 1, 2))
        return carry

    act_three[:, space_one] = jnp.zeros((count_rows, width), wide)
    lax.fori_loop(0, 6, back_one, 0)
    drop_into(act_one, 0, gain_one, bias_one, space_one)
    fold_step(near_step, 1, 3)
    settle_section(2)
    close_back(5)
    move_back_one = swap(5, width)
    move_back_one.start()

    move_back_one.wait()
    terms_one = back_terms(5, 0, width, gain_one)

    def grad_one(index, carry):
        hidden_two[tile(index), :] = back_act(terms_one, act_one, 0, index, space_one)
        return carry

    lax.fori_loop(0, SIDE, grad_one, 0)
    fold_step(far_step, 1, 2)
    if gather:
        tile_sum.pair(1)

    def reduce_group(which, carry):
        put(w_first, which, dot_tn(x_all[:, lanes(which, group)], hidden_two[...]))
        fold_begin(which, 0)
        fold_at(which, 0, (far_step, 1, 3))
        fold_at(which, 2, (core_step, 0, 0))
        fold_at(which, 3, (core_step, 0, 1), (near_step, 0, 0))
        return carry

    lax.fori_loop(0, groups, reduce_group, 0)

    for kind in range(2):
        row = 3 - kind
        pieces = [
            sums_mine[5, row : row + 1, lanes(core, part)],
            sums_mine[4, row : row + 1, lanes(core, part)],
            sums_mine[3, row : row + 1, lanes(core, half)],
        ]
        whole = jnp.concatenate(pieces, axis=1)
        per_kind = whole.shape[1] // LANES
        for spot in range(per_kind):
            grad_norm_out[kind * per_kind + spot : kind * per_kind + spot + 1, :] = whole[
                :, spot * LANES : (spot + 1) * LANES
            ]
    if gather:
        part = width // CUTS
        gram = act_three.at[pl.ds(0, gram_total.shape[0]), pl.ds(half + width, 2 * part)]
        corner_rows = pl.ds(gram_total.shape[0], width)
        squares = [act_three.at[corner_rows, pl.ds(spot * width, width)] for spot in (0, 1, 3)]
        gram_sum = GramSum(place, gram, gram_total, (y_box, z_box), gram_sems)

        def form(slot):
            form_gram(place, slot, share, share_sems, gram, mate_gram, rows_in)
            gram_sum.start()

    def for_duty(slot, *calls):
        if gather:

            @pl.when(share.duty == slot)
            def _():
                for call in calls:
                    call()

    for_duty(2, lambda: form(2))
    fold_step(core_step, 0, 2)
    fold_step(core_step, 0, 3)
    fold_step(far_step, 0, 0)
    settle_section(1)
    fold_step(near_step, 0, 1)
    for_duty(2, lambda: gram_sum.pass_down())
    fold_step(near_step, 0, 2)
    fold_step(far_step, 0, 1)
    fold_step(near_step, 0, 3)
    for_duty(2, lambda: gram_sum.turn_up())
    for_duty(1, lambda: form(1))
    fold_step(far_step, 0, 2)
    fold_step(far_step, 0, 3)
    for_duty(2, lambda: gram_sum.pass_up())
    for_duty(1, lambda: gram_sum.pass_down())
    if gather:
        settle_section(0)
        leave = pltpu.make_async_copy(fresh, fresh_out, sem_local.at[1])
        leave.start()
        tile_sum.pair(2)
        for_duty(0, lambda: form(0), gram_sum.pass_down, gram_sum.turn_up, gram_sum.pass_up, gram_sum.close)
        for_duty(1, gram_sum.turn_up, gram_sum.pass_up, gram_sum.close)
        for_duty(2, gram_sum.close)
        orthogonal(ratios, share, gram_total, squares, rows_in, hidden_two)
        share.finish()
        loss_out[...] = tile_sum.result()
        ortho_leave = pltpu.make_async_copy(back, ortho_out, sem_local.at[2])
        ortho_leave.start()
        gram_sum.drain()
        tile_sum.drain()
        fold.drain()
        leave.wait()
        ortho_leave.wait()
    else:
        outs = [
            pltpu.make_async_copy(ref, out, sem_local.at[slot])
            for slot, (ref, out) in enumerate(zip((w_first, mid_wide.at[pl.ds(0, 9 * width), :], w_last), grads_out))
        ]
        for copy in outs:
            copy.start()
        for copy in outs:
            copy.wait()
    head_leave.wait()
    for copy in to_mate + head_moves:
        copy.wait_send()


def client_pass(gather, ratios, classes, features, labels, flag, params, head, weights):
    pixels, half = features.shape
    images = labels.shape[1]
    count_rows, channels = pixels // 2, 2 * half
    width = params.shape[0] // 2 * LANES - half
    head_rows = classes + -classes % 16
    mine_images = images // 2
    line = SIDE * mine_images
    middle = 9 * width
    blocks = 32
    group = channels // SPOTS[0]
    vmem = pl.BlockSpec(memory_space=pltpu.VMEM)
    smem = pl.BlockSpec(memory_space=pltpu.SMEM)
    spots = SPOTS + (2,)
    scratch = [
        pltpu.VMEM((count_rows, channels), low_type),
        pltpu.VMEM((SPOTS[0] * count_rows, group), low_type),
        pltpu.VMEM(spots + (channels // blocks, width), low_type),
        pltpu.VMEM((middle, width), low_type),
        pltpu.VMEM(spots + (channels // blocks, width), low_type),
        pltpu.VMEM((count_rows, width), wide),
        pltpu.VMEM((count_rows, width), wide),
        pltpu.VMEM((count_rows, channels), wide),
        pltpu.VMEM((count_rows + 2 * line, width), low_type),
        pltpu.VMEM((count_rows + 2 * line, width), low_type),
        pltpu.VMEM((count_rows, width), low_type),
        pltpu.VMEM((count_rows, LANES), wide),
        pltpu.VMEM((2, 2, half + width), wide),
        pltpu.VMEM((2, head_rows, half), low_type),
        pltpu.VMEM((mine_images, channels), wide),
        pltpu.VMEM((mine_images, half), low_type),
        pltpu.VMEM((2, mine_images, half), low_type),
        pltpu.VMEM((2, head_rows, mine_images), low_type),
        pltpu.VMEM((6, 8, channels), wide),
        pltpu.VMEM((6, 8, channels), wide),
        pltpu.VMEM((24, channels), wide),
        pltpu.VMEM((3, 8, channels), wide),
        pltpu.SemaphoreType.DMA((11,)),
        pltpu.SemaphoreType.DMA((2, 6)),
        pltpu.SemaphoreType.DMA((2, 7)),
    ]
    any_space = pl.BlockSpec(memory_space=pl.ANY)
    if gather:
        counts = (channels // blocks, middle // blocks, channels // blocks)
        scratch += [pltpu.SemaphoreType.DMA((2, 3, 3))]
        scratch += [pltpu.SemaphoreType.DMA((2, 4, size)) for size in (6, 8, 6)]
        scratch += [pltpu.VMEM((4, 2, 2, rows, width), low_type) for rows in counts[1:]]
        for lead in ((4, 2), (4,), (4,)):
            scratch += [pltpu.VMEM(lead + (rows, width), low_type) for rows in counts]
        scratch += [pltpu.SemaphoreType.DMA((2, 4, size)) for size in (6, 8, 6, 6)]
        part = width // CUTS
        gram_rows = CUTS * (CUTS + 1) // 4 * part
        many = max(4 * counts[0], 2 * counts[1])
        scratch += [
            pltpu.VMEM((many, width), wide),
            pltpu.VMEM((sum(counts), width), low_type),
            pltpu.VMEM((4, 8, LANES), wide),
            pltpu.VMEM((6, 8, LANES), wide),
            pltpu.VMEM((gram_rows, 2 * part), wide),
            pltpu.VMEM((4, gram_rows // 8, 2 * part), wide),
            pltpu.VMEM((3, gram_rows // 8, 2 * part), wide),
            pltpu.VMEM((gram_rows, 2 * part), wide),
            pltpu.SemaphoreType.DMA((2, 6)),
            pltpu.SemaphoreType.DMA((2, 8)),
            pltpu.SemaphoreType.DMA((2, 14)),
        ]
        grads_shape = [
            jax.ShapeDtypeStruct((sum(counts), width), wide),
            jax.ShapeDtypeStruct((sum(counts), width), low_type),
        ]
        grads_specs = [any_space] * 2
    else:
        grads_shape = [jax.ShapeDtypeStruct(weight.shape, low_type) for weight in weights]
        grads_specs = [any_space] * 3
    return pl.pallas_call(
        functools.partial(client_kernel, gather, ratios, images, classes),
        out_shape=grads_shape
        + [
            jax.ShapeDtypeStruct(params.shape, wide),
            jax.ShapeDtypeStruct((classes * half // LANES, LANES), wide),
            jax.ShapeDtypeStruct((8, LANES), wide),
        ],
        in_specs=[any_space, vmem, smem, vmem, vmem] + [any_space] * len(weights),
        out_specs=grads_specs + [vmem, any_space, vmem],
        scratch_shapes=scratch,
        compiler_params=pltpu.CompilerParams(
            collective_id=0, has_side_effects=True, vmem_limit_bytes=VMEM_BYTES
        ),
    )(features, labels, flag, params, head, *weights)


def adam_update(param, grad, first, second, rate, decay):
    first = adam_first * first + (1.0 - adam_first) * grad
    second = adam_second * second + (1.0 - adam_second) * grad * grad
    first_hat = first / (1.0 - adam_first**STEP)
    second_hat = second / (1.0 - adam_second**STEP)
    return (
        param - rate * (first_hat / (jnp.sqrt(second_hat) + adam_epsilon) + decay * param),
        first,
        second,
    )


def gram_of(section):
    return lax.dot_general(section, section, (((0,), (0,)), ((), ())), precision=precise)


def square(gram):
    return jnp.dot(gram, gram, precision=precise)


def times_poly(left, mixed):
    return schulz_first * left + jnp.dot(left, mixed, precision=precise)


def schulz(sections):
    raw_grams = lax.psum(tuple(gram_of(section) for section in sections), ("client", "chan"))
    factors = [1.0 / (jnp.sqrt(jnp.trace(gram)) + 1e-07) for gram in raw_grams]
    current = [section * factor for section, factor in zip(sections, factors)]
    grams = [gram * (factor * factor) for gram, factor in zip(raw_grams, factors)]
    for turn in range(NS_STEPS):
        mixed = [schulz_second * gram + schulz_third * square(gram) for gram in grams]
        current = [times_poly(current[slot], mixed[slot]) for slot in range(3)]
        if turn + 1 < NS_STEPS:
            grams = [
                times_poly(times_poly(grams[slot], mixed[slot]), mixed[slot]) for slot in range(3)
            ]
    return current


def base_far(ratios, bounds, master, momentum, anchor, loss_tile, grads):
    sums = [
        lax.psum_scatter(flat_rows(grad).astype(wide), ("client", "chan"), scatter_dimension=0, tiled=True)
        for grad in grads
    ]
    grad_base = jnp.concatenate(sums, axis=0)
    momentum_new = momentum_decay * momentum + (grad_base + prox_weight * (master - anchor))
    current = schulz([momentum_new[bounds[slot] : bounds[slot + 1]] for slot in range(3)])
    ortho = jnp.concatenate([current[slot] * ratios[slot] for slot in range(3)], axis=0)
    return momentum_new, ortho, lax.psum(loss_tile, ("client", "chan"))


def as_stored(rows, shape):
    return with_layout_constraint(rows.reshape(shape), Layout(major_to_minor=tuple(range(len(shape)))))


def on_device(
    features,
    labels,
    mask,
    base_master,
    base_momentum,
    global_base,
    norm_params,
    norm_first,
    norm_second,
    head,
    head_first,
    head_second,
):
    halves = lax.axis_size("chan")
    blocks = lax.axis_size("client") * halves
    half = features.shape[2]
    width = base_master.shape[2]
    channels = half * halves
    classes = head.shape[2]
    rows_first = channels // blocks
    rows_mid = 9 * width // blocks
    bounds = (0, rows_first, rows_first + rows_mid, base_master.shape[1])
    ratio = (channels / width) ** 0.5
    ratios = (ratio, 3.0, ratio)
    master, momentum, anchor = base_master[0], base_momentum[0], global_base[0]
    norms = [value.reshape(-1, LANES) for value in (norm_params, norm_first, norm_second)]
    heads = [jnp.transpose(value, (2, 0, 1)).reshape(-1, LANES) for value in (head, head_first, head_second)]
    near = lax.axis_size("client") == SPOTS[0] * SPOTS[1] * SPOTS[2]
    if near:
        weights = [master, momentum, anchor]
    else:
        low_master = master.astype(low_type)
        weights = [
            lax.all_gather(low_master[bounds[slot] : bounds[slot + 1]], ("client", "chan"), axis=0, tiled=True)
            for slot in range(3)
        ]
        split = SPOTS + (2, channels // 32, width)
        weights = [weights[0].reshape(split), weights[1], weights[2].reshape(split)]
    *grads, grad_norm, grad_head, loss_tile = client_pass(
        near, ratios, classes, features[0], labels, mask, norms[0], heads[0], weights
    )
    if near:
        fresh_momentum, ortho = grads
    else:
        fresh_momentum, ortho, loss_tile = base_far(ratios, bounds, master, momentum, anchor, loss_tile, grads)
    loss, momentum_new, base_new, base_low, *fresh = update_pass(
        loss_tile, master, fresh_momentum, ortho, norms, grad_norm, heads, grad_head
    )
    fresh_norms = [as_stored(value, norm_params.shape) for value in fresh[:3]]
    fresh_heads = [jnp.transpose(as_stored(value, (classes, 1, half)), (1, 2, 0)) for value in fresh[3:]]
    return (
        loss,
        base_new[None],
        momentum_new[None],
        base_low[None],
        *fresh_norms,
        *fresh_heads,
    )


def solution(mesh):
    wide_block = P(("client", "chan"), None, None)
    norm_block = P("client", None, "chan", None)
    head_block = P("client", "chan", None)
    return jax.shard_map(
        on_device,
        mesh=mesh,
        in_specs=(P("client", None, "chan"), P("client", None), P("client"))
        + (wide_block,) * 3
        + (norm_block,) * 3
        + (head_block,) * 3,
        out_specs=(P(),) + (wide_block,) * 3 + (norm_block,) * 3 + (head_block,) * 3,
        check_vma=False,
    )
```

```python
import functools

import jax
import jax.numpy as jnp
from jax import lax
from jax.experimental import pallas as pl
from jax.experimental.layout import Layout, with_layout_constraint
from jax.experimental.pallas import tpu as pltpu
from jax.sharding import PartitionSpec as P

NS_STEPS = 5
STEP = 10

low_type = jnp.bfloat16
wide = jnp.float32
MESH = pl.DeviceIdType.MESH
precise = lax.Precision.HIGHEST
norm_epsilon = 1e-05
prox_weight = 0.05
momentum_decay = 0.95
muon_rate = 0.3
muon_decay = 0.1
schulz_first = 3.4445
schulz_second = -4.775
schulz_third = 2.0315
adam_first = 0.9
adam_second = 0.95
adam_epsilon = 1e-08
head_rate = 0.01
head_decay = 0.05
norm_rate = 0.5

SIDE = 7
PIXELS = SIDE * SIDE
LANES = 128
SPOTS = (4, 2, 2)
CUTS = 4
VMEM_BYTES = 62 * 2**20


def dot_nn(left, right):
    return jnp.dot(left, right, preferred_element_type=wide)


def dot_nt(left, right):
    return lax.dot_general(left, right, (((1,), (1,)), ((), ())), preferred_element_type=wide)


def dot_tn(left, right):
    return lax.dot_general(left, right, (((0,), (0,)), ((), ())), preferred_element_type=wide)


def flat_rows(block):
    return block.reshape(-1, block.shape[-1])


def sigmoid(value):
    return 0.5 * jnp.tanh(0.5 * value) + 0.5


def fold_rows(value):
    return jnp.sum(value.reshape(value.shape[0] // 8, 8, value.shape[1]), axis=0)


def column_sum(value):
    return jnp.sum(value, axis=0, keepdims=True)


def remote(src, dst, send_sem, recv_sem, client, core):
    return pltpu.make_async_remote_copy(
        src_ref=src,
        dst_ref=dst,
        send_sem=send_sem,
        recv_sem=recv_sem,
        device_id=(client, core),
        device_id_type=MESH,
    )


class Place:
    def __init__(self):
        self.client = lax.axis_index("client")
        self.core = lax.axis_index("chan")
        self.z = self.client // 4
        self.y = (self.client // 2) % 2
        self.x = self.client % 2
        self.others = [
            self.z + 1 - 2 * (self.z % 2),
            (self.z + 2) % 4,
            3 - self.z,
        ]

    def at(self, z, y, x):
        return z * 4 + y * 2 + x

    def along_x(self):
        return self.at(self.z, self.y, 1 - self.x)

    def along_y(self):
        return self.at(self.z, 1 - self.y, self.x)

    def along_z(self, step):
        return self.at(self.others[step], self.y, self.x)

    def greet(self, whole, across=False):
        barrier = pltpu.get_barrier_semaphore()
        pairs = [(self.client, 1 - self.core)]
        if whole:
            pairs += [(self.along_x(), self.core), (self.along_y(), self.core)]
            pairs += [(self.along_z(step), self.core) for step in range(3)]
        if across:
            pairs += [(self.along_x(), 1 - self.core)]
        for pair in pairs:
            pl.semaphore_signal(barrier, inc=1, device_id=pair, device_id_type=MESH)
        pl.semaphore_wait(barrier, len(pairs))


def cut_rows(counts):
    pieces = []
    for slot, rows in enumerate(counts):
        middle = (rows // 16 + 1) // 2 * 16
        pieces.append((slot, 0, middle, 0))
        pieces.append((slot, middle, rows - middle, 1))
    return pieces


def block_ref(ref, size, z, y, x, core, start, count):
    if len(ref.shape) == 2:
        first = (((z * 2 + y) * 2 + x) * 2 + core) * size + start
        return ref.at[pl.ds(pl.multiple_of(first, 16), count), :]
    return ref.at[z, y, x, core, pl.ds(start, count), :]


class Spread:
    def __init__(self, place, weights, counts, sems):
        self.place = place
        self.weights = weights
        self.counts = counts
        self.pieces = cut_rows(counts)
        self.z_sems, self.near_sems, self.far_sems, self.core_sems = sems
        self.order = [place.z] + place.others

    def z_copy(self, step, slot):
        p = self.place
        ref = block_ref(self.weights[slot], self.counts[slot], p.z, p.y, p.x, p.core, 0, self.counts[slot])
        sems = self.z_sems
        return remote(ref, ref, sems.at[0, step, slot], sems.at[1, step, slot], p.along_z(step), p.core)

    def near_copy(self, turn, number):
        p = self.place
        slot, start, count, way = self.pieces[number]
        ref = block_ref(self.weights[slot], self.counts[slot], self.order[turn], p.y, p.x, p.core, start, count)
        sems = self.near_sems
        return remote(
            ref, ref, sems.at[0, turn, number], sems.at[1, turn, number], (p.along_x, p.along_y)[way](), p.core
        )

    def far_copies(self, turn, number):
        p = self.place
        slot, start, count, way = self.pieces[number]
        spot = self.order[turn]
        sems = self.far_sems
        copies = []
        for part, other in enumerate((0, 1) if slot == 1 else (slice(None),)):
            y, x = (p.y, other) if way == 0 else (other, p.x)
            ref = block_ref(self.weights[slot], self.counts[slot], spot, y, x, p.core, start, count)
            sem = number + 4 * part
            to = (p.along_y, p.along_x)[way]()
            copies.append(remote(ref, ref, sems.at[0, turn, sem], sems.at[1, turn, sem], to, p.core))
        return copies

    def core_copies(self, turn, slot):
        p = self.place
        sems = self.core_sems
        copies = []
        pairs = [(y, x) for y in (0, 1) for x in (0, 1)] if slot == 1 else [(slice(None), slice(None))]
        for part, (y, x) in enumerate(pairs):
            ref = block_ref(self.weights[slot], self.counts[slot], self.order[turn], y, x, p.core, 0, self.counts[slot])
            sem = (0, 2 + part, 1)[slot]
            copies.append(remote(ref, ref, sems.at[0, turn, sem], sems.at[1, turn, sem], p.client, 1 - p.core))
        return copies

    def fill(self, master):
        p = self.place
        start = 0
        for slot in range(3):
            rows = self.counts[slot]
            own = block_ref(self.weights[slot], self.counts[slot], p.z, p.y, p.x, p.core, 0, rows)
            own[...] = master[start : start + rows, :].astype(low_type)
            start += rows

    def begin(self):
        for step in range(3):
            self.z_copy(step, 0).start()
        self.near_start(0)

    def near_start(self, slot):
        for number in (2 * slot, 2 * slot + 1):
            self.near_copy(0, number).start()

    def steps(self):
        near, far, core, start = self.near_step, self.far_step, self.core_step, self.near_start
        groups = [
            [(far, 0, 0), (start, 1)],
            [(near, 1, 0)],
            [(near, 2, 0), (near, 3, 0)],
            [(far, 1, 0), (core, 0, 0), (far, 0, 1)],
            [(far, 2, 0), (far, 3, 0), (core, 1, 0)],
            [(core, 2, 0), (core, 3, 0), (near, 1, 1), (start, 2)],
            [(core, 0, 1), (near, 2, 1)],
            [(far, 1, 1), (near, 3, 1)],
            [(core, 1, 1), (far, 2, 1), (far, 0, 2)],
            [(far, 3, 1), (core, 2, 1), (near, 1, 2)],
            [(core, 3, 1), (core, 0, 2), (near, 2, 2)],
            [(far, 1, 2), (near, 3, 2)],
            [(core, 1, 2), (far, 2, 2)],
            [(far, 3, 2), (core, 2, 2)],
            [(core, 3, 2)],
        ]
        return [[functools.partial(*step) for step in group] for group in groups]

    def near_step(self, turn, slot):
        self.z_copy(turn - 1, slot).wait_recv()
        for number in (2 * slot, 2 * slot + 1):
            self.near_copy(turn, number).start()
        if slot < 2:
            self.z_copy(turn - 1, slot + 1).start()

    def far_step(self, turn, slot):
        for number in (2 * slot, 2 * slot + 1):
            self.near_copy(turn, number).wait_recv()
            for copy in self.far_copies(turn, number):
                copy.start()

    def core_step(self, turn, slot):
        for number in (2 * slot, 2 * slot + 1):
            for copy in self.far_copies(turn, number):
                copy.wait_recv()
        for copy in self.core_copies(turn, slot):
            copy.start()

    def arrive(self, slot):
        for turn in range(4):
            for copy in self.core_copies(turn, slot):
                copy.wait_recv()

    def drain(self, slot):
        for step in range(3):
            self.z_copy(step, slot).wait_send()
        for turn in range(4):
            for copy in self.core_copies(turn, slot):
                copy.wait_send()
            for number in (2 * slot, 2 * slot + 1):
                self.near_copy(turn, number).wait_send()
                for copy in self.far_copies(turn, number):
                    copy.wait_send()


class Fold:
    def __init__(self, place, grads, counts, parts):
        self.place = place
        self.grads = grads
        self.counts = counts
        self.pieces = cut_rows(counts)
        self.core_boxes = [parts[1], parts[0], parts[1]]
        self.near_boxes, self.far_boxes, self.z_boxes = [parts[3 * k + 2 : 3 * k + 5] for k in range(3)]
        self.core_sems, self.near_sems, self.far_sems, self.z_sems = parts[11:]

    def core_copies(self, which, slot):
        p = self.place
        sems = self.core_sems
        copies = []
        pairs = [(y, x) for y in (0, 1) for x in (0, 1)] if slot == 1 else [(slice(None), slice(None))]
        for part, (y, x) in enumerate(pairs):
            ref = block_ref(self.grads[slot], self.counts[slot], which, y, x, 1 - p.core, 0, self.counts[slot])
            box = self.core_boxes[slot].at[which, y, x]
            sem = (0, 2 + part, 1)[slot]
            copies.append(remote(ref, box, sems.at[0, which, sem], sems.at[1, which, sem], p.client, 1 - p.core))
        return copies

    def near_copies(self, which, number):
        p = self.place
        slot, start, count, way = self.pieces[number]
        sems = self.near_sems
        copies = []
        for part, other in enumerate((0, 1) if slot == 1 else (slice(None),)):
            y, x = (other, 1 - p.x) if way == 0 else (1 - p.y, other)
            ref = block_ref(self.grads[slot], self.counts[slot], which, y, x, p.core, start, count)
            box = self.near_boxes[slot].at[which, other, pl.ds(start, count), :]
            sem = number + 4 * part
            to = (p.along_x, p.along_y)[way]()
            copies.append(remote(ref, box, sems.at[0, which, sem], sems.at[1, which, sem], to, p.core))
        return copies

    def far_copy(self, which, number):
        p = self.place
        slot, start, count, way = self.pieces[number]
        y, x = (1 - p.y, p.x) if way == 0 else (p.y, 1 - p.x)
        ref = block_ref(self.grads[slot], self.counts[slot], which, y, x, p.core, start, count)
        box = self.far_boxes[slot].at[which, pl.ds(start, count), :]
        sems = self.far_sems
        return remote(
            ref, box, sems.at[0, which, number], sems.at[1, which, number], (p.along_y, p.along_x)[way](), p.core
        )

    def z_copy(self, which, sender, number):
        p = self.place
        slot, start, count, _ = self.pieces[number]
        rows = pl.ds(start, count)
        sems = self.z_sems
        return remote(
            block_ref(self.grads[slot], self.counts[slot], which, p.y, p.x, p.core, start, count),
            self.z_boxes[slot].at[sender, rows, :],
            sems.at[0, which, number],
            sems.at[1, sender, number],
            p.at(which, p.y, p.x),
            p.core,
        )

    def begin(self, which, slot):
        for copy in self.core_copies(which, slot):
            copy.start()

    def add(self, slot, spots, start, count, box):
        ref = block_ref(self.grads[slot], self.counts[slot], *spots, self.place.core, start, count)
        ref[...] = (ref[...].astype(wide) + box.astype(wide)).astype(low_type)

    def core_step(self, which, slot):
        for copy in self.core_copies(which, slot):
            copy.wait_recv()
        pairs = [(y, x) for y in (0, 1) for x in (0, 1)] if slot == 1 else [(slice(None), slice(None))]
        for y, x in pairs:
            self.add(slot, (which, y, x), 0, self.counts[slot], self.core_boxes[slot][which, y, x])
        for number in (2 * slot, 2 * slot + 1):
            for copy in self.near_copies(which, number):
                copy.start()

    def near_step(self, which, slot):
        p = self.place
        for number in (2 * slot, 2 * slot + 1):
            _, start, count, way = self.pieces[number]
            for copy in self.near_copies(which, number):
                copy.wait_recv()
            for other in (0, 1) if slot == 1 else (slice(None),):
                y, x = (other, p.x) if way == 0 else (p.y, other)
                box = self.near_boxes[slot][which, other, pl.ds(start, count), :]
                self.add(slot, (which, y, x), start, count, box)
            self.far_copy(which, number).start()

    def far_step(self, which, slot):
        p = self.place
        for number in (2 * slot, 2 * slot + 1):
            _, start, count, way = self.pieces[number]
            self.far_copy(which, number).wait_recv()
            box = self.far_boxes[slot][which, pl.ds(start, count), :]
            self.add(slot, (which, p.y, p.x), start, count, box)

            @pl.when(p.z != which)
            def _():
                self.z_copy(which, p.z, number).start()

    def result(self, slot):
        p = self.place
        self.z_boxes[slot][p.z] = block_ref(self.grads[slot], self.counts[slot], p.z, p.y, p.x, p.core, 0, self.counts[slot])[...]
        for sender in range(4):

            @pl.when(p.z != sender)
            def _():
                for number in (2 * slot, 2 * slot + 1):
                    self.z_copy(sender, sender, number).wait_recv()

        total = self.z_boxes[slot][0].astype(wide)
        for sender in range(1, 4):
            total += self.z_boxes[slot][sender].astype(wide)
        return total

    def drain(self):
        for which in range(4):
            for slot in range(3):
                for copy in self.core_copies(which, slot):
                    copy.wait_send()
            for number in range(6):
                for copy in self.near_copies(which, number):
                    copy.wait_send()
                self.far_copy(which, number).wait_send()

            @pl.when(self.place.z != which)
            def _():
                for number in range(6):
                    self.z_copy(which, self.place.z, number).wait_send()
class GramSum:
    def __init__(self, place, data, total, boxes, sems):
        self.place = place
        self.data = data
        self.total = total
        self.y_box, self.z_box = boxes
        self.sems = sems
        self.share = data.shape[0] // 8
        self.down_order = place.others[::-1] + [place.z]

    def rows(self, z, y):
        return pl.ds(pl.multiple_of((z * 2 + y) * self.share, 8), self.share)

    def copy(self, number, src, dst, to):
        sems = self.sems
        return remote(src, dst, sems.at[0, number], sems.at[1, number], to, self.place.core)

    def y_down(self, turn):
        p = self.place
        src = self.data.at[self.rows(self.down_order[turn], 1 - p.y), :]
        return self.copy(turn, src, self.y_box.at[turn], p.along_y())

    def z_down(self, step):
        p = self.place
        src = self.data.at[self.rows(p.others[step], p.y), :]
        return self.copy(4 + step, src, self.z_box.at[step], p.along_z(step))

    def z_up(self, step):
        p = self.place
        ref = self.total.at[self.rows(p.z, p.y), :]
        return self.copy(7 + step, ref, ref, p.along_z(step))

    def y_up(self, turn):
        p = self.place
        ref = self.total.at[self.rows(([p.z] + p.others)[turn], p.y), :]
        return self.copy(10 + turn, ref, ref, p.along_y())

    def run(self):
        p = self.place
        for turn in range(4):
            self.y_down(turn).start()
        for turn in range(4):
            self.y_down(turn).wait_recv()
            self.data[self.rows(self.down_order[turn], p.y), :] += self.y_box[turn]
            if turn < 3:
                self.z_down(2 - turn).start()
        mine = self.rows(p.z, p.y)
        value = self.data[mine, :]
        for step in (2, 1, 0):
            self.z_down(step).wait_recv()
            value += self.z_box[step]
        self.total[mine, :] = value
        for step in range(3):
            self.z_up(step).start()
        self.y_up(0).start()
        for step in range(3):
            self.z_up(step).wait_recv()
            self.y_up(1 + step).start()
        for turn in range(4):
            self.y_up(turn).wait_recv()

    def drain(self):
        for turn in range(4):
            self.y_down(turn).wait_send()
            self.y_up(turn).wait_send()
        for step in range(3):
            self.z_down(step).wait_send()
            self.z_up(step).wait_send()


class TileSum:
    def __init__(self, place, tiles, boxes, sems):
        self.place = place
        self.tiles = tiles
        self.boxes = boxes
        self.sems = sems

    def copy(self, stage, box):
        p = self.place
        to = (p.client, p.along_x(), p.along_y()) + tuple(p.along_z(step) for step in range(3))
        core = 1 - p.core if box == 0 else p.core
        return remote(
            self.tiles.at[stage], self.boxes.at[box], self.sems.at[0, box], self.sems.at[1, box], to[box], core
        )

    def start(self):
        self.copy(0, 0).start()

    def pair(self, stage):
        self.copy(stage, stage).wait_recv()
        self.tiles[stage + 1] = self.tiles[stage] + self.boxes[stage]
        if stage < 2:
            self.copy(stage + 1, stage + 1).start()
        else:
            for step in range(3):
                self.copy(3, 3 + step).start()

    def result(self):
        for step in range(3):
            self.copy(3, 3 + step).wait_recv()
        return (self.tiles[3] + self.boxes[3]) + (self.boxes[4] + self.boxes[5])

    def drain(self):
        for stage in range(3):
            self.copy(stage, stage).wait_send()
        for step in range(3):
            self.copy(3, 3 + step).wait_send()


def halves_of(value):
    high = value.astype(low_type)
    return high, (value - high.astype(wide)).astype(low_type)


class Share:
    def __init__(self, place, sizes, buffers, sems):
        self.place = place
        self.sizes = sizes
        self.fresh, self.rows_in, self.rows_out, self.back = buffers
        self.sems = sems
        self.bounds = [0, sizes[0], sizes[0] + sizes[1], sum(sizes)]
        p = place
        self.duty = jnp.where(p.x == 1, 1, 2 * p.core)
        self.mine = p.x * 2 + p.core

    def section(self, slot):
        return pl.ds(self.bounds[slot], self.sizes[slot])

    def spot(self, slot, x, core):
        number = x if slot == 1 else x * 2 + core
        return pl.ds(pl.multiple_of(number * self.sizes[slot], 16), self.sizes[slot])

    def doer(self, slot):
        return (0, 0) if slot == 0 else (0, 1) if slot == 2 else (1, self.place.core)

    def out_copy(self, slot):
        p = self.place
        x, core = self.doer(slot)
        return remote(
            self.fresh.at[self.section(slot), :],
            self.rows_in.at[self.spot(slot, p.x, p.core), :],
            self.sems.at[0, slot],
            self.sems.at[1, self.mine],
            p.at(p.z, p.y, x),
            core,
        )

    def in_copy(self, slot, x, core):
        p = self.place
        return remote(
            self.fresh.at[self.section(slot), :],
            self.rows_in.at[self.spot(slot, x, core), :],
            self.sems.at[0, slot],
            self.sems.at[1, x * 2 + core],
            p.at(p.z, p.y, x),
            core,
        )

    def back_copy(self, slot, x, core):
        p = self.place
        return remote(
            self.rows_out.at[self.spot(slot, x, core), :],
            self.back.at[self.section(slot), :],
            self.sems.at[0, 3 + x * 2 + core],
            self.sems.at[1, 4 + slot],
            p.at(p.z, p.y, x),
            core,
        )

    def users(self, slot):
        p = self.place
        if slot == 1:
            return [(0, p.core), (1, p.core)]
        return [(x, core) for x in (0, 1) for core in (0, 1)]

    def send(self, slot):
        @pl.when(self.duty != slot)
        def _():
            self.out_copy(slot).start()

        @pl.when(self.duty == slot)
        def _():
            self.rows_in[self.spot(slot, self.place.x, self.place.core), :] = self.fresh[self.section(slot), :]

    def gather(self):
        p = self.place
        for slot in range(3):

            @pl.when(self.duty == slot)
            def _():
                for x, core in self.users(slot):

                    @pl.when((p.x != x) | (p.core != core))
                    def _():
                        self.in_copy(slot, x, core).wait_recv()

    def give_back(self):
        p = self.place
        for slot in range(3):

            @pl.when(self.duty == slot)
            def _():
                for x, core in self.users(slot):

                    @pl.when((p.x != x) | (p.core != core))
                    def _():
                        self.back_copy(slot, x, core).start()

                self.back[self.section(slot), :] = self.rows_out[self.spot(slot, p.x, p.core), :]

    def finish(self):
        p = self.place
        for slot in range(3):

            @pl.when(self.duty != slot)
            def _():
                self.back_copy(slot, p.x, p.core).wait_recv()
                self.out_copy(slot).wait_send()

            @pl.when(self.duty == slot)
            def _():
                for x, core in self.users(slot):

                    @pl.when((p.x != x) | (p.core != core))
                    def _():
                        self.back_copy(slot, x, core).wait_send()


def corner_spot(number, part):
    row, column = number // 2, number % 2
    return slice(row * part, (row + 1) * part), slice(column * part, (column + 1) * part)


def orthogonal(place, ratios, share, share_sems, gram, gram_total, mate_gram, gram_sum, squares, rows_in, low_rows):
    grams, mixed, once = squares
    count, width = rows_in.shape
    part = width // CUTS
    corners = [(row, column) for row in range(CUTS) for column in range(row, CUTS)]
    right_high, right_low = [low_rows.at[pl.ds(count + spot * width, width), :] for spot in range(2)]

    def set_right(value_ref):
        for start in range(0, width, part):
            rows = slice(start, start + part)
            right_high[rows, :], right_low[rows, :] = halves_of(value_ref[rows, :])

    def times_right(value):
        high, low = halves_of(value)
        left = jnp.concatenate([high, high, low], axis=1)
        right = jnp.concatenate([right_high[...], right_low[...], right_high[...]], axis=0)
        return dot_nn(left, right)

    middle = width // 2

    def times_right_even(value, more=()):
        high, low = halves_of(value)
        left = jnp.concatenate([high, high, low], axis=1)
        right = jnp.concatenate([right_high[...], right_low[...], right_high[...]], axis=0)
        upper = left[:middle]
        for rows in more:
            high, low = halves_of(rows)
            upper = jnp.concatenate([upper, jnp.concatenate([high, high, low], axis=1)], axis=0)
        upper = dot_nn(upper, right)
        corner = dot_nn(left[middle:], right[:, middle:])
        lower = jnp.concatenate([upper[:middle, middle:].T, corner], axis=1)
        return jnp.concatenate([upper[:middle], lower], axis=0), upper[middle:]

    share.gather()
    high, low = halves_of(rows_in[...])
    left = jnp.concatenate([high, high, low], axis=0)
    right = jnp.concatenate([high, low, high], axis=0)
    for row in range(CUTS):
        strip = dot_tn(left[:, row * part : (row + 1) * part], right[:, row * part :])
        for column in range(row, CUTS):
            gram[corner_spot(corners.index((row, column)), part)] = strip[
                :, (column - row) * part : (column - row + 1) * part
            ]

    @pl.when(place.x == 1)
    def _():
        swap = remote(gram, mate_gram, share_sems.at[0, 7], share_sems.at[1, 7], place.client, 1 - place.core)
        swap.start()
        swap.wait()
        gram[...] += mate_gram[...]

    gram_sum.run()
    spots = lax.broadcasted_iota(jnp.int32, (part, part), 0)
    diagonal = spots == lax.broadcasted_iota(jnp.int32, (part, part), 1)
    trace = 0.0
    for number, (row, column) in enumerate(corners):
        if row == column:
            trace += jnp.sum(jnp.where(diagonal, gram_total[corner_spot(number, part)], 0.0))
    factor = 1.0 / (jnp.sqrt(trace) + 1e-07)
    square = factor * factor
    for number, (row, column) in enumerate(corners):
        rows, columns = slice(row * part, (row + 1) * part), slice(column * part, (column + 1) * part)
        block = gram_total[corner_spot(number, part)] * square
        grams[rows, columns] = block
        if row < column:
            grams[columns, rows] = block.T
    rows_in[...] = rows_in[...] * factor

    def turn(number, carry):
        set_right(grams)
        mixed[...] = schulz_second * grams[...] + schulz_third * times_right_even(grams[...])[0]
        set_right(mixed)

        @pl.when(number < NS_STEPS - 1)
        def _():
            product, moved = times_right_even(grams[...], (rows_in[...],))
            once[...] = schulz_first * grams[...] + product
            rows_in[...] = schulz_first * rows_in[...] + moved
            grams[...] = schulz_first * once[...] + times_right_even(once[...])[0]

        @pl.when(number == NS_STEPS - 1)
        def _():
            rows_in[...] = schulz_first * rows_in[...] + times_right(rows_in[...])

        return carry

    lax.fori_loop(0, NS_STEPS, turn, 0)
    ratio = jnp.where(share.duty == 1, ratios[1], ratios[0])
    low_rows[0:count, :] = (rows_in[...] * ratio).astype(low_type)
    share.give_back()


def update_kernel(loss_tile, master, fresh_momentum, ortho, *rest):
    norms, grad_norm, heads, grad_head, outs = rest[0:3], rest[3], rest[4:7], rest[7], rest[8:]
    loss_out, *outs = outs
    loss_out[0] = loss_tile[0, 0]
    loss_out[1] = loss_tile[0, 1]
    momentum_out, base_out, low_out = outs[0:3]
    held = master[...]
    momentum_out[...] = fresh_momentum[...]
    fresh = held - muon_rate * (ortho[...].astype(wide) + muon_decay * held)
    base_out[...] = fresh
    low_out[...] = fresh.astype(low_type)
    for targets, values, grad, rate, decay in (
        (outs[3:6], norms, grad_norm, norm_rate, 0.0),
        (outs[6:9], heads, grad_head, head_rate, head_decay),
    ):
        updates = adam_update(values[0][...], grad[...], values[1][...], values[2][...], rate, decay)
        for target, value in zip(targets, updates):
            target[...] = value


def update_pass(loss_tile, master, fresh_momentum, ortho, norms, grad_norm, heads, grad_head):
    vmem = pl.BlockSpec(memory_space=pltpu.VMEM)
    smem = pl.BlockSpec(memory_space=pltpu.SMEM)
    operands = [loss_tile, master, fresh_momentum, ortho, *norms, grad_norm, *heads, grad_head]
    outs = [(2,), master.shape, master.shape, master.shape] + [grad_norm.shape] * 3 + [grad_head.shape] * 3
    types = [wide, wide, wide, low_type] + [wide] * 6
    return pl.pallas_call(
        update_kernel,
        out_shape=[jax.ShapeDtypeStruct(shape, kind) for shape, kind in zip(outs, types)],
        in_specs=[smem] + [vmem] * (len(operands) - 1),
        out_specs=[smem] + [vmem] * (len(outs) - 1),
        compiler_params=pltpu.CompilerParams(vmem_limit_bytes=VMEM_BYTES),
    )(*operands)


def norm_stats(mine, theirs, count):
    gap = mine[0:1] - theirs[0:1]
    mean = 0.5 * (mine[0:1] + theirs[0:1])
    spread = mine[1:2] + theirs[1:2] + gap * gap * (0.5 * count)
    return mean, lax.rsqrt(spread / (2.0 * count) + norm_epsilon)


def client_kernel(
    gather,
    ratios,
    images,
    classes,
    features,
    labels,
    flag,
    params,
    head,
    *rest,
):
    if gather:
        master, momentum, anchor, *rest = rest
    else:
        first_in, middle_in, last_in, *rest = rest
    if gather:
        fresh_out, ortho_out, *rest = rest
    else:
        grads_out, rest = rest[:3], rest[3:]
    (
        grad_norm_out,
        grad_head_out,
        loss_out,
        x_all,
        mid_wide,
        w_first,
        w_middle,
        w_last,
        act_one,
        act_two,
        act_three,
        taps_one,
        taps_two,
        hidden_two,
        stage,
        params_all,
        head_all,
        grad_pool,
        pool_send,
        pool_all,
        logit_grads,
        sums_mine,
        sums_theirs,
        shift,
        fwd_stats,
        sem_local,
        sem_swap,
        sem_misc,
        *near_parts,
    ) = rest
    place = Place()
    core = place.core
    mate = (place.client, 1 - core)
    count_rows, channels = x_all.shape
    half = channels // 2
    width = act_one.shape[1]
    part = width // 2
    mine_images = images // 2
    line = SIDE * mine_images
    total_rows = 2.0 * count_rows

    def tile(index):
        return pl.ds(pl.multiple_of(index * line, line), line)

    def lanes(index, size):
        return pl.ds(pl.multiple_of(index * size, size), size)

    weights = (w_first, w_middle, w_last)
    if gather:
        held = act_three.at[pl.ds(0, master.shape[0]), pl.ds(0, width)]
        load = pltpu.make_async_copy(master, held, sem_local.at[8])
        load.start()
        counts = [channels // 32, 9 * width // 32, channels // 32]
        spread = Spread(place, weights, counts, near_parts[:4])
        fold = Fold(place, (w_first, mid_wide, w_last), counts, near_parts[4:19])
        rows_in, back, tiles, tile_boxes, gram_total, y_box, z_box, mate_gram = near_parts[19:27]
        tile_sems, share_sems, gram_sems = near_parts[27:]
        block_rows = master.shape[0]
        side_space = pl.ds(half, width)
        held_base, held_momentum, held_anchor, fresh = [
            act_three.at[pl.ds(number * block_rows, block_rows), side_space] for number in range(4)
        ]
        rows_in[...] = jnp.zeros_like(rows_in)
        share = Share(place, counts, (fresh, rows_in, hidden_two, back), share_sems)
        tile_sum = TileSum(place, tiles, tile_boxes, tile_sems)
        due = spread.steps()
        load.wait()
        spread.fill(held)
        place.greet(True, True)
        spread.begin()
    else:
        place.greet(False)
        loads = [
            pltpu.make_async_copy(src, dst, sem_local.at[8 + slot])
            for slot, (src, dst) in enumerate(zip((first_in, middle_in, last_in), weights))
        ]
        for load in loads:
            load.start()
        due = []

    quarter = half // 2
    own_rows = pl.ds(pl.multiple_of(core * count_rows, count_rows), count_rows)
    mate_rows = pl.ds(pl.multiple_of((1 - core) * count_rows, count_rows), count_rows)
    top_rows = pl.ds(0, count_rows)
    own_copies = [
        pltpu.make_async_copy(
            features.at[own_rows, pl.ds(side * quarter, quarter)], buffer, sem_local.at[side]
        )
        for side, buffer in enumerate((hidden_two, mid_wide.at[top_rows, :]))
    ]
    per_kind = params.shape[0] // 2
    for kind in range(2):
        rows = [params[kind * per_kind + spot : kind * per_kind + spot + 1, :] for spot in range(per_kind)]
        params_all[core, kind : kind + 1, :] = jnp.concatenate(rows, axis=1)
    head_all[core] = jnp.zeros(head_all.shape[1:], low_type)
    for spot in range(half // LANES):
        head_all[core, 0:classes, spot * LANES : (spot + 1) * LANES] = head[
            pl.ds(spot, classes, stride=half // LANES), :
        ].astype(low_type)
    to_mate = [
        remote(params_all.at[core], params_all.at[core], sem_misc.at[0, 0], sem_misc.at[1, 0], *mate),
        remote(head_all.at[core], head_all.at[core], sem_misc.at[0, 1], sem_misc.at[1, 1], *mate),
    ]
    for side, buffer in enumerate((taps_one, taps_two)):
        to_mate.append(
            remote(
                features.at[mate_rows, pl.ds(side * quarter, quarter)],
                buffer.at[top_rows, :],
                sem_misc.at[0, 5 + side],
                sem_misc.at[1, 5 + side],
                *mate,
            )
        )
    for copy in to_mate + own_copies:
        copy.start()

    def advance(count):
        for group in due[:count]:
            for step in group:
                step()
        del due[:count]

    def advance_at(index, spots):
        for spot, group in zip(spots, due):

            @pl.when(index == spot)
            def _():
                for step in group:
                    step()

    def arrive(slot, left):
        if gather:
            advance(len(due) - left)
            spread.arrive(slot)
        else:
            loads[slot].wait()

    def arrive_turns(slot, turns):
        if gather:
            for turn in turns:
                for copy in spread.core_copies(turn, slot):
                    copy.wait_recv()

    def fold_step(kind, slot, which):
        if gather:
            (fold.core_step, fold.near_step, fold.far_step)[kind](which, slot)

    def fold_at(index, spot, *steps):
        @pl.when(index == spot)
        def _():
            for step in steps:
                fold_step(*step)

    def fold_begin(which, slot):
        if gather:
            fold.begin(which, slot)

    def zero_edges(buffer):
        edge = jnp.zeros((line,) + buffer.shape[1:], low_type)
        buffer[0:line, :] = edge
        buffer[line + count_rows : 2 * line + count_rows, :] = edge

    advance(3)
    for copy in own_copies:
        copy.wait()

    def turn_from(source, base):
        def turn(index, carry):
            stage[...] = source(lanes(index, LANES)).astype(wide)

            def pixel(spot, inner):
                x_all[
                    pl.ds(pl.multiple_of(spot * mine_images, mine_images), mine_images),
                    pl.ds(pl.multiple_of(base + index * LANES, LANES), LANES),
                ] = stage[pl.ds(spot, mine_images, stride=PIXELS), :].astype(low_type)
                return inner

            return lax.fori_loop(0, PIXELS, pixel, carry, unroll=7)

        return turn

    quarters = quarter // LANES
    own_base, mate_base = core * half, (1 - core) * half
    lax.fori_loop(0, quarters, turn_from(lambda columns: hidden_two[:, columns], own_base), 0)
    advance(1)
    lax.fori_loop(
        0,
        quarters,
        turn_from(lambda columns: mid_wide[0:count_rows, columns], own_base + quarter),
        0,
    )
    advance(1)
    for copy in to_mate:
        copy.wait_recv()
    lax.fori_loop(0, quarters, turn_from(lambda columns: taps_one[0:count_rows, columns], mate_base), 0)
    advance(1)
    lax.fori_loop(0, quarters, turn_from(lambda columns: taps_two[0:count_rows, columns], mate_base + quarter), 0)
    zero_edges(taps_one)
    zero_edges(taps_two)
    arrive(0, 9)

    def swap(slot, size):
        return remote(
            sums_mine.at[slot, :, pl.ds(0, size)],
            sums_theirs.at[slot, :, pl.ds(0, size)],
            sem_swap.at[0, slot],
            sem_swap.at[1, slot],
            *mate,
        )

    def gain_bias(lower, upper):
        rows = []
        for kind in range(2):
            pieces = [params_all[side, kind : kind + 1, lower:upper] for side in range(2)]
            rows.append(jnp.concatenate(pieces, axis=1))
        return rows

    def collect(index, value, columns, size):
        @pl.when(index == 0)
        def _():
            shift[0:1, pl.ds(0, size)] = column_sum(fold_rows(value)) / value.shape[0]
            shift[8:24, pl.ds(0, size)] = jnp.zeros((16, size), wide)

        gap = value - shift[0:1, pl.ds(0, size)]
        shift[8:16, pl.ds(0, size)] += fold_rows(gap)
        shift[16:24, pl.ds(0, size)] += fold_rows(gap * gap)

    def close_stats(slot, columns, size):
        sum_gap = column_sum(shift[8:16, pl.ds(0, size)])
        sum_square = column_sum(shift[16:24, pl.ds(0, size)])
        sums_mine[slot, 0:1, columns] = shift[0:1, pl.ds(0, size)] + sum_gap / count_rows
        sums_mine[slot, 1:2, columns] = sum_square - sum_gap * sum_gap / count_rows

    def look_over(act, columns):
        def look(index, carry):
            collect(index, act[tile(index), columns], None, width)
            return carry

        lax.fori_loop(0, SIDE, look, 0)

    groups = SPOTS[0]
    group = channels // groups

    def settle(slot, size):
        mean, scale = norm_stats(
            sums_mine[slot, 0:2, pl.ds(0, size)], sums_theirs[slot, 0:2, pl.ds(0, size)], float(count_rows)
        )
        fwd_stats[slot, 0:1, pl.ds(0, size)] = mean
        fwd_stats[slot, 1:2, pl.ds(0, size)] = scale

    whole_width = pl.ds(0, width)

    def first_part(index, carry):
        act_one[...] += dot_nn(x_all[:, lanes(index, group)], flat_rows(w_first[index]))
        advance_at(index, (0, 1, 2))
        return carry

    act_one[...] = jnp.zeros_like(act_one)
    lax.fori_loop(0, groups, first_part, 0)
    del due[:3]
    look_over(act_one, whole_width)
    close_stats(0, whole_width, width)
    move = swap(0, width)
    move.start()
    advance(1)
    move.wait()
    settle(0, width)

    gain_one, bias_one = gain_bias(0, part)
    gain_two, bias_two = gain_bias(part, width)
    gain_three, bias_three = gain_bias(width, width + half)

    def normal(act, slot, index):
        mean = fwd_stats[slot, 0:1, pl.ds(0, width)]
        return (act[tile(index), :] - mean) * fwd_stats[slot, 1:2, pl.ds(0, width)]

    def hide_one(index, carry):
        value = normal(act_one, 0, index) * gain_one + bias_one
        taps_one[pl.ds(pl.multiple_of((index + 1) * line, line), line), :] = (value * sigmoid(value)).astype(low_type)
        return carry

    lax.fori_loop(0, SIDE, hide_one, 0)
    if gather:
        arrive_turns(1, (0, 1))
    else:
        arrive(1, 0)

    step = mine_images
    piece = width // 2

    def row_windows(buffer, down, start, reach):
        if reach == line:
            return buffer[pl.ds(pl.multiple_of(down * line, line), count_rows), :]
        windows = [
            buffer[pl.ds(pl.multiple_of((down + row) * line + start, step), reach), :] for row in range(SIDE)
        ]
        return jnp.concatenate(windows, axis=0)

    def add_windows(target, columns, value, start, reach):
        for row in range(SIDE):
            rows = slice(row * line + start, row * line + start + reach)
            target[rows, columns] += value[row * reach : (row + 1) * reach]

    low_start, high_start, reaches = (0, 0, step), (step, 0, 0), (line - step, line, line - step)

    early, taps = 4, 9

    def second_part(index, carry):
        tap = jnp.where(place.z < 2, index, (index + taps - early) % taps) if gather else index

        @pl.when(index == early)
        def _():
            arrive_turns(1, (2, 3))

        down = tap // 3
        for over in range(3):

            @pl.when(tap % 3 == over)
            def _():
                left = row_windows(taps_one, down, low_start[over], reaches[over])
                kernel = w_middle[pl.ds(pl.multiple_of(tap * width, width), width), :]
                add_windows(act_two, slice(None), dot_nn(left, kernel), high_start[over], reaches[over])

        advance_at(index, (2, 5, 6, 8))
        return carry

    act_two[...] = jnp.zeros_like(act_two)
    lax.fori_loop(0, taps, second_part, 0)
    del due[:4]
    look_over(act_two, whole_width)
    close_stats(1, whole_width, width)
    move_two = swap(1, width)
    move_two.start()
    arrive(2, 0)
    if gather:
        spread.drain(0)

    def turn_weights(which, carry):
        w_first[which] = jnp.transpose(flat_rows(w_last[which])).reshape(w_first.shape[1:])
        return carry

    lax.fori_loop(0, groups, turn_weights, 0)
    move_two.wait()
    settle(1, width)

    tall = count_rows // 2

    def third_tile(index, carry):
        rows = pl.ds(pl.multiple_of(index * tall, 16), tall)
        act = act_two[rows, :]
        normed = (act - fwd_stats[1, 0:1, whole_width]) * fwd_stats[1, 1:2, whole_width]
        value = normed * gain_two + bias_two
        hidden = (value * sigmoid(value)).astype(low_type)
        hidden_two[rows, :] = hidden
        for which in range(groups):
            columns = slice(which * group, (which + 1) * group)
            value = dot_nn(hidden, flat_rows(w_first[which]))
            act_three[rows, columns] = value
            start = jnp.where(index == 0, column_sum(value[0:8]) / 8.0, shift[0:1, columns])
            gap = value - start
            kept_sums = jnp.where(index == 0, 0.0, shift[8:24, columns])
            shift[0:1, columns] = start
            shift[8:16, columns] = kept_sums[0:8] + fold_rows(gap)
            shift[16:24, columns] = kept_sums[8:16] + fold_rows(gap * gap)
        return carry

    lax.fori_loop(0, 2, third_tile, 0)
    close_stats(2, pl.ds(0, channels), channels)
    move_three = swap(2, channels)
    move_three.start()
    move_three.wait()
    settle(2, channels)

    per_group = group // LANES

    def block_of(spot):
        return pl.ds(pl.multiple_of(spot * mine_images, mine_images), mine_images)

    def mid_line(which, index):
        return pl.ds(pl.multiple_of(which * count_rows + index * line, line), line)

    kept = channels // LANES * mine_images

    def gathered(kind):
        starts = range(kind * kept, (kind + 1) * kept, mine_images)
        return jnp.concatenate([stage[start : start + mine_images, :] for start in starts], axis=1)

    fwd_stats[2, 4:5, :] = fwd_stats[2, 1:2, :] * gain_three
    fwd_stats[2, 5:6, :] = bias_three - fwd_stats[2, 0:1, :] * fwd_stats[2, 4:5, :]

    def emit(index, carry):
        columns = lanes(index, LANES)
        slant, level = fwd_stats[2, 4:5, columns], fwd_stats[2, 5:6, columns]

        def pixels(row, sums):
            pooled, steeps, steeps_act = sums
            found = []
            for spot in range(SIDE):
                where = block_of(row * SIDE + spot)
                act = act_three[where, columns]
                half_total = 0.5 * (act * slant + level + x_all[where, columns].astype(wide))
                rise = 1.0 + jnp.tanh(half_total)
                out = half_total * rise
                steep = rise + out * (2.0 - rise)
                found.append(steep.astype(low_type))
                pooled, steeps, steeps_act = pooled + out, steeps + steep, steeps_act + steep * act
            mid_wide[mid_line(index // per_group, row), lanes(index % per_group, LANES)] = jnp.concatenate(
                found, axis=0
            )
            return pooled, steeps, steeps_act

        zero = jnp.zeros((mine_images, LANES), wide)
        sums = lax.fori_loop(0, SIDE, pixels, (zero, zero, zero))
        for kind, value in enumerate(sums):
            stage[pl.ds(pl.multiple_of(kind * kept + index * mine_images, mine_images), mine_images), :] = value
        return carry

    lax.fori_loop(0, channels // LANES, emit, 0)

    pooled = (gathered(0) / PIXELS).astype(low_type)
    head_full = jnp.concatenate([head_all[0], head_all[1]], axis=1)
    logits = dot_nt(head_full, pooled)
    spots = lax.broadcasted_iota(jnp.int32, logits.shape, 0)
    inside = spots < classes
    first_labels, second_labels = labels[0:1, 0:mine_images], labels[0:1, mine_images:]
    onehot = (spots == jnp.where(core == 0, first_labels, second_labels)).astype(wide)
    top = jnp.max(jnp.where(inside, logits, -jnp.inf), axis=0, keepdims=True)
    powers = jnp.where(inside, jnp.exp(logits - top), 0.0)
    power_sum = jnp.sum(powers, axis=0, keepdims=True)
    picked = jnp.sum(logits * onehot, axis=0, keepdims=True)
    each_loss = top + jnp.log(power_sum) - picked
    taking = flag[0].astype(wide)
    tile_spots = lax.broadcasted_iota(jnp.int32, loss_out.shape, 1)
    loss_out[...] = jnp.where(tile_spots == 0, taking * jnp.sum(each_loss), taking * mine_images)
    grads = (taking / images * (powers / power_sum - onehot)).astype(low_type)
    grad_pool[...] = dot_tn(grads, head_full) * (0.5 / PIXELS)
    logit_grads[core] = grads
    pool_all[core] = pooled[:, 0:half]
    pool_send[...] = pooled[:, half:]

    @pl.when(core == 1)
    def _():
        pool_all[core] = pooled[:, half:]
        pool_send[...] = pooled[:, 0:half]

    head_moves = [
        remote(pool_send, pool_all.at[core], sem_misc.at[0, 3], sem_misc.at[1, 3], *mate),
        remote(logit_grads.at[core], logit_grads.at[core], sem_misc.at[0, 4], sem_misc.at[1, 4], *mate),
    ]

    steeps = gathered(1)
    steeps_normed = (gathered(2) - fwd_stats[2, 0:1, :] * steeps) * fwd_stats[2, 1:2, :]
    sums_mine[3, 0:1, :] = column_sum(grad_pool[...] * steeps)
    sums_mine[3, 1:2, :] = column_sum(grad_pool[...] * steeps_normed)
    move_back = swap(3, channels)
    move_back.start()
    for copy in head_moves:
        copy.start()
    move_back.wait()

    def back_terms(slot, layer, size, gain):
        columns = pl.ds(0, size)
        sums = sums_mine[slot, 0:2, columns] + sums_theirs[slot, 0:2, columns]
        sums_mine[slot, 2:4, columns] = sums
        scale = fwd_stats[layer, 1:2, columns]
        return (
            scale * gain,
            scale * gain * sums[0:1] / total_rows,
            scale * scale * gain * sums[1:2] / total_rows,
        )

    first, second, third = back_terms(3, 2, channels, gain_three)
    fwd_stats[2, 4:5, :] = second - third * fwd_stats[2, 0:1, :]
    fwd_stats[2, 5:6, :] = third
    grad_pool[...] = grad_pool[...] * first

    def pull(index):
        for which in range(groups):
            columns = slice(which * group, (which + 1) * group)
            reach = grad_pool[:, columns]
            steep = mid_wide[mid_line(which, index), :].astype(wide)
            value = jnp.concatenate([reach] * SIDE, axis=0) * steep
            value = value - fwd_stats[2, 4:5, columns] - fwd_stats[2, 5:6, columns] * act_three[tile(index), columns]
            mid_wide[mid_line(which, index), :] = value.astype(low_type)

    pull(0)

    def drop_into(act, slot, gain, bias, columns):
        size = pl.ds(0, width)
        shift[8:24, size] = jnp.zeros((16, width), wide)

        def drop(index, carry):
            normed = normal(act, slot, index)
            norm = normed * gain + bias
            sig = sigmoid(norm)
            grad = act_three[tile(index), columns] * (sig + norm * sig * (1.0 - sig))
            act_three[tile(index), columns] = grad
            shift[8:16, size] += fold_rows(grad)
            shift[16:24, size] += fold_rows(grad * normed)
            return carry

        lax.fori_loop(0, SIDE, drop, 0)

    def close_back(slot):
        size = pl.ds(0, width)
        sums_mine[slot, 0:1, size] = column_sum(shift[8:16, size])
        sums_mine[slot, 1:2, size] = column_sum(shift[16:24, size])

    space_two, space_one = pl.ds(0, width), pl.ds(width, width)

    def mid_group(which):
        return mid_wide[pl.ds(pl.multiple_of(which * count_rows, count_rows), count_rows), :]

    def back_two(index):
        left = jnp.concatenate([mid_wide[mid_line(which, index), :] for which in range(groups)], axis=1)
        value = dot_nn(left, flat_rows(w_last[...]))
        normed = normal(act_two, 1, index)
        norm = normed * gain_two + bias_two
        sig = sigmoid(norm)
        grad = value * (sig + norm * sig * (1.0 - sig))
        act_three[tile(index), space_two] = grad
        size = pl.ds(0, width)
        shift[8:16, size] += fold_rows(grad)
        shift[16:24, size] += fold_rows(grad * normed)

    def back_two_line(index, carry):
        pull(index + 1)
        back_two(index)
        return carry

    shift[8:24, :] = jnp.zeros((16, channels), wide)
    lax.fori_loop(0, SIDE - 1, back_two_line, 0)
    back_two(SIDE - 1)
    close_back(4)
    move_back_two = swap(4, width)
    move_back_two.start()
    if gather:
        base_loads = [
            pltpu.make_async_copy(src, dst, sem_local.at[1 + number])
            for number, (src, dst) in enumerate(
                ((master, held_base), (momentum, held_momentum), (anchor, held_anchor))
            )
        ]
        for load in base_loads:
            load.start()
        tiles[0] = loss_out[...]
        tile_sum.start()

    def settle_section(slot):
        if gather:
            rows = share.section(slot)
            grad = fold.result(slot) + prox_weight * (held_base[rows, :] - held_anchor[rows, :])
            fresh[rows, :] = momentum_decay * held_momentum[rows, :] + grad
            share.send(slot)

    if gather:
        spread.drain(1)
        spread.drain(2)

    def put(ref, which, value):
        ref[which] = value.astype(low_type).reshape(ref.shape[1:])

    def expand_group(which, carry):
        put(w_last, which, dot_tn(mid_group(which), hidden_two[...]))
        fold_begin(which, 2)
        fold_at(which, 2, (0, 2, 0))
        fold_at(which, 3, (0, 2, 1))
        return carry

    lax.fori_loop(0, groups, expand_group, 0)
    move_back_two.wait()
    terms_two = back_terms(4, 1, width, gain_two)

    def back_act(terms, act, layer, index, columns):
        first, second, third = terms
        gap = act[tile(index), :] - fwd_stats[layer, 0:1, pl.ds(0, width)]
        return (first * act_three[tile(index), columns] - second - third * gap).astype(low_type)

    def grad_two(index, carry):
        taps_two[pl.ds(pl.multiple_of((index + 1) * line, line), line), :] = back_act(
            terms_two, act_two, 1, index, space_two
        )
        return carry

    lax.fori_loop(0, SIDE, grad_two, 0)
    fold_step(0, 2, 2)
    fold_step(1, 2, 0)
    core_step, near_step, far_step = 0, 1, 2
    plan = {
        0: [(core_step, 2, 3)],
        1: [(near_step, 2, 1)],
        2: [(far_step, 2, 0), (near_step, 2, 2)],
        3: [(far_step, 2, 1), (near_step, 2, 3)],
        4: [(far_step, 2, 2)],
        5: [(far_step, 2, 3), (core_step, 1, 0)],
        7: [(core_step, 1, 1)],
    }

    def middle_row(down, carry):
        for over in range(3):
            left = row_windows(taps_one, down, low_start[over], reaches[over])
            right = row_windows(taps_two, 1, high_start[over], reaches[over])
            rows = pl.ds(pl.multiple_of((3 * down + over) * width, width), width)
            mid_wide[rows, :] = dot_tn(left, right).astype(low_type)
            for row in range(3):
                tap = 3 * row + over

                @pl.when(down == row)
                def _():
                    if tap >= 2 and tap % 2 == 0:
                        fold_begin(tap // 2 - 1, 1)
                    for step in plan.get(tap, ()):
                        fold_step(*step)

        return carry

    lax.fori_loop(0, 3, middle_row, 0)
    for copy in head_moves:
        copy.wait_recv()
    head_grad = dot_nn(logit_grads[0], pool_all[0]) + dot_nn(logit_grads[1], pool_all[1])
    for spot in range(half // LANES):
        stage[pl.ds(spot, classes, stride=half // LANES), :] = head_grad[
            0:classes, spot * LANES : (spot + 1) * LANES
        ]
    head_space = stage.at[pl.ds(0, grad_head_out.shape[0]), :]
    head_leave = pltpu.make_async_copy(head_space, grad_head_out, sem_local.at[0])
    head_leave.start()
    if gather:
        tile_sum.pair(0)
        for load in base_loads:
            load.wait()

    def back_one(index, carry):
        down, side = index // 2, index % 2
        columns = lanes(2 + side, piece)
        for over in range(3):
            left = row_windows(taps_two, 2 - down, high_start[over], reaches[over])
            start = pl.multiple_of((3 * down + over) * width + side * piece, piece)
            value = dot_nt(left, w_middle[pl.ds(start, piece), :])
            add_windows(act_three, columns, value, low_start[over], reaches[over])
        fold_at(index, 0, (core_step, 1, 2), (near_step, 1, 0))
        fold_at(index, 1, (core_step, 1, 3))
        fold_at(index, 2, (near_step, 1, 1), (far_step, 1, 0))
        fold_at(index, 4, (far_step, 1, 1))
        fold_at(index, 5, (near_step, 1, 2))
        return carry

    act_three[:, space_one] = jnp.zeros((count_rows, width), wide)
    lax.fori_loop(0, 6, back_one, 0)
    drop_into(act_one, 0, gain_one, bias_one, space_one)
    fold_step(near_step, 1, 3)
    settle_section(2)
    close_back(5)
    move_back_one = swap(5, width)
    move_back_one.start()

    move_back_one.wait()
    terms_one = back_terms(5, 0, width, gain_one)

    def grad_one(index, carry):
        hidden_two[tile(index), :] = back_act(terms_one, act_one, 0, index, space_one)
        return carry

    lax.fori_loop(0, SIDE, grad_one, 0)
    fold_step(far_step, 1, 2)
    if gather:
        tile_sum.pair(1)

    def reduce_group(which, carry):
        put(w_first, which, dot_tn(x_all[:, lanes(which, group)], hidden_two[...]))
        fold_begin(which, 0)
        fold_at(which, 0, (far_step, 1, 3))
        fold_at(which, 2, (core_step, 0, 0))
        fold_at(which, 3, (core_step, 0, 1), (near_step, 0, 0))
        return carry

    lax.fori_loop(0, groups, reduce_group, 0)

    for kind in range(2):
        row = 3 - kind
        pieces = [
            sums_mine[5, row : row + 1, lanes(core, part)],
            sums_mine[4, row : row + 1, lanes(core, part)],
            sums_mine[3, row : row + 1, lanes(core, half)],
        ]
        whole = jnp.concatenate(pieces, axis=1)
        per_kind = whole.shape[1] // LANES
        for spot in range(per_kind):
            grad_norm_out[kind * per_kind + spot : kind * per_kind + spot + 1, :] = whole[
                :, spot * LANES : (spot + 1) * LANES
            ]
    for step in (
        (core_step, 0, 2),
        (core_step, 0, 3),
        (far_step, 0, 0),
        (near_step, 0, 1),
        (near_step, 0, 2),
        (far_step, 0, 1),
        (near_step, 0, 3),
        (far_step, 0, 2),
        (far_step, 0, 3),
    ):
        fold_step(*step)
        if step == (far_step, 0, 0):
            settle_section(1)
    if gather:
        settle_section(0)
        leave = pltpu.make_async_copy(fresh, fresh_out, sem_local.at[1])
        leave.start()
        tile_sum.pair(2)
        part = width // CUTS
        gram = act_three.at[pl.ds(0, gram_total.shape[0]), pl.ds(half + width, 2 * part)]
        corner_rows = pl.ds(gram_total.shape[0], width)
        squares = [act_three.at[corner_rows, pl.ds(spot * width, width)] for spot in (0, 1, 3)]
        gram_sum = GramSum(place, gram, gram_total, (y_box, z_box), gram_sems)
        orthogonal(place, ratios, share, share_sems, gram, gram_total, mate_gram, gram_sum, squares, rows_in, hidden_two)
        share.finish()
        loss_out[...] = tile_sum.result()
        ortho_leave = pltpu.make_async_copy(back, ortho_out, sem_local.at[2])
        ortho_leave.start()
        gram_sum.drain()
        tile_sum.drain()
        fold.drain()
        leave.wait()
        ortho_leave.wait()
    else:
        outs = [
            pltpu.make_async_copy(ref, out, sem_local.at[slot])
            for slot, (ref, out) in enumerate(zip((w_first, mid_wide.at[pl.ds(0, 9 * width), :], w_last), grads_out))
        ]
        for copy in outs:
            copy.start()
        for copy in outs:
            copy.wait()
    head_leave.wait()
    for copy in to_mate + head_moves:
        copy.wait_send()


def client_pass(gather, ratios, classes, features, labels, flag, params, head, weights):
    pixels, half = features.shape
    images = labels.shape[1]
    count_rows, channels = pixels // 2, 2 * half
    width = params.shape[0] // 2 * LANES - half
    head_rows = classes + -classes % 16
    mine_images = images // 2
    line = SIDE * mine_images
    middle = 9 * width
    blocks = 32
    group = channels // SPOTS[0]
    vmem = pl.BlockSpec(memory_space=pltpu.VMEM)
    smem = pl.BlockSpec(memory_space=pltpu.SMEM)
    spots = SPOTS + (2,)
    scratch = [
        pltpu.VMEM((count_rows, channels), low_type),
        pltpu.VMEM((SPOTS[0] * count_rows, group), low_type),
        pltpu.VMEM(spots + (channels // blocks, width), low_type),
        pltpu.VMEM((middle, width), low_type),
        pltpu.VMEM(spots + (channels // blocks, width), low_type),
        pltpu.VMEM((count_rows, width), wide),
        pltpu.VMEM((count_rows, width), wide),
        pltpu.VMEM((count_rows, channels), wide),
        pltpu.VMEM((count_rows + 2 * line, width), low_type),
        pltpu.VMEM((count_rows + 2 * line, width), low_type),
        pltpu.VMEM((count_rows, width), low_type),
        pltpu.VMEM((count_rows, LANES), wide),
        pltpu.VMEM((2, 2, half + width), wide),
        pltpu.VMEM((2, head_rows, half), low_type),
        pltpu.VMEM((mine_images, channels), wide),
        pltpu.VMEM((mine_images, half), low_type),
        pltpu.VMEM((2, mine_images, half), low_type),
        pltpu.VMEM((2, head_rows, mine_images), low_type),
        pltpu.VMEM((6, 8, channels), wide),
        pltpu.VMEM((6, 8, channels), wide),
        pltpu.VMEM((24, channels), wide),
        pltpu.VMEM((3, 8, channels), wide),
        pltpu.SemaphoreType.DMA((11,)),
        pltpu.SemaphoreType.DMA((2, 6)),
        pltpu.SemaphoreType.DMA((2, 7)),
    ]
    any_space = pl.BlockSpec(memory_space=pl.ANY)
    if gather:
        counts = (channels // blocks, middle // blocks, channels // blocks)
        scratch += [pltpu.SemaphoreType.DMA((2, 3, 3))]
        scratch += [pltpu.SemaphoreType.DMA((2, 4, size)) for size in (6, 8, 6)]
        scratch += [pltpu.VMEM((4, 2, 2, rows, width), low_type) for rows in counts[1:]]
        for lead in ((4, 2), (4,), (4,)):
            scratch += [pltpu.VMEM(lead + (rows, width), low_type) for rows in counts]
        scratch += [pltpu.SemaphoreType.DMA((2, 4, size)) for size in (6, 8, 6, 6)]
        part = width // CUTS
        gram_rows = CUTS * (CUTS + 1) // 4 * part
        many = max(4 * counts[0], 2 * counts[1])
        scratch += [
            pltpu.VMEM((many, width), wide),
            pltpu.VMEM((sum(counts), width), low_type),
            pltpu.VMEM((4, 8, LANES), wide),
            pltpu.VMEM((6, 8, LANES), wide),
            pltpu.VMEM((gram_rows, 2 * part), wide),
            pltpu.VMEM((4, gram_rows // 8, 2 * part), wide),
            pltpu.VMEM((3, gram_rows // 8, 2 * part), wide),
            pltpu.VMEM((gram_rows, 2 * part), wide),
            pltpu.SemaphoreType.DMA((2, 6)),
            pltpu.SemaphoreType.DMA((2, 8)),
            pltpu.SemaphoreType.DMA((2, 14)),
        ]
        grads_shape = [
            jax.ShapeDtypeStruct((sum(counts), width), wide),
            jax.ShapeDtypeStruct((sum(counts), width), low_type),
        ]
        grads_specs = [any_space] * 2
    else:
        grads_shape = [jax.ShapeDtypeStruct(weight.shape, low_type) for weight in weights]
        grads_specs = [any_space] * 3
    return pl.pallas_call(
        functools.partial(client_kernel, gather, ratios, images, classes),
        out_shape=grads_shape
        + [
            jax.ShapeDtypeStruct(params.shape, wide),
            jax.ShapeDtypeStruct((classes * half // LANES, LANES), wide),
            jax.ShapeDtypeStruct((8, LANES), wide),
        ],
        in_specs=[any_space, vmem, smem, vmem, vmem] + [any_space] * len(weights),
        out_specs=grads_specs + [vmem, any_space, vmem],
        scratch_shapes=scratch,
        compiler_params=pltpu.CompilerParams(
            collective_id=0, has_side_effects=True, vmem_limit_bytes=VMEM_BYTES
        ),
    )(features, labels, flag, params, head, *weights)


def adam_update(param, grad, first, second, rate, decay):
    first = adam_first * first + (1.0 - adam_first) * grad
    second = adam_second * second + (1.0 - adam_second) * grad * grad
    first_hat = first / (1.0 - adam_first**STEP)
    second_hat = second / (1.0 - adam_second**STEP)
    return (
        param - rate * (first_hat / (jnp.sqrt(second_hat) + adam_epsilon) + decay * param),
        first,
        second,
    )


def gram_of(section):
    return lax.dot_general(section, section, (((0,), (0,)), ((), ())), precision=precise)


def square(gram):
    return jnp.dot(gram, gram, precision=precise)


def times_poly(left, mixed):
    return schulz_first * left + jnp.dot(left, mixed, precision=precise)


def schulz(sections):
    raw_grams = lax.psum(tuple(gram_of(section) for section in sections), ("client", "chan"))
    factors = [1.0 / (jnp.sqrt(jnp.trace(gram)) + 1e-07) for gram in raw_grams]
    current = [section * factor for section, factor in zip(sections, factors)]
    grams = [gram * (factor * factor) for gram, factor in zip(raw_grams, factors)]
    for turn in range(NS_STEPS):
        mixed = [schulz_second * gram + schulz_third * square(gram) for gram in grams]
        current = [times_poly(current[slot], mixed[slot]) for slot in range(3)]
        if turn + 1 < NS_STEPS:
            grams = [
                times_poly(times_poly(grams[slot], mixed[slot]), mixed[slot]) for slot in range(3)
            ]
    return current


def base_far(ratios, bounds, master, momentum, anchor, loss_tile, grads):
    sums = [
        lax.psum_scatter(flat_rows(grad).astype(wide), ("client", "chan"), scatter_dimension=0, tiled=True)
        for grad in grads
    ]
    grad_base = jnp.concatenate(sums, axis=0)
    momentum_new = momentum_decay * momentum + (grad_base + prox_weight * (master - anchor))
    current = schulz([momentum_new[bounds[slot] : bounds[slot + 1]] for slot in range(3)])
    ortho = jnp.concatenate([current[slot] * ratios[slot] for slot in range(3)], axis=0)
    return momentum_new, ortho, lax.psum(loss_tile, ("client", "chan"))


def as_stored(rows, shape):
    return with_layout_constraint(rows.reshape(shape), Layout(major_to_minor=tuple(range(len(shape)))))


def on_device(
    features,
    labels,
    mask,
    base_master,
    base_momentum,
    global_base,
    norm_params,
    norm_first,
    norm_second,
    head,
    head_first,
    head_second,
):
    halves = lax.axis_size("chan")
    blocks = lax.axis_size("client") * halves
    half = features.shape[2]
    width = base_master.shape[2]
    channels = half * halves
    classes = head.shape[2]
    rows_first = channels // blocks
    rows_mid = 9 * width // blocks
    bounds = (0, rows_first, rows_first + rows_mid, base_master.shape[1])
    ratio = (channels / width) ** 0.5
    ratios = (ratio, 3.0, ratio)
    master, momentum, anchor = base_master[0], base_momentum[0], global_base[0]
    norms = [value.reshape(-1, LANES) for value in (norm_params, norm_first, norm_second)]
    heads = [jnp.transpose(value, (2, 0, 1)).reshape(-1, LANES) for value in (head, head_first, head_second)]
    near = lax.axis_size("client") == SPOTS[0] * SPOTS[1] * SPOTS[2]
    if near:
        weights = [master, momentum, anchor]
    else:
        low_master = master.astype(low_type)
        weights = [
            lax.all_gather(low_master[bounds[slot] : bounds[slot + 1]], ("client", "chan"), axis=0, tiled=True)
            for slot in range(3)
        ]
        split = SPOTS + (2, channels // 32, width)
        weights = [weights[0].reshape(split), weights[1], weights[2].reshape(split)]
    *grads, grad_norm, grad_head, loss_tile = client_pass(
        near, ratios, classes, features[0], labels, mask, norms[0], heads[0], weights
    )
    if near:
        fresh_momentum, ortho = grads
    else:
        fresh_momentum, ortho, loss_tile = base_far(ratios, bounds, master, momentum, anchor, loss_tile, grads)
    loss, momentum_new, base_new, base_low, *fresh = update_pass(
        loss_tile, master, fresh_momentum, ortho, norms, grad_norm, heads, grad_head
    )
    fresh_norms = [as_stored(value, norm_params.shape) for value in fresh[:3]]
    fresh_heads = [jnp.transpose(as_stored(value, (classes, 1, half)), (1, 2, 0)) for value in fresh[3:]]
    return (
        loss,
        base_new[None],
        momentum_new[None],
        base_low[None],
        *fresh_norms,
        *fresh_heads,
    )


def solution(mesh):
    wide_block = P(("client", "chan"), None, None)
    norm_block = P("client", None, "chan", None)
    head_block = P("client", "chan", None)
    return jax.shard_map(
        on_device,
        mesh=mesh,
        in_specs=(P("client", None, "chan"), P("client", None), P("client"))
        + (wide_block,) * 3
        + (norm_block,) * 3
        + (head_block,) * 3,
        out_specs=(P(),) + (wide_block,) * 3 + (norm_block,) * 3 + (head_block,) * 3,
        check_vma=False,
    )
```

```python
import functools

import jax
import jax.numpy as jnp
from jax import lax
from jax.experimental import pallas as pl
from jax.experimental.layout import Layout, with_layout_constraint
from jax.experimental.pallas import tpu as pltpu
from jax.sharding import PartitionSpec as P

NS_STEPS = 5
STEP = 10

low_type = jnp.bfloat16
wide = jnp.float32
MESH = pl.DeviceIdType.MESH
precise = lax.Precision.HIGHEST
norm_epsilon = 1e-05
prox_weight = 0.05
momentum_decay = 0.95
muon_rate = 0.3
muon_decay = 0.1
schulz_first = 3.4445
schulz_second = -4.775
schulz_third = 2.0315
adam_first = 0.9
adam_second = 0.95
adam_epsilon = 1e-08
head_rate = 0.01
head_decay = 0.05
norm_rate = 0.5

SIDE = 7
PIXELS = SIDE * SIDE
LANES = 128
SPOTS = (4, 2, 2)
CUTS = 4
VMEM_BYTES = 62 * 2**20


def dot_nn(left, right):
    return jnp.dot(left, right, preferred_element_type=wide)


def dot_nt(left, right):
    return lax.dot_general(left, right, (((1,), (1,)), ((), ())), preferred_element_type=wide)


def dot_tn(left, right):
    return lax.dot_general(left, right, (((0,), (0,)), ((), ())), preferred_element_type=wide)


def flat_rows(block):
    return block.reshape(-1, block.shape[-1])


def sigmoid(value):
    return 0.5 * jnp.tanh(0.5 * value) + 0.5


def fold_rows(value):
    return jnp.sum(value.reshape(value.shape[0] // 8, 8, value.shape[1]), axis=0)


def column_sum(value):
    return jnp.sum(value, axis=0, keepdims=True)


def remote(src, dst, send_sem, recv_sem, client, core):
    return pltpu.make_async_remote_copy(
        src_ref=src,
        dst_ref=dst,
        send_sem=send_sem,
        recv_sem=recv_sem,
        device_id=(client, core),
        device_id_type=MESH,
    )


class Place:
    def __init__(self):
        self.client = lax.axis_index("client")
        self.core = lax.axis_index("chan")
        self.z = self.client // 4
        self.y = (self.client // 2) % 2
        self.x = self.client % 2
        self.others = [
            self.z + 1 - 2 * (self.z % 2),
            (self.z + 2) % 4,
            3 - self.z,
        ]

    def at(self, z, y, x):
        return z * 4 + y * 2 + x

    def along_x(self):
        return self.at(self.z, self.y, 1 - self.x)

    def along_y(self):
        return self.at(self.z, 1 - self.y, self.x)

    def along_z(self, step):
        return self.at(self.others[step], self.y, self.x)

    def greet(self, whole, across=False):
        barrier = pltpu.get_barrier_semaphore()
        pairs = [(self.client, 1 - self.core)]
        if whole:
            pairs += [(self.along_x(), self.core), (self.along_y(), self.core)]
            pairs += [(self.along_z(step), self.core) for step in range(3)]
        if across:
            pairs += [(self.along_x(), 1 - self.core)]
        for pair in pairs:
            pl.semaphore_signal(barrier, inc=1, device_id=pair, device_id_type=MESH)
        pl.semaphore_wait(barrier, len(pairs))


def cut_rows(counts):
    pieces = []
    for slot, rows in enumerate(counts):
        middle = (rows // 16 + 1) // 2 * 16
        pieces.append((slot, 0, middle, 0))
        pieces.append((slot, middle, rows - middle, 1))
    return pieces


def block_ref(ref, size, z, y, x, core, start, count):
    if len(ref.shape) == 2:
        first = (((z * 2 + y) * 2 + x) * 2 + core) * size + start
        return ref.at[pl.ds(pl.multiple_of(first, 16), count), :]
    return ref.at[z, y, x, core, pl.ds(start, count), :]


class Spread:
    def __init__(self, place, weights, counts, sems):
        self.place = place
        self.weights = weights
        self.counts = counts
        self.pieces = cut_rows(counts)
        self.z_sems, self.near_sems, self.far_sems, self.core_sems = sems
        self.order = [place.z] + place.others

    def z_copy(self, step, slot):
        p = self.place
        ref = block_ref(self.weights[slot], self.counts[slot], p.z, p.y, p.x, p.core, 0, self.counts[slot])
        sems = self.z_sems
        return remote(ref, ref, sems.at[0, step, slot], sems.at[1, step, slot], p.along_z(step), p.core)

    def near_copy(self, turn, number):
        p = self.place
        slot, start, count, way = self.pieces[number]
        ref = block_ref(self.weights[slot], self.counts[slot], self.order[turn], p.y, p.x, p.core, start, count)
        sems = self.near_sems
        return remote(
            ref, ref, sems.at[0, turn, number], sems.at[1, turn, number], (p.along_x, p.along_y)[way](), p.core
        )

    def far_copies(self, turn, number):
        p = self.place
        slot, start, count, way = self.pieces[number]
        spot = self.order[turn]
        sems = self.far_sems
        copies = []
        for part, other in enumerate((0, 1) if slot == 1 else (slice(None),)):
            y, x = (p.y, other) if way == 0 else (other, p.x)
            ref = block_ref(self.weights[slot], self.counts[slot], spot, y, x, p.core, start, count)
            sem = number + 4 * part
            to = (p.along_y, p.along_x)[way]()
            copies.append(remote(ref, ref, sems.at[0, turn, sem], sems.at[1, turn, sem], to, p.core))
        return copies

    def core_copies(self, turn, slot):
        p = self.place
        sems = self.core_sems
        copies = []
        pairs = [(y, x) for y in (0, 1) for x in (0, 1)] if slot == 1 else [(slice(None), slice(None))]
        for part, (y, x) in enumerate(pairs):
            ref = block_ref(self.weights[slot], self.counts[slot], self.order[turn], y, x, p.core, 0, self.counts[slot])
            sem = (0, 2 + part, 1)[slot]
            copies.append(remote(ref, ref, sems.at[0, turn, sem], sems.at[1, turn, sem], p.client, 1 - p.core))
        return copies

    def fill(self, master):
        p = self.place
        start = 0
        for slot in range(3):
            rows = self.counts[slot]
            own = block_ref(self.weights[slot], self.counts[slot], p.z, p.y, p.x, p.core, 0, rows)
            own[...] = master[start : start + rows, :].astype(low_type)
            start += rows

    def begin(self):
        for step in range(3):
            self.z_copy(step, 0).start()
        self.near_start(0)

    def near_start(self, slot):
        for number in (2 * slot, 2 * slot + 1):
            self.near_copy(0, number).start()

    def steps(self):
        near, far, core, start = self.near_step, self.far_step, self.core_step, self.near_start
        groups = [
            [(far, 0, 0), (start, 1)],
            [(near, 1, 0)],
            [(near, 2, 0), (near, 3, 0)],
            [(far, 1, 0), (core, 0, 0), (far, 0, 1)],
            [(far, 2, 0), (far, 3, 0), (core, 1, 0)],
            [(core, 2, 0), (core, 3, 0), (near, 1, 1), (start, 2)],
            [(core, 0, 1), (near, 2, 1)],
            [(far, 1, 1), (near, 3, 1)],
            [(core, 1, 1), (far, 2, 1), (far, 0, 2)],
            [(far, 3, 1), (core, 2, 1), (near, 1, 2)],
            [(core, 3, 1), (core, 0, 2), (near, 2, 2)],
            [(far, 1, 2), (near, 3, 2)],
            [(core, 1, 2), (far, 2, 2)],
            [(far, 3, 2), (core, 2, 2)],
            [(core, 3, 2)],
        ]
        return [[functools.partial(*step) for step in group] for group in groups]

    def near_step(self, turn, slot):
        self.z_copy(turn - 1, slot).wait_recv()
        for number in (2 * slot, 2 * slot + 1):
            self.near_copy(turn, number).start()
        if slot < 2:
            self.z_copy(turn - 1, slot + 1).start()

    def far_step(self, turn, slot):
        for number in (2 * slot, 2 * slot + 1):
            self.near_copy(turn, number).wait_recv()
            for copy in self.far_copies(turn, number):
                copy.start()

    def core_step(self, turn, slot):
        for number in (2 * slot, 2 * slot + 1):
            for copy in self.far_copies(turn, number):
                copy.wait_recv()
        for copy in self.core_copies(turn, slot):
            copy.start()

    def arrive(self, slot):
        for turn in range(4):
            for copy in self.core_copies(turn, slot):
                copy.wait_recv()

    def drain(self, slot):
        for step in range(3):
            self.z_copy(step, slot).wait_send()
        for turn in range(4):
            for copy in self.core_copies(turn, slot):
                copy.wait_send()
            for number in (2 * slot, 2 * slot + 1):
                self.near_copy(turn, number).wait_send()
                for copy in self.far_copies(turn, number):
                    copy.wait_send()


class Fold:
    def __init__(self, place, grads, counts, parts):
        self.place = place
        self.grads = grads
        self.counts = counts
        self.pieces = cut_rows(counts)
        self.core_boxes = [parts[1], parts[0], parts[1]]
        self.near_boxes, self.far_boxes, self.z_boxes = [parts[3 * k + 2 : 3 * k + 5] for k in range(3)]
        self.core_sems, self.near_sems, self.far_sems, self.z_sems = parts[11:]

    def core_copies(self, which, slot):
        p = self.place
        sems = self.core_sems
        copies = []
        pairs = [(y, x) for y in (0, 1) for x in (0, 1)] if slot == 1 else [(slice(None), slice(None))]
        for part, (y, x) in enumerate(pairs):
            ref = block_ref(self.grads[slot], self.counts[slot], which, y, x, 1 - p.core, 0, self.counts[slot])
            box = self.core_boxes[slot].at[which, y, x]
            sem = (0, 2 + part, 1)[slot]
            copies.append(remote(ref, box, sems.at[0, which, sem], sems.at[1, which, sem], p.client, 1 - p.core))
        return copies

    def near_copies(self, which, number):
        p = self.place
        slot, start, count, way = self.pieces[number]
        sems = self.near_sems
        copies = []
        for part, other in enumerate((0, 1) if slot == 1 else (slice(None),)):
            y, x = (other, 1 - p.x) if way == 0 else (1 - p.y, other)
            ref = block_ref(self.grads[slot], self.counts[slot], which, y, x, p.core, start, count)
            box = self.near_boxes[slot].at[which, other, pl.ds(start, count), :]
            sem = number + 4 * part
            to = (p.along_x, p.along_y)[way]()
            copies.append(remote(ref, box, sems.at[0, which, sem], sems.at[1, which, sem], to, p.core))
        return copies

    def far_copy(self, which, number):
        p = self.place
        slot, start, count, way = self.pieces[number]
        y, x = (1 - p.y, p.x) if way == 0 else (p.y, 1 - p.x)
        ref = block_ref(self.grads[slot], self.counts[slot], which, y, x, p.core, start, count)
        box = self.far_boxes[slot].at[which, pl.ds(start, count), :]
        sems = self.far_sems
        return remote(
            ref, box, sems.at[0, which, number], sems.at[1, which, number], (p.along_y, p.along_x)[way](), p.core
        )

    def z_copy(self, which, sender, number):
        p = self.place
        slot, start, count, _ = self.pieces[number]
        rows = pl.ds(start, count)
        sems = self.z_sems
        return remote(
            block_ref(self.grads[slot], self.counts[slot], which, p.y, p.x, p.core, start, count),
            self.z_boxes[slot].at[sender, rows, :],
            sems.at[0, which, number],
            sems.at[1, sender, number],
            p.at(which, p.y, p.x),
            p.core,
        )

    def begin(self, which, slot):
        for copy in self.core_copies(which, slot):
            copy.start()

    def add(self, slot, spots, start, count, box):
        ref = block_ref(self.grads[slot], self.counts[slot], *spots, self.place.core, start, count)
        ref[...] = (ref[...].astype(wide) + box.astype(wide)).astype(low_type)

    def core_step(self, which, slot):
        for copy in self.core_copies(which, slot):
            copy.wait_recv()
        pairs = [(y, x) for y in (0, 1) for x in (0, 1)] if slot == 1 else [(slice(None), slice(None))]
        for y, x in pairs:
            self.add(slot, (which, y, x), 0, self.counts[slot], self.core_boxes[slot][which, y, x])
        for number in (2 * slot, 2 * slot + 1):
            for copy in self.near_copies(which, number):
                copy.start()

    def near_step(self, which, slot):
        p = self.place
        for number in (2 * slot, 2 * slot + 1):
            _, start, count, way = self.pieces[number]
            for copy in self.near_copies(which, number):
                copy.wait_recv()
            for other in (0, 1) if slot == 1 else (slice(None),):
                y, x = (other, p.x) if way == 0 else (p.y, other)
                box = self.near_boxes[slot][which, other, pl.ds(start, count), :]
                self.add(slot, (which, y, x), start, count, box)
            self.far_copy(which, number).start()

    def far_step(self, which, slot):
        p = self.place
        for number in (2 * slot, 2 * slot + 1):
            _, start, count, way = self.pieces[number]
            self.far_copy(which, number).wait_recv()
            box = self.far_boxes[slot][which, pl.ds(start, count), :]
            self.add(slot, (which, p.y, p.x), start, count, box)

            @pl.when(p.z != which)
            def _():
                self.z_copy(which, p.z, number).start()

    def result(self, slot):
        p = self.place
        self.z_boxes[slot][p.z] = block_ref(self.grads[slot], self.counts[slot], p.z, p.y, p.x, p.core, 0, self.counts[slot])[...]
        for sender in range(4):

            @pl.when(p.z != sender)
            def _():
                for number in (2 * slot, 2 * slot + 1):
                    self.z_copy(sender, sender, number).wait_recv()

        total = self.z_boxes[slot][0].astype(wide)
        for sender in range(1, 4):
            total += self.z_boxes[slot][sender].astype(wide)
        return total

    def drain(self):
        for which in range(4):
            for slot in range(3):
                for copy in self.core_copies(which, slot):
                    copy.wait_send()
            for number in range(6):
                for copy in self.near_copies(which, number):
                    copy.wait_send()
                self.far_copy(which, number).wait_send()

            @pl.when(self.place.z != which)
            def _():
                for number in range(6):
                    self.z_copy(which, self.place.z, number).wait_send()
class GramSum:
    def __init__(self, place, data, total, boxes, sems):
        self.place = place
        self.data = data
        self.total = total
        self.y_box, self.z_box = boxes
        self.sems = sems
        self.share = data.shape[0] // 8
        self.down_order = place.others[::-1] + [place.z]

    def rows(self, z, y):
        return pl.ds(pl.multiple_of((z * 2 + y) * self.share, 8), self.share)

    def copy(self, number, src, dst, to):
        sems = self.sems
        return remote(src, dst, sems.at[0, number], sems.at[1, number], to, self.place.core)

    def y_down(self, turn):
        p = self.place
        src = self.data.at[self.rows(self.down_order[turn], 1 - p.y), :]
        return self.copy(turn, src, self.y_box.at[turn], p.along_y())

    def z_down(self, step):
        p = self.place
        src = self.data.at[self.rows(p.others[step], p.y), :]
        return self.copy(4 + step, src, self.z_box.at[step], p.along_z(step))

    def z_up(self, step):
        p = self.place
        ref = self.total.at[self.rows(p.z, p.y), :]
        return self.copy(7 + step, ref, ref, p.along_z(step))

    def y_up(self, turn):
        p = self.place
        ref = self.total.at[self.rows(([p.z] + p.others)[turn], p.y), :]
        return self.copy(10 + turn, ref, ref, p.along_y())

    def run(self):
        p = self.place
        for turn in range(4):
            self.y_down(turn).start()
        for turn in range(4):
            self.y_down(turn).wait_recv()
            self.data[self.rows(self.down_order[turn], p.y), :] += self.y_box[turn]
            if turn < 3:
                self.z_down(2 - turn).start()
        mine = self.rows(p.z, p.y)
        value = self.data[mine, :]
        for step in (2, 1, 0):
            self.z_down(step).wait_recv()
            value += self.z_box[step]
        self.total[mine, :] = value
        for step in range(3):
            self.z_up(step).start()
        self.y_up(0).start()
        for step in range(3):
            self.z_up(step).wait_recv()
            self.y_up(1 + step).start()
        for turn in range(4):
            self.y_up(turn).wait_recv()

    def drain(self):
        for turn in range(4):
            self.y_down(turn).wait_send()
            self.y_up(turn).wait_send()
        for step in range(3):
            self.z_down(step).wait_send()
            self.z_up(step).wait_send()


class TileSum:
    def __init__(self, place, tiles, boxes, sems):
        self.place = place
        self.tiles = tiles
        self.boxes = boxes
        self.sems = sems

    def copy(self, stage, box):
        p = self.place
        to = (p.client, p.along_x(), p.along_y()) + tuple(p.along_z(step) for step in range(3))
        core = 1 - p.core if box == 0 else p.core
        return remote(
            self.tiles.at[stage], self.boxes.at[box], self.sems.at[0, box], self.sems.at[1, box], to[box], core
        )

    def start(self):
        self.copy(0, 0).start()

    def pair(self, stage):
        self.copy(stage, stage).wait_recv()
        self.tiles[stage + 1] = self.tiles[stage] + self.boxes[stage]
        if stage < 2:
            self.copy(stage + 1, stage + 1).start()
        else:
            for step in range(3):
                self.copy(3, 3 + step).start()

    def result(self):
        for step in range(3):
            self.copy(3, 3 + step).wait_recv()
        return (self.tiles[3] + self.boxes[3]) + (self.boxes[4] + self.boxes[5])

    def drain(self):
        for stage in range(3):
            self.copy(stage, stage).wait_send()
        for step in range(3):
            self.copy(3, 3 + step).wait_send()


def halves_of(value):
    high = value.astype(low_type)
    return high, (value - high.astype(wide)).astype(low_type)


class Share:
    def __init__(self, place, sizes, buffers, sems):
        self.place = place
        self.sizes = sizes
        self.fresh, self.rows_in, self.rows_out, self.back = buffers
        self.sems = sems
        self.bounds = [0, sizes[0], sizes[0] + sizes[1], sum(sizes)]
        p = place
        self.duty = jnp.where(p.x == 1, 1, 2 * p.core)
        self.mine = p.x * 2 + p.core

    def section(self, slot):
        return pl.ds(self.bounds[slot], self.sizes[slot])

    def spot(self, slot, x, core):
        number = x if slot == 1 else x * 2 + core
        return pl.ds(pl.multiple_of(number * self.sizes[slot], 16), self.sizes[slot])

    def doer(self, slot):
        return (0, 0) if slot == 0 else (0, 1) if slot == 2 else (1, self.place.core)

    def out_copy(self, slot):
        p = self.place
        x, core = self.doer(slot)
        return remote(
            self.fresh.at[self.section(slot), :],
            self.rows_in.at[self.spot(slot, p.x, p.core), :],
            self.sems.at[0, slot],
            self.sems.at[1, self.mine],
            p.at(p.z, p.y, x),
            core,
        )

    def in_copy(self, slot, x, core):
        p = self.place
        return remote(
            self.fresh.at[self.section(slot), :],
            self.rows_in.at[self.spot(slot, x, core), :],
            self.sems.at[0, slot],
            self.sems.at[1, x * 2 + core],
            p.at(p.z, p.y, x),
            core,
        )

    def back_copy(self, slot, x, core):
        p = self.place
        return remote(
            self.rows_out.at[self.spot(slot, x, core), :],
            self.back.at[self.section(slot), :],
            self.sems.at[0, 3 + x * 2 + core],
            self.sems.at[1, 4 + slot],
            p.at(p.z, p.y, x),
            core,
        )

    def users(self, slot):
        p = self.place
        if slot == 1:
            return [(0, p.core), (1, p.core)]
        return [(x, core) for x in (0, 1) for core in (0, 1)]

    def send(self, slot):
        @pl.when(self.duty != slot)
        def _():
            self.out_copy(slot).start()

        @pl.when(self.duty == slot)
        def _():
            self.rows_in[self.spot(slot, self.place.x, self.place.core), :] = self.fresh[self.section(slot), :]

    def gather(self):
        p = self.place
        for slot in range(3):

            @pl.when(self.duty == slot)
            def _():
                for x, core in self.users(slot):

                    @pl.when((p.x != x) | (p.core != core))
                    def _():
                        self.in_copy(slot, x, core).wait_recv()

    def give_back(self):
        p = self.place
        for slot in range(3):

            @pl.when(self.duty == slot)
            def _():
                for x, core in self.users(slot):

                    @pl.when((p.x != x) | (p.core != core))
                    def _():
                        self.back_copy(slot, x, core).start()

                self.back[self.section(slot), :] = self.rows_out[self.spot(slot, p.x, p.core), :]

    def finish(self):
        p = self.place
        for slot in range(3):

            @pl.when(self.duty != slot)
            def _():
                self.back_copy(slot, p.x, p.core).wait_recv()
                self.out_copy(slot).wait_send()

            @pl.when(self.duty == slot)
            def _():
                for x, core in self.users(slot):

                    @pl.when((p.x != x) | (p.core != core))
                    def _():
                        self.back_copy(slot, x, core).wait_send()


def corner_spot(number, part):
    row, column = number // 2, number % 2
    return slice(row * part, (row + 1) * part), slice(column * part, (column + 1) * part)


def orthogonal(place, ratios, share, share_sems, gram, gram_total, mate_gram, gram_sum, squares, rows_in, low_rows):
    grams, mixed, once = squares
    count, width = rows_in.shape
    part = width // CUTS
    corners = [(row, column) for row in range(CUTS) for column in range(row, CUTS)]
    right_high, right_low = [low_rows.at[pl.ds(count + spot * width, width), :] for spot in range(2)]

    def set_right(value_ref):
        for start in range(0, width, part):
            rows = slice(start, start + part)
            right_high[rows, :], right_low[rows, :] = halves_of(value_ref[rows, :])

    def times_right(value):
        high, low = halves_of(value)
        left = jnp.concatenate([high, high, low], axis=1)
        right = jnp.concatenate([right_high[...], right_low[...], right_high[...]], axis=0)
        return dot_nn(left, right)

    middle = width // 2

    def times_right_even(value, more=()):
        high, low = halves_of(value)
        left = jnp.concatenate([high, high, low], axis=1)
        right = jnp.concatenate([right_high[...], right_low[...], right_high[...]], axis=0)
        upper = left[:middle]
        for rows in more:
            high, low = halves_of(rows)
            upper = jnp.concatenate([upper, jnp.concatenate([high, high, low], axis=1)], axis=0)
        upper = dot_nn(upper, right)
        corner = dot_nn(left[middle:], right[:, middle:])
        lower = jnp.concatenate([upper[:middle, middle:].T, corner], axis=1)
        return jnp.concatenate([upper[:middle], lower], axis=0), upper[middle:]

    share.gather()
    high, low = halves_of(rows_in[...])
    left = jnp.concatenate([high, high, low], axis=0)
    right = jnp.concatenate([high, low, high], axis=0)
    for row in range(CUTS):
        strip = dot_tn(left[:, row * part : (row + 1) * part], right[:, row * part :])
        for column in range(row, CUTS):
            gram[corner_spot(corners.index((row, column)), part)] = strip[
                :, (column - row) * part : (column - row + 1) * part
            ]

    @pl.when(place.x == 1)
    def _():
        swap = remote(gram, mate_gram, share_sems.at[0, 7], share_sems.at[1, 7], place.client, 1 - place.core)
        swap.start()
        swap.wait()
        gram[...] += mate_gram[...]

    gram_sum.run()
    spots = lax.broadcasted_iota(jnp.int32, (part, part), 0)
    diagonal = spots == lax.broadcasted_iota(jnp.int32, (part, part), 1)
    trace = 0.0
    for number, (row, column) in enumerate(corners):
        if row == column:
            trace += jnp.sum(jnp.where(diagonal, gram_total[corner_spot(number, part)], 0.0))
    factor = 1.0 / (jnp.sqrt(trace) + 1e-07)
    square = factor * factor
    for number, (row, column) in enumerate(corners):
        rows, columns = slice(row * part, (row + 1) * part), slice(column * part, (column + 1) * part)
        block = gram_total[corner_spot(number, part)] * square
        grams[rows, columns] = block
        if row < column:
            grams[columns, rows] = block.T
    rows_in[...] = rows_in[...] * factor

    def turn(number, carry):
        set_right(grams)
        mixed[...] = schulz_second * grams[...] + schulz_third * times_right_even(grams[...])[0]
        set_right(mixed)

        @pl.when(number < NS_STEPS - 1)
        def _():
            product, moved = times_right_even(grams[...], (rows_in[...],))
            once[...] = schulz_first * grams[...] + product
            rows_in[...] = schulz_first * rows_in[...] + moved
            grams[...] = schulz_first * once[...] + times_right_even(once[...])[0]

        @pl.when(number == NS_STEPS - 1)
        def _():
            rows_in[...] = schulz_first * rows_in[...] + times_right(rows_in[...])

        return carry

    lax.fori_loop(0, NS_STEPS, turn, 0)
    ratio = jnp.where(share.duty == 1, ratios[1], ratios[0])
    low_rows[0:count, :] = (rows_in[...] * ratio).astype(low_type)
    share.give_back()


def update_kernel(loss_tile, master, fresh_momentum, ortho, *rest):
    norms, grad_norm, heads, grad_head, outs = rest[0:3], rest[3], rest[4:7], rest[7], rest[8:]
    loss_out, *outs = outs
    loss_out[0] = loss_tile[0, 0]
    loss_out[1] = loss_tile[0, 1]
    momentum_out, base_out, low_out = outs[0:3]
    held = master[...]
    momentum_out[...] = fresh_momentum[...]
    fresh = held - muon_rate * (ortho[...].astype(wide) + muon_decay * held)
    base_out[...] = fresh
    low_out[...] = fresh.astype(low_type)
    for targets, values, grad, rate, decay in (
        (outs[3:6], norms, grad_norm, norm_rate, 0.0),
        (outs[6:9], heads, grad_head, head_rate, head_decay),
    ):
        updates = adam_update(values[0][...], grad[...], values[1][...], values[2][...], rate, decay)
        for target, value in zip(targets, updates):
            target[...] = value


def update_pass(loss_tile, master, fresh_momentum, ortho, norms, grad_norm, heads, grad_head):
    vmem = pl.BlockSpec(memory_space=pltpu.VMEM)
    smem = pl.BlockSpec(memory_space=pltpu.SMEM)
    operands = [loss_tile, master, fresh_momentum, ortho, *norms, grad_norm, *heads, grad_head]
    outs = [(2,), master.shape, master.shape, master.shape] + [grad_norm.shape] * 3 + [grad_head.shape] * 3
    types = [wide, wide, wide, low_type] + [wide] * 6
    return pl.pallas_call(
        update_kernel,
        out_shape=[jax.ShapeDtypeStruct(shape, kind) for shape, kind in zip(outs, types)],
        in_specs=[smem] + [vmem] * (len(operands) - 1),
        out_specs=[smem] + [vmem] * (len(outs) - 1),
        compiler_params=pltpu.CompilerParams(vmem_limit_bytes=VMEM_BYTES),
    )(*operands)


def norm_stats(mine, theirs, count):
    gap = mine[0:1] - theirs[0:1]
    mean = 0.5 * (mine[0:1] + theirs[0:1])
    spread = mine[1:2] + theirs[1:2] + gap * gap * (0.5 * count)
    return mean, lax.rsqrt(spread / (2.0 * count) + norm_epsilon)


def client_kernel(
    gather,
    ratios,
    images,
    classes,
    features,
    labels,
    flag,
    params,
    head,
    *rest,
):
    if gather:
        master, momentum, anchor, *rest = rest
    else:
        first_in, middle_in, last_in, *rest = rest
    if gather:
        fresh_out, ortho_out, *rest = rest
    else:
        grads_out, rest = rest[:3], rest[3:]
    (
        grad_norm_out,
        grad_head_out,
        loss_out,
        x_all,
        mid_wide,
        w_first,
        w_middle,
        w_last,
        act_one,
        act_two,
        act_three,
        taps_one,
        taps_two,
        hidden_two,
        stage,
        params_all,
        head_all,
        grad_pool,
        pool_send,
        pool_all,
        logit_grads,
        sums_mine,
        sums_theirs,
        shift,
        fwd_stats,
        sem_local,
        sem_swap,
        sem_misc,
        *near_parts,
    ) = rest
    place = Place()
    core = place.core
    mate = (place.client, 1 - core)
    count_rows, channels = x_all.shape
    half = channels // 2
    width = act_one.shape[1]
    part = width // 2
    mine_images = images // 2
    line = SIDE * mine_images
    total_rows = 2.0 * count_rows

    def tile(index):
        return pl.ds(pl.multiple_of(index * line, line), line)

    def lanes(index, size):
        return pl.ds(pl.multiple_of(index * size, size), size)

    weights = (w_first, w_middle, w_last)
    if gather:
        held = act_three.at[pl.ds(0, master.shape[0]), pl.ds(0, width)]
        load = pltpu.make_async_copy(master, held, sem_local.at[8])
        load.start()
        counts = [channels // 32, 9 * width // 32, channels // 32]
        spread = Spread(place, weights, counts, near_parts[:4])
        fold = Fold(place, (w_first, mid_wide, w_last), counts, near_parts[4:19])
        rows_in, back, tiles, tile_boxes, gram_total, y_box, z_box, mate_gram = near_parts[19:27]
        tile_sems, share_sems, gram_sems = near_parts[27:]
        block_rows = master.shape[0]
        side_space = pl.ds(half, width)
        held_base, held_momentum, held_anchor, fresh = [
            act_three.at[pl.ds(number * block_rows, block_rows), side_space] for number in range(4)
        ]
        rows_in[...] = jnp.zeros_like(rows_in)
        share = Share(place, counts, (fresh, rows_in, hidden_two, back), share_sems)
        tile_sum = TileSum(place, tiles, tile_boxes, tile_sems)
        due = spread.steps()
        load.wait()
        spread.fill(held)
        place.greet(True, True)
        spread.begin()
    else:
        place.greet(False)
        loads = [
            pltpu.make_async_copy(src, dst, sem_local.at[8 + slot])
            for slot, (src, dst) in enumerate(zip((first_in, middle_in, last_in), weights))
        ]
        for load in loads:
            load.start()
        due = []

    quarter = half // 2
    own_rows = pl.ds(pl.multiple_of(core * count_rows, count_rows), count_rows)
    mate_rows = pl.ds(pl.multiple_of((1 - core) * count_rows, count_rows), count_rows)
    top_rows = pl.ds(0, count_rows)
    own_copies = [
        pltpu.make_async_copy(
            features.at[own_rows, pl.ds(side * quarter, quarter)], buffer, sem_local.at[side]
        )
        for side, buffer in enumerate((hidden_two, mid_wide.at[top_rows, :]))
    ]
    feature_copies = []
    for side, buffer in enumerate((taps_one, taps_two)):
        feature_copies.append(
            remote(
                features.at[mate_rows, pl.ds(side * quarter, quarter)],
                buffer.at[top_rows, :],
                sem_misc.at[0, 5 + side],
                sem_misc.at[1, 5 + side],
                *mate,
            )
        )
    for copy in feature_copies + own_copies:
        copy.start()
    per_kind = params.shape[0] // 2
    for kind in range(2):
        rows = [params[kind * per_kind + spot : kind * per_kind + spot + 1, :] for spot in range(per_kind)]
        params_all[core, kind : kind + 1, :] = jnp.concatenate(rows, axis=1)
    head_all[core] = jnp.zeros(head_all.shape[1:], low_type)
    for spot in range(half // LANES):
        head_all[core, 0:classes, spot * LANES : (spot + 1) * LANES] = head[
            pl.ds(spot, classes, stride=half // LANES), :
        ].astype(low_type)
    to_mate = [
        remote(params_all.at[core], params_all.at[core], sem_misc.at[0, 0], sem_misc.at[1, 0], *mate),
        remote(head_all.at[core], head_all.at[core], sem_misc.at[0, 1], sem_misc.at[1, 1], *mate),
    ]
    for copy in to_mate:
        copy.start()
    to_mate += feature_copies

    def advance(count):
        for group in due[:count]:
            for step in group:
                step()
        del due[:count]

    def advance_at(index, spots):
        for spot, group in zip(spots, due):

            @pl.when(index == spot)
            def _():
                for step in group:
                    step()

    def arrive(slot, left):
        if gather:
            advance(len(due) - left)
            spread.arrive(slot)
        else:
            loads[slot].wait()

    def arrive_turns(slot, turns):
        if gather:
            for turn in turns:
                for copy in spread.core_copies(turn, slot):
                    copy.wait_recv()

    def fold_step(kind, slot, which):
        if gather:
            (fold.core_step, fold.near_step, fold.far_step)[kind](which, slot)

    def fold_at(index, spot, *steps):
        @pl.when(index == spot)
        def _():
            for step in steps:
                fold_step(*step)

    def fold_begin(which, slot):
        if gather:
            fold.begin(which, slot)

    def zero_edges(buffer):
        edge = jnp.zeros((line,) + buffer.shape[1:], low_type)
        buffer[0:line, :] = edge
        buffer[line + count_rows : 2 * line + count_rows, :] = edge

    advance(3)
    for copy in own_copies:
        copy.wait()

    def turn_from(source, base):
        def turn(index, carry):
            stage[...] = source(lanes(index, LANES)).astype(wide)

            def pixel(spot, inner):
                x_all[
                    pl.ds(pl.multiple_of(spot * mine_images, mine_images), mine_images),
                    pl.ds(pl.multiple_of(base + index * LANES, LANES), LANES),
                ] = stage[pl.ds(spot, mine_images, stride=PIXELS), :].astype(low_type)
                return inner

            return lax.fori_loop(0, PIXELS, pixel, carry, unroll=7)

        return turn

    quarters = quarter // LANES
    own_base, mate_base = core * half, (1 - core) * half
    lax.fori_loop(0, quarters, turn_from(lambda columns: hidden_two[:, columns], own_base), 0)
    advance(1)
    lax.fori_loop(
        0,
        quarters,
        turn_from(lambda columns: mid_wide[0:count_rows, columns], own_base + quarter),
        0,
    )
    advance(1)
    for copy in to_mate:
        copy.wait_recv()
    lax.fori_loop(0, quarters, turn_from(lambda columns: taps_one[0:count_rows, columns], mate_base), 0)
    advance(1)
    lax.fori_loop(0, quarters, turn_from(lambda columns: taps_two[0:count_rows, columns], mate_base + quarter), 0)
    zero_edges(taps_one)
    zero_edges(taps_two)
    arrive(0, 9)

    def swap(slot, size):
        return remote(
            sums_mine.at[slot, :, pl.ds(0, size)],
            sums_theirs.at[slot, :, pl.ds(0, size)],
            sem_swap.at[0, slot],
            sem_swap.at[1, slot],
            *mate,
        )

    def gain_bias(lower, upper):
        rows = []
        for kind in range(2):
            pieces = [params_all[side, kind : kind + 1, lower:upper] for side in range(2)]
            rows.append(jnp.concatenate(pieces, axis=1))
        return rows

    def collect(index, value, columns, size):
        @pl.when(index == 0)
        def _():
            shift[0:1, pl.ds(0, size)] = column_sum(fold_rows(value)) / value.shape[0]
            shift[8:24, pl.ds(0, size)] = jnp.zeros((16, size), wide)

        gap = value - shift[0:1, pl.ds(0, size)]
        shift[8:16, pl.ds(0, size)] += fold_rows(gap)
        shift[16:24, pl.ds(0, size)] += fold_rows(gap * gap)

    def close_stats(slot, columns, size):
        sum_gap = column_sum(shift[8:16, pl.ds(0, size)])
        sum_square = column_sum(shift[16:24, pl.ds(0, size)])
        sums_mine[slot, 0:1, columns] = shift[0:1, pl.ds(0, size)] + sum_gap / count_rows
        sums_mine[slot, 1:2, columns] = sum_square - sum_gap * sum_gap / count_rows

    def look_over(act, columns):
        def look(index, carry):
            collect(index, act[tile(index), columns], None, width)
            return carry

        lax.fori_loop(0, SIDE, look, 0)

    groups = SPOTS[0]
    group = channels // groups

    def settle(slot, size):
        mean, scale = norm_stats(
            sums_mine[slot, 0:2, pl.ds(0, size)], sums_theirs[slot, 0:2, pl.ds(0, size)], float(count_rows)
        )
        fwd_stats[slot, 0:1, pl.ds(0, size)] = mean
        fwd_stats[slot, 1:2, pl.ds(0, size)] = scale

    whole_width = pl.ds(0, width)

    def first_part(index, carry):
        act_one[...] += dot_nn(x_all[:, lanes(index, group)], flat_rows(w_first[index]))
        advance_at(index, (0, 1, 2))
        return carry

    act_one[...] = jnp.zeros_like(act_one)
    lax.fori_loop(0, groups, first_part, 0)
    del due[:3]
    look_over(act_one, whole_width)
    close_stats(0, whole_width, width)
    move = swap(0, width)
    move.start()
    advance(1)
    move.wait()
    settle(0, width)

    gain_one, bias_one = gain_bias(0, part)
    gain_two, bias_two = gain_bias(part, width)
    gain_three, bias_three = gain_bias(width, width + half)

    def normal(act, slot, index):
        mean = fwd_stats[slot, 0:1, pl.ds(0, width)]
        return (act[tile(index), :] - mean) * fwd_stats[slot, 1:2, pl.ds(0, width)]

    def hide_one(index, carry):
        value = normal(act_one, 0, index) * gain_one + bias_one
        taps_one[pl.ds(pl.multiple_of((index + 1) * line, line), line), :] = (value * sigmoid(value)).astype(low_type)
        return carry

    lax.fori_loop(0, SIDE, hide_one, 0)
    if gather:
        arrive_turns(1, (0, 1))
    else:
        arrive(1, 0)

    step = mine_images
    piece = width // 2

    def row_windows(buffer, down, start, reach):
        if reach == line:
            return buffer[pl.ds(pl.multiple_of(down * line, line), count_rows), :]
        windows = [
            buffer[pl.ds(pl.multiple_of((down + row) * line + start, step), reach), :] for row in range(SIDE)
        ]
        return jnp.concatenate(windows, axis=0)

    def add_windows(target, columns, value, start, reach):
        for row in range(SIDE):
            rows = slice(row * line + start, row * line + start + reach)
            target[rows, columns] += value[row * reach : (row + 1) * reach]

    low_start, high_start, reaches = (0, 0, step), (step, 0, 0), (line - step, line, line - step)

    early, taps = 4, 9

    def second_part(index, carry):
        tap = jnp.where(place.z < 2, index, (index + taps - early) % taps) if gather else index

        @pl.when(index == early)
        def _():
            arrive_turns(1, (2, 3))

        down = tap // 3
        for over in range(3):

            @pl.when(tap % 3 == over)
            def _():
                left = row_windows(taps_one, down, low_start[over], reaches[over])
                kernel = w_middle[pl.ds(pl.multiple_of(tap * width, width), width), :]
                add_windows(act_two, slice(None), dot_nn(left, kernel), high_start[over], reaches[over])

        advance_at(index, (2, 5, 6, 8))
        return carry

    act_two[...] = jnp.zeros_like(act_two)
    lax.fori_loop(0, taps, second_part, 0)
    del due[:4]
    look_over(act_two, whole_width)
    close_stats(1, whole_width, width)
    move_two = swap(1, width)
    move_two.start()
    arrive(2, 0)
    if gather:
        spread.drain(0)

    def turn_weights(which, carry):
        w_first[which] = jnp.transpose(flat_rows(w_last[which])).reshape(w_first.shape[1:])
        return carry

    lax.fori_loop(0, groups, turn_weights, 0)
    move_two.wait()
    settle(1, width)

    tall = count_rows // 2

    def third_tile(index, carry):
        rows = pl.ds(pl.multiple_of(index * tall, 16), tall)
        act = act_two[rows, :]
        normed = (act - fwd_stats[1, 0:1, whole_width]) * fwd_stats[1, 1:2, whole_width]
        value = normed * gain_two + bias_two
        hidden = (value * sigmoid(value)).astype(low_type)
        hidden_two[rows, :] = hidden
        for which in range(groups):
            columns = slice(which * group, (which + 1) * group)
            value = dot_nn(hidden, flat_rows(w_first[which]))
            act_three[rows, columns] = value
            start = jnp.where(index == 0, column_sum(value[0:8]) / 8.0, shift[0:1, columns])
            gap = value - start
            kept_sums = jnp.where(index == 0, 0.0, shift[8:24, columns])
            shift[0:1, columns] = start
            shift[8:16, columns] = kept_sums[0:8] + fold_rows(gap)
            shift[16:24, columns] = kept_sums[8:16] + fold_rows(gap * gap)
        return carry

    lax.fori_loop(0, 2, third_tile, 0)
    close_stats(2, pl.ds(0, channels), channels)
    move_three = swap(2, channels)
    move_three.start()
    move_three.wait()
    settle(2, channels)

    per_group = group // LANES

    def block_of(spot):
        return pl.ds(pl.multiple_of(spot * mine_images, mine_images), mine_images)

    def mid_line(which, index):
        return pl.ds(pl.multiple_of(which * count_rows + index * line, line), line)

    kept = channels // LANES * mine_images

    def gathered(kind):
        starts = range(kind * kept, (kind + 1) * kept, mine_images)
        return jnp.concatenate([stage[start : start + mine_images, :] for start in starts], axis=1)

    fwd_stats[2, 4:5, :] = fwd_stats[2, 1:2, :] * gain_three
    fwd_stats[2, 5:6, :] = bias_three - fwd_stats[2, 0:1, :] * fwd_stats[2, 4:5, :]

    def emit(index, carry):
        columns = lanes(index, LANES)
        slant, level = fwd_stats[2, 4:5, columns], fwd_stats[2, 5:6, columns]

        def pixels(row, sums):
            pooled, steeps, steeps_act = sums
            found = []
            for spot in range(SIDE):
                where = block_of(row * SIDE + spot)
                act = act_three[where, columns]
                half_total = 0.5 * (act * slant + level + x_all[where, columns].astype(wide))
                rise = 1.0 + jnp.tanh(half_total)
                out = half_total * rise
                steep = rise + out * (2.0 - rise)
                found.append(steep.astype(low_type))
                pooled, steeps, steeps_act = pooled + out, steeps + steep, steeps_act + steep * act
            mid_wide[mid_line(index // per_group, row), lanes(index % per_group, LANES)] = jnp.concatenate(
                found, axis=0
            )
            return pooled, steeps, steeps_act

        zero = jnp.zeros((mine_images, LANES), wide)
        sums = lax.fori_loop(0, SIDE, pixels, (zero, zero, zero))
        for kind, value in enumerate(sums):
            stage[pl.ds(pl.multiple_of(kind * kept + index * mine_images, mine_images), mine_images), :] = value
        return carry

    lax.fori_loop(0, channels // LANES, emit, 0)

    pooled = (gathered(0) / PIXELS).astype(low_type)
    head_full = jnp.concatenate([head_all[0], head_all[1]], axis=1)
    logits = dot_nt(head_full, pooled)
    spots = lax.broadcasted_iota(jnp.int32, logits.shape, 0)
    inside = spots < classes
    first_labels, second_labels = labels[0:1, 0:mine_images], labels[0:1, mine_images:]
    onehot = (spots == jnp.where(core == 0, first_labels, second_labels)).astype(wide)
    top = jnp.max(jnp.where(inside, logits, -jnp.inf), axis=0, keepdims=True)
    powers = jnp.where(inside, jnp.exp(logits - top), 0.0)
    power_sum = jnp.sum(powers, axis=0, keepdims=True)
    picked = jnp.sum(logits * onehot, axis=0, keepdims=True)
    each_loss = top + jnp.log(power_sum) - picked
    taking = flag[0].astype(wide)
    tile_spots = lax.broadcasted_iota(jnp.int32, loss_out.shape, 1)
    loss_out[...] = jnp.where(tile_spots == 0, taking * jnp.sum(each_loss), taking * mine_images)
    grads = (taking / images * (powers / power_sum - onehot)).astype(low_type)
    grad_pool[...] = dot_tn(grads, head_full) * (0.5 / PIXELS)
    logit_grads[core] = grads
    pool_all[core] = pooled[:, 0:half]
    pool_send[...] = pooled[:, half:]

    @pl.when(core == 1)
    def _():
        pool_all[core] = pooled[:, half:]
        pool_send[...] = pooled[:, 0:half]

    head_moves = [
        remote(pool_send, pool_all.at[core], sem_misc.at[0, 3], sem_misc.at[1, 3], *mate),
        remote(logit_grads.at[core], logit_grads.at[core], sem_misc.at[0, 4], sem_misc.at[1, 4], *mate),
    ]

    steeps = gathered(1)
    steeps_normed = (gathered(2) - fwd_stats[2, 0:1, :] * steeps) * fwd_stats[2, 1:2, :]
    sums_mine[3, 0:1, :] = column_sum(grad_pool[...] * steeps)
    sums_mine[3, 1:2, :] = column_sum(grad_pool[...] * steeps_normed)
    move_back = swap(3, channels)
    move_back.start()
    for copy in head_moves:
        copy.start()
    move_back.wait()

    def back_terms(slot, layer, size, gain):
        columns = pl.ds(0, size)
        sums = sums_mine[slot, 0:2, columns] + sums_theirs[slot, 0:2, columns]
        sums_mine[slot, 2:4, columns] = sums
        scale = fwd_stats[layer, 1:2, columns]
        return (
            scale * gain,
            scale * gain * sums[0:1] / total_rows,
            scale * scale * gain * sums[1:2] / total_rows,
        )

    first, second, third = back_terms(3, 2, channels, gain_three)
    fwd_stats[2, 4:5, :] = second - third * fwd_stats[2, 0:1, :]
    fwd_stats[2, 5:6, :] = third
    grad_pool[...] = grad_pool[...] * first

    def pull(index):
        for which in range(groups):
            columns = slice(which * group, (which + 1) * group)
            reach = grad_pool[:, columns]
            steep = mid_wide[mid_line(which, index), :].astype(wide)
            value = jnp.concatenate([reach] * SIDE, axis=0) * steep
            value = value - fwd_stats[2, 4:5, columns] - fwd_stats[2, 5:6, columns] * act_three[tile(index), columns]
            mid_wide[mid_line(which, index), :] = value.astype(low_type)

    pull(0)

    def drop_into(act, slot, gain, bias, columns):
        size = pl.ds(0, width)
        shift[8:24, size] = jnp.zeros((16, width), wide)

        def drop(index, carry):
            normed = normal(act, slot, index)
            norm = normed * gain + bias
            sig = sigmoid(norm)
            grad = act_three[tile(index), columns] * (sig + norm * sig * (1.0 - sig))
            act_three[tile(index), columns] = grad
            shift[8:16, size] += fold_rows(grad)
            shift[16:24, size] += fold_rows(grad * normed)
            return carry

        lax.fori_loop(0, SIDE, drop, 0)

    def close_back(slot):
        size = pl.ds(0, width)
        sums_mine[slot, 0:1, size] = column_sum(shift[8:16, size])
        sums_mine[slot, 1:2, size] = column_sum(shift[16:24, size])

    space_two, space_one = pl.ds(0, width), pl.ds(width, width)

    def mid_group(which):
        return mid_wide[pl.ds(pl.multiple_of(which * count_rows, count_rows), count_rows), :]

    def back_two(first, lines):
        def rows_from(base):
            return pl.ds(pl.multiple_of(base + first * line, line), lines * line)

        left = jnp.concatenate([mid_wide[rows_from(which * count_rows), :] for which in range(groups)], axis=1)
        value = dot_nn(left, flat_rows(w_last[...]))
        normed = (act_two[rows_from(0), :] - fwd_stats[1, 0:1, whole_width]) * fwd_stats[1, 1:2, whole_width]
        norm = normed * gain_two + bias_two
        sig = sigmoid(norm)
        grad = value * (sig + norm * sig * (1.0 - sig))
        act_three[rows_from(0), space_two] = grad
        size = pl.ds(0, width)
        shift[8:16, size] += fold_rows(grad)
        shift[16:24, size] += fold_rows(grad * normed)

    pairs = (SIDE - 1) // 2

    def back_two_loop(index, carry):
        pull(2 * index + 2)
        pull(2 * index + 3)
        back_two(2 * index, 2)
        return carry

    shift[8:24, :] = jnp.zeros((16, channels), wide)
    pull(1)
    lax.fori_loop(0, pairs - 1, back_two_loop, 0)
    pull(SIDE - 1)
    back_two(SIDE - 3, 2)
    back_two(SIDE - 1, 1)
    close_back(4)
    move_back_two = swap(4, width)
    move_back_two.start()
    if gather:
        base_loads = [
            pltpu.make_async_copy(src, dst, sem_local.at[1 + number])
            for number, (src, dst) in enumerate(
                ((master, held_base), (momentum, held_momentum), (anchor, held_anchor))
            )
        ]
        for load in base_loads:
            load.start()
        tiles[0] = loss_out[...]
        tile_sum.start()

    def settle_section(slot):
        if gather:
            rows = share.section(slot)
            grad = fold.result(slot) + prox_weight * (held_base[rows, :] - held_anchor[rows, :])
            fresh[rows, :] = momentum_decay * held_momentum[rows, :] + grad
            share.send(slot)

    if gather:
        spread.drain(1)
        spread.drain(2)

    def put(ref, which, value):
        ref[which] = value.astype(low_type).reshape(ref.shape[1:])

    def expand_group(which, carry):
        put(w_last, which, dot_tn(mid_group(which), hidden_two[...]))
        fold_begin(which, 2)
        fold_at(which, 2, (0, 2, 0))
        fold_at(which, 3, (0, 2, 1))
        return carry

    lax.fori_loop(0, groups, expand_group, 0)
    move_back_two.wait()
    terms_two = back_terms(4, 1, width, gain_two)

    def back_act(terms, act, layer, index, columns):
        first, second, third = terms
        gap = act[tile(index), :] - fwd_stats[layer, 0:1, pl.ds(0, width)]
        return (first * act_three[tile(index), columns] - second - third * gap).astype(low_type)

    def grad_two(index, carry):
        taps_two[pl.ds(pl.multiple_of((index + 1) * line, line), line), :] = back_act(
            terms_two, act_two, 1, index, space_two
        )
        return carry

    lax.fori_loop(0, SIDE, grad_two, 0)
    fold_step(0, 2, 2)
    fold_step(1, 2, 0)
    core_step, near_step, far_step = 0, 1, 2
    plan = {
        0: [(core_step, 2, 3)],
        1: [(near_step, 2, 1)],
        2: [(far_step, 2, 0), (near_step, 2, 2)],
        3: [(far_step, 2, 1), (near_step, 2, 3)],
        4: [(far_step, 2, 2)],
        5: [(far_step, 2, 3), (core_step, 1, 0)],
        7: [(core_step, 1, 1)],
    }

    def middle_row(down, carry):
        for over in range(3):
            left = row_windows(taps_one, down, low_start[over], reaches[over])
            right = row_windows(taps_two, 1, high_start[over], reaches[over])
            rows = pl.ds(pl.multiple_of((3 * down + over) * width, width), width)
            mid_wide[rows, :] = dot_tn(left, right).astype(low_type)
            for row in range(3):
                tap = 3 * row + over

                @pl.when(down == row)
                def _():
                    if tap >= 2 and tap % 2 == 0:
                        fold_begin(tap // 2 - 1, 1)
                    for step in plan.get(tap, ()):
                        fold_step(*step)

        return carry

    lax.fori_loop(0, 3, middle_row, 0)
    for copy in head_moves:
        copy.wait_recv()
    head_grad = dot_nn(logit_grads[0], pool_all[0]) + dot_nn(logit_grads[1], pool_all[1])
    for spot in range(half // LANES):
        stage[pl.ds(spot, classes, stride=half // LANES), :] = head_grad[
            0:classes, spot * LANES : (spot + 1) * LANES
        ]
    head_space = stage.at[pl.ds(0, grad_head_out.shape[0]), :]
    head_leave = pltpu.make_async_copy(head_space, grad_head_out, sem_local.at[0])
    head_leave.start()
    if gather:
        tile_sum.pair(0)
        for load in base_loads:
            load.wait()

    def back_one(index, carry):
        down, side = index // 2, index % 2
        columns = lanes(2 + side, piece)
        for over in range(3):
            left = row_windows(taps_two, 2 - down, high_start[over], reaches[over])
            start = pl.multiple_of((3 * down + over) * width + side * piece, piece)
            value = dot_nt(left, w_middle[pl.ds(start, piece), :])
            add_windows(act_three, columns, value, low_start[over], reaches[over])
        fold_at(index, 0, (core_step, 1, 2), (near_step, 1, 0))
        fold_at(index, 1, (core_step, 1, 3))
        fold_at(index, 2, (near_step, 1, 1), (far_step, 1, 0))
        fold_at(index, 4, (far_step, 1, 1))
        fold_at(index, 5, (near_step, 1, 2))
        return carry

    act_three[:, space_one] = jnp.zeros((count_rows, width), wide)
    lax.fori_loop(0, 6, back_one, 0)
    drop_into(act_one, 0, gain_one, bias_one, space_one)
    fold_step(near_step, 1, 3)
    settle_section(2)
    close_back(5)
    move_back_one = swap(5, width)
    move_back_one.start()

    move_back_one.wait()
    terms_one = back_terms(5, 0, width, gain_one)

    def grad_one(index, carry):
        hidden_two[tile(index), :] = back_act(terms_one, act_one, 0, index, space_one)
        return carry

    lax.fori_loop(0, SIDE, grad_one, 0)
    fold_step(far_step, 1, 2)
    if gather:
        tile_sum.pair(1)

    def reduce_group(which, carry):
        put(w_first, which, dot_tn(x_all[:, lanes(which, group)], hidden_two[...]))
        fold_begin(which, 0)
        fold_at(which, 0, (far_step, 1, 3))
        fold_at(which, 2, (core_step, 0, 0))
        fold_at(which, 3, (core_step, 0, 1), (near_step, 0, 0))
        return carry

    lax.fori_loop(0, groups, reduce_group, 0)

    for kind in range(2):
        row = 3 - kind
        pieces = [
            sums_mine[5, row : row + 1, lanes(core, part)],
            sums_mine[4, row : row + 1, lanes(core, part)],
            sums_mine[3, row : row + 1, lanes(core, half)],
        ]
        whole = jnp.concatenate(pieces, axis=1)
        per_kind = whole.shape[1] // LANES
        for spot in range(per_kind):
            grad_norm_out[kind * per_kind + spot : kind * per_kind + spot + 1, :] = whole[
                :, spot * LANES : (spot + 1) * LANES
            ]
    for step in (
        (core_step, 0, 2),
        (core_step, 0, 3),
        (far_step, 0, 0),
        (near_step, 0, 1),
        (near_step, 0, 2),
        (far_step, 0, 1),
        (near_step, 0, 3),
        (far_step, 0, 2),
        (far_step, 0, 3),
    ):
        fold_step(*step)
        if step == (far_step, 0, 0):
            settle_section(1)
    if gather:
        settle_section(0)
        leave = pltpu.make_async_copy(fresh, fresh_out, sem_local.at[1])
        leave.start()
        tile_sum.pair(2)
        part = width // CUTS
        gram = act_three.at[pl.ds(0, gram_total.shape[0]), pl.ds(half + width, 2 * part)]
        corner_rows = pl.ds(gram_total.shape[0], width)
        squares = [act_three.at[corner_rows, pl.ds(spot * width, width)] for spot in (0, 1, 3)]
        gram_sum = GramSum(place, gram, gram_total, (y_box, z_box), gram_sems)
        orthogonal(place, ratios, share, share_sems, gram, gram_total, mate_gram, gram_sum, squares, rows_in, hidden_two)
        share.finish()
        loss_out[...] = tile_sum.result()
        ortho_leave = pltpu.make_async_copy(back, ortho_out, sem_local.at[2])
        ortho_leave.start()
        gram_sum.drain()
        tile_sum.drain()
        fold.drain()
        leave.wait()
        ortho_leave.wait()
    else:
        outs = [
            pltpu.make_async_copy(ref, out, sem_local.at[slot])
            for slot, (ref, out) in enumerate(zip((w_first, mid_wide.at[pl.ds(0, 9 * width), :], w_last), grads_out))
        ]
        for copy in outs:
            copy.start()
        for copy in outs:
            copy.wait()
    head_leave.wait()
    for copy in to_mate + head_moves:
        copy.wait_send()


def client_pass(gather, ratios, classes, features, labels, flag, params, head, weights):
    pixels, half = features.shape
    images = labels.shape[1]
    count_rows, channels = pixels // 2, 2 * half
    width = params.shape[0] // 2 * LANES - half
    head_rows = classes + -classes % 16
    mine_images = images // 2
    line = SIDE * mine_images
    middle = 9 * width
    blocks = 32
    group = channels // SPOTS[0]
    vmem = pl.BlockSpec(memory_space=pltpu.VMEM)
    smem = pl.BlockSpec(memory_space=pltpu.SMEM)
    spots = SPOTS + (2,)
    scratch = [
        pltpu.VMEM((count_rows, channels), low_type),
        pltpu.VMEM((SPOTS[0] * count_rows, group), low_type),
        pltpu.VMEM(spots + (channels // blocks, width), low_type),
        pltpu.VMEM((middle, width), low_type),
        pltpu.VMEM(spots + (channels // blocks, width), low_type),
        pltpu.VMEM((count_rows, width), wide),
        pltpu.VMEM((count_rows, width), wide),
        pltpu.VMEM((count_rows, channels), wide),
        pltpu.VMEM((count_rows + 2 * line, width), low_type),
        pltpu.VMEM((count_rows + 2 * line, width), low_type),
        pltpu.VMEM((count_rows, width), low_type),
        pltpu.VMEM((count_rows, LANES), wide),
        pltpu.VMEM((2, 2, half + width), wide),
        pltpu.VMEM((2, head_rows, half), low_type),
        pltpu.VMEM((mine_images, channels), wide),
        pltpu.VMEM((mine_images, half), low_type),
        pltpu.VMEM((2, mine_images, half), low_type),
        pltpu.VMEM((2, head_rows, mine_images), low_type),
        pltpu.VMEM((6, 8, channels), wide),
        pltpu.VMEM((6, 8, channels), wide),
        pltpu.VMEM((24, channels), wide),
        pltpu.VMEM((3, 8, channels), wide),
        pltpu.SemaphoreType.DMA((11,)),
        pltpu.SemaphoreType.DMA((2, 6)),
        pltpu.SemaphoreType.DMA((2, 7)),
    ]
    any_space = pl.BlockSpec(memory_space=pl.ANY)
    if gather:
        counts = (channels // blocks, middle // blocks, channels // blocks)
        scratch += [pltpu.SemaphoreType.DMA((2, 3, 3))]
        scratch += [pltpu.SemaphoreType.DMA((2, 4, size)) for size in (6, 8, 6)]
        scratch += [pltpu.VMEM((4, 2, 2, rows, width), low_type) for rows in counts[1:]]
        for lead in ((4, 2), (4,), (4,)):
            scratch += [pltpu.VMEM(lead + (rows, width), low_type) for rows in counts]
        scratch += [pltpu.SemaphoreType.DMA((2, 4, size)) for size in (6, 8, 6, 6)]
        part = width // CUTS
        gram_rows = CUTS * (CUTS + 1) // 4 * part
        many = max(4 * counts[0], 2 * counts[1])
        scratch += [
            pltpu.VMEM((many, width), wide),
            pltpu.VMEM((sum(counts), width), low_type),
            pltpu.VMEM((4, 8, LANES), wide),
            pltpu.VMEM((6, 8, LANES), wide),
            pltpu.VMEM((gram_rows, 2 * part), wide),
            pltpu.VMEM((4, gram_rows // 8, 2 * part), wide),
            pltpu.VMEM((3, gram_rows // 8, 2 * part), wide),
            pltpu.VMEM((gram_rows, 2 * part), wide),
            pltpu.SemaphoreType.DMA((2, 6)),
            pltpu.SemaphoreType.DMA((2, 8)),
            pltpu.SemaphoreType.DMA((2, 14)),
        ]
        grads_shape = [
            jax.ShapeDtypeStruct((sum(counts), width), wide),
            jax.ShapeDtypeStruct((sum(counts), width), low_type),
        ]
        grads_specs = [any_space] * 2
    else:
        grads_shape = [jax.ShapeDtypeStruct(weight.shape, low_type) for weight in weights]
        grads_specs = [any_space] * 3
    return pl.pallas_call(
        functools.partial(client_kernel, gather, ratios, images, classes),
        out_shape=grads_shape
        + [
            jax.ShapeDtypeStruct(params.shape, wide),
            jax.ShapeDtypeStruct((classes * half // LANES, LANES), wide),
            jax.ShapeDtypeStruct((8, LANES), wide),
        ],
        in_specs=[any_space, vmem, smem, vmem, vmem] + [any_space] * len(weights),
        out_specs=grads_specs + [vmem, any_space, vmem],
        scratch_shapes=scratch,
        compiler_params=pltpu.CompilerParams(
            collective_id=0, has_side_effects=True, vmem_limit_bytes=VMEM_BYTES
        ),
    )(features, labels, flag, params, head, *weights)


def adam_update(param, grad, first, second, rate, decay):
    first = adam_first * first + (1.0 - adam_first) * grad
    second = adam_second * second + (1.0 - adam_second) * grad * grad
    first_hat = first / (1.0 - adam_first**STEP)
    second_hat = second / (1.0 - adam_second**STEP)
    return (
        param - rate * (first_hat / (jnp.sqrt(second_hat) + adam_epsilon) + decay * param),
        first,
        second,
    )


def gram_of(section):
    return lax.dot_general(section, section, (((0,), (0,)), ((), ())), precision=precise)


def square(gram):
    return jnp.dot(gram, gram, precision=precise)


def times_poly(left, mixed):
    return schulz_first * left + jnp.dot(left, mixed, precision=precise)


def schulz(sections):
    raw_grams = lax.psum(tuple(gram_of(section) for section in sections), ("client", "chan"))
    factors = [1.0 / (jnp.sqrt(jnp.trace(gram)) + 1e-07) for gram in raw_grams]
    current = [section * factor for section, factor in zip(sections, factors)]
    grams = [gram * (factor * factor) for gram, factor in zip(raw_grams, factors)]
    for turn in range(NS_STEPS):
        mixed = [schulz_second * gram + schulz_third * square(gram) for gram in grams]
        current = [times_poly(current[slot], mixed[slot]) for slot in range(3)]
        if turn + 1 < NS_STEPS:
            grams = [
                times_poly(times_poly(grams[slot], mixed[slot]), mixed[slot]) for slot in range(3)
            ]
    return current


def base_far(ratios, bounds, master, momentum, anchor, loss_tile, grads):
    sums = [
        lax.psum_scatter(flat_rows(grad).astype(wide), ("client", "chan"), scatter_dimension=0, tiled=True)
        for grad in grads
    ]
    grad_base = jnp.concatenate(sums, axis=0)
    momentum_new = momentum_decay * momentum + (grad_base + prox_weight * (master - anchor))
    current = schulz([momentum_new[bounds[slot] : bounds[slot + 1]] for slot in range(3)])
    ortho = jnp.concatenate([current[slot] * ratios[slot] for slot in range(3)], axis=0)
    return momentum_new, ortho, lax.psum(loss_tile, ("client", "chan"))


def as_stored(rows, shape):
    return with_layout_constraint(rows.reshape(shape), Layout(major_to_minor=tuple(range(len(shape)))))


def on_device(
    features,
    labels,
    mask,
    base_master,
    base_momentum,
    global_base,
    norm_params,
    norm_first,
    norm_second,
    head,
    head_first,
    head_second,
):
    halves = lax.axis_size("chan")
    blocks = lax.axis_size("client") * halves
    half = features.shape[2]
    width = base_master.shape[2]
    channels = half * halves
    classes = head.shape[2]
    rows_first = channels // blocks
    rows_mid = 9 * width // blocks
    bounds = (0, rows_first, rows_first + rows_mid, base_master.shape[1])
    ratio = (channels / width) ** 0.5
    ratios = (ratio, 3.0, ratio)
    master, momentum, anchor = base_master[0], base_momentum[0], global_base[0]
    norms = [value.reshape(-1, LANES) for value in (norm_params, norm_first, norm_second)]
    heads = [jnp.transpose(value, (2, 0, 1)).reshape(-1, LANES) for value in (head, head_first, head_second)]
    near = lax.axis_size("client") == SPOTS[0] * SPOTS[1] * SPOTS[2]
    if near:
        weights = [master, momentum, anchor]
    else:
        low_master = master.astype(low_type)
        weights = [
            lax.all_gather(low_master[bounds[slot] : bounds[slot + 1]], ("client", "chan"), axis=0, tiled=True)
            for slot in range(3)
        ]
        split = SPOTS + (2, channels // 32, width)
        weights = [weights[0].reshape(split), weights[1], weights[2].reshape(split)]
    *grads, grad_norm, grad_head, loss_tile = client_pass(
        near, ratios, classes, features[0], labels, mask, norms[0], heads[0], weights
    )
    if near:
        fresh_momentum, ortho = grads
    else:
        fresh_momentum, ortho, loss_tile = base_far(ratios, bounds, master, momentum, anchor, loss_tile, grads)
    loss, momentum_new, base_new, base_low, *fresh = update_pass(
        loss_tile, master, fresh_momentum, ortho, norms, grad_norm, heads, grad_head
    )
    fresh_norms = [as_stored(value, norm_params.shape) for value in fresh[:3]]
    fresh_heads = [jnp.transpose(as_stored(value, (classes, 1, half)), (1, 2, 0)) for value in fresh[3:]]
    return (
        loss,
        base_new[None],
        momentum_new[None],
        base_low[None],
        *fresh_norms,
        *fresh_heads,
    )


def solution(mesh):
    wide_block = P(("client", "chan"), None, None)
    norm_block = P("client", None, "chan", None)
    head_block = P("client", "chan", None)
    return jax.shard_map(
        on_device,
        mesh=mesh,
        in_specs=(P("client", None, "chan"), P("client", None), P("client"))
        + (wide_block,) * 3
        + (norm_block,) * 3
        + (head_block,) * 3,
        out_specs=(P(),) + (wide_block,) * 3 + (norm_block,) * 3 + (head_block,) * 3,
        check_vma=False,
    )
```

```python
import functools

import jax
import jax.numpy as jnp
from jax import lax
from jax.experimental import pallas as pl
from jax.experimental.layout import Layout, with_layout_constraint
from jax.experimental.pallas import tpu as pltpu
from jax.sharding import PartitionSpec as P

NS_STEPS = 5
STEP = 10

low_type = jnp.bfloat16
wide = jnp.float32
MESH = pl.DeviceIdType.MESH
precise = lax.Precision.HIGHEST
norm_epsilon = 1e-05
prox_weight = 0.05
momentum_decay = 0.95
muon_rate = 0.3
muon_decay = 0.1
schulz_first = 3.4445
schulz_second = -4.775
schulz_third = 2.0315
adam_first = 0.9
adam_second = 0.95
adam_epsilon = 1e-08
head_rate = 0.01
head_decay = 0.05
norm_rate = 0.5

SIDE = 7
PIXELS = SIDE * SIDE
LANES = 128
SPOTS = (4, 2, 2)
CUTS = 4
VMEM_BYTES = 62 * 2**20


def dot_nn(left, right):
    return jnp.dot(left, right, preferred_element_type=wide)


def dot_nt(left, right):
    return lax.dot_general(left, right, (((1,), (1,)), ((), ())), preferred_element_type=wide)


def dot_tn(left, right):
    return lax.dot_general(left, right, (((0,), (0,)), ((), ())), preferred_element_type=wide)


def flat_rows(block):
    return block.reshape(-1, block.shape[-1])


def sigmoid(value):
    return 0.5 * jnp.tanh(0.5 * value) + 0.5


def fold_rows(value):
    return jnp.sum(value.reshape(value.shape[0] // 8, 8, value.shape[1]), axis=0)


def column_sum(value):
    return jnp.sum(value, axis=0, keepdims=True)


def remote(src, dst, send_sem, recv_sem, client, core):
    return pltpu.make_async_remote_copy(
        src_ref=src,
        dst_ref=dst,
        send_sem=send_sem,
        recv_sem=recv_sem,
        device_id=(client, core),
        device_id_type=MESH,
    )


class Place:
    def __init__(self):
        self.client = lax.axis_index("client")
        self.core = lax.axis_index("chan")
        self.z = self.client // 4
        self.y = (self.client // 2) % 2
        self.x = self.client % 2
        self.others = [
            self.z + 1 - 2 * (self.z % 2),
            (self.z + 2) % 4,
            3 - self.z,
        ]

    def at(self, z, y, x):
        return z * 4 + y * 2 + x

    def along_x(self):
        return self.at(self.z, self.y, 1 - self.x)

    def along_y(self):
        return self.at(self.z, 1 - self.y, self.x)

    def along_z(self, step):
        return self.at(self.others[step], self.y, self.x)

    def greet(self, whole, across=False):
        barrier = pltpu.get_barrier_semaphore()
        pairs = [(self.client, 1 - self.core)]
        if whole:
            pairs += [(self.along_x(), self.core), (self.along_y(), self.core)]
            pairs += [(self.along_z(step), self.core) for step in range(3)]
        if across:
            pairs += [(self.along_x(), 1 - self.core)]
        for pair in pairs:
            pl.semaphore_signal(barrier, inc=1, device_id=pair, device_id_type=MESH)
        pl.semaphore_wait(barrier, len(pairs))


def cut_rows(counts):
    pieces = []
    for slot, rows in enumerate(counts):
        middle = (rows // 16 + 1) // 2 * 16
        pieces.append((slot, 0, middle, 0))
        pieces.append((slot, middle, rows - middle, 1))
    return pieces


def block_ref(ref, size, z, y, x, core, start, count):
    if len(ref.shape) == 2:
        first = (((z * 2 + y) * 2 + x) * 2 + core) * size + start
        return ref.at[pl.ds(pl.multiple_of(first, 16), count), :]
    return ref.at[z, y, x, core, pl.ds(start, count), :]


class Spread:
    def __init__(self, place, weights, counts, sems):
        self.place = place
        self.weights = weights
        self.counts = counts
        self.pieces = cut_rows(counts)
        self.z_sems, self.near_sems, self.far_sems, self.core_sems = sems
        self.order = [place.z] + place.others

    def z_copy(self, step, slot):
        p = self.place
        ref = block_ref(self.weights[slot], self.counts[slot], p.z, p.y, p.x, p.core, 0, self.counts[slot])
        sems = self.z_sems
        return remote(ref, ref, sems.at[0, step, slot], sems.at[1, step, slot], p.along_z(step), p.core)

    def near_copy(self, turn, number):
        p = self.place
        slot, start, count, way = self.pieces[number]
        ref = block_ref(self.weights[slot], self.counts[slot], self.order[turn], p.y, p.x, p.core, start, count)
        sems = self.near_sems
        return remote(
            ref, ref, sems.at[0, turn, number], sems.at[1, turn, number], (p.along_x, p.along_y)[way](), p.core
        )

    def far_copies(self, turn, number):
        p = self.place
        slot, start, count, way = self.pieces[number]
        spot = self.order[turn]
        sems = self.far_sems
        copies = []
        for part, other in enumerate((0, 1) if slot == 1 else (slice(None),)):
            y, x = (p.y, other) if way == 0 else (other, p.x)
            ref = block_ref(self.weights[slot], self.counts[slot], spot, y, x, p.core, start, count)
            sem = number + 4 * part
            to = (p.along_y, p.along_x)[way]()
            copies.append(remote(ref, ref, sems.at[0, turn, sem], sems.at[1, turn, sem], to, p.core))
        return copies

    def core_copies(self, turn, slot):
        p = self.place
        sems = self.core_sems
        copies = []
        pairs = [(y, x) for y in (0, 1) for x in (0, 1)] if slot == 1 else [(slice(None), slice(None))]
        for part, (y, x) in enumerate(pairs):
            ref = block_ref(self.weights[slot], self.counts[slot], self.order[turn], y, x, p.core, 0, self.counts[slot])
            sem = (0, 2 + part, 1)[slot]
            copies.append(remote(ref, ref, sems.at[0, turn, sem], sems.at[1, turn, sem], p.client, 1 - p.core))
        return copies

    def fill(self, master):
        p = self.place
        start = 0
        for slot in range(3):
            rows = self.counts[slot]
            own = block_ref(self.weights[slot], self.counts[slot], p.z, p.y, p.x, p.core, 0, rows)
            own[...] = master[start : start + rows, :].astype(low_type)
            start += rows

    def begin(self):
        for step in range(3):
            self.z_copy(step, 0).start()
        self.near_start(0)

    def near_start(self, slot):
        for number in (2 * slot, 2 * slot + 1):
            self.near_copy(0, number).start()

    def steps(self):
        near, far, core, start = self.near_step, self.far_step, self.core_step, self.near_start
        groups = [
            [(far, 0, 0), (start, 1)],
            [(near, 1, 0)],
            [(near, 2, 0), (near, 3, 0)],
            [(far, 1, 0), (core, 0, 0), (far, 0, 1)],
            [(far, 2, 0), (far, 3, 0), (core, 1, 0)],
            [(core, 2, 0), (core, 3, 0), (near, 1, 1), (start, 2)],
            [(core, 0, 1), (near, 2, 1)],
            [(far, 1, 1), (near, 3, 1)],
            [(core, 1, 1), (far, 2, 1), (far, 0, 2)],
            [(far, 3, 1), (core, 2, 1), (near, 1, 2)],
            [(core, 3, 1), (core, 0, 2), (near, 2, 2)],
            [(far, 1, 2), (near, 3, 2)],
            [(core, 1, 2), (far, 2, 2)],
            [(far, 3, 2), (core, 2, 2)],
            [(core, 3, 2)],
        ]
        return [[functools.partial(*step) for step in group] for group in groups]

    def near_step(self, turn, slot):
        self.z_copy(turn - 1, slot).wait_recv()
        for number in (2 * slot, 2 * slot + 1):
            self.near_copy(turn, number).start()
        if slot < 2:
            self.z_copy(turn - 1, slot + 1).start()

    def far_step(self, turn, slot):
        for number in (2 * slot, 2 * slot + 1):
            self.near_copy(turn, number).wait_recv()
            for copy in self.far_copies(turn, number):
                copy.start()

    def core_step(self, turn, slot):
        for number in (2 * slot, 2 * slot + 1):
            for copy in self.far_copies(turn, number):
                copy.wait_recv()
        for copy in self.core_copies(turn, slot):
            copy.start()

    def arrive(self, slot):
        for turn in range(4):
            for copy in self.core_copies(turn, slot):
                copy.wait_recv()

    def drain(self, slot):
        for step in range(3):
            self.z_copy(step, slot).wait_send()
        for turn in range(4):
            for copy in self.core_copies(turn, slot):
                copy.wait_send()
            for number in (2 * slot, 2 * slot + 1):
                self.near_copy(turn, number).wait_send()
                for copy in self.far_copies(turn, number):
                    copy.wait_send()


class Fold:
    def __init__(self, place, grads, counts, parts):
        self.place = place
        self.grads = grads
        self.counts = counts
        self.pieces = cut_rows(counts)
        self.core_boxes = [parts[1], parts[0], parts[1]]
        self.near_boxes, self.far_boxes, self.z_boxes = [parts[3 * k + 2 : 3 * k + 5] for k in range(3)]
        self.core_sems, self.near_sems, self.far_sems, self.z_sems = parts[11:]

    def core_copies(self, which, slot):
        p = self.place
        sems = self.core_sems
        copies = []
        pairs = [(y, x) for y in (0, 1) for x in (0, 1)] if slot == 1 else [(slice(None), slice(None))]
        for part, (y, x) in enumerate(pairs):
            ref = block_ref(self.grads[slot], self.counts[slot], which, y, x, 1 - p.core, 0, self.counts[slot])
            box = self.core_boxes[slot].at[which, y, x]
            sem = (0, 2 + part, 1)[slot]
            copies.append(remote(ref, box, sems.at[0, which, sem], sems.at[1, which, sem], p.client, 1 - p.core))
        return copies

    def near_copies(self, which, number):
        p = self.place
        slot, start, count, way = self.pieces[number]
        sems = self.near_sems
        copies = []
        for part, other in enumerate((0, 1) if slot == 1 else (slice(None),)):
            y, x = (other, 1 - p.x) if way == 0 else (1 - p.y, other)
            ref = block_ref(self.grads[slot], self.counts[slot], which, y, x, p.core, start, count)
            box = self.near_boxes[slot].at[which, other, pl.ds(start, count), :]
            sem = number + 4 * part
            to = (p.along_x, p.along_y)[way]()
            copies.append(remote(ref, box, sems.at[0, which, sem], sems.at[1, which, sem], to, p.core))
        return copies

    def far_copy(self, which, number):
        p = self.place
        slot, start, count, way = self.pieces[number]
        y, x = (1 - p.y, p.x) if way == 0 else (p.y, 1 - p.x)
        ref = block_ref(self.grads[slot], self.counts[slot], which, y, x, p.core, start, count)
        box = self.far_boxes[slot].at[which, pl.ds(start, count), :]
        sems = self.far_sems
        return remote(
            ref, box, sems.at[0, which, number], sems.at[1, which, number], (p.along_y, p.along_x)[way](), p.core
        )

    def z_copy(self, which, sender, number):
        p = self.place
        slot, start, count, _ = self.pieces[number]
        rows = pl.ds(start, count)
        sems = self.z_sems
        return remote(
            block_ref(self.grads[slot], self.counts[slot], which, p.y, p.x, p.core, start, count),
            self.z_boxes[slot].at[sender, rows, :],
            sems.at[0, which, number],
            sems.at[1, sender, number],
            p.at(which, p.y, p.x),
            p.core,
        )

    def begin(self, which, slot):
        for copy in self.core_copies(which, slot):
            copy.start()

    def add(self, slot, spots, start, count, box):
        ref = block_ref(self.grads[slot], self.counts[slot], *spots, self.place.core, start, count)
        ref[...] = (ref[...].astype(wide) + box.astype(wide)).astype(low_type)

    def core_step(self, which, slot):
        for copy in self.core_copies(which, slot):
            copy.wait_recv()
        pairs = [(y, x) for y in (0, 1) for x in (0, 1)] if slot == 1 else [(slice(None), slice(None))]
        for y, x in pairs:
            self.add(slot, (which, y, x), 0, self.counts[slot], self.core_boxes[slot][which, y, x])
        for number in (2 * slot, 2 * slot + 1):
            for copy in self.near_copies(which, number):
                copy.start()

    def near_step(self, which, slot):
        p = self.place
        for number in (2 * slot, 2 * slot + 1):
            _, start, count, way = self.pieces[number]
            for copy in self.near_copies(which, number):
                copy.wait_recv()
            for other in (0, 1) if slot == 1 else (slice(None),):
                y, x = (other, p.x) if way == 0 else (p.y, other)
                box = self.near_boxes[slot][which, other, pl.ds(start, count), :]
                self.add(slot, (which, y, x), start, count, box)
            self.far_copy(which, number).start()

    def far_step(self, which, slot):
        p = self.place
        for number in (2 * slot, 2 * slot + 1):
            _, start, count, way = self.pieces[number]
            self.far_copy(which, number).wait_recv()
            box = self.far_boxes[slot][which, pl.ds(start, count), :]
            self.add(slot, (which, p.y, p.x), start, count, box)

            @pl.when(p.z != which)
            def _():
                self.z_copy(which, p.z, number).start()

    def result(self, slot):
        p = self.place
        self.z_boxes[slot][p.z] = block_ref(self.grads[slot], self.counts[slot], p.z, p.y, p.x, p.core, 0, self.counts[slot])[...]
        for sender in range(4):

            @pl.when(p.z != sender)
            def _():
                for number in (2 * slot, 2 * slot + 1):
                    self.z_copy(sender, sender, number).wait_recv()

        total = self.z_boxes[slot][0].astype(wide)
        for sender in range(1, 4):
            total += self.z_boxes[slot][sender].astype(wide)
        return total

    def drain(self):
        for which in range(4):
            for slot in range(3):
                for copy in self.core_copies(which, slot):
                    copy.wait_send()
            for number in range(6):
                for copy in self.near_copies(which, number):
                    copy.wait_send()
                self.far_copy(which, number).wait_send()

            @pl.when(self.place.z != which)
            def _():
                for number in range(6):
                    self.z_copy(which, self.place.z, number).wait_send()
class GramSum:
    def __init__(self, place, data, total, boxes, sems):
        self.place = place
        self.data = data
        self.total = total
        self.y_box, self.z_box = boxes
        self.sems = sems
        self.share = data.shape[0] // 8
        self.down_order = place.others[::-1] + [place.z]

    def rows(self, z, y):
        return pl.ds(pl.multiple_of((z * 2 + y) * self.share, 8), self.share)

    def copy(self, number, src, dst, to):
        sems = self.sems
        return remote(src, dst, sems.at[0, number], sems.at[1, number], to, self.place.core)

    def y_down(self, turn):
        p = self.place
        src = self.data.at[self.rows(self.down_order[turn], 1 - p.y), :]
        return self.copy(turn, src, self.y_box.at[turn], p.along_y())

    def z_down(self, step):
        p = self.place
        src = self.data.at[self.rows(p.others[step], p.y), :]
        return self.copy(4 + step, src, self.z_box.at[step], p.along_z(step))

    def z_up(self, step):
        p = self.place
        ref = self.total.at[self.rows(p.z, p.y), :]
        return self.copy(7 + step, ref, ref, p.along_z(step))

    def y_up(self, turn):
        p = self.place
        ref = self.total.at[self.rows(([p.z] + p.others)[turn], p.y), :]
        return self.copy(10 + turn, ref, ref, p.along_y())

    def run(self):
        p = self.place
        for turn in range(4):
            self.y_down(turn).start()
        for turn in range(4):
            self.y_down(turn).wait_recv()
            self.data[self.rows(self.down_order[turn], p.y), :] += self.y_box[turn]
            if turn < 3:
                self.z_down(2 - turn).start()
        mine = self.rows(p.z, p.y)
        value = self.data[mine, :]
        for step in (2, 1, 0):
            self.z_down(step).wait_recv()
            value += self.z_box[step]
        self.total[mine, :] = value
        for step in range(3):
            self.z_up(step).start()
        self.y_up(0).start()
        for step in range(3):
            self.z_up(step).wait_recv()
            self.y_up(1 + step).start()
        for turn in range(4):
            self.y_up(turn).wait_recv()

    def drain(self):
        for turn in range(4):
            self.y_down(turn).wait_send()
            self.y_up(turn).wait_send()
        for step in range(3):
            self.z_down(step).wait_send()
            self.z_up(step).wait_send()


class TileSum:
    def __init__(self, place, tiles, boxes, sems):
        self.place = place
        self.tiles = tiles
        self.boxes = boxes
        self.sems = sems

    def copy(self, stage, box):
        p = self.place
        to = (p.client, p.along_x(), p.along_y()) + tuple(p.along_z(step) for step in range(3))
        core = 1 - p.core if box == 0 else p.core
        return remote(
            self.tiles.at[stage], self.boxes.at[box], self.sems.at[0, box], self.sems.at[1, box], to[box], core
        )

    def start(self):
        self.copy(0, 0).start()

    def pair(self, stage):
        self.copy(stage, stage).wait_recv()
        self.tiles[stage + 1] = self.tiles[stage] + self.boxes[stage]
        if stage < 2:
            self.copy(stage + 1, stage + 1).start()
        else:
            for step in range(3):
                self.copy(3, 3 + step).start()

    def result(self):
        for step in range(3):
            self.copy(3, 3 + step).wait_recv()
        return (self.tiles[3] + self.boxes[3]) + (self.boxes[4] + self.boxes[5])

    def drain(self):
        for stage in range(3):
            self.copy(stage, stage).wait_send()
        for step in range(3):
            self.copy(3, 3 + step).wait_send()


def halves_of(value):
    high = value.astype(low_type)
    return high, (value - high.astype(wide)).astype(low_type)


class Share:
    def __init__(self, place, sizes, buffers, sems):
        self.place = place
        self.sizes = sizes
        self.fresh, self.rows_in, self.rows_out, self.back = buffers
        self.sems = sems
        self.bounds = [0, sizes[0], sizes[0] + sizes[1], sum(sizes)]
        p = place
        self.duty = jnp.where(p.x == 1, 1, 2 * p.core)
        self.mine = p.x * 2 + p.core

    def section(self, slot):
        return pl.ds(self.bounds[slot], self.sizes[slot])

    def spot(self, slot, x, core):
        number = x if slot == 1 else x * 2 + core
        return pl.ds(pl.multiple_of(number * self.sizes[slot], 16), self.sizes[slot])

    def doer(self, slot):
        return (0, 0) if slot == 0 else (0, 1) if slot == 2 else (1, self.place.core)

    def out_copy(self, slot):
        p = self.place
        x, core = self.doer(slot)
        return remote(
            self.fresh.at[self.section(slot), :],
            self.rows_in.at[self.spot(slot, p.x, p.core), :],
            self.sems.at[0, slot],
            self.sems.at[1, self.mine],
            p.at(p.z, p.y, x),
            core,
        )

    def in_copy(self, slot, x, core):
        p = self.place
        return remote(
            self.fresh.at[self.section(slot), :],
            self.rows_in.at[self.spot(slot, x, core), :],
            self.sems.at[0, slot],
            self.sems.at[1, x * 2 + core],
            p.at(p.z, p.y, x),
            core,
        )

    def back_copy(self, slot, x, core):
        p = self.place
        return remote(
            self.rows_out.at[self.spot(slot, x, core), :],
            self.back.at[self.section(slot), :],
            self.sems.at[0, 3 + x * 2 + core],
            self.sems.at[1, 4 + slot],
            p.at(p.z, p.y, x),
            core,
        )

    def users(self, slot):
        p = self.place
        if slot == 1:
            return [(0, p.core), (1, p.core)]
        return [(x, core) for x in (0, 1) for core in (0, 1)]

    def send(self, slot):
        @pl.when(self.duty != slot)
        def _():
            self.out_copy(slot).start()

        @pl.when(self.duty == slot)
        def _():
            self.rows_in[self.spot(slot, self.place.x, self.place.core), :] = self.fresh[self.section(slot), :]

    def gather(self):
        p = self.place
        for slot in range(3):

            @pl.when(self.duty == slot)
            def _():
                for x, core in self.users(slot):

                    @pl.when((p.x != x) | (p.core != core))
                    def _():
                        self.in_copy(slot, x, core).wait_recv()

    def give_back(self):
        p = self.place
        for slot in range(3):

            @pl.when(self.duty == slot)
            def _():
                for x, core in self.users(slot):

                    @pl.when((p.x != x) | (p.core != core))
                    def _():
                        self.back_copy(slot, x, core).start()

                self.back[self.section(slot), :] = self.rows_out[self.spot(slot, p.x, p.core), :]

    def finish(self):
        p = self.place
        for slot in range(3):

            @pl.when(self.duty != slot)
            def _():
                self.back_copy(slot, p.x, p.core).wait_recv()
                self.out_copy(slot).wait_send()

            @pl.when(self.duty == slot)
            def _():
                for x, core in self.users(slot):

                    @pl.when((p.x != x) | (p.core != core))
                    def _():
                        self.back_copy(slot, x, core).wait_send()


def corner_spot(number, part):
    row, column = number // 2, number % 2
    return slice(row * part, (row + 1) * part), slice(column * part, (column + 1) * part)


def orthogonal(place, ratios, share, share_sems, gram, gram_total, mate_gram, gram_sum, squares, rows_in, low_rows):
    grams, mixed, once = squares
    count, width = rows_in.shape
    part = width // CUTS
    corners = [(row, column) for row in range(CUTS) for column in range(row, CUTS)]
    right_high, right_low = [low_rows.at[pl.ds(count + spot * width, width), :] for spot in range(2)]

    def set_right(value_ref):
        for start in range(0, width, part):
            rows = slice(start, start + part)
            right_high[rows, :], right_low[rows, :] = halves_of(value_ref[rows, :])

    def times_right(value):
        high, low = halves_of(value)
        left = jnp.concatenate([high, high, low], axis=1)
        right = jnp.concatenate([right_high[...], right_low[...], right_high[...]], axis=0)
        return dot_nn(left, right)

    middle = width // 2

    def times_right_even(value, more=()):
        high, low = halves_of(value)
        left = jnp.concatenate([high, high, low], axis=1)
        right = jnp.concatenate([right_high[...], right_low[...], right_high[...]], axis=0)
        upper = left[:middle]
        for rows in more:
            high, low = halves_of(rows)
            upper = jnp.concatenate([upper, jnp.concatenate([high, high, low], axis=1)], axis=0)
        upper = dot_nn(upper, right)
        corner = dot_nn(left[middle:], right[:, middle:])
        lower = jnp.concatenate([upper[:middle, middle:].T, corner], axis=1)
        return jnp.concatenate([upper[:middle], lower], axis=0), upper[middle:]

    share.gather()
    high, low = halves_of(rows_in[...])
    left = jnp.concatenate([high, high, low], axis=0)
    right = jnp.concatenate([high, low, high], axis=0)
    for row in range(CUTS):
        strip = dot_tn(left[:, row * part : (row + 1) * part], right[:, row * part :])
        for column in range(row, CUTS):
            gram[corner_spot(corners.index((row, column)), part)] = strip[
                :, (column - row) * part : (column - row + 1) * part
            ]

    @pl.when(place.x == 1)
    def _():
        swap = remote(gram, mate_gram, share_sems.at[0, 7], share_sems.at[1, 7], place.client, 1 - place.core)
        swap.start()
        swap.wait()
        gram[...] += mate_gram[...]

    gram_sum.run()
    spots = lax.broadcasted_iota(jnp.int32, (part, part), 0)
    diagonal = spots == lax.broadcasted_iota(jnp.int32, (part, part), 1)
    trace = 0.0
    for number, (row, column) in enumerate(corners):
        if row == column:
            trace += jnp.sum(jnp.where(diagonal, gram_total[corner_spot(number, part)], 0.0))
    factor = 1.0 / (jnp.sqrt(trace) + 1e-07)
    square = factor * factor
    for number, (row, column) in enumerate(corners):
        rows, columns = slice(row * part, (row + 1) * part), slice(column * part, (column + 1) * part)
        block = gram_total[corner_spot(number, part)] * square
        grams[rows, columns] = block
        if row < column:
            grams[columns, rows] = block.T
    rows_in[...] = rows_in[...] * factor

    def turn(number, carry):
        set_right(grams)
        mixed[...] = schulz_second * grams[...] + schulz_third * times_right_even(grams[...])[0]
        set_right(mixed)

        @pl.when(number < NS_STEPS - 1)
        def _():
            product, moved = times_right_even(grams[...], (rows_in[...],))
            once[...] = schulz_first * grams[...] + product
            rows_in[...] = schulz_first * rows_in[...] + moved
            grams[...] = schulz_first * once[...] + times_right_even(once[...])[0]

        @pl.when(number == NS_STEPS - 1)
        def _():
            rows_in[...] = schulz_first * rows_in[...] + times_right(rows_in[...])

        return carry

    lax.fori_loop(0, NS_STEPS, turn, 0)
    ratio = jnp.where(share.duty == 1, ratios[1], ratios[0])
    low_rows[0:count, :] = (rows_in[...] * ratio).astype(low_type)
    share.give_back()


def update_kernel(loss_tile, master, fresh_momentum, ortho, *rest):
    norms, grad_norm, heads, grad_head, outs = rest[0:3], rest[3], rest[4:7], rest[7], rest[8:]
    loss_out, *outs = outs
    loss_out[0] = loss_tile[0, 0]
    loss_out[1] = loss_tile[0, 1]
    momentum_out, base_out, low_out = outs[0:3]
    held = master[...]
    momentum_out[...] = fresh_momentum[...]
    fresh = held - muon_rate * (ortho[...].astype(wide) + muon_decay * held)
    base_out[...] = fresh
    low_out[...] = fresh.astype(low_type)
    for targets, values, grad, rate, decay in (
        (outs[3:6], norms, grad_norm, norm_rate, 0.0),
        (outs[6:9], heads, grad_head, head_rate, head_decay),
    ):
        updates = adam_update(values[0][...], grad[...], values[1][...], values[2][...], rate, decay)
        for target, value in zip(targets, updates):
            target[...] = value


def update_pass(loss_tile, master, fresh_momentum, ortho, norms, grad_norm, heads, grad_head):
    vmem = pl.BlockSpec(memory_space=pltpu.VMEM)
    smem = pl.BlockSpec(memory_space=pltpu.SMEM)
    operands = [loss_tile, master, fresh_momentum, ortho, *norms, grad_norm, *heads, grad_head]
    outs = [(2,), master.shape, master.shape, master.shape] + [grad_norm.shape] * 3 + [grad_head.shape] * 3
    types = [wide, wide, wide, low_type] + [wide] * 6
    return pl.pallas_call(
        update_kernel,
        out_shape=[jax.ShapeDtypeStruct(shape, kind) for shape, kind in zip(outs, types)],
        in_specs=[smem] + [vmem] * (len(operands) - 1),
        out_specs=[smem] + [vmem] * (len(outs) - 1),
        compiler_params=pltpu.CompilerParams(vmem_limit_bytes=VMEM_BYTES),
    )(*operands)


def norm_stats(mine, theirs, count):
    gap = mine[0:1] - theirs[0:1]
    mean = 0.5 * (mine[0:1] + theirs[0:1])
    spread = mine[1:2] + theirs[1:2] + gap * gap * (0.5 * count)
    return mean, lax.rsqrt(spread / (2.0 * count) + norm_epsilon)


def client_kernel(
    gather,
    ratios,
    images,
    classes,
    features,
    labels,
    flag,
    params,
    head,
    *rest,
):
    if gather:
        master, momentum, anchor, *rest = rest
    else:
        first_in, middle_in, last_in, *rest = rest
    if gather:
        fresh_out, ortho_out, *rest = rest
    else:
        grads_out, rest = rest[:3], rest[3:]
    (
        grad_norm_out,
        grad_head_out,
        loss_out,
        x_all,
        mid_wide,
        w_first,
        w_middle,
        w_last,
        act_one,
        act_two,
        act_three,
        taps_one,
        taps_two,
        hidden_two,
        stage,
        params_all,
        head_all,
        grad_pool,
        pool_send,
        pool_all,
        logit_grads,
        sums_mine,
        sums_theirs,
        shift,
        fwd_stats,
        sem_local,
        sem_swap,
        sem_misc,
        *near_parts,
    ) = rest
    place = Place()
    core = place.core
    mate = (place.client, 1 - core)
    count_rows, channels = x_all.shape
    half = channels // 2
    width = act_one.shape[1]
    part = width // 2
    mine_images = images // 2
    line = SIDE * mine_images
    total_rows = 2.0 * count_rows

    def tile(index):
        return pl.ds(pl.multiple_of(index * line, line), line)

    def lanes(index, size):
        return pl.ds(pl.multiple_of(index * size, size), size)

    weights = (w_first, w_middle, w_last)
    if gather:
        held = act_three.at[pl.ds(0, master.shape[0]), pl.ds(0, width)]
        load = pltpu.make_async_copy(master, held, sem_local.at[8])
        load.start()
        counts = [channels // 32, 9 * width // 32, channels // 32]
        spread = Spread(place, weights, counts, near_parts[:4])
        fold = Fold(place, (w_first, mid_wide, w_last), counts, near_parts[4:19])
        rows_in, back, tiles, tile_boxes, gram_total, y_box, z_box, mate_gram = near_parts[19:27]
        tile_sems, share_sems, gram_sems = near_parts[27:]
        block_rows = master.shape[0]
        side_space = pl.ds(half, width)
        held_base, held_momentum, held_anchor, fresh = [
            act_three.at[pl.ds(number * block_rows, block_rows), side_space] for number in range(4)
        ]
        rows_in[...] = jnp.zeros_like(rows_in)
        share = Share(place, counts, (fresh, rows_in, hidden_two, back), share_sems)
        tile_sum = TileSum(place, tiles, tile_boxes, tile_sems)
        due = spread.steps()
        load.wait()
        spread.fill(held)
        place.greet(True, True)
        spread.begin()
    else:
        place.greet(False)
        loads = [
            pltpu.make_async_copy(src, dst, sem_local.at[8 + slot])
            for slot, (src, dst) in enumerate(zip((first_in, middle_in, last_in), weights))
        ]
        for load in loads:
            load.start()
        due = []

    quarter = half // 2
    own_rows = pl.ds(pl.multiple_of(core * count_rows, count_rows), count_rows)
    mate_rows = pl.ds(pl.multiple_of((1 - core) * count_rows, count_rows), count_rows)
    top_rows = pl.ds(0, count_rows)
    own_copies = [
        pltpu.make_async_copy(
            features.at[own_rows, pl.ds(side * quarter, quarter)], buffer, sem_local.at[side]
        )
        for side, buffer in enumerate((hidden_two, mid_wide.at[top_rows, :]))
    ]
    feature_copies = []
    for side, buffer in enumerate((taps_one, taps_two)):
        feature_copies.append(
            remote(
                features.at[mate_rows, pl.ds(side * quarter, quarter)],
                buffer.at[top_rows, :],
                sem_misc.at[0, 5 + side],
                sem_misc.at[1, 5 + side],
                *mate,
            )
        )
    for copy in feature_copies + own_copies:
        copy.start()
    per_kind = params.shape[0] // 2
    for kind in range(2):
        rows = [params[kind * per_kind + spot : kind * per_kind + spot + 1, :] for spot in range(per_kind)]
        params_all[core, kind : kind + 1, :] = jnp.concatenate(rows, axis=1)
    head_all[core] = jnp.zeros(head_all.shape[1:], low_type)
    stage[0 : head.shape[0], :] = head[...]
    for spot in range(half // LANES):
        head_all[core, 0:classes, spot * LANES : (spot + 1) * LANES] = stage[
            pl.ds(spot, classes, stride=half // LANES), :
        ].astype(low_type)
    to_mate = [
        remote(params_all.at[core], params_all.at[core], sem_misc.at[0, 0], sem_misc.at[1, 0], *mate),
        remote(head_all.at[core], head_all.at[core], sem_misc.at[0, 1], sem_misc.at[1, 1], *mate),
    ]
    for copy in to_mate:
        copy.start()
    to_mate += feature_copies

    def advance(count):
        for group in due[:count]:
            for step in group:
                step()
        del due[:count]

    def advance_at(index, spots):
        for spot, group in zip(spots, due):

            @pl.when(index == spot)
            def _():
                for step in group:
                    step()

    def arrive(slot, left):
        if gather:
            advance(len(due) - left)
            spread.arrive(slot)
        else:
            loads[slot].wait()

    def arrive_turns(slot, turns):
        if gather:
            for turn in turns:
                for copy in spread.core_copies(turn, slot):
                    copy.wait_recv()

    def fold_step(kind, slot, which):
        if gather:
            (fold.core_step, fold.near_step, fold.far_step)[kind](which, slot)

    def fold_at(index, spot, *steps):
        @pl.when(index == spot)
        def _():
            for step in steps:
                fold_step(*step)

    def fold_begin(which, slot):
        if gather:
            fold.begin(which, slot)

    def zero_edges(buffer):
        edge = jnp.zeros((line,) + buffer.shape[1:], low_type)
        buffer[0:line, :] = edge
        buffer[line + count_rows : 2 * line + count_rows, :] = edge

    advance(3)
    for copy in own_copies:
        copy.wait()

    def turn_from(source, base):
        def turn(index, carry):
            stage[0:count_rows, :] = source(lanes(index, LANES)).astype(wide)

            def pixel(spot, inner):
                x_all[
                    pl.ds(pl.multiple_of(spot * mine_images, mine_images), mine_images),
                    pl.ds(pl.multiple_of(base + index * LANES, LANES), LANES),
                ] = stage[pl.ds(spot, mine_images, stride=PIXELS), :].astype(low_type)
                return inner

            return lax.fori_loop(0, PIXELS, pixel, carry, unroll=7)

        return turn

    quarters = quarter // LANES
    own_base, mate_base = core * half, (1 - core) * half
    lax.fori_loop(0, quarters, turn_from(lambda columns: hidden_two[:, columns], own_base), 0)
    advance(1)
    lax.fori_loop(
        0,
        quarters,
        turn_from(lambda columns: mid_wide[0:count_rows, columns], own_base + quarter),
        0,
    )
    advance(1)
    for copy in to_mate:
        copy.wait_recv()
    lax.fori_loop(0, quarters, turn_from(lambda columns: taps_one[0:count_rows, columns], mate_base), 0)
    advance(1)
    lax.fori_loop(0, quarters, turn_from(lambda columns: taps_two[0:count_rows, columns], mate_base + quarter), 0)
    zero_edges(taps_one)
    zero_edges(taps_two)
    arrive(0, 9)

    def swap(slot, size):
        return remote(
            sums_mine.at[slot, :, pl.ds(0, size)],
            sums_theirs.at[slot, :, pl.ds(0, size)],
            sem_swap.at[0, slot],
            sem_swap.at[1, slot],
            *mate,
        )

    def gain_bias(lower, upper):
        rows = []
        for kind in range(2):
            pieces = [params_all[side, kind : kind + 1, lower:upper] for side in range(2)]
            rows.append(jnp.concatenate(pieces, axis=1))
        return rows

    def collect(index, value, columns, size):
        @pl.when(index == 0)
        def _():
            shift[0:1, pl.ds(0, size)] = column_sum(fold_rows(value)) / value.shape[0]
            shift[8:24, pl.ds(0, size)] = jnp.zeros((16, size), wide)

        gap = value - shift[0:1, pl.ds(0, size)]
        shift[8:16, pl.ds(0, size)] += fold_rows(gap)
        shift[16:24, pl.ds(0, size)] += fold_rows(gap * gap)

    def close_stats(slot, columns, size):
        sum_gap = column_sum(shift[8:16, pl.ds(0, size)])
        sum_square = column_sum(shift[16:24, pl.ds(0, size)])
        sums_mine[slot, 0:1, columns] = shift[0:1, pl.ds(0, size)] + sum_gap / count_rows
        sums_mine[slot, 1:2, columns] = sum_square - sum_gap * sum_gap / count_rows

    def look_over(act, columns):
        def look(index, carry):
            collect(index, act[tile(index), columns], None, width)
            return carry

        lax.fori_loop(0, SIDE, look, 0)

    groups = SPOTS[0]
    group = channels // groups

    def settle(slot, size):
        mean, scale = norm_stats(
            sums_mine[slot, 0:2, pl.ds(0, size)], sums_theirs[slot, 0:2, pl.ds(0, size)], float(count_rows)
        )
        fwd_stats[slot, 0:1, pl.ds(0, size)] = mean
        fwd_stats[slot, 1:2, pl.ds(0, size)] = scale

    whole_width = pl.ds(0, width)

    def first_part(index, carry):
        act_one[...] += dot_nn(x_all[:, lanes(index, group)], flat_rows(w_first[index]))
        advance_at(index, (0, 1, 2))
        return carry

    act_one[...] = jnp.zeros_like(act_one)
    lax.fori_loop(0, groups, first_part, 0)
    del due[:3]
    look_over(act_one, whole_width)
    close_stats(0, whole_width, width)
    move = swap(0, width)
    move.start()
    advance(1)
    move.wait()
    settle(0, width)

    gain_one, bias_one = gain_bias(0, part)
    gain_two, bias_two = gain_bias(part, width)
    gain_three, bias_three = gain_bias(width, width + half)

    def normal(act, slot, index):
        mean = fwd_stats[slot, 0:1, pl.ds(0, width)]
        return (act[tile(index), :] - mean) * fwd_stats[slot, 1:2, pl.ds(0, width)]

    def hide_one(index, carry):
        value = normal(act_one, 0, index) * gain_one + bias_one
        taps_one[pl.ds(pl.multiple_of((index + 1) * line, line), line), :] = (value * sigmoid(value)).astype(low_type)
        return carry

    lax.fori_loop(0, SIDE, hide_one, 0)
    if gather:
        arrive_turns(1, (0, 1))
    else:
        arrive(1, 0)

    step = mine_images
    piece = width // 2

    def row_windows(buffer, down, start, reach):
        if reach == line:
            return buffer[pl.ds(pl.multiple_of(down * line, line), count_rows), :]
        windows = [
            buffer[pl.ds(pl.multiple_of((down + row) * line + start, step), reach), :] for row in range(SIDE)
        ]
        return jnp.concatenate(windows, axis=0)

    def add_windows(target, columns, value, start, reach):
        for row in range(SIDE):
            rows = slice(row * line + start, row * line + start + reach)
            target[rows, columns] += value[row * reach : (row + 1) * reach]

    low_start, high_start, reaches = (0, 0, step), (step, 0, 0), (line - step, line, line - step)

    early, taps = 4, 9

    def second_part(index, carry):
        tap = jnp.where(place.z < 2, index, (index + taps - early) % taps) if gather else index

        @pl.when(index == early)
        def _():
            arrive_turns(1, (2, 3))

        down = tap // 3
        for over in range(3):

            @pl.when(tap % 3 == over)
            def _():
                left = row_windows(taps_one, down, low_start[over], reaches[over])
                kernel = w_middle[pl.ds(pl.multiple_of(tap * width, width), width), :]
                add_windows(act_two, slice(None), dot_nn(left, kernel), high_start[over], reaches[over])

        advance_at(index, (2, 5, 6, 8))
        return carry

    act_two[...] = jnp.zeros_like(act_two)
    lax.fori_loop(0, taps, second_part, 0)
    del due[:4]
    look_over(act_two, whole_width)
    close_stats(1, whole_width, width)
    move_two = swap(1, width)
    move_two.start()
    arrive(2, 0)
    if gather:
        spread.drain(0)

    def turn_weights(which, carry):
        w_first[which] = jnp.transpose(flat_rows(w_last[which])).reshape(w_first.shape[1:])
        return carry

    lax.fori_loop(0, groups, turn_weights, 0)
    move_two.wait()
    settle(1, width)

    tall = count_rows // 2

    def third_tile(index, carry):
        rows = pl.ds(pl.multiple_of(index * tall, 16), tall)
        act = act_two[rows, :]
        normed = (act - fwd_stats[1, 0:1, whole_width]) * fwd_stats[1, 1:2, whole_width]
        value = normed * gain_two + bias_two
        hidden = (value * sigmoid(value)).astype(low_type)
        hidden_two[rows, :] = hidden
        for which in range(groups):
            columns = slice(which * group, (which + 1) * group)
            value = dot_nn(hidden, flat_rows(w_first[which]))
            act_three[rows, columns] = value
            start = jnp.where(index == 0, column_sum(value[0:8]) / 8.0, shift[0:1, columns])
            gap = value - start
            kept_sums = jnp.where(index == 0, 0.0, shift[8:24, columns])
            shift[0:1, columns] = start
            shift[8:16, columns] = kept_sums[0:8] + fold_rows(gap)
            shift[16:24, columns] = kept_sums[8:16] + fold_rows(gap * gap)
        return carry

    lax.fori_loop(0, 2, third_tile, 0)
    close_stats(2, pl.ds(0, channels), channels)
    move_three = swap(2, channels)
    move_three.start()
    move_three.wait()
    settle(2, channels)

    per_group = group // LANES

    def block_of(spot):
        return pl.ds(pl.multiple_of(spot * mine_images, mine_images), mine_images)

    def mid_line(which, index):
        return pl.ds(pl.multiple_of(which * count_rows + index * line, line), line)

    kept = channels // LANES * mine_images

    def gathered(kind):
        starts = range(kind * kept, (kind + 1) * kept, mine_images)
        return jnp.concatenate([stage[start : start + mine_images, :] for start in starts], axis=1)

    fwd_stats[2, 4:5, :] = fwd_stats[2, 1:2, :] * gain_three
    fwd_stats[2, 5:6, :] = bias_three - fwd_stats[2, 0:1, :] * fwd_stats[2, 4:5, :]

    def emit(index, carry):
        columns = lanes(index, LANES)
        slant, level = fwd_stats[2, 4:5, columns], fwd_stats[2, 5:6, columns]

        def pixels(row, sums):
            pooled, steeps, steeps_act = sums
            found = []
            for spot in range(SIDE):
                where = block_of(row * SIDE + spot)
                act = act_three[where, columns]
                half_total = 0.5 * (act * slant + level + x_all[where, columns].astype(wide))
                rise = 1.0 + jnp.tanh(half_total)
                out = half_total * rise
                steep = rise + out * (2.0 - rise)
                found.append(steep.astype(low_type))
                pooled, steeps, steeps_act = pooled + out, steeps + steep, steeps_act + steep * act
            mid_wide[mid_line(index // per_group, row), lanes(index % per_group, LANES)] = jnp.concatenate(
                found, axis=0
            )
            return pooled, steeps, steeps_act

        zero = jnp.zeros((mine_images, LANES), wide)
        sums = lax.fori_loop(0, SIDE, pixels, (zero, zero, zero))
        for kind, value in enumerate(sums):
            stage[pl.ds(pl.multiple_of(kind * kept + index * mine_images, mine_images), mine_images), :] = value
        return carry

    lax.fori_loop(0, channels // LANES, emit, 0)

    pooled = (gathered(0) / PIXELS).astype(low_type)
    head_full = jnp.concatenate([head_all[0], head_all[1]], axis=1)
    logits = dot_nt(head_full, pooled)
    spots = lax.broadcasted_iota(jnp.int32, logits.shape, 0)
    inside = spots < classes
    first_labels, second_labels = labels[0:1, 0:mine_images], labels[0:1, mine_images:]
    onehot = (spots == jnp.where(core == 0, first_labels, second_labels)).astype(wide)
    top = jnp.max(jnp.where(inside, logits, -jnp.inf), axis=0, keepdims=True)
    powers = jnp.where(inside, jnp.exp(logits - top), 0.0)
    power_sum = jnp.sum(powers, axis=0, keepdims=True)
    picked = jnp.sum(logits * onehot, axis=0, keepdims=True)
    each_loss = top + jnp.log(power_sum) - picked
    taking = flag[0].astype(wide)
    tile_spots = lax.broadcasted_iota(jnp.int32, loss_out.shape, 1)
    loss_out[...] = jnp.where(tile_spots == 0, taking * jnp.sum(each_loss), taking * mine_images)
    grads = (taking / images * (powers / power_sum - onehot)).astype(low_type)
    grad_pool[...] = dot_tn(grads, head_full) * (0.5 / PIXELS)
    logit_grads[core] = grads
    pool_all[core] = pooled[:, 0:half]
    pool_send[...] = pooled[:, half:]

    @pl.when(core == 1)
    def _():
        pool_all[core] = pooled[:, half:]
        pool_send[...] = pooled[:, 0:half]

    head_moves = [
        remote(pool_send, pool_all.at[core], sem_misc.at[0, 3], sem_misc.at[1, 3], *mate),
        remote(logit_grads.at[core], logit_grads.at[core], sem_misc.at[0, 4], sem_misc.at[1, 4], *mate),
    ]

    steeps = gathered(1)
    steeps_normed = (gathered(2) - fwd_stats[2, 0:1, :] * steeps) * fwd_stats[2, 1:2, :]
    sums_mine[3, 0:1, :] = column_sum(grad_pool[...] * steeps)
    sums_mine[3, 1:2, :] = column_sum(grad_pool[...] * steeps_normed)
    move_back = swap(3, channels)
    move_back.start()
    for copy in head_moves:
        copy.start()
    move_back.wait()

    def back_terms(slot, layer, size, gain):
        columns = pl.ds(0, size)
        sums = sums_mine[slot, 0:2, columns] + sums_theirs[slot, 0:2, columns]
        sums_mine[slot, 2:4, columns] = sums
        scale = fwd_stats[layer, 1:2, columns]
        return (
            scale * gain,
            scale * gain * sums[0:1] / total_rows,
            scale * scale * gain * sums[1:2] / total_rows,
        )

    first, second, third = back_terms(3, 2, channels, gain_three)
    fwd_stats[2, 4:5, :] = second - third * fwd_stats[2, 0:1, :]
    fwd_stats[2, 5:6, :] = third
    grad_pool[...] = grad_pool[...] * first

    def pull(index):
        for which in range(groups):
            columns = slice(which * group, (which + 1) * group)
            reach = grad_pool[:, columns]
            steep = mid_wide[mid_line(which, index), :].astype(wide)
            value = jnp.concatenate([reach] * SIDE, axis=0) * steep
            value = value - fwd_stats[2, 4:5, columns] - fwd_stats[2, 5:6, columns] * act_three[tile(index), columns]
            mid_wide[mid_line(which, index), :] = value.astype(low_type)

    pull(0)

    def drop_into(act, slot, gain, bias, columns):
        size = pl.ds(0, width)
        shift[8:24, size] = jnp.zeros((16, width), wide)

        def drop(index, carry):
            normed = normal(act, slot, index)
            norm = normed * gain + bias
            sig = sigmoid(norm)
            grad = act_three[tile(index), columns] * (sig + norm * sig * (1.0 - sig))
            act_three[tile(index), columns] = grad
            shift[8:16, size] += fold_rows(grad)
            shift[16:24, size] += fold_rows(grad * normed)
            return carry

        lax.fori_loop(0, SIDE, drop, 0)

    def close_back(slot):
        size = pl.ds(0, width)
        sums_mine[slot, 0:1, size] = column_sum(shift[8:16, size])
        sums_mine[slot, 1:2, size] = column_sum(shift[16:24, size])

    space_two, space_one = pl.ds(0, width), pl.ds(width, width)

    def mid_group(which):
        return mid_wide[pl.ds(pl.multiple_of(which * count_rows, count_rows), count_rows), :]

    def back_two(first, lines):
        def rows_from(base):
            return pl.ds(pl.multiple_of(base + first * line, line), lines * line)

        left = jnp.concatenate([mid_wide[rows_from(which * count_rows), :] for which in range(groups)], axis=1)
        value = dot_nn(left, flat_rows(w_last[...]))
        normed = (act_two[rows_from(0), :] - fwd_stats[1, 0:1, whole_width]) * fwd_stats[1, 1:2, whole_width]
        norm = normed * gain_two + bias_two
        sig = sigmoid(norm)
        grad = value * (sig + norm * sig * (1.0 - sig))
        act_three[rows_from(0), space_two] = grad
        size = pl.ds(0, width)
        shift[8:16, size] += fold_rows(grad)
        shift[16:24, size] += fold_rows(grad * normed)

    pairs = (SIDE - 1) // 2

    def back_two_loop(index, carry):
        pull(2 * index + 2)
        pull(2 * index + 3)
        back_two(2 * index, 2)
        return carry

    shift[8:24, :] = jnp.zeros((16, channels), wide)
    pull(1)
    lax.fori_loop(0, pairs - 1, back_two_loop, 0)
    pull(SIDE - 1)
    back_two(SIDE - 3, 2)
    back_two(SIDE - 1, 1)
    close_back(4)
    move_back_two = swap(4, width)
    move_back_two.start()
    if gather:
        base_loads = [
            pltpu.make_async_copy(src, dst, sem_local.at[1 + number])
            for number, (src, dst) in enumerate(
                ((master, held_base), (momentum, held_momentum), (anchor, held_anchor))
            )
        ]
        for load in base_loads:
            load.start()
        tiles[0] = loss_out[...]
        tile_sum.start()

    def settle_section(slot):
        if gather:
            rows = share.section(slot)
            grad = fold.result(slot) + prox_weight * (held_base[rows, :] - held_anchor[rows, :])
            fresh[rows, :] = momentum_decay * held_momentum[rows, :] + grad
            share.send(slot)

    if gather:
        spread.drain(1)
        spread.drain(2)

    def put(ref, which, value):
        ref[which] = value.astype(low_type).reshape(ref.shape[1:])

    def expand_group(which, carry):
        put(w_last, which, dot_tn(mid_group(which), hidden_two[...]))
        fold_begin(which, 2)
        fold_at(which, 2, (0, 2, 0))
        fold_at(which, 3, (0, 2, 1))
        return carry

    lax.fori_loop(0, groups, expand_group, 0)
    move_back_two.wait()
    terms_two = back_terms(4, 1, width, gain_two)

    def back_act(terms, act, layer, index, columns):
        first, second, third = terms
        gap = act[tile(index), :] - fwd_stats[layer, 0:1, pl.ds(0, width)]
        return (first * act_three[tile(index), columns] - second - third * gap).astype(low_type)

    def grad_two(index, carry):
        taps_two[pl.ds(pl.multiple_of((index + 1) * line, line), line), :] = back_act(
            terms_two, act_two, 1, index, space_two
        )
        return carry

    lax.fori_loop(0, SIDE, grad_two, 0)
    fold_step(0, 2, 2)
    fold_step(1, 2, 0)
    core_step, near_step, far_step = 0, 1, 2
    plan = {
        0: [(core_step, 2, 3)],
        1: [(near_step, 2, 1)],
        2: [(far_step, 2, 0), (near_step, 2, 2)],
        3: [(far_step, 2, 1), (near_step, 2, 3)],
        4: [(far_step, 2, 2)],
        5: [(far_step, 2, 3), (core_step, 1, 0)],
        7: [(core_step, 1, 1)],
    }

    def middle_row(down, carry):
        for over in range(3):
            left = row_windows(taps_one, down, low_start[over], reaches[over])
            right = row_windows(taps_two, 1, high_start[over], reaches[over])
            rows = pl.ds(pl.multiple_of((3 * down + over) * width, width), width)
            mid_wide[rows, :] = dot_tn(left, right).astype(low_type)
            for row in range(3):
                tap = 3 * row + over

                @pl.when(down == row)
                def _():
                    if tap >= 2 and tap % 2 == 0:
                        fold_begin(tap // 2 - 1, 1)
                    for step in plan.get(tap, ()):
                        fold_step(*step)

        return carry

    lax.fori_loop(0, 3, middle_row, 0)
    for copy in head_moves:
        copy.wait_recv()
    head_grad = dot_nn(logit_grads[0], pool_all[0]) + dot_nn(logit_grads[1], pool_all[1])
    for spot in range(half // LANES):
        stage[pl.ds(spot, classes, stride=half // LANES), :] = head_grad[
            0:classes, spot * LANES : (spot + 1) * LANES
        ]
    head_space = stage.at[pl.ds(0, grad_head_out.shape[0]), :]
    head_leave = pltpu.make_async_copy(head_space, grad_head_out, sem_local.at[0])
    head_leave.start()
    if gather:
        tile_sum.pair(0)
        for load in base_loads:
            load.wait()

    def back_one(index, carry):
        down, side = index // 2, index % 2
        columns = lanes(2 + side, piece)
        for over in range(3):
            left = row_windows(taps_two, 2 - down, high_start[over], reaches[over])
            start = pl.multiple_of((3 * down + over) * width + side * piece, piece)
            value = dot_nt(left, w_middle[pl.ds(start, piece), :])
            add_windows(act_three, columns, value, low_start[over], reaches[over])
        fold_at(index, 0, (core_step, 1, 2), (near_step, 1, 0))
        fold_at(index, 1, (core_step, 1, 3))
        fold_at(index, 2, (near_step, 1, 1), (far_step, 1, 0))
        fold_at(index, 4, (far_step, 1, 1))
        fold_at(index, 5, (near_step, 1, 2))
        return carry

    act_three[:, space_one] = jnp.zeros((count_rows, width), wide)
    lax.fori_loop(0, 6, back_one, 0)
    drop_into(act_one, 0, gain_one, bias_one, space_one)
    fold_step(near_step, 1, 3)
    settle_section(2)
    close_back(5)
    move_back_one = swap(5, width)
    move_back_one.start()

    move_back_one.wait()
    terms_one = back_terms(5, 0, width, gain_one)

    def grad_one(index, carry):
        hidden_two[tile(index), :] = back_act(terms_one, act_one, 0, index, space_one)
        return carry

    lax.fori_loop(0, SIDE, grad_one, 0)
    fold_step(far_step, 1, 2)
    if gather:
        tile_sum.pair(1)

    def reduce_group(which, carry):
        put(w_first, which, dot_tn(x_all[:, lanes(which, group)], hidden_two[...]))
        fold_begin(which, 0)
        fold_at(which, 0, (far_step, 1, 3))
        fold_at(which, 2, (core_step, 0, 0))
        fold_at(which, 3, (core_step, 0, 1), (near_step, 0, 0))
        return carry

    lax.fori_loop(0, groups, reduce_group, 0)

    for kind in range(2):
        row = 3 - kind
        pieces = [
            sums_mine[5, row : row + 1, lanes(core, part)],
            sums_mine[4, row : row + 1, lanes(core, part)],
            sums_mine[3, row : row + 1, lanes(core, half)],
        ]
        whole = jnp.concatenate(pieces, axis=1)
        per_kind = whole.shape[1] // LANES
        for spot in range(per_kind):
            grad_norm_out[kind * per_kind + spot : kind * per_kind + spot + 1, :] = whole[
                :, spot * LANES : (spot + 1) * LANES
            ]
    for step in (
        (core_step, 0, 2),
        (core_step, 0, 3),
        (far_step, 0, 0),
        (near_step, 0, 1),
        (near_step, 0, 2),
        (far_step, 0, 1),
        (near_step, 0, 3),
        (far_step, 0, 2),
        (far_step, 0, 3),
    ):
        fold_step(*step)
        if step == (far_step, 0, 0):
            settle_section(1)
    if gather:
        settle_section(0)
        leave = pltpu.make_async_copy(fresh, fresh_out, sem_local.at[1])
        leave.start()
        tile_sum.pair(2)
        part = width // CUTS
        gram = act_three.at[pl.ds(0, gram_total.shape[0]), pl.ds(half + width, 2 * part)]
        corner_rows = pl.ds(gram_total.shape[0], width)
        squares = [act_three.at[corner_rows, pl.ds(spot * width, width)] for spot in (0, 1, 3)]
        gram_sum = GramSum(place, gram, gram_total, (y_box, z_box), gram_sems)
        orthogonal(place, ratios, share, share_sems, gram, gram_total, mate_gram, gram_sum, squares, rows_in, hidden_two)
        share.finish()
        loss_out[...] = tile_sum.result()
        ortho_leave = pltpu.make_async_copy(back, ortho_out, sem_local.at[2])
        ortho_leave.start()
        gram_sum.drain()
        tile_sum.drain()
        fold.drain()
        leave.wait()
        ortho_leave.wait()
    else:
        outs = [
            pltpu.make_async_copy(ref, out, sem_local.at[slot])
            for slot, (ref, out) in enumerate(zip((w_first, mid_wide.at[pl.ds(0, 9 * width), :], w_last), grads_out))
        ]
        for copy in outs:
            copy.start()
        for copy in outs:
            copy.wait()
    head_leave.wait()
    for copy in to_mate + head_moves:
        copy.wait_send()


def client_pass(gather, ratios, classes, features, labels, flag, params, head, weights):
    pixels, half = features.shape
    images = labels.shape[1]
    count_rows, channels = pixels // 2, 2 * half
    width = params.shape[0] // 2 * LANES - half
    head_rows = classes + -classes % 16
    mine_images = images // 2
    line = SIDE * mine_images
    middle = 9 * width
    blocks = 32
    group = channels // SPOTS[0]
    vmem = pl.BlockSpec(memory_space=pltpu.VMEM)
    smem = pl.BlockSpec(memory_space=pltpu.SMEM)
    spots = SPOTS + (2,)
    scratch = [
        pltpu.VMEM((count_rows, channels), low_type),
        pltpu.VMEM((SPOTS[0] * count_rows, group), low_type),
        pltpu.VMEM(spots + (channels // blocks, width), low_type),
        pltpu.VMEM((middle, width), low_type),
        pltpu.VMEM(spots + (channels // blocks, width), low_type),
        pltpu.VMEM((count_rows, width), wide),
        pltpu.VMEM((count_rows, width), wide),
        pltpu.VMEM((count_rows, channels), wide),
        pltpu.VMEM((count_rows + 2 * line, width), low_type),
        pltpu.VMEM((count_rows + 2 * line, width), low_type),
        pltpu.VMEM((count_rows, width), low_type),
        pltpu.VMEM((count_rows + 64, LANES), wide),
        pltpu.VMEM((2, 2, half + width), wide),
        pltpu.VMEM((2, head_rows, half), low_type),
        pltpu.VMEM((mine_images, channels), wide),
        pltpu.VMEM((mine_images, half), low_type),
        pltpu.VMEM((2, mine_images, half), low_type),
        pltpu.VMEM((2, head_rows, mine_images), low_type),
        pltpu.VMEM((6, 8, channels), wide),
        pltpu.VMEM((6, 8, channels), wide),
        pltpu.VMEM((24, channels), wide),
        pltpu.VMEM((3, 8, channels), wide),
        pltpu.SemaphoreType.DMA((11,)),
        pltpu.SemaphoreType.DMA((2, 6)),
        pltpu.SemaphoreType.DMA((2, 7)),
    ]
    any_space = pl.BlockSpec(memory_space=pl.ANY)
    if gather:
        counts = (channels // blocks, middle // blocks, channels // blocks)
        scratch += [pltpu.SemaphoreType.DMA((2, 3, 3))]
        scratch += [pltpu.SemaphoreType.DMA((2, 4, size)) for size in (6, 8, 6)]
        scratch += [pltpu.VMEM((4, 2, 2, rows, width), low_type) for rows in counts[1:]]
        for lead in ((4, 2), (4,), (4,)):
            scratch += [pltpu.VMEM(lead + (rows, width), low_type) for rows in counts]
        scratch += [pltpu.SemaphoreType.DMA((2, 4, size)) for size in (6, 8, 6, 6)]
        part = width // CUTS
        gram_rows = CUTS * (CUTS + 1) // 4 * part
        many = max(4 * counts[0], 2 * counts[1])
        scratch += [
            pltpu.VMEM((many, width), wide),
            pltpu.VMEM((sum(counts), width), low_type),
            pltpu.VMEM((4, 8, LANES), wide),
            pltpu.VMEM((6, 8, LANES), wide),
            pltpu.VMEM((gram_rows, 2 * part), wide),
            pltpu.VMEM((4, gram_rows // 8, 2 * part), wide),
            pltpu.VMEM((3, gram_rows // 8, 2 * part), wide),
            pltpu.VMEM((gram_rows, 2 * part), wide),
            pltpu.SemaphoreType.DMA((2, 6)),
            pltpu.SemaphoreType.DMA((2, 8)),
            pltpu.SemaphoreType.DMA((2, 14)),
        ]
        grads_shape = [
            jax.ShapeDtypeStruct((sum(counts), width), wide),
            jax.ShapeDtypeStruct((sum(counts), width), low_type),
        ]
        grads_specs = [any_space] * 2
    else:
        grads_shape = [jax.ShapeDtypeStruct(weight.shape, low_type) for weight in weights]
        grads_specs = [any_space] * 3
    return pl.pallas_call(
        functools.partial(client_kernel, gather, ratios, images, classes),
        out_shape=grads_shape
        + [
            jax.ShapeDtypeStruct(params.shape, wide),
            jax.ShapeDtypeStruct((classes * half // LANES, LANES), wide),
            jax.ShapeDtypeStruct((8, LANES), wide),
        ],
        in_specs=[any_space, vmem, smem, vmem, vmem] + [any_space] * len(weights),
        out_specs=grads_specs + [vmem, any_space, vmem],
        scratch_shapes=scratch,
        compiler_params=pltpu.CompilerParams(
            collective_id=0, has_side_effects=True, vmem_limit_bytes=VMEM_BYTES
        ),
    )(features, labels, flag, params, head, *weights)


def adam_update(param, grad, first, second, rate, decay):
    first = adam_first * first + (1.0 - adam_first) * grad
    second = adam_second * second + (1.0 - adam_second) * grad * grad
    first_hat = first / (1.0 - adam_first**STEP)
    second_hat = second / (1.0 - adam_second**STEP)
    return (
        param - rate * (first_hat / (jnp.sqrt(second_hat) + adam_epsilon) + decay * param),
        first,
        second,
    )


def gram_of(section):
    return lax.dot_general(section, section, (((0,), (0,)), ((), ())), precision=precise)


def square(gram):
    return jnp.dot(gram, gram, precision=precise)


def times_poly(left, mixed):
    return schulz_first * left + jnp.dot(left, mixed, precision=precise)


def schulz(sections):
    raw_grams = lax.psum(tuple(gram_of(section) for section in sections), ("client", "chan"))
    factors = [1.0 / (jnp.sqrt(jnp.trace(gram)) + 1e-07) for gram in raw_grams]
    current = [section * factor for section, factor in zip(sections, factors)]
    grams = [gram * (factor * factor) for gram, factor in zip(raw_grams, factors)]
    for turn in range(NS_STEPS):
        mixed = [schulz_second * gram + schulz_third * square(gram) for gram in grams]
        current = [times_poly(current[slot], mixed[slot]) for slot in range(3)]
        if turn + 1 < NS_STEPS:
            grams = [
                times_poly(times_poly(grams[slot], mixed[slot]), mixed[slot]) for slot in range(3)
            ]
    return current


def base_far(ratios, bounds, master, momentum, anchor, loss_tile, grads):
    sums = [
        lax.psum_scatter(flat_rows(grad).astype(wide), ("client", "chan"), scatter_dimension=0, tiled=True)
        for grad in grads
    ]
    grad_base = jnp.concatenate(sums, axis=0)
    momentum_new = momentum_decay * momentum + (grad_base + prox_weight * (master - anchor))
    current = schulz([momentum_new[bounds[slot] : bounds[slot + 1]] for slot in range(3)])
    ortho = jnp.concatenate([current[slot] * ratios[slot] for slot in range(3)], axis=0)
    return momentum_new, ortho, lax.psum(loss_tile, ("client", "chan"))


def as_stored(rows, shape):
    return with_layout_constraint(rows.reshape(shape), Layout(major_to_minor=tuple(range(len(shape)))))


def on_device(
    features,
    labels,
    mask,
    base_master,
    base_momentum,
    global_base,
    norm_params,
    norm_first,
    norm_second,
    head,
    head_first,
    head_second,
):
    halves = lax.axis_size("chan")
    blocks = lax.axis_size("client") * halves
    half = features.shape[2]
    width = base_master.shape[2]
    channels = half * halves
    classes = head.shape[2]
    rows_first = channels // blocks
    rows_mid = 9 * width // blocks
    bounds = (0, rows_first, rows_first + rows_mid, base_master.shape[1])
    ratio = (channels / width) ** 0.5
    ratios = (ratio, 3.0, ratio)
    master, momentum, anchor = base_master[0], base_momentum[0], global_base[0]
    norms = [value.reshape(-1, LANES) for value in (norm_params, norm_first, norm_second)]
    heads = [jnp.transpose(value, (2, 0, 1)).reshape(-1, LANES) for value in (head, head_first, head_second)]
    near = lax.axis_size("client") == SPOTS[0] * SPOTS[1] * SPOTS[2]
    if near:
        weights = [master, momentum, anchor]
    else:
        low_master = master.astype(low_type)
        weights = [
            lax.all_gather(low_master[bounds[slot] : bounds[slot + 1]], ("client", "chan"), axis=0, tiled=True)
            for slot in range(3)
        ]
        split = SPOTS + (2, channels // 32, width)
        weights = [weights[0].reshape(split), weights[1], weights[2].reshape(split)]
    *grads, grad_norm, grad_head, loss_tile = client_pass(
        near, ratios, classes, features[0], labels, mask, norms[0], heads[0], weights
    )
    if near:
        fresh_momentum, ortho = grads
    else:
        fresh_momentum, ortho, loss_tile = base_far(ratios, bounds, master, momentum, anchor, loss_tile, grads)
    loss, momentum_new, base_new, base_low, *fresh = update_pass(
        loss_tile, master, fresh_momentum, ortho, norms, grad_norm, heads, grad_head
    )
    fresh_norms = [as_stored(value, norm_params.shape) for value in fresh[:3]]
    fresh_heads = [jnp.transpose(as_stored(value, (classes, 1, half)), (1, 2, 0)) for value in fresh[3:]]
    return (
        loss,
        base_new[None],
        momentum_new[None],
        base_low[None],
        *fresh_norms,
        *fresh_heads,
    )


def solution(mesh):
    wide_block = P(("client", "chan"), None, None)
    norm_block = P("client", None, "chan", None)
    head_block = P("client", "chan", None)
    return jax.shard_map(
        on_device,
        mesh=mesh,
        in_specs=(P("client", None, "chan"), P("client", None), P("client"))
        + (wide_block,) * 3
        + (norm_block,) * 3
        + (head_block,) * 3,
        out_specs=(P(),) + (wide_block,) * 3 + (norm_block,) * 3 + (head_block,) * 3,
        check_vma=False,
    )
```
